32 devices in a mesh: expert: 16 (over z, x, core), fsdp: 2 (over y).
Axes of the slice: x: 2, y: 2, z: 4, core: 2. Of those that a mesh axis runs over, the one named last changes fastest.
Arguments:
- tokens: bfloat16 [2, 2048, 2048], P('fsdp', 'expert'), may hold values from -6 to 6
- routes: int32 [2, 2048, 6], P('fsdp', 'expert'), may hold values from 0 to 15, all different within a row; in each aligned block of 128 rows (0 to 127, 128 to 255, ..., all dimensions but the last counted through in order) at most 64 rows name the same one
- cotangent: bfloat16 [2, 2048, 2048], P('fsdp', 'expert'), may hold values from -6 to 6
- attn_gain: bfloat16 [2048], P('fsdp'), may hold values from 0.5 to 1.5
- w_query: bfloat16 [2048, 3072], P('fsdp'), may hold values from -0.3125 to 0.3125
- latent_weight: bfloat16 [2048, 576], P('fsdp'), may hold values from -0.125 to 0.125
- latent_norm_gain: bfloat16 [512], P('fsdp'), may hold values from 0.5 to 1.5
- expand_weight: bfloat16 [512, 4096], P('fsdp'), may hold values from -0.25 to 0.25
- w_out: bfloat16 [2048, 2048], P('fsdp'), may hold values from -0.25 to 0.25
- ffn_gain: bfloat16 [2048], P('fsdp'), may hold values from 0.5 to 1.5
- w_router: bfloat16 [2048, 16], P('fsdp'), may hold values from -0.0625 to 0.0625
- shared_gate: bfloat16 [2048, 2816], P(('expert', 'fsdp')), may hold values from -0.125 to 0.125
- shared_up: bfloat16 [2048, 2816], P(('expert', 'fsdp')), may hold values from -0.125 to 0.125
- shared_down: bfloat16 [2816, 2048], P(('expert', 'fsdp')), may hold values from -0.15625 to 0.15625
- expert_gate: bfloat16 [16, 2048, 1408], P('expert', None, 'fsdp'), may hold values from -0.125 to 0.125
- expert_up: bfloat16 [16, 2048, 1408], P('expert', None, 'fsdp'), may hold values from -0.125 to 0.125
- expert_down: bfloat16 [16, 1408, 2048], P('expert', 'fsdp'), may hold values from -3 to 3
Outputs:
- output: bfloat16 [2, 2048, 2048], P('fsdp', 'expert')
- tokens_grad: bfloat16 [2, 2048, 2048], P('fsdp', 'expert')
- attn_gain_grad: float32 [2048], P('fsdp')
- w_query_grad: float32 [2048, 3072], P('fsdp')
- w_latent_grad: float32 [2048, 576], P('fsdp')
- latent_gain_grad: float32 [512], P('fsdp')
- w_expand_grad: float32 [512, 4096], P('fsdp')
- w_out_grad: float32 [2048, 2048], P('fsdp')
- ffn_gain_grad: float32 [2048], P('fsdp')
- w_router_grad: float32 [2048, 16], P('fsdp')
- shared_gate_grad: float32 [2048, 2816], P(('expert', 'fsdp'))
- shared_up_grad: float32 [2048, 2816], P(('expert', 'fsdp'))
- shared_down_grad: float32 [2816, 2048], P(('expert', 'fsdp'))
- expert_gate_grad: float32 [16, 2048, 1408], P('expert', None, 'fsdp')
- expert_up_grad: float32 [16, 2048, 1408], P('expert', None, 'fsdp')
- expert_down_grad: float32 [16, 1408, 2048], P('expert', 'fsdp')
The draws below stay inside these ranges and needn't reach their ends.
Inputs may be any that keep to these rules, and one draw needn't show every extreme that they name: `routes`: in each aligned block of 128 rows (the rows of one device), no expert is named by more than 64 routed pairs, a bound that some block reaches; a token names 6 different experts.
All inputs are finite; a program needn't handle non-finite values.
Results may differ from the reference program's by a relative error of at most 0.03.
Values may be sent and summed in bfloat16 or wider, within the bound.
A program may use at most 512 MiB of HBM per device.

```python
import math
import jax
import jax.numpy as jnp
import numpy as np
from jax import lax

MODEL_WIDTH = 2048
HEAD_COUNT = 16
PLAIN_UNITS = 128
ROTARY_UNITS = 64
VALUE_UNITS = 128
LATENT_WIDTH = 512
FF = 1408
TOPK = 6
SHARED = 2
TOK_DEV = 128
EXPERTS = 16
SEQS = 2
SEQ_LEN = 2048
TOKEN_COUNT = 4096
CAP = 64


def block_levels(stream_key, extent, cuts, low, high):
    level = 1.0
    for axis_at, parts in cuts:
        steps = jax.random.uniform(jax.random.fold_in(jax.random.fold_in(stream_key, 6), axis_at), (parts,), jnp.float32, low / len(cuts), high / len(cuts))
        level = level * jnp.repeat(jnp.exp(steps), extent[axis_at] // parts).reshape((-1,) + (1,) * (len(extent) - 1 - axis_at))
    return level


def assign_block(key, own, number, rows, count, top, limit, lean):
    ranking = jax.random.permutation(key, count)
    packed, usual = portions_of(count, rows * top, limit, lean, True), portions_of(count, rows * top, limit, lean, False)
    places = jnp.arange(count)

    def named(tallies, offset_by):
        used = int((tallies > 0).sum())
        fixed = max(1, used // 4)
        moved = fixed + (places - fixed + offset_by * (used - fixed)) % max(1, count - fixed)
        return jnp.zeros((count,), jnp.int32).at[ranking[jnp.where(places < fixed, places, moved)]].set(jnp.asarray(tallies, jnp.int32))

    tallies = jnp.where(number % 4 == 0, named(packed, number // 4), named(usual, number - number // 4 - 1))
    mixed = jax.random.permutation(jax.random.fold_in(own, 3), count)
    donor, sink = mixed[0:count // 2 * 2:2], mixed[1:count // 2 * 2:2]
    room = jnp.minimum(tallies[donor] - 1, limit - tallies[sink]) // 2
    room = jnp.where((donor == ranking[0]) | (sink == ranking[0]) | (tallies[sink] == 0), 0, jnp.maximum(room, 0))
    moved = jax.random.randint(jax.random.fold_in(own, 4), (count // 2,), 0, 1 << 20) % (room + 1)
    tallies = tallies.at[donor].add(-moved).at[sink].add(moved)
    labels = jnp.searchsorted(jnp.cumsum(tallies), jnp.arange(rows * top), side="right").astype(jnp.int32)
    table = labels.reshape(top, rows).T
    table = table[jax.random.permutation(jax.random.fold_in(own, 1), rows)]
    offset_by = jax.random.randint(jax.random.fold_in(own, 2), (rows, 1), 0, top)
    return jnp.take_along_axis(table, (jnp.arange(top)[None, :] + offset_by) % top, axis=1)


def portions_of(number_of, total, bound, slope, full):
    weights = [(1 << 20) // math.isqrt(rank ** slope) + 1 for rank in range(1, number_of + 1)]
    largest = bound if full else min(bound, max(-(-total // number_of), total * weights[0] // sum(weights)))
    least = 1 if total - largest >= number_of - 1 else 0
    given, spare = [largest] + [least] * (number_of - 1), total - largest - least * (number_of - 1)
    while spare > 0:
        candidates = [i for i in range(1, number_of) if given[i] < largest] or [i for i in range(1, number_of) if given[i] < bound]
        pool, budget = sum([weights[i] for i in candidates]), spare
        for i in candidates:
            more = min(bound - given[i], max(1, budget * weights[i] // pool), spare)
            given[i] = given[i] + more
            spare = spare - more
    return np.array(given)


def normal_values(stream_key, dims, width, bound, pieces=(), kind=jnp.bfloat16):
    result = width * jax.random.normal(stream_key, dims, jnp.float32)
    if pieces:
        result = result * block_levels(stream_key, dims, pieces, -0.22, 0.18)
    return jnp.clip(result, -bound, bound).astype(kind)


def setup_inputs(seed: int = 0) -> dict:
    splits = jax.random.split(jax.random.key(seed), 18)
    tokens = normal_values(splits[0], (SEQS, SEQ_LEN, MODEL_WIDTH), 1.0, 6.0, ((0, 2), (1, 16)))
    routes_keys = jax.random.split(jax.random.fold_in(splits[1], 1), SEQS * SEQ_LEN // TOK_DEV)
    routes_turns = jax.random.permutation(jax.random.fold_in(splits[1], 3), SEQS * SEQ_LEN // TOK_DEV)
    routes = jax.vmap(lambda own, number: assign_block(jax.random.fold_in(splits[1], 2), own, number, TOK_DEV, EXPERTS, TOPK, CAP, 1))(routes_keys, routes_turns).reshape((SEQS, SEQ_LEN, TOPK))
    cotangent = normal_values(splits[2], (SEQS, SEQ_LEN, MODEL_WIDTH), 1.0, 6.0, ((0, 2), (1, 16)))
    attn_gain = jnp.clip(1.0 + 0.1 * jax.random.normal(splits[3], (MODEL_WIDTH,), jnp.float32), 0.5, 1.5).astype(jnp.bfloat16)
    w_query = normal_values(splits[4], (MODEL_WIDTH, HEAD_COUNT * (PLAIN_UNITS + ROTARY_UNITS)), (MODEL_WIDTH // 6) ** -0.5, 0.3125, ((0, 2),))
    latent_weight = normal_values(splits[5], (MODEL_WIDTH, LATENT_WIDTH + ROTARY_UNITS), MODEL_WIDTH ** -0.5, 0.125, ((0, 2),))
    latent_norm_gain = jnp.clip(1.0 + 0.1 * jax.random.normal(splits[6], (LATENT_WIDTH,), jnp.float32), 0.5, 1.5).astype(jnp.bfloat16)
    expand_weight = normal_values(splits[7], (LATENT_WIDTH, HEAD_COUNT * (PLAIN_UNITS + VALUE_UNITS)), LATENT_WIDTH ** -0.5, 0.25, ((0, 2),))
    w_out = normal_values(splits[8], (HEAD_COUNT * VALUE_UNITS, MODEL_WIDTH), (HEAD_COUNT * VALUE_UNITS // 4) ** -0.5, 0.25, ((0, 2),))
    ffn_gain = jnp.clip(1.0 + 0.1 * jax.random.normal(splits[9], (MODEL_WIDTH,), jnp.float32), 0.5, 1.5).astype(jnp.bfloat16)
    w_router = normal_values(splits[10], (MODEL_WIDTH, EXPERTS), (4 * MODEL_WIDTH) ** -0.5, 0.0625, ((0, 2),))
    shared_gate = normal_values(splits[11], (MODEL_WIDTH, SHARED * FF), MODEL_WIDTH ** -0.5, 0.125, ((0, 32),))
    shared_up = normal_values(splits[12], (MODEL_WIDTH, SHARED * FF), MODEL_WIDTH ** -0.5, 0.125, ((0, 32),))
    shared_down = normal_values(splits[13], (SHARED * FF, MODEL_WIDTH), (SHARED * FF // 2) ** -0.5, 0.15625, ((0, 32),))
    expert_gate = normal_values(splits[14], (EXPERTS, MODEL_WIDTH, FF), MODEL_WIDTH ** -0.5, 0.125, ((0, 16), (2, 2)))
    expert_up = normal_values(splits[15], (EXPERTS, MODEL_WIDTH, FF), MODEL_WIDTH ** -0.5, 0.125, ((0, 16), (2, 2)))
    expert_down = normal_values(splits[16], (EXPERTS, FF, MODEL_WIDTH), 4 ** -0.5, 3.0, ((0, 16), (1, 2)))
    return {"tokens": tokens, "routes": routes, "cotangent": cotangent, "attn_gain": attn_gain, "w_query": w_query, "latent_weight": latent_weight, "latent_norm_gain": latent_norm_gain, "expand_weight": expand_weight, "w_out": w_out, "ffn_gain": ffn_gain, "w_router": w_router, "shared_gate": shared_gate, "shared_up": shared_up, "shared_down": shared_down, "expert_gate": expert_gate, "expert_up": expert_up, "expert_down": expert_down}


@jax.custom_vjp
def reduced_precision(v):
    return lax.optimization_barrier(v.astype(jnp.bfloat16)).astype(jnp.float32)

@jax.custom_vjp
def low_back(v):
    return v

def low_keep(v):
    return (reduced_precision(v), None)

def low_pass(kept, grad):
    return (grad,)

def back_keep(v):
    return (v, None)

def back_low(kept, grad):
    return (reduced_precision(grad),)
reduced_precision.defvjp(low_keep, low_pass)
low_back.defvjp(back_keep, back_low)
EPS = 1e-06
TOP_PRECISION = lax.Precision.HIGHEST

def matrix_product(left, right):
    return jnp.dot(left, right, precision=TOP_PRECISION, preferred_element_type=jnp.float32)

def root_mean_norm(value, gain):
    return value * lax.rsqrt(lax.optimization_barrier(jnp.mean(value * value, axis=-1, keepdims=True)) + EPS) * gain

def rope_tables(positions):
    half = ROTARY_UNITS // 2
    freqs = 10000.0 ** (-jnp.arange(half, dtype=jnp.float32) * (2.0 / ROTARY_UNITS))
    angles = positions.astype(jnp.float32)[:, None] * freqs[None, :]
    return (jnp.cos(angles), jnp.sin(angles))

def apply_rotary(value, cosine_table, sine_table):
    half = ROTARY_UNITS // 2
    first = value[..., :half]
    second = value[..., half:]
    return jnp.concatenate([first * cosine_table - second * sine_table, first * sine_table + second * cosine_table], axis=-1)

def attend(query, key):
    feature_width = LATENT_WIDTH + ROTARY_UNITS
    block = min(512, SEQ_LEN)
    scale = (PLAIN_UNITS + ROTARY_UNITS) ** (-0.5)
    q_seq = query.reshape(SEQS, SEQ_LEN // block, block, HEAD_COUNT, feature_width)
    k_seq = key.reshape(SEQS, SEQ_LEN, feature_width)
    starts = jnp.arange(SEQ_LEN // block, dtype=jnp.int32) * block

    def one_block(q_block, key_rows, start):
        raw = low_back(jnp.einsum('qhc,kc->qhk', q_block, key_rows, precision=TOP_PRECISION))
        q_pos = start + jnp.arange(block, dtype=jnp.int32)
        k_pos = jnp.arange(SEQ_LEN, dtype=jnp.int32)
        valid = k_pos[None, None, :] <= q_pos[:, None, None]
        scores = jnp.where(valid, raw * scale, -1e+30)
        probabilities = jax.nn.softmax(scores, axis=-1)
        return jnp.einsum('olf,fb->olb', reduced_precision(probabilities), key_rows[:, :LATENT_WIDTH], precision=TOP_PRECISION)
    step = jax.checkpoint(one_block)

    def one_sequence(pair):
        q_blocks, key_rows = pair

        def inner_step(item):
            return step(item[0], key_rows, item[1])
        return lax.map(inner_step, (q_blocks, starts))
    mixed_output = lax.map(one_sequence, (q_seq, k_seq))
    return mixed_output.reshape(TOKEN_COUNT, HEAD_COUNT, LATENT_WIDTH)

def routing_tables(routes):
    blocks = TOKEN_COUNT // TOK_DEV
    flat = routes.reshape(blocks, TOK_DEV * TOPK).astype(jnp.int32)
    names = jnp.arange(EXPERTS, dtype=jnp.int32)
    onehot = (flat[:, :, None] == names[None, None, :]).astype(jnp.int32)
    slot = lax.optimization_barrier(jnp.sum((jnp.cumsum(onehot, axis=1) - onehot) * onehot, axis=2)).astype(jnp.int32)
    block_id = jnp.arange(blocks, dtype=jnp.int32)[:, None]
    place = flat * (blocks * CAP) + block_id * CAP + slot
    token = block_id * TOK_DEV + jnp.arange(TOK_DEV * TOPK, dtype=jnp.int32)[None, :] // TOPK
    table = jnp.full((EXPERTS * blocks * CAP,), TOKEN_COUNT, jnp.int32)
    table = table.at[place.reshape(-1)].set(token.reshape(-1).astype(jnp.int32))
    return (table.reshape(EXPERTS, blocks * CAP), place.reshape(TOKEN_COUNT, TOPK).astype(jnp.int32))

def layer(x, params, chosen, table, place):
    attn_gain, w_query, latent_weight, latent_norm_gain, expand_weight, w_out, ffn_gain, w_router, shared_gate, shared_up, shared_down, expert_gate, expert_up, expert_down = params
    positions = jnp.arange(TOKEN_COUNT, dtype=jnp.int32) % SEQ_LEN
    cosine_table, sine_table = rope_tables(positions)
    normed_in = reduced_precision(root_mean_norm(x, attn_gain))
    query_full = low_back(matrix_product(normed_in, w_query)).reshape(TOKEN_COUNT, HEAD_COUNT, PLAIN_UNITS + ROTARY_UNITS)
    query_nope = reduced_precision(query_full[:, :, :PLAIN_UNITS])
    expanded_latent = expand_weight.reshape(LATENT_WIDTH, HEAD_COUNT, PLAIN_UNITS + VALUE_UNITS)
    query_latent = jnp.einsum('thd,chd->thc', query_nope, expanded_latent[:, :, :PLAIN_UNITS], precision=TOP_PRECISION)
    query_rope = apply_rotary(query_full[:, :, PLAIN_UNITS:], cosine_table[:, None, :], sine_table[:, None, :])
    query = low_back(reduced_precision(jnp.concatenate([query_latent, query_rope], axis=-1)))
    latent_complete = low_back(matrix_product(normed_in, latent_weight))
    latent_state = root_mean_norm(latent_complete[:, :LATENT_WIDTH], latent_norm_gain)
    rotary_key = apply_rotary(latent_complete[:, LATENT_WIDTH:], cosine_table, sine_table)
    key = low_back(reduced_precision(jnp.concatenate([latent_state, rotary_key], axis=-1)))
    mixed_output = low_back(reduced_precision(attend(query, key)))
    heads = jnp.einsum('thc,chv->thv', mixed_output, expanded_latent[:, :, PLAIN_UNITS:], precision=TOP_PRECISION)
    heads = low_back(reduced_precision(heads.reshape(TOKEN_COUNT, HEAD_COUNT * VALUE_UNITS)))
    hidden = x + low_back(matrix_product(heads, w_out))
    normed_ffn = reduced_precision(root_mean_norm(hidden, ffn_gain))
    logits = low_back(matrix_product(normed_ffn, w_router))
    router = jax.nn.softmax(logits, axis=-1)
    gates = lax.optimization_barrier(jnp.sum(chosen * router[:, None, :], axis=-1))
    padded = jnp.concatenate([normed_ffn, jnp.zeros((1, MODEL_WIDTH), jnp.float32)], axis=0)

    def one_expert(rows_id, w_gate, w_up, w_down):
        token_rows = padded[rows_id]
        both = low_back(jnp.concatenate([matrix_product(token_rows, w_gate), matrix_product(token_rows, w_up)], axis=-1))
        act = reduced_precision(jax.nn.silu(both[:, :FF]) * both[:, FF:])
        return low_back(matrix_product(act, w_down))
    expert_step = jax.checkpoint(one_expert)

    def mapped(item):
        return expert_step(item[0], item[1], item[2], item[3])
    outputs = lax.map(mapped, (table, expert_gate, expert_up, expert_down))
    picked = outputs.reshape(-1, MODEL_WIDTH)[place]
    routed = lax.optimization_barrier(jnp.sum(gates[:, :, None] * picked, axis=1))
    shared_units = shared_gate.shape[1]
    both = low_back(jnp.concatenate([matrix_product(normed_ffn, shared_gate), matrix_product(normed_ffn, shared_up)], axis=-1))
    shared_act = reduced_precision(jax.nn.silu(both[:, :shared_units]) * both[:, shared_units:])
    shared = low_back(matrix_product(shared_act, shared_down))
    return hidden + routed + shared

def reference(tokens, routes, cotangent, attn_gain, w_query, latent_weight, latent_norm_gain, expand_weight, w_out, ffn_gain, w_router, shared_gate, shared_up, shared_down, expert_gate, expert_up, expert_down):
    x = tokens.reshape(TOKEN_COUNT, MODEL_WIDTH).astype(jnp.float32)
    grad_out = cotangent.reshape(TOKEN_COUNT, MODEL_WIDTH).astype(jnp.float32)
    flat_routes = routes.reshape(TOKEN_COUNT, TOPK).astype(jnp.int32)
    chosen = (flat_routes[:, :, None] == jnp.arange(EXPERTS, dtype=jnp.int32)[None, None, :]).astype(jnp.float32)
    table, place = routing_tables(routes)
    params = (attn_gain.astype(jnp.float32), w_query.astype(jnp.float32), latent_weight.astype(jnp.float32), latent_norm_gain.astype(jnp.float32), expand_weight.astype(jnp.float32), w_out.astype(jnp.float32), ffn_gain.astype(jnp.float32), w_router.astype(jnp.float32), shared_gate.astype(jnp.float32), shared_up.astype(jnp.float32), shared_down.astype(jnp.float32), expert_gate.astype(jnp.float32), expert_up.astype(jnp.float32), expert_down.astype(jnp.float32))

    def run(x_in, weight_arrays):
        return layer(x_in, weight_arrays, chosen, table, place)
    layer_output, pullback = jax.vjp(run, x, params)
    input_gradient, param_gradients = pullback(grad_out)
    attention_gain_grad, query_weight_gradient, latent_weight_gradient, latent_gain_gradient, expand_weight_gradient, output_weight_gradient, feed_gain_gradient, router_weight_gradient, shared_gate_gradient, shared_up_gradient, shared_down_gradient, expert_gate_gradient, expert_up_gradient, expert_down_gradient = param_gradients
    array_shape = (SEQS, SEQ_LEN, MODEL_WIDTH)
    return (layer_output.reshape(array_shape).astype(jnp.bfloat16), input_gradient.reshape(array_shape).astype(jnp.bfloat16), attention_gain_grad, query_weight_gradient, latent_weight_gradient, latent_gain_gradient, expand_weight_gradient, output_weight_gradient, feed_gain_gradient, router_weight_gradient, shared_gate_gradient, shared_up_gradient, shared_down_gradient, expert_gate_gradient, expert_up_gradient, expert_down_gradient)
```

```python
import jax
import jax.numpy as jnp
from jax import lax
from jax.sharding import PartitionSpec as P

MODEL_WIDTH = 2048
HEAD_COUNT = 16
PLAIN_UNITS = 128
ROTARY_UNITS = 64
VALUE_UNITS = 128
LATENT_WIDTH = 512
TOPK = 6


EPS = 1e-06


def matrix_product(left, right):
    return jnp.dot(left, right, preferred_element_type=jnp.float32)


def inner(left, right):
    return lax.dot_general(
        left, right, (((0,), (0,)), ((), ())), preferred_element_type=jnp.float32
    )


def outer_product(left, right):
    return lax.dot_general(
        left, right, (((1,), (1,)), ((), ())), preferred_element_type=jnp.float32
    )


def norm_forward(value, gain):
    inverse = lax.rsqrt(jnp.mean(value * value, axis=-1, keepdims=True) + EPS)
    return (value * inverse * gain, inverse)


def norm_backward(value, inverse, gain, grad):
    unit = value * inverse
    scaled = grad * gain
    d_value = inverse * (scaled - unit * jnp.mean(scaled * unit, axis=-1, keepdims=True))
    return (d_value, jnp.sum(grad * unit, axis=0))


def rope_tables(positions):
    half = ROTARY_UNITS // 2
    freqs = 10000.0 ** (-jnp.arange(half, dtype=jnp.float32) * (2.0 / ROTARY_UNITS))
    angles = positions.astype(jnp.float32)[:, None] * freqs[None, :]
    return (jnp.cos(angles), jnp.sin(angles))


def apply_rotary(value, cosine_table, sine_table):
    half = ROTARY_UNITS // 2
    first = value[..., :half]
    second = value[..., half:]
    return jnp.concatenate(
        [first * cosine_table - second * sine_table, first * sine_table + second * cosine_table],
        axis=-1,
    )


def reverse_rotary(grad, cosine_table, sine_table):
    half = ROTARY_UNITS // 2
    first = grad[..., :half]
    second = grad[..., half:]
    return jnp.concatenate(
        [first * cosine_table + second * sine_table, second * cosine_table - first * sine_table],
        axis=-1,
    )


def silu_parts(value):
    sigma = jax.nn.sigmoid(value)
    return (value * sigma, sigma * (1.0 + value * (1.0 - sigma)))


def body(
    tokens,
    routes,
    cotangent,
    attn_gain,
    w_query,
    latent_weight,
    latent_norm_gain,
    expand_weight,
    w_out,
    ffn_gain,
    w_router,
    shared_gate,
    shared_up,
    shared_down,
    expert_gate,
    expert_up,
    expert_down,
):
    device_local = tokens.shape[1]
    experts = lax.axis_size("expert")
    shards = lax.axis_size("fsdp")
    position = lax.axis_index("expert")
    capacity = shards * (
        (device_local * TOPK * 4 + experts * 3 * shards - 1) // (experts * 3 * shards)
    )
    seq_len = device_local * experts
    feature_width = LATENT_WIDTH + ROTARY_UNITS
    scale = (PLAIN_UNITS + ROTARY_UNITS) ** (-0.5)
    attention_gain_grad, wq, wlat, g_lat, expand_matrix, wout, g_ffn, wrout = (
        lax.all_gather(attn_gain, "fsdp", axis=0, tiled=True),
        lax.all_gather(w_query, "fsdp", axis=0, tiled=True),
        lax.all_gather(latent_weight, "fsdp", axis=0, tiled=True),
        lax.all_gather(latent_norm_gain, "fsdp", axis=0, tiled=True),
        lax.all_gather(expand_weight, "fsdp", axis=0, tiled=True),
        lax.all_gather(w_out, "fsdp", axis=0, tiled=True),
        lax.all_gather(ffn_gain, "fsdp", axis=0, tiled=True),
        lax.all_gather(w_router, "fsdp", axis=0, tiled=True),
    )
    sgate, sup, sdown = (
        lax.all_gather(shared_gate, ("expert", "fsdp"), axis=0, tiled=True),
        lax.all_gather(shared_up, ("expert", "fsdp"), axis=0, tiled=True),
        lax.all_gather(shared_down, ("expert", "fsdp"), axis=0, tiled=True),
    )
    attention_gain_grad = attention_gain_grad.astype(jnp.float32)
    g_lat = g_lat.astype(jnp.float32)
    g_ffn = g_ffn.astype(jnp.float32)
    x_in = tokens[0].astype(jnp.float32)
    grad_out = cotangent[0].astype(jnp.float32)
    positions = position * device_local + jnp.arange(device_local, dtype=jnp.int32)
    cosine_table, sine_table = rope_tables(positions)
    normed, inv_attn = norm_forward(x_in, attention_gain_grad)
    normed_in = normed.astype(jnp.bfloat16)
    query_full = matrix_product(normed_in, wq).reshape(
        device_local, HEAD_COUNT, PLAIN_UNITS + ROTARY_UNITS
    )
    query_nope = query_full[:, :, :PLAIN_UNITS].astype(jnp.bfloat16)
    expanded_latent = expand_matrix.reshape(LATENT_WIDTH, HEAD_COUNT, PLAIN_UNITS + VALUE_UNITS)
    key_part = expanded_latent[:, :, :PLAIN_UNITS]
    value_part = expanded_latent[:, :, PLAIN_UNITS:]
    query_latent = jnp.einsum(
        "thd,chd->thc", query_nope, key_part, preferred_element_type=jnp.float32
    )
    query_rope = apply_rotary(
        query_full[:, :, PLAIN_UNITS:], cosine_table[:, None, :], sine_table[:, None, :]
    )
    token_rows = device_local * HEAD_COUNT
    query = (
        jnp.concatenate([query_latent, query_rope], axis=-1)
        .astype(jnp.bfloat16)
        .reshape(token_rows, feature_width)
    )
    latent_complete = matrix_product(normed_in, wlat)
    packed_rows = latent_complete[:, :LATENT_WIDTH]
    latent_state, inv_lat = norm_forward(packed_rows, g_lat)
    rotary_key = apply_rotary(latent_complete[:, LATENT_WIDTH:], cosine_table, sine_table)
    key = jnp.concatenate([latent_state, rotary_key], axis=-1).astype(jnp.bfloat16)
    keys_all = lax.all_gather(key, "expert", axis=0, tiled=True)
    block = min(512, seq_len)
    token_tally = (position * device_local + device_local + block - 1) // block
    q_pos = position * device_local + jnp.arange(token_rows, dtype=jnp.int32) // HEAD_COUNT

    def scores_of(index):
        key_rows = lax.dynamic_slice_in_dim(keys_all, index * block, block, 0)
        raw = outer_product(query, key_rows)
        k_pos = index * block + jnp.arange(block, dtype=jnp.int32)
        valid = k_pos[None, :] <= q_pos[:, None]
        return (jnp.where(valid, raw * scale, -1e30), key_rows)

    def stats_step(index, carry):
        top, total = carry
        scores, unused = scores_of(index)
        new_top = jnp.maximum(top, jnp.max(scores, axis=1))
        total = total * jnp.exp(top - new_top) + jnp.sum(jnp.exp(scores - new_top[:, None]), axis=1)
        return (new_top, total)

    top, total = lax.fori_loop(
        0,
        token_tally,
        stats_step,
        (jnp.full((token_rows,), -1e30, jnp.float32), jnp.zeros((token_rows,), jnp.float32)),
    )
    log_total = top + jnp.log(total)

    def mixing_update(index, running_total):
        scores, key_rows = scores_of(index)
        weight_arrays = jnp.exp(scores - log_total[:, None]).astype(jnp.bfloat16)
        return running_total + matrix_product(weight_arrays, key_rows[:, :LATENT_WIDTH])

    mixed_output_sum = lax.fori_loop(
        0, token_tally, mixing_update, jnp.zeros((token_rows, LATENT_WIDTH), jnp.float32)
    )
    mixed_output = mixed_output_sum.astype(jnp.bfloat16).reshape(
        device_local, HEAD_COUNT, LATENT_WIDTH
    )
    heads = jnp.einsum("thc,chv->thv", mixed_output, value_part, preferred_element_type=jnp.float32)
    heads = heads.reshape(device_local, HEAD_COUNT * VALUE_UNITS).astype(jnp.bfloat16)
    hidden = x_in + matrix_product(heads, wout)
    normed2, inv_ffn = norm_forward(hidden, g_ffn)
    normed_ffn = normed2.astype(jnp.bfloat16)
    logits = matrix_product(normed_ffn, wrout)
    router = jax.nn.softmax(logits, axis=-1)
    own_routes = routes[0]
    names = jnp.arange(experts, dtype=jnp.int32)
    chosen = (own_routes[:, :, None] == names[None, None, :]).astype(jnp.float32)
    gates = jnp.sum(chosen * router[:, None, :], axis=-1)
    hits = (own_routes.reshape(device_local * TOPK)[:, None] == names[None, :]).astype(jnp.int32)
    slot = jnp.sum((jnp.cumsum(hits, axis=0) - hits) * hits, axis=1)
    place = own_routes.reshape(device_local * TOPK) * capacity + slot
    token_of = jnp.arange(device_local * TOPK, dtype=jnp.int32) // TOPK
    table = jnp.full((experts * capacity,), device_local, jnp.int32).at[place].set(token_of)
    padded = jnp.concatenate([normed_ffn, jnp.zeros((1, MODEL_WIDTH), jnp.bfloat16)], axis=0)
    buffer = padded[table].reshape(experts, capacity, MODEL_WIDTH)
    w_g, w_u, w_d = (expert_gate[0], expert_up[0], expert_down[0])

    def spread(values):
        return jnp.broadcast_to(values[:, None], (experts, shards, capacity, MODEL_WIDTH)).reshape(
            experts * shards, capacity, MODEL_WIDTH
        )

    def collect(back):
        return jnp.sum(back.reshape(experts, shards, capacity, MODEL_WIDTH), axis=1).reshape(
            experts * capacity, MODEL_WIDTH
        )

    received = lax.all_to_all(
        spread(buffer), ("expert", "fsdp"), split_axis=0, concat_axis=0, tiled=True
    )
    ex_rows = received.reshape(-1, MODEL_WIDTH)
    pre_gate = matrix_product(ex_rows, w_g)
    pre_up = matrix_product(ex_rows, w_u)
    act_gate, slope = silu_parts(pre_gate)
    ex_act = (act_gate * pre_up).astype(jnp.bfloat16)
    ex_out = matrix_product(ex_act, w_d).reshape(received.shape)
    returned = lax.all_to_all(
        ex_out.astype(jnp.bfloat16), ("expert", "fsdp"), split_axis=0, concat_axis=0, tiled=True
    ).astype(ex_out.dtype)
    results = collect(returned)
    picked = results[place].reshape(device_local, TOPK, MODEL_WIDTH)
    routed = jnp.sum(gates[:, :, None] * picked, axis=1)
    sh_gate = matrix_product(normed_ffn, sgate)
    sh_up = matrix_product(normed_ffn, sup)
    sh_silu, sh_slope = silu_parts(sh_gate)
    sh_act = (sh_silu * sh_up).astype(jnp.bfloat16)
    shared = matrix_product(sh_act, sdown)
    output = hidden + routed + shared
    d_shared = grad_out.astype(jnp.bfloat16)
    shared_down_gradient = inner(sh_act, d_shared)
    d_sh_act = outer_product(d_shared, sdown)
    d_sh_gate = (d_sh_act * sh_up * sh_slope).astype(jnp.bfloat16)
    d_sh_up = (d_sh_act * sh_silu).astype(jnp.bfloat16)
    shared_gate_gradient = inner(normed_ffn, d_sh_gate)
    shared_up_gradient = inner(normed_ffn, d_sh_up)
    d_normed_ffn = outer_product(d_sh_gate, sgate) + outer_product(d_sh_up, sup)
    d_picked = (
        (gates[:, :, None] * grad_out[:, None, :])
        .astype(jnp.bfloat16)
        .reshape(device_local * TOPK, MODEL_WIDTH)
    )
    d_gates = jnp.sum(picked * grad_out[:, None, :], axis=2)
    d_buffer = (
        jnp.zeros((experts * capacity, MODEL_WIDTH), jnp.bfloat16)
        .at[place]
        .set(d_picked)
        .reshape(experts, capacity, MODEL_WIDTH)
    )
    d_received = lax.all_to_all(
        spread(d_buffer), ("expert", "fsdp"), split_axis=0, concat_axis=0, tiled=True
    )
    d_rows = d_received.reshape(-1, MODEL_WIDTH)
    d_act = outer_product(d_rows, w_d)
    g_down = inner(ex_act, d_rows)
    d_pre_gate = (d_act * pre_up * slope).astype(jnp.bfloat16)
    d_pre_up = (d_act * act_gate).astype(jnp.bfloat16)
    g_gate = inner(ex_rows, d_pre_gate)
    g_up = inner(ex_rows, d_pre_up)
    d_ex_rows = (outer_product(d_pre_gate, w_g) + outer_product(d_pre_up, w_u)).reshape(
        received.shape
    )
    d_returned = lax.all_to_all(
        d_ex_rows.astype(jnp.bfloat16), ("expert", "fsdp"), split_axis=0, concat_axis=0, tiled=True
    ).astype(d_ex_rows.dtype)
    d_results = collect(d_returned)
    d_normed_ffn = d_normed_ffn + jnp.sum(
        d_results[place].reshape(device_local, TOPK, MODEL_WIDTH), axis=1
    )
    d_router = jnp.sum(chosen * d_gates[:, :, None], axis=1)
    d_logits = (router * (d_router - jnp.sum(router * d_router, axis=1, keepdims=True))).astype(
        jnp.bfloat16
    )
    router_weight_gradient = inner(normed_ffn, d_logits)
    d_normed_ffn = d_normed_ffn + outer_product(d_logits, wrout)
    d_hidden_norm, g_ffn_grad = norm_backward(hidden, inv_ffn, g_ffn, d_normed_ffn)
    d_hidden = grad_out + d_hidden_norm
    d_attn = d_hidden.astype(jnp.bfloat16)
    output_weight_gradient = inner(heads, d_attn)
    d_heads = (
        outer_product(d_attn, wout)
        .astype(jnp.bfloat16)
        .reshape(device_local, HEAD_COUNT, VALUE_UNITS)
    )
    value_weight_gradient = jnp.einsum(
        "thc,thv->chv", mixed_output, d_heads, preferred_element_type=jnp.float32
    )
    mixed_gradient = jnp.einsum(
        "thv,chv->thc", d_heads, value_part, preferred_element_type=jnp.float32
    )
    mixed_gradient = mixed_gradient.astype(jnp.bfloat16).reshape(token_rows, LATENT_WIDTH)
    delta = jnp.sum(mixed_gradient.astype(jnp.float32) * mixed_output_sum, axis=1)

    def back_step(index, carry):
        d_query_acc, d_keys_acc = carry
        scores, key_rows = scores_of(index)
        weight_arrays = jnp.exp(scores - log_total[:, None])
        weight_gradients = outer_product(mixed_gradient, key_rows[:, :LATENT_WIDTH])
        d_scores = (weight_arrays * (weight_gradients - delta[:, None]) * scale).astype(
            jnp.bfloat16
        )
        d_query_acc = d_query_acc + matrix_product(d_scores, key_rows)
        d_values = inner(weight_arrays.astype(jnp.bfloat16), mixed_gradient)
        d_block = inner(d_scores, query) + jnp.concatenate(
            [d_values, jnp.zeros((block, ROTARY_UNITS), jnp.float32)], axis=1
        )
        previous = lax.dynamic_slice_in_dim(d_keys_acc, index * block, block, 0)
        return (
            d_query_acc,
            lax.dynamic_update_slice_in_dim(d_keys_acc, previous + d_block, index * block, 0),
        )

    d_query, d_keys = lax.fori_loop(
        0,
        token_tally,
        back_step,
        (
            jnp.zeros((token_rows, feature_width), jnp.float32),
            jnp.zeros((seq_len, feature_width), jnp.float32),
        ),
    )
    key_gradient = lax.psum_scatter(
        d_keys.astype(jnp.bfloat16), "expert", scatter_dimension=0, tiled=True
    )
    query_up_gradient = d_query.astype(jnp.bfloat16).reshape(
        device_local, HEAD_COUNT, feature_width
    )
    query_latent_gradient = query_up_gradient[:, :, :LATENT_WIDTH]
    key_weight_gradient = jnp.einsum(
        "thc,thd->chd", query_latent_gradient, query_nope, preferred_element_type=jnp.float32
    )
    d_q_nope = jnp.einsum(
        "thc,chd->thd", query_latent_gradient, key_part, preferred_element_type=jnp.float32
    )
    d_q_rope = reverse_rotary(
        query_up_gradient[:, :, LATENT_WIDTH:].astype(jnp.float32),
        cosine_table[:, None, :],
        sine_table[:, None, :],
    )
    d_query_full = (
        jnp.concatenate([d_q_nope, d_q_rope], axis=-1)
        .astype(jnp.bfloat16)
        .reshape(device_local, HEAD_COUNT * (PLAIN_UNITS + ROTARY_UNITS))
    )
    query_weight_gradient = inner(normed_in, d_query_full)
    d_normed_in = outer_product(d_query_full, wq)
    latent_gradient = key_gradient[:, :LATENT_WIDTH].astype(jnp.float32)
    rotary_key_gradient = reverse_rotary(
        key_gradient[:, LATENT_WIDTH:].astype(jnp.float32), cosine_table, sine_table
    )
    d_compact, g_lat_grad = norm_backward(packed_rows, inv_lat, g_lat, latent_gradient)
    d_latent_full = jnp.concatenate([d_compact, rotary_key_gradient], axis=-1).astype(jnp.bfloat16)
    latent_weight_gradient = inner(normed_in, d_latent_full)
    d_normed_in = d_normed_in + outer_product(d_latent_full, wlat)
    d_norm_in, g_attn_grad = norm_backward(x_in, inv_attn, attention_gain_grad, d_normed_in)
    d_tokens = (d_hidden + d_norm_in).astype(jnp.bfloat16)
    expand_weight_gradient = jnp.concatenate(
        [key_weight_gradient, value_weight_gradient], axis=-1
    ).reshape(LATENT_WIDTH, HEAD_COUNT * (PLAIN_UNITS + VALUE_UNITS))
    r_sgate, r_sup, r_sdown = (
        lax.psum_scatter(shared_gate_gradient, ("expert", "fsdp"), scatter_dimension=0, tiled=True),
        lax.psum_scatter(shared_up_gradient, ("expert", "fsdp"), scatter_dimension=0, tiled=True),
        lax.psum_scatter(shared_down_gradient, ("expert", "fsdp"), scatter_dimension=0, tiled=True),
    )
    r_attn, r_query, r_latent, r_lgain, r_expand, r_out, r_fgain, r_router = (
        lax.psum_scatter(
            g_attn_grad.astype(jnp.bfloat16), "fsdp", scatter_dimension=0, tiled=True
        ).astype(jnp.float32),
        lax.psum_scatter(
            query_weight_gradient.astype(jnp.bfloat16), "fsdp", scatter_dimension=0, tiled=True
        ).astype(jnp.float32),
        lax.psum_scatter(
            latent_weight_gradient.astype(jnp.bfloat16), "fsdp", scatter_dimension=0, tiled=True
        ).astype(jnp.float32),
        lax.psum_scatter(
            g_lat_grad.astype(jnp.bfloat16), "fsdp", scatter_dimension=0, tiled=True
        ).astype(jnp.float32),
        lax.psum_scatter(
            expand_weight_gradient.astype(jnp.bfloat16), "fsdp", scatter_dimension=0, tiled=True
        ).astype(jnp.float32),
        lax.psum_scatter(
            output_weight_gradient.astype(jnp.bfloat16), "fsdp", scatter_dimension=0, tiled=True
        ).astype(jnp.float32),
        lax.psum_scatter(
            g_ffn_grad.astype(jnp.bfloat16), "fsdp", scatter_dimension=0, tiled=True
        ).astype(jnp.float32),
        lax.psum_scatter(
            router_weight_gradient.astype(jnp.bfloat16), "fsdp", scatter_dimension=0, tiled=True
        ).astype(jnp.float32),
    )
    r_attn, r_query, r_latent, r_lgain, r_expand, r_out, r_fgain, r_router = (
        lax.psum(r_attn.astype(jnp.bfloat16), "expert").astype(jnp.float32),
        lax.psum(r_query.astype(jnp.bfloat16), "expert").astype(jnp.float32),
        lax.psum(r_latent.astype(jnp.bfloat16), "expert").astype(jnp.float32),
        lax.psum(r_lgain.astype(jnp.bfloat16), "expert").astype(jnp.float32),
        lax.psum(r_expand.astype(jnp.bfloat16), "expert").astype(jnp.float32),
        lax.psum(r_out.astype(jnp.bfloat16), "expert").astype(jnp.float32),
        lax.psum(r_fgain.astype(jnp.bfloat16), "expert").astype(jnp.float32),
        lax.psum(r_router.astype(jnp.bfloat16), "expert").astype(jnp.float32),
    )
    return (
        output.astype(jnp.bfloat16)[None],
        d_tokens[None],
        r_attn,
        r_query,
        r_latent,
        r_lgain,
        r_expand,
        r_out,
        r_fgain,
        r_router,
        r_sgate,
        r_sup,
        r_sdown,
        g_gate[None],
        g_up[None],
        g_down[None],
    )


def seq_gather(rows):
    return lax.all_gather(rows, "expert", axis=0, tiled=True)


def token_gather(rows):
    return lax.all_gather(rows, ("fsdp", "expert"), axis=0, tiled=True)


def token_scatter(partial):
    return lax.psum_scatter(
        partial, ("fsdp", "expert"), scatter_dimension=0, tiled=True
    ).astype(jnp.float32)


def split_body(
    tokens,
    routes,
    cotangent,
    attn_gain,
    w_query,
    latent_weight,
    latent_norm_gain,
    expand_weight,
    w_out,
    ffn_gain,
    w_router,
    shared_gate,
    shared_up,
    shared_down,
    expert_gate,
    expert_up,
    expert_down,
):
    rows = tokens.shape[1]
    experts = lax.axis_size("expert")
    shards = lax.axis_size("fsdp")
    position = lax.axis_index("expert")
    blocks = experts * shards
    seq_len = rows * experts
    capacity = shards * ((rows * TOPK * 4 + experts * 3 * shards - 1) // (experts * 3 * shards))
    head_units = PLAIN_UNITS + ROTARY_UNITS
    pair_units = PLAIN_UNITS + VALUE_UNITS
    feature_width = LATENT_WIDTH + ROTARY_UNITS
    scale = head_units ** (-0.5)

    query_cols = lax.dynamic_slice_in_dim(w_query, position * head_units, head_units, 1)
    expand_cols = lax.dynamic_slice_in_dim(expand_weight, position * pair_units, pair_units, 1)
    packed = jnp.concatenate(
        [latent_weight, query_cols, w_router, attn_gain[:, None], ffn_gain[:, None]], axis=1
    )
    packed = lax.all_gather(packed, "fsdp", axis=0, tiled=True)
    w_front = packed[:, : feature_width + head_units]
    w_latent = packed[:, :feature_width]
    at = feature_width + head_units
    wrout = packed[:, at : at + experts]
    g_attn = packed[:, at + experts].astype(jnp.float32)
    g_ffn = packed[:, at + experts + 1].astype(jnp.float32)
    small = jnp.concatenate([expand_cols, latent_norm_gain[:, None]], axis=1)
    small = lax.all_gather(small, "fsdp", axis=0, tiled=True)
    expand_head = small[:, :pair_units]
    key_part = small[:, :PLAIN_UNITS]
    value_part = small[:, PLAIN_UNITS:pair_units]
    g_lat = small[:, pair_units].astype(jnp.float32)
    wout = lax.all_gather(w_out, "fsdp", axis=0, tiled=True)
    wq = lax.all_gather(w_query, "fsdp", axis=0, tiled=True)
    units = shared_down.shape[0]

    def to_columns(weight):
        parts = weight.reshape(weight.shape[0], blocks, units).transpose(1, 0, 2)
        return lax.all_to_all(
            parts, ("expert", "fsdp"), split_axis=0, concat_axis=0, tiled=True
        ).reshape(-1, units)

    sh_cols = to_columns(jnp.concatenate([shared_gate, shared_up], axis=0)).reshape(
        blocks, 2, shared_gate.shape[0], units
    )
    sgate = sh_cols[:, 0].reshape(-1, units)
    sup = sh_cols[:, 1].reshape(-1, units)

    grad_rows = cotangent[0]
    grad_out = grad_rows.astype(jnp.float32)
    all_routes = token_gather(routes[0])
    all_grads = token_gather(grad_rows)

    x_in = tokens[0].astype(jnp.float32)
    normed, inv_attn = norm_forward(x_in, g_attn)
    normed_in = normed.astype(jnp.bfloat16)
    seq_normed = seq_gather(normed_in)
    cosine_table, sine_table = rope_tables(jnp.arange(seq_len, dtype=jnp.int32))
    front = matrix_product(seq_normed, w_front)
    latent_rows, _ = norm_forward(front[:, :LATENT_WIDTH], g_lat)
    latent_rows = latent_rows.astype(jnp.bfloat16)
    key_rope = apply_rotary(front[:, LATENT_WIDTH:feature_width], cosine_table, sine_table)
    query_full = front[:, feature_width:]
    query_rope = apply_rotary(query_full[:, PLAIN_UNITS:], cosine_table, sine_table)
    query = jnp.concatenate([query_full[:, :PLAIN_UNITS], query_rope], axis=1).astype(jnp.bfloat16)
    pairs = matrix_product(latent_rows, expand_head)
    key = jnp.concatenate([pairs[:, :PLAIN_UNITS], key_rope], axis=1).astype(jnp.bfloat16)
    value = pairs[:, PLAIN_UNITS:].astype(jnp.bfloat16)
    order = jnp.arange(seq_len, dtype=jnp.int32)
    scores = jnp.where(
        order[None, :] <= order[:, None], outer_product(query, key) * scale, -1e30
    )
    top = jnp.max(scores, axis=1, keepdims=True)
    exps = jnp.exp(scores - top)
    probs = exps / jnp.sum(exps, axis=1, keepdims=True)
    low_probs = probs.astype(jnp.bfloat16)
    head_sum = matrix_product(low_probs, value)
    head_rows = head_sum.astype(jnp.bfloat16)
    heads = lax.all_to_all(
        head_rows.reshape(experts, rows, VALUE_UNITS),
        "expert",
        split_axis=0,
        concat_axis=0,
        tiled=True,
    )
    heads = heads.transpose(1, 0, 2).reshape(rows, experts * VALUE_UNITS)
    hidden = x_in + matrix_product(heads, wout)
    normed2, inv_ffn = norm_forward(hidden, g_ffn)
    normed_ffn = normed2.astype(jnp.bfloat16)
    router = jax.nn.softmax(matrix_product(normed_ffn, wrout), axis=-1)

    all_normed = token_gather(normed_ffn)
    mix = matrix_product(all_normed, jnp.concatenate([sgate, sup, wrout], axis=1))
    sh_gate = mix[:, :units]
    sh_up = mix[:, units : 2 * units]
    all_router = jax.nn.softmax(mix[:, 2 * units :], axis=-1)
    names = jnp.arange(experts, dtype=jnp.int32)
    own_gate = jnp.sum(jnp.where(names[None, :] == position, all_router, 0.0), axis=1)
    hit = jnp.any(all_routes == position, axis=1).reshape(blocks, rows)
    count = hit.astype(jnp.int32)
    slot = jnp.cumsum(count, axis=1) - count
    place = jnp.where(hit, slot, -1)
    onehot = place[:, None, :] == jnp.arange(capacity, dtype=jnp.int32)[None, :, None]
    pick = onehot.astype(jnp.bfloat16)
    gate_slot = jnp.sum(
        jnp.where(onehot, own_gate.reshape(blocks, 1, rows), 0.0), axis=2
    ).reshape(-1, 1)

    def take(whole):
        return jnp.einsum(
            "bst,btd->bsd", pick, whole.reshape(blocks, rows, -1),
            preferred_element_type=jnp.bfloat16,
        ).reshape(blocks * capacity, -1)

    def put_back(slots):
        return jnp.einsum(
            "bst,bsd->btd", pick, slots.astype(jnp.bfloat16).reshape(blocks, capacity, -1),
            preferred_element_type=jnp.float32,
        ).reshape(blocks * rows, -1)

    w_g, w_u, w_d = (expert_gate[0], expert_up[0], expert_down[0])
    ex_rows = take(all_normed)
    ex_grads = take(all_grads)
    pre_gate = matrix_product(ex_rows, w_g)
    pre_up = matrix_product(ex_rows, w_u)
    act_gate, slope = silu_parts(pre_gate)
    ex_act = act_gate * pre_up
    scaled_act = (gate_slot * ex_act).astype(jnp.bfloat16)
    back_act = outer_product(ex_grads, w_d)
    d_gate_slot = jnp.sum(ex_act * back_act, axis=1)
    d_act = gate_slot * back_act
    d_pre_gate = (d_act * pre_up * slope).astype(jnp.bfloat16)
    d_pre_up = (d_act * act_gate).astype(jnp.bfloat16)
    g_down = inner(scaled_act, ex_grads)
    g_gate = inner(ex_rows, d_pre_gate)
    g_up = inner(ex_rows, d_pre_up)
    ex_out = matrix_product(scaled_act, w_d)
    d_ex_rows = outer_product(d_pre_gate, w_g) + outer_product(d_pre_up, w_u)

    sh_silu, sh_slope = silu_parts(sh_gate)
    sh_act = (sh_silu * sh_up).astype(jnp.bfloat16)
    d_sh_act = outer_product(all_grads, shared_down)
    d_sh_gate = (d_sh_act * sh_up * sh_slope).astype(jnp.bfloat16)
    d_sh_up = (d_sh_act * sh_silu).astype(jnp.bfloat16)
    g_sdown = inner(sh_act, all_grads)
    g_sgate = inner(all_normed, d_sh_gate)
    g_sup = inner(all_normed, d_sh_up)

    out_part = put_back(ex_out) + matrix_product(sh_act, shared_down)
    d_part = put_back(d_ex_rows) + outer_product(d_sh_gate, sgate) + outer_product(d_sh_up, sup)
    d_gate_rows = jnp.sum(
        jnp.where(onehot, d_gate_slot.reshape(blocks, capacity, 1), 0.0), axis=1
    ).reshape(-1, 1)
    d_gate_cols = jnp.where(
        jnp.arange(128, dtype=jnp.int32)[None, :] == position, d_gate_rows, 0.0
    )
    d_part = jnp.concatenate(
        [d_part.astype(jnp.bfloat16), d_gate_cols.astype(jnp.bfloat16)], axis=1
    )
    d_back = token_scatter(d_part)
    d_normed_ffn = d_back[:, :MODEL_WIDTH]
    d_router = d_back[:, MODEL_WIDTH : MODEL_WIDTH + experts]
    output = hidden + token_scatter(out_part.astype(jnp.bfloat16))

    d_logits = (router * (d_router - jnp.sum(router * d_router, axis=1, keepdims=True))).astype(
        jnp.bfloat16
    )
    g_router = inner(normed_ffn, d_logits)
    d_normed_ffn = d_normed_ffn + outer_product(d_logits, wrout)
    d_hidden_norm, g_ffn_grad = norm_backward(hidden, inv_ffn, g_ffn, d_normed_ffn)
    d_hidden = grad_out + d_hidden_norm
    d_attn = d_hidden.astype(jnp.bfloat16)

    d_heads = outer_product(d_attn, wout).astype(jnp.bfloat16)
    d_heads = d_heads.reshape(rows, experts, VALUE_UNITS).transpose(1, 0, 2)
    d_head = lax.all_to_all(
        d_heads, "expert", split_axis=0, concat_axis=0, tiled=True
    ).reshape(seq_len, VALUE_UNITS)
    seq_d_attn = seq_gather(d_attn)
    g_out_head = inner(head_rows, seq_d_attn)
    delta = jnp.sum(d_head.astype(jnp.float32) * head_sum, axis=1, keepdims=True)
    d_scores = (probs * (outer_product(d_head, value) - delta) * scale).astype(jnp.bfloat16)
    d_query = matrix_product(d_scores, key)
    d_key = inner(d_scores, query)
    d_value = inner(low_probs, d_head).astype(jnp.bfloat16)
    d_key_plain = d_key[:, :PLAIN_UNITS].astype(jnp.bfloat16)
    d_pairs = jnp.concatenate([d_key_plain, d_value], axis=1)
    g_expand_head = inner(latent_rows, d_pairs)
    d_keys = jnp.concatenate(
        [outer_product(d_pairs, expand_head), d_key[:, PLAIN_UNITS:]], axis=1
    )
    key_gradient = lax.psum_scatter(
        d_keys.astype(jnp.bfloat16), "expert", scatter_dimension=0, tiled=True
    ).astype(jnp.float32)
    d_query_full = jnp.concatenate(
        [
            d_query[:, :PLAIN_UNITS],
            reverse_rotary(d_query[:, PLAIN_UNITS:], cosine_table, sine_table),
        ],
        axis=1,
    ).astype(jnp.bfloat16)
    g_query_head = inner(seq_normed, d_query_full)
    own_d_query = lax.all_to_all(
        d_query_full.reshape(experts, rows, head_units),
        "expert",
        split_axis=0,
        concat_axis=0,
        tiled=True,
    )
    own_d_query = own_d_query.transpose(1, 0, 2).reshape(rows, experts * head_units)
    d_normed_in = outer_product(own_d_query, wq)
    own_latent = lax.dynamic_slice_in_dim(front[:, :LATENT_WIDTH], position * rows, rows, 0)
    own_cosine = lax.dynamic_slice_in_dim(cosine_table, position * rows, rows, 0)
    own_sine = lax.dynamic_slice_in_dim(sine_table, position * rows, rows, 0)
    inv_lat = lax.rsqrt(jnp.mean(own_latent * own_latent, axis=-1, keepdims=True) + EPS)
    d_compact, g_lat_grad = norm_backward(
        own_latent, inv_lat, g_lat, key_gradient[:, :LATENT_WIDTH]
    )
    d_rope = reverse_rotary(key_gradient[:, LATENT_WIDTH:], own_cosine, own_sine)
    d_latent_full = jnp.concatenate([d_compact, d_rope], axis=-1).astype(jnp.bfloat16)
    g_latent = inner(normed_in, d_latent_full)
    d_normed_in = d_normed_in + outer_product(d_latent_full, w_latent)
    d_norm_in, g_attn_grad = norm_backward(x_in, inv_attn, g_attn, d_normed_in)
    d_tokens = (d_hidden + d_norm_in).astype(jnp.bfloat16)

    shard = lax.axis_index("fsdp")

    def own_half(whole):
        size = whole.shape[0] // shards
        return lax.dynamic_slice_in_dim(whole, shard * size, size, 0)

    def over_shards(partial):
        return lax.psum_scatter(
            partial.astype(jnp.bfloat16), "fsdp", scatter_dimension=0, tiled=True
        )

    def to_rows(cols):
        back = lax.all_to_all(
            cols.astype(jnp.bfloat16).reshape(blocks, -1, units),
            ("expert", "fsdp"),
            split_axis=0,
            concat_axis=0,
            tiled=True,
        )
        return back.transpose(1, 0, 2).reshape(-1, blocks * units).astype(jnp.float32)

    half = MODEL_WIDTH // blocks
    both = to_rows(
        jnp.stack(
            [g_sgate.reshape(blocks, half, units), g_sup.reshape(blocks, half, units)], axis=1
        )
    )
    r_sgate, r_sup = (both[:half], both[half:])
    r_query = lax.all_gather(over_shards(g_query_head), "expert", axis=1, tiled=True)
    r_expand = lax.all_gather(over_shards(g_expand_head), "expert", axis=1, tiled=True)
    r_out = own_half(
        lax.all_gather(
            lax.psum(g_out_head.astype(jnp.bfloat16), "fsdp"), "expert", axis=0, tiled=True
        )
    )
    columns = jnp.concatenate([g_latent, g_router], axis=1).astype(jnp.bfloat16)
    columns = lax.psum_scatter(columns, ("fsdp", "expert"), scatter_dimension=0, tiled=True)
    columns = lax.all_gather(columns, "expert", axis=0, tiled=True).astype(jnp.float32)
    gains = lax.psum(jnp.concatenate([g_attn_grad, g_ffn_grad, g_lat_grad]), ("fsdp", "expert"))
    return (
        output.astype(jnp.bfloat16)[None],
        d_tokens[None],
        own_half(gains[:MODEL_WIDTH]),
        r_query.astype(jnp.float32),
        columns[:, :feature_width],
        own_half(gains[2 * MODEL_WIDTH :]),
        r_expand.astype(jnp.float32),
        r_out.astype(jnp.float32),
        own_half(gains[MODEL_WIDTH : 2 * MODEL_WIDTH]),
        columns[:, feature_width:],
        r_sgate,
        r_sup,
        g_sdown,
        g_gate[None],
        g_up[None],
        g_down[None],
    )


def solution(mesh):
    whole_heads = mesh.shape["expert"] == HEAD_COUNT
    return jax.shard_map(
        split_body if whole_heads else body,
        mesh=mesh,
        in_specs=(
            P("fsdp", "expert", None),
            P("fsdp", "expert", None),
            P("fsdp", "expert", None),
            P("fsdp"),
            P("fsdp", None),
            P("fsdp", None),
            P("fsdp"),
            P("fsdp", None),
            P("fsdp", None),
            P("fsdp"),
            P("fsdp", None),
            P(("expert", "fsdp"), None),
            P(("expert", "fsdp"), None),
            P(("expert", "fsdp"), None),
            P("expert", None, "fsdp"),
            P("expert", None, "fsdp"),
            P("expert", "fsdp", None),
        ),
        out_specs=(
            P("fsdp", "expert", None),
            P("fsdp", "expert", None),
            P("fsdp"),
            P("fsdp", None),
            P("fsdp", None),
            P("fsdp"),
            P("fsdp", None),
            P("fsdp", None),
            P("fsdp"),
            P("fsdp", None),
            P(("expert", "fsdp"), None),
            P(("expert", "fsdp"), None),
            P(("expert", "fsdp"), None),
            P("expert", None, "fsdp"),
            P("expert", None, "fsdp"),
            P("expert", "fsdp", None),
        ),
        check_vma=False,
    )
```

```python
import functools

import jax
import jax.numpy as jnp
from jax import lax
from jax.experimental import pallas as pl
from jax.experimental.pallas import tpu as pltpu
from jax.sharding import PartitionSpec as P

MODEL_WIDTH = 2048
HEAD_COUNT = 16
PLAIN_UNITS = 128
ROTARY_UNITS = 64
VALUE_UNITS = 128
LATENT_WIDTH = 512
TOPK = 6


EPS = 1e-06


def matrix_product(left, right):
    return jnp.dot(left, right, preferred_element_type=jnp.float32)


def inner(left, right):
    return lax.dot_general(
        left, right, (((0,), (0,)), ((), ())), preferred_element_type=jnp.float32
    )


def outer_product(left, right):
    return lax.dot_general(
        left, right, (((1,), (1,)), ((), ())), preferred_element_type=jnp.float32
    )


def norm_forward(value, gain):
    inverse = lax.rsqrt(jnp.mean(value * value, axis=-1, keepdims=True) + EPS)
    return (value * inverse * gain, inverse)


def norm_backward(value, inverse, gain, grad):
    unit = value * inverse
    scaled = grad * gain
    d_value = inverse * (scaled - unit * jnp.mean(scaled * unit, axis=-1, keepdims=True))
    return (d_value, jnp.sum(grad * unit, axis=0))


def rope_tables(positions):
    half = ROTARY_UNITS // 2
    freqs = 10000.0 ** (-jnp.arange(half, dtype=jnp.float32) * (2.0 / ROTARY_UNITS))
    angles = positions.astype(jnp.float32)[:, None] * freqs[None, :]
    return (jnp.cos(angles), jnp.sin(angles))


def apply_rotary(value, cosine_table, sine_table):
    half = ROTARY_UNITS // 2
    first = value[..., :half]
    second = value[..., half:]
    return jnp.concatenate(
        [first * cosine_table - second * sine_table, first * sine_table + second * cosine_table],
        axis=-1,
    )


def reverse_rotary(grad, cosine_table, sine_table):
    half = ROTARY_UNITS // 2
    first = grad[..., :half]
    second = grad[..., half:]
    return jnp.concatenate(
        [first * cosine_table + second * sine_table, second * cosine_table - first * sine_table],
        axis=-1,
    )


def silu_parts(value):
    sigma = jax.nn.sigmoid(value)
    return (value * sigma, sigma * (1.0 + value * (1.0 - sigma)))


def body(
    tokens,
    routes,
    cotangent,
    attn_gain,
    w_query,
    latent_weight,
    latent_norm_gain,
    expand_weight,
    w_out,
    ffn_gain,
    w_router,
    shared_gate,
    shared_up,
    shared_down,
    expert_gate,
    expert_up,
    expert_down,
):
    device_local = tokens.shape[1]
    experts = lax.axis_size("expert")
    shards = lax.axis_size("fsdp")
    position = lax.axis_index("expert")
    capacity = shards * (
        (device_local * TOPK * 4 + experts * 3 * shards - 1) // (experts * 3 * shards)
    )
    seq_len = device_local * experts
    feature_width = LATENT_WIDTH + ROTARY_UNITS
    scale = (PLAIN_UNITS + ROTARY_UNITS) ** (-0.5)
    attention_gain_grad, wq, wlat, g_lat, expand_matrix, wout, g_ffn, wrout = (
        lax.all_gather(attn_gain, "fsdp", axis=0, tiled=True),
        lax.all_gather(w_query, "fsdp", axis=0, tiled=True),
        lax.all_gather(latent_weight, "fsdp", axis=0, tiled=True),
        lax.all_gather(latent_norm_gain, "fsdp", axis=0, tiled=True),
        lax.all_gather(expand_weight, "fsdp", axis=0, tiled=True),
        lax.all_gather(w_out, "fsdp", axis=0, tiled=True),
        lax.all_gather(ffn_gain, "fsdp", axis=0, tiled=True),
        lax.all_gather(w_router, "fsdp", axis=0, tiled=True),
    )
    sgate, sup, sdown = (
        lax.all_gather(shared_gate, ("expert", "fsdp"), axis=0, tiled=True),
        lax.all_gather(shared_up, ("expert", "fsdp"), axis=0, tiled=True),
        lax.all_gather(shared_down, ("expert", "fsdp"), axis=0, tiled=True),
    )
    attention_gain_grad = attention_gain_grad.astype(jnp.float32)
    g_lat = g_lat.astype(jnp.float32)
    g_ffn = g_ffn.astype(jnp.float32)
    x_in = tokens[0].astype(jnp.float32)
    grad_out = cotangent[0].astype(jnp.float32)
    positions = position * device_local + jnp.arange(device_local, dtype=jnp.int32)
    cosine_table, sine_table = rope_tables(positions)
    normed, inv_attn = norm_forward(x_in, attention_gain_grad)
    normed_in = normed.astype(jnp.bfloat16)
    query_full = matrix_product(normed_in, wq).reshape(
        device_local, HEAD_COUNT, PLAIN_UNITS + ROTARY_UNITS
    )
    query_nope = query_full[:, :, :PLAIN_UNITS].astype(jnp.bfloat16)
    expanded_latent = expand_matrix.reshape(LATENT_WIDTH, HEAD_COUNT, PLAIN_UNITS + VALUE_UNITS)
    key_part = expanded_latent[:, :, :PLAIN_UNITS]
    value_part = expanded_latent[:, :, PLAIN_UNITS:]
    query_latent = jnp.einsum(
        "thd,chd->thc", query_nope, key_part, preferred_element_type=jnp.float32
    )
    query_rope = apply_rotary(
        query_full[:, :, PLAIN_UNITS:], cosine_table[:, None, :], sine_table[:, None, :]
    )
    token_rows = device_local * HEAD_COUNT
    query = (
        jnp.concatenate([query_latent, query_rope], axis=-1)
        .astype(jnp.bfloat16)
        .reshape(token_rows, feature_width)
    )
    latent_complete = matrix_product(normed_in, wlat)
    packed_rows = latent_complete[:, :LATENT_WIDTH]
    latent_state, inv_lat = norm_forward(packed_rows, g_lat)
    rotary_key = apply_rotary(latent_complete[:, LATENT_WIDTH:], cosine_table, sine_table)
    key = jnp.concatenate([latent_state, rotary_key], axis=-1).astype(jnp.bfloat16)
    keys_all = lax.all_gather(key, "expert", axis=0, tiled=True)
    block = min(512, seq_len)
    token_tally = (position * device_local + device_local + block - 1) // block
    q_pos = position * device_local + jnp.arange(token_rows, dtype=jnp.int32) // HEAD_COUNT

    def scores_of(index):
        key_rows = lax.dynamic_slice_in_dim(keys_all, index * block, block, 0)
        raw = outer_product(query, key_rows)
        k_pos = index * block + jnp.arange(block, dtype=jnp.int32)
        valid = k_pos[None, :] <= q_pos[:, None]
        return (jnp.where(valid, raw * scale, -1e30), key_rows)

    def stats_step(index, carry):
        top, total = carry
        scores, unused = scores_of(index)
        new_top = jnp.maximum(top, jnp.max(scores, axis=1))
        total = total * jnp.exp(top - new_top) + jnp.sum(jnp.exp(scores - new_top[:, None]), axis=1)
        return (new_top, total)

    top, total = lax.fori_loop(
        0,
        token_tally,
        stats_step,
        (jnp.full((token_rows,), -1e30, jnp.float32), jnp.zeros((token_rows,), jnp.float32)),
    )
    log_total = top + jnp.log(total)

    def mixing_update(index, running_total):
        scores, key_rows = scores_of(index)
        weight_arrays = jnp.exp(scores - log_total[:, None]).astype(jnp.bfloat16)
        return running_total + matrix_product(weight_arrays, key_rows[:, :LATENT_WIDTH])

    mixed_output_sum = lax.fori_loop(
        0, token_tally, mixing_update, jnp.zeros((token_rows, LATENT_WIDTH), jnp.float32)
    )
    mixed_output = mixed_output_sum.astype(jnp.bfloat16).reshape(
        device_local, HEAD_COUNT, LATENT_WIDTH
    )
    heads = jnp.einsum("thc,chv->thv", mixed_output, value_part, preferred_element_type=jnp.float32)
    heads = heads.reshape(device_local, HEAD_COUNT * VALUE_UNITS).astype(jnp.bfloat16)
    hidden = x_in + matrix_product(heads, wout)
    normed2, inv_ffn = norm_forward(hidden, g_ffn)
    normed_ffn = normed2.astype(jnp.bfloat16)
    logits = matrix_product(normed_ffn, wrout)
    router = jax.nn.softmax(logits, axis=-1)
    own_routes = routes[0]
    names = jnp.arange(experts, dtype=jnp.int32)
    chosen = (own_routes[:, :, None] == names[None, None, :]).astype(jnp.float32)
    gates = jnp.sum(chosen * router[:, None, :], axis=-1)
    hits = (own_routes.reshape(device_local * TOPK)[:, None] == names[None, :]).astype(jnp.int32)
    slot = jnp.sum((jnp.cumsum(hits, axis=0) - hits) * hits, axis=1)
    place = own_routes.reshape(device_local * TOPK) * capacity + slot
    token_of = jnp.arange(device_local * TOPK, dtype=jnp.int32) // TOPK
    table = jnp.full((experts * capacity,), device_local, jnp.int32).at[place].set(token_of)
    padded = jnp.concatenate([normed_ffn, jnp.zeros((1, MODEL_WIDTH), jnp.bfloat16)], axis=0)
    buffer = padded[table].reshape(experts, capacity, MODEL_WIDTH)
    w_g, w_u, w_d = (expert_gate[0], expert_up[0], expert_down[0])

    def spread(values):
        return jnp.broadcast_to(values[:, None], (experts, shards, capacity, MODEL_WIDTH)).reshape(
            experts * shards, capacity, MODEL_WIDTH
        )

    def collect(back):
        return jnp.sum(back.reshape(experts, shards, capacity, MODEL_WIDTH), axis=1).reshape(
            experts * capacity, MODEL_WIDTH
        )

    received = lax.all_to_all(
        spread(buffer), ("expert", "fsdp"), split_axis=0, concat_axis=0, tiled=True
    )
    ex_rows = received.reshape(-1, MODEL_WIDTH)
    pre_gate = matrix_product(ex_rows, w_g)
    pre_up = matrix_product(ex_rows, w_u)
    act_gate, slope = silu_parts(pre_gate)
    ex_act = (act_gate * pre_up).astype(jnp.bfloat16)
    ex_out = matrix_product(ex_act, w_d).reshape(received.shape)
    returned = lax.all_to_all(
        ex_out.astype(jnp.bfloat16), ("expert", "fsdp"), split_axis=0, concat_axis=0, tiled=True
    ).astype(ex_out.dtype)
    results = collect(returned)
    picked = results[place].reshape(device_local, TOPK, MODEL_WIDTH)
    routed = jnp.sum(gates[:, :, None] * picked, axis=1)
    sh_gate = matrix_product(normed_ffn, sgate)
    sh_up = matrix_product(normed_ffn, sup)
    sh_silu, sh_slope = silu_parts(sh_gate)
    sh_act = (sh_silu * sh_up).astype(jnp.bfloat16)
    shared = matrix_product(sh_act, sdown)
    output = hidden + routed + shared
    d_shared = grad_out.astype(jnp.bfloat16)
    shared_down_gradient = inner(sh_act, d_shared)
    d_sh_act = outer_product(d_shared, sdown)
    d_sh_gate = (d_sh_act * sh_up * sh_slope).astype(jnp.bfloat16)
    d_sh_up = (d_sh_act * sh_silu).astype(jnp.bfloat16)
    shared_gate_gradient = inner(normed_ffn, d_sh_gate)
    shared_up_gradient = inner(normed_ffn, d_sh_up)
    d_normed_ffn = outer_product(d_sh_gate, sgate) + outer_product(d_sh_up, sup)
    d_picked = (
        (gates[:, :, None] * grad_out[:, None, :])
        .astype(jnp.bfloat16)
        .reshape(device_local * TOPK, MODEL_WIDTH)
    )
    d_gates = jnp.sum(picked * grad_out[:, None, :], axis=2)
    d_buffer = (
        jnp.zeros((experts * capacity, MODEL_WIDTH), jnp.bfloat16)
        .at[place]
        .set(d_picked)
        .reshape(experts, capacity, MODEL_WIDTH)
    )
    d_received = lax.all_to_all(
        spread(d_buffer), ("expert", "fsdp"), split_axis=0, concat_axis=0, tiled=True
    )
    d_rows = d_received.reshape(-1, MODEL_WIDTH)
    d_act = outer_product(d_rows, w_d)
    g_down = inner(ex_act, d_rows)
    d_pre_gate = (d_act * pre_up * slope).astype(jnp.bfloat16)
    d_pre_up = (d_act * act_gate).astype(jnp.bfloat16)
    g_gate = inner(ex_rows, d_pre_gate)
    g_up = inner(ex_rows, d_pre_up)
    d_ex_rows = (outer_product(d_pre_gate, w_g) + outer_product(d_pre_up, w_u)).reshape(
        received.shape
    )
    d_returned = lax.all_to_all(
        d_ex_rows.astype(jnp.bfloat16), ("expert", "fsdp"), split_axis=0, concat_axis=0, tiled=True
    ).astype(d_ex_rows.dtype)
    d_results = collect(d_returned)
    d_normed_ffn = d_normed_ffn + jnp.sum(
        d_results[place].reshape(device_local, TOPK, MODEL_WIDTH), axis=1
    )
    d_router = jnp.sum(chosen * d_gates[:, :, None], axis=1)
    d_logits = (router * (d_router - jnp.sum(router * d_router, axis=1, keepdims=True))).astype(
        jnp.bfloat16
    )
    router_weight_gradient = inner(normed_ffn, d_logits)
    d_normed_ffn = d_normed_ffn + outer_product(d_logits, wrout)
    d_hidden_norm, g_ffn_grad = norm_backward(hidden, inv_ffn, g_ffn, d_normed_ffn)
    d_hidden = grad_out + d_hidden_norm
    d_attn = d_hidden.astype(jnp.bfloat16)
    output_weight_gradient = inner(heads, d_attn)
    d_heads = (
        outer_product(d_attn, wout)
        .astype(jnp.bfloat16)
        .reshape(device_local, HEAD_COUNT, VALUE_UNITS)
    )
    value_weight_gradient = jnp.einsum(
        "thc,thv->chv", mixed_output, d_heads, preferred_element_type=jnp.float32
    )
    mixed_gradient = jnp.einsum(
        "thv,chv->thc", d_heads, value_part, preferred_element_type=jnp.float32
    )
    mixed_gradient = mixed_gradient.astype(jnp.bfloat16).reshape(token_rows, LATENT_WIDTH)
    delta = jnp.sum(mixed_gradient.astype(jnp.float32) * mixed_output_sum, axis=1)

    def back_step(index, carry):
        d_query_acc, d_keys_acc = carry
        scores, key_rows = scores_of(index)
        weight_arrays = jnp.exp(scores - log_total[:, None])
        weight_gradients = outer_product(mixed_gradient, key_rows[:, :LATENT_WIDTH])
        d_scores = (weight_arrays * (weight_gradients - delta[:, None]) * scale).astype(
            jnp.bfloat16
        )
        d_query_acc = d_query_acc + matrix_product(d_scores, key_rows)
        d_values = inner(weight_arrays.astype(jnp.bfloat16), mixed_gradient)
        d_block = inner(d_scores, query) + jnp.concatenate(
            [d_values, jnp.zeros((block, ROTARY_UNITS), jnp.float32)], axis=1
        )
        previous = lax.dynamic_slice_in_dim(d_keys_acc, index * block, block, 0)
        return (
            d_query_acc,
            lax.dynamic_update_slice_in_dim(d_keys_acc, previous + d_block, index * block, 0),
        )

    d_query, d_keys = lax.fori_loop(
        0,
        token_tally,
        back_step,
        (
            jnp.zeros((token_rows, feature_width), jnp.float32),
            jnp.zeros((seq_len, feature_width), jnp.float32),
        ),
    )
    key_gradient = lax.psum_scatter(
        d_keys.astype(jnp.bfloat16), "expert", scatter_dimension=0, tiled=True
    )
    query_up_gradient = d_query.astype(jnp.bfloat16).reshape(
        device_local, HEAD_COUNT, feature_width
    )
    query_latent_gradient = query_up_gradient[:, :, :LATENT_WIDTH]
    key_weight_gradient = jnp.einsum(
        "thc,thd->chd", query_latent_gradient, query_nope, preferred_element_type=jnp.float32
    )
    d_q_nope = jnp.einsum(
        "thc,chd->thd", query_latent_gradient, key_part, preferred_element_type=jnp.float32
    )
    d_q_rope = reverse_rotary(
        query_up_gradient[:, :, LATENT_WIDTH:].astype(jnp.float32),
        cosine_table[:, None, :],
        sine_table[:, None, :],
    )
    d_query_full = (
        jnp.concatenate([d_q_nope, d_q_rope], axis=-1)
        .astype(jnp.bfloat16)
        .reshape(device_local, HEAD_COUNT * (PLAIN_UNITS + ROTARY_UNITS))
    )
    query_weight_gradient = inner(normed_in, d_query_full)
    d_normed_in = outer_product(d_query_full, wq)
    latent_gradient = key_gradient[:, :LATENT_WIDTH].astype(jnp.float32)
    rotary_key_gradient = reverse_rotary(
        key_gradient[:, LATENT_WIDTH:].astype(jnp.float32), cosine_table, sine_table
    )
    d_compact, g_lat_grad = norm_backward(packed_rows, inv_lat, g_lat, latent_gradient)
    d_latent_full = jnp.concatenate([d_compact, rotary_key_gradient], axis=-1).astype(jnp.bfloat16)
    latent_weight_gradient = inner(normed_in, d_latent_full)
    d_normed_in = d_normed_in + outer_product(d_latent_full, wlat)
    d_norm_in, g_attn_grad = norm_backward(x_in, inv_attn, attention_gain_grad, d_normed_in)
    d_tokens = (d_hidden + d_norm_in).astype(jnp.bfloat16)
    expand_weight_gradient = jnp.concatenate(
        [key_weight_gradient, value_weight_gradient], axis=-1
    ).reshape(LATENT_WIDTH, HEAD_COUNT * (PLAIN_UNITS + VALUE_UNITS))
    r_sgate, r_sup, r_sdown = (
        lax.psum_scatter(shared_gate_gradient, ("expert", "fsdp"), scatter_dimension=0, tiled=True),
        lax.psum_scatter(shared_up_gradient, ("expert", "fsdp"), scatter_dimension=0, tiled=True),
        lax.psum_scatter(shared_down_gradient, ("expert", "fsdp"), scatter_dimension=0, tiled=True),
    )
    r_attn, r_query, r_latent, r_lgain, r_expand, r_out, r_fgain, r_router = (
        lax.psum_scatter(
            g_attn_grad.astype(jnp.bfloat16), "fsdp", scatter_dimension=0, tiled=True
        ).astype(jnp.float32),
        lax.psum_scatter(
            query_weight_gradient.astype(jnp.bfloat16), "fsdp", scatter_dimension=0, tiled=True
        ).astype(jnp.float32),
        lax.psum_scatter(
            latent_weight_gradient.astype(jnp.bfloat16), "fsdp", scatter_dimension=0, tiled=True
        ).astype(jnp.float32),
        lax.psum_scatter(
            g_lat_grad.astype(jnp.bfloat16), "fsdp", scatter_dimension=0, tiled=True
        ).astype(jnp.float32),
        lax.psum_scatter(
            expand_weight_gradient.astype(jnp.bfloat16), "fsdp", scatter_dimension=0, tiled=True
        ).astype(jnp.float32),
        lax.psum_scatter(
            output_weight_gradient.astype(jnp.bfloat16), "fsdp", scatter_dimension=0, tiled=True
        ).astype(jnp.float32),
        lax.psum_scatter(
            g_ffn_grad.astype(jnp.bfloat16), "fsdp", scatter_dimension=0, tiled=True
        ).astype(jnp.float32),
        lax.psum_scatter(
            router_weight_gradient.astype(jnp.bfloat16), "fsdp", scatter_dimension=0, tiled=True
        ).astype(jnp.float32),
    )
    r_attn, r_query, r_latent, r_lgain, r_expand, r_out, r_fgain, r_router = (
        lax.psum(r_attn.astype(jnp.bfloat16), "expert").astype(jnp.float32),
        lax.psum(r_query.astype(jnp.bfloat16), "expert").astype(jnp.float32),
        lax.psum(r_latent.astype(jnp.bfloat16), "expert").astype(jnp.float32),
        lax.psum(r_lgain.astype(jnp.bfloat16), "expert").astype(jnp.float32),
        lax.psum(r_expand.astype(jnp.bfloat16), "expert").astype(jnp.float32),
        lax.psum(r_out.astype(jnp.bfloat16), "expert").astype(jnp.float32),
        lax.psum(r_fgain.astype(jnp.bfloat16), "expert").astype(jnp.float32),
        lax.psum(r_router.astype(jnp.bfloat16), "expert").astype(jnp.float32),
    )
    return (
        output.astype(jnp.bfloat16)[None],
        d_tokens[None],
        r_attn,
        r_query,
        r_latent,
        r_lgain,
        r_expand,
        r_out,
        r_fgain,
        r_router,
        r_sgate,
        r_sup,
        r_sdown,
        g_gate[None],
        g_up[None],
        g_down[None],
    )


LINE = 4
SQUARE = 2
CORES = 2
MESH = pl.DeviceIdType.MESH
VMEM_LIMIT = 56 * 1024 * 1024


class Place:
    def __init__(self):
        index = lax.axis_index("expert")
        self.y = lax.axis_index("fsdp")
        self.c = lax.rem(index, CORES)
        self.b = lax.rem(lax.div(index, CORES), SQUARE)
        self.a = lax.div(index, CORES * SQUARE)

    def device(self, da=0, db=0, dc=0, dy=0):
        b = 1 - self.b if db else self.b
        c = 1 - self.c if dc else self.c
        y = 1 - self.y if dy else self.y
        return (((self.a + da) * SQUARE + b) * CORES + c, y)

    def block(self, full, a, db=0, dc=0, dy=0):
        b = 1 - self.b if db else self.b
        c = 1 - self.c if dc else self.c
        y = 1 - self.y if dy else self.y
        flat = (a * SQUARE + b) * CORES + c
        return y * (LINE * SQUARE * CORES) + flat if full else flat

    def greet(self, with_y):
        barrier = pltpu.get_barrier_semaphore()
        near = [dict(db=1), dict(dc=1)] + ([dict(dy=1)] if with_y else [])
        for step in near:
            pl.semaphore_signal(barrier, inc=1, device_id=self.device(**step), device_id_type=MESH)

        @pl.when(self.a > 0)
        def _():
            pl.semaphore_signal(barrier, inc=1, device_id=self.device(da=-1), device_id_type=MESH)

        @pl.when(self.a < LINE - 1)
        def _():
            pl.semaphore_signal(barrier, inc=1, device_id=self.device(da=1), device_id_type=MESH)

        ends = jnp.logical_or(self.a == 0, self.a == LINE - 1).astype(jnp.int32)
        pl.semaphore_wait(barrier, len(near) + 2 - ends)


class Sender:
    def __init__(self, place, sems):
        self.place, self.sems, self.pending = place, sems, []

    def send(self, src, dst, recv_sem, step, cond=None):
        sem = self.sems.at[len(self.pending)]

        def make():
            return pltpu.make_async_remote_copy(
                src_ref=src,
                dst_ref=dst,
                send_sem=sem,
                recv_sem=recv_sem,
                device_id=self.place.device(**step),
                device_id_type=MESH,
            )

        def start():
            make().start()

        guarded(cond, start)
        self.pending.append((cond, lambda: make().wait_send()))

    def arrived(self, dst, recv_sem):
        pltpu.make_async_remote_copy(
            src_ref=dst,
            dst_ref=dst,
            send_sem=self.sems.at[0],
            recv_sem=recv_sem,
            device_id=self.place.device(dc=1),
            device_id_type=MESH,
        ).wait_recv()

    def finish(self):
        for cond, wait in self.pending:
            guarded(cond, wait)


def guarded(cond, action):
    if cond is None:
        action()
    else:
        pl.when(cond)(action)


def both(first, second):
    if first is None or second is None:
        return second if first is None else first
    return jnp.logical_and(first, second)


def gather_kernel(full, count, pairs, gated, *refs):
    ins, outs = refs[: count + pairs], refs[count + pairs : 2 * (count + pairs)]
    local_sems, send_sems, recv_sems, pair_sems = refs[2 * (count + pairs) :]
    place = Place()
    a = place.a
    sender = Sender(place, send_sems)
    place.greet(full or pairs > 0)
    for at in range(count, count + pairs):
        sender.send(ins[at], outs[at], pair_sems.at[at - count], dict(dy=1))
    own = place.block(full, a)
    for at in range(count):
        pltpu.make_async_copy(ins[at], outs[at].at[own], local_sems.at[at]).start()

    def chunk(at, block, half):
        size = ins[at].shape[0] // 2
        return outs[at].at[block, pl.ds(half * size, size)]

    def sem_of(at, block, half):
        return recv_sems.at[at, block * 2 + half]

    def forward(at, block, half, src, step, cond=None):
        sender.send(src, chunk(at, block, half), sem_of(at, block, half), step, cond)

    def receive(at, block, half, cond):
        guarded(cond, lambda: sender.arrived(chunk(at, block, half), sem_of(at, block, half)))

    def held_by(at, delta, cond):
        if at not in gated:
            return cond
        return both(cond, lax.div(a + delta, LINE // 2) == place.y)

    def from_line(delta, always):
        block = place.block(full, a + delta)
        for half in range(2):
            for at in range(count):
                cond = held_by(at, delta, always)
                size = ins[at].shape[0] // 2
                if delta == 0:
                    src = ins[at].at[pl.ds(half * size, size)]
                else:
                    receive(at, block, half, cond)
                    src = chunk(at, block, half)
                if delta <= 0:
                    forward(at, block, half, src, dict(da=1), both(cond, a < LINE - 1))
                if delta >= 0:
                    forward(at, block, half, src, dict(da=-1), both(cond, a > 0))
                forward(at, block, half, src, dict(db=1), cond)
                if full:
                    forward(at, block, half, src, dict(dy=1), cond)
                forward(at, block, half, src, dict(dc=1), cond)

    def from_side(delta, always):
        for half in range(2):
            for at in range(count):
                cond = held_by(at, delta, always)
                block = place.block(full, a + delta, db=1)
                receive(at, block, half, cond)
                if full and half == 0:
                    forward(at, block, half, chunk(at, block, half), dict(dy=1), cond)
                forward(at, block, half, chunk(at, block, half), dict(dc=1), cond)
                if full:
                    block = place.block(full, a + delta, dy=1)
                    receive(at, block, half, cond)
                    if half == 1:
                        forward(at, block, half, chunk(at, block, half), dict(db=1), cond)
                    forward(at, block, half, chunk(at, block, half), dict(dc=1), cond)

    def from_corner(delta, always):
        for half in range(2):
            for at in range(count):
                cond = held_by(at, delta, always)
                block = place.block(full, a + delta, db=1, dy=1)
                receive(at, block, half, cond)
                forward(at, block, half, chunk(at, block, half), dict(dc=1), cond)

    def from_sibling(delta, always):
        for half in range(2):
            for at in range(count):
                cond = held_by(at, delta, always)
                for db in range(2):
                    for dy in range(2 if full else 1):
                        receive(at, place.block(full, a + delta, db=db, dc=1, dy=dy), half, cond)

    rounds = [[(0, None)]]
    for s in range(1, LINE):
        rounds.append([(-s, a >= s), (s, a + s < LINE)])
    stages = [from_line, from_side] + ([from_corner] if full else []) + [from_sibling]
    for tick in range(len(rounds) + len(stages) - 1):
        for level, stage in enumerate(stages):
            if 0 <= tick - level < len(rounds):
                for delta, cond in rounds[tick - level]:
                    stage(delta, cond)
    for at in range(count, count + pairs):
        sender.arrived(outs[at], pair_sems.at[at - count])
    for at in range(count):
        pltpu.make_async_copy(ins[at], outs[at].at[own], local_sems.at[at]).wait()
    sender.finish()


def gather_rows(arrays, full, collective_id, swapped=(), gated=()):
    blocks = LINE * SQUARE * CORES * (SQUARE if full else 1)
    count, pairs = len(arrays), len(swapped)
    lines = 2 * LINE - 1
    sends = pairs + count * lines * 2 * (9 if full else 5)
    moved = sum(blocks * 2 * x.size * x.dtype.itemsize for x in arrays)
    return pl.pallas_call(
        functools.partial(gather_kernel, full, count, pairs, gated),
        out_shape=[jax.ShapeDtypeStruct((blocks,) + x.shape, x.dtype) for x in arrays]
        + [jax.ShapeDtypeStruct(x.shape, x.dtype) for x in swapped],
        in_specs=[pl.BlockSpec(memory_space=pl.ANY)] * (count + pairs),
        out_specs=[pl.BlockSpec(memory_space=pl.ANY)] * (count + pairs),
        scratch_shapes=[
            pltpu.SemaphoreType.DMA((count,)),
            pltpu.SemaphoreType.DMA((sends,)),
            pltpu.SemaphoreType.DMA((count, blocks * 2)),
            pltpu.SemaphoreType.DMA((max(pairs, 1),)),
        ],
        compiler_params=pltpu.CompilerParams(collective_id=collective_id, has_side_effects=True),
        cost_estimate=pl.CostEstimate(flops=0, bytes_accessed=6 * moved, transcendentals=0),
    )(*arrays, *swapped)


def add_rows(target, sources, size):
    def step(at, carry):
        rows = pl.ds(pl.multiple_of(at * 16, 16), 16)
        total = sources[0][rows, :].astype(jnp.float32)
        for source in sources[1:]:
            total = total + source[rows, :].astype(jnp.float32)
        target[rows, :] = total.astype(target.dtype)
        return carry

    lax.fori_loop(0, size // 16, step, 0)


def scatter_kernel(full, pairs, part, *refs):
    ins, out, outs = refs[:pairs], refs[pairs], refs[pairs + 1 : 2 * pairs + 1]
    mine, got, side, up, down, load_sems, send_sems, recv_sems, pair_sems = refs[2 * pairs + 1 :]
    place = Place()
    a = place.a
    kinds = 4 if full else 2
    size = part.shape[1]
    half = size // 2
    sender = Sender(place, send_sems)
    place.greet(full or pairs > 0)
    for at in range(pairs):
        sender.send(ins[at], outs[at], pair_sems.at[at], dict(dy=1))
    order = [LINE - 1, 0, LINE - 2, 1]
    walk = (3, 1, 2, 0) if full else (1, 0)

    def sem_of(group, target, kind):
        return recv_sems.at[group, target * 4 + kind]

    def load(target, kind):
        block = place.block(full, target, db=kind % 2, dy=kind // 2)
        return pltpu.make_async_copy(
            part.at[block], mine.at[target, kind], load_sems.at[target * 4 + kind]
        )

    for target in order:
        for kind in walk:
            load(target, kind).start()
            block = place.block(full, target, db=kind % 2, dc=1, dy=kind // 2)
            sender.send(
                part.at[block], got.at[target, kind], sem_of(0, target, kind), dict(dc=1)
            )

    def rows_of(ref, which):
        return ref.at[pl.ds(which * half, half)]

    def over_cores(target):
        for kind in walk:
            load(target, kind).wait()
            sender.arrived(got.at[target, kind], sem_of(0, target, kind))
            add_rows(mine.at[target, kind], [mine.at[target, kind], got.at[target, kind]], size)
            held = mine.at[target, kind]
            if kind == 3:
                sender.send(rows_of(held, 0), side.at[target, 4], sem_of(1, target, 0), dict(db=1))
                sender.send(rows_of(held, 1), side.at[target, 5], sem_of(1, target, 1), dict(dy=1))
            if kind == 1:
                sender.send(rows_of(held, 0), side.at[target, 0], sem_of(2, target, 0), dict(db=1))
                if not full:
                    sender.send(
                        rows_of(held, 1), side.at[target, 1], sem_of(2, target, 1), dict(db=1)
                    )
            if kind == 2:
                sender.send(rows_of(held, 1), side.at[target, 3], sem_of(2, target, 3), dict(dy=1))

    def over_corner(target):
        sender.arrived(side.at[target, 4], sem_of(1, target, 0))
        held = rows_of(mine.at[target, 2], 0)
        add_rows(held, [held, side.at[target, 4]], half)
        sender.send(held, side.at[target, 2], sem_of(2, target, 2), dict(dy=1))
        sender.arrived(side.at[target, 5], sem_of(1, target, 1))
        held = rows_of(mine.at[target, 1], 1)
        add_rows(held, [held, side.at[target, 5]], half)
        sender.send(held, side.at[target, 1], sem_of(2, target, 1), dict(db=1))

    def over_line(target):
        for which in range(2):
            held = rows_of(mine.at[target, 0], which)
            parts = [held]
            for source in (0, 2) if full else (0,):
                sender.arrived(side.at[target, source + which], sem_of(2, target, source + which))
                parts.append(side.at[target, source + which])
            below, above = rows_of(up.at[target], which), rows_of(down.at[target], which)
            below_sem, above_sem = sem_of(3, target, which), sem_of(3, target, 2 + which)

            def upward(with_below):
                extra = []
                if with_below:
                    sender.arrived(below, below_sem)
                    extra = [below]
                add_rows(held, parts + extra, half)

            def downward(with_above):
                extra = []
                if with_above:
                    sender.arrived(above, above_sem)
                    extra = [above]
                add_rows(held, parts + extra, half)

            if target > 0:
                pl.when(jnp.logical_and(a < target, a > 0))(lambda: upward(True))
                pl.when(a == 0)(lambda: upward(False))
                sender.send(held, below, below_sem, dict(da=1), a < target)
            if target < LINE - 1:
                pl.when(jnp.logical_and(a > target, a < LINE - 1))(lambda: downward(True))
                pl.when(a == LINE - 1)(lambda: downward(False))
                sender.send(held, above, above_sem, dict(da=-1), a > target)

            def last():
                extra = []
                if target > 0:
                    sender.arrived(below, below_sem)
                    extra.append(below)
                if target < LINE - 1:
                    sender.arrived(above, above_sem)
                    extra.append(above)
                add_rows(rows_of(out, which), parts + extra, half)

            pl.when(a == target)(last)

    stages = [over_cores] + ([over_corner] if full else []) + [over_line]
    for tick in range(len(order) + len(stages) - 1):
        for level, stage in enumerate(stages):
            if 0 <= tick - level < len(order):
                stage(order[tick - level])
    for at in range(pairs):
        sender.arrived(outs[at], pair_sems.at[at])
    sender.finish()


def scatter_rows(part, full, collective_id, swapped=()):
    blocks, rows, width = part.shape
    kinds = 4 if full else 2
    half = rows // 2
    pairs = len(swapped)
    return pl.pallas_call(
        functools.partial(scatter_kernel, full, pairs),
        out_shape=[jax.ShapeDtypeStruct((rows, width), jnp.float32)]
        + [jax.ShapeDtypeStruct(x.shape, x.dtype) for x in swapped],
        in_specs=[pl.BlockSpec(memory_space=pl.ANY)] * (1 + pairs),
        out_specs=[pl.BlockSpec(memory_space=pltpu.VMEM)]
        + [pl.BlockSpec(memory_space=pl.ANY)] * pairs,
        scratch_shapes=[
            pltpu.VMEM((LINE, kinds, rows, width), part.dtype),
            pltpu.VMEM((LINE, kinds, rows, width), part.dtype),
            pltpu.VMEM((LINE, 6, half, width), part.dtype),
            pltpu.VMEM((LINE, rows, width), part.dtype),
            pltpu.VMEM((LINE, rows, width), part.dtype),
            pltpu.SemaphoreType.DMA((LINE * 4,)),
            pltpu.SemaphoreType.DMA((pairs + LINE * (4 + 6 + 4),)),
            pltpu.SemaphoreType.DMA((4, LINE * 4)),
            pltpu.SemaphoreType.DMA((max(pairs, 1),)),
        ],
        compiler_params=pltpu.CompilerParams(
            collective_id=collective_id, has_side_effects=True, vmem_limit_bytes=VMEM_LIMIT
        ),
        cost_estimate=pl.CostEstimate(
            flops=0, bytes_accessed=12 * part.size * part.dtype.itemsize, transcendentals=0
        ),
    )(part, *swapped)


def token_gather(rows):
    return lax.all_gather(rows, ("fsdp", "expert"), axis=0, tiled=True)


def token_scatter(partial):
    return lax.psum_scatter(
        partial, ("fsdp", "expert"), scatter_dimension=0, tiled=True
    ).astype(jnp.float32)


def split_body(
    tokens,
    routes,
    cotangent,
    attn_gain,
    w_query,
    latent_weight,
    latent_norm_gain,
    expand_weight,
    w_out,
    ffn_gain,
    w_router,
    shared_gate,
    shared_up,
    shared_down,
    expert_gate,
    expert_up,
    expert_down,
):
    rows = tokens.shape[1]
    experts = lax.axis_size("expert")
    shards = lax.axis_size("fsdp")
    position = lax.axis_index("expert")
    blocks = experts * shards
    seq_len = rows * experts
    capacity = shards * ((rows * TOPK * 4 + experts * 3 * shards - 1) // (experts * 3 * shards))
    head_units = PLAIN_UNITS + ROTARY_UNITS
    pair_units = PLAIN_UNITS + VALUE_UNITS
    feature_width = LATENT_WIDTH + ROTARY_UNITS
    scale = head_units ** (-0.5)

    shard = lax.axis_index("fsdp")
    first = shard == 0

    query_cols = lax.dynamic_slice_in_dim(w_query, position * head_units, head_units, 1)
    expand_cols = lax.dynamic_slice_in_dim(expand_weight, position * pair_units, pair_units, 1)
    owners = experts // shards
    out_rows = lax.dynamic_slice_in_dim(
        w_out, lax.rem(position, owners) * VALUE_UNITS, VALUE_UNITS, 0
    )
    packed = jnp.concatenate(
        [latent_weight, query_cols, w_router, attn_gain[:, None], ffn_gain[:, None]], axis=1
    )
    small = jnp.concatenate([expand_cols, latent_norm_gain[:, None]], axis=1)
    seq_rows, other_packed, other_small, other_out = gather_rows(
        [tokens[0]], False, 0, swapped=[packed, small, out_rows]
    )

    def whole(own, other):
        return jnp.concatenate([jnp.where(first, own, other), jnp.where(first, other, own)], axis=0)

    packed = whole(packed, other_packed)
    small = whole(small, other_small)
    out_head = jnp.where(lax.div(position, owners) == shard, out_rows, other_out)
    w_front = packed[:, : feature_width + head_units]
    w_latent = packed[:, :feature_width]
    at = feature_width + head_units
    w_query_head = packed[:, feature_width:at]
    wrout = packed[:, at : at + experts]
    g_attn = packed[:, at + experts].astype(jnp.float32)
    g_ffn = packed[:, at + experts + 1].astype(jnp.float32)
    expand_head = small[:, :pair_units]
    g_lat = small[:, pair_units].astype(jnp.float32)
    units = shared_down.shape[0]

    def to_columns(weight):
        parts = weight.reshape(weight.shape[0], blocks, units).transpose(1, 0, 2)
        return lax.all_to_all(
            parts, ("expert", "fsdp"), split_axis=0, concat_axis=0, tiled=True
        ).reshape(-1, units)

    sh_cols = to_columns(jnp.concatenate([shared_gate, shared_up], axis=0)).reshape(
        blocks, 2, shared_gate.shape[0], units
    )
    sgate = sh_cols[:, 0].reshape(-1, units)
    sup = sh_cols[:, 1].reshape(-1, units)

    grad_rows = cotangent[0]
    grad_out = grad_rows.astype(jnp.float32)
    all_routes = token_gather(routes[0])
    all_grads = token_gather(grad_rows)

    x_in = tokens[0].astype(jnp.float32)
    normed, inv_attn = norm_forward(x_in, g_attn)
    normed_in = normed.astype(jnp.bfloat16)
    seq_normed, _ = norm_forward(
        seq_rows.reshape(seq_len, MODEL_WIDTH).astype(jnp.float32), g_attn
    )
    seq_normed = seq_normed.astype(jnp.bfloat16)
    cosine_table, sine_table = rope_tables(jnp.arange(seq_len, dtype=jnp.int32))
    front = matrix_product(seq_normed, w_front)
    latent_rows, _ = norm_forward(front[:, :LATENT_WIDTH], g_lat)
    latent_rows = latent_rows.astype(jnp.bfloat16)
    key_rope = apply_rotary(front[:, LATENT_WIDTH:feature_width], cosine_table, sine_table)
    query_full = front[:, feature_width:]
    query_rope = apply_rotary(query_full[:, PLAIN_UNITS:], cosine_table, sine_table)
    query = jnp.concatenate([query_full[:, :PLAIN_UNITS], query_rope], axis=1).astype(jnp.bfloat16)
    pairs = matrix_product(latent_rows, expand_head)
    key = jnp.concatenate([pairs[:, :PLAIN_UNITS], key_rope], axis=1).astype(jnp.bfloat16)
    value = pairs[:, PLAIN_UNITS:].astype(jnp.bfloat16)
    order = jnp.arange(seq_len, dtype=jnp.int32)
    scores = jnp.where(
        order[None, :] <= order[:, None], outer_product(query, key) * scale, -1e30
    )
    top = jnp.max(scores, axis=1, keepdims=True)
    exps = jnp.exp(scores - top)
    probs = exps / jnp.sum(exps, axis=1, keepdims=True)
    low_probs = probs.astype(jnp.bfloat16)
    head_sum = matrix_product(low_probs, value)
    head_rows = head_sum.astype(jnp.bfloat16)
    head_part = matrix_product(head_rows, out_head).astype(jnp.bfloat16)
    (mixed_rows,) = scatter_rows(head_part.reshape(experts, rows, MODEL_WIDTH), False, 1)
    hidden = x_in + mixed_rows
    normed2, inv_ffn = norm_forward(hidden, g_ffn)
    normed_ffn = normed2.astype(jnp.bfloat16)
    router = jax.nn.softmax(matrix_product(normed_ffn, wrout), axis=-1)

    (all_normed,) = gather_rows([normed_ffn], True, 2)
    all_normed = all_normed.reshape(blocks * rows, MODEL_WIDTH)
    mix = matrix_product(all_normed, jnp.concatenate([sgate, sup, wrout], axis=1))
    sh_gate = mix[:, :units]
    sh_up = mix[:, units : 2 * units]
    all_router = jax.nn.softmax(mix[:, 2 * units :], axis=-1)
    names = jnp.arange(experts, dtype=jnp.int32)
    own_gate = jnp.sum(jnp.where(names[None, :] == position, all_router, 0.0), axis=1)
    hit = jnp.any(all_routes == position, axis=1).reshape(blocks, rows)
    count = hit.astype(jnp.int32)
    slot = jnp.cumsum(count, axis=1) - count
    place = jnp.where(hit, slot, -1)
    onehot = place[:, None, :] == jnp.arange(capacity, dtype=jnp.int32)[None, :, None]
    pick = onehot.astype(jnp.bfloat16)
    gate_slot = jnp.sum(
        jnp.where(onehot, own_gate.reshape(blocks, 1, rows), 0.0), axis=2
    ).reshape(-1, 1)

    def take(whole):
        return jnp.einsum(
            "bst,btd->bsd", pick, whole.reshape(blocks, rows, -1),
            preferred_element_type=jnp.bfloat16,
        ).reshape(blocks * capacity, -1)

    def put_back(slots):
        return jnp.einsum(
            "bst,bsd->btd", pick, slots.astype(jnp.bfloat16).reshape(blocks, capacity, -1),
            preferred_element_type=jnp.float32,
        ).reshape(blocks * rows, -1)

    w_g, w_u, w_d = (expert_gate[0], expert_up[0], expert_down[0])
    ex_rows = take(all_normed)
    ex_grads = take(all_grads)
    pre_gate = matrix_product(ex_rows, w_g)
    pre_up = matrix_product(ex_rows, w_u)
    act_gate, slope = silu_parts(pre_gate)
    ex_act = act_gate * pre_up
    scaled_act = (gate_slot * ex_act).astype(jnp.bfloat16)
    back_act = outer_product(ex_grads, w_d)
    d_gate_slot = jnp.sum(ex_act * back_act, axis=1)
    d_act = gate_slot * back_act
    d_pre_gate = (d_act * pre_up * slope).astype(jnp.bfloat16)
    d_pre_up = (d_act * act_gate).astype(jnp.bfloat16)
    g_down = inner(scaled_act, ex_grads)
    g_gate = inner(ex_rows, d_pre_gate)
    g_up = inner(ex_rows, d_pre_up)
    ex_out = matrix_product(scaled_act, w_d)
    d_ex_rows = outer_product(d_pre_gate, w_g) + outer_product(d_pre_up, w_u)

    sh_silu, sh_slope = silu_parts(sh_gate)
    sh_act = (sh_silu * sh_up).astype(jnp.bfloat16)
    d_sh_act = outer_product(all_grads, shared_down)
    d_sh_gate = (d_sh_act * sh_up * sh_slope).astype(jnp.bfloat16)
    d_sh_up = (d_sh_act * sh_silu).astype(jnp.bfloat16)
    g_sdown = inner(sh_act, all_grads)
    g_sgate = inner(all_normed, d_sh_gate)
    g_sup = inner(all_normed, d_sh_up)

    out_part = put_back(ex_out) + matrix_product(sh_act, shared_down)
    d_part = put_back(d_ex_rows) + outer_product(d_sh_gate, sgate) + outer_product(d_sh_up, sup)
    d_gate_rows = jnp.sum(
        jnp.where(onehot, d_gate_slot.reshape(blocks, capacity, 1), 0.0), axis=1
    ).reshape(-1, 1)
    d_gate_cols = jnp.where(
        jnp.arange(128, dtype=jnp.int32)[None, :] == position, d_gate_rows, 0.0
    )
    d_part = jnp.concatenate(
        [d_part.astype(jnp.bfloat16), d_gate_cols.astype(jnp.bfloat16)], axis=1
    )
    (d_back,) = scatter_rows(d_part.reshape(blocks, rows, -1), True, 3)
    d_normed_ffn = d_back[:, :MODEL_WIDTH]
    d_router = d_back[:, MODEL_WIDTH : MODEL_WIDTH + experts]
    output = hidden + token_scatter(out_part.astype(jnp.bfloat16))

    d_logits = (router * (d_router - jnp.sum(router * d_router, axis=1, keepdims=True))).astype(
        jnp.bfloat16
    )
    g_router = inner(normed_ffn, d_logits)
    d_normed_ffn = d_normed_ffn + outer_product(d_logits, wrout)
    d_hidden_norm, g_ffn_grad = norm_backward(hidden, inv_ffn, g_ffn, d_normed_ffn)
    d_hidden = grad_out + d_hidden_norm
    d_attn = d_hidden.astype(jnp.bfloat16)

    (seq_d_attn,) = gather_rows([d_attn], False, 4)
    seq_d_attn = seq_d_attn.reshape(seq_len, MODEL_WIDTH)
    d_head = outer_product(seq_d_attn, out_head).astype(jnp.bfloat16)
    g_out_head = inner(head_rows, seq_d_attn)
    delta = jnp.sum(d_head.astype(jnp.float32) * head_sum, axis=1, keepdims=True)
    d_scores = (probs * (outer_product(d_head, value) - delta) * scale).astype(jnp.bfloat16)
    d_query = matrix_product(d_scores, key)
    d_key = inner(d_scores, query)
    d_value = inner(low_probs, d_head).astype(jnp.bfloat16)
    d_key_plain = d_key[:, :PLAIN_UNITS].astype(jnp.bfloat16)
    d_pairs = jnp.concatenate([d_key_plain, d_value], axis=1)
    g_expand_head = inner(latent_rows, d_pairs)
    d_keys = jnp.concatenate(
        [outer_product(d_pairs, expand_head), d_key[:, PLAIN_UNITS:]], axis=1
    )
    d_query_full = jnp.concatenate(
        [
            d_query[:, :PLAIN_UNITS],
            reverse_rotary(d_query[:, PLAIN_UNITS:], cosine_table, sine_table),
        ],
        axis=1,
    ).astype(jnp.bfloat16)
    g_query_head = inner(d_query_full, seq_normed).astype(jnp.bfloat16)
    g_expand_head = g_expand_head.astype(jnp.bfloat16)
    g_out_head = g_out_head.astype(jnp.bfloat16)

    def half_of(whole, which, axis):
        size = whole.shape[axis] // shards
        return lax.dynamic_slice_in_dim(whole, which * size, size, axis)

    d_part_in = outer_product(d_query_full, w_query_head)
    d_part_in = jnp.concatenate(
        [d_part_in, d_keys, jnp.zeros((seq_len, ROTARY_UNITS), jnp.float32)], axis=1
    ).astype(jnp.bfloat16)
    d_sums, other_query, other_expand, other_out_grad = scatter_rows(
        d_part_in.reshape(experts, rows, -1),
        False,
        5,
        swapped=[
            half_of(g_query_head, 1 - shard, 1),
            half_of(g_expand_head, 1 - shard, 0),
            g_out_head,
        ],
    )
    d_normed_in = d_sums[:, :MODEL_WIDTH]
    key_gradient = d_sums[:, MODEL_WIDTH : MODEL_WIDTH + feature_width]

    def summed(own, other):
        return (own.astype(jnp.float32) + other.astype(jnp.float32)).astype(jnp.bfloat16)

    own_query = summed(half_of(g_query_head, shard, 1), other_query)
    own_expand = summed(half_of(g_expand_head, shard, 0), other_expand)
    own_out = summed(g_out_head, other_out_grad)
    own_latent = lax.dynamic_slice_in_dim(front[:, :LATENT_WIDTH], position * rows, rows, 0)
    own_cosine = lax.dynamic_slice_in_dim(cosine_table, position * rows, rows, 0)
    own_sine = lax.dynamic_slice_in_dim(sine_table, position * rows, rows, 0)
    inv_lat = lax.rsqrt(jnp.mean(own_latent * own_latent, axis=-1, keepdims=True) + EPS)
    d_compact, g_lat_grad = norm_backward(
        own_latent, inv_lat, g_lat, key_gradient[:, :LATENT_WIDTH]
    )
    d_rope = reverse_rotary(key_gradient[:, LATENT_WIDTH:], own_cosine, own_sine)
    d_latent_full = jnp.concatenate([d_compact, d_rope], axis=-1).astype(jnp.bfloat16)
    g_latent = inner(normed_in, d_latent_full)
    d_normed_in = d_normed_in + outer_product(d_latent_full, w_latent)
    d_norm_in, g_attn_grad = norm_backward(x_in, inv_attn, g_attn, d_normed_in)
    d_tokens = (d_hidden + d_norm_in).astype(jnp.bfloat16)

    def to_rows(cols):
        back = lax.all_to_all(
            cols.astype(jnp.bfloat16).reshape(blocks, -1, units),
            ("expert", "fsdp"),
            split_axis=0,
            concat_axis=0,
            tiled=True,
        )
        return back.transpose(1, 0, 2).reshape(-1, blocks * units).astype(jnp.float32)

    half = MODEL_WIDTH // blocks
    both = to_rows(
        jnp.stack(
            [g_sgate.reshape(blocks, half, units), g_sup.reshape(blocks, half, units)], axis=1
        )
    )
    r_sgate, r_sup = (both[:half], both[half:])
    lat_rows = jnp.zeros((shards, MODEL_WIDTH // shards), jnp.float32)
    lat_rows = lat_rows.at[:, : LATENT_WIDTH // shards].set(g_lat_grad.reshape(shards, -1))
    columns = jnp.concatenate(
        [
            g_latent,
            g_router,
            g_attn_grad[:, None],
            g_ffn_grad[:, None],
            lat_rows.reshape(MODEL_WIDTH, 1),
        ],
        axis=1,
    )
    used = columns.shape[1]
    columns = jnp.pad(columns.astype(jnp.bfloat16), ((0, 0), (0, -used % 128)))
    (columns,) = scatter_rows(columns.reshape(blocks, half, -1), True, 6)
    r_query, r_expand, columns, r_out = gather_rows(
        [own_query, own_expand, columns.astype(jnp.bfloat16), own_out], False, 7, gated=(3,)
    )
    r_query = r_query.reshape(experts * head_units, -1).astype(jnp.float32).T
    r_expand = r_expand.transpose(1, 0, 2).reshape(-1, experts * pair_units)
    r_out = lax.dynamic_slice_in_dim(r_out, shard * owners, owners, 0)
    columns = columns.reshape(MODEL_WIDTH // shards, -1).astype(jnp.float32)
    at = feature_width + experts
    return (
        output.astype(jnp.bfloat16)[None],
        d_tokens[None],
        columns[:, at],
        r_query,
        columns[:, :feature_width],
        columns[: LATENT_WIDTH // shards, at + 2],
        r_expand.astype(jnp.float32),
        r_out.reshape(-1, MODEL_WIDTH).astype(jnp.float32),
        columns[:, at + 1],
        columns[:, feature_width:at],
        r_sgate,
        r_sup,
        g_sdown,
        g_gate[None],
        g_up[None],
        g_down[None],
    )


def solution(mesh):
    shape = (mesh.shape["expert"], mesh.shape["fsdp"])
    split = shape == (LINE * SQUARE * CORES, SQUARE) and shape[0] == HEAD_COUNT
    return jax.shard_map(
        split_body if split else body,
        mesh=mesh,
        in_specs=(
            P("fsdp", "expert", None),
            P("fsdp", "expert", None),
            P("fsdp", "expert", None),
            P("fsdp"),
            P("fsdp", None),
            P("fsdp", None),
            P("fsdp"),
            P("fsdp", None),
            P("fsdp", None),
            P("fsdp"),
            P("fsdp", None),
            P(("expert", "fsdp"), None),
            P(("expert", "fsdp"), None),
            P(("expert", "fsdp"), None),
            P("expert", None, "fsdp"),
            P("expert", None, "fsdp"),
            P("expert", "fsdp", None),
        ),
        out_specs=(
            P("fsdp", "expert", None),
            P("fsdp", "expert", None),
            P("fsdp"),
            P("fsdp", None),
            P("fsdp", None),
            P("fsdp"),
            P("fsdp", None),
            P("fsdp", None),
            P("fsdp"),
            P("fsdp", None),
            P(("expert", "fsdp"), None),
            P(("expert", "fsdp"), None),
            P(("expert", "fsdp"), None),
            P("expert", None, "fsdp"),
            P("expert", None, "fsdp"),
            P("expert", "fsdp", None),
        ),
        check_vma=False,
    )
```

```python
import functools

import jax
import jax.numpy as jnp
from jax import lax
from jax.experimental import pallas as pl
from jax.experimental.pallas import tpu as pltpu
from jax.sharding import PartitionSpec as P

MODEL_WIDTH = 2048
HEAD_COUNT = 16
PLAIN_UNITS = 128
ROTARY_UNITS = 64
VALUE_UNITS = 128
LATENT_WIDTH = 512
TOPK = 6


EPS = 1e-06


def matrix_product(left, right):
    return jnp.dot(left, right, preferred_element_type=jnp.float32)


def inner(left, right):
    return lax.dot_general(
        left, right, (((0,), (0,)), ((), ())), preferred_element_type=jnp.float32
    )


def outer_product(left, right):
    return lax.dot_general(
        left, right, (((1,), (1,)), ((), ())), preferred_element_type=jnp.float32
    )


def norm_forward(value, gain):
    inverse = lax.rsqrt(jnp.mean(value * value, axis=-1, keepdims=True) + EPS)
    return (value * inverse * gain, inverse)


def norm_backward(value, inverse, gain, grad):
    unit = value * inverse
    scaled = grad * gain
    d_value = inverse * (scaled - unit * jnp.mean(scaled * unit, axis=-1, keepdims=True))
    return (d_value, jnp.sum(grad * unit, axis=0))


def rope_tables(positions):
    half = ROTARY_UNITS // 2
    freqs = 10000.0 ** (-jnp.arange(half, dtype=jnp.float32) * (2.0 / ROTARY_UNITS))
    angles = positions.astype(jnp.float32)[:, None] * freqs[None, :]
    return (jnp.cos(angles), jnp.sin(angles))


def apply_rotary(value, cosine_table, sine_table):
    half = ROTARY_UNITS // 2
    first = value[..., :half]
    second = value[..., half:]
    return jnp.concatenate(
        [first * cosine_table - second * sine_table, first * sine_table + second * cosine_table],
        axis=-1,
    )


def reverse_rotary(grad, cosine_table, sine_table):
    half = ROTARY_UNITS // 2
    first = grad[..., :half]
    second = grad[..., half:]
    return jnp.concatenate(
        [first * cosine_table + second * sine_table, second * cosine_table - first * sine_table],
        axis=-1,
    )


def silu_parts(value):
    sigma = jax.nn.sigmoid(value)
    return (value * sigma, sigma * (1.0 + value * (1.0 - sigma)))


def body(
    tokens,
    routes,
    cotangent,
    attn_gain,
    w_query,
    latent_weight,
    latent_norm_gain,
    expand_weight,
    w_out,
    ffn_gain,
    w_router,
    shared_gate,
    shared_up,
    shared_down,
    expert_gate,
    expert_up,
    expert_down,
):
    device_local = tokens.shape[1]
    experts = lax.axis_size("expert")
    shards = lax.axis_size("fsdp")
    position = lax.axis_index("expert")
    capacity = shards * (
        (device_local * TOPK * 4 + experts * 3 * shards - 1) // (experts * 3 * shards)
    )
    seq_len = device_local * experts
    feature_width = LATENT_WIDTH + ROTARY_UNITS
    scale = (PLAIN_UNITS + ROTARY_UNITS) ** (-0.5)
    attention_gain_grad, wq, wlat, g_lat, expand_matrix, wout, g_ffn, wrout = (
        lax.all_gather(attn_gain, "fsdp", axis=0, tiled=True),
        lax.all_gather(w_query, "fsdp", axis=0, tiled=True),
        lax.all_gather(latent_weight, "fsdp", axis=0, tiled=True),
        lax.all_gather(latent_norm_gain, "fsdp", axis=0, tiled=True),
        lax.all_gather(expand_weight, "fsdp", axis=0, tiled=True),
        lax.all_gather(w_out, "fsdp", axis=0, tiled=True),
        lax.all_gather(ffn_gain, "fsdp", axis=0, tiled=True),
        lax.all_gather(w_router, "fsdp", axis=0, tiled=True),
    )
    sgate, sup, sdown = (
        lax.all_gather(shared_gate, ("expert", "fsdp"), axis=0, tiled=True),
        lax.all_gather(shared_up, ("expert", "fsdp"), axis=0, tiled=True),
        lax.all_gather(shared_down, ("expert", "fsdp"), axis=0, tiled=True),
    )
    attention_gain_grad = attention_gain_grad.astype(jnp.float32)
    g_lat = g_lat.astype(jnp.float32)
    g_ffn = g_ffn.astype(jnp.float32)
    x_in = tokens[0].astype(jnp.float32)
    grad_out = cotangent[0].astype(jnp.float32)
    positions = position * device_local + jnp.arange(device_local, dtype=jnp.int32)
    cosine_table, sine_table = rope_tables(positions)
    normed, inv_attn = norm_forward(x_in, attention_gain_grad)
    normed_in = normed.astype(jnp.bfloat16)
    query_full = matrix_product(normed_in, wq).reshape(
        device_local, HEAD_COUNT, PLAIN_UNITS + ROTARY_UNITS
    )
    query_nope = query_full[:, :, :PLAIN_UNITS].astype(jnp.bfloat16)
    expanded_latent = expand_matrix.reshape(LATENT_WIDTH, HEAD_COUNT, PLAIN_UNITS + VALUE_UNITS)
    key_part = expanded_latent[:, :, :PLAIN_UNITS]
    value_part = expanded_latent[:, :, PLAIN_UNITS:]
    query_latent = jnp.einsum(
        "thd,chd->thc", query_nope, key_part, preferred_element_type=jnp.float32
    )
    query_rope = apply_rotary(
        query_full[:, :, PLAIN_UNITS:], cosine_table[:, None, :], sine_table[:, None, :]
    )
    token_rows = device_local * HEAD_COUNT
    query = (
        jnp.concatenate([query_latent, query_rope], axis=-1)
        .astype(jnp.bfloat16)
        .reshape(token_rows, feature_width)
    )
    latent_complete = matrix_product(normed_in, wlat)
    packed_rows = latent_complete[:, :LATENT_WIDTH]
    latent_state, inv_lat = norm_forward(packed_rows, g_lat)
    rotary_key = apply_rotary(latent_complete[:, LATENT_WIDTH:], cosine_table, sine_table)
    key = jnp.concatenate([latent_state, rotary_key], axis=-1).astype(jnp.bfloat16)
    keys_all = lax.all_gather(key, "expert", axis=0, tiled=True)
    block = min(512, seq_len)
    token_tally = (position * device_local + device_local + block - 1) // block
    q_pos = position * device_local + jnp.arange(token_rows, dtype=jnp.int32) // HEAD_COUNT

    def scores_of(index):
        key_rows = lax.dynamic_slice_in_dim(keys_all, index * block, block, 0)
        raw = outer_product(query, key_rows)
        k_pos = index * block + jnp.arange(block, dtype=jnp.int32)
        valid = k_pos[None, :] <= q_pos[:, None]
        return (jnp.where(valid, raw * scale, -1e30), key_rows)

    def stats_step(index, carry):
        top, total = carry
        scores, unused = scores_of(index)
        new_top = jnp.maximum(top, jnp.max(scores, axis=1))
        total = total * jnp.exp(top - new_top) + jnp.sum(jnp.exp(scores - new_top[:, None]), axis=1)
        return (new_top, total)

    top, total = lax.fori_loop(
        0,
        token_tally,
        stats_step,
        (jnp.full((token_rows,), -1e30, jnp.float32), jnp.zeros((token_rows,), jnp.float32)),
    )
    log_total = top + jnp.log(total)

    def mixing_update(index, running_total):
        scores, key_rows = scores_of(index)
        weight_arrays = jnp.exp(scores - log_total[:, None]).astype(jnp.bfloat16)
        return running_total + matrix_product(weight_arrays, key_rows[:, :LATENT_WIDTH])

    mixed_output_sum = lax.fori_loop(
        0, token_tally, mixing_update, jnp.zeros((token_rows, LATENT_WIDTH), jnp.float32)
    )
    mixed_output = mixed_output_sum.astype(jnp.bfloat16).reshape(
        device_local, HEAD_COUNT, LATENT_WIDTH
    )
    heads = jnp.einsum("thc,chv->thv", mixed_output, value_part, preferred_element_type=jnp.float32)
    heads = heads.reshape(device_local, HEAD_COUNT * VALUE_UNITS).astype(jnp.bfloat16)
    hidden = x_in + matrix_product(heads, wout)
    normed2, inv_ffn = norm_forward(hidden, g_ffn)
    normed_ffn = normed2.astype(jnp.bfloat16)
    logits = matrix_product(normed_ffn, wrout)
    router = jax.nn.softmax(logits, axis=-1)
    own_routes = routes[0]
    names = jnp.arange(experts, dtype=jnp.int32)
    chosen = (own_routes[:, :, None] == names[None, None, :]).astype(jnp.float32)
    gates = jnp.sum(chosen * router[:, None, :], axis=-1)
    hits = (own_routes.reshape(device_local * TOPK)[:, None] == names[None, :]).astype(jnp.int32)
    slot = jnp.sum((jnp.cumsum(hits, axis=0) - hits) * hits, axis=1)
    place = own_routes.reshape(device_local * TOPK) * capacity + slot
    token_of = jnp.arange(device_local * TOPK, dtype=jnp.int32) // TOPK
    table = jnp.full((experts * capacity,), device_local, jnp.int32).at[place].set(token_of)
    padded = jnp.concatenate([normed_ffn, jnp.zeros((1, MODEL_WIDTH), jnp.bfloat16)], axis=0)
    buffer = padded[table].reshape(experts, capacity, MODEL_WIDTH)
    w_g, w_u, w_d = (expert_gate[0], expert_up[0], expert_down[0])

    def spread(values):
        return jnp.broadcast_to(values[:, None], (experts, shards, capacity, MODEL_WIDTH)).reshape(
            experts * shards, capacity, MODEL_WIDTH
        )

    def collect(back):
        return jnp.sum(back.reshape(experts, shards, capacity, MODEL_WIDTH), axis=1).reshape(
            experts * capacity, MODEL_WIDTH
        )

    received = lax.all_to_all(
        spread(buffer), ("expert", "fsdp"), split_axis=0, concat_axis=0, tiled=True
    )
    ex_rows = received.reshape(-1, MODEL_WIDTH)
    pre_gate = matrix_product(ex_rows, w_g)
    pre_up = matrix_product(ex_rows, w_u)
    act_gate, slope = silu_parts(pre_gate)
    ex_act = (act_gate * pre_up).astype(jnp.bfloat16)
    ex_out = matrix_product(ex_act, w_d).reshape(received.shape)
    returned = lax.all_to_all(
        ex_out.astype(jnp.bfloat16), ("expert", "fsdp"), split_axis=0, concat_axis=0, tiled=True
    ).astype(ex_out.dtype)
    results = collect(returned)
    picked = results[place].reshape(device_local, TOPK, MODEL_WIDTH)
    routed = jnp.sum(gates[:, :, None] * picked, axis=1)
    sh_gate = matrix_product(normed_ffn, sgate)
    sh_up = matrix_product(normed_ffn, sup)
    sh_silu, sh_slope = silu_parts(sh_gate)
    sh_act = (sh_silu * sh_up).astype(jnp.bfloat16)
    shared = matrix_product(sh_act, sdown)
    output = hidden + routed + shared
    d_shared = grad_out.astype(jnp.bfloat16)
    shared_down_gradient = inner(sh_act, d_shared)
    d_sh_act = outer_product(d_shared, sdown)
    d_sh_gate = (d_sh_act * sh_up * sh_slope).astype(jnp.bfloat16)
    d_sh_up = (d_sh_act * sh_silu).astype(jnp.bfloat16)
    shared_gate_gradient = inner(normed_ffn, d_sh_gate)
    shared_up_gradient = inner(normed_ffn, d_sh_up)
    d_normed_ffn = outer_product(d_sh_gate, sgate) + outer_product(d_sh_up, sup)
    d_picked = (
        (gates[:, :, None] * grad_out[:, None, :])
        .astype(jnp.bfloat16)
        .reshape(device_local * TOPK, MODEL_WIDTH)
    )
    d_gates = jnp.sum(picked * grad_out[:, None, :], axis=2)
    d_buffer = (
        jnp.zeros((experts * capacity, MODEL_WIDTH), jnp.bfloat16)
        .at[place]
        .set(d_picked)
        .reshape(experts, capacity, MODEL_WIDTH)
    )
    d_received = lax.all_to_all(
        spread(d_buffer), ("expert", "fsdp"), split_axis=0, concat_axis=0, tiled=True
    )
    d_rows = d_received.reshape(-1, MODEL_WIDTH)
    d_act = outer_product(d_rows, w_d)
    g_down = inner(ex_act, d_rows)
    d_pre_gate = (d_act * pre_up * slope).astype(jnp.bfloat16)
    d_pre_up = (d_act * act_gate).astype(jnp.bfloat16)
    g_gate = inner(ex_rows, d_pre_gate)
    g_up = inner(ex_rows, d_pre_up)
    d_ex_rows = (outer_product(d_pre_gate, w_g) + outer_product(d_pre_up, w_u)).reshape(
        received.shape
    )
    d_returned = lax.all_to_all(
        d_ex_rows.astype(jnp.bfloat16), ("expert", "fsdp"), split_axis=0, concat_axis=0, tiled=True
    ).astype(d_ex_rows.dtype)
    d_results = collect(d_returned)
    d_normed_ffn = d_normed_ffn + jnp.sum(
        d_results[place].reshape(device_local, TOPK, MODEL_WIDTH), axis=1
    )
    d_router = jnp.sum(chosen * d_gates[:, :, None], axis=1)
    d_logits = (router * (d_router - jnp.sum(router * d_router, axis=1, keepdims=True))).astype(
        jnp.bfloat16
    )
    router_weight_gradient = inner(normed_ffn, d_logits)
    d_normed_ffn = d_normed_ffn + outer_product(d_logits, wrout)
    d_hidden_norm, g_ffn_grad = norm_backward(hidden, inv_ffn, g_ffn, d_normed_ffn)
    d_hidden = grad_out + d_hidden_norm
    d_attn = d_hidden.astype(jnp.bfloat16)
    output_weight_gradient = inner(heads, d_attn)
    d_heads = (
        outer_product(d_attn, wout)
        .astype(jnp.bfloat16)
        .reshape(device_local, HEAD_COUNT, VALUE_UNITS)
    )
    value_weight_gradient = jnp.einsum(
        "thc,thv->chv", mixed_output, d_heads, preferred_element_type=jnp.float32
    )
    mixed_gradient = jnp.einsum(
        "thv,chv->thc", d_heads, value_part, preferred_element_type=jnp.float32
    )
    mixed_gradient = mixed_gradient.astype(jnp.bfloat16).reshape(token_rows, LATENT_WIDTH)
    delta = jnp.sum(mixed_gradient.astype(jnp.float32) * mixed_output_sum, axis=1)

    def back_step(index, carry):
        d_query_acc, d_keys_acc = carry
        scores, key_rows = scores_of(index)
        weight_arrays = jnp.exp(scores - log_total[:, None])
        weight_gradients = outer_product(mixed_gradient, key_rows[:, :LATENT_WIDTH])
        d_scores = (weight_arrays * (weight_gradients - delta[:, None]) * scale).astype(
            jnp.bfloat16
        )
        d_query_acc = d_query_acc + matrix_product(d_scores, key_rows)
        d_values = inner(weight_arrays.astype(jnp.bfloat16), mixed_gradient)
        d_block = inner(d_scores, query) + jnp.concatenate(
            [d_values, jnp.zeros((block, ROTARY_UNITS), jnp.float32)], axis=1
        )
        previous = lax.dynamic_slice_in_dim(d_keys_acc, index * block, block, 0)
        return (
            d_query_acc,
            lax.dynamic_update_slice_in_dim(d_keys_acc, previous + d_block, index * block, 0),
        )

    d_query, d_keys = lax.fori_loop(
        0,
        token_tally,
        back_step,
        (
            jnp.zeros((token_rows, feature_width), jnp.float32),
            jnp.zeros((seq_len, feature_width), jnp.float32),
        ),
    )
    key_gradient = lax.psum_scatter(
        d_keys.astype(jnp.bfloat16), "expert", scatter_dimension=0, tiled=True
    )
    query_up_gradient = d_query.astype(jnp.bfloat16).reshape(
        device_local, HEAD_COUNT, feature_width
    )
    query_latent_gradient = query_up_gradient[:, :, :LATENT_WIDTH]
    key_weight_gradient = jnp.einsum(
        "thc,thd->chd", query_latent_gradient, query_nope, preferred_element_type=jnp.float32
    )
    d_q_nope = jnp.einsum(
        "thc,chd->thd", query_latent_gradient, key_part, preferred_element_type=jnp.float32
    )
    d_q_rope = reverse_rotary(
        query_up_gradient[:, :, LATENT_WIDTH:].astype(jnp.float32),
        cosine_table[:, None, :],
        sine_table[:, None, :],
    )
    d_query_full = (
        jnp.concatenate([d_q_nope, d_q_rope], axis=-1)
        .astype(jnp.bfloat16)
        .reshape(device_local, HEAD_COUNT * (PLAIN_UNITS + ROTARY_UNITS))
    )
    query_weight_gradient = inner(normed_in, d_query_full)
    d_normed_in = outer_product(d_query_full, wq)
    latent_gradient = key_gradient[:, :LATENT_WIDTH].astype(jnp.float32)
    rotary_key_gradient = reverse_rotary(
        key_gradient[:, LATENT_WIDTH:].astype(jnp.float32), cosine_table, sine_table
    )
    d_compact, g_lat_grad = norm_backward(packed_rows, inv_lat, g_lat, latent_gradient)
    d_latent_full = jnp.concatenate([d_compact, rotary_key_gradient], axis=-1).astype(jnp.bfloat16)
    latent_weight_gradient = inner(normed_in, d_latent_full)
    d_normed_in = d_normed_in + outer_product(d_latent_full, wlat)
    d_norm_in, g_attn_grad = norm_backward(x_in, inv_attn, attention_gain_grad, d_normed_in)
    d_tokens = (d_hidden + d_norm_in).astype(jnp.bfloat16)
    expand_weight_gradient = jnp.concatenate(
        [key_weight_gradient, value_weight_gradient], axis=-1
    ).reshape(LATENT_WIDTH, HEAD_COUNT * (PLAIN_UNITS + VALUE_UNITS))
    r_sgate, r_sup, r_sdown = (
        lax.psum_scatter(shared_gate_gradient, ("expert", "fsdp"), scatter_dimension=0, tiled=True),
        lax.psum_scatter(shared_up_gradient, ("expert", "fsdp"), scatter_dimension=0, tiled=True),
        lax.psum_scatter(shared_down_gradient, ("expert", "fsdp"), scatter_dimension=0, tiled=True),
    )
    r_attn, r_query, r_latent, r_lgain, r_expand, r_out, r_fgain, r_router = (
        lax.psum_scatter(
            g_attn_grad.astype(jnp.bfloat16), "fsdp", scatter_dimension=0, tiled=True
        ).astype(jnp.float32),
        lax.psum_scatter(
            query_weight_gradient.astype(jnp.bfloat16), "fsdp", scatter_dimension=0, tiled=True
        ).astype(jnp.float32),
        lax.psum_scatter(
            latent_weight_gradient.astype(jnp.bfloat16), "fsdp", scatter_dimension=0, tiled=True
        ).astype(jnp.float32),
        lax.psum_scatter(
            g_lat_grad.astype(jnp.bfloat16), "fsdp", scatter_dimension=0, tiled=True
        ).astype(jnp.float32),
        lax.psum_scatter(
            expand_weight_gradient.astype(jnp.bfloat16), "fsdp", scatter_dimension=0, tiled=True
        ).astype(jnp.float32),
        lax.psum_scatter(
            output_weight_gradient.astype(jnp.bfloat16), "fsdp", scatter_dimension=0, tiled=True
        ).astype(jnp.float32),
        lax.psum_scatter(
            g_ffn_grad.astype(jnp.bfloat16), "fsdp", scatter_dimension=0, tiled=True
        ).astype(jnp.float32),
        lax.psum_scatter(
            router_weight_gradient.astype(jnp.bfloat16), "fsdp", scatter_dimension=0, tiled=True
        ).astype(jnp.float32),
    )
    r_attn, r_query, r_latent, r_lgain, r_expand, r_out, r_fgain, r_router = (
        lax.psum(r_attn.astype(jnp.bfloat16), "expert").astype(jnp.float32),
        lax.psum(r_query.astype(jnp.bfloat16), "expert").astype(jnp.float32),
        lax.psum(r_latent.astype(jnp.bfloat16), "expert").astype(jnp.float32),
        lax.psum(r_lgain.astype(jnp.bfloat16), "expert").astype(jnp.float32),
        lax.psum(r_expand.astype(jnp.bfloat16), "expert").astype(jnp.float32),
        lax.psum(r_out.astype(jnp.bfloat16), "expert").astype(jnp.float32),
        lax.psum(r_fgain.astype(jnp.bfloat16), "expert").astype(jnp.float32),
        lax.psum(r_router.astype(jnp.bfloat16), "expert").astype(jnp.float32),
    )
    return (
        output.astype(jnp.bfloat16)[None],
        d_tokens[None],
        r_attn,
        r_query,
        r_latent,
        r_lgain,
        r_expand,
        r_out,
        r_fgain,
        r_router,
        r_sgate,
        r_sup,
        r_sdown,
        g_gate[None],
        g_up[None],
        g_down[None],
    )


LINE = 4
SQUARE = 2
CORES = 2
MESH = pl.DeviceIdType.MESH
VMEM_LIMIT = 56 * 1024 * 1024


class Place:
    def __init__(self):
        index = lax.axis_index("expert")
        self.y = lax.axis_index("fsdp")
        self.c = lax.rem(index, CORES)
        self.b = lax.rem(lax.div(index, CORES), SQUARE)
        self.a = lax.div(index, CORES * SQUARE)

    def device(self, da=0, db=0, dc=0, dy=0):
        b = 1 - self.b if db else self.b
        c = 1 - self.c if dc else self.c
        y = 1 - self.y if dy else self.y
        return (((self.a + da) * SQUARE + b) * CORES + c, y)

    def block(self, full, a, db=0, dc=0, dy=0):
        b = 1 - self.b if db else self.b
        c = 1 - self.c if dc else self.c
        y = 1 - self.y if dy else self.y
        flat = (a * SQUARE + b) * CORES + c
        return y * (LINE * SQUARE * CORES) + flat if full else flat

    def greet(self, with_y):
        barrier = pltpu.get_barrier_semaphore()
        near = [dict(db=1), dict(dc=1)] + ([dict(dy=1)] if with_y else [])
        for step in near:
            pl.semaphore_signal(barrier, inc=1, device_id=self.device(**step), device_id_type=MESH)

        @pl.when(self.a > 0)
        def _():
            pl.semaphore_signal(barrier, inc=1, device_id=self.device(da=-1), device_id_type=MESH)

        @pl.when(self.a < LINE - 1)
        def _():
            pl.semaphore_signal(barrier, inc=1, device_id=self.device(da=1), device_id_type=MESH)

        ends = jnp.logical_or(self.a == 0, self.a == LINE - 1).astype(jnp.int32)
        pl.semaphore_wait(barrier, len(near) + 2 - ends)


class Sender:
    def __init__(self, place, sems):
        self.place, self.sems, self.pending = place, sems, []

    def send(self, src, dst, recv_sem, step, cond=None):
        sem = self.sems.at[len(self.pending)]

        def make():
            return pltpu.make_async_remote_copy(
                src_ref=src,
                dst_ref=dst,
                send_sem=sem,
                recv_sem=recv_sem,
                device_id=self.place.device(**step),
                device_id_type=MESH,
            )

        def start():
            make().start()

        guarded(cond, start)
        self.pending.append((cond, lambda: make().wait_send()))

    def arrived(self, dst, recv_sem):
        pltpu.make_async_remote_copy(
            src_ref=dst,
            dst_ref=dst,
            send_sem=self.sems.at[0],
            recv_sem=recv_sem,
            device_id=self.place.device(dc=1),
            device_id_type=MESH,
        ).wait_recv()

    def finish(self):
        for cond, wait in self.pending:
            guarded(cond, wait)


def guarded(cond, action):
    if cond is None:
        action()
    else:
        pl.when(cond)(action)


def both(first, second):
    if first is None or second is None:
        return second if first is None else first
    return jnp.logical_and(first, second)


def gather_kernel(fulls, count, pairs, gated, *refs):
    ins, outs = refs[: count + pairs], refs[count + pairs : 2 * (count + pairs)]
    local_sems, send_sems, recv_sems, pair_sems = refs[2 * (count + pairs) :]
    place = Place()
    a = place.a
    sender = Sender(place, send_sems)
    some = any(fulls)
    place.greet(some or pairs > 0)
    for at in range(count, count + pairs):
        sender.send(ins[at], outs[at], pair_sems.at[at - count], dict(dy=1))

    def own_copy(at):
        return pltpu.make_async_copy(
            ins[at], outs[at].at[place.block(fulls[at], a)], local_sems.at[at]
        )

    for at in range(count):
        own_copy(at).start()

    def chunk(at, block, half):
        size = ins[at].shape[0] // 2
        return outs[at].at[block, pl.ds(half * size, size)]

    def sem_of(at, block, half):
        return recv_sems.at[at, block * 2 + half]

    def forward(at, block, half, src, step, cond=None):
        sender.send(src, chunk(at, block, half), sem_of(at, block, half), step, cond)

    def receive(at, block, half, cond):
        guarded(cond, lambda: sender.arrived(chunk(at, block, half), sem_of(at, block, half)))

    def held_by(at, delta, cond):
        if at not in gated:
            return cond
        return both(cond, lax.div(a + delta, LINE // 2) == place.y)

    def from_line(delta, always):
        for half in range(2):
            for at in range(count):
                full = fulls[at]
                block = place.block(full, a + delta)
                cond = held_by(at, delta, always)
                size = ins[at].shape[0] // 2
                if delta == 0:
                    src = ins[at].at[pl.ds(half * size, size)]
                else:
                    receive(at, block, half, cond)
                    src = chunk(at, block, half)
                if delta <= 0:
                    forward(at, block, half, src, dict(da=1), both(cond, a < LINE - 1))
                if delta >= 0:
                    forward(at, block, half, src, dict(da=-1), both(cond, a > 0))
                forward(at, block, half, src, dict(db=1), cond)
                if full:
                    forward(at, block, half, src, dict(dy=1), cond)
                forward(at, block, half, src, dict(dc=1), cond)

    def from_side(delta, always):
        for half in range(2):
            for at in range(count):
                full = fulls[at]
                cond = held_by(at, delta, always)
                block = place.block(full, a + delta, db=1)
                receive(at, block, half, cond)
                if full and half == 0:
                    forward(at, block, half, chunk(at, block, half), dict(dy=1), cond)
                forward(at, block, half, chunk(at, block, half), dict(dc=1), cond)
                if full:
                    block = place.block(full, a + delta, dy=1)
                    receive(at, block, half, cond)
                    if half == 1:
                        forward(at, block, half, chunk(at, block, half), dict(db=1), cond)
                    forward(at, block, half, chunk(at, block, half), dict(dc=1), cond)

    def from_corner(delta, always):
        for half in range(2):
            for at in range(count):
                if not fulls[at]:
                    continue
                cond = held_by(at, delta, always)
                block = place.block(True, a + delta, db=1, dy=1)
                receive(at, block, half, cond)
                forward(at, block, half, chunk(at, block, half), dict(dc=1), cond)

    def from_sibling(delta, always):
        for half in range(2):
            for at in range(count):
                full = fulls[at]
                cond = held_by(at, delta, always)
                for db in range(2):
                    for dy in range(2 if full else 1):
                        receive(at, place.block(full, a + delta, db=db, dc=1, dy=dy), half, cond)

    rounds = [[(0, None)]]
    for s in range(1, LINE):
        rounds.append([(-s, a >= s), (s, a + s < LINE)])
    stages = [from_line, from_side] + ([from_corner] if some else []) + [from_sibling]
    for tick in range(len(rounds) + len(stages) - 1):
        for level, stage in enumerate(stages):
            if 0 <= tick - level < len(rounds):
                for delta, cond in rounds[tick - level]:
                    stage(delta, cond)
    for at in range(count, count + pairs):
        sender.arrived(outs[at], pair_sems.at[at - count])
    for at in range(count):
        own_copy(at).wait()
    sender.finish()


def gather_rows(arrays, full, collective_id, swapped=(), gated=()):
    count, pairs = len(arrays), len(swapped)
    fulls = full if isinstance(full, tuple) else (full,) * count
    sizes = [LINE * SQUARE * CORES * (SQUARE if reach else 1) for reach in fulls]
    blocks = max(sizes)
    lines = 2 * LINE - 1
    sends = pairs + count * lines * 2 * (9 if any(fulls) else 5)
    moved = sum(blocks * 2 * x.size * x.dtype.itemsize for x in arrays)
    return pl.pallas_call(
        functools.partial(gather_kernel, fulls, count, pairs, gated),
        out_shape=[jax.ShapeDtypeStruct((n,) + x.shape, x.dtype) for n, x in zip(sizes, arrays)]
        + [jax.ShapeDtypeStruct(x.shape, x.dtype) for x in swapped],
        in_specs=[pl.BlockSpec(memory_space=pl.ANY)] * (count + pairs),
        out_specs=[pl.BlockSpec(memory_space=pl.ANY)] * (count + pairs),
        scratch_shapes=[
            pltpu.SemaphoreType.DMA((count,)),
            pltpu.SemaphoreType.DMA((sends,)),
            pltpu.SemaphoreType.DMA((count, blocks * 2)),
            pltpu.SemaphoreType.DMA((max(pairs, 1),)),
        ],
        compiler_params=pltpu.CompilerParams(collective_id=collective_id, has_side_effects=True),
        cost_estimate=pl.CostEstimate(flops=0, bytes_accessed=6 * moved, transcendentals=0),
    )(*arrays, *swapped)


def add_rows(target, sources, size):
    def step(at, carry):
        rows = pl.ds(pl.multiple_of(at * 16, 16), 16)
        total = sources[0][rows, :].astype(jnp.float32)
        for source in sources[1:]:
            total = total + source[rows, :].astype(jnp.float32)
        target[rows, :] = total.astype(target.dtype)
        return carry

    lax.fori_loop(0, size // 16, step, 0)


def scatter_kernel(full, pairs, part, *refs):
    ins, out, outs = refs[:pairs], refs[pairs], refs[pairs + 1 : 2 * pairs + 1]
    mine, got, side, up, down, load_sems, send_sems, recv_sems, pair_sems = refs[2 * pairs + 1 :]
    place = Place()
    a = place.a
    kinds = 4 if full else 2
    size = part.shape[1]
    half = size // 2
    sender = Sender(place, send_sems)
    place.greet(full or pairs > 0)
    for at in range(pairs):
        sender.send(ins[at], outs[at], pair_sems.at[at], dict(dy=1))
    order = [LINE - 1, 0, LINE - 2, 1]
    walk = (3, 1, 2, 0) if full else (1, 0)

    def sem_of(group, target, kind):
        return recv_sems.at[group, target * 4 + kind]

    def load(target, kind):
        block = place.block(full, target, db=kind % 2, dy=kind // 2)
        return pltpu.make_async_copy(
            part.at[block], mine.at[target, kind], load_sems.at[target * 4 + kind]
        )

    for target in order:
        for kind in walk:
            load(target, kind).start()
            block = place.block(full, target, db=kind % 2, dc=1, dy=kind // 2)
            sender.send(
                part.at[block], got.at[target, kind], sem_of(0, target, kind), dict(dc=1)
            )

    def rows_of(ref, which):
        return ref.at[pl.ds(which * half, half)]

    def over_cores(target):
        for kind in walk:
            load(target, kind).wait()
            sender.arrived(got.at[target, kind], sem_of(0, target, kind))
            add_rows(mine.at[target, kind], [mine.at[target, kind], got.at[target, kind]], size)
            held = mine.at[target, kind]
            if kind == 3:
                sender.send(rows_of(held, 0), side.at[target, 4], sem_of(1, target, 0), dict(db=1))
                sender.send(rows_of(held, 1), side.at[target, 5], sem_of(1, target, 1), dict(dy=1))
            if kind == 1:
                sender.send(rows_of(held, 0), side.at[target, 0], sem_of(2, target, 0), dict(db=1))
                if not full:
                    sender.send(
                        rows_of(held, 1), side.at[target, 1], sem_of(2, target, 1), dict(db=1)
                    )
            if kind == 2:
                sender.send(rows_of(held, 1), side.at[target, 3], sem_of(2, target, 3), dict(dy=1))

    def over_corner(target):
        sender.arrived(side.at[target, 4], sem_of(1, target, 0))
        held = rows_of(mine.at[target, 2], 0)
        add_rows(held, [held, side.at[target, 4]], half)
        sender.send(held, side.at[target, 2], sem_of(2, target, 2), dict(dy=1))
        sender.arrived(side.at[target, 5], sem_of(1, target, 1))
        held = rows_of(mine.at[target, 1], 1)
        add_rows(held, [held, side.at[target, 5]], half)
        sender.send(held, side.at[target, 1], sem_of(2, target, 1), dict(db=1))

    def over_line(target):
        for which in range(2):
            held = rows_of(mine.at[target, 0], which)
            parts = [held]
            for source in (0, 2) if full else (0,):
                sender.arrived(side.at[target, source + which], sem_of(2, target, source + which))
                parts.append(side.at[target, source + which])
            below, above = rows_of(up.at[target], which), rows_of(down.at[target], which)
            below_sem, above_sem = sem_of(3, target, which), sem_of(3, target, 2 + which)

            def upward(with_below):
                extra = []
                if with_below:
                    sender.arrived(below, below_sem)
                    extra = [below]
                add_rows(held, parts + extra, half)

            def downward(with_above):
                extra = []
                if with_above:
                    sender.arrived(above, above_sem)
                    extra = [above]
                add_rows(held, parts + extra, half)

            if target > 0:
                pl.when(jnp.logical_and(a < target, a > 0))(lambda: upward(True))
                pl.when(a == 0)(lambda: upward(False))
                sender.send(held, below, below_sem, dict(da=1), a < target)
            if target < LINE - 1:
                pl.when(jnp.logical_and(a > target, a < LINE - 1))(lambda: downward(True))
                pl.when(a == LINE - 1)(lambda: downward(False))
                sender.send(held, above, above_sem, dict(da=-1), a > target)

            def last():
                extra = []
                if target > 0:
                    sender.arrived(below, below_sem)
                    extra.append(below)
                if target < LINE - 1:
                    sender.arrived(above, above_sem)
                    extra.append(above)
                add_rows(rows_of(out, which), parts + extra, half)

            pl.when(a == target)(last)

    stages = [over_cores] + ([over_corner] if full else []) + [over_line]
    for tick in range(len(order) + len(stages) - 1):
        for level, stage in enumerate(stages):
            if 0 <= tick - level < len(order):
                stage(order[tick - level])
    for at in range(pairs):
        sender.arrived(outs[at], pair_sems.at[at])
    sender.finish()


def scatter_rows(part, full, collective_id, swapped=()):
    blocks, rows, width = part.shape
    kinds = 4 if full else 2
    half = rows // 2
    pairs = len(swapped)
    return pl.pallas_call(
        functools.partial(scatter_kernel, full, pairs),
        out_shape=[jax.ShapeDtypeStruct((rows, width), jnp.float32)]
        + [jax.ShapeDtypeStruct(x.shape, x.dtype) for x in swapped],
        in_specs=[pl.BlockSpec(memory_space=pl.ANY)] * (1 + pairs),
        out_specs=[pl.BlockSpec(memory_space=pltpu.VMEM)]
        + [pl.BlockSpec(memory_space=pl.ANY)] * pairs,
        scratch_shapes=[
            pltpu.VMEM((LINE, kinds, rows, width), part.dtype),
            pltpu.VMEM((LINE, kinds, rows, width), part.dtype),
            pltpu.VMEM((LINE, 6, half, width), part.dtype),
            pltpu.VMEM((LINE, rows, width), part.dtype),
            pltpu.VMEM((LINE, rows, width), part.dtype),
            pltpu.SemaphoreType.DMA((LINE * 4,)),
            pltpu.SemaphoreType.DMA((pairs + LINE * (4 + 6 + 4),)),
            pltpu.SemaphoreType.DMA((4, LINE * 4)),
            pltpu.SemaphoreType.DMA((max(pairs, 1),)),
        ],
        compiler_params=pltpu.CompilerParams(
            collective_id=collective_id, has_side_effects=True, vmem_limit_bytes=VMEM_LIMIT
        ),
        cost_estimate=pl.CostEstimate(
            flops=0, bytes_accessed=12 * part.size * part.dtype.itemsize, transcendentals=0
        ),
    )(part, *swapped)


def contract_last(left, right):
    return lax.dot_general(
        left, right, (((1,), (1,)), ((), ())), preferred_element_type=jnp.float32
    )


def contract_first(left, right):
    return lax.dot_general(
        left, right, (((0,), (0,)), ((), ())), preferred_element_type=jnp.float32
    )


def expert_kernel(
    capacity,
    normed,
    grads,
    places,
    router_cols,
    w_gate,
    w_up,
    w_down,
    shared_in,
    shared_out,
    out_part,
    d_part,
    ex_rows,
    ex_grads,
    act_out,
    d_gate_out,
    d_up_out,
    shared_in_grad,
    shared_out_grad,
    in_total,
    out_total,
):
    position = lax.axis_index("expert")
    experts = lax.axis_size("expert")
    group, rows, width = normed.shape
    tokens, slots = group * rows, group * capacity
    bf16 = jnp.bfloat16
    x = normed[...].reshape(tokens, width)
    g = grads[...].reshape(tokens, width)

    slot = lax.broadcasted_iota(jnp.int32, (slots, tokens), 0)
    token = lax.broadcasted_iota(jnp.int32, (slots, tokens), 1)
    same = lax.div(slot, capacity) == lax.div(token, rows)
    place = jnp.broadcast_to(places[0], (slots, tokens))
    hit = jnp.logical_and(same, lax.rem(slot, capacity) == place)
    pick = jnp.where(hit, 1.0, 0.0).astype(bf16)

    r = matrix_product(pick, x).astype(bf16)
    gr = matrix_product(pick, g).astype(bf16)
    ex_rows[...] = r
    ex_grads[...] = gr
    lane = lax.broadcasted_iota(jnp.int32, (slots, router_cols.shape[1]), 1)
    logits = jnp.where(lane < experts, matrix_product(r, router_cols[...]), -1e30)
    exps = jnp.exp(logits - jnp.max(logits, axis=1, keepdims=True))
    gate = jnp.sum(jnp.where(lane == position, exps, 0.0), axis=1, keepdims=True) / jnp.sum(
        exps, axis=1, keepdims=True
    )

    pre_gate = matrix_product(r, w_gate[...])
    pre_up = matrix_product(r, w_up[...])
    act_gate, slope = silu_parts(pre_gate)
    act = act_gate * pre_up
    back = contract_last(gr, w_down[...])
    d_gate_slot = jnp.sum(act * back, axis=1, keepdims=True)
    scaled = (gate * act).astype(bf16)
    d_act = gate * back
    d_pre_gate = (d_act * pre_up * slope).astype(bf16)
    d_pre_up = (d_act * act_gate).astype(bf16)
    act_out[...] = scaled
    d_gate_out[...] = d_pre_gate
    d_up_out[...] = d_pre_up
    ex_out = matrix_product(scaled, w_down[...]).astype(bf16)
    d_ex = contract_last(d_pre_gate, w_gate[...]) + contract_last(d_pre_up, w_up[...])
    d_ex = d_ex.astype(bf16)

    units = shared_out.shape[0]
    mix = matrix_product(x, shared_in[...])
    sh_gate, sh_up = mix[:, :units], mix[:, units:]
    sh_silu, sh_slope = silu_parts(sh_gate)
    sh_act = (sh_silu * sh_up).astype(bf16)
    d_sh_act = contract_last(g, shared_out[...])
    d_mix = jnp.concatenate([d_sh_act * sh_up * sh_slope, d_sh_act * sh_silu], axis=1)
    d_mix = d_mix.astype(bf16)

    out = contract_first(pick, ex_out) + matrix_product(sh_act, shared_out[...])
    out_part[...] = out.astype(bf16).reshape(group, rows, width)
    d_in = contract_first(pick, d_ex) + contract_last(d_mix, shared_in[...])
    d_part[:, :, :width] = d_in.astype(bf16).reshape(group, rows, width)
    column = jnp.where(lane == position, d_gate_slot, 0.0).astype(bf16)
    d_part[:, :, width:] = contract_first(pick, column).astype(bf16).reshape(group, rows, -1)

    step = pl.program_id(0)

    @pl.when(step == 0)
    def _():
        in_total[...] = jnp.zeros_like(in_total)
        out_total[...] = jnp.zeros_like(out_total)

    in_total[...] += contract_first(d_mix, x)
    out_total[...] += contract_first(sh_act, g)

    @pl.when(step == pl.num_programs(0) - 1)
    def _():
        shared_in_grad[...] = in_total[...]
        shared_out_grad[...] = out_total[...]


def expert_phase(
    all_normed, all_grads, places, router_cols, w_gate, w_up, w_down, shared_in, shared_out, capacity
):
    blocks, rows, width = all_normed.shape
    group = 4
    slots = group * capacity
    hidden = w_gate.shape[1]
    units = shared_out.shape[0]
    side = router_cols.shape[1]
    bf16 = jnp.bfloat16

    def by_group(shape):
        zeros = (0,) * (len(shape) - 1)
        return pl.BlockSpec(shape, lambda i: (i,) + zeros)

    def fixed(shape):
        return pl.BlockSpec(
            shape, lambda i: (0,) * len(shape), pipeline_mode=pl.Buffered(buffer_count=1)
        )

    return pl.pallas_call(
        functools.partial(expert_kernel, capacity),
        grid=(blocks // group,),
        out_shape=[
            jax.ShapeDtypeStruct((blocks, rows, width), bf16),
            jax.ShapeDtypeStruct((blocks, rows, width + side), bf16),
            jax.ShapeDtypeStruct((blocks * capacity, width), bf16),
            jax.ShapeDtypeStruct((blocks * capacity, width), bf16),
            jax.ShapeDtypeStruct((blocks * capacity, hidden), bf16),
            jax.ShapeDtypeStruct((blocks * capacity, hidden), bf16),
            jax.ShapeDtypeStruct((blocks * capacity, hidden), bf16),
            jax.ShapeDtypeStruct((2 * units, width), jnp.float32),
            jax.ShapeDtypeStruct((units, width), jnp.float32),
        ],
        in_specs=[
            by_group((group, rows, width)),
            by_group((group, rows, width)),
            by_group((1, 1, group * rows)),
            fixed(router_cols.shape),
            fixed(w_gate.shape),
            fixed(w_up.shape),
            fixed(w_down.shape),
            fixed(shared_in.shape),
            fixed(shared_out.shape),
        ],
        out_specs=[
            by_group((group, rows, width)),
            by_group((group, rows, width + side)),
            by_group((slots, width)),
            by_group((slots, width)),
            by_group((slots, hidden)),
            by_group((slots, hidden)),
            by_group((slots, hidden)),
            fixed((2 * units, width)),
            fixed((units, width)),
        ],
        scratch_shapes=[
            pltpu.VMEM((2 * units, width), jnp.float32),
            pltpu.VMEM((units, width), jnp.float32),
        ],
        compiler_params=pltpu.CompilerParams(vmem_limit_bytes=VMEM_LIMIT),
        cost_estimate=pl.CostEstimate(
            flops=2 * blocks * capacity * width * hidden * 6,
            bytes_accessed=10 * blocks * rows * width * 2,
            transcendentals=blocks * capacity * hidden,
        ),
    )(all_normed, all_grads, places, router_cols, w_gate, w_up, w_down, shared_in, shared_out)


def token_gather(rows):
    return lax.all_gather(rows, ("fsdp", "expert"), axis=0, tiled=True)


def token_scatter(partial):
    return lax.psum_scatter(
        partial, ("fsdp", "expert"), scatter_dimension=0, tiled=True
    ).astype(jnp.float32)


def split_body(
    tokens,
    routes,
    cotangent,
    attn_gain,
    w_query,
    latent_weight,
    latent_norm_gain,
    expand_weight,
    w_out,
    ffn_gain,
    w_router,
    shared_gate,
    shared_up,
    shared_down,
    expert_gate,
    expert_up,
    expert_down,
):
    rows = tokens.shape[1]
    experts = lax.axis_size("expert")
    shards = lax.axis_size("fsdp")
    position = lax.axis_index("expert")
    blocks = experts * shards
    seq_len = rows * experts
    capacity = shards * ((rows * TOPK * 4 + experts * 3 * shards - 1) // (experts * 3 * shards))
    head_units = PLAIN_UNITS + ROTARY_UNITS
    pair_units = PLAIN_UNITS + VALUE_UNITS
    feature_width = LATENT_WIDTH + ROTARY_UNITS
    scale = head_units ** (-0.5)

    shard = lax.axis_index("fsdp")
    first = shard == 0

    query_cols = lax.dynamic_slice_in_dim(w_query, position * head_units, head_units, 1)
    expand_cols = lax.dynamic_slice_in_dim(expand_weight, position * pair_units, pair_units, 1)
    owners = experts // shards
    out_rows = lax.dynamic_slice_in_dim(
        w_out, lax.rem(position, owners) * VALUE_UNITS, VALUE_UNITS, 0
    )
    packed = jnp.concatenate(
        [latent_weight, query_cols, w_router, attn_gain[:, None], ffn_gain[:, None]], axis=1
    )
    small = jnp.concatenate([expand_cols, latent_norm_gain[:, None]], axis=1)
    own_routes = jnp.pad(routes[0], ((0, 0), (0, 128 - TOPK)), constant_values=-1)
    seq_rows, all_routes, other_packed, other_small, other_out = gather_rows(
        [tokens[0], own_routes], (False, True), 0, swapped=[packed, small, out_rows]
    )

    def whole(own, other):
        return jnp.concatenate([jnp.where(first, own, other), jnp.where(first, other, own)], axis=0)

    packed = whole(packed, other_packed)
    small = whole(small, other_small)
    out_head = jnp.where(lax.div(position, owners) == shard, out_rows, other_out)
    w_front = packed[:, : feature_width + head_units]
    w_latent = packed[:, :feature_width]
    at = feature_width + head_units
    w_query_head = packed[:, feature_width:at]
    wrout = packed[:, at : at + experts]
    g_attn = packed[:, at + experts].astype(jnp.float32)
    g_ffn = packed[:, at + experts + 1].astype(jnp.float32)
    expand_head = small[:, :pair_units]
    g_lat = small[:, pair_units].astype(jnp.float32)
    units = shared_down.shape[0]

    def to_columns(weight):
        parts = weight.reshape(weight.shape[0], blocks, units).transpose(1, 0, 2)
        return lax.all_to_all(
            parts, ("expert", "fsdp"), split_axis=0, concat_axis=0, tiled=True
        ).reshape(-1, units)

    sh_cols = to_columns(jnp.concatenate([shared_gate, shared_up], axis=0)).reshape(
        blocks, 2, shared_gate.shape[0], units
    )
    lanes = -(-units // 128) * 128
    sh_cols = jnp.pad(sh_cols, ((0, 0), (0, 0), (0, 0), (0, lanes - units)))
    shared_in = sh_cols.transpose(0, 2, 1, 3).reshape(MODEL_WIDTH, 2 * lanes)
    shared_out = jnp.pad(shared_down, ((0, lanes - units), (0, 0)))
    router_cols = jnp.pad(wrout, ((0, 0), (0, 128 - experts)))
    fill = -expert_gate.shape[2] % 256
    w_g = jnp.pad(expert_gate[0], ((0, 0), (0, fill)))
    w_u = jnp.pad(expert_up[0], ((0, 0), (0, fill)))
    w_d = jnp.pad(expert_down[0], ((0, fill), (0, 0)))
    hit = jnp.any(all_routes == position, axis=2)
    tally = hit.astype(jnp.int32)
    slot = jnp.cumsum(tally, axis=1) - tally
    places = jnp.where(hit, slot, -1).reshape(blocks // 4, 1, 4 * rows)

    grad_rows = cotangent[0]
    grad_out = grad_rows.astype(jnp.float32)
    all_grads = token_gather(grad_rows)

    x_in = tokens[0].astype(jnp.float32)
    normed, inv_attn = norm_forward(x_in, g_attn)
    normed_in = normed.astype(jnp.bfloat16)
    seq_normed, _ = norm_forward(
        seq_rows.reshape(seq_len, MODEL_WIDTH).astype(jnp.float32), g_attn
    )
    seq_normed = seq_normed.astype(jnp.bfloat16)
    cosine_table, sine_table = rope_tables(jnp.arange(seq_len, dtype=jnp.int32))
    front = matrix_product(seq_normed, w_front)
    latent_rows, _ = norm_forward(front[:, :LATENT_WIDTH], g_lat)
    latent_rows = latent_rows.astype(jnp.bfloat16)
    key_rope = apply_rotary(front[:, LATENT_WIDTH:feature_width], cosine_table, sine_table)
    query_full = front[:, feature_width:]
    query_rope = apply_rotary(query_full[:, PLAIN_UNITS:], cosine_table, sine_table)
    query = jnp.concatenate([query_full[:, :PLAIN_UNITS], query_rope], axis=1).astype(jnp.bfloat16)
    pairs = matrix_product(latent_rows, expand_head)
    key = jnp.concatenate([pairs[:, :PLAIN_UNITS], key_rope], axis=1).astype(jnp.bfloat16)
    value = pairs[:, PLAIN_UNITS:].astype(jnp.bfloat16)
    order = jnp.arange(seq_len, dtype=jnp.int32)
    scores = jnp.where(
        order[None, :] <= order[:, None], outer_product(query, key) * scale, -1e30
    )
    top = jnp.max(scores, axis=1, keepdims=True)
    exps = jnp.exp(scores - top)
    probs = exps / jnp.sum(exps, axis=1, keepdims=True)
    low_probs = probs.astype(jnp.bfloat16)
    head_sum = matrix_product(low_probs, value)
    head_rows = head_sum.astype(jnp.bfloat16)
    head_part = matrix_product(head_rows, out_head).astype(jnp.bfloat16)
    (mixed_rows,) = scatter_rows(head_part.reshape(experts, rows, MODEL_WIDTH), False, 1)
    hidden = x_in + mixed_rows
    normed2, inv_ffn = norm_forward(hidden, g_ffn)
    normed_ffn = normed2.astype(jnp.bfloat16)
    router = jax.nn.softmax(matrix_product(normed_ffn, wrout), axis=-1)

    (all_normed,) = gather_rows([normed_ffn], True, 2)
    (
        out_part,
        d_part,
        ex_rows,
        ex_grads,
        scaled_act,
        d_pre_gate,
        d_pre_up,
        g_shared_in,
        g_shared_out,
    ) = expert_phase(
        all_normed,
        all_grads.reshape(all_normed.shape),
        places,
        router_cols,
        w_g,
        w_u,
        w_d,
        shared_in,
        shared_out,
        capacity,
    )
    ff = expert_gate.shape[2]
    g_down = inner(scaled_act, ex_grads)[:ff]
    g_gate = inner(ex_rows, d_pre_gate)[:, :ff]
    g_up = inner(ex_rows, d_pre_up)[:, :ff]
    (d_back,) = scatter_rows(d_part, True, 3)
    out_part, d_back = lax.optimization_barrier((out_part, d_back))
    d_normed_ffn = d_back[:, :MODEL_WIDTH]
    d_router = d_back[:, MODEL_WIDTH : MODEL_WIDTH + experts]
    output = hidden + token_scatter(out_part.reshape(blocks * rows, MODEL_WIDTH))

    d_logits = (router * (d_router - jnp.sum(router * d_router, axis=1, keepdims=True))).astype(
        jnp.bfloat16
    )
    g_router = inner(normed_ffn, d_logits)
    d_normed_ffn = d_normed_ffn + outer_product(d_logits, wrout)
    d_hidden_norm, g_ffn_grad = norm_backward(hidden, inv_ffn, g_ffn, d_normed_ffn)
    d_hidden = grad_out + d_hidden_norm
    d_attn = d_hidden.astype(jnp.bfloat16)

    (seq_d_attn,) = gather_rows([d_attn], False, 4)
    seq_d_attn = seq_d_attn.reshape(seq_len, MODEL_WIDTH)
    d_head = outer_product(seq_d_attn, out_head).astype(jnp.bfloat16)
    g_out_head = inner(head_rows, seq_d_attn)
    delta = jnp.sum(d_head.astype(jnp.float32) * head_sum, axis=1, keepdims=True)
    d_scores = (probs * (outer_product(d_head, value) - delta) * scale).astype(jnp.bfloat16)
    d_query = matrix_product(d_scores, key)
    d_key = inner(d_scores, query)
    d_value = inner(low_probs, d_head).astype(jnp.bfloat16)
    d_key_plain = d_key[:, :PLAIN_UNITS].astype(jnp.bfloat16)
    d_pairs = jnp.concatenate([d_key_plain, d_value], axis=1)
    g_expand_head = inner(latent_rows, d_pairs)
    d_keys = jnp.concatenate(
        [outer_product(d_pairs, expand_head), d_key[:, PLAIN_UNITS:]], axis=1
    )
    d_query_full = jnp.concatenate(
        [
            d_query[:, :PLAIN_UNITS],
            reverse_rotary(d_query[:, PLAIN_UNITS:], cosine_table, sine_table),
        ],
        axis=1,
    ).astype(jnp.bfloat16)
    g_query_head = inner(d_query_full, seq_normed).astype(jnp.bfloat16)
    g_expand_head = g_expand_head.astype(jnp.bfloat16)
    g_out_head = g_out_head.astype(jnp.bfloat16)

    def half_of(whole, which, axis):
        size = whole.shape[axis] // shards
        return lax.dynamic_slice_in_dim(whole, which * size, size, axis)

    d_part_in = outer_product(d_query_full, w_query_head)
    d_part_in = jnp.concatenate(
        [d_part_in, d_keys, jnp.zeros((seq_len, ROTARY_UNITS), jnp.float32)], axis=1
    ).astype(jnp.bfloat16)
    d_sums, other_query, other_expand, other_out_grad = scatter_rows(
        d_part_in.reshape(experts, rows, -1),
        False,
        5,
        swapped=[
            half_of(g_query_head, 1 - shard, 1),
            half_of(g_expand_head, 1 - shard, 0),
            g_out_head,
        ],
    )
    d_normed_in = d_sums[:, :MODEL_WIDTH]
    key_gradient = d_sums[:, MODEL_WIDTH : MODEL_WIDTH + feature_width]

    def summed(own, other):
        return (own.astype(jnp.float32) + other.astype(jnp.float32)).astype(jnp.bfloat16)

    own_query = summed(half_of(g_query_head, shard, 1), other_query)
    own_expand = summed(half_of(g_expand_head, shard, 0), other_expand)
    own_out = summed(g_out_head, other_out_grad)
    own_latent = lax.dynamic_slice_in_dim(front[:, :LATENT_WIDTH], position * rows, rows, 0)
    own_cosine = lax.dynamic_slice_in_dim(cosine_table, position * rows, rows, 0)
    own_sine = lax.dynamic_slice_in_dim(sine_table, position * rows, rows, 0)
    inv_lat = lax.rsqrt(jnp.mean(own_latent * own_latent, axis=-1, keepdims=True) + EPS)
    d_compact, g_lat_grad = norm_backward(
        own_latent, inv_lat, g_lat, key_gradient[:, :LATENT_WIDTH]
    )
    d_rope = reverse_rotary(key_gradient[:, LATENT_WIDTH:], own_cosine, own_sine)
    d_latent_full = jnp.concatenate([d_compact, d_rope], axis=-1).astype(jnp.bfloat16)
    g_latent = inner(normed_in, d_latent_full)
    d_normed_in = d_normed_in + outer_product(d_latent_full, w_latent)
    d_norm_in, g_attn_grad = norm_backward(x_in, inv_attn, g_attn, d_normed_in)
    d_tokens = (d_hidden + d_norm_in).astype(jnp.bfloat16)

    half = MODEL_WIDTH // blocks
    cols = g_shared_in.reshape(2, lanes, blocks, half)[:, :units].astype(jnp.bfloat16)
    cols = lax.all_to_all(
        cols.transpose(2, 0, 1, 3), ("expert", "fsdp"), split_axis=0, concat_axis=0, tiled=True
    )
    cols = cols.transpose(1, 3, 0, 2).reshape(2, half, blocks * units).astype(jnp.float32)
    r_sgate, r_sup = (cols[0], cols[1])
    g_sdown = g_shared_out[:units]
    lat_rows = jnp.zeros((shards, MODEL_WIDTH // shards), jnp.float32)
    lat_rows = lat_rows.at[:, : LATENT_WIDTH // shards].set(g_lat_grad.reshape(shards, -1))
    columns = jnp.concatenate(
        [
            g_latent,
            g_router,
            g_attn_grad[:, None],
            g_ffn_grad[:, None],
            lat_rows.reshape(MODEL_WIDTH, 1),
        ],
        axis=1,
    )
    used = columns.shape[1]
    columns = jnp.pad(columns.astype(jnp.bfloat16), ((0, 0), (0, -used % 128)))
    (columns,) = scatter_rows(columns.reshape(blocks, half, -1), True, 6)
    r_query, r_expand, columns, r_out = gather_rows(
        [own_query, own_expand, columns.astype(jnp.bfloat16), own_out], False, 7, gated=(3,)
    )
    r_query = r_query.reshape(experts * head_units, -1).astype(jnp.float32).T
    r_expand = r_expand.transpose(1, 0, 2).reshape(-1, experts * pair_units)
    r_out = lax.dynamic_slice_in_dim(r_out, shard * owners, owners, 0)
    columns = columns.reshape(MODEL_WIDTH // shards, -1).astype(jnp.float32)
    at = feature_width + experts
    return (
        output.astype(jnp.bfloat16)[None],
        d_tokens[None],
        columns[:, at],
        r_query,
        columns[:, :feature_width],
        columns[: LATENT_WIDTH // shards, at + 2],
        r_expand.astype(jnp.float32),
        r_out.reshape(-1, MODEL_WIDTH).astype(jnp.float32),
        columns[:, at + 1],
        columns[:, feature_width:at],
        r_sgate,
        r_sup,
        g_sdown,
        g_gate[None],
        g_up[None],
        g_down[None],
    )


def solution(mesh):
    shape = (mesh.shape["expert"], mesh.shape["fsdp"])
    split = shape == (LINE * SQUARE * CORES, SQUARE) and shape[0] == HEAD_COUNT
    return jax.shard_map(
        split_body if split else body,
        mesh=mesh,
        in_specs=(
            P("fsdp", "expert", None),
            P("fsdp", "expert", None),
            P("fsdp", "expert", None),
            P("fsdp"),
            P("fsdp", None),
            P("fsdp", None),
            P("fsdp"),
            P("fsdp", None),
            P("fsdp", None),
            P("fsdp"),
            P("fsdp", None),
            P(("expert", "fsdp"), None),
            P(("expert", "fsdp"), None),
            P(("expert", "fsdp"), None),
            P("expert", None, "fsdp"),
            P("expert", None, "fsdp"),
            P("expert", "fsdp", None),
        ),
        out_specs=(
            P("fsdp", "expert", None),
            P("fsdp", "expert", None),
            P("fsdp"),
            P("fsdp", None),
            P("fsdp", None),
            P("fsdp"),
            P("fsdp", None),
            P("fsdp", None),
            P("fsdp"),
            P("fsdp", None),
            P(("expert", "fsdp"), None),
            P(("expert", "fsdp"), None),
            P(("expert", "fsdp"), None),
            P("expert", None, "fsdp"),
            P("expert", None, "fsdp"),
            P("expert", "fsdp", None),
        ),
        check_vma=False,
    )
```

```python
import functools

import jax
import jax.numpy as jnp
from jax import lax
from jax.experimental import pallas as pl
from jax.experimental.pallas import tpu as pltpu
from jax.sharding import PartitionSpec as P

MODEL_WIDTH = 2048
HEAD_COUNT = 16
PLAIN_UNITS = 128
ROTARY_UNITS = 64
VALUE_UNITS = 128
LATENT_WIDTH = 512
TOPK = 6


EPS = 1e-06


def matrix_product(left, right):
    return jnp.dot(left, right, preferred_element_type=jnp.float32)


def inner(left, right):
    return lax.dot_general(
        left, right, (((0,), (0,)), ((), ())), preferred_element_type=jnp.float32
    )


def outer_product(left, right):
    return lax.dot_general(
        left, right, (((1,), (1,)), ((), ())), preferred_element_type=jnp.float32
    )


def norm_forward(value, gain):
    inverse = lax.rsqrt(jnp.mean(value * value, axis=-1, keepdims=True) + EPS)
    return (value * inverse * gain, inverse)


def norm_backward(value, inverse, gain, grad):
    unit = value * inverse
    scaled = grad * gain
    d_value = inverse * (scaled - unit * jnp.mean(scaled * unit, axis=-1, keepdims=True))
    return (d_value, jnp.sum(grad * unit, axis=0))


def rope_tables(positions):
    half = ROTARY_UNITS // 2
    freqs = 10000.0 ** (-jnp.arange(half, dtype=jnp.float32) * (2.0 / ROTARY_UNITS))
    angles = positions.astype(jnp.float32)[:, None] * freqs[None, :]
    return (jnp.cos(angles), jnp.sin(angles))


def apply_rotary(value, cosine_table, sine_table):
    half = ROTARY_UNITS // 2
    first = value[..., :half]
    second = value[..., half:]
    return jnp.concatenate(
        [first * cosine_table - second * sine_table, first * sine_table + second * cosine_table],
        axis=-1,
    )


def reverse_rotary(grad, cosine_table, sine_table):
    half = ROTARY_UNITS // 2
    first = grad[..., :half]
    second = grad[..., half:]
    return jnp.concatenate(
        [first * cosine_table + second * sine_table, second * cosine_table - first * sine_table],
        axis=-1,
    )


def silu_parts(value):
    sigma = jax.nn.sigmoid(value)
    return (value * sigma, sigma * (1.0 + value * (1.0 - sigma)))


def body(
    tokens,
    routes,
    cotangent,
    attn_gain,
    w_query,
    latent_weight,
    latent_norm_gain,
    expand_weight,
    w_out,
    ffn_gain,
    w_router,
    shared_gate,
    shared_up,
    shared_down,
    expert_gate,
    expert_up,
    expert_down,
):
    device_local = tokens.shape[1]
    experts = lax.axis_size("expert")
    shards = lax.axis_size("fsdp")
    position = lax.axis_index("expert")
    capacity = shards * (
        (device_local * TOPK * 4 + experts * 3 * shards - 1) // (experts * 3 * shards)
    )
    seq_len = device_local * experts
    feature_width = LATENT_WIDTH + ROTARY_UNITS
    scale = (PLAIN_UNITS + ROTARY_UNITS) ** (-0.5)
    attention_gain_grad, wq, wlat, g_lat, expand_matrix, wout, g_ffn, wrout = (
        lax.all_gather(attn_gain, "fsdp", axis=0, tiled=True),
        lax.all_gather(w_query, "fsdp", axis=0, tiled=True),
        lax.all_gather(latent_weight, "fsdp", axis=0, tiled=True),
        lax.all_gather(latent_norm_gain, "fsdp", axis=0, tiled=True),
        lax.all_gather(expand_weight, "fsdp", axis=0, tiled=True),
        lax.all_gather(w_out, "fsdp", axis=0, tiled=True),
        lax.all_gather(ffn_gain, "fsdp", axis=0, tiled=True),
        lax.all_gather(w_router, "fsdp", axis=0, tiled=True),
    )
    sgate, sup, sdown = (
        lax.all_gather(shared_gate, ("expert", "fsdp"), axis=0, tiled=True),
        lax.all_gather(shared_up, ("expert", "fsdp"), axis=0, tiled=True),
        lax.all_gather(shared_down, ("expert", "fsdp"), axis=0, tiled=True),
    )
    attention_gain_grad = attention_gain_grad.astype(jnp.float32)
    g_lat = g_lat.astype(jnp.float32)
    g_ffn = g_ffn.astype(jnp.float32)
    x_in = tokens[0].astype(jnp.float32)
    grad_out = cotangent[0].astype(jnp.float32)
    positions = position * device_local + jnp.arange(device_local, dtype=jnp.int32)
    cosine_table, sine_table = rope_tables(positions)
    normed, inv_attn = norm_forward(x_in, attention_gain_grad)
    normed_in = normed.astype(jnp.bfloat16)
    query_full = matrix_product(normed_in, wq).reshape(
        device_local, HEAD_COUNT, PLAIN_UNITS + ROTARY_UNITS
    )
    query_nope = query_full[:, :, :PLAIN_UNITS].astype(jnp.bfloat16)
    expanded_latent = expand_matrix.reshape(LATENT_WIDTH, HEAD_COUNT, PLAIN_UNITS + VALUE_UNITS)
    key_part = expanded_latent[:, :, :PLAIN_UNITS]
    value_part = expanded_latent[:, :, PLAIN_UNITS:]
    query_latent = jnp.einsum(
        "thd,chd->thc", query_nope, key_part, preferred_element_type=jnp.float32
    )
    query_rope = apply_rotary(
        query_full[:, :, PLAIN_UNITS:], cosine_table[:, None, :], sine_table[:, None, :]
    )
    token_rows = device_local * HEAD_COUNT
    query = (
        jnp.concatenate([query_latent, query_rope], axis=-1)
        .astype(jnp.bfloat16)
        .reshape(token_rows, feature_width)
    )
    latent_complete = matrix_product(normed_in, wlat)
    packed_rows = latent_complete[:, :LATENT_WIDTH]
    latent_state, inv_lat = norm_forward(packed_rows, g_lat)
    rotary_key = apply_rotary(latent_complete[:, LATENT_WIDTH:], cosine_table, sine_table)
    key = jnp.concatenate([latent_state, rotary_key], axis=-1).astype(jnp.bfloat16)
    keys_all = lax.all_gather(key, "expert", axis=0, tiled=True)
    block = min(512, seq_len)
    token_tally = (position * device_local + device_local + block - 1) // block
    q_pos = position * device_local + jnp.arange(token_rows, dtype=jnp.int32) // HEAD_COUNT

    def scores_of(index):
        key_rows = lax.dynamic_slice_in_dim(keys_all, index * block, block, 0)
        raw = outer_product(query, key_rows)
        k_pos = index * block + jnp.arange(block, dtype=jnp.int32)
        valid = k_pos[None, :] <= q_pos[:, None]
        return (jnp.where(valid, raw * scale, -1e30), key_rows)

    def stats_step(index, carry):
        top, total = carry
        scores, unused = scores_of(index)
        new_top = jnp.maximum(top, jnp.max(scores, axis=1))
        total = total * jnp.exp(top - new_top) + jnp.sum(jnp.exp(scores - new_top[:, None]), axis=1)
        return (new_top, total)

    top, total = lax.fori_loop(
        0,
        token_tally,
        stats_step,
        (jnp.full((token_rows,), -1e30, jnp.float32), jnp.zeros((token_rows,), jnp.float32)),
    )
    log_total = top + jnp.log(total)

    def mixing_update(index, running_total):
        scores, key_rows = scores_of(index)
        weight_arrays = jnp.exp(scores - log_total[:, None]).astype(jnp.bfloat16)
        return running_total + matrix_product(weight_arrays, key_rows[:, :LATENT_WIDTH])

    mixed_output_sum = lax.fori_loop(
        0, token_tally, mixing_update, jnp.zeros((token_rows, LATENT_WIDTH), jnp.float32)
    )
    mixed_output = mixed_output_sum.astype(jnp.bfloat16).reshape(
        device_local, HEAD_COUNT, LATENT_WIDTH
    )
    heads = jnp.einsum("thc,chv->thv", mixed_output, value_part, preferred_element_type=jnp.float32)
    heads = heads.reshape(device_local, HEAD_COUNT * VALUE_UNITS).astype(jnp.bfloat16)
    hidden = x_in + matrix_product(heads, wout)
    normed2, inv_ffn = norm_forward(hidden, g_ffn)
    normed_ffn = normed2.astype(jnp.bfloat16)
    logits = matrix_product(normed_ffn, wrout)
    router = jax.nn.softmax(logits, axis=-1)
    own_routes = routes[0]
    names = jnp.arange(experts, dtype=jnp.int32)
    chosen = (own_routes[:, :, None] == names[None, None, :]).astype(jnp.float32)
    gates = jnp.sum(chosen * router[:, None, :], axis=-1)
    hits = (own_routes.reshape(device_local * TOPK)[:, None] == names[None, :]).astype(jnp.int32)
    slot = jnp.sum((jnp.cumsum(hits, axis=0) - hits) * hits, axis=1)
    place = own_routes.reshape(device_local * TOPK) * capacity + slot
    token_of = jnp.arange(device_local * TOPK, dtype=jnp.int32) // TOPK
    table = jnp.full((experts * capacity,), device_local, jnp.int32).at[place].set(token_of)
    padded = jnp.concatenate([normed_ffn, jnp.zeros((1, MODEL_WIDTH), jnp.bfloat16)], axis=0)
    buffer = padded[table].reshape(experts, capacity, MODEL_WIDTH)
    w_g, w_u, w_d = (expert_gate[0], expert_up[0], expert_down[0])

    def spread(values):
        return jnp.broadcast_to(values[:, None], (experts, shards, capacity, MODEL_WIDTH)).reshape(
            experts * shards, capacity, MODEL_WIDTH
        )

    def collect(back):
        return jnp.sum(back.reshape(experts, shards, capacity, MODEL_WIDTH), axis=1).reshape(
            experts * capacity, MODEL_WIDTH
        )

    received = lax.all_to_all(
        spread(buffer), ("expert", "fsdp"), split_axis=0, concat_axis=0, tiled=True
    )
    ex_rows = received.reshape(-1, MODEL_WIDTH)
    pre_gate = matrix_product(ex_rows, w_g)
    pre_up = matrix_product(ex_rows, w_u)
    act_gate, slope = silu_parts(pre_gate)
    ex_act = (act_gate * pre_up).astype(jnp.bfloat16)
    ex_out = matrix_product(ex_act, w_d).reshape(received.shape)
    returned = lax.all_to_all(
        ex_out.astype(jnp.bfloat16), ("expert", "fsdp"), split_axis=0, concat_axis=0, tiled=True
    ).astype(ex_out.dtype)
    results = collect(returned)
    picked = results[place].reshape(device_local, TOPK, MODEL_WIDTH)
    routed = jnp.sum(gates[:, :, None] * picked, axis=1)
    sh_gate = matrix_product(normed_ffn, sgate)
    sh_up = matrix_product(normed_ffn, sup)
    sh_silu, sh_slope = silu_parts(sh_gate)
    sh_act = (sh_silu * sh_up).astype(jnp.bfloat16)
    shared = matrix_product(sh_act, sdown)
    output = hidden + routed + shared
    d_shared = grad_out.astype(jnp.bfloat16)
    shared_down_gradient = inner(sh_act, d_shared)
    d_sh_act = outer_product(d_shared, sdown)
    d_sh_gate = (d_sh_act * sh_up * sh_slope).astype(jnp.bfloat16)
    d_sh_up = (d_sh_act * sh_silu).astype(jnp.bfloat16)
    shared_gate_gradient = inner(normed_ffn, d_sh_gate)
    shared_up_gradient = inner(normed_ffn, d_sh_up)
    d_normed_ffn = outer_product(d_sh_gate, sgate) + outer_product(d_sh_up, sup)
    d_picked = (
        (gates[:, :, None] * grad_out[:, None, :])
        .astype(jnp.bfloat16)
        .reshape(device_local * TOPK, MODEL_WIDTH)
    )
    d_gates = jnp.sum(picked * grad_out[:, None, :], axis=2)
    d_buffer = (
        jnp.zeros((experts * capacity, MODEL_WIDTH), jnp.bfloat16)
        .at[place]
        .set(d_picked)
        .reshape(experts, capacity, MODEL_WIDTH)
    )
    d_received = lax.all_to_all(
        spread(d_buffer), ("expert", "fsdp"), split_axis=0, concat_axis=0, tiled=True
    )
    d_rows = d_received.reshape(-1, MODEL_WIDTH)
    d_act = outer_product(d_rows, w_d)
    g_down = inner(ex_act, d_rows)
    d_pre_gate = (d_act * pre_up * slope).astype(jnp.bfloat16)
    d_pre_up = (d_act * act_gate).astype(jnp.bfloat16)
    g_gate = inner(ex_rows, d_pre_gate)
    g_up = inner(ex_rows, d_pre_up)
    d_ex_rows = (outer_product(d_pre_gate, w_g) + outer_product(d_pre_up, w_u)).reshape(
        received.shape
    )
    d_returned = lax.all_to_all(
        d_ex_rows.astype(jnp.bfloat16), ("expert", "fsdp"), split_axis=0, concat_axis=0, tiled=True
    ).astype(d_ex_rows.dtype)
    d_results = collect(d_returned)
    d_normed_ffn = d_normed_ffn + jnp.sum(
        d_results[place].reshape(device_local, TOPK, MODEL_WIDTH), axis=1
    )
    d_router = jnp.sum(chosen * d_gates[:, :, None], axis=1)
    d_logits = (router * (d_router - jnp.sum(router * d_router, axis=1, keepdims=True))).astype(
        jnp.bfloat16
    )
    router_weight_gradient = inner(normed_ffn, d_logits)
    d_normed_ffn = d_normed_ffn + outer_product(d_logits, wrout)
    d_hidden_norm, g_ffn_grad = norm_backward(hidden, inv_ffn, g_ffn, d_normed_ffn)
    d_hidden = grad_out + d_hidden_norm
    d_attn = d_hidden.astype(jnp.bfloat16)
    output_weight_gradient = inner(heads, d_attn)
    d_heads = (
        outer_product(d_attn, wout)
        .astype(jnp.bfloat16)
        .reshape(device_local, HEAD_COUNT, VALUE_UNITS)
    )
    value_weight_gradient = jnp.einsum(
        "thc,thv->chv", mixed_output, d_heads, preferred_element_type=jnp.float32
    )
    mixed_gradient = jnp.einsum(
        "thv,chv->thc", d_heads, value_part, preferred_element_type=jnp.float32
    )
    mixed_gradient = mixed_gradient.astype(jnp.bfloat16).reshape(token_rows, LATENT_WIDTH)
    delta = jnp.sum(mixed_gradient.astype(jnp.float32) * mixed_output_sum, axis=1)

    def back_step(index, carry):
        d_query_acc, d_keys_acc = carry
        scores, key_rows = scores_of(index)
        weight_arrays = jnp.exp(scores - log_total[:, None])
        weight_gradients = outer_product(mixed_gradient, key_rows[:, :LATENT_WIDTH])
        d_scores = (weight_arrays * (weight_gradients - delta[:, None]) * scale).astype(
            jnp.bfloat16
        )
        d_query_acc = d_query_acc + matrix_product(d_scores, key_rows)
        d_values = inner(weight_arrays.astype(jnp.bfloat16), mixed_gradient)
        d_block = inner(d_scores, query) + jnp.concatenate(
            [d_values, jnp.zeros((block, ROTARY_UNITS), jnp.float32)], axis=1
        )
        previous = lax.dynamic_slice_in_dim(d_keys_acc, index * block, block, 0)
        return (
            d_query_acc,
            lax.dynamic_update_slice_in_dim(d_keys_acc, previous + d_block, index * block, 0),
        )

    d_query, d_keys = lax.fori_loop(
        0,
        token_tally,
        back_step,
        (
            jnp.zeros((token_rows, feature_width), jnp.float32),
            jnp.zeros((seq_len, feature_width), jnp.float32),
        ),
    )
    key_gradient = lax.psum_scatter(
        d_keys.astype(jnp.bfloat16), "expert", scatter_dimension=0, tiled=True
    )
    query_up_gradient = d_query.astype(jnp.bfloat16).reshape(
        device_local, HEAD_COUNT, feature_width
    )
    query_latent_gradient = query_up_gradient[:, :, :LATENT_WIDTH]
    key_weight_gradient = jnp.einsum(
        "thc,thd->chd", query_latent_gradient, query_nope, preferred_element_type=jnp.float32
    )
    d_q_nope = jnp.einsum(
        "thc,chd->thd", query_latent_gradient, key_part, preferred_element_type=jnp.float32
    )
    d_q_rope = reverse_rotary(
        query_up_gradient[:, :, LATENT_WIDTH:].astype(jnp.float32),
        cosine_table[:, None, :],
        sine_table[:, None, :],
    )
    d_query_full = (
        jnp.concatenate([d_q_nope, d_q_rope], axis=-1)
        .astype(jnp.bfloat16)
        .reshape(device_local, HEAD_COUNT * (PLAIN_UNITS + ROTARY_UNITS))
    )
    query_weight_gradient = inner(normed_in, d_query_full)
    d_normed_in = outer_product(d_query_full, wq)
    latent_gradient = key_gradient[:, :LATENT_WIDTH].astype(jnp.float32)
    rotary_key_gradient = reverse_rotary(
        key_gradient[:, LATENT_WIDTH:].astype(jnp.float32), cosine_table, sine_table
    )
    d_compact, g_lat_grad = norm_backward(packed_rows, inv_lat, g_lat, latent_gradient)
    d_latent_full = jnp.concatenate([d_compact, rotary_key_gradient], axis=-1).astype(jnp.bfloat16)
    latent_weight_gradient = inner(normed_in, d_latent_full)
    d_normed_in = d_normed_in + outer_product(d_latent_full, wlat)
    d_norm_in, g_attn_grad = norm_backward(x_in, inv_attn, attention_gain_grad, d_normed_in)
    d_tokens = (d_hidden + d_norm_in).astype(jnp.bfloat16)
    expand_weight_gradient = jnp.concatenate(
        [key_weight_gradient, value_weight_gradient], axis=-1
    ).reshape(LATENT_WIDTH, HEAD_COUNT * (PLAIN_UNITS + VALUE_UNITS))
    r_sgate, r_sup, r_sdown = (
        lax.psum_scatter(shared_gate_gradient, ("expert", "fsdp"), scatter_dimension=0, tiled=True),
        lax.psum_scatter(shared_up_gradient, ("expert", "fsdp"), scatter_dimension=0, tiled=True),
        lax.psum_scatter(shared_down_gradient, ("expert", "fsdp"), scatter_dimension=0, tiled=True),
    )
    r_attn, r_query, r_latent, r_lgain, r_expand, r_out, r_fgain, r_router = (
        lax.psum_scatter(
            g_attn_grad.astype(jnp.bfloat16), "fsdp", scatter_dimension=0, tiled=True
        ).astype(jnp.float32),
        lax.psum_scatter(
            query_weight_gradient.astype(jnp.bfloat16), "fsdp", scatter_dimension=0, tiled=True
        ).astype(jnp.float32),
        lax.psum_scatter(
            latent_weight_gradient.astype(jnp.bfloat16), "fsdp", scatter_dimension=0, tiled=True
        ).astype(jnp.float32),
        lax.psum_scatter(
            g_lat_grad.astype(jnp.bfloat16), "fsdp", scatter_dimension=0, tiled=True
        ).astype(jnp.float32),
        lax.psum_scatter(
            expand_weight_gradient.astype(jnp.bfloat16), "fsdp", scatter_dimension=0, tiled=True
        ).astype(jnp.float32),
        lax.psum_scatter(
            output_weight_gradient.astype(jnp.bfloat16), "fsdp", scatter_dimension=0, tiled=True
        ).astype(jnp.float32),
        lax.psum_scatter(
            g_ffn_grad.astype(jnp.bfloat16), "fsdp", scatter_dimension=0, tiled=True
        ).astype(jnp.float32),
        lax.psum_scatter(
            router_weight_gradient.astype(jnp.bfloat16), "fsdp", scatter_dimension=0, tiled=True
        ).astype(jnp.float32),
    )
    r_attn, r_query, r_latent, r_lgain, r_expand, r_out, r_fgain, r_router = (
        lax.psum(r_attn.astype(jnp.bfloat16), "expert").astype(jnp.float32),
        lax.psum(r_query.astype(jnp.bfloat16), "expert").astype(jnp.float32),
        lax.psum(r_latent.astype(jnp.bfloat16), "expert").astype(jnp.float32),
        lax.psum(r_lgain.astype(jnp.bfloat16), "expert").astype(jnp.float32),
        lax.psum(r_expand.astype(jnp.bfloat16), "expert").astype(jnp.float32),
        lax.psum(r_out.astype(jnp.bfloat16), "expert").astype(jnp.float32),
        lax.psum(r_fgain.astype(jnp.bfloat16), "expert").astype(jnp.float32),
        lax.psum(r_router.astype(jnp.bfloat16), "expert").astype(jnp.float32),
    )
    return (
        output.astype(jnp.bfloat16)[None],
        d_tokens[None],
        r_attn,
        r_query,
        r_latent,
        r_lgain,
        r_expand,
        r_out,
        r_fgain,
        r_router,
        r_sgate,
        r_sup,
        r_sdown,
        g_gate[None],
        g_up[None],
        g_down[None],
    )


LINE = 4
SQUARE = 2
CORES = 2
MESH = pl.DeviceIdType.MESH
VMEM_LIMIT = 56 * 1024 * 1024


class Place:
    def __init__(self):
        index = lax.axis_index("expert")
        self.y = lax.axis_index("fsdp")
        self.c = lax.rem(index, CORES)
        self.b = lax.rem(lax.div(index, CORES), SQUARE)
        self.a = lax.div(index, CORES * SQUARE)

    def device(self, da=0, db=0, dc=0, dy=0):
        b = 1 - self.b if db else self.b
        c = 1 - self.c if dc else self.c
        y = 1 - self.y if dy else self.y
        return (((self.a + da) * SQUARE + b) * CORES + c, y)

    def block(self, full, a, db=0, dc=0, dy=0):
        b = 1 - self.b if db else self.b
        c = 1 - self.c if dc else self.c
        y = 1 - self.y if dy else self.y
        flat = (a * SQUARE + b) * CORES + c
        return y * (LINE * SQUARE * CORES) + flat if full else flat

    def greet(self, with_y):
        barrier = pltpu.get_barrier_semaphore()
        near = [dict(db=1), dict(dc=1)] + ([dict(dy=1)] if with_y else [])
        for step in near:
            pl.semaphore_signal(barrier, inc=1, device_id=self.device(**step), device_id_type=MESH)

        @pl.when(self.a > 0)
        def _():
            pl.semaphore_signal(barrier, inc=1, device_id=self.device(da=-1), device_id_type=MESH)

        @pl.when(self.a < LINE - 1)
        def _():
            pl.semaphore_signal(barrier, inc=1, device_id=self.device(da=1), device_id_type=MESH)

        ends = jnp.logical_or(self.a == 0, self.a == LINE - 1).astype(jnp.int32)
        pl.semaphore_wait(barrier, len(near) + 2 - ends)


class Sender:
    def __init__(self, place, sems):
        self.place, self.sems, self.pending = place, sems, []

    def send(self, src, dst, recv_sem, step, cond=None):
        sem = self.sems.at[len(self.pending)]

        def make():
            return pltpu.make_async_remote_copy(
                src_ref=src,
                dst_ref=dst,
                send_sem=sem,
                recv_sem=recv_sem,
                device_id=self.place.device(**step),
                device_id_type=MESH,
            )

        def start():
            make().start()

        guarded(cond, start)
        self.pending.append((cond, lambda: make().wait_send()))

    def arrived(self, dst, recv_sem):
        pltpu.make_async_remote_copy(
            src_ref=dst,
            dst_ref=dst,
            send_sem=self.sems.at[0],
            recv_sem=recv_sem,
            device_id=self.place.device(dc=1),
            device_id_type=MESH,
        ).wait_recv()

    def finish(self):
        for cond, wait in self.pending:
            guarded(cond, wait)


def guarded(cond, action):
    if cond is None:
        action()
    else:
        pl.when(cond)(action)


def both(first, second):
    if first is None or second is None:
        return second if first is None else first
    return jnp.logical_and(first, second)


def gather_kernel(fulls, count, pairs, gated, *refs):
    ins, outs = refs[: count + pairs], refs[count + pairs : 2 * (count + pairs)]
    local_sems, send_sems, recv_sems, pair_sems = refs[2 * (count + pairs) :]
    place = Place()
    a = place.a
    sender = Sender(place, send_sems)
    some = any(fulls)
    place.greet(some or pairs > 0)
    for at in range(count, count + pairs):
        sender.send(ins[at], outs[at], pair_sems.at[at - count], dict(dy=1))

    def own_copy(at):
        return pltpu.make_async_copy(
            ins[at], outs[at].at[place.block(fulls[at], a)], local_sems.at[at]
        )

    for at in range(count):
        own_copy(at).start()

    def chunk(at, block, half):
        size = ins[at].shape[0] // 2
        return outs[at].at[block, pl.ds(half * size, size)]

    def sem_of(at, block, half):
        return recv_sems.at[at, block * 2 + half]

    def forward(at, block, half, src, step, cond=None):
        sender.send(src, chunk(at, block, half), sem_of(at, block, half), step, cond)

    def receive(at, block, half, cond):
        guarded(cond, lambda: sender.arrived(chunk(at, block, half), sem_of(at, block, half)))

    def held_by(at, delta, cond):
        if at not in gated:
            return cond
        return both(cond, lax.div(a + delta, LINE // 2) == place.y)

    def from_line(delta, always):
        for half in range(2):
            for at in range(count):
                full = fulls[at]
                block = place.block(full, a + delta)
                cond = held_by(at, delta, always)
                size = ins[at].shape[0] // 2
                if delta == 0:
                    src = ins[at].at[pl.ds(half * size, size)]
                else:
                    receive(at, block, half, cond)
                    src = chunk(at, block, half)
                if delta <= 0:
                    forward(at, block, half, src, dict(da=1), both(cond, a < LINE - 1))
                if delta >= 0:
                    forward(at, block, half, src, dict(da=-1), both(cond, a > 0))
                forward(at, block, half, src, dict(db=1), cond)
                if full:
                    forward(at, block, half, src, dict(dy=1), cond)
                forward(at, block, half, src, dict(dc=1), cond)

    def from_side(delta, always):
        for half in range(2):
            for at in range(count):
                full = fulls[at]
                cond = held_by(at, delta, always)
                block = place.block(full, a + delta, db=1)
                receive(at, block, half, cond)
                if full and half == 0:
                    forward(at, block, half, chunk(at, block, half), dict(dy=1), cond)
                forward(at, block, half, chunk(at, block, half), dict(dc=1), cond)
                if full:
                    block = place.block(full, a + delta, dy=1)
                    receive(at, block, half, cond)
                    if half == 1:
                        forward(at, block, half, chunk(at, block, half), dict(db=1), cond)
                    forward(at, block, half, chunk(at, block, half), dict(dc=1), cond)

    def from_corner(delta, always):
        for half in range(2):
            for at in range(count):
                if not fulls[at]:
                    continue
                cond = held_by(at, delta, always)
                block = place.block(True, a + delta, db=1, dy=1)
                receive(at, block, half, cond)
                forward(at, block, half, chunk(at, block, half), dict(dc=1), cond)

    def from_sibling(delta, always):
        for half in range(2):
            for at in range(count):
                full = fulls[at]
                cond = held_by(at, delta, always)
                for db in range(2):
                    for dy in range(2 if full else 1):
                        receive(at, place.block(full, a + delta, db=db, dc=1, dy=dy), half, cond)

    rounds = [[(0, None)]]
    for s in range(1, LINE):
        rounds.append([(-s, a >= s), (s, a + s < LINE)])
    stages = [from_line, from_side] + ([from_corner] if some else []) + [from_sibling]
    for tick in range(len(rounds) + len(stages) - 1):
        for level, stage in enumerate(stages):
            if 0 <= tick - level < len(rounds):
                for delta, cond in rounds[tick - level]:
                    stage(delta, cond)
    for at in range(count, count + pairs):
        sender.arrived(outs[at], pair_sems.at[at - count])
    for at in range(count):
        own_copy(at).wait()
    sender.finish()


def gather_rows(arrays, full, collective_id, swapped=(), gated=()):
    count, pairs = len(arrays), len(swapped)
    fulls = full if isinstance(full, tuple) else (full,) * count
    sizes = [LINE * SQUARE * CORES * (SQUARE if reach else 1) for reach in fulls]
    blocks = max(sizes)
    lines = 2 * LINE - 1
    sends = pairs + count * lines * 2 * (9 if any(fulls) else 5)
    moved = sum(blocks * 2 * x.size * x.dtype.itemsize for x in arrays)
    return pl.pallas_call(
        functools.partial(gather_kernel, fulls, count, pairs, gated),
        out_shape=[jax.ShapeDtypeStruct((n,) + x.shape, x.dtype) for n, x in zip(sizes, arrays)]
        + [jax.ShapeDtypeStruct(x.shape, x.dtype) for x in swapped],
        in_specs=[pl.BlockSpec(memory_space=pl.ANY)] * (count + pairs),
        out_specs=[pl.BlockSpec(memory_space=pl.ANY)] * (count + pairs),
        scratch_shapes=[
            pltpu.SemaphoreType.DMA((count,)),
            pltpu.SemaphoreType.DMA((sends,)),
            pltpu.SemaphoreType.DMA((count, blocks * 2)),
            pltpu.SemaphoreType.DMA((max(pairs, 1),)),
        ],
        compiler_params=pltpu.CompilerParams(collective_id=collective_id, has_side_effects=True),
        cost_estimate=pl.CostEstimate(flops=0, bytes_accessed=6 * moved, transcendentals=0),
    )(*arrays, *swapped)


def add_rows(target, sources, size):
    def step(at, carry):
        rows = pl.ds(pl.multiple_of(at * 16, 16), 16)
        total = sources[0][rows, :].astype(jnp.float32)
        for source in sources[1:]:
            total = total + source[rows, :].astype(jnp.float32)
        target[rows, :] = total.astype(target.dtype)
        return carry

    lax.fori_loop(0, size // 16, step, 0)


def scatter_kernel(full, pairs, part, *refs):
    ins, out, outs = refs[:pairs], refs[pairs], refs[pairs + 1 : 2 * pairs + 1]
    mine, got, side, up, down, load_sems, send_sems, recv_sems, pair_sems = refs[2 * pairs + 1 :]
    place = Place()
    a = place.a
    kinds = 4 if full else 2
    size = part.shape[1]
    half = size // 2
    sender = Sender(place, send_sems)
    place.greet(full or pairs > 0)
    for at in range(pairs):
        sender.send(ins[at], outs[at], pair_sems.at[at], dict(dy=1))
    order = [LINE - 1, 0, LINE - 2, 1]
    walk = (3, 1, 2, 0) if full else (1, 0)

    def sem_of(group, target, kind):
        return recv_sems.at[group, target * 4 + kind]

    def load(target, kind):
        block = place.block(full, target, db=kind % 2, dy=kind // 2)
        return pltpu.make_async_copy(
            part.at[block], mine.at[target, kind], load_sems.at[target * 4 + kind]
        )

    for target in order:
        for kind in walk:
            load(target, kind).start()
            block = place.block(full, target, db=kind % 2, dc=1, dy=kind // 2)
            sender.send(
                part.at[block], got.at[target, kind], sem_of(0, target, kind), dict(dc=1)
            )

    def rows_of(ref, which):
        return ref.at[pl.ds(which * half, half)]

    def over_cores(target):
        for kind in walk:
            load(target, kind).wait()
            sender.arrived(got.at[target, kind], sem_of(0, target, kind))
            add_rows(mine.at[target, kind], [mine.at[target, kind], got.at[target, kind]], size)
            held = mine.at[target, kind]
            if kind == 3:
                sender.send(rows_of(held, 0), side.at[target, 4], sem_of(1, target, 0), dict(db=1))
                sender.send(rows_of(held, 1), side.at[target, 5], sem_of(1, target, 1), dict(dy=1))
            if kind == 1:
                sender.send(rows_of(held, 0), side.at[target, 0], sem_of(2, target, 0), dict(db=1))
                if not full:
                    sender.send(
                        rows_of(held, 1), side.at[target, 1], sem_of(2, target, 1), dict(db=1)
                    )
            if kind == 2:
                sender.send(rows_of(held, 1), side.at[target, 3], sem_of(2, target, 3), dict(dy=1))

    def over_corner(target):
        sender.arrived(side.at[target, 4], sem_of(1, target, 0))
        held = rows_of(mine.at[target, 2], 0)
        add_rows(held, [held, side.at[target, 4]], half)
        sender.send(held, side.at[target, 2], sem_of(2, target, 2), dict(dy=1))
        sender.arrived(side.at[target, 5], sem_of(1, target, 1))
        held = rows_of(mine.at[target, 1], 1)
        add_rows(held, [held, side.at[target, 5]], half)
        sender.send(held, side.at[target, 1], sem_of(2, target, 1), dict(db=1))

    def over_line(target):
        for which in range(2):
            held = rows_of(mine.at[target, 0], which)
            parts = [held]
            for source in (0, 2) if full else (0,):
                sender.arrived(side.at[target, source + which], sem_of(2, target, source + which))
                parts.append(side.at[target, source + which])
            below, above = rows_of(up.at[target], which), rows_of(down.at[target], which)
            below_sem, above_sem = sem_of(3, target, which), sem_of(3, target, 2 + which)

            def upward(with_below):
                extra = []
                if with_below:
                    sender.arrived(below, below_sem)
                    extra = [below]
                add_rows(held, parts + extra, half)

            def downward(with_above):
                extra = []
                if with_above:
                    sender.arrived(above, above_sem)
                    extra = [above]
                add_rows(held, parts + extra, half)

            if target > 0:
                pl.when(jnp.logical_and(a < target, a > 0))(lambda: upward(True))
                pl.when(a == 0)(lambda: upward(False))
                sender.send(held, below, below_sem, dict(da=1), a < target)
            if target < LINE - 1:
                pl.when(jnp.logical_and(a > target, a < LINE - 1))(lambda: downward(True))
                pl.when(a == LINE - 1)(lambda: downward(False))
                sender.send(held, above, above_sem, dict(da=-1), a > target)

            def last():
                extra = []
                if target > 0:
                    sender.arrived(below, below_sem)
                    extra.append(below)
                if target < LINE - 1:
                    sender.arrived(above, above_sem)
                    extra.append(above)
                add_rows(rows_of(out, which), parts + extra, half)

            pl.when(a == target)(last)

    stages = [over_cores] + ([over_corner] if full else []) + [over_line]
    for tick in range(len(order) + len(stages) - 1):
        for level, stage in enumerate(stages):
            if 0 <= tick - level < len(order):
                stage(order[tick - level])
    for at in range(pairs):
        sender.arrived(outs[at], pair_sems.at[at])
    sender.finish()


def scatter_rows(part, full, collective_id, swapped=()):
    blocks, rows, width = part.shape
    kinds = 4 if full else 2
    half = rows // 2
    pairs = len(swapped)
    return pl.pallas_call(
        functools.partial(scatter_kernel, full, pairs),
        out_shape=[jax.ShapeDtypeStruct((rows, width), jnp.float32)]
        + [jax.ShapeDtypeStruct(x.shape, x.dtype) for x in swapped],
        in_specs=[pl.BlockSpec(memory_space=pl.ANY)] * (1 + pairs),
        out_specs=[pl.BlockSpec(memory_space=pltpu.VMEM)]
        + [pl.BlockSpec(memory_space=pl.ANY)] * pairs,
        scratch_shapes=[
            pltpu.VMEM((LINE, kinds, rows, width), part.dtype),
            pltpu.VMEM((LINE, kinds, rows, width), part.dtype),
            pltpu.VMEM((LINE, 6, half, width), part.dtype),
            pltpu.VMEM((LINE, rows, width), part.dtype),
            pltpu.VMEM((LINE, rows, width), part.dtype),
            pltpu.SemaphoreType.DMA((LINE * 4,)),
            pltpu.SemaphoreType.DMA((pairs + LINE * (4 + 6 + 4),)),
            pltpu.SemaphoreType.DMA((4, LINE * 4)),
            pltpu.SemaphoreType.DMA((max(pairs, 1),)),
        ],
        compiler_params=pltpu.CompilerParams(
            collective_id=collective_id, has_side_effects=True, vmem_limit_bytes=VMEM_LIMIT
        ),
        cost_estimate=pl.CostEstimate(
            flops=0, bytes_accessed=12 * part.size * part.dtype.itemsize, transcendentals=0
        ),
    )(part, *swapped)


def contract_last(left, right):
    return lax.dot_general(
        left, right, (((1,), (1,)), ((), ())), preferred_element_type=jnp.float32
    )


def contract_first(left, right):
    return lax.dot_general(
        left, right, (((0,), (0,)), ((), ())), preferred_element_type=jnp.float32
    )


def expert_kernel(
    capacity,
    normed,
    grads,
    places,
    router_cols,
    w_gate,
    w_up,
    w_down,
    shared_in,
    shared_out,
    out_part,
    d_part,
    ex_rows,
    ex_grads,
    act_out,
    d_gate_out,
    d_up_out,
    shared_in_grad,
    shared_out_grad,
    in_total,
    out_total,
):
    position = lax.axis_index("expert")
    experts = lax.axis_size("expert")
    group, rows, width = normed.shape
    tokens, slots = group * rows, group * capacity
    bf16 = jnp.bfloat16
    x = normed[...].reshape(tokens, width)
    g = grads[...].reshape(tokens, width)

    slot = lax.broadcasted_iota(jnp.int32, (slots, tokens), 0)
    token = lax.broadcasted_iota(jnp.int32, (slots, tokens), 1)
    same = lax.div(slot, capacity) == lax.div(token, rows)
    place = jnp.broadcast_to(places[0], (slots, tokens))
    hit = jnp.logical_and(same, lax.rem(slot, capacity) == place)
    pick = jnp.where(hit, 1.0, 0.0).astype(bf16)

    r = matrix_product(pick, x).astype(bf16)
    gr = matrix_product(pick, g).astype(bf16)
    ex_rows[...] = r
    ex_grads[...] = gr
    lane = lax.broadcasted_iota(jnp.int32, (slots, router_cols.shape[1]), 1)
    logits = jnp.where(lane < experts, matrix_product(r, router_cols[...]), -1e30)
    exps = jnp.exp(logits - jnp.max(logits, axis=1, keepdims=True))
    gate = jnp.sum(jnp.where(lane == position, exps, 0.0), axis=1, keepdims=True) / jnp.sum(
        exps, axis=1, keepdims=True
    )

    pre_gate = matrix_product(r, w_gate[...])
    pre_up = matrix_product(r, w_up[...])
    act_gate, slope = silu_parts(pre_gate)
    act = act_gate * pre_up
    back = contract_last(gr, w_down[...])
    d_gate_slot = jnp.sum(act * back, axis=1, keepdims=True)
    scaled = (gate * act).astype(bf16)
    d_act = gate * back
    d_pre_gate = (d_act * pre_up * slope).astype(bf16)
    d_pre_up = (d_act * act_gate).astype(bf16)
    act_out[...] = scaled
    d_gate_out[...] = d_pre_gate
    d_up_out[...] = d_pre_up
    ex_out = matrix_product(scaled, w_down[...]).astype(bf16)
    d_ex = contract_last(d_pre_gate, w_gate[...]) + contract_last(d_pre_up, w_up[...])
    d_ex = d_ex.astype(bf16)

    units = shared_out.shape[0]
    mix = matrix_product(x, shared_in[...])
    sh_gate, sh_up = mix[:, :units], mix[:, units:]
    sh_silu, sh_slope = silu_parts(sh_gate)
    sh_act = (sh_silu * sh_up).astype(bf16)
    d_sh_act = contract_last(g, shared_out[...])
    d_mix = jnp.concatenate([d_sh_act * sh_up * sh_slope, d_sh_act * sh_silu], axis=1)
    d_mix = d_mix.astype(bf16)

    out = contract_first(pick, ex_out) + matrix_product(sh_act, shared_out[...])
    out_part[...] = out.astype(bf16).reshape(group, rows, width)
    d_in = contract_first(pick, d_ex) + contract_last(d_mix, shared_in[...])
    d_part[:, :, :width] = d_in.astype(bf16).reshape(group, rows, width)
    column = jnp.where(lane == position, d_gate_slot, 0.0).astype(bf16)
    d_part[:, :, width:] = contract_first(pick, column).astype(bf16).reshape(group, rows, -1)

    step = pl.program_id(0)

    @pl.when(step == 0)
    def _():
        in_total[...] = jnp.zeros_like(in_total)
        out_total[...] = jnp.zeros_like(out_total)

    in_total[...] += contract_first(d_mix, x)
    out_total[...] += contract_first(sh_act, g)

    @pl.when(step == pl.num_programs(0) - 1)
    def _():
        shared_in_grad[...] = in_total[...]
        shared_out_grad[...] = out_total[...]


def expert_phase(
    all_normed, all_grads, places, router_cols, w_gate, w_up, w_down, shared_in, shared_out, capacity
):
    blocks, rows, width = all_normed.shape
    group = 4
    slots = group * capacity
    hidden = w_gate.shape[1]
    units = shared_out.shape[0]
    side = router_cols.shape[1]
    bf16 = jnp.bfloat16

    def by_group(shape):
        zeros = (0,) * (len(shape) - 1)
        return pl.BlockSpec(shape, lambda i: (i,) + zeros)

    def fixed(shape):
        return pl.BlockSpec(
            shape, lambda i: (0,) * len(shape), pipeline_mode=pl.Buffered(buffer_count=1)
        )

    return pl.pallas_call(
        functools.partial(expert_kernel, capacity),
        grid=(blocks // group,),
        out_shape=[
            jax.ShapeDtypeStruct((blocks, rows, width), bf16),
            jax.ShapeDtypeStruct((blocks, rows, width + side), bf16),
            jax.ShapeDtypeStruct((blocks * capacity, width), bf16),
            jax.ShapeDtypeStruct((blocks * capacity, width), bf16),
            jax.ShapeDtypeStruct((blocks * capacity, hidden), bf16),
            jax.ShapeDtypeStruct((blocks * capacity, hidden), bf16),
            jax.ShapeDtypeStruct((blocks * capacity, hidden), bf16),
            jax.ShapeDtypeStruct((2 * units, width), jnp.float32),
            jax.ShapeDtypeStruct((units, width), jnp.float32),
        ],
        in_specs=[
            by_group((group, rows, width)),
            by_group((group, rows, width)),
            by_group((1, 1, group * rows)),
            fixed(router_cols.shape),
            fixed(w_gate.shape),
            fixed(w_up.shape),
            fixed(w_down.shape),
            fixed(shared_in.shape),
            fixed(shared_out.shape),
        ],
        out_specs=[
            by_group((group, rows, width)),
            by_group((group, rows, width + side)),
            by_group((slots, width)),
            by_group((slots, width)),
            by_group((slots, hidden)),
            by_group((slots, hidden)),
            by_group((slots, hidden)),
            fixed((2 * units, width)),
            fixed((units, width)),
        ],
        scratch_shapes=[
            pltpu.VMEM((2 * units, width), jnp.float32),
            pltpu.VMEM((units, width), jnp.float32),
        ],
        compiler_params=pltpu.CompilerParams(vmem_limit_bytes=VMEM_LIMIT),
        cost_estimate=pl.CostEstimate(
            flops=2 * blocks * capacity * width * hidden * 6,
            bytes_accessed=10 * blocks * rows * width * 2,
            transcendentals=blocks * capacity * hidden,
        ),
    )(all_normed, all_grads, places, router_cols, w_gate, w_up, w_down, shared_in, shared_out)


def exchange_kernel(x, out, local_sem, send_sems, recv_sems):
    me, y = lax.axis_index("expert"), lax.axis_index("fsdp")
    count = x.shape[0]
    barrier = pltpu.get_barrier_semaphore()
    peers = [lax.rem(me + step, count) for step in range(1, count)]
    for peer in peers:
        pl.semaphore_signal(barrier, inc=1, device_id=(peer, y), device_id_type=MESH)
    own = pltpu.make_async_copy(x.at[me], out.at[me], local_sem)
    own.start()
    pl.semaphore_wait(barrier, count - 1)
    copies = []
    for at, peer in enumerate(peers):
        copy = pltpu.make_async_remote_copy(
            src_ref=x.at[peer],
            dst_ref=out.at[me],
            send_sem=send_sems.at[at],
            recv_sem=recv_sems.at[at],
            device_id=(peer, y),
            device_id_type=MESH,
        )
        copy.start()
        copies.append(copy)
    for copy in copies:
        copy.wait()
    own.wait()


def exchange(x, collective_id):
    count = x.shape[0]
    return pl.pallas_call(
        exchange_kernel,
        out_shape=jax.ShapeDtypeStruct(x.shape, x.dtype),
        in_specs=[pl.BlockSpec(memory_space=pl.ANY)],
        out_specs=pl.BlockSpec(memory_space=pl.ANY),
        scratch_shapes=[
            pltpu.SemaphoreType.DMA,
            pltpu.SemaphoreType.DMA((count - 1,)),
            pltpu.SemaphoreType.DMA((count - 1,)),
        ],
        compiler_params=pltpu.CompilerParams(collective_id=collective_id, has_side_effects=True),
        cost_estimate=pl.CostEstimate(
            flops=0, bytes_accessed=20 * x.size * x.dtype.itemsize, transcendentals=0
        ),
    )(x)


def swap_halves(value):
    half = value.shape[1] // 2
    return jnp.concatenate([value[:, half:], value[:, :half]], axis=1)


def attend_kernel(
    rows,
    g_attn,
    w_front,
    g_lat,
    expand_head,
    cosines,
    sines,
    normed_out,
    latent_out,
    query_out,
    key_out,
    value_out,
    head_out,
    sum_out,
    log_out,
    keys,
    values,
):
    bf16 = jnp.bfloat16
    size = rows.shape[0]
    scale = (PLAIN_UNITS + ROTARY_UNITS) ** (-0.5)
    step = pl.program_id(0)
    normed, _ = norm_forward(rows[...].astype(jnp.float32), g_attn[...])
    normed = normed.astype(bf16)
    normed_out[...] = normed
    front = matrix_product(normed, w_front[...])
    latent, _ = norm_forward(front[:, :LATENT_WIDTH], g_lat[...])
    latent = latent.astype(bf16)
    latent_out[...] = latent
    width = LATENT_WIDTH + ROTARY_UNITS

    def rotated(value):
        return value * cosines[...] + swap_halves(value) * sines[...]

    pairs = matrix_product(latent, expand_head[...])
    key = jnp.concatenate([pairs[:, :PLAIN_UNITS], rotated(front[:, LATENT_WIDTH:width])], axis=1)
    query = jnp.concatenate(
        [front[:, width : width + PLAIN_UNITS], rotated(front[:, width + PLAIN_UNITS :])], axis=1
    ).astype(bf16)
    key = key.astype(bf16)
    value = pairs[:, PLAIN_UNITS:].astype(bf16)
    query_out[...] = query
    key_out[...] = key
    value_out[...] = value
    here = pl.ds(pl.multiple_of(step * size, size), size)
    keys[here, :] = key
    values[here, :] = value
    row = lax.broadcasted_iota(jnp.int32, (size, size), 0)
    column = lax.broadcasted_iota(jnp.int32, (size, size), 1)
    near = jnp.where(column <= row, contract_last(query, key) * scale, -1e30)

    def over(past):
        top = jnp.max(near, axis=1, keepdims=True)
        if past:
            far = contract_last(query, keys[:past, :]) * scale
            top = jnp.maximum(top, jnp.max(far, axis=1, keepdims=True))
        exps = jnp.exp(near - top)
        total = jnp.sum(exps, axis=1, keepdims=True)
        mixed = matrix_product(exps.astype(bf16), value)
        if past:
            exps = jnp.exp(far - top)
            total = total + jnp.sum(exps, axis=1, keepdims=True)
            mixed = mixed + matrix_product(exps.astype(bf16), values[:past, :])
        mixed = mixed / total
        sum_out[...] = mixed
        head_out[...] = mixed.astype(bf16)
        wide = jnp.broadcast_to(top + jnp.log(total), (size, 128))
        log_out[0] = wide.T[:1, :]

    for at in range(keys.shape[0] // size):
        pl.when(step == at)(functools.partial(over, at * size))


def attend(rows, g_attn, w_front, g_lat, expand_head, cosines, sines):
    seq_len, width = rows.shape
    size = 256
    steps = seq_len // size
    units = PLAIN_UNITS + ROTARY_UNITS
    bf16 = jnp.bfloat16

    def by_step(columns):
        return pl.BlockSpec((size, columns), lambda i: (i, 0))

    def fixed(x):
        return pl.BlockSpec(
            x.shape, lambda i: (0, 0), pipeline_mode=pl.Buffered(buffer_count=1)
        )

    return pl.pallas_call(
        attend_kernel,
        grid=(steps,),
        out_shape=[
            jax.ShapeDtypeStruct((seq_len, width), bf16),
            jax.ShapeDtypeStruct((seq_len, LATENT_WIDTH), bf16),
            jax.ShapeDtypeStruct((seq_len, units), bf16),
            jax.ShapeDtypeStruct((seq_len, units), bf16),
            jax.ShapeDtypeStruct((seq_len, VALUE_UNITS), bf16),
            jax.ShapeDtypeStruct((seq_len, VALUE_UNITS), bf16),
            jax.ShapeDtypeStruct((seq_len, VALUE_UNITS), jnp.float32),
            jax.ShapeDtypeStruct((steps, 1, size), jnp.float32),
        ],
        in_specs=[by_step(width)]
        + [fixed(x) for x in (g_attn, w_front, g_lat, expand_head)]
        + [by_step(ROTARY_UNITS)] * 2,
        out_specs=[
            by_step(width),
            by_step(LATENT_WIDTH),
            by_step(units),
            by_step(units),
            by_step(VALUE_UNITS),
            by_step(VALUE_UNITS),
            by_step(VALUE_UNITS),
            pl.BlockSpec((1, 1, size), lambda i: (i, 0, 0)),
        ],
        scratch_shapes=[
            pltpu.VMEM((seq_len, units), bf16),
            pltpu.VMEM((seq_len, VALUE_UNITS), bf16),
        ],
        compiler_params=pltpu.CompilerParams(vmem_limit_bytes=VMEM_LIMIT),
        cost_estimate=pl.CostEstimate(
            flops=2 * seq_len * (width * 768 + seq_len * units),
            bytes_accessed=3 * rows.size * 2,
            transcendentals=seq_len * seq_len // 2,
        ),
    )(rows, g_attn, w_front, g_lat, expand_head, cosines, sines)


def attend_back_kernel(
    query,
    key,
    value,
    d_head,
    head_sum,
    logs,
    expand_head,
    cosines,
    sines,
    d_query_out,
    d_pairs_out,
    d_keys_out,
    d_key,
    d_value,
    key_turned,
):
    bf16 = jnp.bfloat16
    size = query.shape[0]
    seq_len = key.shape[0]
    scale = (PLAIN_UNITS + ROTARY_UNITS) ** (-0.5)
    step = pl.program_id(0)

    @pl.when(step == 0)
    def _():
        d_key[...] = jnp.zeros_like(d_key)
        d_value[...] = jnp.zeros_like(d_value)
        for at in range(0, seq_len, size):
            part = key[at : at + size, :].astype(jnp.float32)
            key_turned[:, at : at + size] = part.T.astype(bf16)

    q, d_out = query[...], d_head[...]
    product = d_out.astype(jnp.float32) * head_sum[...]
    delta = jnp.sum(product.T, axis=0, keepdims=True)
    log_row = logs[0]
    row = lax.broadcasted_iota(jnp.int32, (size, size), 0)
    column = lax.broadcasted_iota(jnp.int32, (size, size), 1)

    def grads_of(at, mask):
        there = slice(at, at + size)
        scores = contract_last(key[there, :], q) * scale
        if mask:
            scores = jnp.where(row <= column, scores, -1e30)
        probs = jnp.exp(scores - log_row)
        d_probs = contract_last(value[there, :], d_out)
        d_scores = (probs * (d_probs - delta) * scale).astype(bf16)
        d_key[there, :] += matrix_product(d_scores, q)
        d_value[there, :] += matrix_product(probs.astype(bf16), d_out)
        return matrix_product(key_turned[:, there], d_scores)

    def over(past):
        total = grads_of(past, True)
        for at in range(0, past, size):
            total = total + grads_of(at, False)
        d_query = total.T
        d_rope = d_query[:, PLAIN_UNITS:]
        d_rope = d_rope * cosines[...] - swap_halves(d_rope) * sines[...]
        d_query_out[...] = jnp.concatenate([d_query[:, :PLAIN_UNITS], d_rope], axis=1).astype(bf16)

    for at in range(seq_len // size):
        pl.when(step == at)(functools.partial(over, at * size))

    @pl.when(step == seq_len // size - 1)
    def _():
        for at in range(0, seq_len, size):
            there = slice(at, at + size)
            d_pairs = jnp.concatenate(
                [d_key[there, :PLAIN_UNITS], d_value[there, :]], axis=1
            ).astype(bf16)
            d_pairs_out[there, :] = d_pairs
            d_keys_out[there, :LATENT_WIDTH] = contract_last(d_pairs, expand_head[...]).astype(bf16)
            tail = jnp.concatenate(
                [d_key[there, PLAIN_UNITS:], jnp.zeros((size, ROTARY_UNITS), jnp.float32)], axis=1
            )
            d_keys_out[there, LATENT_WIDTH:] = tail.astype(bf16)


def attend_back(query, key, value, d_head, head_sum, logs, expand_head, cosines, sines):
    seq_len, units = query.shape
    steps, _, size = logs.shape
    bf16 = jnp.bfloat16
    keys_width = LATENT_WIDTH + 2 * ROTARY_UNITS

    def by_step(columns):
        return pl.BlockSpec((size, columns), lambda i: (i, 0))

    def fixed(shape):
        return pl.BlockSpec(shape, lambda i: (0, 0), pipeline_mode=pl.Buffered(buffer_count=1))

    return pl.pallas_call(
        attend_back_kernel,
        grid=(steps,),
        out_shape=[
            jax.ShapeDtypeStruct((seq_len, units), bf16),
            jax.ShapeDtypeStruct((seq_len, PLAIN_UNITS + VALUE_UNITS), bf16),
            jax.ShapeDtypeStruct((seq_len, keys_width), bf16),
        ],
        in_specs=[
            by_step(units),
            fixed(key.shape),
            fixed(value.shape),
            by_step(VALUE_UNITS),
            by_step(VALUE_UNITS),
            pl.BlockSpec((1, 1, size), lambda i: (i, 0, 0)),
            fixed(expand_head.shape),
            by_step(ROTARY_UNITS),
            by_step(ROTARY_UNITS),
        ],
        out_specs=[
            by_step(units),
            fixed((seq_len, PLAIN_UNITS + VALUE_UNITS)),
            fixed((seq_len, keys_width)),
        ],
        scratch_shapes=[
            pltpu.VMEM((seq_len, units), jnp.float32),
            pltpu.VMEM((seq_len, VALUE_UNITS), jnp.float32),
            pltpu.VMEM((units, seq_len), bf16),
        ],
        compiler_params=pltpu.CompilerParams(vmem_limit_bytes=VMEM_LIMIT),
        cost_estimate=pl.CostEstimate(
            flops=5 * seq_len * seq_len * units,
            bytes_accessed=8 * seq_len * units * 2,
            transcendentals=seq_len * seq_len // 2,
        ),
    )(query, key, value, d_head, head_sum, logs, expand_head, cosines, sines)


def token_gather(rows):
    return lax.all_gather(rows, ("fsdp", "expert"), axis=0, tiled=True)


def token_scatter(partial):
    return lax.psum_scatter(
        partial, ("fsdp", "expert"), scatter_dimension=0, tiled=True
    ).astype(jnp.float32)


def split_body(
    tokens,
    routes,
    cotangent,
    attn_gain,
    w_query,
    latent_weight,
    latent_norm_gain,
    expand_weight,
    w_out,
    ffn_gain,
    w_router,
    shared_gate,
    shared_up,
    shared_down,
    expert_gate,
    expert_up,
    expert_down,
):
    rows = tokens.shape[1]
    experts = lax.axis_size("expert")
    shards = lax.axis_size("fsdp")
    position = lax.axis_index("expert")
    blocks = experts * shards
    seq_len = rows * experts
    capacity = shards * ((rows * TOPK * 4 + experts * 3 * shards - 1) // (experts * 3 * shards))
    head_units = PLAIN_UNITS + ROTARY_UNITS
    pair_units = PLAIN_UNITS + VALUE_UNITS
    feature_width = LATENT_WIDTH + ROTARY_UNITS
    scale = head_units ** (-0.5)

    shard = lax.axis_index("fsdp")
    first = shard == 0

    query_cols = lax.dynamic_slice_in_dim(w_query, position * head_units, head_units, 1)
    expand_cols = lax.dynamic_slice_in_dim(expand_weight, position * pair_units, pair_units, 1)
    owners = experts // shards
    packed = jnp.concatenate(
        [latent_weight, query_cols, w_router, attn_gain[:, None], ffn_gain[:, None]], axis=1
    )
    small = jnp.concatenate([expand_cols, latent_norm_gain[:, None]], axis=1)
    own_routes = jnp.pad(routes[0], ((0, 0), (0, 128 - TOPK)), constant_values=-1)
    seq_rows, all_routes, other_packed, other_small = gather_rows(
        [tokens[0], own_routes], (False, True), 0, swapped=[packed, small]
    )

    def whole(own, other):
        return jnp.concatenate([jnp.where(first, own, other), jnp.where(first, other, own)], axis=0)

    packed = whole(packed, other_packed)
    small = whole(small, other_small)
    w_front = packed[:, : feature_width + head_units]
    w_latent = packed[:, :feature_width]
    at = feature_width + head_units
    wrout = packed[:, at : at + experts]
    g_attn = packed[:, at + experts].astype(jnp.float32)
    g_ffn = packed[:, at + experts + 1].astype(jnp.float32)
    expand_head = small[:, :pair_units]
    g_lat = small[:, pair_units].astype(jnp.float32)
    units = shared_down.shape[0]

    def to_columns(weight):
        parts = weight.reshape(weight.shape[0], blocks, units).transpose(1, 0, 2)
        return lax.all_to_all(
            parts, ("expert", "fsdp"), split_axis=0, concat_axis=0, tiled=True
        ).reshape(-1, units)

    sh_cols = to_columns(jnp.concatenate([shared_gate, shared_up], axis=0)).reshape(
        blocks, 2, shared_gate.shape[0], units
    )
    lanes = -(-units // 128) * 128
    sh_cols = jnp.pad(sh_cols, ((0, 0), (0, 0), (0, 0), (0, lanes - units)))
    shared_in = sh_cols.transpose(0, 2, 1, 3).reshape(MODEL_WIDTH, 2 * lanes)
    wout = lax.all_gather(w_out, "fsdp", axis=0, tiled=True)
    shared_out = jnp.pad(shared_down, ((0, lanes - units), (0, 0)))
    router_cols = jnp.pad(wrout, ((0, 0), (0, 128 - experts)))
    fill = -expert_gate.shape[2] % 256
    w_g = jnp.pad(expert_gate[0], ((0, 0), (0, fill)))
    w_u = jnp.pad(expert_up[0], ((0, 0), (0, fill)))
    w_d = jnp.pad(expert_down[0], ((0, fill), (0, 0)))
    hit = jnp.any(all_routes == position, axis=2)
    tally = hit.astype(jnp.int32)
    slot = jnp.cumsum(tally, axis=1) - tally
    places = jnp.where(hit, slot, -1).reshape(blocks // 4, 1, 4 * rows)

    grad_rows = cotangent[0]
    grad_out = grad_rows.astype(jnp.float32)
    seq_rows, grad_rows = lax.optimization_barrier((seq_rows, grad_rows))
    all_grads = token_gather(grad_rows)

    x_in = tokens[0].astype(jnp.float32)
    normed, inv_attn = norm_forward(x_in, g_attn)
    normed_in = normed.astype(jnp.bfloat16)
    cosine_table, sine_table = rope_tables(jnp.arange(seq_len, dtype=jnp.int32))
    cosines = jnp.concatenate([cosine_table, cosine_table], axis=1)
    sines = jnp.concatenate([-sine_table, sine_table], axis=1)
    (
        seq_normed,
        latent_rows,
        query,
        key,
        value,
        head_rows,
        head_sum,
        logs,
    ) = attend(
        seq_rows.reshape(seq_len, MODEL_WIDTH),
        g_attn[None],
        w_front,
        g_lat[None],
        expand_head,
        cosines,
        sines,
    )
    w_query, head_rows = lax.optimization_barrier((w_query, head_rows))
    wq = lax.all_gather(w_query, "fsdp", axis=0, tiled=True)
    heads = exchange(head_rows.reshape(experts, rows, VALUE_UNITS), 1)
    heads = heads.transpose(1, 0, 2).reshape(rows, experts * VALUE_UNITS)
    hidden = x_in + matrix_product(heads, wout)
    normed2, inv_ffn = norm_forward(hidden, g_ffn)
    normed_ffn = normed2.astype(jnp.bfloat16)
    router = jax.nn.softmax(matrix_product(normed_ffn, wrout), axis=-1)

    (all_normed,) = gather_rows([normed_ffn], True, 2)
    (
        out_part,
        d_part,
        ex_rows,
        ex_grads,
        scaled_act,
        d_pre_gate,
        d_pre_up,
        g_shared_in,
        g_shared_out,
    ) = expert_phase(
        all_normed,
        all_grads.reshape(all_normed.shape),
        places,
        router_cols,
        w_g,
        w_u,
        w_d,
        shared_in,
        shared_out,
        capacity,
    )
    ff = expert_gate.shape[2]
    g_down = inner(scaled_act, ex_grads)[:ff]
    g_gate = inner(ex_rows, d_pre_gate)[:, :ff]
    g_up = inner(ex_rows, d_pre_up)[:, :ff]
    (d_back,) = scatter_rows(d_part, True, 3)
    out_part, d_back = lax.optimization_barrier((out_part, d_back))
    d_normed_ffn = d_back[:, :MODEL_WIDTH]
    d_router = d_back[:, MODEL_WIDTH : MODEL_WIDTH + experts]
    output = hidden + token_scatter(out_part.reshape(blocks * rows, MODEL_WIDTH))

    d_logits = (router * (d_router - jnp.sum(router * d_router, axis=1, keepdims=True))).astype(
        jnp.bfloat16
    )
    g_router = inner(normed_ffn, d_logits)
    d_normed_ffn = d_normed_ffn + outer_product(d_logits, wrout)
    d_hidden_norm, g_ffn_grad = norm_backward(hidden, inv_ffn, g_ffn, d_normed_ffn)
    d_hidden = grad_out + d_hidden_norm
    d_attn = d_hidden.astype(jnp.bfloat16)

    d_heads = outer_product(d_attn, wout).astype(jnp.bfloat16)
    d_heads = d_heads.reshape(rows, experts, VALUE_UNITS).transpose(1, 0, 2)
    d_head = exchange(d_heads, 4).reshape(seq_len, VALUE_UNITS)
    seq_d_attn = lax.all_gather(d_attn, "expert", axis=0, tiled=True)
    d_query_full, d_pairs, d_keys = attend_back(
        query, key, value, d_head, head_sum, logs, expand_head, cosines, sines
    )
    g_out_head = inner(head_rows, seq_d_attn)
    g_expand_head = inner(latent_rows, d_pairs)
    g_query_head = inner(d_query_full, seq_normed).astype(jnp.bfloat16)
    g_expand_head = g_expand_head.astype(jnp.bfloat16)
    g_out_head = g_out_head.astype(jnp.bfloat16)

    def half_of(whole, which, axis):
        size = whole.shape[axis] // shards
        return lax.dynamic_slice_in_dim(whole, which * size, size, axis)

    own_d_query = exchange(d_query_full.reshape(experts, rows, head_units), 8)
    own_d_query = own_d_query.transpose(1, 0, 2).reshape(rows, experts * head_units)
    d_sums, other_query, other_expand, other_out_grad = scatter_rows(
        d_keys.reshape(experts, rows, -1),
        False,
        5,
        swapped=[
            half_of(g_query_head, 1 - shard, 1),
            half_of(g_expand_head, 1 - shard, 0),
            g_out_head,
        ],
    )
    key_gradient = d_sums[:, :feature_width]
    d_normed_in = outer_product(own_d_query, wq)

    def summed(own, other):
        return (own.astype(jnp.float32) + other.astype(jnp.float32)).astype(jnp.bfloat16)

    own_query = summed(half_of(g_query_head, shard, 1), other_query)
    own_expand = summed(half_of(g_expand_head, shard, 0), other_expand)
    own_out = summed(g_out_head, other_out_grad)
    own_latent = matrix_product(normed_in, w_latent[:, :LATENT_WIDTH])
    own_cosine = lax.dynamic_slice_in_dim(cosine_table, position * rows, rows, 0)
    own_sine = lax.dynamic_slice_in_dim(sine_table, position * rows, rows, 0)
    inv_lat = lax.rsqrt(jnp.mean(own_latent * own_latent, axis=-1, keepdims=True) + EPS)
    d_compact, g_lat_grad = norm_backward(
        own_latent, inv_lat, g_lat, key_gradient[:, :LATENT_WIDTH]
    )
    d_rope = reverse_rotary(key_gradient[:, LATENT_WIDTH:], own_cosine, own_sine)
    d_latent_full = jnp.concatenate([d_compact, d_rope], axis=-1).astype(jnp.bfloat16)
    g_latent = inner(normed_in, d_latent_full)
    d_normed_in = d_normed_in + outer_product(d_latent_full, w_latent)
    d_norm_in, g_attn_grad = norm_backward(x_in, inv_attn, g_attn, d_normed_in)
    d_tokens = (d_hidden + d_norm_in).astype(jnp.bfloat16)

    half = MODEL_WIDTH // blocks
    cols = g_shared_in.reshape(2, lanes, blocks, half)[:, :units].astype(jnp.bfloat16)
    cols = lax.all_to_all(
        cols.transpose(2, 0, 1, 3), ("expert", "fsdp"), split_axis=0, concat_axis=0, tiled=True
    )
    cols = cols.transpose(1, 3, 0, 2).reshape(2, half, blocks * units).astype(jnp.float32)
    r_sgate, r_sup = (cols[0], cols[1])
    g_sdown = g_shared_out[:units]
    lat_rows = jnp.zeros((shards, MODEL_WIDTH // shards), jnp.float32)
    lat_rows = lat_rows.at[:, : LATENT_WIDTH // shards].set(g_lat_grad.reshape(shards, -1))
    columns = jnp.concatenate(
        [
            g_latent,
            g_router,
            g_attn_grad[:, None],
            g_ffn_grad[:, None],
            lat_rows.reshape(MODEL_WIDTH, 1),
        ],
        axis=1,
    )
    used = columns.shape[1]
    columns = jnp.pad(columns.astype(jnp.bfloat16), ((0, 0), (0, -used % 128)))
    (columns,) = scatter_rows(columns.reshape(blocks, half, -1), True, 6)
    r_query, r_expand, columns, r_out = gather_rows(
        [own_query, own_expand, columns.astype(jnp.bfloat16), own_out], False, 7, gated=(3,)
    )
    r_query = r_query.reshape(experts * head_units, -1).astype(jnp.float32).T
    r_expand = r_expand.transpose(1, 0, 2).reshape(-1, experts * pair_units)
    r_out = lax.dynamic_slice_in_dim(r_out, shard * owners, owners, 0)
    columns = columns.reshape(MODEL_WIDTH // shards, -1).astype(jnp.float32)
    at = feature_width + experts
    return (
        output.astype(jnp.bfloat16)[None],
        d_tokens[None],
        columns[:, at],
        r_query,
        columns[:, :feature_width],
        columns[: LATENT_WIDTH // shards, at + 2],
        r_expand.astype(jnp.float32),
        r_out.reshape(-1, MODEL_WIDTH).astype(jnp.float32),
        columns[:, at + 1],
        columns[:, feature_width:at],
        r_sgate,
        r_sup,
        g_sdown,
        g_gate[None],
        g_up[None],
        g_down[None],
    )


def solution(mesh):
    shape = (mesh.shape["expert"], mesh.shape["fsdp"])
    split = shape == (LINE * SQUARE * CORES, SQUARE) and shape[0] == HEAD_COUNT
    return jax.shard_map(
        split_body if split else body,
        mesh=mesh,
        in_specs=(
            P("fsdp", "expert", None),
            P("fsdp", "expert", None),
            P("fsdp", "expert", None),
            P("fsdp"),
            P("fsdp", None),
            P("fsdp", None),
            P("fsdp"),
            P("fsdp", None),
            P("fsdp", None),
            P("fsdp"),
            P("fsdp", None),
            P(("expert", "fsdp"), None),
            P(("expert", "fsdp"), None),
            P(("expert", "fsdp"), None),
            P("expert", None, "fsdp"),
            P("expert", None, "fsdp"),
            P("expert", "fsdp", None),
        ),
        out_specs=(
            P("fsdp", "expert", None),
            P("fsdp", "expert", None),
            P("fsdp"),
            P("fsdp", None),
            P("fsdp", None),
            P("fsdp"),
            P("fsdp", None),
            P("fsdp", None),
            P("fsdp"),
            P("fsdp", None),
            P(("expert", "fsdp"), None),
            P(("expert", "fsdp"), None),
            P(("expert", "fsdp"), None),
            P("expert", None, "fsdp"),
            P("expert", None, "fsdp"),
            P("expert", "fsdp", None),
        ),
        check_vma=False,
    )
```

```python
import functools

import jax
import jax.numpy as jnp
from jax import lax
from jax.experimental import pallas as pl
from jax.experimental.pallas import tpu as pltpu
from jax.sharding import PartitionSpec as P

MODEL_WIDTH = 2048
HEAD_COUNT = 16
PLAIN_UNITS = 128
ROTARY_UNITS = 64
VALUE_UNITS = 128
LATENT_WIDTH = 512
TOPK = 6


EPS = 1e-06


def matrix_product(left, right):
    return jnp.dot(left, right, preferred_element_type=jnp.float32)


def inner(left, right):
    return lax.dot_general(
        left, right, (((0,), (0,)), ((), ())), preferred_element_type=jnp.float32
    )


def outer_product(left, right):
    return lax.dot_general(
        left, right, (((1,), (1,)), ((), ())), preferred_element_type=jnp.float32
    )


def norm_forward(value, gain):
    inverse = lax.rsqrt(jnp.mean(value * value, axis=-1, keepdims=True) + EPS)
    return (value * inverse * gain, inverse)


def norm_backward(value, inverse, gain, grad):
    unit = value * inverse
    scaled = grad * gain
    d_value = inverse * (scaled - unit * jnp.mean(scaled * unit, axis=-1, keepdims=True))
    return (d_value, jnp.sum(grad * unit, axis=0))


def rope_tables(positions):
    half = ROTARY_UNITS // 2
    freqs = 10000.0 ** (-jnp.arange(half, dtype=jnp.float32) * (2.0 / ROTARY_UNITS))
    angles = positions.astype(jnp.float32)[:, None] * freqs[None, :]
    return (jnp.cos(angles), jnp.sin(angles))


def apply_rotary(value, cosine_table, sine_table):
    half = ROTARY_UNITS // 2
    first = value[..., :half]
    second = value[..., half:]
    return jnp.concatenate(
        [first * cosine_table - second * sine_table, first * sine_table + second * cosine_table],
        axis=-1,
    )


def reverse_rotary(grad, cosine_table, sine_table):
    half = ROTARY_UNITS // 2
    first = grad[..., :half]
    second = grad[..., half:]
    return jnp.concatenate(
        [first * cosine_table + second * sine_table, second * cosine_table - first * sine_table],
        axis=-1,
    )


def silu_parts(value):
    sigma = jax.nn.sigmoid(value)
    return (value * sigma, sigma * (1.0 + value * (1.0 - sigma)))


def body(
    tokens,
    routes,
    cotangent,
    attn_gain,
    w_query,
    latent_weight,
    latent_norm_gain,
    expand_weight,
    w_out,
    ffn_gain,
    w_router,
    shared_gate,
    shared_up,
    shared_down,
    expert_gate,
    expert_up,
    expert_down,
):
    device_local = tokens.shape[1]
    experts = lax.axis_size("expert")
    shards = lax.axis_size("fsdp")
    position = lax.axis_index("expert")
    capacity = shards * (
        (device_local * TOPK * 4 + experts * 3 * shards - 1) // (experts * 3 * shards)
    )
    seq_len = device_local * experts
    feature_width = LATENT_WIDTH + ROTARY_UNITS
    scale = (PLAIN_UNITS + ROTARY_UNITS) ** (-0.5)
    attention_gain_grad, wq, wlat, g_lat, expand_matrix, wout, g_ffn, wrout = (
        lax.all_gather(attn_gain, "fsdp", axis=0, tiled=True),
        lax.all_gather(w_query, "fsdp", axis=0, tiled=True),
        lax.all_gather(latent_weight, "fsdp", axis=0, tiled=True),
        lax.all_gather(latent_norm_gain, "fsdp", axis=0, tiled=True),
        lax.all_gather(expand_weight, "fsdp", axis=0, tiled=True),
        lax.all_gather(w_out, "fsdp", axis=0, tiled=True),
        lax.all_gather(ffn_gain, "fsdp", axis=0, tiled=True),
        lax.all_gather(w_router, "fsdp", axis=0, tiled=True),
    )
    sgate, sup, sdown = (
        lax.all_gather(shared_gate, ("expert", "fsdp"), axis=0, tiled=True),
        lax.all_gather(shared_up, ("expert", "fsdp"), axis=0, tiled=True),
        lax.all_gather(shared_down, ("expert", "fsdp"), axis=0, tiled=True),
    )
    attention_gain_grad = attention_gain_grad.astype(jnp.float32)
    g_lat = g_lat.astype(jnp.float32)
    g_ffn = g_ffn.astype(jnp.float32)
    x_in = tokens[0].astype(jnp.float32)
    grad_out = cotangent[0].astype(jnp.float32)
    positions = position * device_local + jnp.arange(device_local, dtype=jnp.int32)
    cosine_table, sine_table = rope_tables(positions)
    normed, inv_attn = norm_forward(x_in, attention_gain_grad)
    normed_in = normed.astype(jnp.bfloat16)
    query_full = matrix_product(normed_in, wq).reshape(
        device_local, HEAD_COUNT, PLAIN_UNITS + ROTARY_UNITS
    )
    query_nope = query_full[:, :, :PLAIN_UNITS].astype(jnp.bfloat16)
    expanded_latent = expand_matrix.reshape(LATENT_WIDTH, HEAD_COUNT, PLAIN_UNITS + VALUE_UNITS)
    key_part = expanded_latent[:, :, :PLAIN_UNITS]
    value_part = expanded_latent[:, :, PLAIN_UNITS:]
    query_latent = jnp.einsum(
        "thd,chd->thc", query_nope, key_part, preferred_element_type=jnp.float32
    )
    query_rope = apply_rotary(
        query_full[:, :, PLAIN_UNITS:], cosine_table[:, None, :], sine_table[:, None, :]
    )
    token_rows = device_local * HEAD_COUNT
    query = (
        jnp.concatenate([query_latent, query_rope], axis=-1)
        .astype(jnp.bfloat16)
        .reshape(token_rows, feature_width)
    )
    latent_complete = matrix_product(normed_in, wlat)
    packed_rows = latent_complete[:, :LATENT_WIDTH]
    latent_state, inv_lat = norm_forward(packed_rows, g_lat)
    rotary_key = apply_rotary(latent_complete[:, LATENT_WIDTH:], cosine_table, sine_table)
    key = jnp.concatenate([latent_state, rotary_key], axis=-1).astype(jnp.bfloat16)
    keys_all = lax.all_gather(key, "expert", axis=0, tiled=True)
    block = min(512, seq_len)
    token_tally = (position * device_local + device_local + block - 1) // block
    q_pos = position * device_local + jnp.arange(token_rows, dtype=jnp.int32) // HEAD_COUNT

    def scores_of(index):
        key_rows = lax.dynamic_slice_in_dim(keys_all, index * block, block, 0)
        raw = outer_product(query, key_rows)
        k_pos = index * block + jnp.arange(block, dtype=jnp.int32)
        valid = k_pos[None, :] <= q_pos[:, None]
        return (jnp.where(valid, raw * scale, -1e30), key_rows)

    def stats_step(index, carry):
        top, total = carry
        scores, unused = scores_of(index)
        new_top = jnp.maximum(top, jnp.max(scores, axis=1))
        total = total * jnp.exp(top - new_top) + jnp.sum(jnp.exp(scores - new_top[:, None]), axis=1)
        return (new_top, total)

    top, total = lax.fori_loop(
        0,
        token_tally,
        stats_step,
        (jnp.full((token_rows,), -1e30, jnp.float32), jnp.zeros((token_rows,), jnp.float32)),
    )
    log_total = top + jnp.log(total)

    def mixing_update(index, running_total):
        scores, key_rows = scores_of(index)
        weight_arrays = jnp.exp(scores - log_total[:, None]).astype(jnp.bfloat16)
        return running_total + matrix_product(weight_arrays, key_rows[:, :LATENT_WIDTH])

    mixed_output_sum = lax.fori_loop(
        0, token_tally, mixing_update, jnp.zeros((token_rows, LATENT_WIDTH), jnp.float32)
    )
    mixed_output = mixed_output_sum.astype(jnp.bfloat16).reshape(
        device_local, HEAD_COUNT, LATENT_WIDTH
    )
    heads = jnp.einsum("thc,chv->thv", mixed_output, value_part, preferred_element_type=jnp.float32)
    heads = heads.reshape(device_local, HEAD_COUNT * VALUE_UNITS).astype(jnp.bfloat16)
    hidden = x_in + matrix_product(heads, wout)
    normed2, inv_ffn = norm_forward(hidden, g_ffn)
    normed_ffn = normed2.astype(jnp.bfloat16)
    logits = matrix_product(normed_ffn, wrout)
    router = jax.nn.softmax(logits, axis=-1)
    own_routes = routes[0]
    names = jnp.arange(experts, dtype=jnp.int32)
    chosen = (own_routes[:, :, None] == names[None, None, :]).astype(jnp.float32)
    gates = jnp.sum(chosen * router[:, None, :], axis=-1)
    hits = (own_routes.reshape(device_local * TOPK)[:, None] == names[None, :]).astype(jnp.int32)
    slot = jnp.sum((jnp.cumsum(hits, axis=0) - hits) * hits, axis=1)
    place = own_routes.reshape(device_local * TOPK) * capacity + slot
    token_of = jnp.arange(device_local * TOPK, dtype=jnp.int32) // TOPK
    table = jnp.full((experts * capacity,), device_local, jnp.int32).at[place].set(token_of)
    padded = jnp.concatenate([normed_ffn, jnp.zeros((1, MODEL_WIDTH), jnp.bfloat16)], axis=0)
    buffer = padded[table].reshape(experts, capacity, MODEL_WIDTH)
    w_g, w_u, w_d = (expert_gate[0], expert_up[0], expert_down[0])

    def spread(values):
        return jnp.broadcast_to(values[:, None], (experts, shards, capacity, MODEL_WIDTH)).reshape(
            experts * shards, capacity, MODEL_WIDTH
        )

    def collect(back):
        return jnp.sum(back.reshape(experts, shards, capacity, MODEL_WIDTH), axis=1).reshape(
            experts * capacity, MODEL_WIDTH
        )

    received = lax.all_to_all(
        spread(buffer), ("expert", "fsdp"), split_axis=0, concat_axis=0, tiled=True
    )
    ex_rows = received.reshape(-1, MODEL_WIDTH)
    pre_gate = matrix_product(ex_rows, w_g)
    pre_up = matrix_product(ex_rows, w_u)
    act_gate, slope = silu_parts(pre_gate)
    ex_act = (act_gate * pre_up).astype(jnp.bfloat16)
    ex_out = matrix_product(ex_act, w_d).reshape(received.shape)
    returned = lax.all_to_all(
        ex_out.astype(jnp.bfloat16), ("expert", "fsdp"), split_axis=0, concat_axis=0, tiled=True
    ).astype(ex_out.dtype)
    results = collect(returned)
    picked = results[place].reshape(device_local, TOPK, MODEL_WIDTH)
    routed = jnp.sum(gates[:, :, None] * picked, axis=1)
    sh_gate = matrix_product(normed_ffn, sgate)
    sh_up = matrix_product(normed_ffn, sup)
    sh_silu, sh_slope = silu_parts(sh_gate)
    sh_act = (sh_silu * sh_up).astype(jnp.bfloat16)
    shared = matrix_product(sh_act, sdown)
    output = hidden + routed + shared
    d_shared = grad_out.astype(jnp.bfloat16)
    shared_down_gradient = inner(sh_act, d_shared)
    d_sh_act = outer_product(d_shared, sdown)
    d_sh_gate = (d_sh_act * sh_up * sh_slope).astype(jnp.bfloat16)
    d_sh_up = (d_sh_act * sh_silu).astype(jnp.bfloat16)
    shared_gate_gradient = inner(normed_ffn, d_sh_gate)
    shared_up_gradient = inner(normed_ffn, d_sh_up)
    d_normed_ffn = outer_product(d_sh_gate, sgate) + outer_product(d_sh_up, sup)
    d_picked = (
        (gates[:, :, None] * grad_out[:, None, :])
        .astype(jnp.bfloat16)
        .reshape(device_local * TOPK, MODEL_WIDTH)
    )
    d_gates = jnp.sum(picked * grad_out[:, None, :], axis=2)
    d_buffer = (
        jnp.zeros((experts * capacity, MODEL_WIDTH), jnp.bfloat16)
        .at[place]
        .set(d_picked)
        .reshape(experts, capacity, MODEL_WIDTH)
    )
    d_received = lax.all_to_all(
        spread(d_buffer), ("expert", "fsdp"), split_axis=0, concat_axis=0, tiled=True
    )
    d_rows = d_received.reshape(-1, MODEL_WIDTH)
    d_act = outer_product(d_rows, w_d)
    g_down = inner(ex_act, d_rows)
    d_pre_gate = (d_act * pre_up * slope).astype(jnp.bfloat16)
    d_pre_up = (d_act * act_gate).astype(jnp.bfloat16)
    g_gate = inner(ex_rows, d_pre_gate)
    g_up = inner(ex_rows, d_pre_up)
    d_ex_rows = (outer_product(d_pre_gate, w_g) + outer_product(d_pre_up, w_u)).reshape(
        received.shape
    )
    d_returned = lax.all_to_all(
        d_ex_rows.astype(jnp.bfloat16), ("expert", "fsdp"), split_axis=0, concat_axis=0, tiled=True
    ).astype(d_ex_rows.dtype)
    d_results = collect(d_returned)
    d_normed_ffn = d_normed_ffn + jnp.sum(
        d_results[place].reshape(device_local, TOPK, MODEL_WIDTH), axis=1
    )
    d_router = jnp.sum(chosen * d_gates[:, :, None], axis=1)
    d_logits = (router * (d_router - jnp.sum(router * d_router, axis=1, keepdims=True))).astype(
        jnp.bfloat16
    )
    router_weight_gradient = inner(normed_ffn, d_logits)
    d_normed_ffn = d_normed_ffn + outer_product(d_logits, wrout)
    d_hidden_norm, g_ffn_grad = norm_backward(hidden, inv_ffn, g_ffn, d_normed_ffn)
    d_hidden = grad_out + d_hidden_norm
    d_attn = d_hidden.astype(jnp.bfloat16)
    output_weight_gradient = inner(heads, d_attn)
    d_heads = (
        outer_product(d_attn, wout)
        .astype(jnp.bfloat16)
        .reshape(device_local, HEAD_COUNT, VALUE_UNITS)
    )
    value_weight_gradient = jnp.einsum(
        "thc,thv->chv", mixed_output, d_heads, preferred_element_type=jnp.float32
    )
    mixed_gradient = jnp.einsum(
        "thv,chv->thc", d_heads, value_part, preferred_element_type=jnp.float32
    )
    mixed_gradient = mixed_gradient.astype(jnp.bfloat16).reshape(token_rows, LATENT_WIDTH)
    delta = jnp.sum(mixed_gradient.astype(jnp.float32) * mixed_output_sum, axis=1)

    def back_step(index, carry):
        d_query_acc, d_keys_acc = carry
        scores, key_rows = scores_of(index)
        weight_arrays = jnp.exp(scores - log_total[:, None])
        weight_gradients = outer_product(mixed_gradient, key_rows[:, :LATENT_WIDTH])
        d_scores = (weight_arrays * (weight_gradients - delta[:, None]) * scale).astype(
            jnp.bfloat16
        )
        d_query_acc = d_query_acc + matrix_product(d_scores, key_rows)
        d_values = inner(weight_arrays.astype(jnp.bfloat16), mixed_gradient)
        d_block = inner(d_scores, query) + jnp.concatenate(
            [d_values, jnp.zeros((block, ROTARY_UNITS), jnp.float32)], axis=1
        )
        previous = lax.dynamic_slice_in_dim(d_keys_acc, index * block, block, 0)
        return (
            d_query_acc,
            lax.dynamic_update_slice_in_dim(d_keys_acc, previous + d_block, index * block, 0),
        )

    d_query, d_keys = lax.fori_loop(
        0,
        token_tally,
        back_step,
        (
            jnp.zeros((token_rows, feature_width), jnp.float32),
            jnp.zeros((seq_len, feature_width), jnp.float32),
        ),
    )
    key_gradient = lax.psum_scatter(
        d_keys.astype(jnp.bfloat16), "expert", scatter_dimension=0, tiled=True
    )
    query_up_gradient = d_query.astype(jnp.bfloat16).reshape(
        device_local, HEAD_COUNT, feature_width
    )
    query_latent_gradient = query_up_gradient[:, :, :LATENT_WIDTH]
    key_weight_gradient = jnp.einsum(
        "thc,thd->chd", query_latent_gradient, query_nope, preferred_element_type=jnp.float32
    )
    d_q_nope = jnp.einsum(
        "thc,chd->thd", query_latent_gradient, key_part, preferred_element_type=jnp.float32
    )
    d_q_rope = reverse_rotary(
        query_up_gradient[:, :, LATENT_WIDTH:].astype(jnp.float32),
        cosine_table[:, None, :],
        sine_table[:, None, :],
    )
    d_query_full = (
        jnp.concatenate([d_q_nope, d_q_rope], axis=-1)
        .astype(jnp.bfloat16)
        .reshape(device_local, HEAD_COUNT * (PLAIN_UNITS + ROTARY_UNITS))
    )
    query_weight_gradient = inner(normed_in, d_query_full)
    d_normed_in = outer_product(d_query_full, wq)
    latent_gradient = key_gradient[:, :LATENT_WIDTH].astype(jnp.float32)
    rotary_key_gradient = reverse_rotary(
        key_gradient[:, LATENT_WIDTH:].astype(jnp.float32), cosine_table, sine_table
    )
    d_compact, g_lat_grad = norm_backward(packed_rows, inv_lat, g_lat, latent_gradient)
    d_latent_full = jnp.concatenate([d_compact, rotary_key_gradient], axis=-1).astype(jnp.bfloat16)
    latent_weight_gradient = inner(normed_in, d_latent_full)
    d_normed_in = d_normed_in + outer_product(d_latent_full, wlat)
    d_norm_in, g_attn_grad = norm_backward(x_in, inv_attn, attention_gain_grad, d_normed_in)
    d_tokens = (d_hidden + d_norm_in).astype(jnp.bfloat16)
    expand_weight_gradient = jnp.concatenate(
        [key_weight_gradient, value_weight_gradient], axis=-1
    ).reshape(LATENT_WIDTH, HEAD_COUNT * (PLAIN_UNITS + VALUE_UNITS))
    r_sgate, r_sup, r_sdown = (
        lax.psum_scatter(shared_gate_gradient, ("expert", "fsdp"), scatter_dimension=0, tiled=True),
        lax.psum_scatter(shared_up_gradient, ("expert", "fsdp"), scatter_dimension=0, tiled=True),
        lax.psum_scatter(shared_down_gradient, ("expert", "fsdp"), scatter_dimension=0, tiled=True),
    )
    r_attn, r_query, r_latent, r_lgain, r_expand, r_out, r_fgain, r_router = (
        lax.psum_scatter(
            g_attn_grad.astype(jnp.bfloat16), "fsdp", scatter_dimension=0, tiled=True
        ).astype(jnp.float32),
        lax.psum_scatter(
            query_weight_gradient.astype(jnp.bfloat16), "fsdp", scatter_dimension=0, tiled=True
        ).astype(jnp.float32),
        lax.psum_scatter(
            latent_weight_gradient.astype(jnp.bfloat16), "fsdp", scatter_dimension=0, tiled=True
        ).astype(jnp.float32),
        lax.psum_scatter(
            g_lat_grad.astype(jnp.bfloat16), "fsdp", scatter_dimension=0, tiled=True
        ).astype(jnp.float32),
        lax.psum_scatter(
            expand_weight_gradient.astype(jnp.bfloat16), "fsdp", scatter_dimension=0, tiled=True
        ).astype(jnp.float32),
        lax.psum_scatter(
            output_weight_gradient.astype(jnp.bfloat16), "fsdp", scatter_dimension=0, tiled=True
        ).astype(jnp.float32),
        lax.psum_scatter(
            g_ffn_grad.astype(jnp.bfloat16), "fsdp", scatter_dimension=0, tiled=True
        ).astype(jnp.float32),
        lax.psum_scatter(
            router_weight_gradient.astype(jnp.bfloat16), "fsdp", scatter_dimension=0, tiled=True
        ).astype(jnp.float32),
    )
    r_attn, r_query, r_latent, r_lgain, r_expand, r_out, r_fgain, r_router = (
        lax.psum(r_attn.astype(jnp.bfloat16), "expert").astype(jnp.float32),
        lax.psum(r_query.astype(jnp.bfloat16), "expert").astype(jnp.float32),
        lax.psum(r_latent.astype(jnp.bfloat16), "expert").astype(jnp.float32),
        lax.psum(r_lgain.astype(jnp.bfloat16), "expert").astype(jnp.float32),
        lax.psum(r_expand.astype(jnp.bfloat16), "expert").astype(jnp.float32),
        lax.psum(r_out.astype(jnp.bfloat16), "expert").astype(jnp.float32),
        lax.psum(r_fgain.astype(jnp.bfloat16), "expert").astype(jnp.float32),
        lax.psum(r_router.astype(jnp.bfloat16), "expert").astype(jnp.float32),
    )
    return (
        output.astype(jnp.bfloat16)[None],
        d_tokens[None],
        r_attn,
        r_query,
        r_latent,
        r_lgain,
        r_expand,
        r_out,
        r_fgain,
        r_router,
        r_sgate,
        r_sup,
        r_sdown,
        g_gate[None],
        g_up[None],
        g_down[None],
    )


LINE = 4
SQUARE = 2
CORES = 2
MESH = pl.DeviceIdType.MESH
VMEM_LIMIT = 56 * 1024 * 1024


class Place:
    def __init__(self):
        index = lax.axis_index("expert")
        self.y = lax.axis_index("fsdp")
        self.c = lax.rem(index, CORES)
        self.b = lax.rem(lax.div(index, CORES), SQUARE)
        self.a = lax.div(index, CORES * SQUARE)

    def device(self, da=0, db=0, dc=0, dy=0):
        b = 1 - self.b if db else self.b
        c = 1 - self.c if dc else self.c
        y = 1 - self.y if dy else self.y
        return (((self.a + da) * SQUARE + b) * CORES + c, y)

    def block(self, full, a, db=0, dc=0, dy=0):
        b = 1 - self.b if db else self.b
        c = 1 - self.c if dc else self.c
        y = 1 - self.y if dy else self.y
        flat = (a * SQUARE + b) * CORES + c
        return y * (LINE * SQUARE * CORES) + flat if full else flat

    def greet(self, with_y):
        barrier = pltpu.get_barrier_semaphore()
        near = [dict(db=1), dict(dc=1)] + ([dict(dy=1)] if with_y else [])
        for step in near:
            pl.semaphore_signal(barrier, inc=1, device_id=self.device(**step), device_id_type=MESH)

        @pl.when(self.a > 0)
        def _():
            pl.semaphore_signal(barrier, inc=1, device_id=self.device(da=-1), device_id_type=MESH)

        @pl.when(self.a < LINE - 1)
        def _():
            pl.semaphore_signal(barrier, inc=1, device_id=self.device(da=1), device_id_type=MESH)

        ends = jnp.logical_or(self.a == 0, self.a == LINE - 1).astype(jnp.int32)
        pl.semaphore_wait(barrier, len(near) + 2 - ends)


class Sender:
    def __init__(self, place, sems):
        self.place, self.sems, self.pending = place, sems, []

    def send(self, src, dst, recv_sem, step, cond=None):
        sem = self.sems.at[len(self.pending)]

        def make():
            return pltpu.make_async_remote_copy(
                src_ref=src,
                dst_ref=dst,
                send_sem=sem,
                recv_sem=recv_sem,
                device_id=self.place.device(**step),
                device_id_type=MESH,
            )

        def start():
            make().start()

        guarded(cond, start)
        self.pending.append((cond, lambda: make().wait_send()))

    def arrived(self, dst, recv_sem):
        pltpu.make_async_remote_copy(
            src_ref=dst,
            dst_ref=dst,
            send_sem=self.sems.at[0],
            recv_sem=recv_sem,
            device_id=self.place.device(dc=1),
            device_id_type=MESH,
        ).wait_recv()

    def finish(self):
        for cond, wait in self.pending:
            guarded(cond, wait)


def guarded(cond, action):
    if cond is None:
        action()
    else:
        pl.when(cond)(action)


def both(first, second):
    if first is None or second is None:
        return second if first is None else first
    return jnp.logical_and(first, second)


def gather_ticks(place, sender, full, gated, ins, outs, local_sems, recv_sems):
    a = place.a
    count = len(ins)

    def own_copy(at):
        return pltpu.make_async_copy(
            ins[at], outs[at].at[place.block(full, a)], local_sems.at[at]
        )

    def chunk(at, block, half):
        size = ins[at].shape[0] // 2
        return outs[at].at[block, pl.ds(half * size, size)]

    def sem_of(at, block, half):
        return recv_sems.at[at, block * 2 + half]

    def forward(at, block, half, src, step, cond=None):
        sender.send(src, chunk(at, block, half), sem_of(at, block, half), step, cond)

    def receive(at, block, half, cond):
        guarded(cond, lambda: sender.arrived(chunk(at, block, half), sem_of(at, block, half)))

    def held_by(at, delta, cond):
        if at not in gated:
            return cond
        return both(cond, lax.div(a + delta, LINE // 2) == place.y)

    def from_line(delta, always):
        for half in range(2):
            for at in range(count):
                block = place.block(full, a + delta)
                cond = held_by(at, delta, always)
                size = ins[at].shape[0] // 2
                if delta == 0:
                    src = ins[at].at[pl.ds(half * size, size)]
                else:
                    receive(at, block, half, cond)
                    src = chunk(at, block, half)
                if delta <= 0:
                    forward(at, block, half, src, dict(da=1), both(cond, a < LINE - 1))
                if delta >= 0:
                    forward(at, block, half, src, dict(da=-1), both(cond, a > 0))
                forward(at, block, half, src, dict(db=1), cond)
                if full:
                    forward(at, block, half, src, dict(dy=1), cond)
                forward(at, block, half, src, dict(dc=1), cond)

    def from_side(delta, always):
        for half in range(2):
            for at in range(count):
                cond = held_by(at, delta, always)
                block = place.block(full, a + delta, db=1)
                receive(at, block, half, cond)
                if full and half == 0:
                    forward(at, block, half, chunk(at, block, half), dict(dy=1), cond)
                forward(at, block, half, chunk(at, block, half), dict(dc=1), cond)
                if full:
                    block = place.block(full, a + delta, dy=1)
                    receive(at, block, half, cond)
                    if half == 1:
                        forward(at, block, half, chunk(at, block, half), dict(db=1), cond)
                    forward(at, block, half, chunk(at, block, half), dict(dc=1), cond)

    def from_corner(delta, always):
        for half in range(2):
            for at in range(count):
                cond = held_by(at, delta, always)
                block = place.block(True, a + delta, db=1, dy=1)
                receive(at, block, half, cond)
                forward(at, block, half, chunk(at, block, half), dict(dc=1), cond)

    def from_sibling(delta, always):
        for half in range(2):
            for at in range(count):
                cond = held_by(at, delta, always)
                for db in range(2):
                    for dy in range(2 if full else 1):
                        receive(at, place.block(full, a + delta, db=db, dc=1, dy=dy), half, cond)

    rounds = [[(0, None)]]
    for s in range(1, LINE):
        rounds.append([(-s, a >= s), (s, a + s < LINE)])
    stages = [from_line, from_side] + ([from_corner] if full else []) + [from_sibling]

    def tick(number):
        if number == 0:
            for at in range(count):
                own_copy(at).start()
        for level, stage in enumerate(stages):
            if 0 <= number - level < len(rounds):
                for delta, cond in rounds[number - level]:
                    stage(delta, cond)
        if number == len(rounds) + len(stages) - 2:
            for at in range(count):
                own_copy(at).wait()

    return [functools.partial(tick, number) for number in range(len(rounds) + len(stages) - 1)]


def send_pairs(sender, ins, outs, sems):
    for at, (src, dst) in enumerate(zip(ins, outs)):
        sender.send(src, dst, sems.at[at], dict(dy=1))


def take_pairs(sender, outs, sems):
    for at, dst in enumerate(outs):
        sender.arrived(dst, sems.at[at])


def gather_kernel(full, count, pairs, gated, *refs):
    ins, outs = refs[: count + pairs], refs[count + pairs : 2 * (count + pairs)]
    local_sems, send_sems, recv_sems, pair_sems = refs[2 * (count + pairs) :]
    place = Place()
    sender = Sender(place, send_sems)
    place.greet(full or pairs > 0)
    send_pairs(sender, ins[count:], outs[count:], pair_sems)
    for tick in gather_ticks(
        place, sender, full, gated, ins[:count], outs[:count], local_sems, recv_sems
    ):
        tick()
    take_pairs(sender, outs[count:], pair_sems)
    sender.finish()


def gather_rows(arrays, full, collective_id, swapped=(), gated=()):
    blocks = LINE * SQUARE * CORES * (SQUARE if full else 1)
    count, pairs = len(arrays), len(swapped)
    lines = 2 * LINE - 1
    sends = pairs + count * lines * 2 * (9 if full else 5)
    moved = sum(blocks * 2 * x.size * x.dtype.itemsize for x in arrays)
    return pl.pallas_call(
        functools.partial(gather_kernel, full, count, pairs, gated),
        out_shape=[jax.ShapeDtypeStruct((blocks,) + x.shape, x.dtype) for x in arrays]
        + [jax.ShapeDtypeStruct(x.shape, x.dtype) for x in swapped],
        in_specs=[pl.BlockSpec(memory_space=pl.ANY)] * (count + pairs),
        out_specs=[pl.BlockSpec(memory_space=pl.ANY)] * (count + pairs),
        scratch_shapes=[
            pltpu.SemaphoreType.DMA((count,)),
            pltpu.SemaphoreType.DMA((sends,)),
            pltpu.SemaphoreType.DMA((count, blocks * 2)),
            pltpu.SemaphoreType.DMA((max(pairs, 1),)),
        ],
        compiler_params=pltpu.CompilerParams(collective_id=collective_id, has_side_effects=True),
        cost_estimate=pl.CostEstimate(flops=0, bytes_accessed=6 * moved, transcendentals=0),
    )(*arrays, *swapped)


def add_rows(target, sources, size):
    def step(at, carry):
        rows = pl.ds(pl.multiple_of(at * 16, 16), 16)
        total = sources[0][rows, :].astype(jnp.float32)
        for source in sources[1:]:
            total = total + source[rows, :].astype(jnp.float32)
        target[rows, :] = total.astype(target.dtype)
        return carry

    lax.fori_loop(0, size // 16, step, 0)


def scatter_ticks(place, sender, full, part, out, scratch):
    mine, got, side, up, down, load_sems, recv_sems = scratch
    a = place.a
    kinds = 4 if full else 2
    size = part.shape[1]
    half = size // 2
    order = [LINE - 1, 0, LINE - 2, 1]
    walk = (3, 1, 2, 0) if full else (1, 0)

    def sem_of(group, target, kind):
        return recv_sems.at[group, target * 4 + kind]

    def load(target, kind):
        block = place.block(full, target, db=kind % 2, dy=kind // 2)
        return pltpu.make_async_copy(
            part.at[block], mine.at[target, kind], load_sems.at[target * 4 + kind]
        )

    def begin():
        for target in order:
            for kind in walk:
                load(target, kind).start()
                block = place.block(full, target, db=kind % 2, dc=1, dy=kind // 2)
                sender.send(
                    part.at[block], got.at[target, kind], sem_of(0, target, kind), dict(dc=1)
                )

    def rows_of(ref, which):
        return ref.at[pl.ds(which * half, half)]

    def over_cores(target):
        for kind in walk:
            load(target, kind).wait()
            sender.arrived(got.at[target, kind], sem_of(0, target, kind))
            add_rows(mine.at[target, kind], [mine.at[target, kind], got.at[target, kind]], size)
            held = mine.at[target, kind]
            if kind == 3:
                sender.send(rows_of(held, 0), side.at[target, 4], sem_of(1, target, 0), dict(db=1))
                sender.send(rows_of(held, 1), side.at[target, 5], sem_of(1, target, 1), dict(dy=1))
            if kind == 1:
                sender.send(rows_of(held, 0), side.at[target, 0], sem_of(2, target, 0), dict(db=1))
                if not full:
                    sender.send(
                        rows_of(held, 1), side.at[target, 1], sem_of(2, target, 1), dict(db=1)
                    )
            if kind == 2:
                sender.send(rows_of(held, 1), side.at[target, 3], sem_of(2, target, 3), dict(dy=1))

    def over_corner(target):
        sender.arrived(side.at[target, 4], sem_of(1, target, 0))
        held = rows_of(mine.at[target, 2], 0)
        add_rows(held, [held, side.at[target, 4]], half)
        sender.send(held, side.at[target, 2], sem_of(2, target, 2), dict(dy=1))
        sender.arrived(side.at[target, 5], sem_of(1, target, 1))
        held = rows_of(mine.at[target, 1], 1)
        add_rows(held, [held, side.at[target, 5]], half)
        sender.send(held, side.at[target, 1], sem_of(2, target, 1), dict(db=1))

    def over_line(target):
        for which in range(2):
            held = rows_of(mine.at[target, 0], which)
            parts = [held]
            for source in (0, 2) if full else (0,):
                sender.arrived(side.at[target, source + which], sem_of(2, target, source + which))
                parts.append(side.at[target, source + which])
            below, above = rows_of(up.at[target], which), rows_of(down.at[target], which)
            below_sem, above_sem = sem_of(3, target, which), sem_of(3, target, 2 + which)

            def upward(with_below):
                extra = []
                if with_below:
                    sender.arrived(below, below_sem)
                    extra = [below]
                add_rows(held, parts + extra, half)

            def downward(with_above):
                extra = []
                if with_above:
                    sender.arrived(above, above_sem)
                    extra = [above]
                add_rows(held, parts + extra, half)

            if target > 0:
                pl.when(jnp.logical_and(a < target, a > 0))(lambda: upward(True))
                pl.when(a == 0)(lambda: upward(False))
                sender.send(held, below, below_sem, dict(da=1), a < target)
            if target < LINE - 1:
                pl.when(jnp.logical_and(a > target, a < LINE - 1))(lambda: downward(True))
                pl.when(a == LINE - 1)(lambda: downward(False))
                sender.send(held, above, above_sem, dict(da=-1), a > target)

            def last():
                extra = []
                if target > 0:
                    sender.arrived(below, below_sem)
                    extra.append(below)
                if target < LINE - 1:
                    sender.arrived(above, above_sem)
                    extra.append(above)
                add_rows(rows_of(out, which), parts + extra, half)

            pl.when(a == target)(last)

    stages = [over_cores] + ([over_corner] if full else []) + [over_line]

    def tick(number):
        if number == 0:
            begin()
        for level, stage in enumerate(stages):
            if 0 <= number - level < len(order):
                stage(order[number - level])

    return [functools.partial(tick, number) for number in range(len(order) + len(stages) - 1)]


def scatter_kernel(full, pairs, part, *refs):
    ins, out, outs = refs[:pairs], refs[pairs], refs[pairs + 1 : 2 * pairs + 1]
    mine, got, side, up, down, load_sems, send_sems, recv_sems, pair_sems = refs[2 * pairs + 1 :]
    place = Place()
    sender = Sender(place, send_sems)
    place.greet(full or pairs > 0)
    send_pairs(sender, ins, outs, pair_sems)
    scratch = (mine, got, side, up, down, load_sems, recv_sems)
    for tick in scatter_ticks(place, sender, full, part, out, scratch):
        tick()
    take_pairs(sender, outs, pair_sems)
    sender.finish()


def scatter_scratch(full, rows, width, dtype, pairs):
    kinds = 4 if full else 2
    return [
        pltpu.VMEM((LINE, kinds, rows, width), dtype),
        pltpu.VMEM((LINE, kinds, rows, width), dtype),
        pltpu.VMEM((LINE, 6, rows // 2, width), dtype),
        pltpu.VMEM((LINE, rows, width), dtype),
        pltpu.VMEM((LINE, rows, width), dtype),
        pltpu.SemaphoreType.DMA((LINE * 4,)),
        pltpu.SemaphoreType.DMA((pairs + LINE * (4 + 6 + 4),)),
        pltpu.SemaphoreType.DMA((4, LINE * 4)),
        pltpu.SemaphoreType.DMA((max(pairs, 1),)),
    ]


def gather_scatter_kernel(count, gated, *refs):
    ins, part = refs[:count], refs[count]
    outs, total = refs[count + 1 : 2 * count + 1], refs[2 * count + 1]
    local_sems, gather_sends, gather_recvs = refs[2 * count + 2 : 2 * count + 5]
    mine, got, side, up, down, load_sems, scatter_sends, scatter_recvs, _ = refs[2 * count + 5 :]
    place = Place()
    gatherer = Sender(place, gather_sends)
    scatterer = Sender(place, scatter_sends)
    place.greet(True)
    scratch = (mine, got, side, up, down, load_sems, scatter_recvs)
    ticks = [
        scatter_ticks(place, scatterer, True, part, total, scratch),
        gather_ticks(place, gatherer, False, gated, ins, outs, local_sems, gather_recvs),
    ]
    for number in range(max(len(steps) for steps in ticks)):
        for steps in ticks:
            if number < len(steps):
                steps[number]()
    scatterer.finish()
    gatherer.finish()


def gather_and_scatter(arrays, part, collective_id, gated=()):
    blocks = LINE * SQUARE * CORES
    count = len(arrays)
    _, rows, width = part.shape
    sends = count * (2 * LINE - 1) * 2 * 5
    moved = sum(blocks * 2 * x.size * x.dtype.itemsize for x in arrays)
    return pl.pallas_call(
        functools.partial(gather_scatter_kernel, count, gated),
        out_shape=[jax.ShapeDtypeStruct((blocks,) + x.shape, x.dtype) for x in arrays]
        + [jax.ShapeDtypeStruct((rows, width), jnp.float32)],
        in_specs=[pl.BlockSpec(memory_space=pl.ANY)] * (count + 1),
        out_specs=[pl.BlockSpec(memory_space=pl.ANY)] * count
        + [pl.BlockSpec(memory_space=pltpu.VMEM)],
        scratch_shapes=[
            pltpu.SemaphoreType.DMA((count,)),
            pltpu.SemaphoreType.DMA((sends,)),
            pltpu.SemaphoreType.DMA((count, blocks * 2)),
        ]
        + scatter_scratch(True, rows, width, part.dtype, 0),
        compiler_params=pltpu.CompilerParams(
            collective_id=collective_id, has_side_effects=True, vmem_limit_bytes=VMEM_LIMIT
        ),
        cost_estimate=pl.CostEstimate(flops=0, bytes_accessed=6 * moved, transcendentals=0),
    )(*arrays, part)


def scatter_rows(part, full, collective_id, swapped=()):
    blocks, rows, width = part.shape
    pairs = len(swapped)
    return pl.pallas_call(
        functools.partial(scatter_kernel, full, pairs),
        out_shape=[jax.ShapeDtypeStruct((rows, width), jnp.float32)]
        + [jax.ShapeDtypeStruct(x.shape, x.dtype) for x in swapped],
        in_specs=[pl.BlockSpec(memory_space=pl.ANY)] * (1 + pairs),
        out_specs=[pl.BlockSpec(memory_space=pltpu.VMEM)]
        + [pl.BlockSpec(memory_space=pl.ANY)] * pairs,
        scratch_shapes=scatter_scratch(full, rows, width, part.dtype, pairs),
        compiler_params=pltpu.CompilerParams(
            collective_id=collective_id, has_side_effects=True, vmem_limit_bytes=VMEM_LIMIT
        ),
        cost_estimate=pl.CostEstimate(
            flops=0, bytes_accessed=12 * part.size * part.dtype.itemsize, transcendentals=0
        ),
    )(part, *swapped)


def contract_last(left, right):
    return lax.dot_general(
        left, right, (((1,), (1,)), ((), ())), preferred_element_type=jnp.float32
    )


def contract_first(left, right):
    return lax.dot_general(
        left, right, (((0,), (0,)), ((), ())), preferred_element_type=jnp.float32
    )


def expert_kernel(
    capacity,
    normed,
    grads,
    routes,
    router_rows,
    w_gate,
    w_up,
    w_down,
    shared_in,
    shared_out,
    out_part,
    d_part,
    ex_rows,
    ex_grads,
    act_out,
    d_gate_out,
    d_up_out,
    shared_in_grad,
    shared_out_grad,
    in_total,
    out_total,
):
    position = lax.axis_index("expert")
    experts = lax.axis_size("expert")
    group, rows, width = normed.shape
    tokens, slots = group * rows, group * capacity
    bf16 = jnp.bfloat16
    x = normed[...].reshape(tokens, width)
    g = grads[...].reshape(tokens, width)

    row = lax.broadcasted_iota(jnp.int32, (tokens, tokens), 0)
    column = lax.broadcasted_iota(jnp.int32, (tokens, tokens), 1)
    before = jnp.logical_and(column < row, lax.div(row, rows) == lax.div(column, rows))
    named = routes[...].reshape(tokens, -1) == position.astype(jnp.float32).astype(bf16)
    hit = jnp.sum(jnp.where(named, 1.0, 0.0), axis=1, keepdims=True)
    tally = matrix_product(
        jnp.where(before, 1.0, 0.0).astype(bf16),
        jnp.broadcast_to(hit, (tokens, 128)).astype(bf16),
    )
    place = jnp.where(hit > 0.5, tally[:, :1], -1.0)
    token = lax.broadcasted_iota(jnp.int32, (tokens, slots), 0)
    slot = lax.broadcasted_iota(jnp.int32, (tokens, slots), 1)
    same = lax.div(slot, capacity) == lax.div(token, rows)
    wanted = lax.rem(slot, capacity).astype(jnp.float32)
    chosen = jnp.where(jnp.logical_and(same, wanted == place), 1.0, 0.0)
    pick = chosen.T.astype(bf16)
    put = chosen.astype(bf16)

    r = matrix_product(pick, x).astype(bf16)
    gr = matrix_product(pick, g).astype(bf16)
    ex_rows[...] = r
    ex_grads[...] = gr
    lane = lax.broadcasted_iota(jnp.int32, (slots, router_rows.shape[0]), 1)
    logits = jnp.where(lane < experts, contract_last(r, router_rows[...]), -1e30)
    exps = jnp.exp(logits - jnp.max(logits, axis=1, keepdims=True))
    gate = jnp.sum(jnp.where(lane == position, exps, 0.0), axis=1, keepdims=True) / jnp.sum(
        exps, axis=1, keepdims=True
    )

    pre_gate = contract_last(r, w_gate[...])
    pre_up = contract_last(r, w_up[...])
    act_gate, slope = silu_parts(pre_gate)
    act = act_gate * pre_up
    back = contract_last(gr, w_down[...])
    d_gate_slot = jnp.sum(act * back, axis=1, keepdims=True)
    scaled = (gate * act).astype(bf16)
    d_act = gate * back
    d_pre_gate = (d_act * pre_up * slope).astype(bf16)
    d_pre_up = (d_act * act_gate).astype(bf16)
    act_out[...] = scaled
    d_gate_out[...] = d_pre_gate
    d_up_out[...] = d_pre_up
    ex_out = matrix_product(scaled, w_down[...]).astype(bf16)
    d_ex = matrix_product(d_pre_gate, w_gate[...]) + matrix_product(d_pre_up, w_up[...])
    d_ex = d_ex.astype(bf16)

    units = shared_out.shape[0]
    mix = matrix_product(x, shared_in[...])
    sh_gate, sh_up = mix[:, :units], mix[:, units:]
    sh_silu, sh_slope = silu_parts(sh_gate)
    sh_act = (sh_silu * sh_up).astype(bf16)
    d_sh_act = contract_last(g, shared_out[...])
    d_mix = jnp.concatenate([d_sh_act * sh_up * sh_slope, d_sh_act * sh_silu], axis=1)
    d_mix = d_mix.astype(bf16)

    out = matrix_product(put, ex_out) + matrix_product(sh_act, shared_out[...])
    out_part[...] = out.astype(bf16).reshape(group, rows, width)
    d_in = matrix_product(put, d_ex) + contract_last(d_mix, shared_in[...])
    d_part[:, :, :width] = d_in.astype(bf16).reshape(group, rows, width)
    lane = lax.broadcasted_iota(jnp.int32, (slots, d_part.shape[2] - width), 1)
    d_gates = jnp.where(lane == position, d_gate_slot, 0.0).astype(bf16)
    d_part[:, :, width:] = matrix_product(put, d_gates).astype(bf16).reshape(group, rows, -1)

    step = pl.program_id(0)

    @pl.when(step == 0)
    def _():
        in_total[...] = jnp.zeros_like(in_total)
        out_total[...] = jnp.zeros_like(out_total)

    in_total[...] += contract_first(d_mix, x)
    out_total[...] += contract_first(sh_act, g)

    @pl.when(step == pl.num_programs(0) - 1)
    def _():
        shared_in_grad[...] = in_total[...].T.astype(bf16)
        shared_out_grad[...] = out_total[...]


def expert_phase(
    all_normed, all_grads, router_rows, w_gate, w_up, w_down, shared_in, shared_out, capacity
):
    blocks, rows, width = all_normed.shape
    group = 4
    slots = group * capacity
    hidden = w_gate.shape[0]
    units = shared_out.shape[0]
    side = all_grads.shape[2] - width
    bf16 = jnp.bfloat16

    def by_group(shape):
        zeros = (0,) * (len(shape) - 1)
        return pl.BlockSpec(shape, lambda i: (i,) + zeros)

    def fixed(shape):
        return pl.BlockSpec(
            shape, lambda i: (0,) * len(shape), pipeline_mode=pl.Buffered(buffer_count=1)
        )

    return pl.pallas_call(
        functools.partial(expert_kernel, capacity),
        grid=(blocks // group,),
        out_shape=[
            jax.ShapeDtypeStruct((blocks, rows, width), bf16),
            jax.ShapeDtypeStruct((blocks, rows, width + side), bf16),
            jax.ShapeDtypeStruct((blocks * capacity, width), bf16),
            jax.ShapeDtypeStruct((blocks * capacity, width), bf16),
            jax.ShapeDtypeStruct((blocks * capacity, hidden), bf16),
            jax.ShapeDtypeStruct((blocks * capacity, hidden), bf16),
            jax.ShapeDtypeStruct((blocks * capacity, hidden), bf16),
            jax.ShapeDtypeStruct((width, 2 * units), bf16),
            jax.ShapeDtypeStruct((units, width), jnp.float32),
        ],
        in_specs=[
            by_group((group, rows, width)),
            by_group((group, rows, width)),
            pl.BlockSpec((group, rows, side), lambda i: (i, 0, width // side)),
            fixed(router_rows.shape),
            fixed(w_gate.shape),
            fixed(w_up.shape),
            fixed(w_down.shape),
            fixed(shared_in.shape),
            fixed(shared_out.shape),
        ],
        out_specs=[
            by_group((group, rows, width)),
            by_group((group, rows, width + side)),
            by_group((slots, width)),
            by_group((slots, width)),
            by_group((slots, hidden)),
            by_group((slots, hidden)),
            by_group((slots, hidden)),
            fixed((width, 2 * units)),
            fixed((units, width)),
        ],
        scratch_shapes=[
            pltpu.VMEM((2 * units, width), jnp.float32),
            pltpu.VMEM((units, width), jnp.float32),
        ],
        compiler_params=pltpu.CompilerParams(vmem_limit_bytes=VMEM_LIMIT),
        cost_estimate=pl.CostEstimate(
            flops=2 * blocks * capacity * width * hidden * 6,
            bytes_accessed=10 * blocks * rows * width * 2,
            transcendentals=blocks * capacity * hidden,
        ),
    )(all_normed, all_grads, all_grads, router_rows, w_gate, w_up, w_down, shared_in, shared_out)


def exchange_kernel(x, out, local_sem, send_sems, recv_sems):
    me, y = lax.axis_index("expert"), lax.axis_index("fsdp")
    count = x.shape[0]
    barrier = pltpu.get_barrier_semaphore()
    peers = [lax.rem(me + step, count) for step in range(1, count)]
    for peer in peers:
        pl.semaphore_signal(barrier, inc=1, device_id=(peer, y), device_id_type=MESH)
    own = pltpu.make_async_copy(x.at[me], out.at[me], local_sem)
    own.start()
    pl.semaphore_wait(barrier, count - 1)
    copies = []
    for at, peer in enumerate(peers):
        copy = pltpu.make_async_remote_copy(
            src_ref=x.at[peer],
            dst_ref=out.at[me],
            send_sem=send_sems.at[at],
            recv_sem=recv_sems.at[at],
            device_id=(peer, y),
            device_id_type=MESH,
        )
        copy.start()
        copies.append(copy)
    for copy in copies:
        copy.wait()
    own.wait()


def exchange(x, collective_id):
    count = x.shape[0]
    return pl.pallas_call(
        exchange_kernel,
        out_shape=jax.ShapeDtypeStruct(x.shape, x.dtype),
        in_specs=[pl.BlockSpec(memory_space=pl.ANY)],
        out_specs=pl.BlockSpec(memory_space=pl.ANY),
        scratch_shapes=[
            pltpu.SemaphoreType.DMA,
            pltpu.SemaphoreType.DMA((count - 1,)),
            pltpu.SemaphoreType.DMA((count - 1,)),
        ],
        compiler_params=pltpu.CompilerParams(collective_id=collective_id, has_side_effects=True),
        cost_estimate=pl.CostEstimate(
            flops=0, bytes_accessed=20 * x.size * x.dtype.itemsize, transcendentals=0
        ),
    )(x)


def swap_halves(value):
    half = value.shape[1] // 2
    return jnp.concatenate([value[:, half:], value[:, :half]], axis=1)


def attend_kernel(
    rows,
    g_attn,
    w_front,
    g_lat,
    expand_head,
    cosines,
    sines,
    normed_out,
    latent_out,
    query_out,
    key_out,
    value_out,
    head_out,
    sum_out,
    log_out,
    keys,
    values,
):
    bf16 = jnp.bfloat16
    size = rows.shape[0]
    scale = (PLAIN_UNITS + ROTARY_UNITS) ** (-0.5)
    step = pl.program_id(0)
    normed, _ = norm_forward(rows[...].astype(jnp.float32), g_attn[...])
    normed = normed.astype(bf16)
    normed_out[...] = normed
    front = contract_last(normed, w_front[...])
    latent, _ = norm_forward(front[:, :LATENT_WIDTH], g_lat[...])
    latent = latent.astype(bf16)
    latent_out[...] = latent
    width = LATENT_WIDTH + ROTARY_UNITS

    def rotated(value):
        return value * cosines[...] + swap_halves(value) * sines[...]

    pairs = matrix_product(latent, expand_head[...])
    key = jnp.concatenate([pairs[:, :PLAIN_UNITS], rotated(front[:, LATENT_WIDTH:width])], axis=1)
    query = jnp.concatenate(
        [front[:, width : width + PLAIN_UNITS], rotated(front[:, width + PLAIN_UNITS :])], axis=1
    ).astype(bf16)
    key = key.astype(bf16)
    value = pairs[:, PLAIN_UNITS:].astype(bf16)
    query_out[...] = query
    key_out[...] = key
    value_out[...] = value
    here = pl.ds(pl.multiple_of(step * size, size), size)
    keys[here, :] = key
    values[here, :] = value
    row = lax.broadcasted_iota(jnp.int32, (size, size), 0)
    column = lax.broadcasted_iota(jnp.int32, (size, size), 1)
    near = jnp.where(column <= row, contract_last(query, key) * scale, -1e30)

    def over(past):
        top = jnp.max(near, axis=1, keepdims=True)
        if past:
            far = contract_last(query, keys[:past, :]) * scale
            top = jnp.maximum(top, jnp.max(far, axis=1, keepdims=True))
        exps = jnp.exp(near - top)
        total = jnp.sum(exps, axis=1, keepdims=True)
        mixed = matrix_product(exps.astype(bf16), value)
        if past:
            exps = jnp.exp(far - top)
            total = total + jnp.sum(exps, axis=1, keepdims=True)
            mixed = mixed + matrix_product(exps.astype(bf16), values[:past, :])
        mixed = mixed / total
        sum_out[...] = mixed
        head_out[...] = mixed.astype(bf16)
        wide = jnp.broadcast_to(top + jnp.log(total), (size, 128))
        log_out[0] = wide.T[:1, :]

    for at in range(keys.shape[0] // size):
        pl.when(step == at)(functools.partial(over, at * size))


def attend(rows, g_attn, w_front, g_lat, expand_head, cosines, sines):
    seq_len, width = rows.shape
    size = 256
    steps = seq_len // size
    units = PLAIN_UNITS + ROTARY_UNITS
    bf16 = jnp.bfloat16

    def by_step(columns):
        return pl.BlockSpec((size, columns), lambda i: (i, 0))

    def fixed(x):
        return pl.BlockSpec(
            x.shape, lambda i: (0, 0), pipeline_mode=pl.Buffered(buffer_count=1)
        )

    return pl.pallas_call(
        attend_kernel,
        grid=(steps,),
        out_shape=[
            jax.ShapeDtypeStruct((seq_len, width), bf16),
            jax.ShapeDtypeStruct((seq_len, LATENT_WIDTH), bf16),
            jax.ShapeDtypeStruct((seq_len, units), bf16),
            jax.ShapeDtypeStruct((seq_len, units), bf16),
            jax.ShapeDtypeStruct((seq_len, VALUE_UNITS), bf16),
            jax.ShapeDtypeStruct((seq_len, VALUE_UNITS), bf16),
            jax.ShapeDtypeStruct((seq_len, VALUE_UNITS), jnp.float32),
            jax.ShapeDtypeStruct((steps, 1, size), jnp.float32),
        ],
        in_specs=[by_step(width)]
        + [fixed(x) for x in (g_attn, w_front, g_lat, expand_head)]
        + [by_step(ROTARY_UNITS)] * 2,
        out_specs=[
            by_step(width),
            by_step(LATENT_WIDTH),
            by_step(units),
            by_step(units),
            by_step(VALUE_UNITS),
            by_step(VALUE_UNITS),
            by_step(VALUE_UNITS),
            pl.BlockSpec((1, 1, size), lambda i: (i, 0, 0)),
        ],
        scratch_shapes=[
            pltpu.VMEM((seq_len, units), bf16),
            pltpu.VMEM((seq_len, VALUE_UNITS), bf16),
        ],
        compiler_params=pltpu.CompilerParams(vmem_limit_bytes=VMEM_LIMIT),
        cost_estimate=pl.CostEstimate(
            flops=2 * seq_len * (width * 768 + seq_len * units),
            bytes_accessed=3 * rows.size * 2,
            transcendentals=seq_len * seq_len // 2,
        ),
    )(rows, g_attn, w_front, g_lat, expand_head, cosines, sines)


def attend_back_kernel(
    query,
    key,
    value,
    d_head,
    head_sum,
    logs,
    expand_head,
    cosines,
    sines,
    d_query_out,
    d_pairs_out,
    d_keys_out,
    d_key,
    d_value,
    key_turned,
):
    bf16 = jnp.bfloat16
    size = query.shape[0]
    seq_len = key.shape[0]
    scale = (PLAIN_UNITS + ROTARY_UNITS) ** (-0.5)
    step = pl.program_id(0)

    @pl.when(step == 0)
    def _():
        d_key[...] = jnp.zeros_like(d_key)
        d_value[...] = jnp.zeros_like(d_value)
        for at in range(0, seq_len, size):
            part = key[at : at + size, :].astype(jnp.float32)
            key_turned[:, at : at + size] = part.T.astype(bf16)

    q, d_out = query[...], d_head[...]
    product = d_out.astype(jnp.float32) * head_sum[...]
    delta = jnp.sum(product.T, axis=0, keepdims=True)
    log_row = logs[0]
    row = lax.broadcasted_iota(jnp.int32, (size, size), 0)
    column = lax.broadcasted_iota(jnp.int32, (size, size), 1)

    def grads_of(at, mask):
        there = slice(at, at + size)
        scores = contract_last(key[there, :], q) * scale
        if mask:
            scores = jnp.where(row <= column, scores, -1e30)
        probs = jnp.exp(scores - log_row)
        d_probs = contract_last(value[there, :], d_out)
        d_scores = (probs * (d_probs - delta) * scale).astype(bf16)
        d_key[there, :] += matrix_product(d_scores, q)
        d_value[there, :] += matrix_product(probs.astype(bf16), d_out)
        return matrix_product(key_turned[:, there], d_scores)

    def over(past):
        total = grads_of(past, True)
        for at in range(0, past, size):
            total = total + grads_of(at, False)
        d_query = total.T
        d_rope = d_query[:, PLAIN_UNITS:]
        d_rope = d_rope * cosines[...] - swap_halves(d_rope) * sines[...]
        d_query_out[...] = jnp.concatenate([d_query[:, :PLAIN_UNITS], d_rope], axis=1).astype(bf16)

    for at in range(seq_len // size):
        pl.when(step == at)(functools.partial(over, at * size))

    @pl.when(step == seq_len // size - 1)
    def _():
        for at in range(0, seq_len, size):
            there = slice(at, at + size)
            d_pairs = jnp.concatenate(
                [d_key[there, :PLAIN_UNITS], d_value[there, :]], axis=1
            ).astype(bf16)
            d_pairs_out[there, :] = d_pairs
            d_keys_out[there, :LATENT_WIDTH] = contract_last(d_pairs, expand_head[...]).astype(bf16)
            tail = jnp.concatenate(
                [d_key[there, PLAIN_UNITS:], jnp.zeros((size, ROTARY_UNITS), jnp.float32)], axis=1
            )
            d_keys_out[there, LATENT_WIDTH:] = tail.astype(bf16)


def attend_back(query, key, value, d_head, head_sum, logs, expand_head, cosines, sines):
    seq_len, units = query.shape
    steps, _, size = logs.shape
    bf16 = jnp.bfloat16
    keys_width = LATENT_WIDTH + 2 * ROTARY_UNITS

    def by_step(columns):
        return pl.BlockSpec((size, columns), lambda i: (i, 0))

    def fixed(shape):
        return pl.BlockSpec(shape, lambda i: (0, 0), pipeline_mode=pl.Buffered(buffer_count=1))

    return pl.pallas_call(
        attend_back_kernel,
        grid=(steps,),
        out_shape=[
            jax.ShapeDtypeStruct((seq_len, units), bf16),
            jax.ShapeDtypeStruct((seq_len, PLAIN_UNITS + VALUE_UNITS), bf16),
            jax.ShapeDtypeStruct((seq_len, keys_width), bf16),
        ],
        in_specs=[
            by_step(units),
            fixed(key.shape),
            fixed(value.shape),
            by_step(VALUE_UNITS),
            by_step(VALUE_UNITS),
            pl.BlockSpec((1, 1, size), lambda i: (i, 0, 0)),
            fixed(expand_head.shape),
            by_step(ROTARY_UNITS),
            by_step(ROTARY_UNITS),
        ],
        out_specs=[
            by_step(units),
            fixed((seq_len, PLAIN_UNITS + VALUE_UNITS)),
            fixed((seq_len, keys_width)),
        ],
        scratch_shapes=[
            pltpu.VMEM((seq_len, units), jnp.float32),
            pltpu.VMEM((seq_len, VALUE_UNITS), jnp.float32),
            pltpu.VMEM((units, seq_len), bf16),
        ],
        compiler_params=pltpu.CompilerParams(vmem_limit_bytes=VMEM_LIMIT),
        cost_estimate=pl.CostEstimate(
            flops=5 * seq_len * seq_len * units,
            bytes_accessed=8 * seq_len * units * 2,
            transcendentals=seq_len * seq_len // 2,
        ),
    )(query, key, value, d_head, head_sum, logs, expand_head, cosines, sines)


def finish_kernel(shard, query, expand, out_rows, query_out, expand_out, out_out):
    heads, units, width = query.shape
    query_out[...] = query[...].reshape(heads * units, width).astype(jnp.float32).T
    for at in range(heads):
        columns = expand.shape[2]
        expand_out[:, at * columns : (at + 1) * columns] = expand[at].astype(jnp.float32)
    out_out[...] = out_rows[0].astype(jnp.float32)


def finish(shard, query, expand, out_rows):
    heads, units, width = query.shape
    _, latents, columns = expand.shape
    _, rows, model = out_rows.shape
    steps = heads // 2
    return pl.pallas_call(
        finish_kernel,
        out_shape=[
            jax.ShapeDtypeStruct((width, heads * units), jnp.float32),
            jax.ShapeDtypeStruct((latents, heads * columns), jnp.float32),
            jax.ShapeDtypeStruct((steps * rows, model), jnp.float32),
        ],
        grid_spec=pltpu.PrefetchScalarGridSpec(
            num_scalar_prefetch=1,
            grid=(steps,),
            in_specs=[
                pl.BlockSpec((2, units, width), lambda i, shard: (i, 0, 0)),
                pl.BlockSpec((2, latents, columns), lambda i, shard: (i, 0, 0)),
                pl.BlockSpec((1, rows, model), lambda i, shard: (shard[0] * steps + i, 0, 0)),
            ],
            out_specs=[
                pl.BlockSpec((width, 2 * units), lambda i, shard: (0, i)),
                pl.BlockSpec((latents, 2 * columns), lambda i, shard: (0, i)),
                pl.BlockSpec((rows, model), lambda i, shard: (i, 0)),
            ],
        ),
        compiler_params=pltpu.CompilerParams(vmem_limit_bytes=VMEM_LIMIT),
        cost_estimate=pl.CostEstimate(
            flops=0, bytes_accessed=6 * heads * units * width, transcendentals=0
        ),
    )(shard.reshape(1), query, expand, out_rows)


def token_gather(rows):
    return lax.all_gather(rows, ("fsdp", "expert"), axis=0, tiled=True)


def token_scatter(partial):
    return lax.psum_scatter(
        partial, ("fsdp", "expert"), scatter_dimension=0, tiled=True
    ).astype(jnp.float32)


def split_body(
    tokens,
    routes,
    cotangent,
    attn_gain,
    w_query,
    latent_weight,
    latent_norm_gain,
    expand_weight,
    w_out,
    ffn_gain,
    w_router,
    shared_gate,
    shared_up,
    shared_down,
    expert_gate,
    expert_up,
    expert_down,
):
    rows = tokens.shape[1]
    experts = lax.axis_size("expert")
    shards = lax.axis_size("fsdp")
    position = lax.axis_index("expert")
    blocks = experts * shards
    seq_len = rows * experts
    capacity = shards * ((rows * TOPK * 4 + experts * 3 * shards - 1) // (experts * 3 * shards))
    head_units = PLAIN_UNITS + ROTARY_UNITS
    pair_units = PLAIN_UNITS + VALUE_UNITS
    feature_width = LATENT_WIDTH + ROTARY_UNITS
    scale = head_units ** (-0.5)

    shard = lax.axis_index("fsdp")
    first = shard == 0

    query_cols = lax.dynamic_slice_in_dim(w_query, position * head_units, head_units, 1)
    expand_cols = lax.dynamic_slice_in_dim(expand_weight, position * pair_units, pair_units, 1)
    owners = experts // shards
    lat_row = jnp.pad(latent_norm_gain, (0, w_query.shape[0] - latent_norm_gain.shape[0]))
    packed = jnp.concatenate(
        [latent_weight.T, query_cols.T, w_router.T, attn_gain[None], ffn_gain[None], lat_row[None]],
        axis=0,
    )
    packed = jnp.pad(packed, ((0, -packed.shape[0] % 32), (0, 0)))
    seq_rows, other_packed, other_expand = gather_rows(
        [tokens[0]], False, 0, swapped=[packed, expand_cols]
    )

    def whole(own, other, axis):
        return jnp.concatenate(
            [jnp.where(first, own, other), jnp.where(first, other, own)], axis=axis
        )

    lat_half = latent_norm_gain.shape[0]
    at = feature_width + head_units
    packed_rows = whole(packed, other_packed, 1)
    expand_head = whole(expand_cols, other_expand, 0)
    w_front = packed_rows[:at]
    w_latent = packed_rows[:feature_width]
    router_rows = packed_rows[at:]
    wrout = packed_rows[at : at + experts]
    g_attn = packed_rows[at + experts].astype(jnp.float32)
    g_ffn = packed_rows[at + experts + 1].astype(jnp.float32)
    lat_row = packed_rows[at + experts + 2]
    g_lat = jnp.concatenate(
        [lat_row[:lat_half], lat_row[w_query.shape[0] : w_query.shape[0] + lat_half]]
    ).astype(jnp.float32)
    units = shared_down.shape[0]

    def to_columns(weight):
        parts = weight.reshape(weight.shape[0], blocks, units).transpose(1, 0, 2)
        return lax.all_to_all(
            parts, ("expert", "fsdp"), split_axis=0, concat_axis=0, tiled=True
        ).reshape(-1, units)

    sh_cols = to_columns(jnp.concatenate([shared_gate, shared_up], axis=0)).reshape(
        blocks, 2, shared_gate.shape[0], units
    )
    lanes = -(-units // 128) * 128
    sh_cols = jnp.pad(sh_cols, ((0, 0), (0, 0), (0, 0), (0, lanes - units)))
    shared_in = sh_cols.transpose(0, 2, 1, 3).reshape(MODEL_WIDTH, 2 * lanes)
    wout = lax.all_gather(w_out, "fsdp", axis=0, tiled=True)
    shared_out = jnp.pad(shared_down, ((0, lanes - units), (0, 0)))
    grad_rows = cotangent[0]
    grad_out = grad_rows.astype(jnp.float32)
    own_routes = jnp.pad(routes[0], ((0, 0), (0, 128 - TOPK)), constant_values=-1)
    grad_rows = jnp.concatenate([grad_rows, own_routes.astype(jnp.bfloat16)], axis=1)
    seq_rows, grad_rows = lax.optimization_barrier((seq_rows, grad_rows))
    all_grads = token_gather(grad_rows)

    x_in = tokens[0].astype(jnp.float32)
    normed, inv_attn = norm_forward(x_in, g_attn)
    normed_in = normed.astype(jnp.bfloat16)
    cosine_table, sine_table = rope_tables(jnp.arange(seq_len, dtype=jnp.int32))
    cosines = jnp.concatenate([cosine_table, cosine_table], axis=1)
    sines = jnp.concatenate([-sine_table, sine_table], axis=1)
    (
        seq_normed,
        latent_rows,
        query,
        key,
        value,
        head_rows,
        head_sum,
        logs,
    ) = attend(
        seq_rows.reshape(seq_len, MODEL_WIDTH),
        g_attn[None],
        w_front,
        g_lat[None],
        expand_head,
        cosines,
        sines,
    )
    heads = exchange(head_rows.reshape(experts, rows, VALUE_UNITS), 1)
    heads = heads.transpose(1, 0, 2).reshape(rows, experts * VALUE_UNITS)
    hidden = x_in + matrix_product(heads, wout)
    normed2, inv_ffn = norm_forward(hidden, g_ffn)
    normed_ffn = normed2.astype(jnp.bfloat16)
    router = jax.nn.softmax(outer_product(normed_ffn, wrout), axis=-1)

    (all_normed,) = gather_rows([normed_ffn], True, 2)
    w_query, all_normed = lax.optimization_barrier((w_query, all_normed))
    wq = lax.all_gather(w_query, "fsdp", axis=0, tiled=True)
    (
        out_part,
        d_part,
        ex_rows,
        ex_grads,
        scaled_act,
        d_pre_gate,
        d_pre_up,
        g_shared_in,
        g_shared_out,
    ) = expert_phase(
        all_normed,
        all_grads.reshape(blocks, rows, -1),
        router_rows,
        expert_gate[0].T,
        expert_up[0].T,
        expert_down[0],
        shared_in,
        shared_out,
        capacity,
    )
    g_down = inner(scaled_act, ex_grads)
    g_gate = inner(d_pre_gate, ex_rows).T
    g_up = inner(d_pre_up, ex_rows).T
    (d_back,) = scatter_rows(d_part, True, 3)
    out_part, d_back = lax.optimization_barrier((out_part, d_back))
    d_normed_ffn = d_back[:, :MODEL_WIDTH]
    d_router = d_back[:, MODEL_WIDTH : MODEL_WIDTH + experts]
    output = hidden + token_scatter(out_part.reshape(blocks * rows, MODEL_WIDTH))

    d_logits = (router * (d_router - jnp.sum(router * d_router, axis=1, keepdims=True))).astype(
        jnp.bfloat16
    )
    g_router = inner(d_logits, normed_ffn)
    d_normed_ffn = d_normed_ffn + matrix_product(d_logits, wrout)
    d_hidden_norm, g_ffn_grad = norm_backward(hidden, inv_ffn, g_ffn, d_normed_ffn)
    d_hidden = grad_out + d_hidden_norm
    d_attn = d_hidden.astype(jnp.bfloat16)

    d_heads = outer_product(d_attn, wout).astype(jnp.bfloat16)
    d_heads = d_heads.reshape(rows, experts, VALUE_UNITS).transpose(1, 0, 2)
    d_head = exchange(d_heads, 4).reshape(seq_len, VALUE_UNITS)
    seq_d_attn = lax.all_gather(d_attn, "expert", axis=0, tiled=True)
    d_query_full, d_pairs, d_keys = attend_back(
        query, key, value, d_head, head_sum, logs, expand_head, cosines, sines
    )
    g_out_head = inner(head_rows, seq_d_attn)
    g_expand_head = inner(latent_rows, d_pairs)
    g_query_head = inner(d_query_full, seq_normed).astype(jnp.bfloat16)
    g_expand_head = g_expand_head.astype(jnp.bfloat16)
    g_out_head = g_out_head.astype(jnp.bfloat16)

    def half_of(whole, which, axis):
        size = whole.shape[axis] // shards
        return lax.dynamic_slice_in_dim(whole, which * size, size, axis)

    own_d_query = exchange(d_query_full.reshape(experts, rows, head_units), 8)
    own_d_query = own_d_query.transpose(1, 0, 2).reshape(rows, experts * head_units)
    d_sums, other_query, other_expand, other_out_grad = scatter_rows(
        d_keys.reshape(experts, rows, -1),
        False,
        5,
        swapped=[
            half_of(g_query_head, 1 - shard, 1),
            half_of(g_expand_head, 1 - shard, 0),
            g_out_head,
        ],
    )
    key_gradient = d_sums[:, :feature_width]
    d_normed_in = outer_product(own_d_query, wq)

    def summed(own, other):
        return (own.astype(jnp.float32) + other.astype(jnp.float32)).astype(jnp.bfloat16)

    own_query = summed(half_of(g_query_head, shard, 1), other_query)
    own_expand = summed(half_of(g_expand_head, shard, 0), other_expand)
    own_out = summed(g_out_head, other_out_grad)
    own_latent = outer_product(normed_in, w_latent[:LATENT_WIDTH])
    own_cosine = lax.dynamic_slice_in_dim(cosine_table, position * rows, rows, 0)
    own_sine = lax.dynamic_slice_in_dim(sine_table, position * rows, rows, 0)
    inv_lat = lax.rsqrt(jnp.mean(own_latent * own_latent, axis=-1, keepdims=True) + EPS)
    d_compact, g_lat_grad = norm_backward(
        own_latent, inv_lat, g_lat, key_gradient[:, :LATENT_WIDTH]
    )
    d_rope = reverse_rotary(key_gradient[:, LATENT_WIDTH:], own_cosine, own_sine)
    d_latent_full = jnp.concatenate([d_compact, d_rope], axis=-1).astype(jnp.bfloat16)
    g_latent = inner(d_latent_full, normed_in)
    d_normed_in = d_normed_in + matrix_product(d_latent_full, w_latent)
    d_norm_in, g_attn_grad = norm_backward(x_in, inv_attn, g_attn, d_normed_in)
    d_tokens = (d_hidden + d_norm_in).astype(jnp.bfloat16)

    half = MODEL_WIDTH // blocks
    cols = lax.all_to_all(
        g_shared_in.reshape(blocks, half, 2 * lanes),
        ("expert", "fsdp"),
        split_axis=0,
        concat_axis=0,
        tiled=True,
    )
    cols = cols.transpose(1, 0, 2).astype(jnp.float32)
    r_sgate = cols[:, :, :units].reshape(half, blocks * units)
    r_sup = cols[:, :, lanes : lanes + units].reshape(half, blocks * units)
    g_sdown = g_shared_out[:units]
    model_half = MODEL_WIDTH // shards
    small_rows = jnp.concatenate([g_latent, g_router, g_attn_grad[None], g_ffn_grad[None]], axis=0)
    used = small_rows.shape[0]
    share = 2 * 32 * (-(-(used + 1) // (2 * 32 * experts)))

    def rows_for(which):
        here = small_rows[:, which * model_half : (which + 1) * model_half]
        lat = jnp.pad(
            g_lat_grad[which * lat_half : (which + 1) * lat_half], (0, model_half - lat_half)
        )
        full = jnp.concatenate([here, lat[None]], axis=0).astype(jnp.bfloat16)
        full = jnp.pad(full, ((0, experts * share - used - 1), (0, 0)))
        return full.reshape(experts, share, model_half)

    small_part = jnp.concatenate([rows_for(which) for which in range(shards)], axis=0)
    r_query, r_expand, r_out, small_sum = gather_and_scatter(
        [own_query, own_expand, own_out], small_part, 6, gated=(2,)
    )
    (small_all,) = gather_rows([small_sum.astype(jnp.bfloat16)], False, 7)
    r_query, r_expand, r_out = finish(shard, r_query, r_expand, r_out)
    small_all = small_all.reshape(experts * share, model_half).astype(jnp.float32)
    return (
        output.astype(jnp.bfloat16)[None],
        d_tokens[None],
        small_all[feature_width + experts],
        r_query,
        small_all[:feature_width].T,
        small_all[feature_width + experts + 2, :lat_half],
        r_expand,
        r_out,
        small_all[feature_width + experts + 1],
        small_all[feature_width : feature_width + experts].T,
        r_sgate,
        r_sup,
        g_sdown,
        g_gate[None],
        g_up[None],
        g_down[None],
    )


def solution(mesh):
    shape = (mesh.shape["expert"], mesh.shape["fsdp"])
    split = shape == (LINE * SQUARE * CORES, SQUARE) and shape[0] == HEAD_COUNT
    return jax.shard_map(
        split_body if split else body,
        mesh=mesh,
        in_specs=(
            P("fsdp", "expert", None),
            P("fsdp", "expert", None),
            P("fsdp", "expert", None),
            P("fsdp"),
            P("fsdp", None),
            P("fsdp", None),
            P("fsdp"),
            P("fsdp", None),
            P("fsdp", None),
            P("fsdp"),
            P("fsdp", None),
            P(("expert", "fsdp"), None),
            P(("expert", "fsdp"), None),
            P(("expert", "fsdp"), None),
            P("expert", None, "fsdp"),
            P("expert", None, "fsdp"),
            P("expert", "fsdp", None),
        ),
        out_specs=(
            P("fsdp", "expert", None),
            P("fsdp", "expert", None),
            P("fsdp"),
            P("fsdp", None),
            P("fsdp", None),
            P("fsdp"),
            P("fsdp", None),
            P("fsdp", None),
            P("fsdp"),
            P("fsdp", None),
            P(("expert", "fsdp"), None),
            P(("expert", "fsdp"), None),
            P(("expert", "fsdp"), None),
            P("expert", None, "fsdp"),
            P("expert", None, "fsdp"),
            P("expert", "fsdp", None),
        ),
        check_vma=False,
    )
```

```python
import functools

import jax
import jax.numpy as jnp
from jax import lax
from jax.experimental import pallas as pl
from jax.experimental.pallas import tpu as pltpu
from jax.sharding import PartitionSpec as P

MODEL_WIDTH = 2048
HEAD_COUNT = 16
PLAIN_UNITS = 128
ROTARY_UNITS = 64
VALUE_UNITS = 128
LATENT_WIDTH = 512
TOPK = 6


EPS = 1e-06


def matrix_product(left, right):
    return jnp.dot(left, right, preferred_element_type=jnp.float32)


def inner(left, right):
    return lax.dot_general(
        left, right, (((0,), (0,)), ((), ())), preferred_element_type=jnp.float32
    )


def outer_product(left, right):
    return lax.dot_general(
        left, right, (((1,), (1,)), ((), ())), preferred_element_type=jnp.float32
    )


def norm_forward(value, gain):
    inverse = lax.rsqrt(jnp.mean(value * value, axis=-1, keepdims=True) + EPS)
    return (value * inverse * gain, inverse)


def norm_backward(value, inverse, gain, grad):
    unit = value * inverse
    scaled = grad * gain
    d_value = inverse * (scaled - unit * jnp.mean(scaled * unit, axis=-1, keepdims=True))
    return (d_value, jnp.sum(grad * unit, axis=0))


def rope_tables(positions):
    half = ROTARY_UNITS // 2
    freqs = 10000.0 ** (-jnp.arange(half, dtype=jnp.float32) * (2.0 / ROTARY_UNITS))
    angles = positions.astype(jnp.float32)[:, None] * freqs[None, :]
    return (jnp.cos(angles), jnp.sin(angles))


def apply_rotary(value, cosine_table, sine_table):
    half = ROTARY_UNITS // 2
    first = value[..., :half]
    second = value[..., half:]
    return jnp.concatenate(
        [first * cosine_table - second * sine_table, first * sine_table + second * cosine_table],
        axis=-1,
    )


def reverse_rotary(grad, cosine_table, sine_table):
    half = ROTARY_UNITS // 2
    first = grad[..., :half]
    second = grad[..., half:]
    return jnp.concatenate(
        [first * cosine_table + second * sine_table, second * cosine_table - first * sine_table],
        axis=-1,
    )


def silu_parts(value):
    sigma = jax.nn.sigmoid(value)
    return (value * sigma, sigma * (1.0 + value * (1.0 - sigma)))


def body(
    tokens,
    routes,
    cotangent,
    attn_gain,
    w_query,
    latent_weight,
    latent_norm_gain,
    expand_weight,
    w_out,
    ffn_gain,
    w_router,
    shared_gate,
    shared_up,
    shared_down,
    expert_gate,
    expert_up,
    expert_down,
):
    device_local = tokens.shape[1]
    experts = lax.axis_size("expert")
    shards = lax.axis_size("fsdp")
    position = lax.axis_index("expert")
    capacity = shards * (
        (device_local * TOPK * 4 + experts * 3 * shards - 1) // (experts * 3 * shards)
    )
    seq_len = device_local * experts
    feature_width = LATENT_WIDTH + ROTARY_UNITS
    scale = (PLAIN_UNITS + ROTARY_UNITS) ** (-0.5)
    attention_gain_grad, wq, wlat, g_lat, expand_matrix, wout, g_ffn, wrout = (
        lax.all_gather(attn_gain, "fsdp", axis=0, tiled=True),
        lax.all_gather(w_query, "fsdp", axis=0, tiled=True),
        lax.all_gather(latent_weight, "fsdp", axis=0, tiled=True),
        lax.all_gather(latent_norm_gain, "fsdp", axis=0, tiled=True),
        lax.all_gather(expand_weight, "fsdp", axis=0, tiled=True),
        lax.all_gather(w_out, "fsdp", axis=0, tiled=True),
        lax.all_gather(ffn_gain, "fsdp", axis=0, tiled=True),
        lax.all_gather(w_router, "fsdp", axis=0, tiled=True),
    )
    sgate, sup, sdown = (
        lax.all_gather(shared_gate, ("expert", "fsdp"), axis=0, tiled=True),
        lax.all_gather(shared_up, ("expert", "fsdp"), axis=0, tiled=True),
        lax.all_gather(shared_down, ("expert", "fsdp"), axis=0, tiled=True),
    )
    attention_gain_grad = attention_gain_grad.astype(jnp.float32)
    g_lat = g_lat.astype(jnp.float32)
    g_ffn = g_ffn.astype(jnp.float32)
    x_in = tokens[0].astype(jnp.float32)
    grad_out = cotangent[0].astype(jnp.float32)
    positions = position * device_local + jnp.arange(device_local, dtype=jnp.int32)
    cosine_table, sine_table = rope_tables(positions)
    normed, inv_attn = norm_forward(x_in, attention_gain_grad)
    normed_in = normed.astype(jnp.bfloat16)
    query_full = matrix_product(normed_in, wq).reshape(
        device_local, HEAD_COUNT, PLAIN_UNITS + ROTARY_UNITS
    )
    query_nope = query_full[:, :, :PLAIN_UNITS].astype(jnp.bfloat16)
    expanded_latent = expand_matrix.reshape(LATENT_WIDTH, HEAD_COUNT, PLAIN_UNITS + VALUE_UNITS)
    key_part = expanded_latent[:, :, :PLAIN_UNITS]
    value_part = expanded_latent[:, :, PLAIN_UNITS:]
    query_latent = jnp.einsum(
        "thd,chd->thc", query_nope, key_part, preferred_element_type=jnp.float32
    )
    query_rope = apply_rotary(
        query_full[:, :, PLAIN_UNITS:], cosine_table[:, None, :], sine_table[:, None, :]
    )
    token_rows = device_local * HEAD_COUNT
    query = (
        jnp.concatenate([query_latent, query_rope], axis=-1)
        .astype(jnp.bfloat16)
        .reshape(token_rows, feature_width)
    )
    latent_complete = matrix_product(normed_in, wlat)
    packed_rows = latent_complete[:, :LATENT_WIDTH]
    latent_state, inv_lat = norm_forward(packed_rows, g_lat)
    rotary_key = apply_rotary(latent_complete[:, LATENT_WIDTH:], cosine_table, sine_table)
    key = jnp.concatenate([latent_state, rotary_key], axis=-1).astype(jnp.bfloat16)
    keys_all = lax.all_gather(key, "expert", axis=0, tiled=True)
    block = min(512, seq_len)
    token_tally = (position * device_local + device_local + block - 1) // block
    q_pos = position * device_local + jnp.arange(token_rows, dtype=jnp.int32) // HEAD_COUNT

    def scores_of(index):
        key_rows = lax.dynamic_slice_in_dim(keys_all, index * block, block, 0)
        raw = outer_product(query, key_rows)
        k_pos = index * block + jnp.arange(block, dtype=jnp.int32)
        valid = k_pos[None, :] <= q_pos[:, None]
        return (jnp.where(valid, raw * scale, -1e30), key_rows)

    def stats_step(index, carry):
        top, total = carry
        scores, unused = scores_of(index)
        new_top = jnp.maximum(top, jnp.max(scores, axis=1))
        total = total * jnp.exp(top - new_top) + jnp.sum(jnp.exp(scores - new_top[:, None]), axis=1)
        return (new_top, total)

    top, total = lax.fori_loop(
        0,
        token_tally,
        stats_step,
        (jnp.full((token_rows,), -1e30, jnp.float32), jnp.zeros((token_rows,), jnp.float32)),
    )
    log_total = top + jnp.log(total)

    def mixing_update(index, running_total):
        scores, key_rows = scores_of(index)
        weight_arrays = jnp.exp(scores - log_total[:, None]).astype(jnp.bfloat16)
        return running_total + matrix_product(weight_arrays, key_rows[:, :LATENT_WIDTH])

    mixed_output_sum = lax.fori_loop(
        0, token_tally, mixing_update, jnp.zeros((token_rows, LATENT_WIDTH), jnp.float32)
    )
    mixed_output = mixed_output_sum.astype(jnp.bfloat16).reshape(
        device_local, HEAD_COUNT, LATENT_WIDTH
    )
    heads = jnp.einsum("thc,chv->thv", mixed_output, value_part, preferred_element_type=jnp.float32)
    heads = heads.reshape(device_local, HEAD_COUNT * VALUE_UNITS).astype(jnp.bfloat16)
    hidden = x_in + matrix_product(heads, wout)
    normed2, inv_ffn = norm_forward(hidden, g_ffn)
    normed_ffn = normed2.astype(jnp.bfloat16)
    logits = matrix_product(normed_ffn, wrout)
    router = jax.nn.softmax(logits, axis=-1)
    own_routes = routes[0]
    names = jnp.arange(experts, dtype=jnp.int32)
    chosen = (own_routes[:, :, None] == names[None, None, :]).astype(jnp.float32)
    gates = jnp.sum(chosen * router[:, None, :], axis=-1)
    hits = (own_routes.reshape(device_local * TOPK)[:, None] == names[None, :]).astype(jnp.int32)
    slot = jnp.sum((jnp.cumsum(hits, axis=0) - hits) * hits, axis=1)
    place = own_routes.reshape(device_local * TOPK) * capacity + slot
    token_of = jnp.arange(device_local * TOPK, dtype=jnp.int32) // TOPK
    table = jnp.full((experts * capacity,), device_local, jnp.int32).at[place].set(token_of)
    padded = jnp.concatenate([normed_ffn, jnp.zeros((1, MODEL_WIDTH), jnp.bfloat16)], axis=0)
    buffer = padded[table].reshape(experts, capacity, MODEL_WIDTH)
    w_g, w_u, w_d = (expert_gate[0], expert_up[0], expert_down[0])

    def spread(values):
        return jnp.broadcast_to(values[:, None], (experts, shards, capacity, MODEL_WIDTH)).reshape(
            experts * shards, capacity, MODEL_WIDTH
        )

    def collect(back):
        return jnp.sum(back.reshape(experts, shards, capacity, MODEL_WIDTH), axis=1).reshape(
            experts * capacity, MODEL_WIDTH
        )

    received = lax.all_to_all(
        spread(buffer), ("expert", "fsdp"), split_axis=0, concat_axis=0, tiled=True
    )
    ex_rows = received.reshape(-1, MODEL_WIDTH)
    pre_gate = matrix_product(ex_rows, w_g)
    pre_up = matrix_product(ex_rows, w_u)
    act_gate, slope = silu_parts(pre_gate)
    ex_act = (act_gate * pre_up).astype(jnp.bfloat16)
    ex_out = matrix_product(ex_act, w_d).reshape(received.shape)
    returned = lax.all_to_all(
        ex_out.astype(jnp.bfloat16), ("expert", "fsdp"), split_axis=0, concat_axis=0, tiled=True
    ).astype(ex_out.dtype)
    results = collect(returned)
    picked = results[place].reshape(device_local, TOPK, MODEL_WIDTH)
    routed = jnp.sum(gates[:, :, None] * picked, axis=1)
    sh_gate = matrix_product(normed_ffn, sgate)
    sh_up = matrix_product(normed_ffn, sup)
    sh_silu, sh_slope = silu_parts(sh_gate)
    sh_act = (sh_silu * sh_up).astype(jnp.bfloat16)
    shared = matrix_product(sh_act, sdown)
    output = hidden + routed + shared
    d_shared = grad_out.astype(jnp.bfloat16)
    shared_down_gradient = inner(sh_act, d_shared)
    d_sh_act = outer_product(d_shared, sdown)
    d_sh_gate = (d_sh_act * sh_up * sh_slope).astype(jnp.bfloat16)
    d_sh_up = (d_sh_act * sh_silu).astype(jnp.bfloat16)
    shared_gate_gradient = inner(normed_ffn, d_sh_gate)
    shared_up_gradient = inner(normed_ffn, d_sh_up)
    d_normed_ffn = outer_product(d_sh_gate, sgate) + outer_product(d_sh_up, sup)
    d_picked = (
        (gates[:, :, None] * grad_out[:, None, :])
        .astype(jnp.bfloat16)
        .reshape(device_local * TOPK, MODEL_WIDTH)
    )
    d_gates = jnp.sum(picked * grad_out[:, None, :], axis=2)
    d_buffer = (
        jnp.zeros((experts * capacity, MODEL_WIDTH), jnp.bfloat16)
        .at[place]
        .set(d_picked)
        .reshape(experts, capacity, MODEL_WIDTH)
    )
    d_received = lax.all_to_all(
        spread(d_buffer), ("expert", "fsdp"), split_axis=0, concat_axis=0, tiled=True
    )
    d_rows = d_received.reshape(-1, MODEL_WIDTH)
    d_act = outer_product(d_rows, w_d)
    g_down = inner(ex_act, d_rows)
    d_pre_gate = (d_act * pre_up * slope).astype(jnp.bfloat16)
    d_pre_up = (d_act * act_gate).astype(jnp.bfloat16)
    g_gate = inner(ex_rows, d_pre_gate)
    g_up = inner(ex_rows, d_pre_up)
    d_ex_rows = (outer_product(d_pre_gate, w_g) + outer_product(d_pre_up, w_u)).reshape(
        received.shape
    )
    d_returned = lax.all_to_all(
        d_ex_rows.astype(jnp.bfloat16), ("expert", "fsdp"), split_axis=0, concat_axis=0, tiled=True
    ).astype(d_ex_rows.dtype)
    d_results = collect(d_returned)
    d_normed_ffn = d_normed_ffn + jnp.sum(
        d_results[place].reshape(device_local, TOPK, MODEL_WIDTH), axis=1
    )
    d_router = jnp.sum(chosen * d_gates[:, :, None], axis=1)
    d_logits = (router * (d_router - jnp.sum(router * d_router, axis=1, keepdims=True))).astype(
        jnp.bfloat16
    )
    router_weight_gradient = inner(normed_ffn, d_logits)
    d_normed_ffn = d_normed_ffn + outer_product(d_logits, wrout)
    d_hidden_norm, g_ffn_grad = norm_backward(hidden, inv_ffn, g_ffn, d_normed_ffn)
    d_hidden = grad_out + d_hidden_norm
    d_attn = d_hidden.astype(jnp.bfloat16)
    output_weight_gradient = inner(heads, d_attn)
    d_heads = (
        outer_product(d_attn, wout)
        .astype(jnp.bfloat16)
        .reshape(device_local, HEAD_COUNT, VALUE_UNITS)
    )
    value_weight_gradient = jnp.einsum(
        "thc,thv->chv", mixed_output, d_heads, preferred_element_type=jnp.float32
    )
    mixed_gradient = jnp.einsum(
        "thv,chv->thc", d_heads, value_part, preferred_element_type=jnp.float32
    )
    mixed_gradient = mixed_gradient.astype(jnp.bfloat16).reshape(token_rows, LATENT_WIDTH)
    delta = jnp.sum(mixed_gradient.astype(jnp.float32) * mixed_output_sum, axis=1)

    def back_step(index, carry):
        d_query_acc, d_keys_acc = carry
        scores, key_rows = scores_of(index)
        weight_arrays = jnp.exp(scores - log_total[:, None])
        weight_gradients = outer_product(mixed_gradient, key_rows[:, :LATENT_WIDTH])
        d_scores = (weight_arrays * (weight_gradients - delta[:, None]) * scale).astype(
            jnp.bfloat16
        )
        d_query_acc = d_query_acc + matrix_product(d_scores, key_rows)
        d_values = inner(weight_arrays.astype(jnp.bfloat16), mixed_gradient)
        d_block = inner(d_scores, query) + jnp.concatenate(
            [d_values, jnp.zeros((block, ROTARY_UNITS), jnp.float32)], axis=1
        )
        previous = lax.dynamic_slice_in_dim(d_keys_acc, index * block, block, 0)
        return (
            d_query_acc,
            lax.dynamic_update_slice_in_dim(d_keys_acc, previous + d_block, index * block, 0),
        )

    d_query, d_keys = lax.fori_loop(
        0,
        token_tally,
        back_step,
        (
            jnp.zeros((token_rows, feature_width), jnp.float32),
            jnp.zeros((seq_len, feature_width), jnp.float32),
        ),
    )
    key_gradient = lax.psum_scatter(
        d_keys.astype(jnp.bfloat16), "expert", scatter_dimension=0, tiled=True
    )
    query_up_gradient = d_query.astype(jnp.bfloat16).reshape(
        device_local, HEAD_COUNT, feature_width
    )
    query_latent_gradient = query_up_gradient[:, :, :LATENT_WIDTH]
    key_weight_gradient = jnp.einsum(
        "thc,thd->chd", query_latent_gradient, query_nope, preferred_element_type=jnp.float32
    )
    d_q_nope = jnp.einsum(
        "thc,chd->thd", query_latent_gradient, key_part, preferred_element_type=jnp.float32
    )
    d_q_rope = reverse_rotary(
        query_up_gradient[:, :, LATENT_WIDTH:].astype(jnp.float32),
        cosine_table[:, None, :],
        sine_table[:, None, :],
    )
    d_query_full = (
        jnp.concatenate([d_q_nope, d_q_rope], axis=-1)
        .astype(jnp.bfloat16)
        .reshape(device_local, HEAD_COUNT * (PLAIN_UNITS + ROTARY_UNITS))
    )
    query_weight_gradient = inner(normed_in, d_query_full)
    d_normed_in = outer_product(d_query_full, wq)
    latent_gradient = key_gradient[:, :LATENT_WIDTH].astype(jnp.float32)
    rotary_key_gradient = reverse_rotary(
        key_gradient[:, LATENT_WIDTH:].astype(jnp.float32), cosine_table, sine_table
    )
    d_compact, g_lat_grad = norm_backward(packed_rows, inv_lat, g_lat, latent_gradient)
    d_latent_full = jnp.concatenate([d_compact, rotary_key_gradient], axis=-1).astype(jnp.bfloat16)
    latent_weight_gradient = inner(normed_in, d_latent_full)
    d_normed_in = d_normed_in + outer_product(d_latent_full, wlat)
    d_norm_in, g_attn_grad = norm_backward(x_in, inv_attn, attention_gain_grad, d_normed_in)
    d_tokens = (d_hidden + d_norm_in).astype(jnp.bfloat16)
    expand_weight_gradient = jnp.concatenate(
        [key_weight_gradient, value_weight_gradient], axis=-1
    ).reshape(LATENT_WIDTH, HEAD_COUNT * (PLAIN_UNITS + VALUE_UNITS))
    r_sgate, r_sup, r_sdown = (
        lax.psum_scatter(shared_gate_gradient, ("expert", "fsdp"), scatter_dimension=0, tiled=True),
        lax.psum_scatter(shared_up_gradient, ("expert", "fsdp"), scatter_dimension=0, tiled=True),
        lax.psum_scatter(shared_down_gradient, ("expert", "fsdp"), scatter_dimension=0, tiled=True),
    )
    r_attn, r_query, r_latent, r_lgain, r_expand, r_out, r_fgain, r_router = (
        lax.psum_scatter(
            g_attn_grad.astype(jnp.bfloat16), "fsdp", scatter_dimension=0, tiled=True
        ).astype(jnp.float32),
        lax.psum_scatter(
            query_weight_gradient.astype(jnp.bfloat16), "fsdp", scatter_dimension=0, tiled=True
        ).astype(jnp.float32),
        lax.psum_scatter(
            latent_weight_gradient.astype(jnp.bfloat16), "fsdp", scatter_dimension=0, tiled=True
        ).astype(jnp.float32),
        lax.psum_scatter(
            g_lat_grad.astype(jnp.bfloat16), "fsdp", scatter_dimension=0, tiled=True
        ).astype(jnp.float32),
        lax.psum_scatter(
            expand_weight_gradient.astype(jnp.bfloat16), "fsdp", scatter_dimension=0, tiled=True
        ).astype(jnp.float32),
        lax.psum_scatter(
            output_weight_gradient.astype(jnp.bfloat16), "fsdp", scatter_dimension=0, tiled=True
        ).astype(jnp.float32),
        lax.psum_scatter(
            g_ffn_grad.astype(jnp.bfloat16), "fsdp", scatter_dimension=0, tiled=True
        ).astype(jnp.float32),
        lax.psum_scatter(
            router_weight_gradient.astype(jnp.bfloat16), "fsdp", scatter_dimension=0, tiled=True
        ).astype(jnp.float32),
    )
    r_attn, r_query, r_latent, r_lgain, r_expand, r_out, r_fgain, r_router = (
        lax.psum(r_attn.astype(jnp.bfloat16), "expert").astype(jnp.float32),
        lax.psum(r_query.astype(jnp.bfloat16), "expert").astype(jnp.float32),
        lax.psum(r_latent.astype(jnp.bfloat16), "expert").astype(jnp.float32),
        lax.psum(r_lgain.astype(jnp.bfloat16), "expert").astype(jnp.float32),
        lax.psum(r_expand.astype(jnp.bfloat16), "expert").astype(jnp.float32),
        lax.psum(r_out.astype(jnp.bfloat16), "expert").astype(jnp.float32),
        lax.psum(r_fgain.astype(jnp.bfloat16), "expert").astype(jnp.float32),
        lax.psum(r_router.astype(jnp.bfloat16), "expert").astype(jnp.float32),
    )
    return (
        output.astype(jnp.bfloat16)[None],
        d_tokens[None],
        r_attn,
        r_query,
        r_latent,
        r_lgain,
        r_expand,
        r_out,
        r_fgain,
        r_router,
        r_sgate,
        r_sup,
        r_sdown,
        g_gate[None],
        g_up[None],
        g_down[None],
    )


LINE = 4
SQUARE = 2
CORES = 2
MESH = pl.DeviceIdType.MESH
VMEM_LIMIT = 56 * 1024 * 1024


class Place:
    def __init__(self):
        index = lax.axis_index("expert")
        self.y = lax.axis_index("fsdp")
        self.c = lax.rem(index, CORES)
        self.b = lax.rem(lax.div(index, CORES), SQUARE)
        self.a = lax.div(index, CORES * SQUARE)

    def device(self, da=0, db=0, dc=0, dy=0):
        b = 1 - self.b if db else self.b
        c = 1 - self.c if dc else self.c
        y = 1 - self.y if dy else self.y
        return (((self.a + da) * SQUARE + b) * CORES + c, y)

    def block(self, full, a, db=0, dc=0, dy=0):
        b = 1 - self.b if db else self.b
        c = 1 - self.c if dc else self.c
        y = 1 - self.y if dy else self.y
        flat = (a * SQUARE + b) * CORES + c
        return y * (LINE * SQUARE * CORES) + flat if full else flat

    def greet(self, with_y):
        barrier = pltpu.get_barrier_semaphore()
        near = [dict(db=1), dict(dc=1)] + ([dict(dy=1)] if with_y else [])
        for step in near:
            pl.semaphore_signal(barrier, inc=1, device_id=self.device(**step), device_id_type=MESH)

        @pl.when(self.a > 0)
        def _():
            pl.semaphore_signal(barrier, inc=1, device_id=self.device(da=-1), device_id_type=MESH)

        @pl.when(self.a < LINE - 1)
        def _():
            pl.semaphore_signal(barrier, inc=1, device_id=self.device(da=1), device_id_type=MESH)

        ends = jnp.logical_or(self.a == 0, self.a == LINE - 1).astype(jnp.int32)
        pl.semaphore_wait(barrier, len(near) + 2 - ends)


class Sender:
    def __init__(self, place, sems):
        self.place, self.sems, self.pending = place, sems, []

    def send(self, src, dst, recv_sem, step, cond=None):
        sem = self.sems.at[len(self.pending)]

        def make():
            return pltpu.make_async_remote_copy(
                src_ref=src,
                dst_ref=dst,
                send_sem=sem,
                recv_sem=recv_sem,
                device_id=self.place.device(**step),
                device_id_type=MESH,
            )

        def start():
            make().start()

        guarded(cond, start)
        self.pending.append((cond, lambda: make().wait_send()))

    def arrived(self, dst, recv_sem):
        pltpu.make_async_remote_copy(
            src_ref=dst,
            dst_ref=dst,
            send_sem=self.sems.at[0],
            recv_sem=recv_sem,
            device_id=self.place.device(dc=1),
            device_id_type=MESH,
        ).wait_recv()

    def finish(self):
        for cond, wait in self.pending:
            guarded(cond, wait)


def guarded(cond, action):
    if cond is None:
        action()
    else:
        pl.when(cond)(action)


def both(first, second):
    if first is None or second is None:
        return second if first is None else first
    return jnp.logical_and(first, second)


def gather_ticks(place, sender, full, gated, ins, outs, local_sems, recv_sems):
    a = place.a
    count = len(ins)

    def own_copy(at):
        return pltpu.make_async_copy(
            ins[at], outs[at].at[place.block(full, a)], local_sems.at[at]
        )

    def chunk(at, block, half):
        size = ins[at].shape[0] // 2
        return outs[at].at[block, pl.ds(half * size, size)]

    def sem_of(at, block, half):
        return recv_sems.at[at, block * 2 + half]

    def forward(at, block, half, src, step, cond=None):
        sender.send(src, chunk(at, block, half), sem_of(at, block, half), step, cond)

    def receive(at, block, half, cond):
        guarded(cond, lambda: sender.arrived(chunk(at, block, half), sem_of(at, block, half)))

    def held_by(at, delta, cond):
        if at not in gated:
            return cond
        return both(cond, lax.div(a + delta, LINE // 2) == place.y)

    def from_line(delta, always):
        for half in range(2):
            for at in range(count):
                block = place.block(full, a + delta)
                cond = held_by(at, delta, always)
                size = ins[at].shape[0] // 2
                if delta == 0:
                    src = ins[at].at[pl.ds(half * size, size)]
                else:
                    receive(at, block, half, cond)
                    src = chunk(at, block, half)
                if delta <= 0:
                    forward(at, block, half, src, dict(da=1), both(cond, a < LINE - 1))
                if delta >= 0:
                    forward(at, block, half, src, dict(da=-1), both(cond, a > 0))
                forward(at, block, half, src, dict(db=1), cond)
                if full:
                    forward(at, block, half, src, dict(dy=1), cond)
                forward(at, block, half, src, dict(dc=1), cond)

    def from_side(delta, always):
        for half in range(2):
            for at in range(count):
                cond = held_by(at, delta, always)
                block = place.block(full, a + delta, db=1)
                receive(at, block, half, cond)
                if full and half == 0:
                    forward(at, block, half, chunk(at, block, half), dict(dy=1), cond)
                forward(at, block, half, chunk(at, block, half), dict(dc=1), cond)
                if full:
                    block = place.block(full, a + delta, dy=1)
                    receive(at, block, half, cond)
                    if half == 1:
                        forward(at, block, half, chunk(at, block, half), dict(db=1), cond)
                    forward(at, block, half, chunk(at, block, half), dict(dc=1), cond)

    def from_corner(delta, always):
        for half in range(2):
            for at in range(count):
                cond = held_by(at, delta, always)
                block = place.block(True, a + delta, db=1, dy=1)
                receive(at, block, half, cond)
                forward(at, block, half, chunk(at, block, half), dict(dc=1), cond)

    def from_sibling(delta, always):
        for half in range(2):
            for at in range(count):
                cond = held_by(at, delta, always)
                for db in range(2):
                    for dy in range(2 if full else 1):
                        receive(at, place.block(full, a + delta, db=db, dc=1, dy=dy), half, cond)

    rounds = [[(0, None)]]
    for s in range(1, LINE):
        rounds.append([(-s, a >= s), (s, a + s < LINE)])
    stages = [from_line, from_side] + ([from_corner] if full else []) + [from_sibling]

    def tick(number):
        if number == 0:
            for at in range(count):
                own_copy(at).start()
        for level, stage in enumerate(stages):
            if 0 <= number - level < len(rounds):
                for delta, cond in rounds[number - level]:
                    stage(delta, cond)
        if number == len(rounds) + len(stages) - 2:
            for at in range(count):
                own_copy(at).wait()

    return [functools.partial(tick, number) for number in range(len(rounds) + len(stages) - 1)]


def send_pairs(sender, ins, outs, sems):
    for at, (src, dst) in enumerate(zip(ins, outs)):
        sender.send(src, dst, sems.at[at], dict(dy=1))


def take_pairs(sender, outs, sems):
    for at, dst in enumerate(outs):
        sender.arrived(dst, sems.at[at])


def gather_kernel(full, count, pairs, gated, *refs):
    ins, outs = refs[: count + pairs], refs[count + pairs : 2 * (count + pairs)]
    local_sems, send_sems, recv_sems, pair_sems = refs[2 * (count + pairs) :]
    place = Place()
    sender = Sender(place, send_sems)
    place.greet(full or pairs > 0)
    send_pairs(sender, ins[count:], outs[count:], pair_sems)
    for tick in gather_ticks(
        place, sender, full, gated, ins[:count], outs[:count], local_sems, recv_sems
    ):
        tick()
    take_pairs(sender, outs[count:], pair_sems)
    sender.finish()


def gather_rows(arrays, full, collective_id, swapped=(), gated=()):
    blocks = LINE * SQUARE * CORES * (SQUARE if full else 1)
    count, pairs = len(arrays), len(swapped)
    lines = 2 * LINE - 1
    sends = pairs + count * lines * 2 * (9 if full else 5)
    moved = sum(blocks * 2 * x.size * x.dtype.itemsize for x in arrays)
    return pl.pallas_call(
        functools.partial(gather_kernel, full, count, pairs, gated),
        out_shape=[jax.ShapeDtypeStruct((blocks,) + x.shape, x.dtype) for x in arrays]
        + [jax.ShapeDtypeStruct(x.shape, x.dtype) for x in swapped],
        in_specs=[pl.BlockSpec(memory_space=pl.ANY)] * (count + pairs),
        out_specs=[pl.BlockSpec(memory_space=pl.ANY)] * (count + pairs),
        scratch_shapes=[
            pltpu.SemaphoreType.DMA((count,)),
            pltpu.SemaphoreType.DMA((sends,)),
            pltpu.SemaphoreType.DMA((count, blocks * 2)),
            pltpu.SemaphoreType.DMA((max(pairs, 1),)),
        ],
        compiler_params=pltpu.CompilerParams(collective_id=collective_id, has_side_effects=True),
        cost_estimate=pl.CostEstimate(flops=0, bytes_accessed=6 * moved, transcendentals=0),
    )(*arrays, *swapped)


def add_rows(target, sources, size):
    def step(at, carry):
        rows = pl.ds(pl.multiple_of(at * 16, 16), 16)
        total = sources[0][rows, :].astype(jnp.float32)
        for source in sources[1:]:
            total = total + source[rows, :].astype(jnp.float32)
        target[rows, :] = total.astype(target.dtype)
        return carry

    lax.fori_loop(0, size // 16, step, 0)


def scatter_ticks(place, sender, full, part, out, scratch):
    mine, got, side, up, down, load_sems, recv_sems = scratch
    a = place.a
    kinds = 4 if full else 2
    size = part.shape[1]
    half = size // 2
    order = [LINE - 1, 0, LINE - 2, 1]
    walk = (3, 1, 2, 0) if full else (1, 0)

    def sem_of(group, target, kind):
        return recv_sems.at[group, target * 4 + kind]

    def load(target, kind):
        block = place.block(full, target, db=kind % 2, dy=kind // 2)
        return pltpu.make_async_copy(
            part.at[block], mine.at[target, kind], load_sems.at[target * 4 + kind]
        )

    def begin():
        for target in order:
            for kind in walk:
                load(target, kind).start()
                block = place.block(full, target, db=kind % 2, dc=1, dy=kind // 2)
                sender.send(
                    part.at[block], got.at[target, kind], sem_of(0, target, kind), dict(dc=1)
                )

    def rows_of(ref, which):
        return ref.at[pl.ds(which * half, half)]

    def over_cores(target):
        for kind in walk:
            load(target, kind).wait()
            sender.arrived(got.at[target, kind], sem_of(0, target, kind))
            add_rows(mine.at[target, kind], [mine.at[target, kind], got.at[target, kind]], size)
            held = mine.at[target, kind]
            if kind == 3:
                sender.send(rows_of(held, 0), side.at[target, 4], sem_of(1, target, 0), dict(db=1))
                sender.send(rows_of(held, 1), side.at[target, 5], sem_of(1, target, 1), dict(dy=1))
            if kind == 1:
                sender.send(rows_of(held, 0), side.at[target, 0], sem_of(2, target, 0), dict(db=1))
                if not full:
                    sender.send(
                        rows_of(held, 1), side.at[target, 1], sem_of(2, target, 1), dict(db=1)
                    )
            if kind == 2:
                sender.send(rows_of(held, 1), side.at[target, 3], sem_of(2, target, 3), dict(dy=1))

    def over_corner(target):
        sender.arrived(side.at[target, 4], sem_of(1, target, 0))
        held = rows_of(mine.at[target, 2], 0)
        add_rows(held, [held, side.at[target, 4]], half)
        sender.send(held, side.at[target, 2], sem_of(2, target, 2), dict(dy=1))
        sender.arrived(side.at[target, 5], sem_of(1, target, 1))
        held = rows_of(mine.at[target, 1], 1)
        add_rows(held, [held, side.at[target, 5]], half)
        sender.send(held, side.at[target, 1], sem_of(2, target, 1), dict(db=1))

    def over_line(target):
        for which in range(2):
            held = rows_of(mine.at[target, 0], which)
            parts = [held]
            for source in (0, 2) if full else (0,):
                sender.arrived(side.at[target, source + which], sem_of(2, target, source + which))
                parts.append(side.at[target, source + which])
            below, above = rows_of(up.at[target], which), rows_of(down.at[target], which)
            below_sem, above_sem = sem_of(3, target, which), sem_of(3, target, 2 + which)

            def upward(with_below):
                extra = []
                if with_below:
                    sender.arrived(below, below_sem)
                    extra = [below]
                add_rows(held, parts + extra, half)

            def downward(with_above):
                extra = []
                if with_above:
                    sender.arrived(above, above_sem)
                    extra = [above]
                add_rows(held, parts + extra, half)

            if target > 0:
                pl.when(jnp.logical_and(a < target, a > 0))(lambda: upward(True))
                pl.when(a == 0)(lambda: upward(False))
                sender.send(held, below, below_sem, dict(da=1), a < target)
            if target < LINE - 1:
                pl.when(jnp.logical_and(a > target, a < LINE - 1))(lambda: downward(True))
                pl.when(a == LINE - 1)(lambda: downward(False))
                sender.send(held, above, above_sem, dict(da=-1), a > target)

            def last():
                extra = []
                if target > 0:
                    sender.arrived(below, below_sem)
                    extra.append(below)
                if target < LINE - 1:
                    sender.arrived(above, above_sem)
                    extra.append(above)
                add_rows(rows_of(out, which), parts + extra, half)

            pl.when(a == target)(last)

    stages = [over_cores] + ([over_corner] if full else []) + [over_line]

    def tick(number):
        if number == 0:
            begin()
        for level, stage in enumerate(stages):
            if 0 <= number - level < len(order):
                stage(order[number - level])

    return [functools.partial(tick, number) for number in range(len(order) + len(stages) - 1)]


def scatter_kernel(full, pairs, part, *refs):
    ins, out, outs = refs[:pairs], refs[pairs], refs[pairs + 1 : 2 * pairs + 1]
    mine, got, side, up, down, load_sems, send_sems, recv_sems, pair_sems = refs[2 * pairs + 1 :]
    place = Place()
    sender = Sender(place, send_sems)
    place.greet(full or pairs > 0)
    send_pairs(sender, ins, outs, pair_sems)
    scratch = (mine, got, side, up, down, load_sems, recv_sems)
    for tick in scatter_ticks(place, sender, full, part, out, scratch):
        tick()
    take_pairs(sender, outs, pair_sems)
    sender.finish()


def scatter_scratch(full, rows, width, dtype, pairs):
    kinds = 4 if full else 2
    return [
        pltpu.VMEM((LINE, kinds, rows, width), dtype),
        pltpu.VMEM((LINE, kinds, rows, width), dtype),
        pltpu.VMEM((LINE, 6, rows // 2, width), dtype),
        pltpu.VMEM((LINE, rows, width), dtype),
        pltpu.VMEM((LINE, rows, width), dtype),
        pltpu.SemaphoreType.DMA((LINE * 4,)),
        pltpu.SemaphoreType.DMA((pairs + LINE * (4 + 6 + 4),)),
        pltpu.SemaphoreType.DMA((4, LINE * 4)),
        pltpu.SemaphoreType.DMA((max(pairs, 1),)),
    ]


def gather_scatter_kernel(count, gated, *refs):
    ins, part = refs[:count], refs[count]
    outs, total = refs[count + 1 : 2 * count + 1], refs[2 * count + 1]
    local_sems, gather_sends, gather_recvs = refs[2 * count + 2 : 2 * count + 5]
    mine, got, side, up, down, load_sems, scatter_sends, scatter_recvs, _ = refs[2 * count + 5 :]
    place = Place()
    gatherer = Sender(place, gather_sends)
    scatterer = Sender(place, scatter_sends)
    place.greet(True)
    scratch = (mine, got, side, up, down, load_sems, scatter_recvs)
    ticks = [
        scatter_ticks(place, scatterer, True, part, total, scratch),
        gather_ticks(place, gatherer, False, gated, ins, outs, local_sems, gather_recvs),
    ]
    for number in range(max(len(steps) for steps in ticks)):
        for steps in ticks:
            if number < len(steps):
                steps[number]()
    scatterer.finish()
    gatherer.finish()


def gather_and_scatter(arrays, part, collective_id, gated=()):
    blocks = LINE * SQUARE * CORES
    count = len(arrays)
    _, rows, width = part.shape
    sends = count * (2 * LINE - 1) * 2 * 5
    moved = sum(blocks * 2 * x.size * x.dtype.itemsize for x in arrays)
    return pl.pallas_call(
        functools.partial(gather_scatter_kernel, count, gated),
        out_shape=[jax.ShapeDtypeStruct((blocks,) + x.shape, x.dtype) for x in arrays]
        + [jax.ShapeDtypeStruct((rows, width), jnp.float32)],
        in_specs=[pl.BlockSpec(memory_space=pl.ANY)] * (count + 1),
        out_specs=[pl.BlockSpec(memory_space=pl.ANY)] * count
        + [pl.BlockSpec(memory_space=pltpu.VMEM)],
        scratch_shapes=[
            pltpu.SemaphoreType.DMA((count,)),
            pltpu.SemaphoreType.DMA((sends,)),
            pltpu.SemaphoreType.DMA((count, blocks * 2)),
        ]
        + scatter_scratch(True, rows, width, part.dtype, 0),
        compiler_params=pltpu.CompilerParams(
            collective_id=collective_id, has_side_effects=True, vmem_limit_bytes=VMEM_LIMIT
        ),
        cost_estimate=pl.CostEstimate(flops=0, bytes_accessed=6 * moved, transcendentals=0),
    )(*arrays, part)


def scatter_rows(part, full, collective_id, swapped=()):
    blocks, rows, width = part.shape
    pairs = len(swapped)
    return pl.pallas_call(
        functools.partial(scatter_kernel, full, pairs),
        out_shape=[jax.ShapeDtypeStruct((rows, width), jnp.float32)]
        + [jax.ShapeDtypeStruct(x.shape, x.dtype) for x in swapped],
        in_specs=[pl.BlockSpec(memory_space=pl.ANY)] * (1 + pairs),
        out_specs=[pl.BlockSpec(memory_space=pltpu.VMEM)]
        + [pl.BlockSpec(memory_space=pl.ANY)] * pairs,
        scratch_shapes=scatter_scratch(full, rows, width, part.dtype, pairs),
        compiler_params=pltpu.CompilerParams(
            collective_id=collective_id, has_side_effects=True, vmem_limit_bytes=VMEM_LIMIT
        ),
        cost_estimate=pl.CostEstimate(
            flops=0, bytes_accessed=12 * part.size * part.dtype.itemsize, transcendentals=0
        ),
    )(part, *swapped)


def contract_last(left, right):
    return lax.dot_general(
        left, right, (((1,), (1,)), ((), ())), preferred_element_type=jnp.float32
    )


def contract_first(left, right):
    return lax.dot_general(
        left, right, (((0,), (0,)), ((), ())), preferred_element_type=jnp.float32
    )


def expert_kernel(
    capacity,
    normed,
    grads,
    routes,
    router_rows,
    w_gate,
    w_up,
    w_down,
    shared_in,
    shared_out,
    out_part,
    d_part,
    ex_rows,
    ex_grads,
    act_out,
    d_gate_out,
    d_up_out,
    shared_in_grad,
    shared_out_grad,
    in_total,
    out_total,
):
    position = lax.axis_index("expert")
    experts = lax.axis_size("expert")
    group, rows, width = normed.shape
    tokens, slots = group * rows, group * capacity
    bf16 = jnp.bfloat16
    x = normed[...].reshape(tokens, width)
    g = grads[...].reshape(tokens, width)

    row = lax.broadcasted_iota(jnp.int32, (tokens, tokens), 0)
    column = lax.broadcasted_iota(jnp.int32, (tokens, tokens), 1)
    before = jnp.logical_and(column < row, lax.div(row, rows) == lax.div(column, rows))
    named = routes[...].reshape(tokens, -1) == position.astype(jnp.float32).astype(bf16)
    hit = jnp.sum(jnp.where(named, 1.0, 0.0), axis=1, keepdims=True)
    tally = matrix_product(
        jnp.where(before, 1.0, 0.0).astype(bf16),
        jnp.broadcast_to(hit, (tokens, 128)).astype(bf16),
    )
    place = jnp.where(hit > 0.5, tally[:, :1], -1.0)
    token = lax.broadcasted_iota(jnp.int32, (tokens, slots), 0)
    slot = lax.broadcasted_iota(jnp.int32, (tokens, slots), 1)
    same = lax.div(slot, capacity) == lax.div(token, rows)
    wanted = lax.rem(slot, capacity).astype(jnp.float32)
    chosen = jnp.where(jnp.logical_and(same, wanted == place), 1.0, 0.0)
    pick = chosen.T.astype(bf16)
    put = chosen.astype(bf16)

    r = matrix_product(pick, x).astype(bf16)
    gr = matrix_product(pick, g).astype(bf16)
    ex_rows[...] = r
    ex_grads[...] = gr
    lane = lax.broadcasted_iota(jnp.int32, (slots, router_rows.shape[0]), 1)
    logits = jnp.where(lane < experts, contract_last(r, router_rows[...]), -1e30)
    exps = jnp.exp(logits - jnp.max(logits, axis=1, keepdims=True))
    gate = jnp.sum(jnp.where(lane == position, exps, 0.0), axis=1, keepdims=True) / jnp.sum(
        exps, axis=1, keepdims=True
    )

    pre_gate = contract_last(r, w_gate[...])
    pre_up = contract_last(r, w_up[...])
    act_gate, slope = silu_parts(pre_gate)
    act = act_gate * pre_up
    back = contract_last(gr, w_down[...])
    d_gate_slot = jnp.sum(act * back, axis=1, keepdims=True)
    scaled = (gate * act).astype(bf16)
    d_act = gate * back
    d_pre_gate = (d_act * pre_up * slope).astype(bf16)
    d_pre_up = (d_act * act_gate).astype(bf16)
    act_out[...] = scaled
    d_gate_out[...] = d_pre_gate
    d_up_out[...] = d_pre_up
    ex_out = matrix_product(scaled, w_down[...]).astype(bf16)
    d_ex = matrix_product(d_pre_gate, w_gate[...]) + matrix_product(d_pre_up, w_up[...])
    d_ex = d_ex.astype(bf16)

    units = shared_out.shape[0]
    mix = matrix_product(x, shared_in[...])
    sh_gate, sh_up = mix[:, :units], mix[:, units:]
    sh_silu, sh_slope = silu_parts(sh_gate)
    sh_act = (sh_silu * sh_up).astype(bf16)
    d_sh_act = contract_last(g, shared_out[...])
    d_mix = jnp.concatenate([d_sh_act * sh_up * sh_slope, d_sh_act * sh_silu], axis=1)
    d_mix = d_mix.astype(bf16)

    out = matrix_product(put, ex_out) + matrix_product(sh_act, shared_out[...])
    out_part[...] = out.astype(bf16).reshape(group, rows, width)
    d_in = matrix_product(put, d_ex) + contract_last(d_mix, shared_in[...])
    d_part[:, :, :width] = d_in.astype(bf16).reshape(group, rows, width)
    lane = lax.broadcasted_iota(jnp.int32, (slots, d_part.shape[2] - width), 1)
    d_gates = jnp.where(lane == position, d_gate_slot, 0.0).astype(bf16)
    d_part[:, :, width:] = matrix_product(put, d_gates).astype(bf16).reshape(group, rows, -1)

    step = pl.program_id(0)

    @pl.when(step == 0)
    def _():
        in_total[...] = jnp.zeros_like(in_total)
        out_total[...] = jnp.zeros_like(out_total)

    in_total[...] += contract_first(d_mix, x)
    out_total[...] += contract_first(sh_act, g)

    @pl.when(step == pl.num_programs(0) - 1)
    def _():
        shared_in_grad[...] = in_total[...].T.astype(bf16)
        shared_out_grad[...] = out_total[...]


def expert_phase(
    all_normed, all_grads, router_rows, w_gate, w_up, w_down, shared_in, shared_out, capacity
):
    blocks, rows, width = all_normed.shape
    group = 4
    slots = group * capacity
    hidden = w_gate.shape[0]
    units = shared_out.shape[0]
    side = all_grads.shape[2] - width
    bf16 = jnp.bfloat16

    def by_group(shape):
        zeros = (0,) * (len(shape) - 1)
        return pl.BlockSpec(shape, lambda i: (i,) + zeros)

    def fixed(shape):
        return pl.BlockSpec(
            shape, lambda i: (0,) * len(shape), pipeline_mode=pl.Buffered(buffer_count=1)
        )

    return pl.pallas_call(
        functools.partial(expert_kernel, capacity),
        grid=(blocks // group,),
        out_shape=[
            jax.ShapeDtypeStruct((blocks, rows, width), bf16),
            jax.ShapeDtypeStruct((blocks, rows, width + side), bf16),
            jax.ShapeDtypeStruct((blocks * capacity, width), bf16),
            jax.ShapeDtypeStruct((blocks * capacity, width), bf16),
            jax.ShapeDtypeStruct((blocks * capacity, hidden), bf16),
            jax.ShapeDtypeStruct((blocks * capacity, hidden), bf16),
            jax.ShapeDtypeStruct((blocks * capacity, hidden), bf16),
            jax.ShapeDtypeStruct((width, 2 * units), bf16),
            jax.ShapeDtypeStruct((units, width), jnp.float32),
        ],
        in_specs=[
            by_group((group, rows, width)),
            by_group((group, rows, width)),
            pl.BlockSpec((group, rows, side), lambda i: (i, 0, width // side)),
            fixed(router_rows.shape),
            fixed(w_gate.shape),
            fixed(w_up.shape),
            fixed(w_down.shape),
            fixed(shared_in.shape),
            fixed(shared_out.shape),
        ],
        out_specs=[
            by_group((group, rows, width)),
            by_group((group, rows, width + side)),
            by_group((slots, width)),
            by_group((slots, width)),
            by_group((slots, hidden)),
            by_group((slots, hidden)),
            by_group((slots, hidden)),
            fixed((width, 2 * units)),
            fixed((units, width)),
        ],
        scratch_shapes=[
            pltpu.VMEM((2 * units, width), jnp.float32),
            pltpu.VMEM((units, width), jnp.float32),
        ],
        compiler_params=pltpu.CompilerParams(vmem_limit_bytes=VMEM_LIMIT),
        cost_estimate=pl.CostEstimate(
            flops=2 * blocks * capacity * width * hidden * 6,
            bytes_accessed=10 * blocks * rows * width * 2,
            transcendentals=blocks * capacity * hidden,
        ),
    )(all_normed, all_grads, all_grads, router_rows, w_gate, w_up, w_down, shared_in, shared_out)


def exchange_kernel(x, out, local_sem, send_sems, recv_sems):
    me, y = lax.axis_index("expert"), lax.axis_index("fsdp")
    count = x.shape[0]
    barrier = pltpu.get_barrier_semaphore()
    peers = [lax.rem(me + step, count) for step in range(1, count)]
    for peer in peers:
        pl.semaphore_signal(barrier, inc=1, device_id=(peer, y), device_id_type=MESH)
    own = pltpu.make_async_copy(x.at[me], out.at[me], local_sem)
    own.start()
    pl.semaphore_wait(barrier, count - 1)
    copies = []
    for at, peer in enumerate(peers):
        copy = pltpu.make_async_remote_copy(
            src_ref=x.at[peer],
            dst_ref=out.at[me],
            send_sem=send_sems.at[at],
            recv_sem=recv_sems.at[at],
            device_id=(peer, y),
            device_id_type=MESH,
        )
        copy.start()
        copies.append(copy)
    for copy in copies:
        copy.wait()
    own.wait()


def exchange(x, collective_id):
    count = x.shape[0]
    return pl.pallas_call(
        exchange_kernel,
        out_shape=jax.ShapeDtypeStruct(x.shape, x.dtype),
        in_specs=[pl.BlockSpec(memory_space=pl.ANY)],
        out_specs=pl.BlockSpec(memory_space=pl.ANY),
        scratch_shapes=[
            pltpu.SemaphoreType.DMA,
            pltpu.SemaphoreType.DMA((count - 1,)),
            pltpu.SemaphoreType.DMA((count - 1,)),
        ],
        compiler_params=pltpu.CompilerParams(collective_id=collective_id, has_side_effects=True),
        cost_estimate=pl.CostEstimate(
            flops=0, bytes_accessed=20 * x.size * x.dtype.itemsize, transcendentals=0
        ),
    )(x)


def swap_halves(value):
    half = value.shape[1] // 2
    return jnp.concatenate([value[:, half:], value[:, :half]], axis=1)


def greet_plane(place):
    me = lax.axis_index("expert")
    count = LINE * SQUARE * CORES
    barrier = pltpu.get_barrier_semaphore()
    for step in range(1, count):
        peer = (lax.rem(me + step, count), place.y)
        pl.semaphore_signal(barrier, inc=1, device_id=peer, device_id_type=MESH)
    pl.semaphore_signal(barrier, inc=1, device_id=place.device(dy=1), device_id_type=MESH)
    pl.semaphore_wait(barrier, count)


def sums_kernel(pairs, moved, small, large, *refs):
    ins = refs[:pairs]
    moved_out, small_out, large_out = refs[pairs : pairs + 3]
    outs = refs[pairs + 3 : 2 * pairs + 3]
    rest = refs[2 * pairs + 3 :]
    local_sem, exchange_sends, exchange_recvs = rest[:3]
    first, second = rest[3:12], rest[12:21]
    place = Place()
    me = lax.axis_index("expert")
    count = moved.shape[0]
    greet_plane(place)
    own = pltpu.make_async_copy(moved.at[me], moved_out.at[me], local_sem)
    own.start()
    copies = []
    for at in range(count - 1):
        copy = pltpu.make_async_remote_copy(
            src_ref=moved.at[lax.rem(me + at + 1, count)],
            dst_ref=moved_out.at[me],
            send_sem=exchange_sends.at[at],
            recv_sem=exchange_recvs.at[at],
            device_id=(lax.rem(me + at + 1, count), place.y),
            device_id_type=MESH,
        )
        copy.start()
        copies.append(copy)
    senders = [Sender(place, first[6]), Sender(place, second[6])]
    send_pairs(senders[0], ins, outs, first[8])
    ticks = [
        scatter_ticks(place, senders[0], False, small, small_out, first[:6] + (first[7],)),
        scatter_ticks(place, senders[1], True, large, large_out, second[:6] + (second[7],)),
    ]
    for number in range(max(len(steps) for steps in ticks)):
        for steps in ticks:
            if number < len(steps):
                steps[number]()
    take_pairs(senders[0], outs, first[8])
    for sender in senders:
        sender.finish()
    for copy in copies:
        copy.wait()
    own.wait()


def exchange_and_sums(moved, small, large, swapped, collective_id):
    count, pairs = moved.shape[0], len(swapped)
    hbm = pl.BlockSpec(memory_space=pl.ANY)
    vmem = pl.BlockSpec(memory_space=pltpu.VMEM)
    return pl.pallas_call(
        functools.partial(sums_kernel, pairs),
        out_shape=[
            jax.ShapeDtypeStruct(moved.shape, moved.dtype),
            jax.ShapeDtypeStruct(small.shape[1:], jnp.float32),
            jax.ShapeDtypeStruct(large.shape[1:], jnp.float32),
        ]
        + [jax.ShapeDtypeStruct(x.shape, x.dtype) for x in swapped],
        in_specs=[hbm] * (3 + pairs),
        out_specs=[hbm, vmem, vmem] + [hbm] * pairs,
        scratch_shapes=[
            pltpu.SemaphoreType.DMA,
            pltpu.SemaphoreType.DMA((count - 1,)),
            pltpu.SemaphoreType.DMA((count - 1,)),
        ]
        + scatter_scratch(False, *small.shape[1:], small.dtype, pairs)
        + scatter_scratch(True, *large.shape[1:], large.dtype, 0),
        compiler_params=pltpu.CompilerParams(
            collective_id=collective_id, has_side_effects=True, vmem_limit_bytes=VMEM_LIMIT
        ),
        cost_estimate=pl.CostEstimate(
            flops=0, bytes_accessed=12 * large.size * 2, transcendentals=0
        ),
    )(moved, small, large, *swapped)


def attend_kernel(
    rows,
    g_attn,
    w_front,
    g_lat,
    expand_head,
    cosines,
    sines,
    normed_out,
    latent_out,
    query_out,
    key_out,
    value_out,
    head_out,
    sum_out,
    log_out,
    keys,
    values,
):
    bf16 = jnp.bfloat16
    size = rows.shape[0]
    scale = (PLAIN_UNITS + ROTARY_UNITS) ** (-0.5)
    step = pl.program_id(0)
    normed, _ = norm_forward(rows[...].astype(jnp.float32), g_attn[...])
    normed = normed.astype(bf16)
    normed_out[...] = normed
    front = contract_last(normed, w_front[...])
    latent, _ = norm_forward(front[:, :LATENT_WIDTH], g_lat[...])
    latent = latent.astype(bf16)
    latent_out[...] = latent
    width = LATENT_WIDTH + ROTARY_UNITS

    def rotated(value):
        return value * cosines[...] + swap_halves(value) * sines[...]

    pairs = matrix_product(latent, expand_head[...])
    key = jnp.concatenate([pairs[:, :PLAIN_UNITS], rotated(front[:, LATENT_WIDTH:width])], axis=1)
    query = jnp.concatenate(
        [front[:, width : width + PLAIN_UNITS], rotated(front[:, width + PLAIN_UNITS :])], axis=1
    ).astype(bf16)
    key = key.astype(bf16)
    value = pairs[:, PLAIN_UNITS:].astype(bf16)
    query_out[...] = query
    key_out[...] = key
    value_out[...] = value
    here = pl.ds(pl.multiple_of(step * size, size), size)
    keys[here, :] = key
    values[here, :] = value
    row = lax.broadcasted_iota(jnp.int32, (size, size), 0)
    column = lax.broadcasted_iota(jnp.int32, (size, size), 1)
    near = jnp.where(column <= row, contract_last(query, key) * scale, -1e30)

    def over(past):
        top = jnp.max(near, axis=1, keepdims=True)
        if past:
            far = contract_last(query, keys[:past, :]) * scale
            top = jnp.maximum(top, jnp.max(far, axis=1, keepdims=True))
        exps = jnp.exp(near - top)
        total = jnp.sum(exps, axis=1, keepdims=True)
        mixed = matrix_product(exps.astype(bf16), value)
        if past:
            exps = jnp.exp(far - top)
            total = total + jnp.sum(exps, axis=1, keepdims=True)
            mixed = mixed + matrix_product(exps.astype(bf16), values[:past, :])
        mixed = mixed / total
        sum_out[...] = mixed
        head_out[...] = mixed.astype(bf16)
        wide = jnp.broadcast_to(top + jnp.log(total), (size, 128))
        log_out[0] = wide.T[:1, :]

    for at in range(keys.shape[0] // size):
        pl.when(step == at)(functools.partial(over, at * size))


def attend(rows, g_attn, w_front, g_lat, expand_head, cosines, sines):
    seq_len, width = rows.shape
    size = 256
    steps = seq_len // size
    units = PLAIN_UNITS + ROTARY_UNITS
    bf16 = jnp.bfloat16

    def by_step(columns):
        return pl.BlockSpec((size, columns), lambda i: (i, 0))

    def fixed(x):
        return pl.BlockSpec(
            x.shape, lambda i: (0, 0), pipeline_mode=pl.Buffered(buffer_count=1)
        )

    return pl.pallas_call(
        attend_kernel,
        grid=(steps,),
        out_shape=[
            jax.ShapeDtypeStruct((seq_len, width), bf16),
            jax.ShapeDtypeStruct((seq_len, LATENT_WIDTH), bf16),
            jax.ShapeDtypeStruct((seq_len, units), bf16),
            jax.ShapeDtypeStruct((seq_len, units), bf16),
            jax.ShapeDtypeStruct((seq_len, VALUE_UNITS), bf16),
            jax.ShapeDtypeStruct((seq_len, VALUE_UNITS), bf16),
            jax.ShapeDtypeStruct((seq_len, VALUE_UNITS), jnp.float32),
            jax.ShapeDtypeStruct((steps, 1, size), jnp.float32),
        ],
        in_specs=[by_step(width)]
        + [fixed(x) for x in (g_attn, w_front, g_lat, expand_head)]
        + [by_step(ROTARY_UNITS)] * 2,
        out_specs=[
            by_step(width),
            by_step(LATENT_WIDTH),
            by_step(units),
            by_step(units),
            by_step(VALUE_UNITS),
            by_step(VALUE_UNITS),
            by_step(VALUE_UNITS),
            pl.BlockSpec((1, 1, size), lambda i: (i, 0, 0)),
        ],
        scratch_shapes=[
            pltpu.VMEM((seq_len, units), bf16),
            pltpu.VMEM((seq_len, VALUE_UNITS), bf16),
        ],
        compiler_params=pltpu.CompilerParams(vmem_limit_bytes=VMEM_LIMIT),
        cost_estimate=pl.CostEstimate(
            flops=2 * seq_len * (width * 768 + seq_len * units),
            bytes_accessed=3 * rows.size * 2,
            transcendentals=seq_len * seq_len // 2,
        ),
    )(rows, g_attn, w_front, g_lat, expand_head, cosines, sines)


def attend_back_kernel(
    query,
    key,
    value,
    d_head,
    head_sum,
    logs,
    expand_head,
    cosines,
    sines,
    d_query_out,
    d_pairs_out,
    d_keys_out,
    d_key,
    d_value,
    key_turned,
):
    bf16 = jnp.bfloat16
    size = query.shape[0]
    seq_len = key.shape[0]
    scale = (PLAIN_UNITS + ROTARY_UNITS) ** (-0.5)
    step = pl.program_id(0)

    @pl.when(step == 0)
    def _():
        d_key[...] = jnp.zeros_like(d_key)
        d_value[...] = jnp.zeros_like(d_value)
        for at in range(0, seq_len, size):
            part = key[at : at + size, :].astype(jnp.float32)
            key_turned[:, at : at + size] = part.T.astype(bf16)

    q, d_out = query[...], d_head[...]
    product = d_out.astype(jnp.float32) * head_sum[...]
    delta = jnp.sum(product.T, axis=0, keepdims=True)
    log_row = logs[0]
    row = lax.broadcasted_iota(jnp.int32, (size, size), 0)
    column = lax.broadcasted_iota(jnp.int32, (size, size), 1)

    def grads_of(at, mask):
        there = slice(at, at + size)
        scores = contract_last(key[there, :], q) * scale
        if mask:
            scores = jnp.where(row <= column, scores, -1e30)
        probs = jnp.exp(scores - log_row)
        d_probs = contract_last(value[there, :], d_out)
        d_scores = (probs * (d_probs - delta) * scale).astype(bf16)
        d_key[there, :] += matrix_product(d_scores, q)
        d_value[there, :] += matrix_product(probs.astype(bf16), d_out)
        return matrix_product(key_turned[:, there], d_scores)

    def over(past):
        total = grads_of(past, True)
        for at in range(0, past, size):
            total = total + grads_of(at, False)
        d_query = total.T
        d_rope = d_query[:, PLAIN_UNITS:]
        d_rope = d_rope * cosines[...] - swap_halves(d_rope) * sines[...]
        d_query_out[...] = jnp.concatenate([d_query[:, :PLAIN_UNITS], d_rope], axis=1).astype(bf16)

    for at in range(seq_len // size):
        pl.when(step == at)(functools.partial(over, at * size))

    @pl.when(step == seq_len // size - 1)
    def _():
        for at in range(0, seq_len, size):
            there = slice(at, at + size)
            d_pairs = jnp.concatenate(
                [d_key[there, :PLAIN_UNITS], d_value[there, :]], axis=1
            ).astype(bf16)
            d_pairs_out[there, :] = d_pairs
            d_keys_out[there, :LATENT_WIDTH] = contract_last(d_pairs, expand_head[...]).astype(bf16)
            tail = jnp.concatenate(
                [d_key[there, PLAIN_UNITS:], jnp.zeros((size, ROTARY_UNITS), jnp.float32)], axis=1
            )
            d_keys_out[there, LATENT_WIDTH:] = tail.astype(bf16)


def attend_back(query, key, value, d_head, head_sum, logs, expand_head, cosines, sines):
    seq_len, units = query.shape
    steps, _, size = logs.shape
    bf16 = jnp.bfloat16
    keys_width = LATENT_WIDTH + 2 * ROTARY_UNITS

    def by_step(columns):
        return pl.BlockSpec((size, columns), lambda i: (i, 0))

    def fixed(shape):
        return pl.BlockSpec(shape, lambda i: (0, 0), pipeline_mode=pl.Buffered(buffer_count=1))

    return pl.pallas_call(
        attend_back_kernel,
        grid=(steps,),
        out_shape=[
            jax.ShapeDtypeStruct((seq_len, units), bf16),
            jax.ShapeDtypeStruct((seq_len, PLAIN_UNITS + VALUE_UNITS), bf16),
            jax.ShapeDtypeStruct((seq_len, keys_width), bf16),
        ],
        in_specs=[
            by_step(units),
            fixed(key.shape),
            fixed(value.shape),
            by_step(VALUE_UNITS),
            by_step(VALUE_UNITS),
            pl.BlockSpec((1, 1, size), lambda i: (i, 0, 0)),
            fixed(expand_head.shape),
            by_step(ROTARY_UNITS),
            by_step(ROTARY_UNITS),
        ],
        out_specs=[
            by_step(units),
            fixed((seq_len, PLAIN_UNITS + VALUE_UNITS)),
            fixed((seq_len, keys_width)),
        ],
        scratch_shapes=[
            pltpu.VMEM((seq_len, units), jnp.float32),
            pltpu.VMEM((seq_len, VALUE_UNITS), jnp.float32),
            pltpu.VMEM((units, seq_len), bf16),
        ],
        compiler_params=pltpu.CompilerParams(vmem_limit_bytes=VMEM_LIMIT),
        cost_estimate=pl.CostEstimate(
            flops=5 * seq_len * seq_len * units,
            bytes_accessed=8 * seq_len * units * 2,
            transcendentals=seq_len * seq_len // 2,
        ),
    )(query, key, value, d_head, head_sum, logs, expand_head, cosines, sines)


def finish_kernel(shard, query, expand, out_rows, query_out, expand_out, out_out):
    heads, units, width = query.shape
    query_out[...] = query[...].reshape(heads * units, width).astype(jnp.float32).T
    for at in range(heads):
        columns = expand.shape[2]
        expand_out[:, at * columns : (at + 1) * columns] = expand[at].astype(jnp.float32)
    out_out[...] = out_rows[0].astype(jnp.float32)


def finish(shard, query, expand, out_rows):
    heads, units, width = query.shape
    _, latents, columns = expand.shape
    _, rows, model = out_rows.shape
    steps = heads // 2
    return pl.pallas_call(
        finish_kernel,
        out_shape=[
            jax.ShapeDtypeStruct((width, heads * units), jnp.float32),
            jax.ShapeDtypeStruct((latents, heads * columns), jnp.float32),
            jax.ShapeDtypeStruct((steps * rows, model), jnp.float32),
        ],
        grid_spec=pltpu.PrefetchScalarGridSpec(
            num_scalar_prefetch=1,
            grid=(steps,),
            in_specs=[
                pl.BlockSpec((2, units, width), lambda i, shard: (i, 0, 0)),
                pl.BlockSpec((2, latents, columns), lambda i, shard: (i, 0, 0)),
                pl.BlockSpec((1, rows, model), lambda i, shard: (shard[0] * steps + i, 0, 0)),
            ],
            out_specs=[
                pl.BlockSpec((width, 2 * units), lambda i, shard: (0, i)),
                pl.BlockSpec((latents, 2 * columns), lambda i, shard: (0, i)),
                pl.BlockSpec((rows, model), lambda i, shard: (i, 0)),
            ],
        ),
        compiler_params=pltpu.CompilerParams(vmem_limit_bytes=VMEM_LIMIT),
        cost_estimate=pl.CostEstimate(
            flops=0, bytes_accessed=6 * heads * units * width, transcendentals=0
        ),
    )(shard.reshape(1), query, expand, out_rows)


def token_gather(rows):
    return lax.all_gather(rows, ("fsdp", "expert"), axis=0, tiled=True)


def split_body(
    tokens,
    routes,
    cotangent,
    attn_gain,
    w_query,
    latent_weight,
    latent_norm_gain,
    expand_weight,
    w_out,
    ffn_gain,
    w_router,
    shared_gate,
    shared_up,
    shared_down,
    expert_gate,
    expert_up,
    expert_down,
):
    rows = tokens.shape[1]
    experts = lax.axis_size("expert")
    shards = lax.axis_size("fsdp")
    position = lax.axis_index("expert")
    blocks = experts * shards
    seq_len = rows * experts
    capacity = shards * ((rows * TOPK * 4 + experts * 3 * shards - 1) // (experts * 3 * shards))
    head_units = PLAIN_UNITS + ROTARY_UNITS
    pair_units = PLAIN_UNITS + VALUE_UNITS
    feature_width = LATENT_WIDTH + ROTARY_UNITS
    scale = head_units ** (-0.5)

    shard = lax.axis_index("fsdp")
    first = shard == 0

    query_cols = lax.dynamic_slice_in_dim(w_query, position * head_units, head_units, 1)
    expand_cols = lax.dynamic_slice_in_dim(expand_weight, position * pair_units, pair_units, 1)
    owners = experts // shards
    lat_row = jnp.pad(latent_norm_gain, (0, w_query.shape[0] - latent_norm_gain.shape[0]))
    packed = jnp.concatenate(
        [latent_weight.T, query_cols.T, w_router.T, attn_gain[None], ffn_gain[None], lat_row[None]],
        axis=0,
    )
    packed = jnp.pad(packed, ((0, -packed.shape[0] % 32), (0, 0)))
    seq_rows, other_packed, other_expand = gather_rows(
        [tokens[0]], False, 0, swapped=[packed, expand_cols]
    )

    def whole(own, other, axis):
        return jnp.concatenate(
            [jnp.where(first, own, other), jnp.where(first, other, own)], axis=axis
        )

    lat_half = latent_norm_gain.shape[0]
    at = feature_width + head_units
    packed_rows = whole(packed, other_packed, 1)
    expand_head = whole(expand_cols, other_expand, 0)
    w_front = packed_rows[:at]
    w_latent = packed_rows[:feature_width]
    router_rows = packed_rows[at:]
    wrout = packed_rows[at : at + experts]
    g_attn = packed_rows[at + experts].astype(jnp.float32)
    g_ffn = packed_rows[at + experts + 1].astype(jnp.float32)
    lat_row = packed_rows[at + experts + 2]
    g_lat = jnp.concatenate(
        [lat_row[:lat_half], lat_row[w_query.shape[0] : w_query.shape[0] + lat_half]]
    ).astype(jnp.float32)
    units = shared_down.shape[0]

    def to_columns(weight):
        parts = weight.reshape(weight.shape[0], blocks, units).transpose(1, 0, 2)
        return lax.all_to_all(
            parts, ("expert", "fsdp"), split_axis=0, concat_axis=0, tiled=True
        ).reshape(-1, units)

    sh_cols = to_columns(jnp.concatenate([shared_gate, shared_up], axis=0)).reshape(
        blocks, 2, shared_gate.shape[0], units
    )
    lanes = -(-units // 128) * 128
    sh_cols = jnp.pad(sh_cols, ((0, 0), (0, 0), (0, 0), (0, lanes - units)))
    shared_in = sh_cols.transpose(0, 2, 1, 3).reshape(MODEL_WIDTH, 2 * lanes)
    shared_out = jnp.pad(shared_down, ((0, lanes - units), (0, 0)))
    core = lax.rem(position, CORES)

    def by_cores(weight):
        size = weight.shape[0] // CORES
        own = lax.dynamic_slice_in_dim(weight, core * size, size, 0)
        own = lax.all_gather(own, "fsdp", axis=0, tiled=True)
        swap = [(index, index ^ 1) for index in range(experts)]
        return own, lax.ppermute(own, "expert", swap)

    def core_columns(value, which):
        size = value.shape[1] // (CORES * shards)
        parts = [
            lax.dynamic_slice_in_dim(value, (at * CORES + which) * size, size, 1)
            for at in range(shards)
        ]
        return jnp.concatenate(parts, axis=1)

    def in_order(own, other):
        lower, upper = jnp.where(core == 0, own, other), jnp.where(core == 0, other, own)
        size = own.shape[1] // shards
        parts = []
        for at in range(shards):
            parts += [lower[:, at * size : (at + 1) * size], upper[:, at * size : (at + 1) * size]]
        return jnp.concatenate(parts, axis=1)

    out_own, out_other = by_cores(w_out)
    grad_rows = cotangent[0]
    grad_out = grad_rows.astype(jnp.float32)
    own_routes = jnp.pad(routes[0], ((0, 0), (0, 128 - TOPK)), constant_values=-1)
    grad_rows = jnp.concatenate([grad_rows, own_routes.astype(jnp.bfloat16)], axis=1)
    seq_rows, grad_rows, shared_in, shared_out = lax.optimization_barrier(
        (seq_rows, grad_rows, shared_in, shared_out)
    )
    all_grads = token_gather(grad_rows)

    x_in = tokens[0].astype(jnp.float32)
    normed, inv_attn = norm_forward(x_in, g_attn)
    normed_in = normed.astype(jnp.bfloat16)
    cosine_table, sine_table = rope_tables(jnp.arange(seq_len, dtype=jnp.int32))
    cosines = jnp.concatenate([cosine_table, cosine_table], axis=1)
    sines = jnp.concatenate([-sine_table, sine_table], axis=1)
    (
        seq_normed,
        latent_rows,
        query,
        key,
        value,
        head_rows,
        head_sum,
        logs,
    ) = attend(
        seq_rows.reshape(seq_len, MODEL_WIDTH),
        g_attn[None],
        w_front,
        g_lat[None],
        expand_head,
        cosines,
        sines,
    )
    heads = exchange(head_rows.reshape(experts, rows, VALUE_UNITS), 1)
    heads = heads.transpose(1, 0, 2).reshape(rows, experts * VALUE_UNITS)
    hidden = x_in + matrix_product(core_columns(heads, core), out_own)
    hidden = hidden + matrix_product(core_columns(heads, 1 - core), out_other)
    normed2, inv_ffn = norm_forward(hidden, g_ffn)
    normed_ffn = normed2.astype(jnp.bfloat16)
    router = jax.nn.softmax(outer_product(normed_ffn, wrout), axis=-1)

    (all_normed,) = gather_rows([normed_ffn], True, 2)
    w_query, all_normed = lax.optimization_barrier((w_query, all_normed))
    query_own, query_other = by_cores(w_query)
    (
        out_part,
        d_part,
        ex_rows,
        ex_grads,
        scaled_act,
        d_pre_gate,
        d_pre_up,
        g_shared_in,
        g_shared_out,
    ) = expert_phase(
        all_normed,
        all_grads.reshape(blocks, rows, -1),
        router_rows,
        expert_gate[0].T,
        expert_up[0].T,
        expert_down[0],
        shared_in,
        shared_out,
        capacity,
    )
    g_down = inner(scaled_act, ex_grads)
    g_gate = inner(d_pre_gate, ex_rows).T
    g_up = inner(d_pre_up, ex_rows).T
    (d_back,) = scatter_rows(d_part, True, 3)
    d_normed_ffn = d_back[:, :MODEL_WIDTH]
    d_router = d_back[:, MODEL_WIDTH : MODEL_WIDTH + experts]

    d_logits = (router * (d_router - jnp.sum(router * d_router, axis=1, keepdims=True))).astype(
        jnp.bfloat16
    )
    g_router = inner(d_logits, normed_ffn)
    d_normed_ffn = d_normed_ffn + matrix_product(d_logits, wrout)
    d_hidden_norm, g_ffn_grad = norm_backward(hidden, inv_ffn, g_ffn, d_normed_ffn)
    d_hidden = grad_out + d_hidden_norm
    d_attn = d_hidden.astype(jnp.bfloat16)

    d_heads = in_order(outer_product(d_attn, out_own), outer_product(d_attn, out_other))
    d_heads = d_heads.astype(jnp.bfloat16)
    d_heads = d_heads.reshape(rows, experts, VALUE_UNITS).transpose(1, 0, 2)
    d_head = exchange(d_heads, 4).reshape(seq_len, VALUE_UNITS)
    seq_d_attn = lax.all_gather(d_attn, "expert", axis=0, tiled=True)
    d_query_full, d_pairs, d_keys = attend_back(
        query, key, value, d_head, head_sum, logs, expand_head, cosines, sines
    )
    g_out_head = inner(head_rows, seq_d_attn)
    g_expand_head = inner(latent_rows, d_pairs)
    g_query_head = inner(d_query_full, seq_normed).astype(jnp.bfloat16)
    g_expand_head = g_expand_head.astype(jnp.bfloat16)
    g_out_head = g_out_head.astype(jnp.bfloat16)

    def half_of(whole, which, axis):
        size = whole.shape[axis] // shards
        return lax.dynamic_slice_in_dim(whole, which * size, size, axis)

    own_d_query, d_sums, out_sum, other_query, other_expand, other_out_grad = exchange_and_sums(
        d_query_full.reshape(experts, rows, head_units),
        d_keys.reshape(experts, rows, -1),
        out_part,
        [
            half_of(g_query_head, 1 - shard, 1),
            half_of(g_expand_head, 1 - shard, 0),
            g_out_head,
        ],
        5,
    )
    output = hidden + out_sum
    own_d_query = own_d_query.transpose(1, 0, 2).reshape(rows, experts * head_units)
    key_gradient = d_sums[:, :feature_width]
    d_normed_in = in_order(
        outer_product(own_d_query, query_own), outer_product(own_d_query, query_other)
    )

    def summed(own, other):
        return (own.astype(jnp.float32) + other.astype(jnp.float32)).astype(jnp.bfloat16)

    own_query = summed(half_of(g_query_head, shard, 1), other_query)
    own_expand = summed(half_of(g_expand_head, shard, 0), other_expand)
    own_out = summed(g_out_head, other_out_grad)
    own_latent = outer_product(normed_in, w_latent[:LATENT_WIDTH])
    own_cosine = lax.dynamic_slice_in_dim(cosine_table, position * rows, rows, 0)
    own_sine = lax.dynamic_slice_in_dim(sine_table, position * rows, rows, 0)
    inv_lat = lax.rsqrt(jnp.mean(own_latent * own_latent, axis=-1, keepdims=True) + EPS)
    d_compact, g_lat_grad = norm_backward(
        own_latent, inv_lat, g_lat, key_gradient[:, :LATENT_WIDTH]
    )
    d_rope = reverse_rotary(key_gradient[:, LATENT_WIDTH:], own_cosine, own_sine)
    d_latent_full = jnp.concatenate([d_compact, d_rope], axis=-1).astype(jnp.bfloat16)
    g_latent = inner(d_latent_full, normed_in)
    d_normed_in = d_normed_in + matrix_product(d_latent_full, w_latent)
    d_norm_in, g_attn_grad = norm_backward(x_in, inv_attn, g_attn, d_normed_in)
    d_tokens = (d_hidden + d_norm_in).astype(jnp.bfloat16)

    half = MODEL_WIDTH // blocks
    cols = lax.all_to_all(
        g_shared_in.reshape(blocks, half, 2 * lanes),
        ("expert", "fsdp"),
        split_axis=0,
        concat_axis=0,
        tiled=True,
    )
    cols = cols.transpose(1, 0, 2).astype(jnp.float32)
    r_sgate = cols[:, :, :units].reshape(half, blocks * units)
    r_sup = cols[:, :, lanes : lanes + units].reshape(half, blocks * units)
    g_sdown = g_shared_out[:units]
    model_half = MODEL_WIDTH // shards
    small_rows = jnp.concatenate([g_latent, g_router, g_attn_grad[None], g_ffn_grad[None]], axis=0)
    used = small_rows.shape[0]
    share = 2 * 32 * (-(-(used + 1) // (2 * 32 * experts)))

    def rows_for(which):
        here = small_rows[:, which * model_half : (which + 1) * model_half]
        lat = jnp.pad(
            g_lat_grad[which * lat_half : (which + 1) * lat_half], (0, model_half - lat_half)
        )
        full = jnp.concatenate([here, lat[None]], axis=0).astype(jnp.bfloat16)
        full = jnp.pad(full, ((0, experts * share - used - 1), (0, 0)))
        return full.reshape(experts, share, model_half)

    small_part = jnp.concatenate([rows_for(which) for which in range(shards)], axis=0)
    r_query, r_expand, r_out, small_sum = gather_and_scatter(
        [own_query, own_expand, own_out], small_part, 6, gated=(2,)
    )
    (small_all,) = gather_rows([small_sum.astype(jnp.bfloat16)], False, 7)
    r_query, r_expand, r_out = finish(shard, r_query, r_expand, r_out)
    small_all = small_all.reshape(experts * share, model_half).astype(jnp.float32)
    return (
        output.astype(jnp.bfloat16)[None],
        d_tokens[None],
        small_all[feature_width + experts],
        r_query,
        small_all[:feature_width].T,
        small_all[feature_width + experts + 2, :lat_half],
        r_expand,
        r_out,
        small_all[feature_width + experts + 1],
        small_all[feature_width : feature_width + experts].T,
        r_sgate,
        r_sup,
        g_sdown,
        g_gate[None],
        g_up[None],
        g_down[None],
    )


def solution(mesh):
    shape = (mesh.shape["expert"], mesh.shape["fsdp"])
    split = shape == (LINE * SQUARE * CORES, SQUARE) and shape[0] == HEAD_COUNT
    return jax.shard_map(
        split_body if split else body,
        mesh=mesh,
        in_specs=(
            P("fsdp", "expert", None),
            P("fsdp", "expert", None),
            P("fsdp", "expert", None),
            P("fsdp"),
            P("fsdp", None),
            P("fsdp", None),
            P("fsdp"),
            P("fsdp", None),
            P("fsdp", None),
            P("fsdp"),
            P("fsdp", None),
            P(("expert", "fsdp"), None),
            P(("expert", "fsdp"), None),
            P(("expert", "fsdp"), None),
            P("expert", None, "fsdp"),
            P("expert", None, "fsdp"),
            P("expert", "fsdp", None),
        ),
        out_specs=(
            P("fsdp", "expert", None),
            P("fsdp", "expert", None),
            P("fsdp"),
            P("fsdp", None),
            P("fsdp", None),
            P("fsdp"),
            P("fsdp", None),
            P("fsdp", None),
            P("fsdp"),
            P("fsdp", None),
            P(("expert", "fsdp"), None),
            P(("expert", "fsdp"), None),
            P(("expert", "fsdp"), None),
            P("expert", None, "fsdp"),
            P("expert", None, "fsdp"),
            P("expert", "fsdp", None),
        ),
        check_vma=False,
    )
```

```python
import functools

import jax
import jax.numpy as jnp
import numpy as np
from jax import lax
from jax.experimental import pallas as pl
from jax.experimental.pallas import tpu as pltpu
from jax.sharding import PartitionSpec as P

MODEL_WIDTH = 2048
HEAD_COUNT = 16
PLAIN_UNITS = 128
ROTARY_UNITS = 64
VALUE_UNITS = 128
LATENT_WIDTH = 512
TOPK = 6


EPS = 1e-06


def matrix_product(left, right):
    return jnp.dot(left, right, preferred_element_type=jnp.float32)


def inner(left, right):
    return lax.dot_general(
        left, right, (((0,), (0,)), ((), ())), preferred_element_type=jnp.float32
    )


def outer_product(left, right):
    return lax.dot_general(
        left, right, (((1,), (1,)), ((), ())), preferred_element_type=jnp.float32
    )


def norm_forward(value, gain):
    inverse = lax.rsqrt(jnp.mean(value * value, axis=-1, keepdims=True) + EPS)
    return (value * inverse * gain, inverse)


def norm_backward(value, inverse, gain, grad):
    unit = value * inverse
    scaled = grad * gain
    d_value = inverse * (scaled - unit * jnp.mean(scaled * unit, axis=-1, keepdims=True))
    return (d_value, jnp.sum(grad * unit, axis=0))


def rope_tables(positions):
    half = ROTARY_UNITS // 2
    freqs = 10000.0 ** (-jnp.arange(half, dtype=jnp.float32) * (2.0 / ROTARY_UNITS))
    angles = positions.astype(jnp.float32)[:, None] * freqs[None, :]
    return (jnp.cos(angles), jnp.sin(angles))


def apply_rotary(value, cosine_table, sine_table):
    half = ROTARY_UNITS // 2
    first = value[..., :half]
    second = value[..., half:]
    return jnp.concatenate(
        [first * cosine_table - second * sine_table, first * sine_table + second * cosine_table],
        axis=-1,
    )


def reverse_rotary(grad, cosine_table, sine_table):
    half = ROTARY_UNITS // 2
    first = grad[..., :half]
    second = grad[..., half:]
    return jnp.concatenate(
        [first * cosine_table + second * sine_table, second * cosine_table - first * sine_table],
        axis=-1,
    )


def silu_parts(value):
    sigma = jax.nn.sigmoid(value)
    return (value * sigma, sigma * (1.0 + value * (1.0 - sigma)))


def body(
    tokens,
    routes,
    cotangent,
    attn_gain,
    w_query,
    latent_weight,
    latent_norm_gain,
    expand_weight,
    w_out,
    ffn_gain,
    w_router,
    shared_gate,
    shared_up,
    shared_down,
    expert_gate,
    expert_up,
    expert_down,
):
    device_local = tokens.shape[1]
    experts = lax.axis_size("expert")
    shards = lax.axis_size("fsdp")
    position = lax.axis_index("expert")
    capacity = shards * (
        (device_local * TOPK * 4 + experts * 3 * shards - 1) // (experts * 3 * shards)
    )
    seq_len = device_local * experts
    feature_width = LATENT_WIDTH + ROTARY_UNITS
    scale = (PLAIN_UNITS + ROTARY_UNITS) ** (-0.5)
    attention_gain_grad, wq, wlat, g_lat, expand_matrix, wout, g_ffn, wrout = (
        lax.all_gather(attn_gain, "fsdp", axis=0, tiled=True),
        lax.all_gather(w_query, "fsdp", axis=0, tiled=True),
        lax.all_gather(latent_weight, "fsdp", axis=0, tiled=True),
        lax.all_gather(latent_norm_gain, "fsdp", axis=0, tiled=True),
        lax.all_gather(expand_weight, "fsdp", axis=0, tiled=True),
        lax.all_gather(w_out, "fsdp", axis=0, tiled=True),
        lax.all_gather(ffn_gain, "fsdp", axis=0, tiled=True),
        lax.all_gather(w_router, "fsdp", axis=0, tiled=True),
    )
    sgate, sup, sdown = (
        lax.all_gather(shared_gate, ("expert", "fsdp"), axis=0, tiled=True),
        lax.all_gather(shared_up, ("expert", "fsdp"), axis=0, tiled=True),
        lax.all_gather(shared_down, ("expert", "fsdp"), axis=0, tiled=True),
    )
    attention_gain_grad = attention_gain_grad.astype(jnp.float32)
    g_lat = g_lat.astype(jnp.float32)
    g_ffn = g_ffn.astype(jnp.float32)
    x_in = tokens[0].astype(jnp.float32)
    grad_out = cotangent[0].astype(jnp.float32)
    positions = position * device_local + jnp.arange(device_local, dtype=jnp.int32)
    cosine_table, sine_table = rope_tables(positions)
    normed, inv_attn = norm_forward(x_in, attention_gain_grad)
    normed_in = normed.astype(jnp.bfloat16)
    query_full = matrix_product(normed_in, wq).reshape(
        device_local, HEAD_COUNT, PLAIN_UNITS + ROTARY_UNITS
    )
    query_nope = query_full[:, :, :PLAIN_UNITS].astype(jnp.bfloat16)
    expanded_latent = expand_matrix.reshape(LATENT_WIDTH, HEAD_COUNT, PLAIN_UNITS + VALUE_UNITS)
    key_part = expanded_latent[:, :, :PLAIN_UNITS]
    value_part = expanded_latent[:, :, PLAIN_UNITS:]
    query_latent = jnp.einsum(
        "thd,chd->thc", query_nope, key_part, preferred_element_type=jnp.float32
    )
    query_rope = apply_rotary(
        query_full[:, :, PLAIN_UNITS:], cosine_table[:, None, :], sine_table[:, None, :]
    )
    token_rows = device_local * HEAD_COUNT
    query = (
        jnp.concatenate([query_latent, query_rope], axis=-1)
        .astype(jnp.bfloat16)
        .reshape(token_rows, feature_width)
    )
    latent_complete = matrix_product(normed_in, wlat)
    packed_rows = latent_complete[:, :LATENT_WIDTH]
    latent_state, inv_lat = norm_forward(packed_rows, g_lat)
    rotary_key = apply_rotary(latent_complete[:, LATENT_WIDTH:], cosine_table, sine_table)
    key = jnp.concatenate([latent_state, rotary_key], axis=-1).astype(jnp.bfloat16)
    keys_all = lax.all_gather(key, "expert", axis=0, tiled=True)
    block = min(512, seq_len)
    token_tally = (position * device_local + device_local + block - 1) // block
    q_pos = position * device_local + jnp.arange(token_rows, dtype=jnp.int32) // HEAD_COUNT

    def scores_of(index):
        key_rows = lax.dynamic_slice_in_dim(keys_all, index * block, block, 0)
        raw = outer_product(query, key_rows)
        k_pos = index * block + jnp.arange(block, dtype=jnp.int32)
        valid = k_pos[None, :] <= q_pos[:, None]
        return (jnp.where(valid, raw * scale, -1e30), key_rows)

    def stats_step(index, carry):
        top, total = carry
        scores, unused = scores_of(index)
        new_top = jnp.maximum(top, jnp.max(scores, axis=1))
        total = total * jnp.exp(top - new_top) + jnp.sum(jnp.exp(scores - new_top[:, None]), axis=1)
        return (new_top, total)

    top, total = lax.fori_loop(
        0,
        token_tally,
        stats_step,
        (jnp.full((token_rows,), -1e30, jnp.float32), jnp.zeros((token_rows,), jnp.float32)),
    )
    log_total = top + jnp.log(total)

    def mixing_update(index, running_total):
        scores, key_rows = scores_of(index)
        weight_arrays = jnp.exp(scores - log_total[:, None]).astype(jnp.bfloat16)
        return running_total + matrix_product(weight_arrays, key_rows[:, :LATENT_WIDTH])

    mixed_output_sum = lax.fori_loop(
        0, token_tally, mixing_update, jnp.zeros((token_rows, LATENT_WIDTH), jnp.float32)
    )
    mixed_output = mixed_output_sum.astype(jnp.bfloat16).reshape(
        device_local, HEAD_COUNT, LATENT_WIDTH
    )
    heads = jnp.einsum("thc,chv->thv", mixed_output, value_part, preferred_element_type=jnp.float32)
    heads = heads.reshape(device_local, HEAD_COUNT * VALUE_UNITS).astype(jnp.bfloat16)
    hidden = x_in + matrix_product(heads, wout)
    normed2, inv_ffn = norm_forward(hidden, g_ffn)
    normed_ffn = normed2.astype(jnp.bfloat16)
    logits = matrix_product(normed_ffn, wrout)
    router = jax.nn.softmax(logits, axis=-1)
    own_routes = routes[0]
    names = jnp.arange(experts, dtype=jnp.int32)
    chosen = (own_routes[:, :, None] == names[None, None, :]).astype(jnp.float32)
    gates = jnp.sum(chosen * router[:, None, :], axis=-1)
    hits = (own_routes.reshape(device_local * TOPK)[:, None] == names[None, :]).astype(jnp.int32)
    slot = jnp.sum((jnp.cumsum(hits, axis=0) - hits) * hits, axis=1)
    place = own_routes.reshape(device_local * TOPK) * capacity + slot
    token_of = jnp.arange(device_local * TOPK, dtype=jnp.int32) // TOPK
    table = jnp.full((experts * capacity,), device_local, jnp.int32).at[place].set(token_of)
    padded = jnp.concatenate([normed_ffn, jnp.zeros((1, MODEL_WIDTH), jnp.bfloat16)], axis=0)
    buffer = padded[table].reshape(experts, capacity, MODEL_WIDTH)
    w_g, w_u, w_d = (expert_gate[0], expert_up[0], expert_down[0])

    def spread(values):
        return jnp.broadcast_to(values[:, None], (experts, shards, capacity, MODEL_WIDTH)).reshape(
            experts * shards, capacity, MODEL_WIDTH
        )

    def collect(back):
        return jnp.sum(back.reshape(experts, shards, capacity, MODEL_WIDTH), axis=1).reshape(
            experts * capacity, MODEL_WIDTH
        )

    received = lax.all_to_all(
        spread(buffer), ("expert", "fsdp"), split_axis=0, concat_axis=0, tiled=True
    )
    ex_rows = received.reshape(-1, MODEL_WIDTH)
    pre_gate = matrix_product(ex_rows, w_g)
    pre_up = matrix_product(ex_rows, w_u)
    act_gate, slope = silu_parts(pre_gate)
    ex_act = (act_gate * pre_up).astype(jnp.bfloat16)
    ex_out = matrix_product(ex_act, w_d).reshape(received.shape)
    returned = lax.all_to_all(
        ex_out.astype(jnp.bfloat16), ("expert", "fsdp"), split_axis=0, concat_axis=0, tiled=True
    ).astype(ex_out.dtype)
    results = collect(returned)
    picked = results[place].reshape(device_local, TOPK, MODEL_WIDTH)
    routed = jnp.sum(gates[:, :, None] * picked, axis=1)
    sh_gate = matrix_product(normed_ffn, sgate)
    sh_up = matrix_product(normed_ffn, sup)
    sh_silu, sh_slope = silu_parts(sh_gate)
    sh_act = (sh_silu * sh_up).astype(jnp.bfloat16)
    shared = matrix_product(sh_act, sdown)
    output = hidden + routed + shared
    d_shared = grad_out.astype(jnp.bfloat16)
    shared_down_gradient = inner(sh_act, d_shared)
    d_sh_act = outer_product(d_shared, sdown)
    d_sh_gate = (d_sh_act * sh_up * sh_slope).astype(jnp.bfloat16)
    d_sh_up = (d_sh_act * sh_silu).astype(jnp.bfloat16)
    shared_gate_gradient = inner(normed_ffn, d_sh_gate)
    shared_up_gradient = inner(normed_ffn, d_sh_up)
    d_normed_ffn = outer_product(d_sh_gate, sgate) + outer_product(d_sh_up, sup)
    d_picked = (
        (gates[:, :, None] * grad_out[:, None, :])
        .astype(jnp.bfloat16)
        .reshape(device_local * TOPK, MODEL_WIDTH)
    )
    d_gates = jnp.sum(picked * grad_out[:, None, :], axis=2)
    d_buffer = (
        jnp.zeros((experts * capacity, MODEL_WIDTH), jnp.bfloat16)
        .at[place]
        .set(d_picked)
        .reshape(experts, capacity, MODEL_WIDTH)
    )
    d_received = lax.all_to_all(
        spread(d_buffer), ("expert", "fsdp"), split_axis=0, concat_axis=0, tiled=True
    )
    d_rows = d_received.reshape(-1, MODEL_WIDTH)
    d_act = outer_product(d_rows, w_d)
    g_down = inner(ex_act, d_rows)
    d_pre_gate = (d_act * pre_up * slope).astype(jnp.bfloat16)
    d_pre_up = (d_act * act_gate).astype(jnp.bfloat16)
    g_gate = inner(ex_rows, d_pre_gate)
    g_up = inner(ex_rows, d_pre_up)
    d_ex_rows = (outer_product(d_pre_gate, w_g) + outer_product(d_pre_up, w_u)).reshape(
        received.shape
    )
    d_returned = lax.all_to_all(
        d_ex_rows.astype(jnp.bfloat16), ("expert", "fsdp"), split_axis=0, concat_axis=0, tiled=True
    ).astype(d_ex_rows.dtype)
    d_results = collect(d_returned)
    d_normed_ffn = d_normed_ffn + jnp.sum(
        d_results[place].reshape(device_local, TOPK, MODEL_WIDTH), axis=1
    )
    d_router = jnp.sum(chosen * d_gates[:, :, None], axis=1)
    d_logits = (router * (d_router - jnp.sum(router * d_router, axis=1, keepdims=True))).astype(
        jnp.bfloat16
    )
    router_weight_gradient = inner(normed_ffn, d_logits)
    d_normed_ffn = d_normed_ffn + outer_product(d_logits, wrout)
    d_hidden_norm, g_ffn_grad = norm_backward(hidden, inv_ffn, g_ffn, d_normed_ffn)
    d_hidden = grad_out + d_hidden_norm
    d_attn = d_hidden.astype(jnp.bfloat16)
    output_weight_gradient = inner(heads, d_attn)
    d_heads = (
        outer_product(d_attn, wout)
        .astype(jnp.bfloat16)
        .reshape(device_local, HEAD_COUNT, VALUE_UNITS)
    )
    value_weight_gradient = jnp.einsum(
        "thc,thv->chv", mixed_output, d_heads, preferred_element_type=jnp.float32
    )
    mixed_gradient = jnp.einsum(
        "thv,chv->thc", d_heads, value_part, preferred_element_type=jnp.float32
    )
    mixed_gradient = mixed_gradient.astype(jnp.bfloat16).reshape(token_rows, LATENT_WIDTH)
    delta = jnp.sum(mixed_gradient.astype(jnp.float32) * mixed_output_sum, axis=1)

    def back_step(index, carry):
        d_query_acc, d_keys_acc = carry
        scores, key_rows = scores_of(index)
        weight_arrays = jnp.exp(scores - log_total[:, None])
        weight_gradients = outer_product(mixed_gradient, key_rows[:, :LATENT_WIDTH])
        d_scores = (weight_arrays * (weight_gradients - delta[:, None]) * scale).astype(
            jnp.bfloat16
        )
        d_query_acc = d_query_acc + matrix_product(d_scores, key_rows)
        d_values = inner(weight_arrays.astype(jnp.bfloat16), mixed_gradient)
        d_block = inner(d_scores, query) + jnp.concatenate(
            [d_values, jnp.zeros((block, ROTARY_UNITS), jnp.float32)], axis=1
        )
        previous = lax.dynamic_slice_in_dim(d_keys_acc, index * block, block, 0)
        return (
            d_query_acc,
            lax.dynamic_update_slice_in_dim(d_keys_acc, previous + d_block, index * block, 0),
        )

    d_query, d_keys = lax.fori_loop(
        0,
        token_tally,
        back_step,
        (
            jnp.zeros((token_rows, feature_width), jnp.float32),
            jnp.zeros((seq_len, feature_width), jnp.float32),
        ),
    )
    key_gradient = lax.psum_scatter(
        d_keys.astype(jnp.bfloat16), "expert", scatter_dimension=0, tiled=True
    )
    query_up_gradient = d_query.astype(jnp.bfloat16).reshape(
        device_local, HEAD_COUNT, feature_width
    )
    query_latent_gradient = query_up_gradient[:, :, :LATENT_WIDTH]
    key_weight_gradient = jnp.einsum(
        "thc,thd->chd", query_latent_gradient, query_nope, preferred_element_type=jnp.float32
    )
    d_q_nope = jnp.einsum(
        "thc,chd->thd", query_latent_gradient, key_part, preferred_element_type=jnp.float32
    )
    d_q_rope = reverse_rotary(
        query_up_gradient[:, :, LATENT_WIDTH:].astype(jnp.float32),
        cosine_table[:, None, :],
        sine_table[:, None, :],
    )
    d_query_full = (
        jnp.concatenate([d_q_nope, d_q_rope], axis=-1)
        .astype(jnp.bfloat16)
        .reshape(device_local, HEAD_COUNT * (PLAIN_UNITS + ROTARY_UNITS))
    )
    query_weight_gradient = inner(normed_in, d_query_full)
    d_normed_in = outer_product(d_query_full, wq)
    latent_gradient = key_gradient[:, :LATENT_WIDTH].astype(jnp.float32)
    rotary_key_gradient = reverse_rotary(
        key_gradient[:, LATENT_WIDTH:].astype(jnp.float32), cosine_table, sine_table
    )
    d_compact, g_lat_grad = norm_backward(packed_rows, inv_lat, g_lat, latent_gradient)
    d_latent_full = jnp.concatenate([d_compact, rotary_key_gradient], axis=-1).astype(jnp.bfloat16)
    latent_weight_gradient = inner(normed_in, d_latent_full)
    d_normed_in = d_normed_in + outer_product(d_latent_full, wlat)
    d_norm_in, g_attn_grad = norm_backward(x_in, inv_attn, attention_gain_grad, d_normed_in)
    d_tokens = (d_hidden + d_norm_in).astype(jnp.bfloat16)
    expand_weight_gradient = jnp.concatenate(
        [key_weight_gradient, value_weight_gradient], axis=-1
    ).reshape(LATENT_WIDTH, HEAD_COUNT * (PLAIN_UNITS + VALUE_UNITS))
    r_sgate, r_sup, r_sdown = (
        lax.psum_scatter(shared_gate_gradient, ("expert", "fsdp"), scatter_dimension=0, tiled=True),
        lax.psum_scatter(shared_up_gradient, ("expert", "fsdp"), scatter_dimension=0, tiled=True),
        lax.psum_scatter(shared_down_gradient, ("expert", "fsdp"), scatter_dimension=0, tiled=True),
    )
    r_attn, r_query, r_latent, r_lgain, r_expand, r_out, r_fgain, r_router = (
        lax.psum_scatter(
            g_attn_grad.astype(jnp.bfloat16), "fsdp", scatter_dimension=0, tiled=True
        ).astype(jnp.float32),
        lax.psum_scatter(
            query_weight_gradient.astype(jnp.bfloat16), "fsdp", scatter_dimension=0, tiled=True
        ).astype(jnp.float32),
        lax.psum_scatter(
            latent_weight_gradient.astype(jnp.bfloat16), "fsdp", scatter_dimension=0, tiled=True
        ).astype(jnp.float32),
        lax.psum_scatter(
            g_lat_grad.astype(jnp.bfloat16), "fsdp", scatter_dimension=0, tiled=True
        ).astype(jnp.float32),
        lax.psum_scatter(
            expand_weight_gradient.astype(jnp.bfloat16), "fsdp", scatter_dimension=0, tiled=True
        ).astype(jnp.float32),
        lax.psum_scatter(
            output_weight_gradient.astype(jnp.bfloat16), "fsdp", scatter_dimension=0, tiled=True
        ).astype(jnp.float32),
        lax.psum_scatter(
            g_ffn_grad.astype(jnp.bfloat16), "fsdp", scatter_dimension=0, tiled=True
        ).astype(jnp.float32),
        lax.psum_scatter(
            router_weight_gradient.astype(jnp.bfloat16), "fsdp", scatter_dimension=0, tiled=True
        ).astype(jnp.float32),
    )
    r_attn, r_query, r_latent, r_lgain, r_expand, r_out, r_fgain, r_router = (
        lax.psum(r_attn.astype(jnp.bfloat16), "expert").astype(jnp.float32),
        lax.psum(r_query.astype(jnp.bfloat16), "expert").astype(jnp.float32),
        lax.psum(r_latent.astype(jnp.bfloat16), "expert").astype(jnp.float32),
        lax.psum(r_lgain.astype(jnp.bfloat16), "expert").astype(jnp.float32),
        lax.psum(r_expand.astype(jnp.bfloat16), "expert").astype(jnp.float32),
        lax.psum(r_out.astype(jnp.bfloat16), "expert").astype(jnp.float32),
        lax.psum(r_fgain.astype(jnp.bfloat16), "expert").astype(jnp.float32),
        lax.psum(r_router.astype(jnp.bfloat16), "expert").astype(jnp.float32),
    )
    return (
        output.astype(jnp.bfloat16)[None],
        d_tokens[None],
        r_attn,
        r_query,
        r_latent,
        r_lgain,
        r_expand,
        r_out,
        r_fgain,
        r_router,
        r_sgate,
        r_sup,
        r_sdown,
        g_gate[None],
        g_up[None],
        g_down[None],
    )


LINE = 4
SQUARE = 2
CORES = 2
MESH = pl.DeviceIdType.MESH
VMEM_LIMIT = 56 * 1024 * 1024


class Place:
    def __init__(self):
        index = lax.axis_index("expert")
        self.y = lax.axis_index("fsdp")
        self.c = lax.rem(index, CORES)
        self.b = lax.rem(lax.div(index, CORES), SQUARE)
        self.a = lax.div(index, CORES * SQUARE)

    def device(self, da=0, db=0, dc=0, dy=0):
        b = 1 - self.b if db else self.b
        c = 1 - self.c if dc else self.c
        y = 1 - self.y if dy else self.y
        return (((self.a + da) * SQUARE + b) * CORES + c, y)

    def block(self, full, a, db=0, dc=0, dy=0):
        b = 1 - self.b if db else self.b
        c = 1 - self.c if dc else self.c
        y = 1 - self.y if dy else self.y
        flat = (a * SQUARE + b) * CORES + c
        return y * (LINE * SQUARE * CORES) + flat if full else flat

    def greet(self, with_y):
        barrier = pltpu.get_barrier_semaphore()
        near = [dict(db=1), dict(dc=1)] + ([dict(dy=1)] if with_y else [])
        for step in near:
            pl.semaphore_signal(barrier, inc=1, device_id=self.device(**step), device_id_type=MESH)

        @pl.when(self.a > 0)
        def _():
            pl.semaphore_signal(barrier, inc=1, device_id=self.device(da=-1), device_id_type=MESH)

        @pl.when(self.a < LINE - 1)
        def _():
            pl.semaphore_signal(barrier, inc=1, device_id=self.device(da=1), device_id_type=MESH)

        ends = jnp.logical_or(self.a == 0, self.a == LINE - 1).astype(jnp.int32)
        pl.semaphore_wait(barrier, len(near) + 2 - ends)


class Sender:
    def __init__(self, place, sems):
        self.place, self.sems, self.pending = place, sems, []

    def send(self, src, dst, recv_sem, step, cond=None):
        sem = self.sems.at[len(self.pending)]

        def make():
            return pltpu.make_async_remote_copy(
                src_ref=src,
                dst_ref=dst,
                send_sem=sem,
                recv_sem=recv_sem,
                device_id=self.place.device(**step),
                device_id_type=MESH,
            )

        def start():
            make().start()

        guarded(cond, start)
        self.pending.append((cond, lambda: make().wait_send()))

    def arrived(self, dst, recv_sem):
        pltpu.make_async_remote_copy(
            src_ref=dst,
            dst_ref=dst,
            send_sem=self.sems.at[0],
            recv_sem=recv_sem,
            device_id=self.place.device(dc=1),
            device_id_type=MESH,
        ).wait_recv()

    def finish(self):
        for cond, wait in self.pending:
            guarded(cond, wait)


def guarded(cond, action):
    if cond is None:
        action()
    else:
        pl.when(cond)(action)


def both(first, second):
    if first is None or second is None:
        return second if first is None else first
    return jnp.logical_and(first, second)


def gather_ticks(place, sender, full, gated, ins, outs, local_sems, recv_sems):
    a = place.a
    count = len(ins)

    def own_copy(at):
        return pltpu.make_async_copy(
            ins[at], outs[at].at[place.block(full, a)], local_sems.at[at]
        )

    def chunk(at, block, half):
        size = ins[at].shape[0] // 2
        return outs[at].at[block, pl.ds(half * size, size)]

    def sem_of(at, block, half):
        return recv_sems.at[at, block * 2 + half]

    def forward(at, block, half, src, step, cond=None):
        sender.send(src, chunk(at, block, half), sem_of(at, block, half), step, cond)

    def receive(at, block, half, cond):
        guarded(cond, lambda: sender.arrived(chunk(at, block, half), sem_of(at, block, half)))

    def held_by(at, delta, cond):
        if at not in gated:
            return cond
        return both(cond, lax.div(a + delta, LINE // 2) == place.y)

    def from_line(delta, always):
        for half in range(2):
            for at in range(count):
                block = place.block(full, a + delta)
                cond = held_by(at, delta, always)
                size = ins[at].shape[0] // 2
                if delta == 0:
                    src = ins[at].at[pl.ds(half * size, size)]
                else:
                    receive(at, block, half, cond)
                    src = chunk(at, block, half)
                if delta <= 0:
                    forward(at, block, half, src, dict(da=1), both(cond, a < LINE - 1))
                if delta >= 0:
                    forward(at, block, half, src, dict(da=-1), both(cond, a > 0))
                forward(at, block, half, src, dict(db=1), cond)
                if full:
                    forward(at, block, half, src, dict(dy=1), cond)
                forward(at, block, half, src, dict(dc=1), cond)

    def from_side(delta, always):
        for half in range(2):
            for at in range(count):
                cond = held_by(at, delta, always)
                block = place.block(full, a + delta, db=1)
                receive(at, block, half, cond)
                if full and half == 0:
                    forward(at, block, half, chunk(at, block, half), dict(dy=1), cond)
                forward(at, block, half, chunk(at, block, half), dict(dc=1), cond)
                if full:
                    block = place.block(full, a + delta, dy=1)
                    receive(at, block, half, cond)
                    if half == 1:
                        forward(at, block, half, chunk(at, block, half), dict(db=1), cond)
                    forward(at, block, half, chunk(at, block, half), dict(dc=1), cond)

    def from_corner(delta, always):
        for half in range(2):
            for at in range(count):
                cond = held_by(at, delta, always)
                block = place.block(True, a + delta, db=1, dy=1)
                receive(at, block, half, cond)
                forward(at, block, half, chunk(at, block, half), dict(dc=1), cond)

    def from_sibling(delta, always):
        for half in range(2):
            for at in range(count):
                cond = held_by(at, delta, always)
                for db in range(2):
                    for dy in range(2 if full else 1):
                        receive(at, place.block(full, a + delta, db=db, dc=1, dy=dy), half, cond)

    rounds = [[(0, None)]]
    for s in range(1, LINE):
        rounds.append([(-s, a >= s), (s, a + s < LINE)])
    stages = [from_line, from_side] + ([from_corner] if full else []) + [from_sibling]

    def tick(number):
        if number == 0:
            for at in range(count):
                own_copy(at).start()
        for level, stage in enumerate(stages):
            if 0 <= number - level < len(rounds):
                for delta, cond in rounds[number - level]:
                    stage(delta, cond)
        if number == len(rounds) + len(stages) - 2:
            for at in range(count):
                own_copy(at).wait()

    return [functools.partial(tick, number) for number in range(len(rounds) + len(stages) - 1)]


def send_pairs(sender, ins, outs, sems):
    for at, (src, dst) in enumerate(zip(ins, outs)):
        sender.send(src, dst, sems.at[at], dict(dy=1))


def take_pairs(sender, outs, sems):
    for at, dst in enumerate(outs):
        sender.arrived(dst, sems.at[at])


def gather_kernel(full, count, pairs, gated, *refs):
    ins, outs = refs[: count + pairs], refs[count + pairs : 2 * (count + pairs)]
    local_sems, send_sems, recv_sems, pair_sems = refs[2 * (count + pairs) :]
    place = Place()
    sender = Sender(place, send_sems)
    place.greet(full or pairs > 0)
    send_pairs(sender, ins[count:], outs[count:], pair_sems)
    for tick in gather_ticks(
        place, sender, full, gated, ins[:count], outs[:count], local_sems, recv_sems
    ):
        tick()
    take_pairs(sender, outs[count:], pair_sems)
    sender.finish()


def gather_rows(arrays, full, collective_id, swapped=(), gated=()):
    blocks = LINE * SQUARE * CORES * (SQUARE if full else 1)
    count, pairs = len(arrays), len(swapped)
    lines = 2 * LINE - 1
    sends = pairs + count * lines * 2 * (9 if full else 5)
    moved = sum(blocks * 2 * x.size * x.dtype.itemsize for x in arrays)
    return pl.pallas_call(
        functools.partial(gather_kernel, full, count, pairs, gated),
        out_shape=[jax.ShapeDtypeStruct((blocks,) + x.shape, x.dtype) for x in arrays]
        + [jax.ShapeDtypeStruct(x.shape, x.dtype) for x in swapped],
        in_specs=[pl.BlockSpec(memory_space=pl.ANY)] * (count + pairs),
        out_specs=[pl.BlockSpec(memory_space=pl.ANY)] * (count + pairs),
        scratch_shapes=[
            pltpu.SemaphoreType.DMA((count,)),
            pltpu.SemaphoreType.DMA((sends,)),
            pltpu.SemaphoreType.DMA((count, blocks * 2)),
            pltpu.SemaphoreType.DMA((max(pairs, 1),)),
        ],
        compiler_params=pltpu.CompilerParams(collective_id=collective_id, has_side_effects=True),
        cost_estimate=pl.CostEstimate(flops=0, bytes_accessed=6 * moved, transcendentals=0),
    )(*arrays, *swapped)


def add_rows(target, sources, size):
    def step(at, carry):
        rows = pl.ds(pl.multiple_of(at * 16, 16), 16)
        total = sources[0][rows, :].astype(jnp.float32)
        for source in sources[1:]:
            total = total + source[rows, :].astype(jnp.float32)
        target[rows, :] = total.astype(target.dtype)
        return carry

    lax.fori_loop(0, size // 16, step, 0)


def scatter_ticks(place, sender, full, part, out, scratch):
    mine, got, side, up, down, load_sems, recv_sems = scratch
    a = place.a
    kinds = 4 if full else 2
    size = part.shape[1]
    half = size // 2
    order = [LINE - 1, 0, LINE - 2, 1]
    walk = (3, 1, 2, 0) if full else (1, 0)

    def sem_of(group, target, kind):
        return recv_sems.at[group, target * 4 + kind]

    def load(target, kind):
        block = place.block(full, target, db=kind % 2, dy=kind // 2)
        return pltpu.make_async_copy(
            part.at[block], mine.at[target, kind], load_sems.at[target * 4 + kind]
        )

    def begin():
        for target in order:
            for kind in walk:
                load(target, kind).start()
                block = place.block(full, target, db=kind % 2, dc=1, dy=kind // 2)
                sender.send(
                    part.at[block], got.at[target, kind], sem_of(0, target, kind), dict(dc=1)
                )

    def rows_of(ref, which):
        return ref.at[pl.ds(which * half, half)]

    def over_cores(target):
        for kind in walk:
            load(target, kind).wait()
            sender.arrived(got.at[target, kind], sem_of(0, target, kind))
            add_rows(mine.at[target, kind], [mine.at[target, kind], got.at[target, kind]], size)
            held = mine.at[target, kind]
            if kind == 3:
                sender.send(rows_of(held, 0), side.at[target, 4], sem_of(1, target, 0), dict(db=1))
                sender.send(rows_of(held, 1), side.at[target, 5], sem_of(1, target, 1), dict(dy=1))
            if kind == 1:
                sender.send(rows_of(held, 0), side.at[target, 0], sem_of(2, target, 0), dict(db=1))
                if not full:
                    sender.send(
                        rows_of(held, 1), side.at[target, 1], sem_of(2, target, 1), dict(db=1)
                    )
            if kind == 2:
                sender.send(rows_of(held, 1), side.at[target, 3], sem_of(2, target, 3), dict(dy=1))

    def over_corner(target):
        sender.arrived(side.at[target, 4], sem_of(1, target, 0))
        held = rows_of(mine.at[target, 2], 0)
        add_rows(held, [held, side.at[target, 4]], half)
        sender.send(held, side.at[target, 2], sem_of(2, target, 2), dict(dy=1))
        sender.arrived(side.at[target, 5], sem_of(1, target, 1))
        held = rows_of(mine.at[target, 1], 1)
        add_rows(held, [held, side.at[target, 5]], half)
        sender.send(held, side.at[target, 1], sem_of(2, target, 1), dict(db=1))

    def over_line(target):
        for which in range(2):
            held = rows_of(mine.at[target, 0], which)
            parts = [held]
            for source in (0, 2) if full else (0,):
                sender.arrived(side.at[target, source + which], sem_of(2, target, source + which))
                parts.append(side.at[target, source + which])
            below, above = rows_of(up.at[target], which), rows_of(down.at[target], which)
            below_sem, above_sem = sem_of(3, target, which), sem_of(3, target, 2 + which)

            def upward(with_below):
                extra = []
                if with_below:
                    sender.arrived(below, below_sem)
                    extra = [below]
                add_rows(held, parts + extra, half)

            def downward(with_above):
                extra = []
                if with_above:
                    sender.arrived(above, above_sem)
                    extra = [above]
                add_rows(held, parts + extra, half)

            if target > 0:
                pl.when(jnp.logical_and(a < target, a > 0))(lambda: upward(True))
                pl.when(a == 0)(lambda: upward(False))
                sender.send(held, below, below_sem, dict(da=1), a < target)
            if target < LINE - 1:
                pl.when(jnp.logical_and(a > target, a < LINE - 1))(lambda: downward(True))
                pl.when(a == LINE - 1)(lambda: downward(False))
                sender.send(held, above, above_sem, dict(da=-1), a > target)

            def last():
                extra = []
                if target > 0:
                    sender.arrived(below, below_sem)
                    extra.append(below)
                if target < LINE - 1:
                    sender.arrived(above, above_sem)
                    extra.append(above)
                add_rows(rows_of(out, which), parts + extra, half)

            pl.when(a == target)(last)

    stages = [over_cores] + ([over_corner] if full else []) + [over_line]

    def tick(number):
        if number == 0:
            begin()
        for level, stage in enumerate(stages):
            if 0 <= number - level < len(order):
                stage(order[number - level])

    return [functools.partial(tick, number) for number in range(len(order) + len(stages) - 1)]


def scatter_kernel(full, pairs, part, *refs):
    ins, out, outs = refs[:pairs], refs[pairs], refs[pairs + 1 : 2 * pairs + 1]
    mine, got, side, up, down, load_sems, send_sems, recv_sems, pair_sems = refs[2 * pairs + 1 :]
    place = Place()
    sender = Sender(place, send_sems)
    place.greet(full or pairs > 0)
    send_pairs(sender, ins, outs, pair_sems)
    scratch = (mine, got, side, up, down, load_sems, recv_sems)
    for tick in scatter_ticks(place, sender, full, part, out, scratch):
        tick()
    take_pairs(sender, outs, pair_sems)
    sender.finish()


def scatter_scratch(full, rows, width, dtype, pairs):
    kinds = 4 if full else 2
    return [
        pltpu.VMEM((LINE, kinds, rows, width), dtype),
        pltpu.VMEM((LINE, kinds, rows, width), dtype),
        pltpu.VMEM((LINE, 6, rows // 2, width), dtype),
        pltpu.VMEM((LINE, rows, width), dtype),
        pltpu.VMEM((LINE, rows, width), dtype),
        pltpu.SemaphoreType.DMA((LINE * 4,)),
        pltpu.SemaphoreType.DMA((pairs + LINE * (4 + 6 + 4),)),
        pltpu.SemaphoreType.DMA((4, LINE * 4)),
        pltpu.SemaphoreType.DMA((max(pairs, 1),)),
    ]


def gather_scatter_kernel(count, sums, gated, *refs):
    ins, parts = refs[:count], refs[count : count + sums]
    outs, totals = refs[count + sums : 2 * count + sums], refs[2 * count + sums : 2 * count + 2 * sums]
    rest = refs[2 * count + 2 * sums :]
    local_sems, gather_sends, gather_recvs = rest[:3]
    place = Place()
    senders = [Sender(place, gather_sends)]
    place.greet(True)
    ticks = []
    for at in range(sums):
        scratch = rest[3 + 9 * at : 12 + 9 * at]
        senders.append(Sender(place, scratch[6]))
        ticks.append(
            scatter_ticks(
                place, senders[-1], True, parts[at], totals[at], scratch[:6] + (scratch[7],)
            )
        )
    ticks.append(
        gather_ticks(place, senders[0], False, gated, ins, outs, local_sems, gather_recvs)
    )
    for number in range(max(len(steps) for steps in ticks)):
        for steps in ticks:
            if number < len(steps):
                steps[number]()
    for sender in senders:
        sender.finish()


def gather_and_scatter(arrays, parts, collective_id, gated=()):
    blocks = LINE * SQUARE * CORES
    count, sums = len(arrays), len(parts)
    sends = count * (2 * LINE - 1) * 2 * 5
    moved = sum(blocks * 2 * x.size * x.dtype.itemsize for x in arrays)
    scratch = []
    for part in parts:
        scratch += scatter_scratch(True, *part.shape[1:], part.dtype, 0)
    return pl.pallas_call(
        functools.partial(gather_scatter_kernel, count, sums, gated),
        out_shape=[jax.ShapeDtypeStruct((blocks,) + x.shape, x.dtype) for x in arrays]
        + [jax.ShapeDtypeStruct(x.shape[1:], jnp.float32) for x in parts],
        in_specs=[pl.BlockSpec(memory_space=pl.ANY)] * (count + sums),
        out_specs=[pl.BlockSpec(memory_space=pl.ANY)] * count
        + [pl.BlockSpec(memory_space=pltpu.VMEM)] * sums,
        scratch_shapes=[
            pltpu.SemaphoreType.DMA((count,)),
            pltpu.SemaphoreType.DMA((sends,)),
            pltpu.SemaphoreType.DMA((count, blocks * 2)),
        ]
        + scratch,
        compiler_params=pltpu.CompilerParams(
            collective_id=collective_id, has_side_effects=True, vmem_limit_bytes=VMEM_LIMIT
        ),
        cost_estimate=pl.CostEstimate(flops=0, bytes_accessed=6 * moved, transcendentals=0),
    )(*arrays, *parts)


def product_step(left, right, out):
    out[...] = inner(left[...], right[...])


def scatter_products_kernel(count, part, *refs):
    lefts, rights = refs[:count], refs[count : 2 * count]
    total, outs = refs[2 * count], refs[2 * count + 1 : 3 * count + 1]
    scratch = refs[3 * count + 1 :]
    place = Place()
    sender = Sender(place, scratch[6])
    place.greet(True)
    ticks = scatter_ticks(place, sender, True, part, total, scratch[:6] + (scratch[7],))
    tile = 256
    for number, tick in enumerate(ticks):
        tick()
        if number < count:
            slots, hidden = lefts[number].shape
            width = rights[number].shape[1]
            pltpu.emit_pipeline(
                product_step,
                grid=(width // tile,),
                in_specs=[
                    pl.BlockSpec((slots, hidden), lambda i: (0, 0)),
                    pl.BlockSpec((slots, tile), lambda i: (0, i)),
                ],
                out_specs=[pl.BlockSpec((hidden, tile), lambda i: (0, i))],
            )(lefts[number], rights[number], outs[number])
    sender.finish()


def scatter_and_products(part, lefts, rights, collective_id):
    _, rows, width = part.shape
    count = len(lefts)
    hbm = pl.BlockSpec(memory_space=pl.ANY)
    return pl.pallas_call(
        functools.partial(scatter_products_kernel, count),
        out_shape=[jax.ShapeDtypeStruct((rows, width), jnp.float32)]
        + [
            jax.ShapeDtypeStruct((left.shape[1], right.shape[1]), jnp.float32)
            for left, right in zip(lefts, rights)
        ],
        in_specs=[hbm] * (1 + 2 * count),
        out_specs=[pl.BlockSpec(memory_space=pltpu.VMEM)] + [hbm] * count,
        scratch_shapes=scatter_scratch(True, rows, width, part.dtype, 0),
        compiler_params=pltpu.CompilerParams(
            collective_id=collective_id, has_side_effects=True, vmem_limit_bytes=VMEM_LIMIT
        ),
        cost_estimate=pl.CostEstimate(
            flops=0, bytes_accessed=12 * part.size * part.dtype.itemsize, transcendentals=0
        ),
    )(part, *lefts, *rights)


def scatter_rows(part, full, collective_id, swapped=()):
    blocks, rows, width = part.shape
    pairs = len(swapped)
    return pl.pallas_call(
        functools.partial(scatter_kernel, full, pairs),
        out_shape=[jax.ShapeDtypeStruct((rows, width), jnp.float32)]
        + [jax.ShapeDtypeStruct(x.shape, x.dtype) for x in swapped],
        in_specs=[pl.BlockSpec(memory_space=pl.ANY)] * (1 + pairs),
        out_specs=[pl.BlockSpec(memory_space=pltpu.VMEM)]
        + [pl.BlockSpec(memory_space=pl.ANY)] * pairs,
        scratch_shapes=scatter_scratch(full, rows, width, part.dtype, pairs),
        compiler_params=pltpu.CompilerParams(
            collective_id=collective_id, has_side_effects=True, vmem_limit_bytes=VMEM_LIMIT
        ),
        cost_estimate=pl.CostEstimate(
            flops=0, bytes_accessed=12 * part.size * part.dtype.itemsize, transcendentals=0
        ),
    )(part, *swapped)


def contract_last(left, right):
    return lax.dot_general(
        left, right, (((1,), (1,)), ((), ())), preferred_element_type=jnp.float32
    )


def contract_first(left, right):
    return lax.dot_general(
        left, right, (((0,), (0,)), ((), ())), preferred_element_type=jnp.float32
    )


def expert_kernel(
    capacity,
    normed,
    grads,
    routes,
    router_rows,
    w_gate,
    w_up,
    w_down,
    shared_in,
    shared_out,
    out_part,
    d_part,
    ex_rows,
    ex_grads,
    act_out,
    d_gate_out,
    d_up_out,
    shared_in_grad,
    shared_out_grad,
    in_total,
    out_total,
):
    position = lax.axis_index("expert")
    experts = lax.axis_size("expert")
    group, rows, width = normed.shape
    tokens, slots = group * rows, group * capacity
    bf16 = jnp.bfloat16
    x = normed[...].reshape(tokens, width)
    g = grads[...].reshape(tokens, width)

    row = lax.broadcasted_iota(jnp.int32, (tokens, tokens), 0)
    column = lax.broadcasted_iota(jnp.int32, (tokens, tokens), 1)
    before = jnp.logical_and(column < row, lax.div(row, rows) == lax.div(column, rows))
    named = routes[...].reshape(tokens, -1) == position.astype(jnp.float32).astype(bf16)
    hit = jnp.sum(jnp.where(named, 1.0, 0.0), axis=1, keepdims=True)
    tally = matrix_product(
        jnp.where(before, 1.0, 0.0).astype(bf16),
        jnp.broadcast_to(hit, (tokens, 128)).astype(bf16),
    )
    place = jnp.where(hit > 0.5, tally[:, :1], -1.0)
    token = lax.broadcasted_iota(jnp.int32, (tokens, slots), 0)
    slot = lax.broadcasted_iota(jnp.int32, (tokens, slots), 1)
    same = lax.div(slot, capacity) == lax.div(token, rows)
    wanted = lax.rem(slot, capacity).astype(jnp.float32)
    chosen = jnp.where(jnp.logical_and(same, wanted == place), 1.0, 0.0)
    pick = chosen.T.astype(bf16)
    put = chosen.astype(bf16)

    r = matrix_product(pick, x).astype(bf16)
    gr = matrix_product(pick, g).astype(bf16)
    ex_rows[...] = r
    ex_grads[...] = gr
    lane = lax.broadcasted_iota(jnp.int32, (slots, router_rows.shape[0]), 1)
    logits = jnp.where(lane < experts, contract_last(r, router_rows[...]), -1e30)
    exps = jnp.exp(logits - jnp.max(logits, axis=1, keepdims=True))
    gate = jnp.sum(jnp.where(lane == position, exps, 0.0), axis=1, keepdims=True) / jnp.sum(
        exps, axis=1, keepdims=True
    )

    pre_gate = contract_last(r, w_gate[...])
    pre_up = contract_last(r, w_up[...])
    act_gate, slope = silu_parts(pre_gate)
    act = act_gate * pre_up
    back = contract_last(gr, w_down[...])
    d_gate_slot = jnp.sum(act * back, axis=1, keepdims=True)
    scaled = (gate * act).astype(bf16)
    d_act = gate * back
    d_pre_gate = (d_act * pre_up * slope).astype(bf16)
    d_pre_up = (d_act * act_gate).astype(bf16)
    act_out[...] = scaled
    d_gate_out[...] = d_pre_gate
    d_up_out[...] = d_pre_up
    ex_out = matrix_product(scaled, w_down[...]).astype(bf16)
    d_ex = matrix_product(d_pre_gate, w_gate[...]) + matrix_product(d_pre_up, w_up[...])
    d_ex = d_ex.astype(bf16)

    units = shared_out.shape[0]
    mix = matrix_product(x, shared_in[...])
    sh_gate, sh_up = mix[:, :units], mix[:, units:]
    sh_silu, sh_slope = silu_parts(sh_gate)
    sh_act = (sh_silu * sh_up).astype(bf16)
    d_sh_act = contract_last(g, shared_out[...])
    d_mix = jnp.concatenate([d_sh_act * sh_up * sh_slope, d_sh_act * sh_silu], axis=1)
    d_mix = d_mix.astype(bf16)

    out = matrix_product(put, ex_out) + matrix_product(sh_act, shared_out[...])
    out_part[...] = out.astype(bf16).reshape(group, rows, width)
    d_in = matrix_product(put, d_ex) + contract_last(d_mix, shared_in[...])
    d_part[:, :, :width] = d_in.astype(bf16).reshape(group, rows, width)
    lane = lax.broadcasted_iota(jnp.int32, (slots, d_part.shape[2] - width), 1)
    d_gates = jnp.where(lane == position, d_gate_slot, 0.0).astype(bf16)
    d_part[:, :, width:] = matrix_product(put, d_gates).astype(bf16).reshape(group, rows, -1)

    step = pl.program_id(0)

    @pl.when(step == 0)
    def _():
        in_total[...] = jnp.zeros_like(in_total)
        out_total[...] = jnp.zeros_like(out_total)

    in_total[...] += contract_first(d_mix, x)
    out_total[...] += contract_first(sh_act, g)

    @pl.when(step == pl.num_programs(0) - 1)
    def _():
        shared_in_grad[...] = in_total[...].T.astype(bf16)
        shared_out_grad[...] = out_total[...]


def expert_phase(
    all_normed, all_grads, router_rows, w_gate, w_up, w_down, shared_in, shared_out, capacity
):
    blocks, rows, width = all_normed.shape
    group = 4
    slots = group * capacity
    hidden = w_gate.shape[0]
    units = shared_out.shape[0]
    side = all_grads.shape[2] - width
    bf16 = jnp.bfloat16

    def by_group(shape):
        zeros = (0,) * (len(shape) - 1)
        return pl.BlockSpec(shape, lambda i: (i,) + zeros)

    def fixed(shape):
        return pl.BlockSpec(
            shape, lambda i: (0,) * len(shape), pipeline_mode=pl.Buffered(buffer_count=1)
        )

    return pl.pallas_call(
        functools.partial(expert_kernel, capacity),
        grid=(blocks // group,),
        out_shape=[
            jax.ShapeDtypeStruct((blocks, rows, width), bf16),
            jax.ShapeDtypeStruct((blocks, rows, width + side), bf16),
            jax.ShapeDtypeStruct((blocks * capacity, width), bf16),
            jax.ShapeDtypeStruct((blocks * capacity, width), bf16),
            jax.ShapeDtypeStruct((blocks * capacity, hidden), bf16),
            jax.ShapeDtypeStruct((blocks * capacity, hidden), bf16),
            jax.ShapeDtypeStruct((blocks * capacity, hidden), bf16),
            jax.ShapeDtypeStruct((width, 2 * units), bf16),
            jax.ShapeDtypeStruct((units, width), jnp.float32),
        ],
        in_specs=[
            by_group((group, rows, width)),
            by_group((group, rows, width)),
            pl.BlockSpec((group, rows, side), lambda i: (i, 0, width // side)),
            fixed(router_rows.shape),
            fixed(w_gate.shape),
            fixed(w_up.shape),
            fixed(w_down.shape),
            fixed(shared_in.shape),
            fixed(shared_out.shape),
        ],
        out_specs=[
            by_group((group, rows, width)),
            by_group((group, rows, width + side)),
            by_group((slots, width)),
            by_group((slots, width)),
            by_group((slots, hidden)),
            by_group((slots, hidden)),
            by_group((slots, hidden)),
            fixed((width, 2 * units)),
            fixed((units, width)),
        ],
        scratch_shapes=[
            pltpu.VMEM((2 * units, width), jnp.float32),
            pltpu.VMEM((units, width), jnp.float32),
        ],
        compiler_params=pltpu.CompilerParams(vmem_limit_bytes=VMEM_LIMIT),
        cost_estimate=pl.CostEstimate(
            flops=2 * blocks * capacity * width * hidden * 6,
            bytes_accessed=10 * blocks * rows * width * 2,
            transcendentals=blocks * capacity * hidden,
        ),
    )(all_normed, all_grads, all_grads, router_rows, w_gate, w_up, w_down, shared_in, shared_out)


def exchange_kernel(x, out, local_sem, send_sems, recv_sems):
    me, y = lax.axis_index("expert"), lax.axis_index("fsdp")
    count = x.shape[0]
    barrier = pltpu.get_barrier_semaphore()
    peers = [lax.rem(me + step, count) for step in range(1, count)]
    for peer in peers:
        pl.semaphore_signal(barrier, inc=1, device_id=(peer, y), device_id_type=MESH)
    own = pltpu.make_async_copy(x.at[me], out.at[me], local_sem)
    own.start()
    pl.semaphore_wait(barrier, count - 1)
    copies = []
    for at, peer in enumerate(peers):
        copy = pltpu.make_async_remote_copy(
            src_ref=x.at[peer],
            dst_ref=out.at[me],
            send_sem=send_sems.at[at],
            recv_sem=recv_sems.at[at],
            device_id=(peer, y),
            device_id_type=MESH,
        )
        copy.start()
        copies.append(copy)
    for copy in copies:
        copy.wait()
    own.wait()


def exchange(x, collective_id):
    count = x.shape[0]
    return pl.pallas_call(
        exchange_kernel,
        out_shape=jax.ShapeDtypeStruct(x.shape, x.dtype),
        in_specs=[pl.BlockSpec(memory_space=pl.ANY)],
        out_specs=pl.BlockSpec(memory_space=pl.ANY),
        scratch_shapes=[
            pltpu.SemaphoreType.DMA,
            pltpu.SemaphoreType.DMA((count - 1,)),
            pltpu.SemaphoreType.DMA((count - 1,)),
        ],
        compiler_params=pltpu.CompilerParams(collective_id=collective_id, has_side_effects=True),
        cost_estimate=pl.CostEstimate(
            flops=0, bytes_accessed=20 * x.size * x.dtype.itemsize, transcendentals=0
        ),
    )(x)


def swap_halves(value):
    half = value.shape[1] // 2
    return jnp.concatenate([value[:, half:], value[:, :half]], axis=1)


def greet_plane(place):
    me = lax.axis_index("expert")
    count = LINE * SQUARE * CORES
    barrier = pltpu.get_barrier_semaphore()
    for step in range(1, count):
        peer = (lax.rem(me + step, count), place.y)
        pl.semaphore_signal(barrier, inc=1, device_id=peer, device_id_type=MESH)
    pl.semaphore_signal(barrier, inc=1, device_id=place.device(dy=1), device_id_type=MESH)
    pl.semaphore_wait(barrier, count)


def exchange_sum_kernel(pairs, moved, part, *refs):
    ins = refs[:pairs]
    moved_out, total = refs[pairs : pairs + 2]
    outs = refs[pairs + 2 : 2 * pairs + 2]
    rest = refs[2 * pairs + 2 :]
    local_sem, exchange_sends, exchange_recvs = rest[:3]
    scratch = rest[3:]
    place = Place()
    me = lax.axis_index("expert")
    count = moved.shape[0]
    greet_plane(place)
    own = pltpu.make_async_copy(moved.at[me], moved_out.at[me], local_sem)
    own.start()
    copies = []
    for at in range(count - 1):
        copy = pltpu.make_async_remote_copy(
            src_ref=moved.at[lax.rem(me + at + 1, count)],
            dst_ref=moved_out.at[me],
            send_sem=exchange_sends.at[at],
            recv_sem=exchange_recvs.at[at],
            device_id=(lax.rem(me + at + 1, count), place.y),
            device_id_type=MESH,
        )
        copy.start()
        copies.append(copy)
    sender = Sender(place, scratch[6])
    send_pairs(sender, ins, outs, scratch[8])
    for tick in scatter_ticks(place, sender, False, part, total, scratch[:6] + (scratch[7],)):
        tick()
    take_pairs(sender, outs, scratch[8])
    sender.finish()
    for copy in copies:
        copy.wait()
    own.wait()


def exchange_and_sum(moved, part, swapped, collective_id):
    count, pairs = moved.shape[0], len(swapped)
    hbm = pl.BlockSpec(memory_space=pl.ANY)
    return pl.pallas_call(
        functools.partial(exchange_sum_kernel, pairs),
        out_shape=[
            jax.ShapeDtypeStruct(moved.shape, moved.dtype),
            jax.ShapeDtypeStruct(part.shape[1:], jnp.float32),
        ]
        + [jax.ShapeDtypeStruct(x.shape, x.dtype) for x in swapped],
        in_specs=[hbm] * (2 + pairs),
        out_specs=[hbm, pl.BlockSpec(memory_space=pltpu.VMEM)] + [hbm] * pairs,
        scratch_shapes=[
            pltpu.SemaphoreType.DMA,
            pltpu.SemaphoreType.DMA((count - 1,)),
            pltpu.SemaphoreType.DMA((count - 1,)),
        ]
        + scatter_scratch(False, *part.shape[1:], part.dtype, pairs),
        compiler_params=pltpu.CompilerParams(
            collective_id=collective_id, has_side_effects=True, vmem_limit_bytes=VMEM_LIMIT
        ),
        cost_estimate=pl.CostEstimate(
            flops=0, bytes_accessed=12 * part.size * 2, transcendentals=0
        ),
    )(moved, part, *swapped)


def attend_kernel(
    rows,
    g_attn,
    w_front,
    g_lat,
    expand_head,
    cosines,
    sines,
    normed_out,
    latent_out,
    query_out,
    key_out,
    value_out,
    head_out,
    sum_out,
    log_out,
    keys,
    values,
):
    bf16 = jnp.bfloat16
    size = rows.shape[0]
    scale = (PLAIN_UNITS + ROTARY_UNITS) ** (-0.5)
    step = pl.program_id(0)
    normed, _ = norm_forward(rows[...].astype(jnp.float32), g_attn[...])
    normed = normed.astype(bf16)
    normed_out[...] = normed
    front = contract_last(normed, w_front[...])
    latent, _ = norm_forward(front[:, :LATENT_WIDTH], g_lat[...])
    latent = latent.astype(bf16)
    latent_out[...] = latent
    width = LATENT_WIDTH + ROTARY_UNITS

    def rotated(value):
        return value * cosines[...] + swap_halves(value) * sines[...]

    pairs = matrix_product(latent, expand_head[...])
    key = jnp.concatenate([pairs[:, :PLAIN_UNITS], rotated(front[:, LATENT_WIDTH:width])], axis=1)
    query = jnp.concatenate(
        [front[:, width : width + PLAIN_UNITS], rotated(front[:, width + PLAIN_UNITS :])], axis=1
    ).astype(bf16)
    key = key.astype(bf16)
    value = pairs[:, PLAIN_UNITS:].astype(bf16)
    query_out[...] = query
    key_out[...] = key
    value_out[...] = value
    here = pl.ds(pl.multiple_of(step * size, size), size)
    keys[here, :] = key
    values[here, :] = value
    row = lax.broadcasted_iota(jnp.int32, (size, size), 0)
    column = lax.broadcasted_iota(jnp.int32, (size, size), 1)
    near = jnp.where(column <= row, contract_last(query, key) * scale, -1e30)

    def over(past):
        top = jnp.max(near, axis=1, keepdims=True)
        if past:
            far = contract_last(query, keys[:past, :]) * scale
            top = jnp.maximum(top, jnp.max(far, axis=1, keepdims=True))
        exps = jnp.exp(near - top)
        total = jnp.sum(exps, axis=1, keepdims=True)
        mixed = matrix_product(exps.astype(bf16), value)
        if past:
            exps = jnp.exp(far - top)
            total = total + jnp.sum(exps, axis=1, keepdims=True)
            mixed = mixed + matrix_product(exps.astype(bf16), values[:past, :])
        mixed = mixed / total
        sum_out[...] = mixed
        head_out[...] = mixed.astype(bf16)
        wide = jnp.broadcast_to(top + jnp.log(total), (size, 128))
        log_out[0] = wide.T[:1, :]

    for at in range(keys.shape[0] // size):
        pl.when(step == at)(functools.partial(over, at * size))


def attend(rows, g_attn, w_front, g_lat, expand_head, cosines, sines):
    seq_len, width = rows.shape
    size = 256
    steps = seq_len // size
    units = PLAIN_UNITS + ROTARY_UNITS
    bf16 = jnp.bfloat16

    def by_step(columns):
        return pl.BlockSpec((size, columns), lambda i: (i, 0))

    def fixed(x):
        return pl.BlockSpec(
            x.shape, lambda i: (0, 0), pipeline_mode=pl.Buffered(buffer_count=1)
        )

    return pl.pallas_call(
        attend_kernel,
        grid=(steps,),
        out_shape=[
            jax.ShapeDtypeStruct((seq_len, width), bf16),
            jax.ShapeDtypeStruct((seq_len, LATENT_WIDTH), bf16),
            jax.ShapeDtypeStruct((seq_len, units), bf16),
            jax.ShapeDtypeStruct((seq_len, units), bf16),
            jax.ShapeDtypeStruct((seq_len, VALUE_UNITS), bf16),
            jax.ShapeDtypeStruct((seq_len, VALUE_UNITS), bf16),
            jax.ShapeDtypeStruct((seq_len, VALUE_UNITS), jnp.float32),
            jax.ShapeDtypeStruct((steps, 1, size), jnp.float32),
        ],
        in_specs=[by_step(width)]
        + [fixed(x) for x in (g_attn, w_front, g_lat, expand_head)]
        + [by_step(ROTARY_UNITS)] * 2,
        out_specs=[
            by_step(width),
            by_step(LATENT_WIDTH),
            by_step(units),
            by_step(units),
            by_step(VALUE_UNITS),
            by_step(VALUE_UNITS),
            by_step(VALUE_UNITS),
            pl.BlockSpec((1, 1, size), lambda i: (i, 0, 0)),
        ],
        scratch_shapes=[
            pltpu.VMEM((seq_len, units), bf16),
            pltpu.VMEM((seq_len, VALUE_UNITS), bf16),
        ],
        compiler_params=pltpu.CompilerParams(vmem_limit_bytes=VMEM_LIMIT),
        cost_estimate=pl.CostEstimate(
            flops=2 * seq_len * (width * 768 + seq_len * units),
            bytes_accessed=3 * rows.size * 2,
            transcendentals=seq_len * seq_len // 2,
        ),
    )(rows, g_attn, w_front, g_lat, expand_head, cosines, sines)


def attend_back_kernel(
    query,
    key,
    value,
    d_head,
    head_sum,
    logs,
    expand_head,
    cosines,
    sines,
    d_query_out,
    d_pairs_out,
    d_keys_out,
    d_key,
    d_value,
    key_turned,
):
    bf16 = jnp.bfloat16
    size = query.shape[0]
    seq_len = key.shape[0]
    scale = (PLAIN_UNITS + ROTARY_UNITS) ** (-0.5)
    step = pl.program_id(0)

    @pl.when(step == 0)
    def _():
        d_key[...] = jnp.zeros_like(d_key)
        d_value[...] = jnp.zeros_like(d_value)
        for at in range(0, seq_len, size):
            part = key[at : at + size, :].astype(jnp.float32)
            key_turned[:, at : at + size] = part.T.astype(bf16)

    q, d_out = query[...], d_head[...]
    product = d_out.astype(jnp.float32) * head_sum[...]
    delta = jnp.sum(product.T, axis=0, keepdims=True)
    log_row = logs[0]
    row = lax.broadcasted_iota(jnp.int32, (size, size), 0)
    column = lax.broadcasted_iota(jnp.int32, (size, size), 1)

    def grads_of(at, mask):
        there = slice(at, at + size)
        scores = contract_last(key[there, :], q) * scale
        if mask:
            scores = jnp.where(row <= column, scores, -1e30)
        probs = jnp.exp(scores - log_row)
        d_probs = contract_last(value[there, :], d_out)
        d_scores = (probs * (d_probs - delta) * scale).astype(bf16)
        d_key[there, :] += matrix_product(d_scores, q)
        d_value[there, :] += matrix_product(probs.astype(bf16), d_out)
        return matrix_product(key_turned[:, there], d_scores)

    def over(past):
        total = grads_of(past, True)
        for at in range(0, past, size):
            total = total + grads_of(at, False)
        d_query = total.T
        d_rope = d_query[:, PLAIN_UNITS:]
        d_rope = d_rope * cosines[...] - swap_halves(d_rope) * sines[...]
        d_query_out[...] = jnp.concatenate([d_query[:, :PLAIN_UNITS], d_rope], axis=1).astype(bf16)

    for at in range(seq_len // size):
        pl.when(step == at)(functools.partial(over, at * size))

    @pl.when(step == seq_len // size - 1)
    def _():
        for at in range(0, seq_len, size):
            there = slice(at, at + size)
            d_pairs = jnp.concatenate(
                [d_key[there, :PLAIN_UNITS], d_value[there, :]], axis=1
            ).astype(bf16)
            d_pairs_out[there, :] = d_pairs
            d_keys_out[there, :LATENT_WIDTH] = contract_last(d_pairs, expand_head[...]).astype(bf16)
            tail = jnp.concatenate(
                [d_key[there, PLAIN_UNITS:], jnp.zeros((size, ROTARY_UNITS), jnp.float32)], axis=1
            )
            d_keys_out[there, LATENT_WIDTH:] = tail.astype(bf16)


def attend_back(query, key, value, d_head, head_sum, logs, expand_head, cosines, sines):
    seq_len, units = query.shape
    steps, _, size = logs.shape
    bf16 = jnp.bfloat16
    keys_width = LATENT_WIDTH + 2 * ROTARY_UNITS

    def by_step(columns):
        return pl.BlockSpec((size, columns), lambda i: (i, 0))

    def fixed(shape):
        return pl.BlockSpec(shape, lambda i: (0, 0), pipeline_mode=pl.Buffered(buffer_count=1))

    return pl.pallas_call(
        attend_back_kernel,
        grid=(steps,),
        out_shape=[
            jax.ShapeDtypeStruct((seq_len, units), bf16),
            jax.ShapeDtypeStruct((seq_len, PLAIN_UNITS + VALUE_UNITS), bf16),
            jax.ShapeDtypeStruct((seq_len, keys_width), bf16),
        ],
        in_specs=[
            by_step(units),
            fixed(key.shape),
            fixed(value.shape),
            by_step(VALUE_UNITS),
            by_step(VALUE_UNITS),
            pl.BlockSpec((1, 1, size), lambda i: (i, 0, 0)),
            fixed(expand_head.shape),
            by_step(ROTARY_UNITS),
            by_step(ROTARY_UNITS),
        ],
        out_specs=[
            by_step(units),
            fixed((seq_len, PLAIN_UNITS + VALUE_UNITS)),
            fixed((seq_len, keys_width)),
        ],
        scratch_shapes=[
            pltpu.VMEM((seq_len, units), jnp.float32),
            pltpu.VMEM((seq_len, VALUE_UNITS), jnp.float32),
            pltpu.VMEM((units, seq_len), bf16),
        ],
        compiler_params=pltpu.CompilerParams(vmem_limit_bytes=VMEM_LIMIT),
        cost_estimate=pl.CostEstimate(
            flops=5 * seq_len * seq_len * units,
            bytes_accessed=8 * seq_len * units * 2,
            transcendentals=seq_len * seq_len // 2,
        ),
    )(query, key, value, d_head, head_sum, logs, expand_head, cosines, sines)


def finish_kernel(shard, query, expand, out_rows, query_out, expand_out, out_out):
    heads, units, width = query.shape
    query_out[...] = query[...].reshape(heads * units, width).astype(jnp.float32).T
    for at in range(heads):
        columns = expand.shape[2]
        expand_out[:, at * columns : (at + 1) * columns] = expand[at].astype(jnp.float32)
    out_out[...] = out_rows[0].astype(jnp.float32)


def finish(shard, query, expand, out_rows):
    heads, units, width = query.shape
    _, latents, columns = expand.shape
    _, rows, model = out_rows.shape
    steps = heads // 2
    return pl.pallas_call(
        finish_kernel,
        out_shape=[
            jax.ShapeDtypeStruct((width, heads * units), jnp.float32),
            jax.ShapeDtypeStruct((latents, heads * columns), jnp.float32),
            jax.ShapeDtypeStruct((steps * rows, model), jnp.float32),
        ],
        grid_spec=pltpu.PrefetchScalarGridSpec(
            num_scalar_prefetch=1,
            grid=(steps,),
            in_specs=[
                pl.BlockSpec((2, units, width), lambda i, shard: (i, 0, 0)),
                pl.BlockSpec((2, latents, columns), lambda i, shard: (i, 0, 0)),
                pl.BlockSpec((1, rows, model), lambda i, shard: (shard[0] * steps + i, 0, 0)),
            ],
            out_specs=[
                pl.BlockSpec((width, 2 * units), lambda i, shard: (0, i)),
                pl.BlockSpec((latents, 2 * columns), lambda i, shard: (0, i)),
                pl.BlockSpec((rows, model), lambda i, shard: (i, 0)),
            ],
        ),
        compiler_params=pltpu.CompilerParams(vmem_limit_bytes=VMEM_LIMIT),
        cost_estimate=pl.CostEstimate(
            flops=0, bytes_accessed=6 * heads * units * width, transcendentals=0
        ),
    )(shard.reshape(1), query, expand, out_rows)


def token_gather(rows):
    return lax.all_gather(rows, ("fsdp", "expert"), axis=0, tiled=True)


def split_body(
    tokens,
    routes,
    cotangent,
    attn_gain,
    w_query,
    latent_weight,
    latent_norm_gain,
    expand_weight,
    w_out,
    ffn_gain,
    w_router,
    shared_gate,
    shared_up,
    shared_down,
    expert_gate,
    expert_up,
    expert_down,
):
    rows = tokens.shape[1]
    experts = lax.axis_size("expert")
    shards = lax.axis_size("fsdp")
    position = lax.axis_index("expert")
    blocks = experts * shards
    seq_len = rows * experts
    capacity = shards * ((rows * TOPK * 4 + experts * 3 * shards - 1) // (experts * 3 * shards))
    head_units = PLAIN_UNITS + ROTARY_UNITS
    pair_units = PLAIN_UNITS + VALUE_UNITS
    feature_width = LATENT_WIDTH + ROTARY_UNITS
    scale = head_units ** (-0.5)

    shard = lax.axis_index("fsdp")
    first = shard == 0

    query_cols = lax.dynamic_slice_in_dim(w_query, position * head_units, head_units, 1)
    expand_cols = lax.dynamic_slice_in_dim(expand_weight, position * pair_units, pair_units, 1)
    owners = experts // shards
    lat_row = jnp.pad(latent_norm_gain, (0, w_query.shape[0] - latent_norm_gain.shape[0]))
    packed = jnp.concatenate(
        [latent_weight.T, query_cols.T, w_router.T, attn_gain[None], ffn_gain[None], lat_row[None]],
        axis=0,
    )
    packed = jnp.pad(packed, ((0, -packed.shape[0] % 32), (0, 0)))
    seq_rows, other_packed, other_expand = gather_rows(
        [tokens[0]], False, 0, swapped=[packed, expand_cols]
    )

    def whole(own, other, axis):
        return jnp.concatenate(
            [jnp.where(first, own, other), jnp.where(first, other, own)], axis=axis
        )

    lat_half = latent_norm_gain.shape[0]
    at = feature_width + head_units
    packed_rows = whole(packed, other_packed, 1)
    expand_head = whole(expand_cols, other_expand, 0)
    w_front = packed_rows[:at]
    w_latent = packed_rows[:feature_width]
    router_rows = packed_rows[at:]
    wrout = packed_rows[at : at + experts]
    g_attn = packed_rows[at + experts].astype(jnp.float32)
    g_ffn = packed_rows[at + experts + 1].astype(jnp.float32)
    lat_row = packed_rows[at + experts + 2]
    g_lat = jnp.concatenate(
        [lat_row[:lat_half], lat_row[w_query.shape[0] : w_query.shape[0] + lat_half]]
    ).astype(jnp.float32)
    units = shared_down.shape[0]

    core = lax.rem(position, CORES)

    def by_cores(weight):
        size = weight.shape[0] // CORES
        own = lax.dynamic_slice_in_dim(weight, core * size, size, 0)
        own = lax.all_gather(own, "fsdp", axis=0, tiled=True)
        swap = [(index, index ^ 1) for index in range(experts)]
        return own, lax.ppermute(own, "expert", swap)

    def core_columns(value, which):
        size = value.shape[1] // (CORES * shards)
        parts = [
            lax.dynamic_slice_in_dim(value, (at * CORES + which) * size, size, 1)
            for at in range(shards)
        ]
        return jnp.concatenate(parts, axis=1)

    def in_order(own, other):
        lower, upper = jnp.where(core == 0, own, other), jnp.where(core == 0, other, own)
        size = own.shape[1] // shards
        parts = []
        for at in range(shards):
            parts += [lower[:, at * size : (at + 1) * size], upper[:, at * size : (at + 1) * size]]
        return jnp.concatenate(parts, axis=1)

    out_own, out_other = by_cores(w_out)
    grad_rows = cotangent[0]
    grad_out = grad_rows.astype(jnp.float32)
    own_routes = jnp.pad(routes[0], ((0, 0), (0, 128 - TOPK)), constant_values=-1)
    grad_rows = jnp.concatenate([grad_rows, own_routes.astype(jnp.bfloat16)], axis=1)
    seq_rows, grad_rows, shared_gate, shared_up = lax.optimization_barrier(
        (seq_rows, grad_rows, shared_gate, shared_up)
    )
    def to_columns(weight):
        parts = weight.reshape(weight.shape[0], blocks, units).transpose(1, 0, 2)
        return lax.all_to_all(
            parts, ("expert", "fsdp"), split_axis=0, concat_axis=0, tiled=True
        ).reshape(-1, units)

    sh_cols = to_columns(jnp.concatenate([shared_gate, shared_up], axis=0)).reshape(
        blocks, 2, shared_gate.shape[0], units
    )
    lanes = -(-units // 128) * 128
    sh_cols = jnp.pad(sh_cols, ((0, 0), (0, 0), (0, 0), (0, lanes - units)))
    shared_in = sh_cols.transpose(0, 2, 1, 3).reshape(MODEL_WIDTH, 2 * lanes)
    shared_out = jnp.pad(shared_down, ((0, lanes - units), (0, 0)))
    all_grads = token_gather(grad_rows)

    x_in = tokens[0].astype(jnp.float32)
    normed, inv_attn = norm_forward(x_in, g_attn)
    normed_in = normed.astype(jnp.bfloat16)
    half_units = ROTARY_UNITS // 2
    freqs = 10000.0 ** (-np.arange(half_units) * (2.0 / ROTARY_UNITS))
    angles = np.arange(seq_len)[:, None] * freqs[None, :]
    cosine_table = jnp.asarray(np.cos(angles), jnp.float32)
    sine_table = jnp.asarray(np.sin(angles), jnp.float32)
    cosines = jnp.asarray(np.concatenate([np.cos(angles)] * 2, axis=1), jnp.float32)
    sines = jnp.asarray(np.concatenate([-np.sin(angles), np.sin(angles)], axis=1), jnp.float32)
    (
        seq_normed,
        latent_rows,
        query,
        key,
        value,
        head_rows,
        head_sum,
        logs,
    ) = attend(
        seq_rows.reshape(seq_len, MODEL_WIDTH),
        g_attn[None],
        w_front,
        g_lat[None],
        expand_head,
        cosines,
        sines,
    )
    head_rows, shared_in = lax.optimization_barrier((head_rows, shared_in))
    heads = exchange(head_rows.reshape(experts, rows, VALUE_UNITS), 1)
    heads = heads.transpose(1, 0, 2).reshape(rows, experts * VALUE_UNITS)
    hidden = x_in + matrix_product(core_columns(heads, core), out_own)
    hidden = hidden + matrix_product(core_columns(heads, 1 - core), out_other)
    normed2, inv_ffn = norm_forward(hidden, g_ffn)
    normed_ffn = normed2.astype(jnp.bfloat16)
    router = jax.nn.softmax(outer_product(normed_ffn, wrout), axis=-1)

    (all_normed,) = gather_rows([normed_ffn], True, 2)
    w_query, all_normed = lax.optimization_barrier((w_query, all_normed))
    query_own, query_other = by_cores(w_query)
    (
        out_part,
        d_part,
        ex_rows,
        ex_grads,
        scaled_act,
        d_pre_gate,
        d_pre_up,
        g_shared_in,
        g_shared_out,
    ) = expert_phase(
        all_normed,
        all_grads.reshape(blocks, rows, -1),
        router_rows,
        expert_gate[0].T,
        expert_up[0].T,
        expert_down[0],
        shared_in,
        shared_out,
        capacity,
    )
    d_back, g_down, g_gate, g_up = scatter_and_products(
        d_part, [scaled_act, d_pre_gate, d_pre_up], [ex_grads, ex_rows, ex_rows], 3
    )
    d_normed_ffn = d_back[:, :MODEL_WIDTH]
    d_router = d_back[:, MODEL_WIDTH : MODEL_WIDTH + experts]

    d_logits = (router * (d_router - jnp.sum(router * d_router, axis=1, keepdims=True))).astype(
        jnp.bfloat16
    )
    g_router = inner(d_logits, normed_ffn)
    d_normed_ffn = d_normed_ffn + matrix_product(d_logits, wrout)
    d_hidden_norm, g_ffn_grad = norm_backward(hidden, inv_ffn, g_ffn, d_normed_ffn)
    d_hidden = grad_out + d_hidden_norm
    d_attn = d_hidden.astype(jnp.bfloat16)

    d_heads = in_order(outer_product(d_attn, out_own), outer_product(d_attn, out_other))
    d_heads = d_heads.astype(jnp.bfloat16)
    d_heads = d_heads.reshape(rows, experts, VALUE_UNITS).transpose(1, 0, 2)
    d_head = exchange(d_heads, 4).reshape(seq_len, VALUE_UNITS)
    seq_d_attn = lax.all_gather(d_attn, "expert", axis=0, tiled=True)
    d_query_full, d_pairs, d_keys = attend_back(
        query, key, value, d_head, head_sum, logs, expand_head, cosines, sines
    )
    g_out_head = inner(head_rows, seq_d_attn)
    g_expand_head = inner(latent_rows, d_pairs)
    g_query_head = inner(d_query_full, seq_normed).astype(jnp.bfloat16)
    g_expand_head = g_expand_head.astype(jnp.bfloat16)
    g_out_head = g_out_head.astype(jnp.bfloat16)

    def half_of(whole, which, axis):
        size = whole.shape[axis] // shards
        return lax.dynamic_slice_in_dim(whole, which * size, size, axis)

    own_d_query, d_sums, other_query, other_expand, other_out_grad = exchange_and_sum(
        d_query_full.reshape(experts, rows, head_units),
        d_keys.reshape(experts, rows, -1),
        [
            half_of(g_query_head, 1 - shard, 1),
            half_of(g_expand_head, 1 - shard, 0),
            g_out_head,
        ],
        5,
    )
    own_d_query = own_d_query.transpose(1, 0, 2).reshape(rows, experts * head_units)
    key_gradient = d_sums[:, :feature_width]
    d_normed_in = in_order(
        outer_product(own_d_query, query_own), outer_product(own_d_query, query_other)
    )

    def summed(own, other):
        return (own.astype(jnp.float32) + other.astype(jnp.float32)).astype(jnp.bfloat16)

    own_query = summed(half_of(g_query_head, shard, 1), other_query)
    own_expand = summed(half_of(g_expand_head, shard, 0), other_expand)
    own_out = summed(g_out_head, other_out_grad)
    own_latent = outer_product(normed_in, w_latent[:LATENT_WIDTH])
    own_cosine = lax.dynamic_slice_in_dim(cosine_table, position * rows, rows, 0)
    own_sine = lax.dynamic_slice_in_dim(sine_table, position * rows, rows, 0)
    inv_lat = lax.rsqrt(jnp.mean(own_latent * own_latent, axis=-1, keepdims=True) + EPS)
    d_compact, g_lat_grad = norm_backward(
        own_latent, inv_lat, g_lat, key_gradient[:, :LATENT_WIDTH]
    )
    d_rope = reverse_rotary(key_gradient[:, LATENT_WIDTH:], own_cosine, own_sine)
    d_latent_full = jnp.concatenate([d_compact, d_rope], axis=-1).astype(jnp.bfloat16)
    g_latent = inner(d_latent_full, normed_in)
    d_normed_in = d_normed_in + matrix_product(d_latent_full, w_latent)
    d_norm_in, g_attn_grad = norm_backward(x_in, inv_attn, g_attn, d_normed_in)
    d_tokens = (d_hidden + d_norm_in).astype(jnp.bfloat16)

    half = MODEL_WIDTH // blocks
    cols = lax.all_to_all(
        g_shared_in.reshape(blocks, half, 2 * lanes),
        ("expert", "fsdp"),
        split_axis=0,
        concat_axis=0,
        tiled=True,
    )
    cols = cols.transpose(1, 0, 2).astype(jnp.float32)
    r_sgate = cols[:, :, :units].reshape(half, blocks * units)
    r_sup = cols[:, :, lanes : lanes + units].reshape(half, blocks * units)
    g_sdown = g_shared_out[:units]
    model_half = MODEL_WIDTH // shards
    small_rows = jnp.concatenate([g_latent, g_router, g_attn_grad[None], g_ffn_grad[None]], axis=0)
    used = small_rows.shape[0]
    share = 2 * 32 * (-(-(used + 1) // (2 * 32 * experts)))

    def rows_for(which):
        here = small_rows[:, which * model_half : (which + 1) * model_half]
        lat = jnp.pad(
            g_lat_grad[which * lat_half : (which + 1) * lat_half], (0, model_half - lat_half)
        )
        full = jnp.concatenate([here, lat[None]], axis=0).astype(jnp.bfloat16)
        full = jnp.pad(full, ((0, experts * share - used - 1), (0, 0)))
        return full.reshape(experts, share, model_half)

    small_part = jnp.concatenate([rows_for(which) for which in range(shards)], axis=0)
    r_query, r_expand, r_out, small_sum, out_sum = gather_and_scatter(
        [own_query, own_expand, own_out], [small_part, out_part], 6, gated=(2,)
    )
    output = hidden + out_sum
    (small_all,) = gather_rows([small_sum.astype(jnp.bfloat16)], False, 7)
    r_query, r_expand, r_out = finish(shard, r_query, r_expand, r_out)
    small_all = small_all.reshape(experts * share, model_half).astype(jnp.float32)
    return (
        output.astype(jnp.bfloat16)[None],
        d_tokens[None],
        small_all[feature_width + experts],
        r_query,
        small_all[:feature_width].T,
        small_all[feature_width + experts + 2, :lat_half],
        r_expand,
        r_out,
        small_all[feature_width + experts + 1],
        small_all[feature_width : feature_width + experts].T,
        r_sgate,
        r_sup,
        g_sdown,
        g_gate.T[None],
        g_up.T[None],
        g_down[None],
    )


def solution(mesh):
    shape = (mesh.shape["expert"], mesh.shape["fsdp"])
    split = shape == (LINE * SQUARE * CORES, SQUARE) and shape[0] == HEAD_COUNT
    return jax.shard_map(
        split_body if split else body,
        mesh=mesh,
        in_specs=(
            P("fsdp", "expert", None),
            P("fsdp", "expert", None),
            P("fsdp", "expert", None),
            P("fsdp"),
            P("fsdp", None),
            P("fsdp", None),
            P("fsdp"),
            P("fsdp", None),
            P("fsdp", None),
            P("fsdp"),
            P("fsdp", None),
            P(("expert", "fsdp"), None),
            P(("expert", "fsdp"), None),
            P(("expert", "fsdp"), None),
            P("expert", None, "fsdp"),
            P("expert", None, "fsdp"),
            P("expert", "fsdp", None),
        ),
        out_specs=(
            P("fsdp", "expert", None),
            P("fsdp", "expert", None),
            P("fsdp"),
            P("fsdp", None),
            P("fsdp", None),
            P("fsdp"),
            P("fsdp", None),
            P("fsdp", None),
            P("fsdp"),
            P("fsdp", None),
            P(("expert", "fsdp"), None),
            P(("expert", "fsdp"), None),
            P(("expert", "fsdp"), None),
            P("expert", None, "fsdp"),
            P("expert", None, "fsdp"),
            P("expert", "fsdp", None),
        ),
        check_vma=False,
    )
```

```python
import functools

import jax
import jax.numpy as jnp
import numpy as np
from jax import lax
from jax.experimental import pallas as pl
from jax.experimental.pallas import tpu as pltpu
from jax.sharding import PartitionSpec as P

MODEL_WIDTH = 2048
HEAD_COUNT = 16
PLAIN_UNITS = 128
ROTARY_UNITS = 64
VALUE_UNITS = 128
LATENT_WIDTH = 512
TOPK = 6


EPS = 1e-06


def matrix_product(left, right):
    return jnp.dot(left, right, preferred_element_type=jnp.float32)


def inner(left, right):
    return lax.dot_general(
        left, right, (((0,), (0,)), ((), ())), preferred_element_type=jnp.float32
    )


def outer_product(left, right):
    return lax.dot_general(
        left, right, (((1,), (1,)), ((), ())), preferred_element_type=jnp.float32
    )


def norm_forward(value, gain):
    inverse = lax.rsqrt(jnp.mean(value * value, axis=-1, keepdims=True) + EPS)
    return (value * inverse * gain, inverse)


def norm_backward(value, inverse, gain, grad):
    unit = value * inverse
    scaled = grad * gain
    d_value = inverse * (scaled - unit * jnp.mean(scaled * unit, axis=-1, keepdims=True))
    return (d_value, jnp.sum(grad * unit, axis=0))


def rope_tables(positions):
    half = ROTARY_UNITS // 2
    freqs = 10000.0 ** (-jnp.arange(half, dtype=jnp.float32) * (2.0 / ROTARY_UNITS))
    angles = positions.astype(jnp.float32)[:, None] * freqs[None, :]
    return (jnp.cos(angles), jnp.sin(angles))


def apply_rotary(value, cosine_table, sine_table):
    half = ROTARY_UNITS // 2
    first = value[..., :half]
    second = value[..., half:]
    return jnp.concatenate(
        [first * cosine_table - second * sine_table, first * sine_table + second * cosine_table],
        axis=-1,
    )


def reverse_rotary(grad, cosine_table, sine_table):
    half = ROTARY_UNITS // 2
    first = grad[..., :half]
    second = grad[..., half:]
    return jnp.concatenate(
        [first * cosine_table + second * sine_table, second * cosine_table - first * sine_table],
        axis=-1,
    )


def silu_parts(value):
    sigma = jax.nn.sigmoid(value)
    return (value * sigma, sigma * (1.0 + value * (1.0 - sigma)))


def body(
    tokens,
    routes,
    cotangent,
    attn_gain,
    w_query,
    latent_weight,
    latent_norm_gain,
    expand_weight,
    w_out,
    ffn_gain,
    w_router,
    shared_gate,
    shared_up,
    shared_down,
    expert_gate,
    expert_up,
    expert_down,
):
    device_local = tokens.shape[1]
    experts = lax.axis_size("expert")
    shards = lax.axis_size("fsdp")
    position = lax.axis_index("expert")
    capacity = shards * (
        (device_local * TOPK * 4 + experts * 3 * shards - 1) // (experts * 3 * shards)
    )
    seq_len = device_local * experts
    feature_width = LATENT_WIDTH + ROTARY_UNITS
    scale = (PLAIN_UNITS + ROTARY_UNITS) ** (-0.5)
    attention_gain_grad, wq, wlat, g_lat, expand_matrix, wout, g_ffn, wrout = (
        lax.all_gather(attn_gain, "fsdp", axis=0, tiled=True),
        lax.all_gather(w_query, "fsdp", axis=0, tiled=True),
        lax.all_gather(latent_weight, "fsdp", axis=0, tiled=True),
        lax.all_gather(latent_norm_gain, "fsdp", axis=0, tiled=True),
        lax.all_gather(expand_weight, "fsdp", axis=0, tiled=True),
        lax.all_gather(w_out, "fsdp", axis=0, tiled=True),
        lax.all_gather(ffn_gain, "fsdp", axis=0, tiled=True),
        lax.all_gather(w_router, "fsdp", axis=0, tiled=True),
    )
    sgate, sup, sdown = (
        lax.all_gather(shared_gate, ("expert", "fsdp"), axis=0, tiled=True),
        lax.all_gather(shared_up, ("expert", "fsdp"), axis=0, tiled=True),
        lax.all_gather(shared_down, ("expert", "fsdp"), axis=0, tiled=True),
    )
    attention_gain_grad = attention_gain_grad.astype(jnp.float32)
    g_lat = g_lat.astype(jnp.float32)
    g_ffn = g_ffn.astype(jnp.float32)
    x_in = tokens[0].astype(jnp.float32)
    grad_out = cotangent[0].astype(jnp.float32)
    positions = position * device_local + jnp.arange(device_local, dtype=jnp.int32)
    cosine_table, sine_table = rope_tables(positions)
    normed, inv_attn = norm_forward(x_in, attention_gain_grad)
    normed_in = normed.astype(jnp.bfloat16)
    query_full = matrix_product(normed_in, wq).reshape(
        device_local, HEAD_COUNT, PLAIN_UNITS + ROTARY_UNITS
    )
    query_nope = query_full[:, :, :PLAIN_UNITS].astype(jnp.bfloat16)
    expanded_latent = expand_matrix.reshape(LATENT_WIDTH, HEAD_COUNT, PLAIN_UNITS + VALUE_UNITS)
    key_part = expanded_latent[:, :, :PLAIN_UNITS]
    value_part = expanded_latent[:, :, PLAIN_UNITS:]
    query_latent = jnp.einsum(
        "thd,chd->thc", query_nope, key_part, preferred_element_type=jnp.float32
    )
    query_rope = apply_rotary(
        query_full[:, :, PLAIN_UNITS:], cosine_table[:, None, :], sine_table[:, None, :]
    )
    token_rows = device_local * HEAD_COUNT
    query = (
        jnp.concatenate([query_latent, query_rope], axis=-1)
        .astype(jnp.bfloat16)
        .reshape(token_rows, feature_width)
    )
    latent_complete = matrix_product(normed_in, wlat)
    packed_rows = latent_complete[:, :LATENT_WIDTH]
    latent_state, inv_lat = norm_forward(packed_rows, g_lat)
    rotary_key = apply_rotary(latent_complete[:, LATENT_WIDTH:], cosine_table, sine_table)
    key = jnp.concatenate([latent_state, rotary_key], axis=-1).astype(jnp.bfloat16)
    keys_all = lax.all_gather(key, "expert", axis=0, tiled=True)
    block = min(512, seq_len)
    token_tally = (position * device_local + device_local + block - 1) // block
    q_pos = position * device_local + jnp.arange(token_rows, dtype=jnp.int32) // HEAD_COUNT

    def scores_of(index):
        key_rows = lax.dynamic_slice_in_dim(keys_all, index * block, block, 0)
        raw = outer_product(query, key_rows)
        k_pos = index * block + jnp.arange(block, dtype=jnp.int32)
        valid = k_pos[None, :] <= q_pos[:, None]
        return (jnp.where(valid, raw * scale, -1e30), key_rows)

    def stats_step(index, carry):
        top, total = carry
        scores, unused = scores_of(index)
        new_top = jnp.maximum(top, jnp.max(scores, axis=1))
        total = total * jnp.exp(top - new_top) + jnp.sum(jnp.exp(scores - new_top[:, None]), axis=1)
        return (new_top, total)

    top, total = lax.fori_loop(
        0,
        token_tally,
        stats_step,
        (jnp.full((token_rows,), -1e30, jnp.float32), jnp.zeros((token_rows,), jnp.float32)),
    )
    log_total = top + jnp.log(total)

    def mixing_update(index, running_total):
        scores, key_rows = scores_of(index)
        weight_arrays = jnp.exp(scores - log_total[:, None]).astype(jnp.bfloat16)
        return running_total + matrix_product(weight_arrays, key_rows[:, :LATENT_WIDTH])

    mixed_output_sum = lax.fori_loop(
        0, token_tally, mixing_update, jnp.zeros((token_rows, LATENT_WIDTH), jnp.float32)
    )
    mixed_output = mixed_output_sum.astype(jnp.bfloat16).reshape(
        device_local, HEAD_COUNT, LATENT_WIDTH
    )
    heads = jnp.einsum("thc,chv->thv", mixed_output, value_part, preferred_element_type=jnp.float32)
    heads = heads.reshape(device_local, HEAD_COUNT * VALUE_UNITS).astype(jnp.bfloat16)
    hidden = x_in + matrix_product(heads, wout)
    normed2, inv_ffn = norm_forward(hidden, g_ffn)
    normed_ffn = normed2.astype(jnp.bfloat16)
    logits = matrix_product(normed_ffn, wrout)
    router = jax.nn.softmax(logits, axis=-1)
    own_routes = routes[0]
    names = jnp.arange(experts, dtype=jnp.int32)
    chosen = (own_routes[:, :, None] == names[None, None, :]).astype(jnp.float32)
    gates = jnp.sum(chosen * router[:, None, :], axis=-1)
    hits = (own_routes.reshape(device_local * TOPK)[:, None] == names[None, :]).astype(jnp.int32)
    slot = jnp.sum((jnp.cumsum(hits, axis=0) - hits) * hits, axis=1)
    place = own_routes.reshape(device_local * TOPK) * capacity + slot
    token_of = jnp.arange(device_local * TOPK, dtype=jnp.int32) // TOPK
    table = jnp.full((experts * capacity,), device_local, jnp.int32).at[place].set(token_of)
    padded = jnp.concatenate([normed_ffn, jnp.zeros((1, MODEL_WIDTH), jnp.bfloat16)], axis=0)
    buffer = padded[table].reshape(experts, capacity, MODEL_WIDTH)
    w_g, w_u, w_d = (expert_gate[0], expert_up[0], expert_down[0])

    def spread(values):
        return jnp.broadcast_to(values[:, None], (experts, shards, capacity, MODEL_WIDTH)).reshape(
            experts * shards, capacity, MODEL_WIDTH
        )

    def collect(back):
        return jnp.sum(back.reshape(experts, shards, capacity, MODEL_WIDTH), axis=1).reshape(
            experts * capacity, MODEL_WIDTH
        )

    received = lax.all_to_all(
        spread(buffer), ("expert", "fsdp"), split_axis=0, concat_axis=0, tiled=True
    )
    ex_rows = received.reshape(-1, MODEL_WIDTH)
    pre_gate = matrix_product(ex_rows, w_g)
    pre_up = matrix_product(ex_rows, w_u)
    act_gate, slope = silu_parts(pre_gate)
    ex_act = (act_gate * pre_up).astype(jnp.bfloat16)
    ex_out = matrix_product(ex_act, w_d).reshape(received.shape)
    returned = lax.all_to_all(
        ex_out.astype(jnp.bfloat16), ("expert", "fsdp"), split_axis=0, concat_axis=0, tiled=True
    ).astype(ex_out.dtype)
    results = collect(returned)
    picked = results[place].reshape(device_local, TOPK, MODEL_WIDTH)
    routed = jnp.sum(gates[:, :, None] * picked, axis=1)
    sh_gate = matrix_product(normed_ffn, sgate)
    sh_up = matrix_product(normed_ffn, sup)
    sh_silu, sh_slope = silu_parts(sh_gate)
    sh_act = (sh_silu * sh_up).astype(jnp.bfloat16)
    shared = matrix_product(sh_act, sdown)
    output = hidden + routed + shared
    d_shared = grad_out.astype(jnp.bfloat16)
    shared_down_gradient = inner(sh_act, d_shared)
    d_sh_act = outer_product(d_shared, sdown)
    d_sh_gate = (d_sh_act * sh_up * sh_slope).astype(jnp.bfloat16)
    d_sh_up = (d_sh_act * sh_silu).astype(jnp.bfloat16)
    shared_gate_gradient = inner(normed_ffn, d_sh_gate)
    shared_up_gradient = inner(normed_ffn, d_sh_up)
    d_normed_ffn = outer_product(d_sh_gate, sgate) + outer_product(d_sh_up, sup)
    d_picked = (
        (gates[:, :, None] * grad_out[:, None, :])
        .astype(jnp.bfloat16)
        .reshape(device_local * TOPK, MODEL_WIDTH)
    )
    d_gates = jnp.sum(picked * grad_out[:, None, :], axis=2)
    d_buffer = (
        jnp.zeros((experts * capacity, MODEL_WIDTH), jnp.bfloat16)
        .at[place]
        .set(d_picked)
        .reshape(experts, capacity, MODEL_WIDTH)
    )
    d_received = lax.all_to_all(
        spread(d_buffer), ("expert", "fsdp"), split_axis=0, concat_axis=0, tiled=True
    )
    d_rows = d_received.reshape(-1, MODEL_WIDTH)
    d_act = outer_product(d_rows, w_d)
    g_down = inner(ex_act, d_rows)
    d_pre_gate = (d_act * pre_up * slope).astype(jnp.bfloat16)
    d_pre_up = (d_act * act_gate).astype(jnp.bfloat16)
    g_gate = inner(ex_rows, d_pre_gate)
    g_up = inner(ex_rows, d_pre_up)
    d_ex_rows = (outer_product(d_pre_gate, w_g) + outer_product(d_pre_up, w_u)).reshape(
        received.shape
    )
    d_returned = lax.all_to_all(
        d_ex_rows.astype(jnp.bfloat16), ("expert", "fsdp"), split_axis=0, concat_axis=0, tiled=True
    ).astype(d_ex_rows.dtype)
    d_results = collect(d_returned)
    d_normed_ffn = d_normed_ffn + jnp.sum(
        d_results[place].reshape(device_local, TOPK, MODEL_WIDTH), axis=1
    )
    d_router = jnp.sum(chosen * d_gates[:, :, None], axis=1)
    d_logits = (router * (d_router - jnp.sum(router * d_router, axis=1, keepdims=True))).astype(
        jnp.bfloat16
    )
    router_weight_gradient = inner(normed_ffn, d_logits)
    d_normed_ffn = d_normed_ffn + outer_product(d_logits, wrout)
    d_hidden_norm, g_ffn_grad = norm_backward(hidden, inv_ffn, g_ffn, d_normed_ffn)
    d_hidden = grad_out + d_hidden_norm
    d_attn = d_hidden.astype(jnp.bfloat16)
    output_weight_gradient = inner(heads, d_attn)
    d_heads = (
        outer_product(d_attn, wout)
        .astype(jnp.bfloat16)
        .reshape(device_local, HEAD_COUNT, VALUE_UNITS)
    )
    value_weight_gradient = jnp.einsum(
        "thc,thv->chv", mixed_output, d_heads, preferred_element_type=jnp.float32
    )
    mixed_gradient = jnp.einsum(
        "thv,chv->thc", d_heads, value_part, preferred_element_type=jnp.float32
    )
    mixed_gradient = mixed_gradient.astype(jnp.bfloat16).reshape(token_rows, LATENT_WIDTH)
    delta = jnp.sum(mixed_gradient.astype(jnp.float32) * mixed_output_sum, axis=1)

    def back_step(index, carry):
        d_query_acc, d_keys_acc = carry
        scores, key_rows = scores_of(index)
        weight_arrays = jnp.exp(scores - log_total[:, None])
        weight_gradients = outer_product(mixed_gradient, key_rows[:, :LATENT_WIDTH])
        d_scores = (weight_arrays * (weight_gradients - delta[:, None]) * scale).astype(
            jnp.bfloat16
        )
        d_query_acc = d_query_acc + matrix_product(d_scores, key_rows)
        d_values = inner(weight_arrays.astype(jnp.bfloat16), mixed_gradient)
        d_block = inner(d_scores, query) + jnp.concatenate(
            [d_values, jnp.zeros((block, ROTARY_UNITS), jnp.float32)], axis=1
        )
        previous = lax.dynamic_slice_in_dim(d_keys_acc, index * block, block, 0)
        return (
            d_query_acc,
            lax.dynamic_update_slice_in_dim(d_keys_acc, previous + d_block, index * block, 0),
        )

    d_query, d_keys = lax.fori_loop(
        0,
        token_tally,
        back_step,
        (
            jnp.zeros((token_rows, feature_width), jnp.float32),
            jnp.zeros((seq_len, feature_width), jnp.float32),
        ),
    )
    key_gradient = lax.psum_scatter(
        d_keys.astype(jnp.bfloat16), "expert", scatter_dimension=0, tiled=True
    )
    query_up_gradient = d_query.astype(jnp.bfloat16).reshape(
        device_local, HEAD_COUNT, feature_width
    )
    query_latent_gradient = query_up_gradient[:, :, :LATENT_WIDTH]
    key_weight_gradient = jnp.einsum(
        "thc,thd->chd", query_latent_gradient, query_nope, preferred_element_type=jnp.float32
    )
    d_q_nope = jnp.einsum(
        "thc,chd->thd", query_latent_gradient, key_part, preferred_element_type=jnp.float32
    )
    d_q_rope = reverse_rotary(
        query_up_gradient[:, :, LATENT_WIDTH:].astype(jnp.float32),
        cosine_table[:, None, :],
        sine_table[:, None, :],
    )
    d_query_full = (
        jnp.concatenate([d_q_nope, d_q_rope], axis=-1)
        .astype(jnp.bfloat16)
        .reshape(device_local, HEAD_COUNT * (PLAIN_UNITS + ROTARY_UNITS))
    )
    query_weight_gradient = inner(normed_in, d_query_full)
    d_normed_in = outer_product(d_query_full, wq)
    latent_gradient = key_gradient[:, :LATENT_WIDTH].astype(jnp.float32)
    rotary_key_gradient = reverse_rotary(
        key_gradient[:, LATENT_WIDTH:].astype(jnp.float32), cosine_table, sine_table
    )
    d_compact, g_lat_grad = norm_backward(packed_rows, inv_lat, g_lat, latent_gradient)
    d_latent_full = jnp.concatenate([d_compact, rotary_key_gradient], axis=-1).astype(jnp.bfloat16)
    latent_weight_gradient = inner(normed_in, d_latent_full)
    d_normed_in = d_normed_in + outer_product(d_latent_full, wlat)
    d_norm_in, g_attn_grad = norm_backward(x_in, inv_attn, attention_gain_grad, d_normed_in)
    d_tokens = (d_hidden + d_norm_in).astype(jnp.bfloat16)
    expand_weight_gradient = jnp.concatenate(
        [key_weight_gradient, value_weight_gradient], axis=-1
    ).reshape(LATENT_WIDTH, HEAD_COUNT * (PLAIN_UNITS + VALUE_UNITS))
    r_sgate, r_sup, r_sdown = (
        lax.psum_scatter(shared_gate_gradient, ("expert", "fsdp"), scatter_dimension=0, tiled=True),
        lax.psum_scatter(shared_up_gradient, ("expert", "fsdp"), scatter_dimension=0, tiled=True),
        lax.psum_scatter(shared_down_gradient, ("expert", "fsdp"), scatter_dimension=0, tiled=True),
    )
    r_attn, r_query, r_latent, r_lgain, r_expand, r_out, r_fgain, r_router = (
        lax.psum_scatter(
            g_attn_grad.astype(jnp.bfloat16), "fsdp", scatter_dimension=0, tiled=True
        ).astype(jnp.float32),
        lax.psum_scatter(
            query_weight_gradient.astype(jnp.bfloat16), "fsdp", scatter_dimension=0, tiled=True
        ).astype(jnp.float32),
        lax.psum_scatter(
            latent_weight_gradient.astype(jnp.bfloat16), "fsdp", scatter_dimension=0, tiled=True
        ).astype(jnp.float32),
        lax.psum_scatter(
            g_lat_grad.astype(jnp.bfloat16), "fsdp", scatter_dimension=0, tiled=True
        ).astype(jnp.float32),
        lax.psum_scatter(
            expand_weight_gradient.astype(jnp.bfloat16), "fsdp", scatter_dimension=0, tiled=True
        ).astype(jnp.float32),
        lax.psum_scatter(
            output_weight_gradient.astype(jnp.bfloat16), "fsdp", scatter_dimension=0, tiled=True
        ).astype(jnp.float32),
        lax.psum_scatter(
            g_ffn_grad.astype(jnp.bfloat16), "fsdp", scatter_dimension=0, tiled=True
        ).astype(jnp.float32),
        lax.psum_scatter(
            router_weight_gradient.astype(jnp.bfloat16), "fsdp", scatter_dimension=0, tiled=True
        ).astype(jnp.float32),
    )
    r_attn, r_query, r_latent, r_lgain, r_expand, r_out, r_fgain, r_router = (
        lax.psum(r_attn.astype(jnp.bfloat16), "expert").astype(jnp.float32),
        lax.psum(r_query.astype(jnp.bfloat16), "expert").astype(jnp.float32),
        lax.psum(r_latent.astype(jnp.bfloat16), "expert").astype(jnp.float32),
        lax.psum(r_lgain.astype(jnp.bfloat16), "expert").astype(jnp.float32),
        lax.psum(r_expand.astype(jnp.bfloat16), "expert").astype(jnp.float32),
        lax.psum(r_out.astype(jnp.bfloat16), "expert").astype(jnp.float32),
        lax.psum(r_fgain.astype(jnp.bfloat16), "expert").astype(jnp.float32),
        lax.psum(r_router.astype(jnp.bfloat16), "expert").astype(jnp.float32),
    )
    return (
        output.astype(jnp.bfloat16)[None],
        d_tokens[None],
        r_attn,
        r_query,
        r_latent,
        r_lgain,
        r_expand,
        r_out,
        r_fgain,
        r_router,
        r_sgate,
        r_sup,
        r_sdown,
        g_gate[None],
        g_up[None],
        g_down[None],
    )


LINE = 4
SQUARE = 2
CORES = 2
MESH = pl.DeviceIdType.MESH
VMEM_LIMIT = 56 * 1024 * 1024


class Place:
    def __init__(self):
        index = lax.axis_index("expert")
        self.y = lax.axis_index("fsdp")
        self.c = lax.rem(index, CORES)
        self.b = lax.rem(lax.div(index, CORES), SQUARE)
        self.a = lax.div(index, CORES * SQUARE)

    def device(self, da=0, db=0, dc=0, dy=0):
        b = 1 - self.b if db else self.b
        c = 1 - self.c if dc else self.c
        y = 1 - self.y if dy else self.y
        return (((self.a + da) * SQUARE + b) * CORES + c, y)

    def block(self, full, a, db=0, dc=0, dy=0):
        b = 1 - self.b if db else self.b
        c = 1 - self.c if dc else self.c
        y = 1 - self.y if dy else self.y
        flat = (a * SQUARE + b) * CORES + c
        return y * (LINE * SQUARE * CORES) + flat if full else flat

    def greet(self, with_y):
        barrier = pltpu.get_barrier_semaphore()
        near = [dict(db=1), dict(dc=1)] + ([dict(dy=1)] if with_y else [])
        for step in near:
            pl.semaphore_signal(barrier, inc=1, device_id=self.device(**step), device_id_type=MESH)

        @pl.when(self.a > 0)
        def _():
            pl.semaphore_signal(barrier, inc=1, device_id=self.device(da=-1), device_id_type=MESH)

        @pl.when(self.a < LINE - 1)
        def _():
            pl.semaphore_signal(barrier, inc=1, device_id=self.device(da=1), device_id_type=MESH)

        ends = jnp.logical_or(self.a == 0, self.a == LINE - 1).astype(jnp.int32)
        pl.semaphore_wait(barrier, len(near) + 2 - ends)


class Sender:
    def __init__(self, place, sems):
        self.place, self.sems, self.pending = place, sems, []

    def send(self, src, dst, recv_sem, step, cond=None):
        sem = self.sems.at[len(self.pending)]

        def make():
            return pltpu.make_async_remote_copy(
                src_ref=src,
                dst_ref=dst,
                send_sem=sem,
                recv_sem=recv_sem,
                device_id=self.place.device(**step),
                device_id_type=MESH,
            )

        def start():
            make().start()

        guarded(cond, start)
        self.pending.append((cond, lambda: make().wait_send()))

    def arrived(self, dst, recv_sem):
        pltpu.make_async_remote_copy(
            src_ref=dst,
            dst_ref=dst,
            send_sem=self.sems.at[0],
            recv_sem=recv_sem,
            device_id=self.place.device(dc=1),
            device_id_type=MESH,
        ).wait_recv()

    def finish(self):
        for cond, wait in self.pending:
            guarded(cond, wait)


def guarded(cond, action):
    if cond is None:
        action()
    else:
        pl.when(cond)(action)


def both(first, second):
    if first is None or second is None:
        return second if first is None else first
    return jnp.logical_and(first, second)


def gather_ticks(place, sender, full, gated, ins, outs, local_sems, recv_sems):
    a = place.a
    count = len(ins)

    def own_copy(at):
        return pltpu.make_async_copy(
            ins[at], outs[at].at[place.block(full, a)], local_sems.at[at]
        )

    def chunk(at, block, half):
        size = ins[at].shape[0] // 2
        return outs[at].at[block, pl.ds(half * size, size)]

    def sem_of(at, block, half):
        return recv_sems.at[at, block * 2 + half]

    def forward(at, block, half, src, step, cond=None):
        sender.send(src, chunk(at, block, half), sem_of(at, block, half), step, cond)

    def receive(at, block, half, cond):
        guarded(cond, lambda: sender.arrived(chunk(at, block, half), sem_of(at, block, half)))

    def held_by(at, delta, cond):
        if at not in gated:
            return cond
        return both(cond, lax.div(a + delta, LINE // 2) == place.y)

    def from_line(delta, always):
        for half in range(2):
            for at in range(count):
                block = place.block(full, a + delta)
                cond = held_by(at, delta, always)
                size = ins[at].shape[0] // 2
                if delta == 0:
                    src = ins[at].at[pl.ds(half * size, size)]
                else:
                    receive(at, block, half, cond)
                    src = chunk(at, block, half)
                if delta <= 0:
                    forward(at, block, half, src, dict(da=1), both(cond, a < LINE - 1))
                if delta >= 0:
                    forward(at, block, half, src, dict(da=-1), both(cond, a > 0))
                forward(at, block, half, src, dict(db=1), cond)
                if full:
                    forward(at, block, half, src, dict(dy=1), cond)
                forward(at, block, half, src, dict(dc=1), cond)

    def from_side(delta, always):
        for half in range(2):
            for at in range(count):
                cond = held_by(at, delta, always)
                block = place.block(full, a + delta, db=1)
                receive(at, block, half, cond)
                if full and half == 0:
                    forward(at, block, half, chunk(at, block, half), dict(dy=1), cond)
                forward(at, block, half, chunk(at, block, half), dict(dc=1), cond)
                if full:
                    block = place.block(full, a + delta, dy=1)
                    receive(at, block, half, cond)
                    if half == 1:
                        forward(at, block, half, chunk(at, block, half), dict(db=1), cond)
                    forward(at, block, half, chunk(at, block, half), dict(dc=1), cond)

    def from_corner(delta, always):
        for half in range(2):
            for at in range(count):
                cond = held_by(at, delta, always)
                block = place.block(True, a + delta, db=1, dy=1)
                receive(at, block, half, cond)
                forward(at, block, half, chunk(at, block, half), dict(dc=1), cond)

    def from_sibling(delta, always):
        for half in range(2):
            for at in range(count):
                cond = held_by(at, delta, always)
                for db in range(2):
                    for dy in range(2 if full else 1):
                        receive(at, place.block(full, a + delta, db=db, dc=1, dy=dy), half, cond)

    rounds = [[(0, None)]]
    for s in range(1, LINE):
        rounds.append([(-s, a >= s), (s, a + s < LINE)])
    stages = [from_line, from_side] + ([from_corner] if full else []) + [from_sibling]

    def tick(number):
        if number == 0:
            for at in range(count):
                own_copy(at).start()
        for level, stage in enumerate(stages):
            if 0 <= number - level < len(rounds):
                for delta, cond in rounds[number - level]:
                    stage(delta, cond)
        if number == len(rounds) + len(stages) - 2:
            for at in range(count):
                own_copy(at).wait()

    return [functools.partial(tick, number) for number in range(len(rounds) + len(stages) - 1)]


def send_pairs(sender, ins, outs, sems):
    for at, (src, dst) in enumerate(zip(ins, outs)):
        sender.send(src, dst, sems.at[at], dict(dy=1))


def take_pairs(sender, outs, sems):
    for at, dst in enumerate(outs):
        sender.arrived(dst, sems.at[at])


def gather_kernel(full, count, pairs, gated, *refs):
    ins, outs = refs[: count + pairs], refs[count + pairs : 2 * (count + pairs)]
    local_sems, send_sems, recv_sems, pair_sems = refs[2 * (count + pairs) :]
    place = Place()
    sender = Sender(place, send_sems)
    place.greet(full or pairs > 0)
    send_pairs(sender, ins[count:], outs[count:], pair_sems)
    for tick in gather_ticks(
        place, sender, full, gated, ins[:count], outs[:count], local_sems, recv_sems
    ):
        tick()
    take_pairs(sender, outs[count:], pair_sems)
    sender.finish()


def gather_rows(arrays, full, collective_id, swapped=(), gated=()):
    blocks = LINE * SQUARE * CORES * (SQUARE if full else 1)
    count, pairs = len(arrays), len(swapped)
    lines = 2 * LINE - 1
    sends = pairs + count * lines * 2 * (9 if full else 5)
    moved = sum(blocks * 2 * x.size * x.dtype.itemsize for x in arrays)
    return pl.pallas_call(
        functools.partial(gather_kernel, full, count, pairs, gated),
        out_shape=[jax.ShapeDtypeStruct((blocks,) + x.shape, x.dtype) for x in arrays]
        + [jax.ShapeDtypeStruct(x.shape, x.dtype) for x in swapped],
        in_specs=[pl.BlockSpec(memory_space=pl.ANY)] * (count + pairs),
        out_specs=[pl.BlockSpec(memory_space=pl.ANY)] * (count + pairs),
        scratch_shapes=[
            pltpu.SemaphoreType.DMA((count,)),
            pltpu.SemaphoreType.DMA((sends,)),
            pltpu.SemaphoreType.DMA((count, blocks * 2)),
            pltpu.SemaphoreType.DMA((max(pairs, 1),)),
        ],
        compiler_params=pltpu.CompilerParams(collective_id=collective_id, has_side_effects=True),
        cost_estimate=pl.CostEstimate(flops=0, bytes_accessed=6 * moved, transcendentals=0),
    )(*arrays, *swapped)


def add_rows(target, sources, size):
    def step(at, carry):
        rows = pl.ds(pl.multiple_of(at * 16, 16), 16)
        total = sources[0][rows, :].astype(jnp.float32)
        for source in sources[1:]:
            total = total + source[rows, :].astype(jnp.float32)
        target[rows, :] = total.astype(target.dtype)
        return carry

    lax.fori_loop(0, size // 16, step, 0)


def scatter_ticks(place, sender, full, part, out, scratch):
    mine, got, side, up, down, load_sems, recv_sems = scratch
    a = place.a
    kinds = 4 if full else 2
    size = part.shape[1]
    half = size // 2
    order = [LINE - 1, 0, LINE - 2, 1]
    walk = (3, 1, 2, 0) if full else (1, 0)

    def sem_of(group, target, kind):
        return recv_sems.at[group, target * 4 + kind]

    def load(target, kind):
        block = place.block(full, target, db=kind % 2, dy=kind // 2)
        return pltpu.make_async_copy(
            part.at[block], mine.at[target, kind], load_sems.at[target * 4 + kind]
        )

    def begin():
        for target in order:
            for kind in walk:
                load(target, kind).start()
                block = place.block(full, target, db=kind % 2, dc=1, dy=kind // 2)
                sender.send(
                    part.at[block], got.at[target, kind], sem_of(0, target, kind), dict(dc=1)
                )

    def rows_of(ref, which):
        return ref.at[pl.ds(which * half, half)]

    def over_cores(target):
        for kind in walk:
            load(target, kind).wait()
            sender.arrived(got.at[target, kind], sem_of(0, target, kind))
            add_rows(mine.at[target, kind], [mine.at[target, kind], got.at[target, kind]], size)
            held = mine.at[target, kind]
            if kind == 3:
                sender.send(rows_of(held, 0), side.at[target, 4], sem_of(1, target, 0), dict(db=1))
                sender.send(rows_of(held, 1), side.at[target, 5], sem_of(1, target, 1), dict(dy=1))
            if kind == 1:
                sender.send(rows_of(held, 0), side.at[target, 0], sem_of(2, target, 0), dict(db=1))
                if not full:
                    sender.send(
                        rows_of(held, 1), side.at[target, 1], sem_of(2, target, 1), dict(db=1)
                    )
            if kind == 2:
                sender.send(rows_of(held, 1), side.at[target, 3], sem_of(2, target, 3), dict(dy=1))

    def over_corner(target):
        sender.arrived(side.at[target, 4], sem_of(1, target, 0))
        held = rows_of(mine.at[target, 2], 0)
        add_rows(held, [held, side.at[target, 4]], half)
        sender.send(held, side.at[target, 2], sem_of(2, target, 2), dict(dy=1))
        sender.arrived(side.at[target, 5], sem_of(1, target, 1))
        held = rows_of(mine.at[target, 1], 1)
        add_rows(held, [held, side.at[target, 5]], half)
        sender.send(held, side.at[target, 1], sem_of(2, target, 1), dict(db=1))

    def over_line(target):
        for which in range(2):
            held = rows_of(mine.at[target, 0], which)
            parts = [held]
            for source in (0, 2) if full else (0,):
                sender.arrived(side.at[target, source + which], sem_of(2, target, source + which))
                parts.append(side.at[target, source + which])
            below, above = rows_of(up.at[target], which), rows_of(down.at[target], which)
            below_sem, above_sem = sem_of(3, target, which), sem_of(3, target, 2 + which)

            def upward(with_below):
                extra = []
                if with_below:
                    sender.arrived(below, below_sem)
                    extra = [below]
                add_rows(held, parts + extra, half)

            def downward(with_above):
                extra = []
                if with_above:
                    sender.arrived(above, above_sem)
                    extra = [above]
                add_rows(held, parts + extra, half)

            if target > 0:
                pl.when(jnp.logical_and(a < target, a > 0))(lambda: upward(True))
                pl.when(a == 0)(lambda: upward(False))
                sender.send(held, below, below_sem, dict(da=1), a < target)
            if target < LINE - 1:
                pl.when(jnp.logical_and(a > target, a < LINE - 1))(lambda: downward(True))
                pl.when(a == LINE - 1)(lambda: downward(False))
                sender.send(held, above, above_sem, dict(da=-1), a > target)

            def last():
                extra = []
                if target > 0:
                    sender.arrived(below, below_sem)
                    extra.append(below)
                if target < LINE - 1:
                    sender.arrived(above, above_sem)
                    extra.append(above)
                add_rows(rows_of(out, which), parts + extra, half)

            pl.when(a == target)(last)

    stages = [over_cores] + ([over_corner] if full else []) + [over_line]

    def tick(number):
        if number == 0:
            begin()
        for level, stage in enumerate(stages):
            if 0 <= number - level < len(order):
                stage(order[number - level])

    return [functools.partial(tick, number) for number in range(len(order) + len(stages) - 1)]


def scatter_kernel(full, pairs, part, *refs):
    ins, out, outs = refs[:pairs], refs[pairs], refs[pairs + 1 : 2 * pairs + 1]
    mine, got, side, up, down, load_sems, send_sems, recv_sems, pair_sems = refs[2 * pairs + 1 :]
    place = Place()
    sender = Sender(place, send_sems)
    place.greet(full or pairs > 0)
    send_pairs(sender, ins, outs, pair_sems)
    scratch = (mine, got, side, up, down, load_sems, recv_sems)
    for tick in scatter_ticks(place, sender, full, part, out, scratch):
        tick()
    take_pairs(sender, outs, pair_sems)
    sender.finish()


def scatter_scratch(full, rows, width, dtype, pairs):
    kinds = 4 if full else 2
    return [
        pltpu.VMEM((LINE, kinds, rows, width), dtype),
        pltpu.VMEM((LINE, kinds, rows, width), dtype),
        pltpu.VMEM((LINE, 6, rows // 2, width), dtype),
        pltpu.VMEM((LINE, rows, width), dtype),
        pltpu.VMEM((LINE, rows, width), dtype),
        pltpu.SemaphoreType.DMA((LINE * 4,)),
        pltpu.SemaphoreType.DMA((pairs + LINE * (4 + 6 + 4),)),
        pltpu.SemaphoreType.DMA((4, LINE * 4)),
        pltpu.SemaphoreType.DMA((max(pairs, 1),)),
    ]


def gather_scatter_kernel(count, gated, *refs):
    ins, part = refs[:count], refs[count]
    outs, total = refs[count + 1 : 2 * count + 1], refs[2 * count + 1]
    local_sems, gather_sends, gather_recvs = refs[2 * count + 2 : 2 * count + 5]
    mine, got, side, up, down, load_sems, scatter_sends, scatter_recvs, _ = refs[2 * count + 5 :]
    place = Place()
    gatherer = Sender(place, gather_sends)
    scatterer = Sender(place, scatter_sends)
    place.greet(True)
    scratch = (mine, got, side, up, down, load_sems, scatter_recvs)
    ticks = [
        scatter_ticks(place, scatterer, True, part, total, scratch),
        gather_ticks(place, gatherer, False, gated, ins, outs, local_sems, gather_recvs),
    ]
    for number in range(max(len(steps) for steps in ticks)):
        for steps in ticks:
            if number < len(steps):
                steps[number]()
    scatterer.finish()
    gatherer.finish()


def gather_and_scatter(arrays, part, collective_id, gated=()):
    blocks = LINE * SQUARE * CORES
    count = len(arrays)
    _, rows, width = part.shape
    sends = count * (2 * LINE - 1) * 2 * 5
    moved = sum(blocks * 2 * x.size * x.dtype.itemsize for x in arrays)
    return pl.pallas_call(
        functools.partial(gather_scatter_kernel, count, gated),
        out_shape=[jax.ShapeDtypeStruct((blocks,) + x.shape, x.dtype) for x in arrays]
        + [jax.ShapeDtypeStruct((rows, width), jnp.float32)],
        in_specs=[pl.BlockSpec(memory_space=pl.ANY)] * (count + 1),
        out_specs=[pl.BlockSpec(memory_space=pl.ANY)] * count
        + [pl.BlockSpec(memory_space=pltpu.VMEM)],
        scratch_shapes=[
            pltpu.SemaphoreType.DMA((count,)),
            pltpu.SemaphoreType.DMA((sends,)),
            pltpu.SemaphoreType.DMA((count, blocks * 2)),
        ]
        + scatter_scratch(True, rows, width, part.dtype, 0),
        compiler_params=pltpu.CompilerParams(
            collective_id=collective_id, has_side_effects=True, vmem_limit_bytes=VMEM_LIMIT
        ),
        cost_estimate=pl.CostEstimate(flops=0, bytes_accessed=6 * moved, transcendentals=0),
    )(*arrays, part)


def scatter_rows(part, full, collective_id, swapped=()):
    blocks, rows, width = part.shape
    pairs = len(swapped)
    return pl.pallas_call(
        functools.partial(scatter_kernel, full, pairs),
        out_shape=[jax.ShapeDtypeStruct((rows, width), jnp.float32)]
        + [jax.ShapeDtypeStruct(x.shape, x.dtype) for x in swapped],
        in_specs=[pl.BlockSpec(memory_space=pl.ANY)] * (1 + pairs),
        out_specs=[pl.BlockSpec(memory_space=pltpu.VMEM)]
        + [pl.BlockSpec(memory_space=pl.ANY)] * pairs,
        scratch_shapes=scatter_scratch(full, rows, width, part.dtype, pairs),
        compiler_params=pltpu.CompilerParams(
            collective_id=collective_id, has_side_effects=True, vmem_limit_bytes=VMEM_LIMIT
        ),
        cost_estimate=pl.CostEstimate(
            flops=0, bytes_accessed=12 * part.size * part.dtype.itemsize, transcendentals=0
        ),
    )(part, *swapped)


def contract_last(left, right):
    return lax.dot_general(
        left, right, (((1,), (1,)), ((), ())), preferred_element_type=jnp.float32
    )


def contract_first(left, right):
    return lax.dot_general(
        left, right, (((0,), (0,)), ((), ())), preferred_element_type=jnp.float32
    )


def expert_kernel(
    capacity,
    normed,
    grads,
    routes,
    router_rows,
    w_gate,
    w_up,
    w_down,
    shared_in,
    shared_out,
    out_part,
    d_part,
    ex_rows,
    ex_grads,
    act_out,
    d_gate_out,
    d_up_out,
    shared_in_grad,
    shared_out_grad,
    in_total,
    out_total,
):
    position = lax.axis_index("expert")
    experts = lax.axis_size("expert")
    group, rows, width = normed.shape
    tokens, slots = group * rows, group * capacity
    bf16 = jnp.bfloat16
    x = normed[...].reshape(tokens, width)
    g = grads[...].reshape(tokens, width)

    row = lax.broadcasted_iota(jnp.int32, (tokens, tokens), 0)
    column = lax.broadcasted_iota(jnp.int32, (tokens, tokens), 1)
    before = jnp.logical_and(column < row, lax.div(row, rows) == lax.div(column, rows))
    named = routes[...].reshape(tokens, -1) == position.astype(jnp.float32).astype(bf16)
    hit = jnp.sum(jnp.where(named, 1.0, 0.0), axis=1, keepdims=True)
    tally = matrix_product(
        jnp.where(before, 1.0, 0.0).astype(bf16),
        jnp.broadcast_to(hit, (tokens, 128)).astype(bf16),
    )
    place = jnp.where(hit > 0.5, tally[:, :1], -1.0)
    token = lax.broadcasted_iota(jnp.int32, (tokens, slots), 0)
    slot = lax.broadcasted_iota(jnp.int32, (tokens, slots), 1)
    same = lax.div(slot, capacity) == lax.div(token, rows)
    wanted = lax.rem(slot, capacity).astype(jnp.float32)
    chosen = jnp.where(jnp.logical_and(same, wanted == place), 1.0, 0.0)
    pick = chosen.T.astype(bf16)
    put = chosen.astype(bf16)

    r = matrix_product(pick, x).astype(bf16)
    gr = matrix_product(pick, g).astype(bf16)
    ex_rows[...] = r
    ex_grads[...] = gr
    lane = lax.broadcasted_iota(jnp.int32, (slots, router_rows.shape[0]), 1)
    logits = jnp.where(lane < experts, contract_last(r, router_rows[...]), -1e30)
    exps = jnp.exp(logits - jnp.max(logits, axis=1, keepdims=True))
    gate = jnp.sum(jnp.where(lane == position, exps, 0.0), axis=1, keepdims=True) / jnp.sum(
        exps, axis=1, keepdims=True
    )

    pre_gate = contract_last(r, w_gate[...])
    pre_up = contract_last(r, w_up[...])
    act_gate, slope = silu_parts(pre_gate)
    act = act_gate * pre_up
    back = contract_last(gr, w_down[...])
    d_gate_slot = jnp.sum(act * back, axis=1, keepdims=True)
    scaled = (gate * act).astype(bf16)
    d_act = gate * back
    d_pre_gate = (d_act * pre_up * slope).astype(bf16)
    d_pre_up = (d_act * act_gate).astype(bf16)
    act_out[...] = scaled
    d_gate_out[...] = d_pre_gate
    d_up_out[...] = d_pre_up
    ex_out = matrix_product(scaled, w_down[...]).astype(bf16)
    d_ex = matrix_product(d_pre_gate, w_gate[...]) + matrix_product(d_pre_up, w_up[...])
    d_ex = d_ex.astype(bf16)

    units = shared_out.shape[0]
    mix = matrix_product(x, shared_in[...])
    sh_gate, sh_up = mix[:, :units], mix[:, units:]
    sh_silu, sh_slope = silu_parts(sh_gate)
    sh_act = (sh_silu * sh_up).astype(bf16)
    d_sh_act = contract_last(g, shared_out[...])
    d_mix = jnp.concatenate([d_sh_act * sh_up * sh_slope, d_sh_act * sh_silu], axis=1)
    d_mix = d_mix.astype(bf16)

    out = matrix_product(put, ex_out) + matrix_product(sh_act, shared_out[...])
    out_part[...] = out.astype(bf16).reshape(group, rows, width)
    d_in = matrix_product(put, d_ex) + contract_last(d_mix, shared_in[...])
    d_part[:, :, :width] = d_in.astype(bf16).reshape(group, rows, width)
    lane = lax.broadcasted_iota(jnp.int32, (slots, d_part.shape[2] - width), 1)
    d_gates = jnp.where(lane == position, d_gate_slot, 0.0).astype(bf16)
    d_part[:, :, width:] = matrix_product(put, d_gates).astype(bf16).reshape(group, rows, -1)

    step = pl.program_id(0)

    @pl.when(step == 0)
    def _():
        in_total[...] = jnp.zeros_like(in_total)
        out_total[...] = jnp.zeros_like(out_total)

    in_total[...] += contract_first(d_mix, x)
    out_total[...] += contract_first(sh_act, g)

    @pl.when(step == pl.num_programs(0) - 1)
    def _():
        shared_in_grad[...] = in_total[...].T.astype(bf16)
        shared_out_grad[...] = out_total[...]


def expert_phase(
    all_normed, all_grads, router_rows, w_gate, w_up, w_down, shared_in, shared_out, capacity
):
    blocks, rows, width = all_normed.shape
    group = 4
    slots = group * capacity
    hidden = w_gate.shape[0]
    units = shared_out.shape[0]
    side = all_grads.shape[2] - width
    bf16 = jnp.bfloat16

    def by_group(shape):
        zeros = (0,) * (len(shape) - 1)
        return pl.BlockSpec(shape, lambda i: (i,) + zeros)

    def fixed(shape):
        return pl.BlockSpec(
            shape, lambda i: (0,) * len(shape), pipeline_mode=pl.Buffered(buffer_count=1)
        )

    return pl.pallas_call(
        functools.partial(expert_kernel, capacity),
        grid=(blocks // group,),
        out_shape=[
            jax.ShapeDtypeStruct((blocks, rows, width), bf16),
            jax.ShapeDtypeStruct((blocks, rows, width + side), bf16),
            jax.ShapeDtypeStruct((blocks * capacity, width), bf16),
            jax.ShapeDtypeStruct((blocks * capacity, width), bf16),
            jax.ShapeDtypeStruct((blocks * capacity, hidden), bf16),
            jax.ShapeDtypeStruct((blocks * capacity, hidden), bf16),
            jax.ShapeDtypeStruct((blocks * capacity, hidden), bf16),
            jax.ShapeDtypeStruct((width, 2 * units), bf16),
            jax.ShapeDtypeStruct((units, width), jnp.float32),
        ],
        in_specs=[
            by_group((group, rows, width)),
            by_group((group, rows, width)),
            pl.BlockSpec((group, rows, side), lambda i: (i, 0, width // side)),
            fixed(router_rows.shape),
            fixed(w_gate.shape),
            fixed(w_up.shape),
            fixed(w_down.shape),
            fixed(shared_in.shape),
            fixed(shared_out.shape),
        ],
        out_specs=[
            by_group((group, rows, width)),
            by_group((group, rows, width + side)),
            by_group((slots, width)),
            by_group((slots, width)),
            by_group((slots, hidden)),
            by_group((slots, hidden)),
            by_group((slots, hidden)),
            fixed((width, 2 * units)),
            fixed((units, width)),
        ],
        scratch_shapes=[
            pltpu.VMEM((2 * units, width), jnp.float32),
            pltpu.VMEM((units, width), jnp.float32),
        ],
        compiler_params=pltpu.CompilerParams(vmem_limit_bytes=VMEM_LIMIT),
        cost_estimate=pl.CostEstimate(
            flops=2 * blocks * capacity * width * hidden * 6,
            bytes_accessed=10 * blocks * rows * width * 2,
            transcendentals=blocks * capacity * hidden,
        ),
    )(all_normed, all_grads, all_grads, router_rows, w_gate, w_up, w_down, shared_in, shared_out)


def exchange_kernel(x, out, local_sem, send_sems, recv_sems):
    me, y = lax.axis_index("expert"), lax.axis_index("fsdp")
    count = x.shape[0]
    barrier = pltpu.get_barrier_semaphore()
    peers = [lax.rem(me + step, count) for step in range(1, count)]
    for peer in peers:
        pl.semaphore_signal(barrier, inc=1, device_id=(peer, y), device_id_type=MESH)
    own = pltpu.make_async_copy(x.at[me], out.at[me], local_sem)
    own.start()
    pl.semaphore_wait(barrier, count - 1)
    copies = []
    for at, peer in enumerate(peers):
        copy = pltpu.make_async_remote_copy(
            src_ref=x.at[peer],
            dst_ref=out.at[me],
            send_sem=send_sems.at[at],
            recv_sem=recv_sems.at[at],
            device_id=(peer, y),
            device_id_type=MESH,
        )
        copy.start()
        copies.append(copy)
    for copy in copies:
        copy.wait()
    own.wait()


def exchange(x, collective_id):
    count = x.shape[0]
    return pl.pallas_call(
        exchange_kernel,
        out_shape=jax.ShapeDtypeStruct(x.shape, x.dtype),
        in_specs=[pl.BlockSpec(memory_space=pl.ANY)],
        out_specs=pl.BlockSpec(memory_space=pl.ANY),
        scratch_shapes=[
            pltpu.SemaphoreType.DMA,
            pltpu.SemaphoreType.DMA((count - 1,)),
            pltpu.SemaphoreType.DMA((count - 1,)),
        ],
        compiler_params=pltpu.CompilerParams(collective_id=collective_id, has_side_effects=True),
        cost_estimate=pl.CostEstimate(
            flops=0, bytes_accessed=20 * x.size * x.dtype.itemsize, transcendentals=0
        ),
    )(x)


def swap_halves(value):
    half = value.shape[1] // 2
    return jnp.concatenate([value[:, half:], value[:, :half]], axis=1)


def greet_plane(place):
    me = lax.axis_index("expert")
    count = LINE * SQUARE * CORES
    barrier = pltpu.get_barrier_semaphore()
    for step in range(1, count):
        peer = (lax.rem(me + step, count), place.y)
        pl.semaphore_signal(barrier, inc=1, device_id=peer, device_id_type=MESH)
    pl.semaphore_signal(barrier, inc=1, device_id=place.device(dy=1), device_id_type=MESH)
    pl.semaphore_wait(barrier, count)


def sums_kernel(pairs, moved, small, large, *refs):
    ins = refs[:pairs]
    moved_out, small_out, large_out = refs[pairs : pairs + 3]
    outs = refs[pairs + 3 : 2 * pairs + 3]
    rest = refs[2 * pairs + 3 :]
    local_sem, exchange_sends, exchange_recvs = rest[:3]
    first, second = rest[3:12], rest[12:21]
    place = Place()
    me = lax.axis_index("expert")
    count = moved.shape[0]
    greet_plane(place)
    own = pltpu.make_async_copy(moved.at[me], moved_out.at[me], local_sem)
    own.start()
    copies = []
    for at in range(count - 1):
        copy = pltpu.make_async_remote_copy(
            src_ref=moved.at[lax.rem(me + at + 1, count)],
            dst_ref=moved_out.at[me],
            send_sem=exchange_sends.at[at],
            recv_sem=exchange_recvs.at[at],
            device_id=(lax.rem(me + at + 1, count), place.y),
            device_id_type=MESH,
        )
        copy.start()
        copies.append(copy)
    senders = [Sender(place, first[6]), Sender(place, second[6])]
    send_pairs(senders[0], ins, outs, first[8])
    ticks = [
        scatter_ticks(place, senders[0], False, small, small_out, first[:6] + (first[7],)),
        scatter_ticks(place, senders[1], True, large, large_out, second[:6] + (second[7],)),
    ]
    for number in range(max(len(steps) for steps in ticks)):
        for steps in ticks:
            if number < len(steps):
                steps[number]()
    take_pairs(senders[0], outs, first[8])
    for sender in senders:
        sender.finish()
    for copy in copies:
        copy.wait()
    own.wait()


def exchange_and_sums(moved, small, large, swapped, collective_id):
    count, pairs = moved.shape[0], len(swapped)
    hbm = pl.BlockSpec(memory_space=pl.ANY)
    vmem = pl.BlockSpec(memory_space=pltpu.VMEM)
    return pl.pallas_call(
        functools.partial(sums_kernel, pairs),
        out_shape=[
            jax.ShapeDtypeStruct(moved.shape, moved.dtype),
            jax.ShapeDtypeStruct(small.shape[1:], jnp.float32),
            jax.ShapeDtypeStruct(large.shape[1:], jnp.float32),
        ]
        + [jax.ShapeDtypeStruct(x.shape, x.dtype) for x in swapped],
        in_specs=[hbm] * (3 + pairs),
        out_specs=[hbm, vmem, vmem] + [hbm] * pairs,
        scratch_shapes=[
            pltpu.SemaphoreType.DMA,
            pltpu.SemaphoreType.DMA((count - 1,)),
            pltpu.SemaphoreType.DMA((count - 1,)),
        ]
        + scatter_scratch(False, *small.shape[1:], small.dtype, pairs)
        + scatter_scratch(True, *large.shape[1:], large.dtype, 0),
        compiler_params=pltpu.CompilerParams(
            collective_id=collective_id, has_side_effects=True, vmem_limit_bytes=VMEM_LIMIT
        ),
        cost_estimate=pl.CostEstimate(
            flops=0, bytes_accessed=12 * large.size * 2, transcendentals=0
        ),
    )(moved, small, large, *swapped)


def attend_kernel(
    rows,
    g_attn,
    w_front,
    g_lat,
    expand_head,
    cosines,
    sines,
    normed_out,
    latent_out,
    query_out,
    key_out,
    value_out,
    head_out,
    sum_out,
    log_out,
    keys,
    values,
):
    bf16 = jnp.bfloat16
    size = rows.shape[0]
    scale = (PLAIN_UNITS + ROTARY_UNITS) ** (-0.5)
    step = pl.program_id(0)
    normed, _ = norm_forward(rows[...].astype(jnp.float32), g_attn[...])
    normed = normed.astype(bf16)
    normed_out[...] = normed
    front = contract_last(normed, w_front[...])
    latent, _ = norm_forward(front[:, :LATENT_WIDTH], g_lat[...])
    latent = latent.astype(bf16)
    latent_out[...] = latent
    width = LATENT_WIDTH + ROTARY_UNITS

    def rotated(value):
        return value * cosines[...] + swap_halves(value) * sines[...]

    pairs = matrix_product(latent, expand_head[...])
    key = jnp.concatenate([pairs[:, :PLAIN_UNITS], rotated(front[:, LATENT_WIDTH:width])], axis=1)
    query = jnp.concatenate(
        [front[:, width : width + PLAIN_UNITS], rotated(front[:, width + PLAIN_UNITS :])], axis=1
    ).astype(bf16)
    key = key.astype(bf16)
    value = pairs[:, PLAIN_UNITS:].astype(bf16)
    query_out[...] = query
    key_out[...] = key
    value_out[...] = value
    here = pl.ds(pl.multiple_of(step * size, size), size)
    keys[here, :] = key
    values[here, :] = value
    row = lax.broadcasted_iota(jnp.int32, (size, size), 0)
    column = lax.broadcasted_iota(jnp.int32, (size, size), 1)
    near = jnp.where(column <= row, contract_last(query, key) * scale, -1e30)

    def over(past):
        top = jnp.max(near, axis=1, keepdims=True)
        if past:
            far = contract_last(query, keys[:past, :]) * scale
            top = jnp.maximum(top, jnp.max(far, axis=1, keepdims=True))
        exps = jnp.exp(near - top)
        total = jnp.sum(exps, axis=1, keepdims=True)
        mixed = matrix_product(exps.astype(bf16), value)
        if past:
            exps = jnp.exp(far - top)
            total = total + jnp.sum(exps, axis=1, keepdims=True)
            mixed = mixed + matrix_product(exps.astype(bf16), values[:past, :])
        mixed = mixed / total
        sum_out[...] = mixed
        head_out[...] = mixed.astype(bf16)
        wide = jnp.broadcast_to(top + jnp.log(total), (size, 128))
        log_out[0] = wide.T[:1, :]

    for at in range(keys.shape[0] // size):
        pl.when(step == at)(functools.partial(over, at * size))


def attend(rows, g_attn, w_front, g_lat, expand_head, cosines, sines):
    seq_len, width = rows.shape
    size = 256
    steps = seq_len // size
    units = PLAIN_UNITS + ROTARY_UNITS
    bf16 = jnp.bfloat16

    def by_step(columns):
        return pl.BlockSpec((size, columns), lambda i: (i, 0))

    def fixed(x):
        return pl.BlockSpec(
            x.shape, lambda i: (0, 0), pipeline_mode=pl.Buffered(buffer_count=1)
        )

    return pl.pallas_call(
        attend_kernel,
        grid=(steps,),
        out_shape=[
            jax.ShapeDtypeStruct((seq_len, width), bf16),
            jax.ShapeDtypeStruct((seq_len, LATENT_WIDTH), bf16),
            jax.ShapeDtypeStruct((seq_len, units), bf16),
            jax.ShapeDtypeStruct((seq_len, units), bf16),
            jax.ShapeDtypeStruct((seq_len, VALUE_UNITS), bf16),
            jax.ShapeDtypeStruct((seq_len, VALUE_UNITS), bf16),
            jax.ShapeDtypeStruct((seq_len, VALUE_UNITS), jnp.float32),
            jax.ShapeDtypeStruct((steps, 1, size), jnp.float32),
        ],
        in_specs=[by_step(width)]
        + [fixed(x) for x in (g_attn, w_front, g_lat, expand_head)]
        + [by_step(ROTARY_UNITS)] * 2,
        out_specs=[
            by_step(width),
            by_step(LATENT_WIDTH),
            by_step(units),
            by_step(units),
            by_step(VALUE_UNITS),
            by_step(VALUE_UNITS),
            by_step(VALUE_UNITS),
            pl.BlockSpec((1, 1, size), lambda i: (i, 0, 0)),
        ],
        scratch_shapes=[
            pltpu.VMEM((seq_len, units), bf16),
            pltpu.VMEM((seq_len, VALUE_UNITS), bf16),
        ],
        compiler_params=pltpu.CompilerParams(vmem_limit_bytes=VMEM_LIMIT),
        cost_estimate=pl.CostEstimate(
            flops=2 * seq_len * (width * 768 + seq_len * units),
            bytes_accessed=3 * rows.size * 2,
            transcendentals=seq_len * seq_len // 2,
        ),
    )(rows, g_attn, w_front, g_lat, expand_head, cosines, sines)


def attend_back_kernel(
    query,
    key,
    value,
    d_head,
    head_sum,
    logs,
    expand_head,
    cosines,
    sines,
    d_query_out,
    d_pairs_out,
    d_keys_out,
    d_key,
    d_value,
    key_turned,
):
    bf16 = jnp.bfloat16
    size = query.shape[0]
    seq_len = key.shape[0]
    scale = (PLAIN_UNITS + ROTARY_UNITS) ** (-0.5)
    step = pl.program_id(0)

    @pl.when(step == 0)
    def _():
        d_key[...] = jnp.zeros_like(d_key)
        d_value[...] = jnp.zeros_like(d_value)
        for at in range(0, seq_len, size):
            part = key[at : at + size, :].astype(jnp.float32)
            key_turned[:, at : at + size] = part.T.astype(bf16)

    q, d_out = query[...], d_head[...]
    product = d_out.astype(jnp.float32) * head_sum[...]
    delta = jnp.sum(product.T, axis=0, keepdims=True)
    log_row = logs[0]
    row = lax.broadcasted_iota(jnp.int32, (size, size), 0)
    column = lax.broadcasted_iota(jnp.int32, (size, size), 1)

    def grads_of(at, mask):
        there = slice(at, at + size)
        scores = contract_last(key[there, :], q) * scale
        if mask:
            scores = jnp.where(row <= column, scores, -1e30)
        probs = jnp.exp(scores - log_row)
        d_probs = contract_last(value[there, :], d_out)
        d_scores = (probs * (d_probs - delta) * scale).astype(bf16)
        d_key[there, :] += matrix_product(d_scores, q)
        d_value[there, :] += matrix_product(probs.astype(bf16), d_out)
        return matrix_product(key_turned[:, there], d_scores)

    def over(past):
        total = grads_of(past, True)
        for at in range(0, past, size):
            total = total + grads_of(at, False)
        d_query = total.T
        d_rope = d_query[:, PLAIN_UNITS:]
        d_rope = d_rope * cosines[...] - swap_halves(d_rope) * sines[...]
        d_query_out[...] = jnp.concatenate([d_query[:, :PLAIN_UNITS], d_rope], axis=1).astype(bf16)

    for at in range(seq_len // size):
        pl.when(step == at)(functools.partial(over, at * size))

    @pl.when(step == seq_len // size - 1)
    def _():
        for at in range(0, seq_len, size):
            there = slice(at, at + size)
            d_pairs = jnp.concatenate(
                [d_key[there, :PLAIN_UNITS], d_value[there, :]], axis=1
            ).astype(bf16)
            d_pairs_out[there, :] = d_pairs
            d_keys_out[there, :LATENT_WIDTH] = contract_last(d_pairs, expand_head[...]).astype(bf16)
            tail = jnp.concatenate(
                [d_key[there, PLAIN_UNITS:], jnp.zeros((size, ROTARY_UNITS), jnp.float32)], axis=1
            )
            d_keys_out[there, LATENT_WIDTH:] = tail.astype(bf16)


def attend_back(query, key, value, d_head, head_sum, logs, expand_head, cosines, sines):
    seq_len, units = query.shape
    steps, _, size = logs.shape
    bf16 = jnp.bfloat16
    keys_width = LATENT_WIDTH + 2 * ROTARY_UNITS

    def by_step(columns):
        return pl.BlockSpec((size, columns), lambda i: (i, 0))

    def fixed(shape):
        return pl.BlockSpec(shape, lambda i: (0, 0), pipeline_mode=pl.Buffered(buffer_count=1))

    return pl.pallas_call(
        attend_back_kernel,
        grid=(steps,),
        out_shape=[
            jax.ShapeDtypeStruct((seq_len, units), bf16),
            jax.ShapeDtypeStruct((seq_len, PLAIN_UNITS + VALUE_UNITS), bf16),
            jax.ShapeDtypeStruct((seq_len, keys_width), bf16),
        ],
        in_specs=[
            by_step(units),
            fixed(key.shape),
            fixed(value.shape),
            by_step(VALUE_UNITS),
            by_step(VALUE_UNITS),
            pl.BlockSpec((1, 1, size), lambda i: (i, 0, 0)),
            fixed(expand_head.shape),
            by_step(ROTARY_UNITS),
            by_step(ROTARY_UNITS),
        ],
        out_specs=[
            by_step(units),
            fixed((seq_len, PLAIN_UNITS + VALUE_UNITS)),
            fixed((seq_len, keys_width)),
        ],
        scratch_shapes=[
            pltpu.VMEM((seq_len, units), jnp.float32),
            pltpu.VMEM((seq_len, VALUE_UNITS), jnp.float32),
            pltpu.VMEM((units, seq_len), bf16),
        ],
        compiler_params=pltpu.CompilerParams(vmem_limit_bytes=VMEM_LIMIT),
        cost_estimate=pl.CostEstimate(
            flops=5 * seq_len * seq_len * units,
            bytes_accessed=8 * seq_len * units * 2,
            transcendentals=seq_len * seq_len // 2,
        ),
    )(query, key, value, d_head, head_sum, logs, expand_head, cosines, sines)


def finish_kernel(query, expand, out_rows, query_out, expand_out, out_out):
    heads, units, width = query.shape
    query_out[...] = query[...].reshape(heads * units, width).astype(jnp.float32).T
    for at in range(heads):
        columns = expand.shape[2]
        expand_out[:, at * columns : (at + 1) * columns] = expand[at].astype(jnp.float32)
    out_out[...] = out_rows[...].reshape(out_out.shape).astype(jnp.float32)


def finish(query, expand, out_rows):
    heads, units, width = query.shape
    _, latents, columns = expand.shape
    _, rows, model = out_rows.shape
    return pl.pallas_call(
        finish_kernel,
        grid=(heads // 2,),
        out_shape=[
            jax.ShapeDtypeStruct((width, heads * units), jnp.float32),
            jax.ShapeDtypeStruct((latents, heads * columns), jnp.float32),
            jax.ShapeDtypeStruct((heads * rows, model), jnp.float32),
        ],
        in_specs=[
            pl.BlockSpec((2, units, width), lambda i: (i, 0, 0)),
            pl.BlockSpec((2, latents, columns), lambda i: (i, 0, 0)),
            pl.BlockSpec((2, rows, model), lambda i: (i, 0, 0)),
        ],
        out_specs=[
            pl.BlockSpec((width, 2 * units), lambda i: (0, i)),
            pl.BlockSpec((latents, 2 * columns), lambda i: (0, i)),
            pl.BlockSpec((2 * rows, model), lambda i: (i, 0)),
        ],
        compiler_params=pltpu.CompilerParams(vmem_limit_bytes=VMEM_LIMIT),
        cost_estimate=pl.CostEstimate(
            flops=0, bytes_accessed=6 * heads * units * width, transcendentals=0
        ),
    )(query, expand, out_rows)


def token_gather(rows):
    return lax.all_gather(rows, ("fsdp", "expert"), axis=0, tiled=True)


def split_body(
    tokens,
    routes,
    cotangent,
    attn_gain,
    w_query,
    latent_weight,
    latent_norm_gain,
    expand_weight,
    w_out,
    ffn_gain,
    w_router,
    shared_gate,
    shared_up,
    shared_down,
    expert_gate,
    expert_up,
    expert_down,
):
    rows = tokens.shape[1]
    experts = lax.axis_size("expert")
    shards = lax.axis_size("fsdp")
    position = lax.axis_index("expert")
    blocks = experts * shards
    seq_len = rows * experts
    capacity = shards * ((rows * TOPK * 4 + experts * 3 * shards - 1) // (experts * 3 * shards))
    head_units = PLAIN_UNITS + ROTARY_UNITS
    pair_units = PLAIN_UNITS + VALUE_UNITS
    feature_width = LATENT_WIDTH + ROTARY_UNITS
    scale = head_units ** (-0.5)

    shard = lax.axis_index("fsdp")
    first = shard == 0

    query_cols = lax.dynamic_slice_in_dim(w_query, position * head_units, head_units, 1)
    expand_cols = lax.dynamic_slice_in_dim(expand_weight, position * pair_units, pair_units, 1)
    owners = experts // shards
    lat_row = jnp.pad(latent_norm_gain, (0, w_query.shape[0] - latent_norm_gain.shape[0]))
    packed = jnp.concatenate(
        [latent_weight.T, query_cols.T, w_router.T, attn_gain[None], ffn_gain[None], lat_row[None]],
        axis=0,
    )
    packed = jnp.pad(packed, ((0, -packed.shape[0] % 32), (0, 0)))
    seq_rows, other_packed, other_expand = gather_rows(
        [tokens[0]], False, 0, swapped=[packed, expand_cols]
    )

    def whole(own, other, axis):
        return jnp.concatenate(
            [jnp.where(first, own, other), jnp.where(first, other, own)], axis=axis
        )

    lat_half = latent_norm_gain.shape[0]
    at = feature_width + head_units
    packed_rows = whole(packed, other_packed, 1)
    expand_head = whole(expand_cols, other_expand, 0)
    w_front = packed_rows[:at]
    w_latent = packed_rows[:feature_width]
    router_rows = packed_rows[at:]
    wrout = packed_rows[at : at + experts]
    g_attn = packed_rows[at + experts].astype(jnp.float32)
    g_ffn = packed_rows[at + experts + 1].astype(jnp.float32)
    lat_row = packed_rows[at + experts + 2]
    g_lat = jnp.concatenate(
        [lat_row[:lat_half], lat_row[w_query.shape[0] : w_query.shape[0] + lat_half]]
    ).astype(jnp.float32)
    units = shared_down.shape[0]

    core = lax.rem(position, CORES)

    def by_cores(weight):
        size = weight.shape[0] // CORES
        own = lax.dynamic_slice_in_dim(weight, core * size, size, 0)
        own = lax.all_gather(own, "fsdp", axis=0, tiled=True)
        swap = [(index, index ^ 1) for index in range(experts)]
        return own, lax.ppermute(own, "expert", swap)

    def core_columns(value, which):
        size = value.shape[1] // (CORES * shards)
        parts = [
            lax.dynamic_slice_in_dim(value, (at * CORES + which) * size, size, 1)
            for at in range(shards)
        ]
        return jnp.concatenate(parts, axis=1)

    def in_order(own, other):
        lower, upper = jnp.where(core == 0, own, other), jnp.where(core == 0, other, own)
        size = own.shape[1] // shards
        parts = []
        for at in range(shards):
            parts += [lower[:, at * size : (at + 1) * size], upper[:, at * size : (at + 1) * size]]
        return jnp.concatenate(parts, axis=1)

    out_own, out_other = by_cores(w_out)
    grad_rows = cotangent[0]
    grad_out = grad_rows.astype(jnp.float32)
    own_routes = jnp.pad(routes[0], ((0, 0), (0, 128 - TOPK)), constant_values=-1)
    grad_rows = jnp.concatenate([grad_rows, own_routes.astype(jnp.bfloat16)], axis=1)
    seq_rows, grad_rows, shared_gate, shared_up = lax.optimization_barrier(
        (seq_rows, grad_rows, shared_gate, shared_up)
    )
    def to_columns(weight):
        parts = weight.reshape(weight.shape[0], blocks, units).transpose(1, 0, 2)
        return lax.all_to_all(
            parts, ("expert", "fsdp"), split_axis=0, concat_axis=0, tiled=True
        ).reshape(-1, units)

    sh_cols = to_columns(jnp.concatenate([shared_gate, shared_up], axis=0)).reshape(
        blocks, 2, shared_gate.shape[0], units
    )
    lanes = -(-units // 128) * 128
    sh_cols = jnp.pad(sh_cols, ((0, 0), (0, 0), (0, 0), (0, lanes - units)))
    shared_in = sh_cols.transpose(0, 2, 1, 3).reshape(MODEL_WIDTH, 2 * lanes)
    shared_out = jnp.pad(shared_down, ((0, lanes - units), (0, 0)))
    all_grads = token_gather(grad_rows)

    x_in = tokens[0].astype(jnp.float32)
    normed, inv_attn = norm_forward(x_in, g_attn)
    normed_in = normed.astype(jnp.bfloat16)
    half_units = ROTARY_UNITS // 2
    freqs = 10000.0 ** (-np.arange(half_units) * (2.0 / ROTARY_UNITS))
    angles = np.arange(seq_len)[:, None] * freqs[None, :]
    cosine_table = jnp.asarray(np.cos(angles), jnp.float32)
    sine_table = jnp.asarray(np.sin(angles), jnp.float32)
    cosines = jnp.asarray(np.concatenate([np.cos(angles)] * 2, axis=1), jnp.float32)
    sines = jnp.asarray(np.concatenate([-np.sin(angles), np.sin(angles)], axis=1), jnp.float32)
    (
        seq_normed,
        latent_rows,
        query,
        key,
        value,
        head_rows,
        head_sum,
        logs,
    ) = attend(
        seq_rows.reshape(seq_len, MODEL_WIDTH),
        g_attn[None],
        w_front,
        g_lat[None],
        expand_head,
        cosines,
        sines,
    )
    head_rows, shared_in = lax.optimization_barrier((head_rows, shared_in))
    heads = exchange(head_rows.reshape(experts, rows, VALUE_UNITS), 1)
    heads = heads.transpose(1, 0, 2).reshape(rows, experts * VALUE_UNITS)
    hidden = x_in + matrix_product(core_columns(heads, core), out_own)
    hidden = hidden + matrix_product(core_columns(heads, 1 - core), out_other)
    normed2, inv_ffn = norm_forward(hidden, g_ffn)
    normed_ffn = normed2.astype(jnp.bfloat16)
    router = jax.nn.softmax(outer_product(normed_ffn, wrout), axis=-1)

    (all_normed,) = gather_rows([normed_ffn], True, 2)
    w_query, all_normed = lax.optimization_barrier((w_query, all_normed))
    query_own, query_other = by_cores(w_query)
    (
        out_part,
        d_part,
        ex_rows,
        ex_grads,
        scaled_act,
        d_pre_gate,
        d_pre_up,
        g_shared_in,
        g_shared_out,
    ) = expert_phase(
        all_normed,
        all_grads.reshape(blocks, rows, -1),
        router_rows,
        expert_gate[0].T,
        expert_up[0].T,
        expert_down[0],
        shared_in,
        shared_out,
        capacity,
    )
    g_down = inner(scaled_act, ex_grads)
    g_gate = inner(d_pre_gate, ex_rows).T
    g_up = inner(d_pre_up, ex_rows).T
    (d_back,) = scatter_rows(d_part, True, 3)
    out_part, d_back = lax.optimization_barrier((out_part, d_back))
    out_sum = lax.psum_scatter(
        out_part.reshape(blocks * rows, MODEL_WIDTH),
        ("fsdp", "expert"),
        scatter_dimension=0,
        tiled=True,
    )
    output = hidden + out_sum.astype(jnp.float32)
    d_normed_ffn = d_back[:, :MODEL_WIDTH]
    d_router = d_back[:, MODEL_WIDTH : MODEL_WIDTH + experts]

    d_logits = (router * (d_router - jnp.sum(router * d_router, axis=1, keepdims=True))).astype(
        jnp.bfloat16
    )
    g_router = inner(d_logits, normed_ffn)
    d_normed_ffn = d_normed_ffn + matrix_product(d_logits, wrout)
    d_hidden_norm, g_ffn_grad = norm_backward(hidden, inv_ffn, g_ffn, d_normed_ffn)
    d_hidden = grad_out + d_hidden_norm
    d_attn = d_hidden.astype(jnp.bfloat16)

    d_heads = in_order(outer_product(d_attn, out_own), outer_product(d_attn, out_other))
    d_heads = d_heads.astype(jnp.bfloat16)
    d_heads = d_heads.reshape(rows, experts, VALUE_UNITS).transpose(1, 0, 2)
    d_head = exchange(d_heads, 4).reshape(seq_len, VALUE_UNITS)
    out_grad_part = inner(heads, d_attn).astype(jnp.bfloat16)
    d_query_full, d_pairs, d_keys = attend_back(
        query, key, value, d_head, head_sum, logs, expand_head, cosines, sines
    )
    g_expand_head = inner(latent_rows, d_pairs)
    g_query_head = inner(d_query_full, seq_normed).astype(jnp.bfloat16)
    g_expand_head = g_expand_head.astype(jnp.bfloat16)

    def half_of(whole, which, axis):
        size = whole.shape[axis] // shards
        return lax.dynamic_slice_in_dim(whole, which * size, size, axis)

    own_d_query, d_sums, own_out, other_query, other_expand = exchange_and_sums(
        d_query_full.reshape(experts, rows, head_units),
        d_keys.reshape(experts, rows, -1),
        out_grad_part.reshape(blocks, -1, MODEL_WIDTH),
        [half_of(g_query_head, 1 - shard, 1), half_of(g_expand_head, 1 - shard, 0)],
        5,
    )
    own_d_query = own_d_query.transpose(1, 0, 2).reshape(rows, experts * head_units)
    key_gradient = d_sums[:, :feature_width]
    d_normed_in = in_order(
        outer_product(own_d_query, query_own), outer_product(own_d_query, query_other)
    )

    def summed(own, other):
        return (own.astype(jnp.float32) + other.astype(jnp.float32)).astype(jnp.bfloat16)

    own_query = summed(half_of(g_query_head, shard, 1), other_query)
    own_expand = summed(half_of(g_expand_head, shard, 0), other_expand)
    own_out = own_out.astype(jnp.bfloat16)
    own_latent = outer_product(normed_in, w_latent[:LATENT_WIDTH])
    own_cosine = lax.dynamic_slice_in_dim(cosine_table, position * rows, rows, 0)
    own_sine = lax.dynamic_slice_in_dim(sine_table, position * rows, rows, 0)
    inv_lat = lax.rsqrt(jnp.mean(own_latent * own_latent, axis=-1, keepdims=True) + EPS)
    d_compact, g_lat_grad = norm_backward(
        own_latent, inv_lat, g_lat, key_gradient[:, :LATENT_WIDTH]
    )
    d_rope = reverse_rotary(key_gradient[:, LATENT_WIDTH:], own_cosine, own_sine)
    d_latent_full = jnp.concatenate([d_compact, d_rope], axis=-1).astype(jnp.bfloat16)
    g_latent = inner(d_latent_full, normed_in)
    d_normed_in = d_normed_in + matrix_product(d_latent_full, w_latent)
    d_norm_in, g_attn_grad = norm_backward(x_in, inv_attn, g_attn, d_normed_in)
    d_tokens = (d_hidden + d_norm_in).astype(jnp.bfloat16)

    half = MODEL_WIDTH // blocks
    cols = lax.all_to_all(
        g_shared_in.reshape(blocks, half, 2 * lanes),
        ("expert", "fsdp"),
        split_axis=0,
        concat_axis=0,
        tiled=True,
    )
    cols = cols.transpose(1, 0, 2).astype(jnp.float32)
    r_sgate = cols[:, :, :units].reshape(half, blocks * units)
    r_sup = cols[:, :, lanes : lanes + units].reshape(half, blocks * units)
    g_sdown = g_shared_out[:units]
    model_half = MODEL_WIDTH // shards
    small_rows = jnp.concatenate([g_latent, g_router, g_attn_grad[None], g_ffn_grad[None]], axis=0)
    used = small_rows.shape[0]
    share = 2 * 32 * (-(-(used + 1) // (2 * 32 * experts)))

    def rows_for(which):
        here = small_rows[:, which * model_half : (which + 1) * model_half]
        lat = jnp.pad(
            g_lat_grad[which * lat_half : (which + 1) * lat_half], (0, model_half - lat_half)
        )
        full = jnp.concatenate([here, lat[None]], axis=0).astype(jnp.bfloat16)
        full = jnp.pad(full, ((0, experts * share - used - 1), (0, 0)))
        return full.reshape(experts, share, model_half)

    small_part = jnp.concatenate([rows_for(which) for which in range(shards)], axis=0)
    r_query, r_expand, r_out, small_sum = gather_and_scatter(
        [own_query, own_expand, own_out], small_part, 6
    )
    (small_all,) = gather_rows([small_sum.astype(jnp.bfloat16)], False, 7)
    r_query, r_expand, r_out = finish(r_query, r_expand, r_out)
    small_all = small_all.reshape(experts * share, model_half).astype(jnp.float32)
    return (
        output.astype(jnp.bfloat16)[None],
        d_tokens[None],
        small_all[feature_width + experts],
        r_query,
        small_all[:feature_width].T,
        small_all[feature_width + experts + 2, :lat_half],
        r_expand,
        r_out,
        small_all[feature_width + experts + 1],
        small_all[feature_width : feature_width + experts].T,
        r_sgate,
        r_sup,
        g_sdown,
        g_gate[None],
        g_up[None],
        g_down[None],
    )


def solution(mesh):
    shape = (mesh.shape["expert"], mesh.shape["fsdp"])
    split = shape == (LINE * SQUARE * CORES, SQUARE) and shape[0] == HEAD_COUNT
    return jax.shard_map(
        split_body if split else body,
        mesh=mesh,
        in_specs=(
            P("fsdp", "expert", None),
            P("fsdp", "expert", None),
            P("fsdp", "expert", None),
            P("fsdp"),
            P("fsdp", None),
            P("fsdp", None),
            P("fsdp"),
            P("fsdp", None),
            P("fsdp", None),
            P("fsdp"),
            P("fsdp", None),
            P(("expert", "fsdp"), None),
            P(("expert", "fsdp"), None),
            P(("expert", "fsdp"), None),
            P("expert", None, "fsdp"),
            P("expert", None, "fsdp"),
            P("expert", "fsdp", None),
        ),
        out_specs=(
            P("fsdp", "expert", None),
            P("fsdp", "expert", None),
            P("fsdp"),
            P("fsdp", None),
            P("fsdp", None),
            P("fsdp"),
            P("fsdp", None),
            P("fsdp", None),
            P("fsdp"),
            P("fsdp", None),
            P(("expert", "fsdp"), None),
            P(("expert", "fsdp"), None),
            P(("expert", "fsdp"), None),
            P("expert", None, "fsdp"),
            P("expert", None, "fsdp"),
            P("expert", "fsdp", None),
        ),
        check_vma=False,
    )
```

```python
import functools

import jax
import jax.numpy as jnp
import numpy as np
from jax import lax
from jax.experimental import pallas as pl
from jax.experimental.pallas import tpu as pltpu
from jax.sharding import PartitionSpec as P

MODEL_WIDTH = 2048
HEAD_COUNT = 16
PLAIN_UNITS = 128
ROTARY_UNITS = 64
VALUE_UNITS = 128
LATENT_WIDTH = 512
TOPK = 6


EPS = 1e-06


def matrix_product(left, right):
    return jnp.dot(left, right, preferred_element_type=jnp.float32)


def inner(left, right):
    return lax.dot_general(
        left, right, (((0,), (0,)), ((), ())), preferred_element_type=jnp.float32
    )


def outer_product(left, right):
    return lax.dot_general(
        left, right, (((1,), (1,)), ((), ())), preferred_element_type=jnp.float32
    )


def norm_forward(value, gain):
    inverse = lax.rsqrt(jnp.mean(value * value, axis=-1, keepdims=True) + EPS)
    return (value * inverse * gain, inverse)


def norm_backward(value, inverse, gain, grad):
    unit = value * inverse
    scaled = grad * gain
    d_value = inverse * (scaled - unit * jnp.mean(scaled * unit, axis=-1, keepdims=True))
    return (d_value, jnp.sum(grad * unit, axis=0))


def rope_tables(positions):
    half = ROTARY_UNITS // 2
    freqs = 10000.0 ** (-jnp.arange(half, dtype=jnp.float32) * (2.0 / ROTARY_UNITS))
    angles = positions.astype(jnp.float32)[:, None] * freqs[None, :]
    return (jnp.cos(angles), jnp.sin(angles))


def apply_rotary(value, cosine_table, sine_table):
    half = ROTARY_UNITS // 2
    first = value[..., :half]
    second = value[..., half:]
    return jnp.concatenate(
        [first * cosine_table - second * sine_table, first * sine_table + second * cosine_table],
        axis=-1,
    )


def reverse_rotary(grad, cosine_table, sine_table):
    half = ROTARY_UNITS // 2
    first = grad[..., :half]
    second = grad[..., half:]
    return jnp.concatenate(
        [first * cosine_table + second * sine_table, second * cosine_table - first * sine_table],
        axis=-1,
    )


def silu_parts(value):
    sigma = jax.nn.sigmoid(value)
    return (value * sigma, sigma * (1.0 + value * (1.0 - sigma)))


def body(
    tokens,
    routes,
    cotangent,
    attn_gain,
    w_query,
    latent_weight,
    latent_norm_gain,
    expand_weight,
    w_out,
    ffn_gain,
    w_router,
    shared_gate,
    shared_up,
    shared_down,
    expert_gate,
    expert_up,
    expert_down,
):
    device_local = tokens.shape[1]
    experts = lax.axis_size("expert")
    shards = lax.axis_size("fsdp")
    position = lax.axis_index("expert")
    capacity = shards * (
        (device_local * TOPK * 4 + experts * 3 * shards - 1) // (experts * 3 * shards)
    )
    seq_len = device_local * experts
    feature_width = LATENT_WIDTH + ROTARY_UNITS
    scale = (PLAIN_UNITS + ROTARY_UNITS) ** (-0.5)
    attention_gain_grad, wq, wlat, g_lat, expand_matrix, wout, g_ffn, wrout = (
        lax.all_gather(attn_gain, "fsdp", axis=0, tiled=True),
        lax.all_gather(w_query, "fsdp", axis=0, tiled=True),
        lax.all_gather(latent_weight, "fsdp", axis=0, tiled=True),
        lax.all_gather(latent_norm_gain, "fsdp", axis=0, tiled=True),
        lax.all_gather(expand_weight, "fsdp", axis=0, tiled=True),
        lax.all_gather(w_out, "fsdp", axis=0, tiled=True),
        lax.all_gather(ffn_gain, "fsdp", axis=0, tiled=True),
        lax.all_gather(w_router, "fsdp", axis=0, tiled=True),
    )
    sgate, sup, sdown = (
        lax.all_gather(shared_gate, ("expert", "fsdp"), axis=0, tiled=True),
        lax.all_gather(shared_up, ("expert", "fsdp"), axis=0, tiled=True),
        lax.all_gather(shared_down, ("expert", "fsdp"), axis=0, tiled=True),
    )
    attention_gain_grad = attention_gain_grad.astype(jnp.float32)
    g_lat = g_lat.astype(jnp.float32)
    g_ffn = g_ffn.astype(jnp.float32)
    x_in = tokens[0].astype(jnp.float32)
    grad_out = cotangent[0].astype(jnp.float32)
    positions = position * device_local + jnp.arange(device_local, dtype=jnp.int32)
    cosine_table, sine_table = rope_tables(positions)
    normed, inv_attn = norm_forward(x_in, attention_gain_grad)
    normed_in = normed.astype(jnp.bfloat16)
    query_full = matrix_product(normed_in, wq).reshape(
        device_local, HEAD_COUNT, PLAIN_UNITS + ROTARY_UNITS
    )
    query_nope = query_full[:, :, :PLAIN_UNITS].astype(jnp.bfloat16)
    expanded_latent = expand_matrix.reshape(LATENT_WIDTH, HEAD_COUNT, PLAIN_UNITS + VALUE_UNITS)
    key_part = expanded_latent[:, :, :PLAIN_UNITS]
    value_part = expanded_latent[:, :, PLAIN_UNITS:]
    query_latent = jnp.einsum(
        "thd,chd->thc", query_nope, key_part, preferred_element_type=jnp.float32
    )
    query_rope = apply_rotary(
        query_full[:, :, PLAIN_UNITS:], cosine_table[:, None, :], sine_table[:, None, :]
    )
    token_rows = device_local * HEAD_COUNT
    query = (
        jnp.concatenate([query_latent, query_rope], axis=-1)
        .astype(jnp.bfloat16)
        .reshape(token_rows, feature_width)
    )
    latent_complete = matrix_product(normed_in, wlat)
    packed_rows = latent_complete[:, :LATENT_WIDTH]
    latent_state, inv_lat = norm_forward(packed_rows, g_lat)
    rotary_key = apply_rotary(latent_complete[:, LATENT_WIDTH:], cosine_table, sine_table)
    key = jnp.concatenate([latent_state, rotary_key], axis=-1).astype(jnp.bfloat16)
    keys_all = lax.all_gather(key, "expert", axis=0, tiled=True)
    block = min(512, seq_len)
    token_tally = (position * device_local + device_local + block - 1) // block
    q_pos = position * device_local + jnp.arange(token_rows, dtype=jnp.int32) // HEAD_COUNT

    def scores_of(index):
        key_rows = lax.dynamic_slice_in_dim(keys_all, index * block, block, 0)
        raw = outer_product(query, key_rows)
        k_pos = index * block + jnp.arange(block, dtype=jnp.int32)
        valid = k_pos[None, :] <= q_pos[:, None]
        return (jnp.where(valid, raw * scale, -1e30), key_rows)

    def stats_step(index, carry):
        top, total = carry
        scores, unused = scores_of(index)
        new_top = jnp.maximum(top, jnp.max(scores, axis=1))
        total = total * jnp.exp(top - new_top) + jnp.sum(jnp.exp(scores - new_top[:, None]), axis=1)
        return (new_top, total)

    top, total = lax.fori_loop(
        0,
        token_tally,
        stats_step,
        (jnp.full((token_rows,), -1e30, jnp.float32), jnp.zeros((token_rows,), jnp.float32)),
    )
    log_total = top + jnp.log(total)

    def mixing_update(index, running_total):
        scores, key_rows = scores_of(index)
        weight_arrays = jnp.exp(scores - log_total[:, None]).astype(jnp.bfloat16)
        return running_total + matrix_product(weight_arrays, key_rows[:, :LATENT_WIDTH])

    mixed_output_sum = lax.fori_loop(
        0, token_tally, mixing_update, jnp.zeros((token_rows, LATENT_WIDTH), jnp.float32)
    )
    mixed_output = mixed_output_sum.astype(jnp.bfloat16).reshape(
        device_local, HEAD_COUNT, LATENT_WIDTH
    )
    heads = jnp.einsum("thc,chv->thv", mixed_output, value_part, preferred_element_type=jnp.float32)
    heads = heads.reshape(device_local, HEAD_COUNT * VALUE_UNITS).astype(jnp.bfloat16)
    hidden = x_in + matrix_product(heads, wout)
    normed2, inv_ffn = norm_forward(hidden, g_ffn)
    normed_ffn = normed2.astype(jnp.bfloat16)
    logits = matrix_product(normed_ffn, wrout)
    router = jax.nn.softmax(logits, axis=-1)
    own_routes = routes[0]
    names = jnp.arange(experts, dtype=jnp.int32)
    chosen = (own_routes[:, :, None] == names[None, None, :]).astype(jnp.float32)
    gates = jnp.sum(chosen * router[:, None, :], axis=-1)
    hits = (own_routes.reshape(device_local * TOPK)[:, None] == names[None, :]).astype(jnp.int32)
    slot = jnp.sum((jnp.cumsum(hits, axis=0) - hits) * hits, axis=1)
    place = own_routes.reshape(device_local * TOPK) * capacity + slot
    token_of = jnp.arange(device_local * TOPK, dtype=jnp.int32) // TOPK
    table = jnp.full((experts * capacity,), device_local, jnp.int32).at[place].set(token_of)
    padded = jnp.concatenate([normed_ffn, jnp.zeros((1, MODEL_WIDTH), jnp.bfloat16)], axis=0)
    buffer = padded[table].reshape(experts, capacity, MODEL_WIDTH)
    w_g, w_u, w_d = (expert_gate[0], expert_up[0], expert_down[0])

    def spread(values):
        return jnp.broadcast_to(values[:, None], (experts, shards, capacity, MODEL_WIDTH)).reshape(
            experts * shards, capacity, MODEL_WIDTH
        )

    def collect(back):
        return jnp.sum(back.reshape(experts, shards, capacity, MODEL_WIDTH), axis=1).reshape(
            experts * capacity, MODEL_WIDTH
        )

    received = lax.all_to_all(
        spread(buffer), ("expert", "fsdp"), split_axis=0, concat_axis=0, tiled=True
    )
    ex_rows = received.reshape(-1, MODEL_WIDTH)
    pre_gate = matrix_product(ex_rows, w_g)
    pre_up = matrix_product(ex_rows, w_u)
    act_gate, slope = silu_parts(pre_gate)
    ex_act = (act_gate * pre_up).astype(jnp.bfloat16)
    ex_out = matrix_product(ex_act, w_d).reshape(received.shape)
    returned = lax.all_to_all(
        ex_out.astype(jnp.bfloat16), ("expert", "fsdp"), split_axis=0, concat_axis=0, tiled=True
    ).astype(ex_out.dtype)
    results = collect(returned)
    picked = results[place].reshape(device_local, TOPK, MODEL_WIDTH)
    routed = jnp.sum(gates[:, :, None] * picked, axis=1)
    sh_gate = matrix_product(normed_ffn, sgate)
    sh_up = matrix_product(normed_ffn, sup)
    sh_silu, sh_slope = silu_parts(sh_gate)
    sh_act = (sh_silu * sh_up).astype(jnp.bfloat16)
    shared = matrix_product(sh_act, sdown)
    output = hidden + routed + shared
    d_shared = grad_out.astype(jnp.bfloat16)
    shared_down_gradient = inner(sh_act, d_shared)
    d_sh_act = outer_product(d_shared, sdown)
    d_sh_gate = (d_sh_act * sh_up * sh_slope).astype(jnp.bfloat16)
    d_sh_up = (d_sh_act * sh_silu).astype(jnp.bfloat16)
    shared_gate_gradient = inner(normed_ffn, d_sh_gate)
    shared_up_gradient = inner(normed_ffn, d_sh_up)
    d_normed_ffn = outer_product(d_sh_gate, sgate) + outer_product(d_sh_up, sup)
    d_picked = (
        (gates[:, :, None] * grad_out[:, None, :])
        .astype(jnp.bfloat16)
        .reshape(device_local * TOPK, MODEL_WIDTH)
    )
    d_gates = jnp.sum(picked * grad_out[:, None, :], axis=2)
    d_buffer = (
        jnp.zeros((experts * capacity, MODEL_WIDTH), jnp.bfloat16)
        .at[place]
        .set(d_picked)
        .reshape(experts, capacity, MODEL_WIDTH)
    )
    d_received = lax.all_to_all(
        spread(d_buffer), ("expert", "fsdp"), split_axis=0, concat_axis=0, tiled=True
    )
    d_rows = d_received.reshape(-1, MODEL_WIDTH)
    d_act = outer_product(d_rows, w_d)
    g_down = inner(ex_act, d_rows)
    d_pre_gate = (d_act * pre_up * slope).astype(jnp.bfloat16)
    d_pre_up = (d_act * act_gate).astype(jnp.bfloat16)
    g_gate = inner(ex_rows, d_pre_gate)
    g_up = inner(ex_rows, d_pre_up)
    d_ex_rows = (outer_product(d_pre_gate, w_g) + outer_product(d_pre_up, w_u)).reshape(
        received.shape
    )
    d_returned = lax.all_to_all(
        d_ex_rows.astype(jnp.bfloat16), ("expert", "fsdp"), split_axis=0, concat_axis=0, tiled=True
    ).astype(d_ex_rows.dtype)
    d_results = collect(d_returned)
    d_normed_ffn = d_normed_ffn + jnp.sum(
        d_results[place].reshape(device_local, TOPK, MODEL_WIDTH), axis=1
    )
    d_router = jnp.sum(chosen * d_gates[:, :, None], axis=1)
    d_logits = (router * (d_router - jnp.sum(router * d_router, axis=1, keepdims=True))).astype(
        jnp.bfloat16
    )
    router_weight_gradient = inner(normed_ffn, d_logits)
    d_normed_ffn = d_normed_ffn + outer_product(d_logits, wrout)
    d_hidden_norm, g_ffn_grad = norm_backward(hidden, inv_ffn, g_ffn, d_normed_ffn)
    d_hidden = grad_out + d_hidden_norm
    d_attn = d_hidden.astype(jnp.bfloat16)
    output_weight_gradient = inner(heads, d_attn)
    d_heads = (
        outer_product(d_attn, wout)
        .astype(jnp.bfloat16)
        .reshape(device_local, HEAD_COUNT, VALUE_UNITS)
    )
    value_weight_gradient = jnp.einsum(
        "thc,thv->chv", mixed_output, d_heads, preferred_element_type=jnp.float32
    )
    mixed_gradient = jnp.einsum(
        "thv,chv->thc", d_heads, value_part, preferred_element_type=jnp.float32
    )
    mixed_gradient = mixed_gradient.astype(jnp.bfloat16).reshape(token_rows, LATENT_WIDTH)
    delta = jnp.sum(mixed_gradient.astype(jnp.float32) * mixed_output_sum, axis=1)

    def back_step(index, carry):
        d_query_acc, d_keys_acc = carry
        scores, key_rows = scores_of(index)
        weight_arrays = jnp.exp(scores - log_total[:, None])
        weight_gradients = outer_product(mixed_gradient, key_rows[:, :LATENT_WIDTH])
        d_scores = (weight_arrays * (weight_gradients - delta[:, None]) * scale).astype(
            jnp.bfloat16
        )
        d_query_acc = d_query_acc + matrix_product(d_scores, key_rows)
        d_values = inner(weight_arrays.astype(jnp.bfloat16), mixed_gradient)
        d_block = inner(d_scores, query) + jnp.concatenate(
            [d_values, jnp.zeros((block, ROTARY_UNITS), jnp.float32)], axis=1
        )
        previous = lax.dynamic_slice_in_dim(d_keys_acc, index * block, block, 0)
        return (
            d_query_acc,
            lax.dynamic_update_slice_in_dim(d_keys_acc, previous + d_block, index * block, 0),
        )

    d_query, d_keys = lax.fori_loop(
        0,
        token_tally,
        back_step,
        (
            jnp.zeros((token_rows, feature_width), jnp.float32),
            jnp.zeros((seq_len, feature_width), jnp.float32),
        ),
    )
    key_gradient = lax.psum_scatter(
        d_keys.astype(jnp.bfloat16), "expert", scatter_dimension=0, tiled=True
    )
    query_up_gradient = d_query.astype(jnp.bfloat16).reshape(
        device_local, HEAD_COUNT, feature_width
    )
    query_latent_gradient = query_up_gradient[:, :, :LATENT_WIDTH]
    key_weight_gradient = jnp.einsum(
        "thc,thd->chd", query_latent_gradient, query_nope, preferred_element_type=jnp.float32
    )
    d_q_nope = jnp.einsum(
        "thc,chd->thd", query_latent_gradient, key_part, preferred_element_type=jnp.float32
    )
    d_q_rope = reverse_rotary(
        query_up_gradient[:, :, LATENT_WIDTH:].astype(jnp.float32),
        cosine_table[:, None, :],
        sine_table[:, None, :],
    )
    d_query_full = (
        jnp.concatenate([d_q_nope, d_q_rope], axis=-1)
        .astype(jnp.bfloat16)
        .reshape(device_local, HEAD_COUNT * (PLAIN_UNITS + ROTARY_UNITS))
    )
    query_weight_gradient = inner(normed_in, d_query_full)
    d_normed_in = outer_product(d_query_full, wq)
    latent_gradient = key_gradient[:, :LATENT_WIDTH].astype(jnp.float32)
    rotary_key_gradient = reverse_rotary(
        key_gradient[:, LATENT_WIDTH:].astype(jnp.float32), cosine_table, sine_table
    )
    d_compact, g_lat_grad = norm_backward(packed_rows, inv_lat, g_lat, latent_gradient)
    d_latent_full = jnp.concatenate([d_compact, rotary_key_gradient], axis=-1).astype(jnp.bfloat16)
    latent_weight_gradient = inner(normed_in, d_latent_full)
    d_normed_in = d_normed_in + outer_product(d_latent_full, wlat)
    d_norm_in, g_attn_grad = norm_backward(x_in, inv_attn, attention_gain_grad, d_normed_in)
    d_tokens = (d_hidden + d_norm_in).astype(jnp.bfloat16)
    expand_weight_gradient = jnp.concatenate(
        [key_weight_gradient, value_weight_gradient], axis=-1
    ).reshape(LATENT_WIDTH, HEAD_COUNT * (PLAIN_UNITS + VALUE_UNITS))
    r_sgate, r_sup, r_sdown = (
        lax.psum_scatter(shared_gate_gradient, ("expert", "fsdp"), scatter_dimension=0, tiled=True),
        lax.psum_scatter(shared_up_gradient, ("expert", "fsdp"), scatter_dimension=0, tiled=True),
        lax.psum_scatter(shared_down_gradient, ("expert", "fsdp"), scatter_dimension=0, tiled=True),
    )
    r_attn, r_query, r_latent, r_lgain, r_expand, r_out, r_fgain, r_router = (
        lax.psum_scatter(
            g_attn_grad.astype(jnp.bfloat16), "fsdp", scatter_dimension=0, tiled=True
        ).astype(jnp.float32),
        lax.psum_scatter(
            query_weight_gradient.astype(jnp.bfloat16), "fsdp", scatter_dimension=0, tiled=True
        ).astype(jnp.float32),
        lax.psum_scatter(
            latent_weight_gradient.astype(jnp.bfloat16), "fsdp", scatter_dimension=0, tiled=True
        ).astype(jnp.float32),
        lax.psum_scatter(
            g_lat_grad.astype(jnp.bfloat16), "fsdp", scatter_dimension=0, tiled=True
        ).astype(jnp.float32),
        lax.psum_scatter(
            expand_weight_gradient.astype(jnp.bfloat16), "fsdp", scatter_dimension=0, tiled=True
        ).astype(jnp.float32),
        lax.psum_scatter(
            output_weight_gradient.astype(jnp.bfloat16), "fsdp", scatter_dimension=0, tiled=True
        ).astype(jnp.float32),
        lax.psum_scatter(
            g_ffn_grad.astype(jnp.bfloat16), "fsdp", scatter_dimension=0, tiled=True
        ).astype(jnp.float32),
        lax.psum_scatter(
            router_weight_gradient.astype(jnp.bfloat16), "fsdp", scatter_dimension=0, tiled=True
        ).astype(jnp.float32),
    )
    r_attn, r_query, r_latent, r_lgain, r_expand, r_out, r_fgain, r_router = (
        lax.psum(r_attn.astype(jnp.bfloat16), "expert").astype(jnp.float32),
        lax.psum(r_query.astype(jnp.bfloat16), "expert").astype(jnp.float32),
        lax.psum(r_latent.astype(jnp.bfloat16), "expert").astype(jnp.float32),
        lax.psum(r_lgain.astype(jnp.bfloat16), "expert").astype(jnp.float32),
        lax.psum(r_expand.astype(jnp.bfloat16), "expert").astype(jnp.float32),
        lax.psum(r_out.astype(jnp.bfloat16), "expert").astype(jnp.float32),
        lax.psum(r_fgain.astype(jnp.bfloat16), "expert").astype(jnp.float32),
        lax.psum(r_router.astype(jnp.bfloat16), "expert").astype(jnp.float32),
    )
    return (
        output.astype(jnp.bfloat16)[None],
        d_tokens[None],
        r_attn,
        r_query,
        r_latent,
        r_lgain,
        r_expand,
        r_out,
        r_fgain,
        r_router,
        r_sgate,
        r_sup,
        r_sdown,
        g_gate[None],
        g_up[None],
        g_down[None],
    )


LINE = 4
SQUARE = 2
CORES = 2
MESH = pl.DeviceIdType.MESH
VMEM_LIMIT = 56 * 1024 * 1024


class Place:
    def __init__(self):
        index = lax.axis_index("expert")
        self.y = lax.axis_index("fsdp")
        self.c = lax.rem(index, CORES)
        self.b = lax.rem(lax.div(index, CORES), SQUARE)
        self.a = lax.div(index, CORES * SQUARE)

    def device(self, da=0, db=0, dc=0, dy=0):
        b = 1 - self.b if db else self.b
        c = 1 - self.c if dc else self.c
        y = 1 - self.y if dy else self.y
        return (((self.a + da) * SQUARE + b) * CORES + c, y)

    def block(self, full, a, db=0, dc=0, dy=0):
        b = 1 - self.b if db else self.b
        c = 1 - self.c if dc else self.c
        y = 1 - self.y if dy else self.y
        flat = (a * SQUARE + b) * CORES + c
        return y * (LINE * SQUARE * CORES) + flat if full else flat

    def greet(self, with_y):
        barrier = pltpu.get_barrier_semaphore()
        near = [dict(db=1), dict(dc=1)] + ([dict(dy=1)] if with_y else [])
        for step in near:
            pl.semaphore_signal(barrier, inc=1, device_id=self.device(**step), device_id_type=MESH)

        @pl.when(self.a > 0)
        def _():
            pl.semaphore_signal(barrier, inc=1, device_id=self.device(da=-1), device_id_type=MESH)

        @pl.when(self.a < LINE - 1)
        def _():
            pl.semaphore_signal(barrier, inc=1, device_id=self.device(da=1), device_id_type=MESH)

        ends = jnp.logical_or(self.a == 0, self.a == LINE - 1).astype(jnp.int32)
        pl.semaphore_wait(barrier, len(near) + 2 - ends)


class Sender:
    def __init__(self, place, sems):
        self.place, self.sems, self.pending = place, sems, []

    def send(self, src, dst, recv_sem, step, cond=None):
        sem = self.sems.at[len(self.pending)]

        def make():
            return pltpu.make_async_remote_copy(
                src_ref=src,
                dst_ref=dst,
                send_sem=sem,
                recv_sem=recv_sem,
                device_id=self.place.device(**step),
                device_id_type=MESH,
            )

        def start():
            make().start()

        guarded(cond, start)
        self.pending.append((cond, lambda: make().wait_send()))

    def arrived(self, dst, recv_sem):
        pltpu.make_async_remote_copy(
            src_ref=dst,
            dst_ref=dst,
            send_sem=self.sems.at[0],
            recv_sem=recv_sem,
            device_id=self.place.device(dc=1),
            device_id_type=MESH,
        ).wait_recv()

    def finish(self):
        for cond, wait in self.pending:
            guarded(cond, wait)


def guarded(cond, action):
    if cond is None:
        action()
    else:
        pl.when(cond)(action)


def both(first, second):
    if first is None or second is None:
        return second if first is None else first
    return jnp.logical_and(first, second)


def gather_ticks(place, sender, full, gated, ins, outs, local_sems, recv_sems):
    a = place.a
    count = len(ins)

    def own_copy(at):
        return pltpu.make_async_copy(
            ins[at], outs[at].at[place.block(full, a)], local_sems.at[at]
        )

    def chunk(at, block, half):
        size = ins[at].shape[0] // 2
        return outs[at].at[block, pl.ds(half * size, size)]

    def sem_of(at, block, half):
        return recv_sems.at[at, block * 2 + half]

    def forward(at, block, half, src, step, cond=None):
        sender.send(src, chunk(at, block, half), sem_of(at, block, half), step, cond)

    def receive(at, block, half, cond):
        guarded(cond, lambda: sender.arrived(chunk(at, block, half), sem_of(at, block, half)))

    def held_by(at, delta, cond):
        if at not in gated:
            return cond
        return both(cond, lax.div(a + delta, LINE // 2) == place.y)

    def from_line(delta, always):
        for half in range(2):
            for at in range(count):
                block = place.block(full, a + delta)
                cond = held_by(at, delta, always)
                size = ins[at].shape[0] // 2
                if delta == 0:
                    src = ins[at].at[pl.ds(half * size, size)]
                else:
                    receive(at, block, half, cond)
                    src = chunk(at, block, half)
                if delta <= 0:
                    forward(at, block, half, src, dict(da=1), both(cond, a < LINE - 1))
                if delta >= 0:
                    forward(at, block, half, src, dict(da=-1), both(cond, a > 0))
                forward(at, block, half, src, dict(db=1), cond)
                if full:
                    forward(at, block, half, src, dict(dy=1), cond)
                forward(at, block, half, src, dict(dc=1), cond)

    def from_side(delta, always):
        for half in range(2):
            for at in range(count):
                cond = held_by(at, delta, always)
                block = place.block(full, a + delta, db=1)
                receive(at, block, half, cond)
                if full and half == 0:
                    forward(at, block, half, chunk(at, block, half), dict(dy=1), cond)
                forward(at, block, half, chunk(at, block, half), dict(dc=1), cond)
                if full:
                    block = place.block(full, a + delta, dy=1)
                    receive(at, block, half, cond)
                    if half == 1:
                        forward(at, block, half, chunk(at, block, half), dict(db=1), cond)
                    forward(at, block, half, chunk(at, block, half), dict(dc=1), cond)

    def from_corner(delta, always):
        for half in range(2):
            for at in range(count):
                cond = held_by(at, delta, always)
                block = place.block(True, a + delta, db=1, dy=1)
                receive(at, block, half, cond)
                forward(at, block, half, chunk(at, block, half), dict(dc=1), cond)

    def from_sibling(delta, always):
        for half in range(2):
            for at in range(count):
                cond = held_by(at, delta, always)
                for db in range(2):
                    for dy in range(2 if full else 1):
                        receive(at, place.block(full, a + delta, db=db, dc=1, dy=dy), half, cond)

    rounds = [[(0, None)]]
    for s in range(1, LINE):
        rounds.append([(-s, a >= s), (s, a + s < LINE)])
    stages = [from_line, from_side] + ([from_corner] if full else []) + [from_sibling]

    def tick(number):
        if number == 0:
            for at in range(count):
                own_copy(at).start()
        for level, stage in enumerate(stages):
            if 0 <= number - level < len(rounds):
                for delta, cond in rounds[number - level]:
                    stage(delta, cond)
        if number == len(rounds) + len(stages) - 2:
            for at in range(count):
                own_copy(at).wait()

    return [functools.partial(tick, number) for number in range(len(rounds) + len(stages) - 1)]


def send_pairs(sender, ins, outs, sems):
    for at, (src, dst) in enumerate(zip(ins, outs)):
        sender.send(src, dst, sems.at[at], dict(dy=1))


def take_pairs(sender, outs, sems):
    for at, dst in enumerate(outs):
        sender.arrived(dst, sems.at[at])


def gather_kernel(full, count, pairs, gated, *refs):
    ins, outs = refs[: count + pairs], refs[count + pairs : 2 * (count + pairs)]
    local_sems, send_sems, recv_sems, pair_sems = refs[2 * (count + pairs) :]
    place = Place()
    sender = Sender(place, send_sems)
    place.greet(full or pairs > 0)
    send_pairs(sender, ins[count:], outs[count:], pair_sems)
    for tick in gather_ticks(
        place, sender, full, gated, ins[:count], outs[:count], local_sems, recv_sems
    ):
        tick()
    take_pairs(sender, outs[count:], pair_sems)
    sender.finish()


def gather_rows(arrays, full, collective_id, swapped=(), gated=()):
    blocks = LINE * SQUARE * CORES * (SQUARE if full else 1)
    count, pairs = len(arrays), len(swapped)
    lines = 2 * LINE - 1
    sends = pairs + count * lines * 2 * (9 if full else 5)
    moved = sum(blocks * 2 * x.size * x.dtype.itemsize for x in arrays)
    return pl.pallas_call(
        functools.partial(gather_kernel, full, count, pairs, gated),
        out_shape=[jax.ShapeDtypeStruct((blocks,) + x.shape, x.dtype) for x in arrays]
        + [jax.ShapeDtypeStruct(x.shape, x.dtype) for x in swapped],
        in_specs=[pl.BlockSpec(memory_space=pl.ANY)] * (count + pairs),
        out_specs=[pl.BlockSpec(memory_space=pl.ANY)] * (count + pairs),
        scratch_shapes=[
            pltpu.SemaphoreType.DMA((count,)),
            pltpu.SemaphoreType.DMA((sends,)),
            pltpu.SemaphoreType.DMA((count, blocks * 2)),
            pltpu.SemaphoreType.DMA((max(pairs, 1),)),
        ],
        compiler_params=pltpu.CompilerParams(collective_id=collective_id, has_side_effects=True),
        cost_estimate=pl.CostEstimate(flops=0, bytes_accessed=6 * moved, transcendentals=0),
    )(*arrays, *swapped)


def add_rows(target, sources, size):
    def step(at, carry):
        rows = pl.ds(pl.multiple_of(at * 16, 16), 16)
        total = sources[0][rows, :].astype(jnp.float32)
        for source in sources[1:]:
            total = total + source[rows, :].astype(jnp.float32)
        target[rows, :] = total.astype(target.dtype)
        return carry

    lax.fori_loop(0, size // 16, step, 0)


def scatter_ticks(place, sender, full, part, out, scratch):
    mine, got, side, up, down, load_sems, recv_sems = scratch
    a = place.a
    kinds = 4 if full else 2
    size = part.shape[1]
    half = size // 2
    order = [LINE - 1, 0, LINE - 2, 1]
    walk = (3, 1, 2, 0) if full else (1, 0)

    def sem_of(group, target, kind):
        return recv_sems.at[group, target * 4 + kind]

    def load(target, kind):
        block = place.block(full, target, db=kind % 2, dy=kind // 2)
        return pltpu.make_async_copy(
            part.at[block], mine.at[target, kind], load_sems.at[target * 4 + kind]
        )

    def begin():
        for target in order:
            for kind in walk:
                load(target, kind).start()
                block = place.block(full, target, db=kind % 2, dc=1, dy=kind // 2)
                sender.send(
                    part.at[block], got.at[target, kind], sem_of(0, target, kind), dict(dc=1)
                )

    def rows_of(ref, which):
        return ref.at[pl.ds(which * half, half)]

    def over_cores(target):
        for kind in walk:
            load(target, kind).wait()
            sender.arrived(got.at[target, kind], sem_of(0, target, kind))
            add_rows(mine.at[target, kind], [mine.at[target, kind], got.at[target, kind]], size)
            held = mine.at[target, kind]
            if kind == 3:
                sender.send(rows_of(held, 0), side.at[target, 4], sem_of(1, target, 0), dict(db=1))
                sender.send(rows_of(held, 1), side.at[target, 5], sem_of(1, target, 1), dict(dy=1))
            if kind == 1:
                sender.send(rows_of(held, 0), side.at[target, 0], sem_of(2, target, 0), dict(db=1))
                if not full:
                    sender.send(
                        rows_of(held, 1), side.at[target, 1], sem_of(2, target, 1), dict(db=1)
                    )
            if kind == 2:
                sender.send(rows_of(held, 1), side.at[target, 3], sem_of(2, target, 3), dict(dy=1))

    def over_corner(target):
        sender.arrived(side.at[target, 4], sem_of(1, target, 0))
        held = rows_of(mine.at[target, 2], 0)
        add_rows(held, [held, side.at[target, 4]], half)
        sender.send(held, side.at[target, 2], sem_of(2, target, 2), dict(dy=1))
        sender.arrived(side.at[target, 5], sem_of(1, target, 1))
        held = rows_of(mine.at[target, 1], 1)
        add_rows(held, [held, side.at[target, 5]], half)
        sender.send(held, side.at[target, 1], sem_of(2, target, 1), dict(db=1))

    def over_line(target):
        for which in range(2):
            held = rows_of(mine.at[target, 0], which)
            parts = [held]
            for source in (0, 2) if full else (0,):
                sender.arrived(side.at[target, source + which], sem_of(2, target, source + which))
                parts.append(side.at[target, source + which])
            below, above = rows_of(up.at[target], which), rows_of(down.at[target], which)
            below_sem, above_sem = sem_of(3, target, which), sem_of(3, target, 2 + which)

            def upward(with_below):
                extra = []
                if with_below:
                    sender.arrived(below, below_sem)
                    extra = [below]
                add_rows(held, parts + extra, half)

            def downward(with_above):
                extra = []
                if with_above:
                    sender.arrived(above, above_sem)
                    extra = [above]
                add_rows(held, parts + extra, half)

            if target > 0:
                pl.when(jnp.logical_and(a < target, a > 0))(lambda: upward(True))
                pl.when(a == 0)(lambda: upward(False))
                sender.send(held, below, below_sem, dict(da=1), a < target)
            if target < LINE - 1:
                pl.when(jnp.logical_and(a > target, a < LINE - 1))(lambda: downward(True))
                pl.when(a == LINE - 1)(lambda: downward(False))
                sender.send(held, above, above_sem, dict(da=-1), a > target)

            def last():
                extra = []
                if target > 0:
                    sender.arrived(below, below_sem)
                    extra.append(below)
                if target < LINE - 1:
                    sender.arrived(above, above_sem)
                    extra.append(above)
                add_rows(rows_of(out, which), parts + extra, half)

            pl.when(a == target)(last)

    stages = [over_cores] + ([over_corner] if full else []) + [over_line]

    def tick(number):
        if number == 0:
            begin()
        for level, stage in enumerate(stages):
            if 0 <= number - level < len(order):
                stage(order[number - level])

    return [functools.partial(tick, number) for number in range(len(order) + len(stages) - 1)]


def scatter_kernel(full, pairs, part, *refs):
    ins, out, outs = refs[:pairs], refs[pairs], refs[pairs + 1 : 2 * pairs + 1]
    mine, got, side, up, down, load_sems, send_sems, recv_sems, pair_sems = refs[2 * pairs + 1 :]
    place = Place()
    sender = Sender(place, send_sems)
    place.greet(full or pairs > 0)
    send_pairs(sender, ins, outs, pair_sems)
    scratch = (mine, got, side, up, down, load_sems, recv_sems)
    for tick in scatter_ticks(place, sender, full, part, out, scratch):
        tick()
    take_pairs(sender, outs, pair_sems)
    sender.finish()


def scatter_scratch(full, rows, width, dtype, pairs):
    kinds = 4 if full else 2
    return [
        pltpu.VMEM((LINE, kinds, rows, width), dtype),
        pltpu.VMEM((LINE, kinds, rows, width), dtype),
        pltpu.VMEM((LINE, 6, rows // 2, width), dtype),
        pltpu.VMEM((LINE, rows, width), dtype),
        pltpu.VMEM((LINE, rows, width), dtype),
        pltpu.SemaphoreType.DMA((LINE * 4,)),
        pltpu.SemaphoreType.DMA((pairs + LINE * (4 + 6 + 4),)),
        pltpu.SemaphoreType.DMA((4, LINE * 4)),
        pltpu.SemaphoreType.DMA((max(pairs, 1),)),
    ]


def gather_scatter_kernel(count, gated, *refs):
    ins, part = refs[:count], refs[count]
    outs, total = refs[count + 1 : 2 * count + 1], refs[2 * count + 1]
    local_sems, gather_sends, gather_recvs = refs[2 * count + 2 : 2 * count + 5]
    mine, got, side, up, down, load_sems, scatter_sends, scatter_recvs, _ = refs[2 * count + 5 :]
    place = Place()
    gatherer = Sender(place, gather_sends)
    scatterer = Sender(place, scatter_sends)
    place.greet(True)
    scratch = (mine, got, side, up, down, load_sems, scatter_recvs)
    ticks = [
        scatter_ticks(place, scatterer, True, part, total, scratch),
        gather_ticks(place, gatherer, False, gated, ins, outs, local_sems, gather_recvs),
    ]
    for number in range(max(len(steps) for steps in ticks)):
        for steps in ticks:
            if number < len(steps):
                steps[number]()
    scatterer.finish()
    gatherer.finish()


def gather_and_scatter(arrays, part, collective_id, gated=()):
    blocks = LINE * SQUARE * CORES
    count = len(arrays)
    _, rows, width = part.shape
    sends = count * (2 * LINE - 1) * 2 * 5
    moved = sum(blocks * 2 * x.size * x.dtype.itemsize for x in arrays)
    return pl.pallas_call(
        functools.partial(gather_scatter_kernel, count, gated),
        out_shape=[jax.ShapeDtypeStruct((blocks,) + x.shape, x.dtype) for x in arrays]
        + [jax.ShapeDtypeStruct((rows, width), jnp.float32)],
        in_specs=[pl.BlockSpec(memory_space=pl.ANY)] * (count + 1),
        out_specs=[pl.BlockSpec(memory_space=pl.ANY)] * count
        + [pl.BlockSpec(memory_space=pltpu.VMEM)],
        scratch_shapes=[
            pltpu.SemaphoreType.DMA((count,)),
            pltpu.SemaphoreType.DMA((sends,)),
            pltpu.SemaphoreType.DMA((count, blocks * 2)),
        ]
        + scatter_scratch(True, rows, width, part.dtype, 0),
        compiler_params=pltpu.CompilerParams(
            collective_id=collective_id, has_side_effects=True, vmem_limit_bytes=VMEM_LIMIT
        ),
        cost_estimate=pl.CostEstimate(flops=0, bytes_accessed=6 * moved, transcendentals=0),
    )(*arrays, part)


def scatter_rows(part, full, collective_id, swapped=()):
    blocks, rows, width = part.shape
    pairs = len(swapped)
    return pl.pallas_call(
        functools.partial(scatter_kernel, full, pairs),
        out_shape=[jax.ShapeDtypeStruct((rows, width), jnp.float32)]
        + [jax.ShapeDtypeStruct(x.shape, x.dtype) for x in swapped],
        in_specs=[pl.BlockSpec(memory_space=pl.ANY)] * (1 + pairs),
        out_specs=[pl.BlockSpec(memory_space=pltpu.VMEM)]
        + [pl.BlockSpec(memory_space=pl.ANY)] * pairs,
        scratch_shapes=scatter_scratch(full, rows, width, part.dtype, pairs),
        compiler_params=pltpu.CompilerParams(
            collective_id=collective_id, has_side_effects=True, vmem_limit_bytes=VMEM_LIMIT
        ),
        cost_estimate=pl.CostEstimate(
            flops=0, bytes_accessed=12 * part.size * part.dtype.itemsize, transcendentals=0
        ),
    )(part, *swapped)


def contract_last(left, right):
    return lax.dot_general(
        left, right, (((1,), (1,)), ((), ())), preferred_element_type=jnp.float32
    )


def contract_first(left, right):
    return lax.dot_general(
        left, right, (((0,), (0,)), ((), ())), preferred_element_type=jnp.float32
    )


def expert_kernel(
    capacity,
    normed,
    grads,
    routes,
    router_rows,
    w_gate,
    w_up,
    w_down,
    shared_in,
    shared_out,
    out_part,
    d_part,
    ex_rows,
    ex_grads,
    act_out,
    d_gate_out,
    d_up_out,
    shared_in_grad,
    shared_out_grad,
    in_total,
    out_total,
):
    position = lax.axis_index("expert")
    experts = lax.axis_size("expert")
    group, rows, width = normed.shape
    tokens, slots = group * rows, group * capacity
    bf16 = jnp.bfloat16
    x = normed[...].reshape(tokens, width)
    g = grads[...].reshape(tokens, width)

    row = lax.broadcasted_iota(jnp.int32, (tokens, tokens), 0)
    column = lax.broadcasted_iota(jnp.int32, (tokens, tokens), 1)
    before = jnp.logical_and(column < row, lax.div(row, rows) == lax.div(column, rows))
    named = routes[...].reshape(tokens, -1) == position.astype(jnp.float32).astype(bf16)
    hit = jnp.sum(jnp.where(named, 1.0, 0.0), axis=1, keepdims=True)
    tally = matrix_product(
        jnp.where(before, 1.0, 0.0).astype(bf16),
        jnp.broadcast_to(hit, (tokens, 128)).astype(bf16),
    )
    place = jnp.where(hit > 0.5, tally[:, :1], -1.0)
    token = lax.broadcasted_iota(jnp.int32, (tokens, slots), 0)
    slot = lax.broadcasted_iota(jnp.int32, (tokens, slots), 1)
    same = lax.div(slot, capacity) == lax.div(token, rows)
    wanted = lax.rem(slot, capacity).astype(jnp.float32)
    chosen = jnp.where(jnp.logical_and(same, wanted == place), 1.0, 0.0)
    pick = chosen.T.astype(bf16)
    put = chosen.astype(bf16)

    r = matrix_product(pick, x).astype(bf16)
    gr = matrix_product(pick, g).astype(bf16)
    ex_rows[...] = r
    ex_grads[...] = gr
    lane = lax.broadcasted_iota(jnp.int32, (slots, router_rows.shape[0]), 1)
    logits = jnp.where(lane < experts, contract_last(r, router_rows[...]), -1e30)
    exps = jnp.exp(logits - jnp.max(logits, axis=1, keepdims=True))
    gate = jnp.sum(jnp.where(lane == position, exps, 0.0), axis=1, keepdims=True) / jnp.sum(
        exps, axis=1, keepdims=True
    )

    pre_gate = contract_last(r, w_gate[...])
    pre_up = contract_last(r, w_up[...])
    act_gate, slope = silu_parts(pre_gate)
    act = act_gate * pre_up
    back = contract_last(gr, w_down[...])
    d_gate_slot = jnp.sum(act * back, axis=1, keepdims=True)
    scaled = (gate * act).astype(bf16)
    d_act = gate * back
    d_pre_gate = (d_act * pre_up * slope).astype(bf16)
    d_pre_up = (d_act * act_gate).astype(bf16)
    act_out[...] = scaled
    d_gate_out[...] = d_pre_gate
    d_up_out[...] = d_pre_up
    ex_out = matrix_product(scaled, w_down[...]).astype(bf16)
    d_ex = matrix_product(d_pre_gate, w_gate[...]) + matrix_product(d_pre_up, w_up[...])
    d_ex = d_ex.astype(bf16)

    units = shared_out.shape[0]
    mix = matrix_product(x, shared_in[...])
    sh_gate, sh_up = mix[:, :units], mix[:, units:]
    sh_silu, sh_slope = silu_parts(sh_gate)
    sh_act = (sh_silu * sh_up).astype(bf16)
    d_sh_act = contract_last(g, shared_out[...])
    d_mix = jnp.concatenate([d_sh_act * sh_up * sh_slope, d_sh_act * sh_silu], axis=1)
    d_mix = d_mix.astype(bf16)

    out = matrix_product(put, ex_out) + matrix_product(sh_act, shared_out[...])
    out_part[...] = out.astype(bf16).reshape(group, rows, width)
    d_in = matrix_product(put, d_ex) + contract_last(d_mix, shared_in[...])
    d_part[:, :, :width] = d_in.astype(bf16).reshape(group, rows, width)
    lane = lax.broadcasted_iota(jnp.int32, (slots, d_part.shape[2] - width), 1)
    d_gates = jnp.where(lane == position, d_gate_slot, 0.0).astype(bf16)
    d_part[:, :, width:] = matrix_product(put, d_gates).astype(bf16).reshape(group, rows, -1)

    step = pl.program_id(0)

    @pl.when(step == 0)
    def _():
        in_total[...] = jnp.zeros_like(in_total)
        out_total[...] = jnp.zeros_like(out_total)

    in_total[...] += contract_first(d_mix, x)
    out_total[...] += contract_first(sh_act, g)

    @pl.when(step == pl.num_programs(0) - 1)
    def _():
        shared_in_grad[...] = in_total[...].T.astype(bf16)
        shared_out_grad[...] = out_total[...]


def expert_phase(
    all_normed, all_grads, router_rows, w_gate, w_up, w_down, shared_in, shared_out, capacity
):
    blocks, rows, width = all_normed.shape
    group = 4
    slots = group * capacity
    hidden = w_gate.shape[0]
    units = shared_out.shape[0]
    side = all_grads.shape[2] - width
    bf16 = jnp.bfloat16

    def by_group(shape):
        zeros = (0,) * (len(shape) - 1)
        return pl.BlockSpec(shape, lambda i: (i,) + zeros)

    def fixed(shape):
        return pl.BlockSpec(
            shape, lambda i: (0,) * len(shape), pipeline_mode=pl.Buffered(buffer_count=1)
        )

    return pl.pallas_call(
        functools.partial(expert_kernel, capacity),
        grid=(blocks // group,),
        out_shape=[
            jax.ShapeDtypeStruct((blocks, rows, width), bf16),
            jax.ShapeDtypeStruct((blocks, rows, width + side), bf16),
            jax.ShapeDtypeStruct((blocks * capacity, width), bf16),
            jax.ShapeDtypeStruct((blocks * capacity, width), bf16),
            jax.ShapeDtypeStruct((blocks * capacity, hidden), bf16),
            jax.ShapeDtypeStruct((blocks * capacity, hidden), bf16),
            jax.ShapeDtypeStruct((blocks * capacity, hidden), bf16),
            jax.ShapeDtypeStruct((width, 2 * units), bf16),
            jax.ShapeDtypeStruct((units, width), jnp.float32),
        ],
        in_specs=[
            by_group((group, rows, width)),
            by_group((group, rows, width)),
            pl.BlockSpec((group, rows, side), lambda i: (i, 0, width // side)),
            fixed(router_rows.shape),
            fixed(w_gate.shape),
            fixed(w_up.shape),
            fixed(w_down.shape),
            fixed(shared_in.shape),
            fixed(shared_out.shape),
        ],
        out_specs=[
            by_group((group, rows, width)),
            by_group((group, rows, width + side)),
            by_group((slots, width)),
            by_group((slots, width)),
            by_group((slots, hidden)),
            by_group((slots, hidden)),
            by_group((slots, hidden)),
            fixed((width, 2 * units)),
            fixed((units, width)),
        ],
        scratch_shapes=[
            pltpu.VMEM((2 * units, width), jnp.float32),
            pltpu.VMEM((units, width), jnp.float32),
        ],
        compiler_params=pltpu.CompilerParams(vmem_limit_bytes=VMEM_LIMIT),
        cost_estimate=pl.CostEstimate(
            flops=2 * blocks * capacity * width * hidden * 6,
            bytes_accessed=10 * blocks * rows * width * 2,
            transcendentals=blocks * capacity * hidden,
        ),
    )(all_normed, all_grads, all_grads, router_rows, w_gate, w_up, w_down, shared_in, shared_out)


def exchange_kernel(x, out, local_sem, send_sems, recv_sems):
    me, y = lax.axis_index("expert"), lax.axis_index("fsdp")
    count = x.shape[0]
    barrier = pltpu.get_barrier_semaphore()
    peers = [lax.rem(me + step, count) for step in range(1, count)]
    for peer in peers:
        pl.semaphore_signal(barrier, inc=1, device_id=(peer, y), device_id_type=MESH)
    own = pltpu.make_async_copy(x.at[me], out.at[me], local_sem)
    own.start()
    pl.semaphore_wait(barrier, count - 1)
    copies = []
    for at, peer in enumerate(peers):
        copy = pltpu.make_async_remote_copy(
            src_ref=x.at[peer],
            dst_ref=out.at[me],
            send_sem=send_sems.at[at],
            recv_sem=recv_sems.at[at],
            device_id=(peer, y),
            device_id_type=MESH,
        )
        copy.start()
        copies.append(copy)
    for copy in copies:
        copy.wait()
    own.wait()


def exchange(x, collective_id):
    count = x.shape[0]
    return pl.pallas_call(
        exchange_kernel,
        out_shape=jax.ShapeDtypeStruct(x.shape, x.dtype),
        in_specs=[pl.BlockSpec(memory_space=pl.ANY)],
        out_specs=pl.BlockSpec(memory_space=pl.ANY),
        scratch_shapes=[
            pltpu.SemaphoreType.DMA,
            pltpu.SemaphoreType.DMA((count - 1,)),
            pltpu.SemaphoreType.DMA((count - 1,)),
        ],
        compiler_params=pltpu.CompilerParams(collective_id=collective_id, has_side_effects=True),
        cost_estimate=pl.CostEstimate(
            flops=0, bytes_accessed=20 * x.size * x.dtype.itemsize, transcendentals=0
        ),
    )(x)


def swap_halves(value):
    half = value.shape[1] // 2
    return jnp.concatenate([value[:, half:], value[:, :half]], axis=1)


def greet_plane(place):
    me = lax.axis_index("expert")
    count = LINE * SQUARE * CORES
    barrier = pltpu.get_barrier_semaphore()
    for step in range(1, count):
        peer = (lax.rem(me + step, count), place.y)
        pl.semaphore_signal(barrier, inc=1, device_id=peer, device_id_type=MESH)
    pl.semaphore_signal(barrier, inc=1, device_id=place.device(dy=1), device_id_type=MESH)
    pl.semaphore_wait(barrier, count)


def sums_kernel(pairs, moved, small, large, *refs):
    ins = refs[:pairs]
    moved_out, small_out, large_out = refs[pairs : pairs + 3]
    outs = refs[pairs + 3 : 2 * pairs + 3]
    rest = refs[2 * pairs + 3 :]
    local_sem, exchange_sends, exchange_recvs = rest[:3]
    first, second = rest[3:12], rest[12:21]
    place = Place()
    me = lax.axis_index("expert")
    count = moved.shape[0]
    greet_plane(place)
    own = pltpu.make_async_copy(moved.at[me], moved_out.at[me], local_sem)
    own.start()
    copies = []
    for at in range(count - 1):
        copy = pltpu.make_async_remote_copy(
            src_ref=moved.at[lax.rem(me + at + 1, count)],
            dst_ref=moved_out.at[me],
            send_sem=exchange_sends.at[at],
            recv_sem=exchange_recvs.at[at],
            device_id=(lax.rem(me + at + 1, count), place.y),
            device_id_type=MESH,
        )
        copy.start()
        copies.append(copy)
    senders = [Sender(place, first[6]), Sender(place, second[6])]
    send_pairs(senders[0], ins, outs, first[8])
    ticks = [
        scatter_ticks(place, senders[0], False, small, small_out, first[:6] + (first[7],)),
        scatter_ticks(place, senders[1], True, large, large_out, second[:6] + (second[7],)),
    ]
    for number in range(max(len(steps) for steps in ticks)):
        for steps in ticks:
            if number < len(steps):
                steps[number]()
    take_pairs(senders[0], outs, first[8])
    for sender in senders:
        sender.finish()
    for copy in copies:
        copy.wait()
    own.wait()


def exchange_and_sums(moved, small, large, swapped, collective_id):
    count, pairs = moved.shape[0], len(swapped)
    hbm = pl.BlockSpec(memory_space=pl.ANY)
    vmem = pl.BlockSpec(memory_space=pltpu.VMEM)
    return pl.pallas_call(
        functools.partial(sums_kernel, pairs),
        out_shape=[
            jax.ShapeDtypeStruct(moved.shape, moved.dtype),
            jax.ShapeDtypeStruct(small.shape[1:], jnp.float32),
            jax.ShapeDtypeStruct(large.shape[1:], jnp.float32),
        ]
        + [jax.ShapeDtypeStruct(x.shape, x.dtype) for x in swapped],
        in_specs=[hbm] * (3 + pairs),
        out_specs=[hbm, vmem, vmem] + [hbm] * pairs,
        scratch_shapes=[
            pltpu.SemaphoreType.DMA,
            pltpu.SemaphoreType.DMA((count - 1,)),
            pltpu.SemaphoreType.DMA((count - 1,)),
        ]
        + scatter_scratch(False, *small.shape[1:], small.dtype, pairs)
        + scatter_scratch(True, *large.shape[1:], large.dtype, 0),
        compiler_params=pltpu.CompilerParams(
            collective_id=collective_id, has_side_effects=True, vmem_limit_bytes=VMEM_LIMIT
        ),
        cost_estimate=pl.CostEstimate(
            flops=0, bytes_accessed=12 * large.size * 2, transcendentals=0
        ),
    )(moved, small, large, *swapped)


def attend_kernel(
    rows,
    g_attn,
    w_front,
    g_lat,
    expand_head,
    cosines,
    sines,
    normed_out,
    latent_out,
    query_out,
    key_out,
    value_out,
    head_out,
    sum_out,
    log_out,
    keys,
    values,
):
    bf16 = jnp.bfloat16
    size = rows.shape[0]
    scale = (PLAIN_UNITS + ROTARY_UNITS) ** (-0.5)
    step = pl.program_id(0)
    normed, _ = norm_forward(rows[...].astype(jnp.float32), g_attn[...])
    normed = normed.astype(bf16)
    normed_out[...] = normed
    front = contract_last(normed, w_front[...])
    latent, _ = norm_forward(front[:, :LATENT_WIDTH], g_lat[...])
    latent = latent.astype(bf16)
    latent_out[...] = latent
    width = LATENT_WIDTH + ROTARY_UNITS

    def rotated(value):
        return value * cosines[...] + swap_halves(value) * sines[...]

    pairs = matrix_product(latent, expand_head[...])
    key = jnp.concatenate([pairs[:, :PLAIN_UNITS], rotated(front[:, LATENT_WIDTH:width])], axis=1)
    query = jnp.concatenate(
        [front[:, width : width + PLAIN_UNITS], rotated(front[:, width + PLAIN_UNITS :])], axis=1
    ).astype(bf16)
    key = key.astype(bf16)
    value = pairs[:, PLAIN_UNITS:].astype(bf16)
    query_out[...] = query
    key_out[...] = key
    value_out[...] = value
    here = pl.ds(pl.multiple_of(step * size, size), size)
    keys[here, :] = key
    values[here, :] = value
    row = lax.broadcasted_iota(jnp.int32, (size, size), 0)
    column = lax.broadcasted_iota(jnp.int32, (size, size), 1)
    near = jnp.where(column <= row, contract_last(query, key) * scale, -1e30)

    def over(past):
        top = jnp.max(near, axis=1, keepdims=True)
        if past:
            far = contract_last(query, keys[:past, :]) * scale
            top = jnp.maximum(top, jnp.max(far, axis=1, keepdims=True))
        exps = jnp.exp(near - top)
        total = jnp.sum(exps, axis=1, keepdims=True)
        mixed = matrix_product(exps.astype(bf16), value)
        if past:
            exps = jnp.exp(far - top)
            total = total + jnp.sum(exps, axis=1, keepdims=True)
            mixed = mixed + matrix_product(exps.astype(bf16), values[:past, :])
        mixed = mixed / total
        sum_out[...] = mixed
        head_out[...] = mixed.astype(bf16)
        wide = jnp.broadcast_to(top + jnp.log(total), (size, 128))
        log_out[0] = wide.T[:1, :]

    for at in range(keys.shape[0] // size):
        pl.when(step == at)(functools.partial(over, at * size))


def attend(rows, g_attn, w_front, g_lat, expand_head, cosines, sines):
    seq_len, width = rows.shape
    size = 256
    steps = seq_len // size
    units = PLAIN_UNITS + ROTARY_UNITS
    bf16 = jnp.bfloat16

    def by_step(columns):
        return pl.BlockSpec((size, columns), lambda i: (i, 0))

    def fixed(x):
        return pl.BlockSpec(
            x.shape, lambda i: (0, 0), pipeline_mode=pl.Buffered(buffer_count=1)
        )

    return pl.pallas_call(
        attend_kernel,
        grid=(steps,),
        out_shape=[
            jax.ShapeDtypeStruct((seq_len, width), bf16),
            jax.ShapeDtypeStruct((seq_len, LATENT_WIDTH), bf16),
            jax.ShapeDtypeStruct((seq_len, units), bf16),
            jax.ShapeDtypeStruct((seq_len, units), bf16),
            jax.ShapeDtypeStruct((seq_len, VALUE_UNITS), bf16),
            jax.ShapeDtypeStruct((seq_len, VALUE_UNITS), bf16),
            jax.ShapeDtypeStruct((seq_len, VALUE_UNITS), jnp.float32),
            jax.ShapeDtypeStruct((steps, 1, size), jnp.float32),
        ],
        in_specs=[by_step(width)]
        + [fixed(x) for x in (g_attn, w_front, g_lat, expand_head)]
        + [by_step(ROTARY_UNITS)] * 2,
        out_specs=[
            by_step(width),
            by_step(LATENT_WIDTH),
            by_step(units),
            by_step(units),
            by_step(VALUE_UNITS),
            by_step(VALUE_UNITS),
            by_step(VALUE_UNITS),
            pl.BlockSpec((1, 1, size), lambda i: (i, 0, 0)),
        ],
        scratch_shapes=[
            pltpu.VMEM((seq_len, units), bf16),
            pltpu.VMEM((seq_len, VALUE_UNITS), bf16),
        ],
        compiler_params=pltpu.CompilerParams(vmem_limit_bytes=VMEM_LIMIT),
        cost_estimate=pl.CostEstimate(
            flops=2 * seq_len * (width * 768 + seq_len * units),
            bytes_accessed=3 * rows.size * 2,
            transcendentals=seq_len * seq_len // 2,
        ),
    )(rows, g_attn, w_front, g_lat, expand_head, cosines, sines)


def attend_back_kernel(
    query,
    key,
    value,
    d_head,
    head_sum,
    logs,
    expand_head,
    cosines,
    sines,
    d_query_out,
    d_pairs_out,
    d_keys_out,
    d_key,
    d_value,
    key_turned,
):
    bf16 = jnp.bfloat16
    size = query.shape[0]
    seq_len = key.shape[0]
    scale = (PLAIN_UNITS + ROTARY_UNITS) ** (-0.5)
    step = pl.program_id(0)

    @pl.when(step == 0)
    def _():
        d_key[...] = jnp.zeros_like(d_key)
        d_value[...] = jnp.zeros_like(d_value)
        for at in range(0, seq_len, size):
            part = key[at : at + size, :].astype(jnp.float32)
            key_turned[:, at : at + size] = part.T.astype(bf16)

    q, d_out = query[...], d_head[...]
    product = d_out.astype(jnp.float32) * head_sum[...]
    delta = jnp.sum(product.T, axis=0, keepdims=True)
    log_row = logs[0]
    row = lax.broadcasted_iota(jnp.int32, (size, size), 0)
    column = lax.broadcasted_iota(jnp.int32, (size, size), 1)

    def grads_of(at, mask):
        there = slice(at, at + size)
        scores = contract_last(key[there, :], q) * scale
        if mask:
            scores = jnp.where(row <= column, scores, -1e30)
        probs = jnp.exp(scores - log_row)
        d_probs = contract_last(value[there, :], d_out)
        d_scores = (probs * (d_probs - delta) * scale).astype(bf16)
        d_key[there, :] += matrix_product(d_scores, q)
        d_value[there, :] += matrix_product(probs.astype(bf16), d_out)
        return matrix_product(key_turned[:, there], d_scores)

    def over(past):
        total = grads_of(past, True)
        for at in range(0, past, size):
            total = total + grads_of(at, False)
        d_query = total.T
        d_rope = d_query[:, PLAIN_UNITS:]
        d_rope = d_rope * cosines[...] - swap_halves(d_rope) * sines[...]
        d_query_out[...] = jnp.concatenate([d_query[:, :PLAIN_UNITS], d_rope], axis=1).astype(bf16)

    for at in range(seq_len // size):
        pl.when(step == at)(functools.partial(over, at * size))

    @pl.when(step == seq_len // size - 1)
    def _():
        for at in range(0, seq_len, size):
            there = slice(at, at + size)
            d_pairs = jnp.concatenate(
                [d_key[there, :PLAIN_UNITS], d_value[there, :]], axis=1
            ).astype(bf16)
            d_pairs_out[there, :] = d_pairs
            d_keys_out[there, :LATENT_WIDTH] = contract_last(d_pairs, expand_head[...]).astype(bf16)
            tail = jnp.concatenate(
                [d_key[there, PLAIN_UNITS:], jnp.zeros((size, ROTARY_UNITS), jnp.float32)], axis=1
            )
            d_keys_out[there, LATENT_WIDTH:] = tail.astype(bf16)


def attend_back(query, key, value, d_head, head_sum, logs, expand_head, cosines, sines):
    seq_len, units = query.shape
    steps, _, size = logs.shape
    bf16 = jnp.bfloat16
    keys_width = LATENT_WIDTH + 2 * ROTARY_UNITS

    def by_step(columns):
        return pl.BlockSpec((size, columns), lambda i: (i, 0))

    def fixed(shape):
        return pl.BlockSpec(shape, lambda i: (0, 0), pipeline_mode=pl.Buffered(buffer_count=1))

    return pl.pallas_call(
        attend_back_kernel,
        grid=(steps,),
        out_shape=[
            jax.ShapeDtypeStruct((seq_len, units), bf16),
            jax.ShapeDtypeStruct((seq_len, PLAIN_UNITS + VALUE_UNITS), bf16),
            jax.ShapeDtypeStruct((seq_len, keys_width), bf16),
        ],
        in_specs=[
            by_step(units),
            fixed(key.shape),
            fixed(value.shape),
            by_step(VALUE_UNITS),
            by_step(VALUE_UNITS),
            pl.BlockSpec((1, 1, size), lambda i: (i, 0, 0)),
            fixed(expand_head.shape),
            by_step(ROTARY_UNITS),
            by_step(ROTARY_UNITS),
        ],
        out_specs=[
            by_step(units),
            fixed((seq_len, PLAIN_UNITS + VALUE_UNITS)),
            fixed((seq_len, keys_width)),
        ],
        scratch_shapes=[
            pltpu.VMEM((seq_len, units), jnp.float32),
            pltpu.VMEM((seq_len, VALUE_UNITS), jnp.float32),
            pltpu.VMEM((units, seq_len), bf16),
        ],
        compiler_params=pltpu.CompilerParams(vmem_limit_bytes=VMEM_LIMIT),
        cost_estimate=pl.CostEstimate(
            flops=5 * seq_len * seq_len * units,
            bytes_accessed=8 * seq_len * units * 2,
            transcendentals=seq_len * seq_len // 2,
        ),
    )(query, key, value, d_head, head_sum, logs, expand_head, cosines, sines)


def finish_kernel(query, expand, out_rows, query_out, expand_out, out_out):
    heads, units, width = query.shape
    query_out[...] = query[...].reshape(heads * units, width).astype(jnp.float32).T
    for at in range(heads):
        columns = expand.shape[2]
        expand_out[:, at * columns : (at + 1) * columns] = expand[at].astype(jnp.float32)
    out_out[...] = out_rows[...].reshape(out_out.shape).astype(jnp.float32)


def finish(query, expand, out_rows):
    heads, units, width = query.shape
    _, latents, columns = expand.shape
    _, rows, model = out_rows.shape
    return pl.pallas_call(
        finish_kernel,
        grid=(heads // 2,),
        out_shape=[
            jax.ShapeDtypeStruct((width, heads * units), jnp.float32),
            jax.ShapeDtypeStruct((latents, heads * columns), jnp.float32),
            jax.ShapeDtypeStruct((heads * rows, model), jnp.float32),
        ],
        in_specs=[
            pl.BlockSpec((2, units, width), lambda i: (i, 0, 0)),
            pl.BlockSpec((2, latents, columns), lambda i: (i, 0, 0)),
            pl.BlockSpec((2, rows, model), lambda i: (i, 0, 0)),
        ],
        out_specs=[
            pl.BlockSpec((width, 2 * units), lambda i: (0, i)),
            pl.BlockSpec((latents, 2 * columns), lambda i: (0, i)),
            pl.BlockSpec((2 * rows, model), lambda i: (i, 0)),
        ],
        compiler_params=pltpu.CompilerParams(vmem_limit_bytes=VMEM_LIMIT),
        cost_estimate=pl.CostEstimate(
            flops=0, bytes_accessed=6 * heads * units * width, transcendentals=0
        ),
    )(query, expand, out_rows)


def token_gather(rows):
    return lax.all_gather(rows, ("fsdp", "expert"), axis=0, tiled=True)


def split_body(
    tokens,
    routes,
    cotangent,
    attn_gain,
    w_query,
    latent_weight,
    latent_norm_gain,
    expand_weight,
    w_out,
    ffn_gain,
    w_router,
    shared_gate,
    shared_up,
    shared_down,
    expert_gate,
    expert_up,
    expert_down,
):
    rows = tokens.shape[1]
    experts = lax.axis_size("expert")
    shards = lax.axis_size("fsdp")
    position = lax.axis_index("expert")
    blocks = experts * shards
    seq_len = rows * experts
    capacity = shards * ((rows * TOPK * 4 + experts * 3 * shards - 1) // (experts * 3 * shards))
    head_units = PLAIN_UNITS + ROTARY_UNITS
    pair_units = PLAIN_UNITS + VALUE_UNITS
    feature_width = LATENT_WIDTH + ROTARY_UNITS
    scale = head_units ** (-0.5)

    shard = lax.axis_index("fsdp")
    first = shard == 0

    query_cols = lax.dynamic_slice_in_dim(w_query, position * head_units, head_units, 1)
    expand_cols = lax.dynamic_slice_in_dim(expand_weight, position * pair_units, pair_units, 1)
    owners = experts // shards
    lat_row = jnp.pad(latent_norm_gain, (0, w_query.shape[0] - latent_norm_gain.shape[0]))
    packed = jnp.concatenate(
        [latent_weight.T, query_cols.T, w_router.T, attn_gain[None], ffn_gain[None], lat_row[None]],
        axis=0,
    )
    packed = jnp.pad(packed, ((0, -packed.shape[0] % 32), (0, 0)))
    seq_rows, other_packed, other_expand = gather_rows(
        [tokens[0]], False, 0, swapped=[packed, expand_cols]
    )

    def whole(own, other, axis):
        return jnp.concatenate(
            [jnp.where(first, own, other), jnp.where(first, other, own)], axis=axis
        )

    lat_half = latent_norm_gain.shape[0]
    at = feature_width + head_units
    packed_rows = whole(packed, other_packed, 1)
    expand_head = whole(expand_cols, other_expand, 0)
    w_front = packed_rows[:at]
    w_latent = packed_rows[:feature_width]
    router_rows = packed_rows[at:]
    wrout = packed_rows[at : at + experts]
    g_attn = packed_rows[at + experts].astype(jnp.float32)
    g_ffn = packed_rows[at + experts + 1].astype(jnp.float32)
    lat_row = packed_rows[at + experts + 2]
    g_lat = jnp.concatenate(
        [lat_row[:lat_half], lat_row[w_query.shape[0] : w_query.shape[0] + lat_half]]
    ).astype(jnp.float32)
    units = shared_down.shape[0]

    core = lax.rem(position, CORES)

    def by_cores(weight):
        size = weight.shape[0] // CORES
        own = lax.dynamic_slice_in_dim(weight, core * size, size, 0)
        own = lax.all_gather(own, "fsdp", axis=0, tiled=True)
        swap = [(index, index ^ 1) for index in range(experts)]
        return own, lax.ppermute(own, "expert", swap)

    def core_columns(value, which):
        size = value.shape[1] // (CORES * shards)
        parts = [
            lax.dynamic_slice_in_dim(value, (at * CORES + which) * size, size, 1)
            for at in range(shards)
        ]
        return jnp.concatenate(parts, axis=1)

    def in_order(own, other):
        lower, upper = jnp.where(core == 0, own, other), jnp.where(core == 0, other, own)
        size = own.shape[1] // shards
        parts = []
        for at in range(shards):
            parts += [lower[:, at * size : (at + 1) * size], upper[:, at * size : (at + 1) * size]]
        return jnp.concatenate(parts, axis=1)

    out_own, out_other = by_cores(w_out)
    grad_rows = cotangent[0]
    grad_out = grad_rows.astype(jnp.float32)
    own_routes = jnp.pad(routes[0], ((0, 0), (0, 128 - TOPK)), constant_values=-1)
    grad_rows = jnp.concatenate([grad_rows, own_routes.astype(jnp.bfloat16)], axis=1)
    seq_rows, grad_rows, shared_gate, shared_up = lax.optimization_barrier(
        (seq_rows, grad_rows, shared_gate, shared_up)
    )
    def to_columns(weight):
        parts = weight.reshape(weight.shape[0], blocks, units).transpose(1, 0, 2)
        return lax.all_to_all(
            parts, ("expert", "fsdp"), split_axis=0, concat_axis=0, tiled=True
        ).reshape(-1, units)

    sh_cols = to_columns(jnp.concatenate([shared_gate, shared_up], axis=0)).reshape(
        blocks, 2, shared_gate.shape[0], units
    )
    lanes = -(-units // 128) * 128
    sh_cols = jnp.pad(sh_cols, ((0, 0), (0, 0), (0, 0), (0, lanes - units)))
    shared_in = sh_cols.transpose(0, 2, 1, 3).reshape(MODEL_WIDTH, 2 * lanes)
    shared_out = jnp.pad(shared_down, ((0, lanes - units), (0, 0)))
    all_grads = token_gather(grad_rows)

    x_in = tokens[0].astype(jnp.float32)
    normed, inv_attn = norm_forward(x_in, g_attn)
    normed_in = normed.astype(jnp.bfloat16)
    half_units = ROTARY_UNITS // 2
    freqs = 10000.0 ** (-np.arange(half_units) * (2.0 / ROTARY_UNITS))
    angles = np.arange(seq_len)[:, None] * freqs[None, :]
    cosine_table = jnp.asarray(np.cos(angles), jnp.float32)
    sine_table = jnp.asarray(np.sin(angles), jnp.float32)
    cosines = jnp.asarray(np.concatenate([np.cos(angles)] * 2, axis=1), jnp.float32)
    sines = jnp.asarray(np.concatenate([-np.sin(angles), np.sin(angles)], axis=1), jnp.float32)
    (
        seq_normed,
        latent_rows,
        query,
        key,
        value,
        head_rows,
        head_sum,
        logs,
    ) = attend(
        seq_rows.reshape(seq_len, MODEL_WIDTH),
        g_attn[None],
        w_front,
        g_lat[None],
        expand_head,
        cosines,
        sines,
    )
    head_rows, shared_in = lax.optimization_barrier((head_rows, shared_in))
    heads = exchange(head_rows.reshape(experts, rows, VALUE_UNITS), 1)
    heads = heads.transpose(1, 0, 2).reshape(rows, experts * VALUE_UNITS)
    hidden = x_in + matrix_product(core_columns(heads, core), out_own)
    hidden = hidden + matrix_product(core_columns(heads, 1 - core), out_other)
    normed2, inv_ffn = norm_forward(hidden, g_ffn)
    normed_ffn = normed2.astype(jnp.bfloat16)
    router = jax.nn.softmax(outer_product(normed_ffn, wrout), axis=-1)

    (all_normed,) = gather_rows([normed_ffn], True, 2)
    w_query, all_normed = lax.optimization_barrier((w_query, all_normed))
    query_own, query_other = by_cores(w_query)
    (
        out_part,
        d_part,
        ex_rows,
        ex_grads,
        scaled_act,
        d_pre_gate,
        d_pre_up,
        g_shared_in,
        g_shared_out,
    ) = expert_phase(
        all_normed,
        all_grads.reshape(blocks, rows, -1),
        router_rows,
        expert_gate[0].T,
        expert_up[0].T,
        expert_down[0],
        shared_in,
        shared_out,
        capacity,
    )
    g_down = inner(scaled_act, ex_grads)
    g_gate = inner(d_pre_gate, ex_rows).T
    g_up = inner(d_pre_up, ex_rows).T
    (d_back,) = scatter_rows(d_part, True, 3)
    out_part, d_back = lax.optimization_barrier((out_part, d_back))
    out_sum = lax.psum_scatter(
        out_part.reshape(blocks * rows, MODEL_WIDTH),
        ("fsdp", "expert"),
        scatter_dimension=0,
        tiled=True,
    )
    d_normed_ffn = d_back[:, :MODEL_WIDTH]
    d_router = d_back[:, MODEL_WIDTH : MODEL_WIDTH + experts]

    d_logits = (router * (d_router - jnp.sum(router * d_router, axis=1, keepdims=True))).astype(
        jnp.bfloat16
    )
    g_router = inner(d_logits, normed_ffn)
    d_normed_ffn = d_normed_ffn + matrix_product(d_logits, wrout)
    d_hidden_norm, g_ffn_grad = norm_backward(hidden, inv_ffn, g_ffn, d_normed_ffn)
    d_hidden = grad_out + d_hidden_norm
    d_attn = d_hidden.astype(jnp.bfloat16)

    d_heads = in_order(outer_product(d_attn, out_own), outer_product(d_attn, out_other))
    d_heads = d_heads.astype(jnp.bfloat16)
    d_heads = d_heads.reshape(rows, experts, VALUE_UNITS).transpose(1, 0, 2)
    d_head = exchange(d_heads, 4).reshape(seq_len, VALUE_UNITS)
    out_grad_part = inner(heads, d_attn).astype(jnp.bfloat16)
    d_query_full, d_pairs, d_keys = attend_back(
        query, key, value, d_head, head_sum, logs, expand_head, cosines, sines
    )
    g_expand_head = inner(latent_rows, d_pairs)
    g_query_head = inner(d_query_full, seq_normed).astype(jnp.bfloat16)
    g_expand_head = g_expand_head.astype(jnp.bfloat16)

    def half_of(whole, which, axis):
        size = whole.shape[axis] // shards
        return lax.dynamic_slice_in_dim(whole, which * size, size, axis)

    own_d_query, d_sums, own_out, other_query, other_expand = exchange_and_sums(
        d_query_full.reshape(experts, rows, head_units),
        d_keys.reshape(experts, rows, -1),
        out_grad_part.reshape(blocks, -1, MODEL_WIDTH),
        [half_of(g_query_head, 1 - shard, 1), half_of(g_expand_head, 1 - shard, 0)],
        5,
    )
    own_d_query = own_d_query.transpose(1, 0, 2).reshape(rows, experts * head_units)
    key_gradient = d_sums[:, :feature_width]
    d_normed_in = in_order(
        outer_product(own_d_query, query_own), outer_product(own_d_query, query_other)
    )

    def summed(own, other):
        return (own.astype(jnp.float32) + other.astype(jnp.float32)).astype(jnp.bfloat16)

    own_query = summed(half_of(g_query_head, shard, 1), other_query)
    own_expand = summed(half_of(g_expand_head, shard, 0), other_expand)
    own_out = own_out.astype(jnp.bfloat16)
    own_latent = outer_product(normed_in, w_latent[:LATENT_WIDTH])
    own_cosine = lax.dynamic_slice_in_dim(cosine_table, position * rows, rows, 0)
    own_sine = lax.dynamic_slice_in_dim(sine_table, position * rows, rows, 0)
    inv_lat = lax.rsqrt(jnp.mean(own_latent * own_latent, axis=-1, keepdims=True) + EPS)
    d_compact, g_lat_grad = norm_backward(
        own_latent, inv_lat, g_lat, key_gradient[:, :LATENT_WIDTH]
    )
    d_rope = reverse_rotary(key_gradient[:, LATENT_WIDTH:], own_cosine, own_sine)
    d_latent_full = jnp.concatenate([d_compact, d_rope], axis=-1).astype(jnp.bfloat16)
    g_latent = inner(d_latent_full, normed_in)
    d_normed_in = d_normed_in + matrix_product(d_latent_full, w_latent)
    d_norm_in, g_attn_grad = norm_backward(x_in, inv_attn, g_attn, d_normed_in)
    d_tokens = (d_hidden + d_norm_in).astype(jnp.bfloat16)

    half = MODEL_WIDTH // blocks
    cols = lax.all_to_all(
        g_shared_in.reshape(blocks, half, 2 * lanes),
        ("expert", "fsdp"),
        split_axis=0,
        concat_axis=0,
        tiled=True,
    )
    cols = cols.transpose(1, 0, 2).astype(jnp.float32)
    r_sgate = cols[:, :, :units].reshape(half, blocks * units)
    r_sup = cols[:, :, lanes : lanes + units].reshape(half, blocks * units)
    g_sdown = g_shared_out[:units]
    model_half = MODEL_WIDTH // shards
    small_rows = jnp.concatenate([g_latent, g_router, g_attn_grad[None], g_ffn_grad[None]], axis=0)
    used = small_rows.shape[0]
    share = 2 * 32 * (-(-(used + 1) // (2 * 32 * experts)))

    def rows_for(which):
        here = small_rows[:, which * model_half : (which + 1) * model_half]
        lat = jnp.pad(
            g_lat_grad[which * lat_half : (which + 1) * lat_half], (0, model_half - lat_half)
        )
        full = jnp.concatenate([here, lat[None]], axis=0).astype(jnp.bfloat16)
        full = jnp.pad(full, ((0, experts * share - used - 1), (0, 0)))
        return full.reshape(experts, share, model_half)

    small_part = jnp.concatenate([rows_for(which) for which in range(shards)], axis=0)
    r_query, r_expand, r_out, small_sum = gather_and_scatter(
        [own_query, own_expand, own_out], small_part, 6
    )
    hidden, small_sum = lax.optimization_barrier((hidden, small_sum))
    output = hidden + out_sum.astype(jnp.float32)
    (small_all,) = gather_rows([small_sum.astype(jnp.bfloat16)], False, 7)
    r_query, r_expand, r_out = finish(r_query, r_expand, r_out)
    small_all = small_all.reshape(experts * share, model_half).astype(jnp.float32)
    return (
        output.astype(jnp.bfloat16)[None],
        d_tokens[None],
        small_all[feature_width + experts],
        r_query,
        small_all[:feature_width].T,
        small_all[feature_width + experts + 2, :lat_half],
        r_expand,
        r_out,
        small_all[feature_width + experts + 1],
        small_all[feature_width : feature_width + experts].T,
        r_sgate,
        r_sup,
        g_sdown,
        g_gate[None],
        g_up[None],
        g_down[None],
    )


def solution(mesh):
    shape = (mesh.shape["expert"], mesh.shape["fsdp"])
    split = shape == (LINE * SQUARE * CORES, SQUARE) and shape[0] == HEAD_COUNT
    return jax.shard_map(
        split_body if split else body,
        mesh=mesh,
        in_specs=(
            P("fsdp", "expert", None),
            P("fsdp", "expert", None),
            P("fsdp", "expert", None),
            P("fsdp"),
            P("fsdp", None),
            P("fsdp", None),
            P("fsdp"),
            P("fsdp", None),
            P("fsdp", None),
            P("fsdp"),
            P("fsdp", None),
            P(("expert", "fsdp"), None),
            P(("expert", "fsdp"), None),
            P(("expert", "fsdp"), None),
            P("expert", None, "fsdp"),
            P("expert", None, "fsdp"),
            P("expert", "fsdp", None),
        ),
        out_specs=(
            P("fsdp", "expert", None),
            P("fsdp", "expert", None),
            P("fsdp"),
            P("fsdp", None),
            P("fsdp", None),
            P("fsdp"),
            P("fsdp", None),
            P("fsdp", None),
            P("fsdp"),
            P("fsdp", None),
            P(("expert", "fsdp"), None),
            P(("expert", "fsdp"), None),
            P(("expert", "fsdp"), None),
            P("expert", None, "fsdp"),
            P("expert", None, "fsdp"),
            P("expert", "fsdp", None),
        ),
        check_vma=False,
    )
```

```python
import functools

import jax
import jax.numpy as jnp
import numpy as np
from jax import lax
from jax.experimental import pallas as pl
from jax.experimental.pallas import tpu as pltpu
from jax.sharding import PartitionSpec as P

MODEL_WIDTH = 2048
HEAD_COUNT = 16
PLAIN_UNITS = 128
ROTARY_UNITS = 64
VALUE_UNITS = 128
LATENT_WIDTH = 512
TOPK = 6


EPS = 1e-06


def matrix_product(left, right):
    return jnp.dot(left, right, preferred_element_type=jnp.float32)


def inner(left, right):
    return lax.dot_general(
        left, right, (((0,), (0,)), ((), ())), preferred_element_type=jnp.float32
    )


def outer_product(left, right):
    return lax.dot_general(
        left, right, (((1,), (1,)), ((), ())), preferred_element_type=jnp.float32
    )


def norm_forward(value, gain):
    inverse = lax.rsqrt(jnp.mean(value * value, axis=-1, keepdims=True) + EPS)
    return (value * inverse * gain, inverse)


def norm_backward(value, inverse, gain, grad):
    unit = value * inverse
    scaled = grad * gain
    d_value = inverse * (scaled - unit * jnp.mean(scaled * unit, axis=-1, keepdims=True))
    return (d_value, jnp.sum(grad * unit, axis=0))


def rope_tables(positions):
    half = ROTARY_UNITS // 2
    freqs = 10000.0 ** (-jnp.arange(half, dtype=jnp.float32) * (2.0 / ROTARY_UNITS))
    angles = positions.astype(jnp.float32)[:, None] * freqs[None, :]
    return (jnp.cos(angles), jnp.sin(angles))


def apply_rotary(value, cosine_table, sine_table):
    half = ROTARY_UNITS // 2
    first = value[..., :half]
    second = value[..., half:]
    return jnp.concatenate(
        [first * cosine_table - second * sine_table, first * sine_table + second * cosine_table],
        axis=-1,
    )


def reverse_rotary(grad, cosine_table, sine_table):
    half = ROTARY_UNITS // 2
    first = grad[..., :half]
    second = grad[..., half:]
    return jnp.concatenate(
        [first * cosine_table + second * sine_table, second * cosine_table - first * sine_table],
        axis=-1,
    )


def silu_parts(value):
    sigma = jax.nn.sigmoid(value)
    return (value * sigma, sigma * (1.0 + value * (1.0 - sigma)))


def body(
    tokens,
    routes,
    cotangent,
    attn_gain,
    w_query,
    latent_weight,
    latent_norm_gain,
    expand_weight,
    w_out,
    ffn_gain,
    w_router,
    shared_gate,
    shared_up,
    shared_down,
    expert_gate,
    expert_up,
    expert_down,
):
    device_local = tokens.shape[1]
    experts = lax.axis_size("expert")
    shards = lax.axis_size("fsdp")
    position = lax.axis_index("expert")
    capacity = shards * (
        (device_local * TOPK * 4 + experts * 3 * shards - 1) // (experts * 3 * shards)
    )
    seq_len = device_local * experts
    feature_width = LATENT_WIDTH + ROTARY_UNITS
    scale = (PLAIN_UNITS + ROTARY_UNITS) ** (-0.5)
    attention_gain_grad, wq, wlat, g_lat, expand_matrix, wout, g_ffn, wrout = (
        lax.all_gather(attn_gain, "fsdp", axis=0, tiled=True),
        lax.all_gather(w_query, "fsdp", axis=0, tiled=True),
        lax.all_gather(latent_weight, "fsdp", axis=0, tiled=True),
        lax.all_gather(latent_norm_gain, "fsdp", axis=0, tiled=True),
        lax.all_gather(expand_weight, "fsdp", axis=0, tiled=True),
        lax.all_gather(w_out, "fsdp", axis=0, tiled=True),
        lax.all_gather(ffn_gain, "fsdp", axis=0, tiled=True),
        lax.all_gather(w_router, "fsdp", axis=0, tiled=True),
    )
    sgate, sup, sdown = (
        lax.all_gather(shared_gate, ("expert", "fsdp"), axis=0, tiled=True),
        lax.all_gather(shared_up, ("expert", "fsdp"), axis=0, tiled=True),
        lax.all_gather(shared_down, ("expert", "fsdp"), axis=0, tiled=True),
    )
    attention_gain_grad = attention_gain_grad.astype(jnp.float32)
    g_lat = g_lat.astype(jnp.float32)
    g_ffn = g_ffn.astype(jnp.float32)
    x_in = tokens[0].astype(jnp.float32)
    grad_out = cotangent[0].astype(jnp.float32)
    positions = position * device_local + jnp.arange(device_local, dtype=jnp.int32)
    cosine_table, sine_table = rope_tables(positions)
    normed, inv_attn = norm_forward(x_in, attention_gain_grad)
    normed_in = normed.astype(jnp.bfloat16)
    query_full = matrix_product(normed_in, wq).reshape(
        device_local, HEAD_COUNT, PLAIN_UNITS + ROTARY_UNITS
    )
    query_nope = query_full[:, :, :PLAIN_UNITS].astype(jnp.bfloat16)
    expanded_latent = expand_matrix.reshape(LATENT_WIDTH, HEAD_COUNT, PLAIN_UNITS + VALUE_UNITS)
    key_part = expanded_latent[:, :, :PLAIN_UNITS]
    value_part = expanded_latent[:, :, PLAIN_UNITS:]
    query_latent = jnp.einsum(
        "thd,chd->thc", query_nope, key_part, preferred_element_type=jnp.float32
    )
    query_rope = apply_rotary(
        query_full[:, :, PLAIN_UNITS:], cosine_table[:, None, :], sine_table[:, None, :]
    )
    token_rows = device_local * HEAD_COUNT
    query = (
        jnp.concatenate([query_latent, query_rope], axis=-1)
        .astype(jnp.bfloat16)
        .reshape(token_rows, feature_width)
    )
    latent_complete = matrix_product(normed_in, wlat)
    packed_rows = latent_complete[:, :LATENT_WIDTH]
    latent_state, inv_lat = norm_forward(packed_rows, g_lat)
    rotary_key = apply_rotary(latent_complete[:, LATENT_WIDTH:], cosine_table, sine_table)
    key = jnp.concatenate([latent_state, rotary_key], axis=-1).astype(jnp.bfloat16)
    keys_all = lax.all_gather(key, "expert", axis=0, tiled=True)
    block = min(512, seq_len)
    token_tally = (position * device_local + device_local + block - 1) // block
    q_pos = position * device_local + jnp.arange(token_rows, dtype=jnp.int32) // HEAD_COUNT

    def scores_of(index):
        key_rows = lax.dynamic_slice_in_dim(keys_all, index * block, block, 0)
        raw = outer_product(query, key_rows)
        k_pos = index * block + jnp.arange(block, dtype=jnp.int32)
        valid = k_pos[None, :] <= q_pos[:, None]
        return (jnp.where(valid, raw * scale, -1e30), key_rows)

    def stats_step(index, carry):
        top, total = carry
        scores, unused = scores_of(index)
        new_top = jnp.maximum(top, jnp.max(scores, axis=1))
        total = total * jnp.exp(top - new_top) + jnp.sum(jnp.exp(scores - new_top[:, None]), axis=1)
        return (new_top, total)

    top, total = lax.fori_loop(
        0,
        token_tally,
        stats_step,
        (jnp.full((token_rows,), -1e30, jnp.float32), jnp.zeros((token_rows,), jnp.float32)),
    )
    log_total = top + jnp.log(total)

    def mixing_update(index, running_total):
        scores, key_rows = scores_of(index)
        weight_arrays = jnp.exp(scores - log_total[:, None]).astype(jnp.bfloat16)
        return running_total + matrix_product(weight_arrays, key_rows[:, :LATENT_WIDTH])

    mixed_output_sum = lax.fori_loop(
        0, token_tally, mixing_update, jnp.zeros((token_rows, LATENT_WIDTH), jnp.float32)
    )
    mixed_output = mixed_output_sum.astype(jnp.bfloat16).reshape(
        device_local, HEAD_COUNT, LATENT_WIDTH
    )
    heads = jnp.einsum("thc,chv->thv", mixed_output, value_part, preferred_element_type=jnp.float32)
    heads = heads.reshape(device_local, HEAD_COUNT * VALUE_UNITS).astype(jnp.bfloat16)
    hidden = x_in + matrix_product(heads, wout)
    normed2, inv_ffn = norm_forward(hidden, g_ffn)
    normed_ffn = normed2.astype(jnp.bfloat16)
    logits = matrix_product(normed_ffn, wrout)
    router = jax.nn.softmax(logits, axis=-1)
    own_routes = routes[0]
    names = jnp.arange(experts, dtype=jnp.int32)
    chosen = (own_routes[:, :, None] == names[None, None, :]).astype(jnp.float32)
    gates = jnp.sum(chosen * router[:, None, :], axis=-1)
    hits = (own_routes.reshape(device_local * TOPK)[:, None] == names[None, :]).astype(jnp.int32)
    slot = jnp.sum((jnp.cumsum(hits, axis=0) - hits) * hits, axis=1)
    place = own_routes.reshape(device_local * TOPK) * capacity + slot
    token_of = jnp.arange(device_local * TOPK, dtype=jnp.int32) // TOPK
    table = jnp.full((experts * capacity,), device_local, jnp.int32).at[place].set(token_of)
    padded = jnp.concatenate([normed_ffn, jnp.zeros((1, MODEL_WIDTH), jnp.bfloat16)], axis=0)
    buffer = padded[table].reshape(experts, capacity, MODEL_WIDTH)
    w_g, w_u, w_d = (expert_gate[0], expert_up[0], expert_down[0])

    def spread(values):
        return jnp.broadcast_to(values[:, None], (experts, shards, capacity, MODEL_WIDTH)).reshape(
            experts * shards, capacity, MODEL_WIDTH
        )

    def collect(back):
        return jnp.sum(back.reshape(experts, shards, capacity, MODEL_WIDTH), axis=1).reshape(
            experts * capacity, MODEL_WIDTH
        )

    received = lax.all_to_all(
        spread(buffer), ("expert", "fsdp"), split_axis=0, concat_axis=0, tiled=True
    )
    ex_rows = received.reshape(-1, MODEL_WIDTH)
    pre_gate = matrix_product(ex_rows, w_g)
    pre_up = matrix_product(ex_rows, w_u)
    act_gate, slope = silu_parts(pre_gate)
    ex_act = (act_gate * pre_up).astype(jnp.bfloat16)
    ex_out = matrix_product(ex_act, w_d).reshape(received.shape)
    returned = lax.all_to_all(
        ex_out.astype(jnp.bfloat16), ("expert", "fsdp"), split_axis=0, concat_axis=0, tiled=True
    ).astype(ex_out.dtype)
    results = collect(returned)
    picked = results[place].reshape(device_local, TOPK, MODEL_WIDTH)
    routed = jnp.sum(gates[:, :, None] * picked, axis=1)
    sh_gate = matrix_product(normed_ffn, sgate)
    sh_up = matrix_product(normed_ffn, sup)
    sh_silu, sh_slope = silu_parts(sh_gate)
    sh_act = (sh_silu * sh_up).astype(jnp.bfloat16)
    shared = matrix_product(sh_act, sdown)
    output = hidden + routed + shared
    d_shared = grad_out.astype(jnp.bfloat16)
    shared_down_gradient = inner(sh_act, d_shared)
    d_sh_act = outer_product(d_shared, sdown)
    d_sh_gate = (d_sh_act * sh_up * sh_slope).astype(jnp.bfloat16)
    d_sh_up = (d_sh_act * sh_silu).astype(jnp.bfloat16)
    shared_gate_gradient = inner(normed_ffn, d_sh_gate)
    shared_up_gradient = inner(normed_ffn, d_sh_up)
    d_normed_ffn = outer_product(d_sh_gate, sgate) + outer_product(d_sh_up, sup)
    d_picked = (
        (gates[:, :, None] * grad_out[:, None, :])
        .astype(jnp.bfloat16)
        .reshape(device_local * TOPK, MODEL_WIDTH)
    )
    d_gates = jnp.sum(picked * grad_out[:, None, :], axis=2)
    d_buffer = (
        jnp.zeros((experts * capacity, MODEL_WIDTH), jnp.bfloat16)
        .at[place]
        .set(d_picked)
        .reshape(experts, capacity, MODEL_WIDTH)
    )
    d_received = lax.all_to_all(
        spread(d_buffer), ("expert", "fsdp"), split_axis=0, concat_axis=0, tiled=True
    )
    d_rows = d_received.reshape(-1, MODEL_WIDTH)
    d_act = outer_product(d_rows, w_d)
    g_down = inner(ex_act, d_rows)
    d_pre_gate = (d_act * pre_up * slope).astype(jnp.bfloat16)
    d_pre_up = (d_act * act_gate).astype(jnp.bfloat16)
    g_gate = inner(ex_rows, d_pre_gate)
    g_up = inner(ex_rows, d_pre_up)
    d_ex_rows = (outer_product(d_pre_gate, w_g) + outer_product(d_pre_up, w_u)).reshape(
        received.shape
    )
    d_returned = lax.all_to_all(
        d_ex_rows.astype(jnp.bfloat16), ("expert", "fsdp"), split_axis=0, concat_axis=0, tiled=True
    ).astype(d_ex_rows.dtype)
    d_results = collect(d_returned)
    d_normed_ffn = d_normed_ffn + jnp.sum(
        d_results[place].reshape(device_local, TOPK, MODEL_WIDTH), axis=1
    )
    d_router = jnp.sum(chosen * d_gates[:, :, None], axis=1)
    d_logits = (router * (d_router - jnp.sum(router * d_router, axis=1, keepdims=True))).astype(
        jnp.bfloat16
    )
    router_weight_gradient = inner(normed_ffn, d_logits)
    d_normed_ffn = d_normed_ffn + outer_product(d_logits, wrout)
    d_hidden_norm, g_ffn_grad = norm_backward(hidden, inv_ffn, g_ffn, d_normed_ffn)
    d_hidden = grad_out + d_hidden_norm
    d_attn = d_hidden.astype(jnp.bfloat16)
    output_weight_gradient = inner(heads, d_attn)
    d_heads = (
        outer_product(d_attn, wout)
        .astype(jnp.bfloat16)
        .reshape(device_local, HEAD_COUNT, VALUE_UNITS)
    )
    value_weight_gradient = jnp.einsum(
        "thc,thv->chv", mixed_output, d_heads, preferred_element_type=jnp.float32
    )
    mixed_gradient = jnp.einsum(
        "thv,chv->thc", d_heads, value_part, preferred_element_type=jnp.float32
    )
    mixed_gradient = mixed_gradient.astype(jnp.bfloat16).reshape(token_rows, LATENT_WIDTH)
    delta = jnp.sum(mixed_gradient.astype(jnp.float32) * mixed_output_sum, axis=1)

    def back_step(index, carry):
        d_query_acc, d_keys_acc = carry
        scores, key_rows = scores_of(index)
        weight_arrays = jnp.exp(scores - log_total[:, None])
        weight_gradients = outer_product(mixed_gradient, key_rows[:, :LATENT_WIDTH])
        d_scores = (weight_arrays * (weight_gradients - delta[:, None]) * scale).astype(
            jnp.bfloat16
        )
        d_query_acc = d_query_acc + matrix_product(d_scores, key_rows)
        d_values = inner(weight_arrays.astype(jnp.bfloat16), mixed_gradient)
        d_block = inner(d_scores, query) + jnp.concatenate(
            [d_values, jnp.zeros((block, ROTARY_UNITS), jnp.float32)], axis=1
        )
        previous = lax.dynamic_slice_in_dim(d_keys_acc, index * block, block, 0)
        return (
            d_query_acc,
            lax.dynamic_update_slice_in_dim(d_keys_acc, previous + d_block, index * block, 0),
        )

    d_query, d_keys = lax.fori_loop(
        0,
        token_tally,
        back_step,
        (
            jnp.zeros((token_rows, feature_width), jnp.float32),
            jnp.zeros((seq_len, feature_width), jnp.float32),
        ),
    )
    key_gradient = lax.psum_scatter(
        d_keys.astype(jnp.bfloat16), "expert", scatter_dimension=0, tiled=True
    )
    query_up_gradient = d_query.astype(jnp.bfloat16).reshape(
        device_local, HEAD_COUNT, feature_width
    )
    query_latent_gradient = query_up_gradient[:, :, :LATENT_WIDTH]
    key_weight_gradient = jnp.einsum(
        "thc,thd->chd", query_latent_gradient, query_nope, preferred_element_type=jnp.float32
    )
    d_q_nope = jnp.einsum(
        "thc,chd->thd", query_latent_gradient, key_part, preferred_element_type=jnp.float32
    )
    d_q_rope = reverse_rotary(
        query_up_gradient[:, :, LATENT_WIDTH:].astype(jnp.float32),
        cosine_table[:, None, :],
        sine_table[:, None, :],
    )
    d_query_full = (
        jnp.concatenate([d_q_nope, d_q_rope], axis=-1)
        .astype(jnp.bfloat16)
        .reshape(device_local, HEAD_COUNT * (PLAIN_UNITS + ROTARY_UNITS))
    )
    query_weight_gradient = inner(normed_in, d_query_full)
    d_normed_in = outer_product(d_query_full, wq)
    latent_gradient = key_gradient[:, :LATENT_WIDTH].astype(jnp.float32)
    rotary_key_gradient = reverse_rotary(
        key_gradient[:, LATENT_WIDTH:].astype(jnp.float32), cosine_table, sine_table
    )
    d_compact, g_lat_grad = norm_backward(packed_rows, inv_lat, g_lat, latent_gradient)
    d_latent_full = jnp.concatenate([d_compact, rotary_key_gradient], axis=-1).astype(jnp.bfloat16)
    latent_weight_gradient = inner(normed_in, d_latent_full)
    d_normed_in = d_normed_in + outer_product(d_latent_full, wlat)
    d_norm_in, g_attn_grad = norm_backward(x_in, inv_attn, attention_gain_grad, d_normed_in)
    d_tokens = (d_hidden + d_norm_in).astype(jnp.bfloat16)
    expand_weight_gradient = jnp.concatenate(
        [key_weight_gradient, value_weight_gradient], axis=-1
    ).reshape(LATENT_WIDTH, HEAD_COUNT * (PLAIN_UNITS + VALUE_UNITS))
    r_sgate, r_sup, r_sdown = (
        lax.psum_scatter(shared_gate_gradient, ("expert", "fsdp"), scatter_dimension=0, tiled=True),
        lax.psum_scatter(shared_up_gradient, ("expert", "fsdp"), scatter_dimension=0, tiled=True),
        lax.psum_scatter(shared_down_gradient, ("expert", "fsdp"), scatter_dimension=0, tiled=True),
    )
    r_attn, r_query, r_latent, r_lgain, r_expand, r_out, r_fgain, r_router = (
        lax.psum_scatter(
            g_attn_grad.astype(jnp.bfloat16), "fsdp", scatter_dimension=0, tiled=True
        ).astype(jnp.float32),
        lax.psum_scatter(
            query_weight_gradient.astype(jnp.bfloat16), "fsdp", scatter_dimension=0, tiled=True
        ).astype(jnp.float32),
        lax.psum_scatter(
            latent_weight_gradient.astype(jnp.bfloat16), "fsdp", scatter_dimension=0, tiled=True
        ).astype(jnp.float32),
        lax.psum_scatter(
            g_lat_grad.astype(jnp.bfloat16), "fsdp", scatter_dimension=0, tiled=True
        ).astype(jnp.float32),
        lax.psum_scatter(
            expand_weight_gradient.astype(jnp.bfloat16), "fsdp", scatter_dimension=0, tiled=True
        ).astype(jnp.float32),
        lax.psum_scatter(
            output_weight_gradient.astype(jnp.bfloat16), "fsdp", scatter_dimension=0, tiled=True
        ).astype(jnp.float32),
        lax.psum_scatter(
            g_ffn_grad.astype(jnp.bfloat16), "fsdp", scatter_dimension=0, tiled=True
        ).astype(jnp.float32),
        lax.psum_scatter(
            router_weight_gradient.astype(jnp.bfloat16), "fsdp", scatter_dimension=0, tiled=True
        ).astype(jnp.float32),
    )
    r_attn, r_query, r_latent, r_lgain, r_expand, r_out, r_fgain, r_router = (
        lax.psum(r_attn.astype(jnp.bfloat16), "expert").astype(jnp.float32),
        lax.psum(r_query.astype(jnp.bfloat16), "expert").astype(jnp.float32),
        lax.psum(r_latent.astype(jnp.bfloat16), "expert").astype(jnp.float32),
        lax.psum(r_lgain.astype(jnp.bfloat16), "expert").astype(jnp.float32),
        lax.psum(r_expand.astype(jnp.bfloat16), "expert").astype(jnp.float32),
        lax.psum(r_out.astype(jnp.bfloat16), "expert").astype(jnp.float32),
        lax.psum(r_fgain.astype(jnp.bfloat16), "expert").astype(jnp.float32),
        lax.psum(r_router.astype(jnp.bfloat16), "expert").astype(jnp.float32),
    )
    return (
        output.astype(jnp.bfloat16)[None],
        d_tokens[None],
        r_attn,
        r_query,
        r_latent,
        r_lgain,
        r_expand,
        r_out,
        r_fgain,
        r_router,
        r_sgate,
        r_sup,
        r_sdown,
        g_gate[None],
        g_up[None],
        g_down[None],
    )


LINE = 4
SQUARE = 2
CORES = 2
MESH = pl.DeviceIdType.MESH
VMEM_LIMIT = 56 * 1024 * 1024


class Place:
    def __init__(self):
        index = lax.axis_index("expert")
        self.y = lax.axis_index("fsdp")
        self.c = lax.rem(index, CORES)
        self.b = lax.rem(lax.div(index, CORES), SQUARE)
        self.a = lax.div(index, CORES * SQUARE)

    def device(self, da=0, db=0, dc=0, dy=0):
        b = 1 - self.b if db else self.b
        c = 1 - self.c if dc else self.c
        y = 1 - self.y if dy else self.y
        return (((self.a + da) * SQUARE + b) * CORES + c, y)

    def block(self, full, a, db=0, dc=0, dy=0):
        b = 1 - self.b if db else self.b
        c = 1 - self.c if dc else self.c
        y = 1 - self.y if dy else self.y
        flat = (a * SQUARE + b) * CORES + c
        return y * (LINE * SQUARE * CORES) + flat if full else flat

    def greet(self, with_y):
        barrier = pltpu.get_barrier_semaphore()
        near = [dict(db=1), dict(dc=1)] + ([dict(dy=1)] if with_y else [])
        for step in near:
            pl.semaphore_signal(barrier, inc=1, device_id=self.device(**step), device_id_type=MESH)

        @pl.when(self.a > 0)
        def _():
            pl.semaphore_signal(barrier, inc=1, device_id=self.device(da=-1), device_id_type=MESH)

        @pl.when(self.a < LINE - 1)
        def _():
            pl.semaphore_signal(barrier, inc=1, device_id=self.device(da=1), device_id_type=MESH)

        ends = jnp.logical_or(self.a == 0, self.a == LINE - 1).astype(jnp.int32)
        pl.semaphore_wait(barrier, len(near) + 2 - ends)


class Sender:
    def __init__(self, place, sems):
        self.place, self.sems, self.pending = place, sems, []

    def send(self, src, dst, recv_sem, step, cond=None):
        sem = self.sems.at[len(self.pending)]

        def make():
            return pltpu.make_async_remote_copy(
                src_ref=src,
                dst_ref=dst,
                send_sem=sem,
                recv_sem=recv_sem,
                device_id=self.place.device(**step),
                device_id_type=MESH,
            )

        def start():
            make().start()

        guarded(cond, start)
        self.pending.append((cond, lambda: make().wait_send()))

    def arrived(self, dst, recv_sem):
        pltpu.make_async_remote_copy(
            src_ref=dst,
            dst_ref=dst,
            send_sem=self.sems.at[0],
            recv_sem=recv_sem,
            device_id=self.place.device(dc=1),
            device_id_type=MESH,
        ).wait_recv()

    def finish(self):
        for cond, wait in self.pending:
            guarded(cond, wait)


def guarded(cond, action):
    if cond is None:
        action()
    else:
        pl.when(cond)(action)


def both(first, second):
    if first is None or second is None:
        return second if first is None else first
    return jnp.logical_and(first, second)


def gather_ticks(place, sender, full, gated, ins, outs, local_sems, recv_sems):
    a = place.a
    count = len(ins)

    def own_copy(at):
        return pltpu.make_async_copy(
            ins[at], outs[at].at[place.block(full, a)], local_sems.at[at]
        )

    def chunk(at, block, half):
        size = ins[at].shape[0] // 2
        return outs[at].at[block, pl.ds(half * size, size)]

    def sem_of(at, block, half):
        return recv_sems.at[at, block * 2 + half]

    def forward(at, block, half, src, step, cond=None):
        sender.send(src, chunk(at, block, half), sem_of(at, block, half), step, cond)

    def receive(at, block, half, cond):
        guarded(cond, lambda: sender.arrived(chunk(at, block, half), sem_of(at, block, half)))

    def held_by(at, delta, cond):
        if at not in gated:
            return cond
        return both(cond, lax.div(a + delta, LINE // 2) == place.y)

    def from_line(delta, always):
        for half in range(2):
            for at in range(count):
                block = place.block(full, a + delta)
                cond = held_by(at, delta, always)
                size = ins[at].shape[0] // 2
                if delta == 0:
                    src = ins[at].at[pl.ds(half * size, size)]
                else:
                    receive(at, block, half, cond)
                    src = chunk(at, block, half)
                if delta <= 0:
                    forward(at, block, half, src, dict(da=1), both(cond, a < LINE - 1))
                if delta >= 0:
                    forward(at, block, half, src, dict(da=-1), both(cond, a > 0))
                forward(at, block, half, src, dict(db=1), cond)
                if full:
                    forward(at, block, half, src, dict(dy=1), cond)
                forward(at, block, half, src, dict(dc=1), cond)

    def from_side(delta, always):
        for half in range(2):
            for at in range(count):
                cond = held_by(at, delta, always)
                block = place.block(full, a + delta, db=1)
                receive(at, block, half, cond)
                if full and half == 0:
                    forward(at, block, half, chunk(at, block, half), dict(dy=1), cond)
                forward(at, block, half, chunk(at, block, half), dict(dc=1), cond)
                if full:
                    block = place.block(full, a + delta, dy=1)
                    receive(at, block, half, cond)
                    if half == 1:
                        forward(at, block, half, chunk(at, block, half), dict(db=1), cond)
                    forward(at, block, half, chunk(at, block, half), dict(dc=1), cond)

    def from_corner(delta, always):
        for half in range(2):
            for at in range(count):
                cond = held_by(at, delta, always)
                block = place.block(True, a + delta, db=1, dy=1)
                receive(at, block, half, cond)
                forward(at, block, half, chunk(at, block, half), dict(dc=1), cond)

    def from_sibling(delta, always):
        for half in range(2):
            for at in range(count):
                cond = held_by(at, delta, always)
                for db in range(2):
                    for dy in range(2 if full else 1):
                        receive(at, place.block(full, a + delta, db=db, dc=1, dy=dy), half, cond)

    rounds = [[(0, None)]]
    for s in range(1, LINE):
        rounds.append([(-s, a >= s), (s, a + s < LINE)])
    stages = [from_line, from_side] + ([from_corner] if full else []) + [from_sibling]

    def tick(number):
        if number == 0:
            for at in range(count):
                own_copy(at).start()
        for level, stage in enumerate(stages):
            if 0 <= number - level < len(rounds):
                for delta, cond in rounds[number - level]:
                    stage(delta, cond)
        if number == len(rounds) + len(stages) - 2:
            for at in range(count):
                own_copy(at).wait()

    return [functools.partial(tick, number) for number in range(len(rounds) + len(stages) - 1)]


def send_pairs(sender, ins, outs, sems):
    for at, (src, dst) in enumerate(zip(ins, outs)):
        sender.send(src, dst, sems.at[at], dict(dy=1))


def take_pairs(sender, outs, sems):
    for at, dst in enumerate(outs):
        sender.arrived(dst, sems.at[at])


def gather_kernel(full, count, pairs, halved, gated, *refs):
    arrays = count + pairs + halved
    ins, outs = refs[:arrays], refs[arrays : 2 * arrays]
    local_sems, send_sems, recv_sems, pair_sems, half_sems = refs[2 * arrays :]
    place = Place()
    sender = Sender(place, send_sems)
    place.greet(full or pairs + halved > 0)
    shared = range(count + pairs, arrays)

    def part(ref, core):
        size = ref.shape[0] // CORES
        return ref.at[pl.ds(pl.multiple_of(core * size, 16), size)]

    send_pairs(sender, ins[count : count + pairs], outs[count : count + pairs], pair_sems)
    for at in shared:
        sender.send(
            part(ins[at], place.c), part(outs[at], place.c), half_sems.at[at - count - pairs, 0],
            dict(dy=1),
        )
    ticks = gather_ticks(
        place, sender, full, gated, ins[:count], outs[:count], local_sems, recv_sems
    )
    for number, tick in enumerate(ticks):
        if number == len(ticks) - 1:
            for at in shared:
                here = part(outs[at], place.c)
                sender.arrived(here, half_sems.at[at - count - pairs, 0])
                sender.send(here, here, half_sems.at[at - count - pairs, 1], dict(dc=1))
        tick()
    for at in shared:
        sender.arrived(part(outs[at], 1 - place.c), half_sems.at[at - count - pairs, 1])
    take_pairs(sender, outs[count : count + pairs], pair_sems)
    sender.finish()


def gather_rows(arrays, full, collective_id, swapped=(), halved=(), gated=()):
    blocks = LINE * SQUARE * CORES * (SQUARE if full else 1)
    count, pairs, shared = len(arrays), len(swapped), len(halved)
    lines = 2 * LINE - 1
    sends = pairs + 2 * shared + count * lines * 2 * (9 if full else 5)
    moved = sum(blocks * 2 * x.size * x.dtype.itemsize for x in arrays)
    return pl.pallas_call(
        functools.partial(gather_kernel, full, count, pairs, shared, gated),
        out_shape=[jax.ShapeDtypeStruct((blocks,) + x.shape, x.dtype) for x in arrays]
        + [jax.ShapeDtypeStruct(x.shape, x.dtype) for x in (*swapped, *halved)],
        in_specs=[pl.BlockSpec(memory_space=pl.ANY)] * (count + pairs + shared),
        out_specs=[pl.BlockSpec(memory_space=pl.ANY)] * (count + pairs + shared),
        scratch_shapes=[
            pltpu.SemaphoreType.DMA((count,)),
            pltpu.SemaphoreType.DMA((sends,)),
            pltpu.SemaphoreType.DMA((count, blocks * 2)),
            pltpu.SemaphoreType.DMA((max(pairs, 1),)),
            pltpu.SemaphoreType.DMA((max(shared, 1), 2)),
        ],
        compiler_params=pltpu.CompilerParams(collective_id=collective_id, has_side_effects=True),
        cost_estimate=pl.CostEstimate(flops=0, bytes_accessed=6 * moved, transcendentals=0),
    )(*arrays, *swapped, *halved)


def add_rows(target, sources, size):
    def step(at, carry):
        rows = pl.ds(pl.multiple_of(at * 16, 16), 16)
        total = sources[0][rows, :].astype(jnp.float32)
        for source in sources[1:]:
            total = total + source[rows, :].astype(jnp.float32)
        target[rows, :] = total.astype(target.dtype)
        return carry

    lax.fori_loop(0, size // 16, step, 0)


def scatter_ticks(place, sender, full, part, out, scratch):
    mine, got, side, up, down, load_sems, recv_sems = scratch
    a = place.a
    kinds = 4 if full else 2
    size = part.shape[1]
    half = size // 2
    order = [LINE - 1, 0, LINE - 2, 1]
    walk = (3, 1, 2, 0) if full else (1, 0)

    def sem_of(group, target, kind):
        return recv_sems.at[group, target * 4 + kind]

    def load(target, kind):
        block = place.block(full, target, db=kind % 2, dy=kind // 2)
        return pltpu.make_async_copy(
            part.at[block], mine.at[target, kind], load_sems.at[target * 4 + kind]
        )

    def begin():
        for target in order:
            for kind in walk:
                load(target, kind).start()
                block = place.block(full, target, db=kind % 2, dc=1, dy=kind // 2)
                sender.send(
                    part.at[block], got.at[target, kind], sem_of(0, target, kind), dict(dc=1)
                )

    def rows_of(ref, which):
        return ref.at[pl.ds(which * half, half)]

    def over_cores(target):
        for kind in walk:
            load(target, kind).wait()
            sender.arrived(got.at[target, kind], sem_of(0, target, kind))
            add_rows(mine.at[target, kind], [mine.at[target, kind], got.at[target, kind]], size)
            held = mine.at[target, kind]
            if kind == 3:
                sender.send(rows_of(held, 0), side.at[target, 4], sem_of(1, target, 0), dict(db=1))
                sender.send(rows_of(held, 1), side.at[target, 5], sem_of(1, target, 1), dict(dy=1))
            if kind == 1:
                sender.send(rows_of(held, 0), side.at[target, 0], sem_of(2, target, 0), dict(db=1))
                if not full:
                    sender.send(
                        rows_of(held, 1), side.at[target, 1], sem_of(2, target, 1), dict(db=1)
                    )
            if kind == 2:
                sender.send(rows_of(held, 1), side.at[target, 3], sem_of(2, target, 3), dict(dy=1))

    def over_corner(target):
        sender.arrived(side.at[target, 4], sem_of(1, target, 0))
        held = rows_of(mine.at[target, 2], 0)
        add_rows(held, [held, side.at[target, 4]], half)
        sender.send(held, side.at[target, 2], sem_of(2, target, 2), dict(dy=1))
        sender.arrived(side.at[target, 5], sem_of(1, target, 1))
        held = rows_of(mine.at[target, 1], 1)
        add_rows(held, [held, side.at[target, 5]], half)
        sender.send(held, side.at[target, 1], sem_of(2, target, 1), dict(db=1))

    def gathered(target, which):
        held = rows_of(mine.at[target, 0], which)
        parts = [held]
        for source in (0, 2) if full else (0,):
            sender.arrived(side.at[target, source + which], sem_of(2, target, source + which))
            parts.append(side.at[target, source + which])
        return held, parts

    def line_slots(target, which):
        below, above = rows_of(up.at[target], which), rows_of(down.at[target], which)
        return below, sem_of(3, target, which), above, sem_of(3, target, 2 + which)

    def over_line(target):
        def relay(which, slot, slot_sem, at_end):
            held, parts = gathered(target, which)

            def with_slot():
                sender.arrived(slot, slot_sem)
                add_rows(held, parts + [slot], half)

            pl.when(jnp.logical_not(at_end))(with_slot)
            pl.when(at_end)(lambda: add_rows(held, parts, half))

        for which in range(2):
            below, below_sem, above, above_sem = line_slots(target, which)
            held = rows_of(mine.at[target, 0], which)
            if target > 0:
                pl.when(a < target)(
                    functools.partial(relay, which, below, below_sem, a == 0)
                )
                sender.send(held, below, below_sem, dict(da=1), a < target)
            if target < LINE - 1:
                pl.when(a > target)(
                    functools.partial(relay, which, above, above_sem, a == LINE - 1)
                )
                sender.send(held, above, above_sem, dict(da=-1), a > target)

    def own_total(target):
        for which in range(2):
            below, below_sem, above, above_sem = line_slots(target, which)
            _, parts = gathered(target, which)
            if target > 0:
                sender.arrived(below, below_sem)
                parts.append(below)
            if target < LINE - 1:
                sender.arrived(above, above_sem)
                parts.append(above)
            add_rows(rows_of(out, which), parts, half)

    stages = [over_cores] + ([over_corner] if full else []) + [over_line]

    def tick(number):
        if number == 0:
            begin()
        for level, stage in enumerate(stages):
            if 0 <= number - level < len(order):
                stage(order[number - level])
        if number == len(order) + len(stages) - 2:
            for target in range(LINE):
                pl.when(a == target)(functools.partial(own_total, target))

    return [functools.partial(tick, number) for number in range(len(order) + len(stages) - 1)]


def scatter_kernel(full, pairs, part, *refs):
    ins, out, outs = refs[:pairs], refs[pairs], refs[pairs + 1 : 2 * pairs + 1]
    mine, got, side, up, down, load_sems, send_sems, recv_sems, pair_sems = refs[2 * pairs + 1 :]
    place = Place()
    sender = Sender(place, send_sems)
    place.greet(full or pairs > 0)
    send_pairs(sender, ins, outs, pair_sems)
    scratch = (mine, got, side, up, down, load_sems, recv_sems)
    for tick in scatter_ticks(place, sender, full, part, out, scratch):
        tick()
    take_pairs(sender, outs, pair_sems)
    sender.finish()


def scatter_scratch(full, rows, width, dtype, pairs):
    kinds = 4 if full else 2
    return [
        pltpu.VMEM((LINE, kinds, rows, width), dtype),
        pltpu.VMEM((LINE, kinds, rows, width), dtype),
        pltpu.VMEM((LINE, 6, rows // 2, width), dtype),
        pltpu.VMEM((LINE, rows, width), dtype),
        pltpu.VMEM((LINE, rows, width), dtype),
        pltpu.SemaphoreType.DMA((LINE * 4,)),
        pltpu.SemaphoreType.DMA((pairs + LINE * (4 + 6 + 4),)),
        pltpu.SemaphoreType.DMA((4, LINE * 4)),
        pltpu.SemaphoreType.DMA((max(pairs, 1),)),
    ]


def gather_scatter_kernel(count, gated, *refs):
    ins, part = refs[:count], refs[count]
    outs, total = refs[count + 1 : 2 * count + 1], refs[2 * count + 1]
    local_sems, gather_sends, gather_recvs = refs[2 * count + 2 : 2 * count + 5]
    mine, got, side, up, down, load_sems, scatter_sends, scatter_recvs, _ = refs[2 * count + 5 :]
    place = Place()
    gatherer = Sender(place, gather_sends)
    scatterer = Sender(place, scatter_sends)
    place.greet(True)
    scratch = (mine, got, side, up, down, load_sems, scatter_recvs)
    ticks = [
        scatter_ticks(place, scatterer, True, part, total, scratch),
        gather_ticks(place, gatherer, False, gated, ins, outs, local_sems, gather_recvs),
    ]
    for number in range(max(len(steps) for steps in ticks)):
        for steps in ticks:
            if number < len(steps):
                steps[number]()
    scatterer.finish()
    gatherer.finish()


def gather_and_scatter(arrays, part, collective_id, gated=()):
    blocks = LINE * SQUARE * CORES
    count = len(arrays)
    _, rows, width = part.shape
    sends = count * (2 * LINE - 1) * 2 * 5
    moved = sum(blocks * 2 * x.size * x.dtype.itemsize for x in arrays)
    return pl.pallas_call(
        functools.partial(gather_scatter_kernel, count, gated),
        out_shape=[jax.ShapeDtypeStruct((blocks,) + x.shape, x.dtype) for x in arrays]
        + [jax.ShapeDtypeStruct((rows, width), jnp.float32)],
        in_specs=[pl.BlockSpec(memory_space=pl.ANY)] * (count + 1),
        out_specs=[pl.BlockSpec(memory_space=pl.ANY)] * count
        + [pl.BlockSpec(memory_space=pltpu.VMEM)],
        scratch_shapes=[
            pltpu.SemaphoreType.DMA((count,)),
            pltpu.SemaphoreType.DMA((sends,)),
            pltpu.SemaphoreType.DMA((count, blocks * 2)),
        ]
        + scatter_scratch(True, rows, width, part.dtype, 0),
        compiler_params=pltpu.CompilerParams(
            collective_id=collective_id, has_side_effects=True, vmem_limit_bytes=VMEM_LIMIT
        ),
        cost_estimate=pl.CostEstimate(flops=0, bytes_accessed=6 * moved, transcendentals=0),
    )(*arrays, part)


def scatter_rows(part, full, collective_id, swapped=()):
    blocks, rows, width = part.shape
    pairs = len(swapped)
    return pl.pallas_call(
        functools.partial(scatter_kernel, full, pairs),
        out_shape=[jax.ShapeDtypeStruct((rows, width), jnp.float32)]
        + [jax.ShapeDtypeStruct(x.shape, x.dtype) for x in swapped],
        in_specs=[pl.BlockSpec(memory_space=pl.ANY)] * (1 + pairs),
        out_specs=[pl.BlockSpec(memory_space=pltpu.VMEM)]
        + [pl.BlockSpec(memory_space=pl.ANY)] * pairs,
        scratch_shapes=scatter_scratch(full, rows, width, part.dtype, pairs),
        compiler_params=pltpu.CompilerParams(
            collective_id=collective_id, has_side_effects=True, vmem_limit_bytes=VMEM_LIMIT
        ),
        cost_estimate=pl.CostEstimate(
            flops=0, bytes_accessed=12 * part.size * part.dtype.itemsize, transcendentals=0
        ),
    )(part, *swapped)


def contract_last(left, right):
    return lax.dot_general(
        left, right, (((1,), (1,)), ((), ())), preferred_element_type=jnp.float32
    )


def contract_first(left, right):
    return lax.dot_general(
        left, right, (((0,), (0,)), ((), ())), preferred_element_type=jnp.float32
    )


def expert_kernel(
    capacity,
    normed,
    grads,
    routes,
    router_rows,
    w_gate,
    w_up,
    w_down,
    shared_in,
    shared_out,
    out_part,
    d_part,
    ex_rows,
    ex_grads,
    act_out,
    d_gate_out,
    d_up_out,
    shared_in_grad,
    shared_out_grad,
    in_total,
    out_total,
):
    position = lax.axis_index("expert")
    experts = lax.axis_size("expert")
    group, rows, width = normed.shape
    tokens, slots = group * rows, group * capacity
    bf16 = jnp.bfloat16
    x = normed[...].reshape(tokens, width)
    g = grads[...].reshape(tokens, width)

    row = lax.broadcasted_iota(jnp.int32, (tokens, tokens), 0)
    column = lax.broadcasted_iota(jnp.int32, (tokens, tokens), 1)
    before = jnp.logical_and(column < row, lax.div(row, rows) == lax.div(column, rows))
    named = routes[...].reshape(tokens, -1) == position.astype(jnp.float32).astype(bf16)
    hit = jnp.sum(jnp.where(named, 1.0, 0.0), axis=1, keepdims=True)
    tally = matrix_product(
        jnp.where(before, 1.0, 0.0).astype(bf16),
        jnp.broadcast_to(hit, (tokens, 128)).astype(bf16),
    )
    place = jnp.where(hit > 0.5, tally[:, :1], -1.0)
    token = lax.broadcasted_iota(jnp.int32, (tokens, slots), 0)
    slot = lax.broadcasted_iota(jnp.int32, (tokens, slots), 1)
    same = lax.div(slot, capacity) == lax.div(token, rows)
    wanted = lax.rem(slot, capacity).astype(jnp.float32)
    chosen = jnp.where(jnp.logical_and(same, wanted == place), 1.0, 0.0)
    pick = chosen.T.astype(bf16)
    put = chosen.astype(bf16)

    r = matrix_product(pick, x).astype(bf16)
    gr = matrix_product(pick, g).astype(bf16)
    ex_rows[...] = r
    ex_grads[...] = gr
    lane = lax.broadcasted_iota(jnp.int32, (slots, router_rows.shape[0]), 1)
    logits = jnp.where(lane < experts, contract_last(r, router_rows[...]), -1e30)
    exps = jnp.exp(logits - jnp.max(logits, axis=1, keepdims=True))
    gate = jnp.sum(jnp.where(lane == position, exps, 0.0), axis=1, keepdims=True) / jnp.sum(
        exps, axis=1, keepdims=True
    )

    pre_gate = contract_last(r, w_gate[...])
    pre_up = contract_last(r, w_up[...])
    act_gate, slope = silu_parts(pre_gate)
    act = act_gate * pre_up
    back = contract_last(gr, w_down[...])
    d_gate_slot = jnp.sum(act * back, axis=1, keepdims=True)
    scaled = (gate * act).astype(bf16)
    d_act = gate * back
    d_pre_gate = (d_act * pre_up * slope).astype(bf16)
    d_pre_up = (d_act * act_gate).astype(bf16)
    act_out[...] = scaled
    d_gate_out[...] = d_pre_gate
    d_up_out[...] = d_pre_up
    ex_out = matrix_product(scaled, w_down[...]).astype(bf16)
    d_ex = matrix_product(d_pre_gate, w_gate[...]) + matrix_product(d_pre_up, w_up[...])
    d_ex = d_ex.astype(bf16)

    units = shared_out.shape[0]
    mix = matrix_product(x, shared_in[...])
    sh_gate, sh_up = mix[:, :units], mix[:, units:]
    sh_silu, sh_slope = silu_parts(sh_gate)
    sh_act = (sh_silu * sh_up).astype(bf16)
    d_sh_act = contract_last(g, shared_out[...])
    d_mix = jnp.concatenate([d_sh_act * sh_up * sh_slope, d_sh_act * sh_silu], axis=1)
    d_mix = d_mix.astype(bf16)

    out = matrix_product(put, ex_out) + matrix_product(sh_act, shared_out[...])
    out_part[...] = out.astype(bf16).reshape(group, rows, width)
    d_in = matrix_product(put, d_ex) + contract_last(d_mix, shared_in[...])
    d_part[:, :, :width] = d_in.astype(bf16).reshape(group, rows, width)
    lane = lax.broadcasted_iota(jnp.int32, (slots, d_part.shape[2] - width), 1)
    d_gates = jnp.where(lane == position, d_gate_slot, 0.0).astype(bf16)
    d_part[:, :, width:] = matrix_product(put, d_gates).astype(bf16).reshape(group, rows, -1)

    step = pl.program_id(0)

    @pl.when(step == 0)
    def _():
        in_total[...] = jnp.zeros_like(in_total)
        out_total[...] = jnp.zeros_like(out_total)

    in_total[...] += contract_first(d_mix, x)
    out_total[...] += contract_first(sh_act, g)

    @pl.when(step == pl.num_programs(0) - 1)
    def _():
        shared_in_grad[...] = in_total[...].T.astype(bf16)
        shared_out_grad[...] = out_total[...]


def expert_phase(
    all_normed, all_grads, router_rows, w_gate, w_up, w_down, shared_in, shared_out, capacity
):
    blocks, rows, width = all_normed.shape
    group = 4
    slots = group * capacity
    hidden = w_gate.shape[0]
    units = shared_out.shape[0]
    side = all_grads.shape[2] - width
    bf16 = jnp.bfloat16

    def by_group(shape):
        zeros = (0,) * (len(shape) - 1)
        return pl.BlockSpec(shape, lambda i: (i,) + zeros)

    def fixed(shape):
        return pl.BlockSpec(
            shape, lambda i: (0,) * len(shape), pipeline_mode=pl.Buffered(buffer_count=1)
        )

    return pl.pallas_call(
        functools.partial(expert_kernel, capacity),
        grid=(blocks // group,),
        out_shape=[
            jax.ShapeDtypeStruct((blocks, rows, width), bf16),
            jax.ShapeDtypeStruct((blocks, rows, width + side), bf16),
            jax.ShapeDtypeStruct((blocks * capacity, width), bf16),
            jax.ShapeDtypeStruct((blocks * capacity, width), bf16),
            jax.ShapeDtypeStruct((blocks * capacity, hidden), bf16),
            jax.ShapeDtypeStruct((blocks * capacity, hidden), bf16),
            jax.ShapeDtypeStruct((blocks * capacity, hidden), bf16),
            jax.ShapeDtypeStruct((width, 2 * units), bf16),
            jax.ShapeDtypeStruct((units, width), jnp.float32),
        ],
        in_specs=[
            by_group((group, rows, width)),
            by_group((group, rows, width)),
            pl.BlockSpec((group, rows, side), lambda i: (i, 0, width // side)),
            fixed(router_rows.shape),
            fixed(w_gate.shape),
            fixed(w_up.shape),
            fixed(w_down.shape),
            fixed(shared_in.shape),
            fixed(shared_out.shape),
        ],
        out_specs=[
            by_group((group, rows, width)),
            by_group((group, rows, width + side)),
            by_group((slots, width)),
            by_group((slots, width)),
            by_group((slots, hidden)),
            by_group((slots, hidden)),
            by_group((slots, hidden)),
            fixed((width, 2 * units)),
            fixed((units, width)),
        ],
        scratch_shapes=[
            pltpu.VMEM((2 * units, width), jnp.float32),
            pltpu.VMEM((units, width), jnp.float32),
        ],
        compiler_params=pltpu.CompilerParams(vmem_limit_bytes=VMEM_LIMIT),
        cost_estimate=pl.CostEstimate(
            flops=2 * blocks * capacity * width * hidden * 6,
            bytes_accessed=10 * blocks * rows * width * 2,
            transcendentals=blocks * capacity * hidden,
        ),
    )(all_normed, all_grads, all_grads, router_rows, w_gate, w_up, w_down, shared_in, shared_out)


def exchange_kernel(x, out, local_sem, send_sems, recv_sems):
    me, y = lax.axis_index("expert"), lax.axis_index("fsdp")
    count = x.shape[0]
    barrier = pltpu.get_barrier_semaphore()
    peers = [lax.rem(me + step, count) for step in range(1, count)]
    for peer in peers:
        pl.semaphore_signal(barrier, inc=1, device_id=(peer, y), device_id_type=MESH)
    own = pltpu.make_async_copy(x.at[me], out.at[me], local_sem)
    own.start()
    pl.semaphore_wait(barrier, count - 1)
    copies = []
    for at, peer in enumerate(peers):
        copy = pltpu.make_async_remote_copy(
            src_ref=x.at[peer],
            dst_ref=out.at[me],
            send_sem=send_sems.at[at],
            recv_sem=recv_sems.at[at],
            device_id=(peer, y),
            device_id_type=MESH,
        )
        copy.start()
        copies.append(copy)
    for copy in copies:
        copy.wait()
    own.wait()


def exchange(x, collective_id):
    count = x.shape[0]
    return pl.pallas_call(
        exchange_kernel,
        out_shape=jax.ShapeDtypeStruct(x.shape, x.dtype),
        in_specs=[pl.BlockSpec(memory_space=pl.ANY)],
        out_specs=pl.BlockSpec(memory_space=pl.ANY),
        scratch_shapes=[
            pltpu.SemaphoreType.DMA,
            pltpu.SemaphoreType.DMA((count - 1,)),
            pltpu.SemaphoreType.DMA((count - 1,)),
        ],
        compiler_params=pltpu.CompilerParams(collective_id=collective_id, has_side_effects=True),
        cost_estimate=pl.CostEstimate(
            flops=0, bytes_accessed=20 * x.size * x.dtype.itemsize, transcendentals=0
        ),
    )(x)


def swap_halves(value):
    half = value.shape[1] // 2
    return jnp.concatenate([value[:, half:], value[:, :half]], axis=1)


def greet_plane(place):
    me = lax.axis_index("expert")
    count = LINE * SQUARE * CORES
    barrier = pltpu.get_barrier_semaphore()
    for step in range(1, count):
        peer = (lax.rem(me + step, count), place.y)
        pl.semaphore_signal(barrier, inc=1, device_id=peer, device_id_type=MESH)
    pl.semaphore_signal(barrier, inc=1, device_id=place.device(dy=1), device_id_type=MESH)
    pl.semaphore_wait(barrier, count)


def sums_kernel(pairs, moved, small, large, *refs):
    ins = refs[:pairs]
    moved_out, small_out, large_out = refs[pairs : pairs + 3]
    outs = refs[pairs + 3 : 2 * pairs + 3]
    rest = refs[2 * pairs + 3 :]
    local_sem, exchange_sends, exchange_recvs = rest[:3]
    first, second = rest[3:12], rest[12:21]
    place = Place()
    me = lax.axis_index("expert")
    count = moved.shape[0]
    greet_plane(place)
    own = pltpu.make_async_copy(moved.at[me], moved_out.at[me], local_sem)
    own.start()
    copies = []
    for at in range(count - 1):
        copy = pltpu.make_async_remote_copy(
            src_ref=moved.at[lax.rem(me + at + 1, count)],
            dst_ref=moved_out.at[me],
            send_sem=exchange_sends.at[at],
            recv_sem=exchange_recvs.at[at],
            device_id=(lax.rem(me + at + 1, count), place.y),
            device_id_type=MESH,
        )
        copy.start()
        copies.append(copy)
    senders = [Sender(place, first[6]), Sender(place, second[6])]
    send_pairs(senders[0], ins, outs, first[8])
    ticks = [
        scatter_ticks(place, senders[0], False, small, small_out, first[:6] + (first[7],)),
        scatter_ticks(place, senders[1], True, large, large_out, second[:6] + (second[7],)),
    ]
    for number in range(max(len(steps) for steps in ticks)):
        for steps in ticks:
            if number < len(steps):
                steps[number]()
    take_pairs(senders[0], outs, first[8])
    for sender in senders:
        sender.finish()
    for copy in copies:
        copy.wait()
    own.wait()


def exchange_and_sums(moved, small, large, swapped, collective_id):
    count, pairs = moved.shape[0], len(swapped)
    hbm = pl.BlockSpec(memory_space=pl.ANY)
    vmem = pl.BlockSpec(memory_space=pltpu.VMEM)
    return pl.pallas_call(
        functools.partial(sums_kernel, pairs),
        out_shape=[
            jax.ShapeDtypeStruct(moved.shape, moved.dtype),
            jax.ShapeDtypeStruct(small.shape[1:], jnp.float32),
            jax.ShapeDtypeStruct(large.shape[1:], jnp.float32),
        ]
        + [jax.ShapeDtypeStruct(x.shape, x.dtype) for x in swapped],
        in_specs=[hbm] * (3 + pairs),
        out_specs=[hbm, vmem, vmem] + [hbm] * pairs,
        scratch_shapes=[
            pltpu.SemaphoreType.DMA,
            pltpu.SemaphoreType.DMA((count - 1,)),
            pltpu.SemaphoreType.DMA((count - 1,)),
        ]
        + scatter_scratch(False, *small.shape[1:], small.dtype, pairs)
        + scatter_scratch(True, *large.shape[1:], large.dtype, 0),
        compiler_params=pltpu.CompilerParams(
            collective_id=collective_id, has_side_effects=True, vmem_limit_bytes=VMEM_LIMIT
        ),
        cost_estimate=pl.CostEstimate(
            flops=0, bytes_accessed=12 * large.size * 2, transcendentals=0
        ),
    )(moved, small, large, *swapped)


def attend_kernel(
    rows,
    g_attn,
    w_front,
    g_lat,
    expand_head,
    cosines,
    sines,
    normed_out,
    latent_out,
    query_out,
    key_out,
    value_out,
    head_out,
    sum_out,
    log_out,
    keys,
    values,
):
    bf16 = jnp.bfloat16
    size = rows.shape[0]
    scale = (PLAIN_UNITS + ROTARY_UNITS) ** (-0.5)
    step = pl.program_id(0)
    normed, _ = norm_forward(rows[...].astype(jnp.float32), g_attn[...])
    normed = normed.astype(bf16)
    normed_out[...] = normed
    front = contract_last(normed, w_front[...])
    latent, _ = norm_forward(front[:, :LATENT_WIDTH], g_lat[...])
    latent = latent.astype(bf16)
    latent_out[...] = latent
    width = LATENT_WIDTH + ROTARY_UNITS

    def rotated(value):
        return value * cosines[...] + swap_halves(value) * sines[...]

    pairs = matrix_product(latent, expand_head[...])
    key = jnp.concatenate([pairs[:, :PLAIN_UNITS], rotated(front[:, LATENT_WIDTH:width])], axis=1)
    query = jnp.concatenate(
        [front[:, width : width + PLAIN_UNITS], rotated(front[:, width + PLAIN_UNITS :])], axis=1
    ).astype(bf16)
    key = key.astype(bf16)
    value = pairs[:, PLAIN_UNITS:].astype(bf16)
    query_out[...] = query
    key_out[...] = key
    value_out[...] = value
    here = pl.ds(pl.multiple_of(step * size, size), size)
    keys[here, :] = key
    values[here, :] = value
    row = lax.broadcasted_iota(jnp.int32, (size, size), 0)
    column = lax.broadcasted_iota(jnp.int32, (size, size), 1)
    near = jnp.where(column <= row, contract_last(query, key) * scale, -1e30)

    def over(past):
        top = jnp.max(near, axis=1, keepdims=True)
        if past:
            far = contract_last(query, keys[:past, :]) * scale
            top = jnp.maximum(top, jnp.max(far, axis=1, keepdims=True))
        exps = jnp.exp(near - top)
        total = jnp.sum(exps, axis=1, keepdims=True)
        mixed = matrix_product(exps.astype(bf16), value)
        if past:
            exps = jnp.exp(far - top)
            total = total + jnp.sum(exps, axis=1, keepdims=True)
            mixed = mixed + matrix_product(exps.astype(bf16), values[:past, :])
        mixed = mixed / total
        sum_out[...] = mixed
        head_out[...] = mixed.astype(bf16)
        wide = jnp.broadcast_to(top + jnp.log(total), (size, 128))
        log_out[0] = wide.T[:1, :]

    for at in range(keys.shape[0] // size):
        pl.when(step == at)(functools.partial(over, at * size))


def attend(rows, g_attn, w_front, g_lat, expand_head, cosines, sines):
    seq_len, width = rows.shape
    size = 256
    steps = seq_len // size
    units = PLAIN_UNITS + ROTARY_UNITS
    bf16 = jnp.bfloat16

    def by_step(columns):
        return pl.BlockSpec((size, columns), lambda i: (i, 0))

    def fixed(x):
        return pl.BlockSpec(
            x.shape, lambda i: (0, 0), pipeline_mode=pl.Buffered(buffer_count=1)
        )

    return pl.pallas_call(
        attend_kernel,
        grid=(steps,),
        out_shape=[
            jax.ShapeDtypeStruct((seq_len, width), bf16),
            jax.ShapeDtypeStruct((seq_len, LATENT_WIDTH), bf16),
            jax.ShapeDtypeStruct((seq_len, units), bf16),
            jax.ShapeDtypeStruct((seq_len, units), bf16),
            jax.ShapeDtypeStruct((seq_len, VALUE_UNITS), bf16),
            jax.ShapeDtypeStruct((seq_len, VALUE_UNITS), bf16),
            jax.ShapeDtypeStruct((seq_len, VALUE_UNITS), jnp.float32),
            jax.ShapeDtypeStruct((steps, 1, size), jnp.float32),
        ],
        in_specs=[by_step(width)]
        + [fixed(x) for x in (g_attn, w_front, g_lat, expand_head)]
        + [by_step(ROTARY_UNITS)] * 2,
        out_specs=[
            by_step(width),
            by_step(LATENT_WIDTH),
            by_step(units),
            by_step(units),
            by_step(VALUE_UNITS),
            by_step(VALUE_UNITS),
            by_step(VALUE_UNITS),
            pl.BlockSpec((1, 1, size), lambda i: (i, 0, 0)),
        ],
        scratch_shapes=[
            pltpu.VMEM((seq_len, units), bf16),
            pltpu.VMEM((seq_len, VALUE_UNITS), bf16),
        ],
        compiler_params=pltpu.CompilerParams(vmem_limit_bytes=VMEM_LIMIT),
        cost_estimate=pl.CostEstimate(
            flops=2 * seq_len * (width * 768 + seq_len * units),
            bytes_accessed=3 * rows.size * 2,
            transcendentals=seq_len * seq_len // 2,
        ),
    )(rows, g_attn, w_front, g_lat, expand_head, cosines, sines)


def attend_back_kernel(
    query,
    key,
    value,
    d_head,
    head_sum,
    logs,
    expand_head,
    cosines,
    sines,
    d_query_out,
    d_pairs_out,
    d_keys_out,
    d_key,
    d_value,
    key_turned,
):
    bf16 = jnp.bfloat16
    size = query.shape[0]
    seq_len = key.shape[0]
    scale = (PLAIN_UNITS + ROTARY_UNITS) ** (-0.5)
    step = pl.program_id(0)

    @pl.when(step == 0)
    def _():
        d_key[...] = jnp.zeros_like(d_key)
        d_value[...] = jnp.zeros_like(d_value)
        for at in range(0, seq_len, size):
            part = key[at : at + size, :].astype(jnp.float32)
            key_turned[:, at : at + size] = part.T.astype(bf16)

    q, d_out = query[...], d_head[...]
    product = d_out.astype(jnp.float32) * head_sum[...]
    delta = jnp.sum(product.T, axis=0, keepdims=True)
    log_row = logs[0]
    row = lax.broadcasted_iota(jnp.int32, (size, size), 0)
    column = lax.broadcasted_iota(jnp.int32, (size, size), 1)

    def grads_of(at, mask):
        there = slice(at, at + size)
        scores = contract_last(key[there, :], q) * scale
        if mask:
            scores = jnp.where(row <= column, scores, -1e30)
        probs = jnp.exp(scores - log_row)
        d_probs = contract_last(value[there, :], d_out)
        d_scores = (probs * (d_probs - delta) * scale).astype(bf16)
        d_key[there, :] += matrix_product(d_scores, q)
        d_value[there, :] += matrix_product(probs.astype(bf16), d_out)
        return matrix_product(key_turned[:, there], d_scores)

    def over(past):
        total = grads_of(past, True)
        for at in range(0, past, size):
            total = total + grads_of(at, False)
        d_query = total.T
        d_rope = d_query[:, PLAIN_UNITS:]
        d_rope = d_rope * cosines[...] - swap_halves(d_rope) * sines[...]
        d_query_out[...] = jnp.concatenate([d_query[:, :PLAIN_UNITS], d_rope], axis=1).astype(bf16)

    for at in range(seq_len // size):
        pl.when(step == at)(functools.partial(over, at * size))

    @pl.when(step == seq_len // size - 1)
    def _():
        for at in range(0, seq_len, size):
            there = slice(at, at + size)
            d_pairs = jnp.concatenate(
                [d_key[there, :PLAIN_UNITS], d_value[there, :]], axis=1
            ).astype(bf16)
            d_pairs_out[there, :] = d_pairs
            d_keys_out[there, :LATENT_WIDTH] = contract_last(d_pairs, expand_head[...]).astype(bf16)
            tail = jnp.concatenate(
                [d_key[there, PLAIN_UNITS:], jnp.zeros((size, ROTARY_UNITS), jnp.float32)], axis=1
            )
            d_keys_out[there, LATENT_WIDTH:] = tail.astype(bf16)


def attend_back(query, key, value, d_head, head_sum, logs, expand_head, cosines, sines):
    seq_len, units = query.shape
    steps, _, size = logs.shape
    bf16 = jnp.bfloat16
    keys_width = LATENT_WIDTH + 2 * ROTARY_UNITS

    def by_step(columns):
        return pl.BlockSpec((size, columns), lambda i: (i, 0))

    def fixed(shape):
        return pl.BlockSpec(shape, lambda i: (0, 0), pipeline_mode=pl.Buffered(buffer_count=1))

    return pl.pallas_call(
        attend_back_kernel,
        grid=(steps,),
        out_shape=[
            jax.ShapeDtypeStruct((seq_len, units), bf16),
            jax.ShapeDtypeStruct((seq_len, PLAIN_UNITS + VALUE_UNITS), bf16),
            jax.ShapeDtypeStruct((seq_len, keys_width), bf16),
        ],
        in_specs=[
            by_step(units),
            fixed(key.shape),
            fixed(value.shape),
            by_step(VALUE_UNITS),
            by_step(VALUE_UNITS),
            pl.BlockSpec((1, 1, size), lambda i: (i, 0, 0)),
            fixed(expand_head.shape),
            by_step(ROTARY_UNITS),
            by_step(ROTARY_UNITS),
        ],
        out_specs=[
            by_step(units),
            fixed((seq_len, PLAIN_UNITS + VALUE_UNITS)),
            fixed((seq_len, keys_width)),
        ],
        scratch_shapes=[
            pltpu.VMEM((seq_len, units), jnp.float32),
            pltpu.VMEM((seq_len, VALUE_UNITS), jnp.float32),
            pltpu.VMEM((units, seq_len), bf16),
        ],
        compiler_params=pltpu.CompilerParams(vmem_limit_bytes=VMEM_LIMIT),
        cost_estimate=pl.CostEstimate(
            flops=5 * seq_len * seq_len * units,
            bytes_accessed=8 * seq_len * units * 2,
            transcendentals=seq_len * seq_len // 2,
        ),
    )(query, key, value, d_head, head_sum, logs, expand_head, cosines, sines)


def finish_kernel(query, expand, out_rows, query_out, expand_out, out_out):
    heads, units, width = query.shape
    query_out[...] = query[...].reshape(heads * units, width).astype(jnp.float32).T
    for at in range(heads):
        columns = expand.shape[2]
        expand_out[:, at * columns : (at + 1) * columns] = expand[at].astype(jnp.float32)
    out_out[...] = out_rows[...].reshape(out_out.shape).astype(jnp.float32)


def finish(query, expand, out_rows):
    heads, units, width = query.shape
    _, latents, columns = expand.shape
    _, rows, model = out_rows.shape
    return pl.pallas_call(
        finish_kernel,
        grid=(heads // 2,),
        out_shape=[
            jax.ShapeDtypeStruct((width, heads * units), jnp.float32),
            jax.ShapeDtypeStruct((latents, heads * columns), jnp.float32),
            jax.ShapeDtypeStruct((heads * rows, model), jnp.float32),
        ],
        in_specs=[
            pl.BlockSpec((2, units, width), lambda i: (i, 0, 0)),
            pl.BlockSpec((2, latents, columns), lambda i: (i, 0, 0)),
            pl.BlockSpec((2, rows, model), lambda i: (i, 0, 0)),
        ],
        out_specs=[
            pl.BlockSpec((width, 2 * units), lambda i: (0, i)),
            pl.BlockSpec((latents, 2 * columns), lambda i: (0, i)),
            pl.BlockSpec((2 * rows, model), lambda i: (i, 0)),
        ],
        compiler_params=pltpu.CompilerParams(vmem_limit_bytes=VMEM_LIMIT),
        cost_estimate=pl.CostEstimate(
            flops=0, bytes_accessed=6 * heads * units * width, transcendentals=0
        ),
    )(query, expand, out_rows)


def token_gather(rows):
    return lax.all_gather(rows, ("fsdp", "expert"), axis=0, tiled=True)


def split_body(
    tokens,
    routes,
    cotangent,
    attn_gain,
    w_query,
    latent_weight,
    latent_norm_gain,
    expand_weight,
    w_out,
    ffn_gain,
    w_router,
    shared_gate,
    shared_up,
    shared_down,
    expert_gate,
    expert_up,
    expert_down,
):
    rows = tokens.shape[1]
    experts = lax.axis_size("expert")
    shards = lax.axis_size("fsdp")
    position = lax.axis_index("expert")
    blocks = experts * shards
    seq_len = rows * experts
    capacity = shards * ((rows * TOPK * 4 + experts * 3 * shards - 1) // (experts * 3 * shards))
    head_units = PLAIN_UNITS + ROTARY_UNITS
    pair_units = PLAIN_UNITS + VALUE_UNITS
    feature_width = LATENT_WIDTH + ROTARY_UNITS
    scale = head_units ** (-0.5)

    shard = lax.axis_index("fsdp")
    first = shard == 0

    query_cols = lax.dynamic_slice_in_dim(w_query, position * head_units, head_units, 1)
    expand_cols = lax.dynamic_slice_in_dim(expand_weight, position * pair_units, pair_units, 1)
    owners = experts // shards
    lat_row = jnp.pad(latent_norm_gain, (0, w_query.shape[0] - latent_norm_gain.shape[0]))
    packed = jnp.concatenate(
        [query_cols.T, w_router.T, attn_gain[None], ffn_gain[None], lat_row[None]],
        axis=0,
    )
    packed = jnp.pad(packed, ((0, -packed.shape[0] % 32), (0, 0)))
    seq_rows, other_packed, other_expand, other_latent = gather_rows(
        [tokens[0]], False, 0, swapped=[packed, expand_cols], halved=[latent_weight.T]
    )

    def whole(own, other, axis):
        return jnp.concatenate(
            [jnp.where(first, own, other), jnp.where(first, other, own)], axis=axis
        )

    lat_half = latent_norm_gain.shape[0]
    at = head_units
    packed_rows = whole(packed, other_packed, 1)
    expand_head = whole(expand_cols, other_expand, 0)
    w_latent = whole(latent_weight.T, other_latent, 1)
    w_front = jnp.concatenate([w_latent, packed_rows[:at]], axis=0)
    router_rows = packed_rows[at:]
    wrout = packed_rows[at : at + experts]
    g_attn = packed_rows[at + experts].astype(jnp.float32)
    g_ffn = packed_rows[at + experts + 1].astype(jnp.float32)
    lat_row = packed_rows[at + experts + 2]
    g_lat = jnp.concatenate(
        [lat_row[:lat_half], lat_row[w_query.shape[0] : w_query.shape[0] + lat_half]]
    ).astype(jnp.float32)
    units = shared_down.shape[0]

    core = lax.rem(position, CORES)

    def by_cores(weight):
        size = weight.shape[0] // CORES
        own = lax.dynamic_slice_in_dim(weight, core * size, size, 0)
        own = lax.all_gather(own, "fsdp", axis=0, tiled=True)
        swap = [(index, index ^ 1) for index in range(experts)]
        return own, lax.ppermute(own, "expert", swap)

    def core_columns(value, which):
        size = value.shape[1] // (CORES * shards)
        parts = [
            lax.dynamic_slice_in_dim(value, (at * CORES + which) * size, size, 1)
            for at in range(shards)
        ]
        return jnp.concatenate(parts, axis=1)

    def in_order(own, other):
        lower, upper = jnp.where(core == 0, own, other), jnp.where(core == 0, other, own)
        size = own.shape[1] // shards
        parts = []
        for at in range(shards):
            parts += [lower[:, at * size : (at + 1) * size], upper[:, at * size : (at + 1) * size]]
        return jnp.concatenate(parts, axis=1)

    out_own, out_other = by_cores(w_out)
    grad_rows = cotangent[0]
    grad_out = grad_rows.astype(jnp.float32)
    own_routes = jnp.pad(routes[0], ((0, 0), (0, 128 - TOPK)), constant_values=-1)
    grad_rows = jnp.concatenate([grad_rows, own_routes.astype(jnp.bfloat16)], axis=1)
    seq_rows, grad_rows, shared_gate, shared_up = lax.optimization_barrier(
        (seq_rows, grad_rows, shared_gate, shared_up)
    )
    def to_columns(weight):
        parts = weight.reshape(weight.shape[0], blocks, units).transpose(1, 0, 2)
        return lax.all_to_all(
            parts, ("expert", "fsdp"), split_axis=0, concat_axis=0, tiled=True
        ).reshape(-1, units)

    sh_cols = to_columns(jnp.concatenate([shared_gate, shared_up], axis=0)).reshape(
        blocks, 2, shared_gate.shape[0], units
    )
    lanes = -(-units // 128) * 128
    sh_cols = jnp.pad(sh_cols, ((0, 0), (0, 0), (0, 0), (0, lanes - units)))
    shared_in = sh_cols.transpose(0, 2, 1, 3).reshape(MODEL_WIDTH, 2 * lanes)
    shared_out = jnp.pad(shared_down, ((0, lanes - units), (0, 0)))
    all_grads = token_gather(grad_rows)

    x_in = tokens[0].astype(jnp.float32)
    normed, inv_attn = norm_forward(x_in, g_attn)
    normed_in = normed.astype(jnp.bfloat16)
    half_units = ROTARY_UNITS // 2
    freqs = 10000.0 ** (-np.arange(half_units) * (2.0 / ROTARY_UNITS))
    angles = np.arange(seq_len)[:, None] * freqs[None, :]
    cosine_table = jnp.asarray(np.cos(angles), jnp.float32)
    sine_table = jnp.asarray(np.sin(angles), jnp.float32)
    cosines = jnp.asarray(np.concatenate([np.cos(angles)] * 2, axis=1), jnp.float32)
    sines = jnp.asarray(np.concatenate([-np.sin(angles), np.sin(angles)], axis=1), jnp.float32)
    (
        seq_normed,
        latent_rows,
        query,
        key,
        value,
        head_rows,
        head_sum,
        logs,
    ) = attend(
        seq_rows.reshape(seq_len, MODEL_WIDTH),
        g_attn[None],
        w_front,
        g_lat[None],
        expand_head,
        cosines,
        sines,
    )
    head_rows, shared_in = lax.optimization_barrier((head_rows, shared_in))
    heads = exchange(head_rows.reshape(experts, rows, VALUE_UNITS), 1)
    heads = heads.transpose(1, 0, 2).reshape(rows, experts * VALUE_UNITS)
    hidden = x_in + matrix_product(core_columns(heads, core), out_own)
    hidden = hidden + matrix_product(core_columns(heads, 1 - core), out_other)
    normed2, inv_ffn = norm_forward(hidden, g_ffn)
    normed_ffn = normed2.astype(jnp.bfloat16)
    router = jax.nn.softmax(outer_product(normed_ffn, wrout), axis=-1)

    (all_normed,) = gather_rows([normed_ffn], True, 2)
    w_query, all_normed = lax.optimization_barrier((w_query, all_normed))
    query_own, query_other = by_cores(w_query)
    (
        out_part,
        d_part,
        ex_rows,
        ex_grads,
        scaled_act,
        d_pre_gate,
        d_pre_up,
        g_shared_in,
        g_shared_out,
    ) = expert_phase(
        all_normed,
        all_grads.reshape(blocks, rows, -1),
        router_rows,
        expert_gate[0].T,
        expert_up[0].T,
        expert_down[0],
        shared_in,
        shared_out,
        capacity,
    )
    g_down = inner(scaled_act, ex_grads)
    g_gate = inner(d_pre_gate, ex_rows).T
    g_up = inner(d_pre_up, ex_rows).T
    (d_back,) = scatter_rows(d_part, True, 3)
    out_part, d_back = lax.optimization_barrier((out_part, d_back))
    out_sum = lax.psum_scatter(
        out_part.reshape(blocks * rows, MODEL_WIDTH),
        ("fsdp", "expert"),
        scatter_dimension=0,
        tiled=True,
    )
    d_normed_ffn = d_back[:, :MODEL_WIDTH]
    d_router = d_back[:, MODEL_WIDTH : MODEL_WIDTH + experts]

    d_logits = (router * (d_router - jnp.sum(router * d_router, axis=1, keepdims=True))).astype(
        jnp.bfloat16
    )
    g_router = inner(d_logits, normed_ffn)
    d_normed_ffn = d_normed_ffn + matrix_product(d_logits, wrout)
    d_hidden_norm, g_ffn_grad = norm_backward(hidden, inv_ffn, g_ffn, d_normed_ffn)
    d_hidden = grad_out + d_hidden_norm
    d_attn = d_hidden.astype(jnp.bfloat16)

    d_heads = in_order(outer_product(d_attn, out_own), outer_product(d_attn, out_other))
    d_heads = d_heads.astype(jnp.bfloat16)
    d_heads = d_heads.reshape(rows, experts, VALUE_UNITS).transpose(1, 0, 2)
    d_head = exchange(d_heads, 4).reshape(seq_len, VALUE_UNITS)
    out_grad_part = inner(heads, d_attn).astype(jnp.bfloat16)
    d_query_full, d_pairs, d_keys = attend_back(
        query, key, value, d_head, head_sum, logs, expand_head, cosines, sines
    )
    g_expand_head = inner(latent_rows, d_pairs)
    g_query_head = inner(d_query_full, seq_normed).astype(jnp.bfloat16)
    g_expand_head = g_expand_head.astype(jnp.bfloat16)

    def half_of(whole, which, axis):
        size = whole.shape[axis] // shards
        return lax.dynamic_slice_in_dim(whole, which * size, size, axis)

    own_d_query, d_sums, own_out, other_query, other_expand = exchange_and_sums(
        d_query_full.reshape(experts, rows, head_units),
        d_keys.reshape(experts, rows, -1),
        out_grad_part.reshape(blocks, -1, MODEL_WIDTH),
        [half_of(g_query_head, 1 - shard, 1), half_of(g_expand_head, 1 - shard, 0)],
        5,
    )
    own_d_query = own_d_query.transpose(1, 0, 2).reshape(rows, experts * head_units)
    key_gradient = d_sums[:, :feature_width]
    d_normed_in = in_order(
        outer_product(own_d_query, query_own), outer_product(own_d_query, query_other)
    )

    def summed(own, other):
        return (own.astype(jnp.float32) + other.astype(jnp.float32)).astype(jnp.bfloat16)

    own_query = summed(half_of(g_query_head, shard, 1), other_query)
    own_expand = summed(half_of(g_expand_head, shard, 0), other_expand)
    own_out = own_out.astype(jnp.bfloat16)
    own_latent = outer_product(normed_in, w_latent[:LATENT_WIDTH])
    own_cosine = lax.dynamic_slice_in_dim(cosine_table, position * rows, rows, 0)
    own_sine = lax.dynamic_slice_in_dim(sine_table, position * rows, rows, 0)
    inv_lat = lax.rsqrt(jnp.mean(own_latent * own_latent, axis=-1, keepdims=True) + EPS)
    d_compact, g_lat_grad = norm_backward(
        own_latent, inv_lat, g_lat, key_gradient[:, :LATENT_WIDTH]
    )
    d_rope = reverse_rotary(key_gradient[:, LATENT_WIDTH:], own_cosine, own_sine)
    d_latent_full = jnp.concatenate([d_compact, d_rope], axis=-1).astype(jnp.bfloat16)
    g_latent = inner(d_latent_full, normed_in)
    d_normed_in = d_normed_in + matrix_product(d_latent_full, w_latent)
    d_norm_in, g_attn_grad = norm_backward(x_in, inv_attn, g_attn, d_normed_in)
    d_tokens = (d_hidden + d_norm_in).astype(jnp.bfloat16)

    half = MODEL_WIDTH // blocks
    cols = lax.all_to_all(
        g_shared_in.reshape(blocks, half, 2 * lanes),
        ("expert", "fsdp"),
        split_axis=0,
        concat_axis=0,
        tiled=True,
    )
    cols = cols.transpose(1, 0, 2).astype(jnp.float32)
    r_sgate = cols[:, :, :units].reshape(half, blocks * units)
    r_sup = cols[:, :, lanes : lanes + units].reshape(half, blocks * units)
    g_sdown = g_shared_out[:units]
    model_half = MODEL_WIDTH // shards
    small_rows = jnp.concatenate([g_latent, g_router, g_attn_grad[None], g_ffn_grad[None]], axis=0)
    used = small_rows.shape[0]
    share = 2 * 32 * (-(-(used + 1) // (2 * 32 * experts)))

    def rows_for(which):
        here = small_rows[:, which * model_half : (which + 1) * model_half]
        lat = jnp.pad(
            g_lat_grad[which * lat_half : (which + 1) * lat_half], (0, model_half - lat_half)
        )
        full = jnp.concatenate([here, lat[None]], axis=0).astype(jnp.bfloat16)
        full = jnp.pad(full, ((0, experts * share - used - 1), (0, 0)))
        return full.reshape(experts, share, model_half)

    small_part = jnp.concatenate([rows_for(which) for which in range(shards)], axis=0)
    r_query, r_expand, r_out, small_sum = gather_and_scatter(
        [own_query, own_expand, own_out], small_part, 6
    )
    hidden, small_sum = lax.optimization_barrier((hidden, small_sum))
    output = hidden + out_sum.astype(jnp.float32)
    (small_all,) = gather_rows([small_sum.astype(jnp.bfloat16)], False, 7)
    r_query, r_expand, r_out = finish(r_query, r_expand, r_out)
    small_all = small_all.reshape(experts * share, model_half).astype(jnp.float32)
    return (
        output.astype(jnp.bfloat16)[None],
        d_tokens[None],
        small_all[feature_width + experts],
        r_query,
        small_all[:feature_width].T,
        small_all[feature_width + experts + 2, :lat_half],
        r_expand,
        r_out,
        small_all[feature_width + experts + 1],
        small_all[feature_width : feature_width + experts].T,
        r_sgate,
        r_sup,
        g_sdown,
        g_gate[None],
        g_up[None],
        g_down[None],
    )


def solution(mesh):
    shape = (mesh.shape["expert"], mesh.shape["fsdp"])
    split = shape == (LINE * SQUARE * CORES, SQUARE) and shape[0] == HEAD_COUNT
    return jax.shard_map(
        split_body if split else body,
        mesh=mesh,
        in_specs=(
            P("fsdp", "expert", None),
            P("fsdp", "expert", None),
            P("fsdp", "expert", None),
            P("fsdp"),
            P("fsdp", None),
            P("fsdp", None),
            P("fsdp"),
            P("fsdp", None),
            P("fsdp", None),
            P("fsdp"),
            P("fsdp", None),
            P(("expert", "fsdp"), None),
            P(("expert", "fsdp"), None),
            P(("expert", "fsdp"), None),
            P("expert", None, "fsdp"),
            P("expert", None, "fsdp"),
            P("expert", "fsdp", None),
        ),
        out_specs=(
            P("fsdp", "expert", None),
            P("fsdp", "expert", None),
            P("fsdp"),
            P("fsdp", None),
            P("fsdp", None),
            P("fsdp"),
            P("fsdp", None),
            P("fsdp", None),
            P("fsdp"),
            P("fsdp", None),
            P(("expert", "fsdp"), None),
            P(("expert", "fsdp"), None),
            P(("expert", "fsdp"), None),
            P("expert", None, "fsdp"),
            P("expert", None, "fsdp"),
            P("expert", "fsdp", None),
        ),
        check_vma=False,
    )
```

```python
import functools

import jax
import jax.numpy as jnp
import numpy as np
from jax import lax
from jax.experimental import pallas as pl
from jax.experimental.pallas import tpu as pltpu
from jax.sharding import PartitionSpec as P

MODEL_WIDTH = 2048
HEAD_COUNT = 16
PLAIN_UNITS = 128
ROTARY_UNITS = 64
VALUE_UNITS = 128
LATENT_WIDTH = 512
TOPK = 6


EPS = 1e-06


def matrix_product(left, right):
    return jnp.dot(left, right, preferred_element_type=jnp.float32)


def inner(left, right):
    return lax.dot_general(
        left, right, (((0,), (0,)), ((), ())), preferred_element_type=jnp.float32
    )


def outer_product(left, right):
    return lax.dot_general(
        left, right, (((1,), (1,)), ((), ())), preferred_element_type=jnp.float32
    )


def norm_forward(value, gain):
    inverse = lax.rsqrt(jnp.mean(value * value, axis=-1, keepdims=True) + EPS)
    return (value * inverse * gain, inverse)


def norm_backward(value, inverse, gain, grad):
    unit = value * inverse
    scaled = grad * gain
    d_value = inverse * (scaled - unit * jnp.mean(scaled * unit, axis=-1, keepdims=True))
    return (d_value, jnp.sum(grad * unit, axis=0))


def rope_tables(positions):
    half = ROTARY_UNITS // 2
    freqs = 10000.0 ** (-jnp.arange(half, dtype=jnp.float32) * (2.0 / ROTARY_UNITS))
    angles = positions.astype(jnp.float32)[:, None] * freqs[None, :]
    return (jnp.cos(angles), jnp.sin(angles))


def apply_rotary(value, cosine_table, sine_table):
    half = ROTARY_UNITS // 2
    first = value[..., :half]
    second = value[..., half:]
    return jnp.concatenate(
        [first * cosine_table - second * sine_table, first * sine_table + second * cosine_table],
        axis=-1,
    )


def reverse_rotary(grad, cosine_table, sine_table):
    half = ROTARY_UNITS // 2
    first = grad[..., :half]
    second = grad[..., half:]
    return jnp.concatenate(
        [first * cosine_table + second * sine_table, second * cosine_table - first * sine_table],
        axis=-1,
    )


def silu_parts(value):
    sigma = jax.nn.sigmoid(value)
    return (value * sigma, sigma * (1.0 + value * (1.0 - sigma)))


def body(
    tokens,
    routes,
    cotangent,
    attn_gain,
    w_query,
    latent_weight,
    latent_norm_gain,
    expand_weight,
    w_out,
    ffn_gain,
    w_router,
    shared_gate,
    shared_up,
    shared_down,
    expert_gate,
    expert_up,
    expert_down,
):
    device_local = tokens.shape[1]
    experts = lax.axis_size("expert")
    shards = lax.axis_size("fsdp")
    position = lax.axis_index("expert")
    capacity = shards * (
        (device_local * TOPK * 4 + experts * 3 * shards - 1) // (experts * 3 * shards)
    )
    seq_len = device_local * experts
    feature_width = LATENT_WIDTH + ROTARY_UNITS
    scale = (PLAIN_UNITS + ROTARY_UNITS) ** (-0.5)
    attention_gain_grad, wq, wlat, g_lat, expand_matrix, wout, g_ffn, wrout = (
        lax.all_gather(attn_gain, "fsdp", axis=0, tiled=True),
        lax.all_gather(w_query, "fsdp", axis=0, tiled=True),
        lax.all_gather(latent_weight, "fsdp", axis=0, tiled=True),
        lax.all_gather(latent_norm_gain, "fsdp", axis=0, tiled=True),
        lax.all_gather(expand_weight, "fsdp", axis=0, tiled=True),
        lax.all_gather(w_out, "fsdp", axis=0, tiled=True),
        lax.all_gather(ffn_gain, "fsdp", axis=0, tiled=True),
        lax.all_gather(w_router, "fsdp", axis=0, tiled=True),
    )
    sgate, sup, sdown = (
        lax.all_gather(shared_gate, ("expert", "fsdp"), axis=0, tiled=True),
        lax.all_gather(shared_up, ("expert", "fsdp"), axis=0, tiled=True),
        lax.all_gather(shared_down, ("expert", "fsdp"), axis=0, tiled=True),
    )
    attention_gain_grad = attention_gain_grad.astype(jnp.float32)
    g_lat = g_lat.astype(jnp.float32)
    g_ffn = g_ffn.astype(jnp.float32)
    x_in = tokens[0].astype(jnp.float32)
    grad_out = cotangent[0].astype(jnp.float32)
    positions = position * device_local + jnp.arange(device_local, dtype=jnp.int32)
    cosine_table, sine_table = rope_tables(positions)
    normed, inv_attn = norm_forward(x_in, attention_gain_grad)
    normed_in = normed.astype(jnp.bfloat16)
    query_full = matrix_product(normed_in, wq).reshape(
        device_local, HEAD_COUNT, PLAIN_UNITS + ROTARY_UNITS
    )
    query_nope = query_full[:, :, :PLAIN_UNITS].astype(jnp.bfloat16)
    expanded_latent = expand_matrix.reshape(LATENT_WIDTH, HEAD_COUNT, PLAIN_UNITS + VALUE_UNITS)
    key_part = expanded_latent[:, :, :PLAIN_UNITS]
    value_part = expanded_latent[:, :, PLAIN_UNITS:]
    query_latent = jnp.einsum(
        "thd,chd->thc", query_nope, key_part, preferred_element_type=jnp.float32
    )
    query_rope = apply_rotary(
        query_full[:, :, PLAIN_UNITS:], cosine_table[:, None, :], sine_table[:, None, :]
    )
    token_rows = device_local * HEAD_COUNT
    query = (
        jnp.concatenate([query_latent, query_rope], axis=-1)
        .astype(jnp.bfloat16)
        .reshape(token_rows, feature_width)
    )
    latent_complete = matrix_product(normed_in, wlat)
    packed_rows = latent_complete[:, :LATENT_WIDTH]
    latent_state, inv_lat = norm_forward(packed_rows, g_lat)
    rotary_key = apply_rotary(latent_complete[:, LATENT_WIDTH:], cosine_table, sine_table)
    key = jnp.concatenate([latent_state, rotary_key], axis=-1).astype(jnp.bfloat16)
    keys_all = lax.all_gather(key, "expert", axis=0, tiled=True)
    block = min(512, seq_len)
    token_tally = (position * device_local + device_local + block - 1) // block
    q_pos = position * device_local + jnp.arange(token_rows, dtype=jnp.int32) // HEAD_COUNT

    def scores_of(index):
        key_rows = lax.dynamic_slice_in_dim(keys_all, index * block, block, 0)
        raw = outer_product(query, key_rows)
        k_pos = index * block + jnp.arange(block, dtype=jnp.int32)
        valid = k_pos[None, :] <= q_pos[:, None]
        return (jnp.where(valid, raw * scale, -1e30), key_rows)

    def stats_step(index, carry):
        top, total = carry
        scores, unused = scores_of(index)
        new_top = jnp.maximum(top, jnp.max(scores, axis=1))
        total = total * jnp.exp(top - new_top) + jnp.sum(jnp.exp(scores - new_top[:, None]), axis=1)
        return (new_top, total)

    top, total = lax.fori_loop(
        0,
        token_tally,
        stats_step,
        (jnp.full((token_rows,), -1e30, jnp.float32), jnp.zeros((token_rows,), jnp.float32)),
    )
    log_total = top + jnp.log(total)

    def mixing_update(index, running_total):
        scores, key_rows = scores_of(index)
        weight_arrays = jnp.exp(scores - log_total[:, None]).astype(jnp.bfloat16)
        return running_total + matrix_product(weight_arrays, key_rows[:, :LATENT_WIDTH])

    mixed_output_sum = lax.fori_loop(
        0, token_tally, mixing_update, jnp.zeros((token_rows, LATENT_WIDTH), jnp.float32)
    )
    mixed_output = mixed_output_sum.astype(jnp.bfloat16).reshape(
        device_local, HEAD_COUNT, LATENT_WIDTH
    )
    heads = jnp.einsum("thc,chv->thv", mixed_output, value_part, preferred_element_type=jnp.float32)
    heads = heads.reshape(device_local, HEAD_COUNT * VALUE_UNITS).astype(jnp.bfloat16)
    hidden = x_in + matrix_product(heads, wout)
    normed2, inv_ffn = norm_forward(hidden, g_ffn)
    normed_ffn = normed2.astype(jnp.bfloat16)
    logits = matrix_product(normed_ffn, wrout)
    router = jax.nn.softmax(logits, axis=-1)
    own_routes = routes[0]
    names = jnp.arange(experts, dtype=jnp.int32)
    chosen = (own_routes[:, :, None] == names[None, None, :]).astype(jnp.float32)
    gates = jnp.sum(chosen * router[:, None, :], axis=-1)
    hits = (own_routes.reshape(device_local * TOPK)[:, None] == names[None, :]).astype(jnp.int32)
    slot = jnp.sum((jnp.cumsum(hits, axis=0) - hits) * hits, axis=1)
    place = own_routes.reshape(device_local * TOPK) * capacity + slot
    token_of = jnp.arange(device_local * TOPK, dtype=jnp.int32) // TOPK
    table = jnp.full((experts * capacity,), device_local, jnp.int32).at[place].set(token_of)
    padded = jnp.concatenate([normed_ffn, jnp.zeros((1, MODEL_WIDTH), jnp.bfloat16)], axis=0)
    buffer = padded[table].reshape(experts, capacity, MODEL_WIDTH)
    w_g, w_u, w_d = (expert_gate[0], expert_up[0], expert_down[0])

    def spread(values):
        return jnp.broadcast_to(values[:, None], (experts, shards, capacity, MODEL_WIDTH)).reshape(
            experts * shards, capacity, MODEL_WIDTH
        )

    def collect(back):
        return jnp.sum(back.reshape(experts, shards, capacity, MODEL_WIDTH), axis=1).reshape(
            experts * capacity, MODEL_WIDTH
        )

    received = lax.all_to_all(
        spread(buffer), ("expert", "fsdp"), split_axis=0, concat_axis=0, tiled=True
    )
    ex_rows = received.reshape(-1, MODEL_WIDTH)
    pre_gate = matrix_product(ex_rows, w_g)
    pre_up = matrix_product(ex_rows, w_u)
    act_gate, slope = silu_parts(pre_gate)
    ex_act = (act_gate * pre_up).astype(jnp.bfloat16)
    ex_out = matrix_product(ex_act, w_d).reshape(received.shape)
    returned = lax.all_to_all(
        ex_out.astype(jnp.bfloat16), ("expert", "fsdp"), split_axis=0, concat_axis=0, tiled=True
    ).astype(ex_out.dtype)
    results = collect(returned)
    picked = results[place].reshape(device_local, TOPK, MODEL_WIDTH)
    routed = jnp.sum(gates[:, :, None] * picked, axis=1)
    sh_gate = matrix_product(normed_ffn, sgate)
    sh_up = matrix_product(normed_ffn, sup)
    sh_silu, sh_slope = silu_parts(sh_gate)
    sh_act = (sh_silu * sh_up).astype(jnp.bfloat16)
    shared = matrix_product(sh_act, sdown)
    output = hidden + routed + shared
    d_shared = grad_out.astype(jnp.bfloat16)
    shared_down_gradient = inner(sh_act, d_shared)
    d_sh_act = outer_product(d_shared, sdown)
    d_sh_gate = (d_sh_act * sh_up * sh_slope).astype(jnp.bfloat16)
    d_sh_up = (d_sh_act * sh_silu).astype(jnp.bfloat16)
    shared_gate_gradient = inner(normed_ffn, d_sh_gate)
    shared_up_gradient = inner(normed_ffn, d_sh_up)
    d_normed_ffn = outer_product(d_sh_gate, sgate) + outer_product(d_sh_up, sup)
    d_picked = (
        (gates[:, :, None] * grad_out[:, None, :])
        .astype(jnp.bfloat16)
        .reshape(device_local * TOPK, MODEL_WIDTH)
    )
    d_gates = jnp.sum(picked * grad_out[:, None, :], axis=2)
    d_buffer = (
        jnp.zeros((experts * capacity, MODEL_WIDTH), jnp.bfloat16)
        .at[place]
        .set(d_picked)
        .reshape(experts, capacity, MODEL_WIDTH)
    )
    d_received = lax.all_to_all(
        spread(d_buffer), ("expert", "fsdp"), split_axis=0, concat_axis=0, tiled=True
    )
    d_rows = d_received.reshape(-1, MODEL_WIDTH)
    d_act = outer_product(d_rows, w_d)
    g_down = inner(ex_act, d_rows)
    d_pre_gate = (d_act * pre_up * slope).astype(jnp.bfloat16)
    d_pre_up = (d_act * act_gate).astype(jnp.bfloat16)
    g_gate = inner(ex_rows, d_pre_gate)
    g_up = inner(ex_rows, d_pre_up)
    d_ex_rows = (outer_product(d_pre_gate, w_g) + outer_product(d_pre_up, w_u)).reshape(
        received.shape
    )
    d_returned = lax.all_to_all(
        d_ex_rows.astype(jnp.bfloat16), ("expert", "fsdp"), split_axis=0, concat_axis=0, tiled=True
    ).astype(d_ex_rows.dtype)
    d_results = collect(d_returned)
    d_normed_ffn = d_normed_ffn + jnp.sum(
        d_results[place].reshape(device_local, TOPK, MODEL_WIDTH), axis=1
    )
    d_router = jnp.sum(chosen * d_gates[:, :, None], axis=1)
    d_logits = (router * (d_router - jnp.sum(router * d_router, axis=1, keepdims=True))).astype(
        jnp.bfloat16
    )
    router_weight_gradient = inner(normed_ffn, d_logits)
    d_normed_ffn = d_normed_ffn + outer_product(d_logits, wrout)
    d_hidden_norm, g_ffn_grad = norm_backward(hidden, inv_ffn, g_ffn, d_normed_ffn)
    d_hidden = grad_out + d_hidden_norm
    d_attn = d_hidden.astype(jnp.bfloat16)
    output_weight_gradient = inner(heads, d_attn)
    d_heads = (
        outer_product(d_attn, wout)
        .astype(jnp.bfloat16)
        .reshape(device_local, HEAD_COUNT, VALUE_UNITS)
    )
    value_weight_gradient = jnp.einsum(
        "thc,thv->chv", mixed_output, d_heads, preferred_element_type=jnp.float32
    )
    mixed_gradient = jnp.einsum(
        "thv,chv->thc", d_heads, value_part, preferred_element_type=jnp.float32
    )
    mixed_gradient = mixed_gradient.astype(jnp.bfloat16).reshape(token_rows, LATENT_WIDTH)
    delta = jnp.sum(mixed_gradient.astype(jnp.float32) * mixed_output_sum, axis=1)

    def back_step(index, carry):
        d_query_acc, d_keys_acc = carry
        scores, key_rows = scores_of(index)
        weight_arrays = jnp.exp(scores - log_total[:, None])
        weight_gradients = outer_product(mixed_gradient, key_rows[:, :LATENT_WIDTH])
        d_scores = (weight_arrays * (weight_gradients - delta[:, None]) * scale).astype(
            jnp.bfloat16
        )
        d_query_acc = d_query_acc + matrix_product(d_scores, key_rows)
        d_values = inner(weight_arrays.astype(jnp.bfloat16), mixed_gradient)
        d_block = inner(d_scores, query) + jnp.concatenate(
            [d_values, jnp.zeros((block, ROTARY_UNITS), jnp.float32)], axis=1
        )
        previous = lax.dynamic_slice_in_dim(d_keys_acc, index * block, block, 0)
        return (
            d_query_acc,
            lax.dynamic_update_slice_in_dim(d_keys_acc, previous + d_block, index * block, 0),
        )

    d_query, d_keys = lax.fori_loop(
        0,
        token_tally,
        back_step,
        (
            jnp.zeros((token_rows, feature_width), jnp.float32),
            jnp.zeros((seq_len, feature_width), jnp.float32),
        ),
    )
    key_gradient = lax.psum_scatter(
        d_keys.astype(jnp.bfloat16), "expert", scatter_dimension=0, tiled=True
    )
    query_up_gradient = d_query.astype(jnp.bfloat16).reshape(
        device_local, HEAD_COUNT, feature_width
    )
    query_latent_gradient = query_up_gradient[:, :, :LATENT_WIDTH]
    key_weight_gradient = jnp.einsum(
        "thc,thd->chd", query_latent_gradient, query_nope, preferred_element_type=jnp.float32
    )
    d_q_nope = jnp.einsum(
        "thc,chd->thd", query_latent_gradient, key_part, preferred_element_type=jnp.float32
    )
    d_q_rope = reverse_rotary(
        query_up_gradient[:, :, LATENT_WIDTH:].astype(jnp.float32),
        cosine_table[:, None, :],
        sine_table[:, None, :],
    )
    d_query_full = (
        jnp.concatenate([d_q_nope, d_q_rope], axis=-1)
        .astype(jnp.bfloat16)
        .reshape(device_local, HEAD_COUNT * (PLAIN_UNITS + ROTARY_UNITS))
    )
    query_weight_gradient = inner(normed_in, d_query_full)
    d_normed_in = outer_product(d_query_full, wq)
    latent_gradient = key_gradient[:, :LATENT_WIDTH].astype(jnp.float32)
    rotary_key_gradient = reverse_rotary(
        key_gradient[:, LATENT_WIDTH:].astype(jnp.float32), cosine_table, sine_table
    )
    d_compact, g_lat_grad = norm_backward(packed_rows, inv_lat, g_lat, latent_gradient)
    d_latent_full = jnp.concatenate([d_compact, rotary_key_gradient], axis=-1).astype(jnp.bfloat16)
    latent_weight_gradient = inner(normed_in, d_latent_full)
    d_normed_in = d_normed_in + outer_product(d_latent_full, wlat)
    d_norm_in, g_attn_grad = norm_backward(x_in, inv_attn, attention_gain_grad, d_normed_in)
    d_tokens = (d_hidden + d_norm_in).astype(jnp.bfloat16)
    expand_weight_gradient = jnp.concatenate(
        [key_weight_gradient, value_weight_gradient], axis=-1
    ).reshape(LATENT_WIDTH, HEAD_COUNT * (PLAIN_UNITS + VALUE_UNITS))
    r_sgate, r_sup, r_sdown = (
        lax.psum_scatter(shared_gate_gradient, ("expert", "fsdp"), scatter_dimension=0, tiled=True),
        lax.psum_scatter(shared_up_gradient, ("expert", "fsdp"), scatter_dimension=0, tiled=True),
        lax.psum_scatter(shared_down_gradient, ("expert", "fsdp"), scatter_dimension=0, tiled=True),
    )
    r_attn, r_query, r_latent, r_lgain, r_expand, r_out, r_fgain, r_router = (
        lax.psum_scatter(
            g_attn_grad.astype(jnp.bfloat16), "fsdp", scatter_dimension=0, tiled=True
        ).astype(jnp.float32),
        lax.psum_scatter(
            query_weight_gradient.astype(jnp.bfloat16), "fsdp", scatter_dimension=0, tiled=True
        ).astype(jnp.float32),
        lax.psum_scatter(
            latent_weight_gradient.astype(jnp.bfloat16), "fsdp", scatter_dimension=0, tiled=True
        ).astype(jnp.float32),
        lax.psum_scatter(
            g_lat_grad.astype(jnp.bfloat16), "fsdp", scatter_dimension=0, tiled=True
        ).astype(jnp.float32),
        lax.psum_scatter(
            expand_weight_gradient.astype(jnp.bfloat16), "fsdp", scatter_dimension=0, tiled=True
        ).astype(jnp.float32),
        lax.psum_scatter(
            output_weight_gradient.astype(jnp.bfloat16), "fsdp", scatter_dimension=0, tiled=True
        ).astype(jnp.float32),
        lax.psum_scatter(
            g_ffn_grad.astype(jnp.bfloat16), "fsdp", scatter_dimension=0, tiled=True
        ).astype(jnp.float32),
        lax.psum_scatter(
            router_weight_gradient.astype(jnp.bfloat16), "fsdp", scatter_dimension=0, tiled=True
        ).astype(jnp.float32),
    )
    r_attn, r_query, r_latent, r_lgain, r_expand, r_out, r_fgain, r_router = (
        lax.psum(r_attn.astype(jnp.bfloat16), "expert").astype(jnp.float32),
        lax.psum(r_query.astype(jnp.bfloat16), "expert").astype(jnp.float32),
        lax.psum(r_latent.astype(jnp.bfloat16), "expert").astype(jnp.float32),
        lax.psum(r_lgain.astype(jnp.bfloat16), "expert").astype(jnp.float32),
        lax.psum(r_expand.astype(jnp.bfloat16), "expert").astype(jnp.float32),
        lax.psum(r_out.astype(jnp.bfloat16), "expert").astype(jnp.float32),
        lax.psum(r_fgain.astype(jnp.bfloat16), "expert").astype(jnp.float32),
        lax.psum(r_router.astype(jnp.bfloat16), "expert").astype(jnp.float32),
    )
    return (
        output.astype(jnp.bfloat16)[None],
        d_tokens[None],
        r_attn,
        r_query,
        r_latent,
        r_lgain,
        r_expand,
        r_out,
        r_fgain,
        r_router,
        r_sgate,
        r_sup,
        r_sdown,
        g_gate[None],
        g_up[None],
        g_down[None],
    )


LINE = 4
SQUARE = 2
CORES = 2
MESH = pl.DeviceIdType.MESH
VMEM_LIMIT = 56 * 1024 * 1024


class Place:
    def __init__(self):
        index = lax.axis_index("expert")
        self.y = lax.axis_index("fsdp")
        self.c = lax.rem(index, CORES)
        self.b = lax.rem(lax.div(index, CORES), SQUARE)
        self.a = lax.div(index, CORES * SQUARE)

    def device(self, da=0, db=0, dc=0, dy=0):
        b = 1 - self.b if db else self.b
        c = 1 - self.c if dc else self.c
        y = 1 - self.y if dy else self.y
        return (((self.a + da) * SQUARE + b) * CORES + c, y)

    def block(self, full, a, db=0, dc=0, dy=0):
        b = 1 - self.b if db else self.b
        c = 1 - self.c if dc else self.c
        y = 1 - self.y if dy else self.y
        flat = (a * SQUARE + b) * CORES + c
        return y * (LINE * SQUARE * CORES) + flat if full else flat

    def greet(self, with_y):
        barrier = pltpu.get_barrier_semaphore()
        near = [dict(db=1), dict(dc=1)] + ([dict(dy=1)] if with_y else [])
        for step in near:
            pl.semaphore_signal(barrier, inc=1, device_id=self.device(**step), device_id_type=MESH)

        @pl.when(self.a > 0)
        def _():
            pl.semaphore_signal(barrier, inc=1, device_id=self.device(da=-1), device_id_type=MESH)

        @pl.when(self.a < LINE - 1)
        def _():
            pl.semaphore_signal(barrier, inc=1, device_id=self.device(da=1), device_id_type=MESH)

        ends = jnp.logical_or(self.a == 0, self.a == LINE - 1).astype(jnp.int32)
        pl.semaphore_wait(barrier, len(near) + 2 - ends)


class Sender:
    def __init__(self, place, sems):
        self.place, self.sems, self.pending = place, sems, []

    def send(self, src, dst, recv_sem, step, cond=None):
        sem = self.sems.at[len(self.pending)]

        def make():
            return pltpu.make_async_remote_copy(
                src_ref=src,
                dst_ref=dst,
                send_sem=sem,
                recv_sem=recv_sem,
                device_id=self.place.device(**step),
                device_id_type=MESH,
            )

        def start():
            make().start()

        guarded(cond, start)
        self.pending.append((cond, lambda: make().wait_send()))

    def arrived(self, dst, recv_sem):
        pltpu.make_async_remote_copy(
            src_ref=dst,
            dst_ref=dst,
            send_sem=self.sems.at[0],
            recv_sem=recv_sem,
            device_id=self.place.device(dc=1),
            device_id_type=MESH,
        ).wait_recv()

    def finish(self):
        for cond, wait in self.pending:
            guarded(cond, wait)


def guarded(cond, action):
    if cond is None:
        action()
    else:
        pl.when(cond)(action)


def both(first, second):
    if first is None or second is None:
        return second if first is None else first
    return jnp.logical_and(first, second)


def gather_ticks(place, sender, full, gated, ins, outs, local_sems, recv_sems):
    a = place.a
    count = len(ins)

    def own_copy(at):
        return pltpu.make_async_copy(
            ins[at], outs[at].at[place.block(full, a)], local_sems.at[at]
        )

    def chunk(at, block, half):
        size = ins[at].shape[0] // 2
        return outs[at].at[block, pl.ds(half * size, size)]

    def sem_of(at, block, half):
        return recv_sems.at[at, block * 2 + half]

    def forward(at, block, half, src, step, cond=None):
        sender.send(src, chunk(at, block, half), sem_of(at, block, half), step, cond)

    def receive(at, block, half, cond):
        guarded(cond, lambda: sender.arrived(chunk(at, block, half), sem_of(at, block, half)))

    def held_by(at, delta, cond):
        if at not in gated:
            return cond
        return both(cond, lax.div(a + delta, LINE // 2) == place.y)

    def from_line(delta, always):
        for half in range(2):
            for at in range(count):
                block = place.block(full, a + delta)
                cond = held_by(at, delta, always)
                size = ins[at].shape[0] // 2
                if delta == 0:
                    src = ins[at].at[pl.ds(half * size, size)]
                else:
                    receive(at, block, half, cond)
                    src = chunk(at, block, half)
                if delta <= 0:
                    forward(at, block, half, src, dict(da=1), both(cond, a < LINE - 1))
                if delta >= 0:
                    forward(at, block, half, src, dict(da=-1), both(cond, a > 0))
                forward(at, block, half, src, dict(db=1), cond)
                if full:
                    forward(at, block, half, src, dict(dy=1), cond)
                forward(at, block, half, src, dict(dc=1), cond)

    def from_side(delta, always):
        for half in range(2):
            for at in range(count):
                cond = held_by(at, delta, always)
                block = place.block(full, a + delta, db=1)
                receive(at, block, half, cond)
                if full and half == 0:
                    forward(at, block, half, chunk(at, block, half), dict(dy=1), cond)
                forward(at, block, half, chunk(at, block, half), dict(dc=1), cond)
                if full:
                    block = place.block(full, a + delta, dy=1)
                    receive(at, block, half, cond)
                    if half == 1:
                        forward(at, block, half, chunk(at, block, half), dict(db=1), cond)
                    forward(at, block, half, chunk(at, block, half), dict(dc=1), cond)

    def from_corner(delta, always):
        for half in range(2):
            for at in range(count):
                cond = held_by(at, delta, always)
                block = place.block(True, a + delta, db=1, dy=1)
                receive(at, block, half, cond)
                forward(at, block, half, chunk(at, block, half), dict(dc=1), cond)

    def from_sibling(delta, always):
        for half in range(2):
            for at in range(count):
                cond = held_by(at, delta, always)
                for db in range(2):
                    for dy in range(2 if full else 1):
                        receive(at, place.block(full, a + delta, db=db, dc=1, dy=dy), half, cond)

    rounds = [[(0, None)]]
    for s in range(1, LINE):
        rounds.append([(-s, a >= s), (s, a + s < LINE)])
    stages = [from_line, from_side] + ([from_corner] if full else []) + [from_sibling]

    def tick(number):
        if number == 0:
            for at in range(count):
                own_copy(at).start()
        for level, stage in enumerate(stages):
            if 0 <= number - level < len(rounds):
                for delta, cond in rounds[number - level]:
                    stage(delta, cond)
        if number == len(rounds) + len(stages) - 2:
            for at in range(count):
                own_copy(at).wait()

    return [functools.partial(tick, number) for number in range(len(rounds) + len(stages) - 1)]


def send_pairs(sender, ins, outs, sems):
    for at, (src, dst) in enumerate(zip(ins, outs)):
        sender.send(src, dst, sems.at[at], dict(dy=1))


def take_pairs(sender, outs, sems):
    for at, dst in enumerate(outs):
        sender.arrived(dst, sems.at[at])


def gather_kernel(full, count, pairs, halved, gated, *refs):
    arrays = count + pairs + halved
    ins, outs = refs[:arrays], refs[arrays : 2 * arrays]
    local_sems, send_sems, recv_sems, pair_sems, half_sems = refs[2 * arrays :]
    place = Place()
    sender = Sender(place, send_sems)
    place.greet(full or pairs + halved > 0)
    shared = range(count + pairs, arrays)

    def part(ref, core):
        size = ref.shape[0] // CORES
        return ref.at[pl.ds(pl.multiple_of(core * size, 16), size)]

    send_pairs(sender, ins[count : count + pairs], outs[count : count + pairs], pair_sems)
    for at in shared:
        sender.send(
            part(ins[at], place.c), part(outs[at], place.c), half_sems.at[at - count - pairs, 0],
            dict(dy=1),
        )
    ticks = gather_ticks(
        place, sender, full, gated, ins[:count], outs[:count], local_sems, recv_sems
    )
    for number, tick in enumerate(ticks):
        if number == len(ticks) - 1:
            for at in shared:
                here = part(outs[at], place.c)
                sender.arrived(here, half_sems.at[at - count - pairs, 0])
                sender.send(here, here, half_sems.at[at - count - pairs, 1], dict(dc=1))
        tick()
    for at in shared:
        sender.arrived(part(outs[at], 1 - place.c), half_sems.at[at - count - pairs, 1])
    take_pairs(sender, outs[count : count + pairs], pair_sems)
    sender.finish()


def gather_rows(arrays, full, collective_id, swapped=(), halved=(), gated=()):
    blocks = LINE * SQUARE * CORES * (SQUARE if full else 1)
    count, pairs, shared = len(arrays), len(swapped), len(halved)
    lines = 2 * LINE - 1
    sends = pairs + 2 * shared + count * lines * 2 * (9 if full else 5)
    moved = sum(blocks * 2 * x.size * x.dtype.itemsize for x in arrays)
    return pl.pallas_call(
        functools.partial(gather_kernel, full, count, pairs, shared, gated),
        out_shape=[jax.ShapeDtypeStruct((blocks,) + x.shape, x.dtype) for x in arrays]
        + [jax.ShapeDtypeStruct(x.shape, x.dtype) for x in (*swapped, *halved)],
        in_specs=[pl.BlockSpec(memory_space=pl.ANY)] * (count + pairs + shared),
        out_specs=[pl.BlockSpec(memory_space=pl.ANY)] * (count + pairs + shared),
        scratch_shapes=[
            pltpu.SemaphoreType.DMA((count,)),
            pltpu.SemaphoreType.DMA((sends,)),
            pltpu.SemaphoreType.DMA((count, blocks * 2)),
            pltpu.SemaphoreType.DMA((max(pairs, 1),)),
            pltpu.SemaphoreType.DMA((max(shared, 1), 2)),
        ],
        compiler_params=pltpu.CompilerParams(collective_id=collective_id, has_side_effects=True),
        cost_estimate=pl.CostEstimate(flops=0, bytes_accessed=6 * moved, transcendentals=0),
    )(*arrays, *swapped, *halved)


def add_rows(target, sources, size):
    def step(at, carry):
        rows = pl.ds(pl.multiple_of(at * 16, 16), 16)
        total = sources[0][rows, :].astype(jnp.float32)
        for source in sources[1:]:
            total = total + source[rows, :].astype(jnp.float32)
        target[rows, :] = total.astype(target.dtype)
        return carry

    lax.fori_loop(0, size // 16, step, 0)


def scatter_ticks(place, sender, full, part, out, scratch):
    mine, got, side, up, down, load_sems, recv_sems = scratch
    a = place.a
    kinds = 4 if full else 2
    size = part.shape[1]
    half = size // 2
    order = [LINE - 1, 0, LINE - 2, 1]
    walk = (3, 1, 2, 0) if full else (1, 0)

    def sem_of(group, target, kind):
        return recv_sems.at[group, target * 4 + kind]

    def load(target, kind):
        block = place.block(full, target, db=kind % 2, dy=kind // 2)
        return pltpu.make_async_copy(
            part.at[block], mine.at[target, kind], load_sems.at[target * 4 + kind]
        )

    def begin():
        for target in order:
            for kind in walk:
                load(target, kind).start()
                block = place.block(full, target, db=kind % 2, dc=1, dy=kind // 2)
                sender.send(
                    part.at[block], got.at[target, kind], sem_of(0, target, kind), dict(dc=1)
                )

    def rows_of(ref, which):
        return ref.at[pl.ds(which * half, half)]

    def over_cores(target):
        for kind in walk:
            load(target, kind).wait()
            sender.arrived(got.at[target, kind], sem_of(0, target, kind))
            add_rows(mine.at[target, kind], [mine.at[target, kind], got.at[target, kind]], size)
            held = mine.at[target, kind]
            if kind == 3:
                sender.send(rows_of(held, 0), side.at[target, 4], sem_of(1, target, 0), dict(db=1))
                sender.send(rows_of(held, 1), side.at[target, 5], sem_of(1, target, 1), dict(dy=1))
            if kind == 1:
                sender.send(rows_of(held, 0), side.at[target, 0], sem_of(2, target, 0), dict(db=1))
                if not full:
                    sender.send(
                        rows_of(held, 1), side.at[target, 1], sem_of(2, target, 1), dict(db=1)
                    )
            if kind == 2:
                sender.send(rows_of(held, 1), side.at[target, 3], sem_of(2, target, 3), dict(dy=1))

    def over_corner(target):
        sender.arrived(side.at[target, 4], sem_of(1, target, 0))
        held = rows_of(mine.at[target, 2], 0)
        add_rows(held, [held, side.at[target, 4]], half)
        sender.send(held, side.at[target, 2], sem_of(2, target, 2), dict(dy=1))
        sender.arrived(side.at[target, 5], sem_of(1, target, 1))
        held = rows_of(mine.at[target, 1], 1)
        add_rows(held, [held, side.at[target, 5]], half)
        sender.send(held, side.at[target, 1], sem_of(2, target, 1), dict(db=1))

    def gathered(target, which):
        held = rows_of(mine.at[target, 0], which)
        parts = [held]
        for source in (0, 2) if full else (0,):
            sender.arrived(side.at[target, source + which], sem_of(2, target, source + which))
            parts.append(side.at[target, source + which])
        return held, parts

    def line_slots(target, which):
        below, above = rows_of(up.at[target], which), rows_of(down.at[target], which)
        return below, sem_of(3, target, which), above, sem_of(3, target, 2 + which)

    def over_line(target):
        def relay(which, slot, slot_sem, at_end):
            held, parts = gathered(target, which)

            def with_slot():
                sender.arrived(slot, slot_sem)
                add_rows(held, parts + [slot], half)

            pl.when(jnp.logical_not(at_end))(with_slot)
            pl.when(at_end)(lambda: add_rows(held, parts, half))

        for which in range(2):
            below, below_sem, above, above_sem = line_slots(target, which)
            held = rows_of(mine.at[target, 0], which)
            if target > 0:
                pl.when(a < target)(
                    functools.partial(relay, which, below, below_sem, a == 0)
                )
                sender.send(held, below, below_sem, dict(da=1), a < target)
            if target < LINE - 1:
                pl.when(a > target)(
                    functools.partial(relay, which, above, above_sem, a == LINE - 1)
                )
                sender.send(held, above, above_sem, dict(da=-1), a > target)

    def own_total(target):
        for which in range(2):
            below, below_sem, above, above_sem = line_slots(target, which)
            _, parts = gathered(target, which)
            if target > 0:
                sender.arrived(below, below_sem)
                parts.append(below)
            if target < LINE - 1:
                sender.arrived(above, above_sem)
                parts.append(above)
            add_rows(rows_of(out, which), parts, half)

    stages = [over_cores] + ([over_corner] if full else []) + [over_line]

    def tick(number):
        if number == 0:
            begin()
        for level, stage in enumerate(stages):
            if 0 <= number - level < len(order):
                stage(order[number - level])
        if number == len(order) + len(stages) - 2:
            for target in range(LINE):
                pl.when(a == target)(functools.partial(own_total, target))

    return [functools.partial(tick, number) for number in range(len(order) + len(stages) - 1)]


def scatter_kernel(full, pairs, part, *refs):
    ins, out, outs = refs[:pairs], refs[pairs], refs[pairs + 1 : 2 * pairs + 1]
    mine, got, side, up, down, load_sems, send_sems, recv_sems, pair_sems = refs[2 * pairs + 1 :]
    place = Place()
    sender = Sender(place, send_sems)
    place.greet(full or pairs > 0)
    send_pairs(sender, ins, outs, pair_sems)
    scratch = (mine, got, side, up, down, load_sems, recv_sems)
    for tick in scatter_ticks(place, sender, full, part, out, scratch):
        tick()
    take_pairs(sender, outs, pair_sems)
    sender.finish()


def scatter_scratch(full, rows, width, dtype, pairs):
    kinds = 4 if full else 2
    return [
        pltpu.VMEM((LINE, kinds, rows, width), dtype),
        pltpu.VMEM((LINE, kinds, rows, width), dtype),
        pltpu.VMEM((LINE, 6, rows // 2, width), dtype),
        pltpu.VMEM((LINE, rows, width), dtype),
        pltpu.VMEM((LINE, rows, width), dtype),
        pltpu.SemaphoreType.DMA((LINE * 4,)),
        pltpu.SemaphoreType.DMA((pairs + LINE * (4 + 6 + 4),)),
        pltpu.SemaphoreType.DMA((4, LINE * 4)),
        pltpu.SemaphoreType.DMA((max(pairs, 1),)),
    ]


def gather_scatter_kernel(count, gated, *refs):
    ins, part = refs[:count], refs[count]
    outs, total = refs[count + 1 : 2 * count + 1], refs[2 * count + 1]
    local_sems, gather_sends, gather_recvs = refs[2 * count + 2 : 2 * count + 5]
    mine, got, side, up, down, load_sems, scatter_sends, scatter_recvs, _ = refs[2 * count + 5 :]
    place = Place()
    gatherer = Sender(place, gather_sends)
    scatterer = Sender(place, scatter_sends)
    place.greet(True)
    scratch = (mine, got, side, up, down, load_sems, scatter_recvs)
    ticks = [
        scatter_ticks(place, scatterer, True, part, total, scratch),
        gather_ticks(place, gatherer, False, gated, ins, outs, local_sems, gather_recvs),
    ]
    for number in range(max(len(steps) for steps in ticks)):
        for steps in ticks:
            if number < len(steps):
                steps[number]()
    scatterer.finish()
    gatherer.finish()


def gather_and_scatter(arrays, part, collective_id, gated=()):
    blocks = LINE * SQUARE * CORES
    count = len(arrays)
    _, rows, width = part.shape
    sends = count * (2 * LINE - 1) * 2 * 5
    moved = sum(blocks * 2 * x.size * x.dtype.itemsize for x in arrays)
    return pl.pallas_call(
        functools.partial(gather_scatter_kernel, count, gated),
        out_shape=[jax.ShapeDtypeStruct((blocks,) + x.shape, x.dtype) for x in arrays]
        + [jax.ShapeDtypeStruct((rows, width), jnp.float32)],
        in_specs=[pl.BlockSpec(memory_space=pl.ANY)] * (count + 1),
        out_specs=[pl.BlockSpec(memory_space=pl.ANY)] * count
        + [pl.BlockSpec(memory_space=pltpu.VMEM)],
        scratch_shapes=[
            pltpu.SemaphoreType.DMA((count,)),
            pltpu.SemaphoreType.DMA((sends,)),
            pltpu.SemaphoreType.DMA((count, blocks * 2)),
        ]
        + scatter_scratch(True, rows, width, part.dtype, 0),
        compiler_params=pltpu.CompilerParams(
            collective_id=collective_id, has_side_effects=True, vmem_limit_bytes=VMEM_LIMIT
        ),
        cost_estimate=pl.CostEstimate(flops=0, bytes_accessed=6 * moved, transcendentals=0),
    )(*arrays, part)


def scatter_rows(part, full, collective_id, swapped=()):
    blocks, rows, width = part.shape
    pairs = len(swapped)
    return pl.pallas_call(
        functools.partial(scatter_kernel, full, pairs),
        out_shape=[jax.ShapeDtypeStruct((rows, width), jnp.float32)]
        + [jax.ShapeDtypeStruct(x.shape, x.dtype) for x in swapped],
        in_specs=[pl.BlockSpec(memory_space=pl.ANY)] * (1 + pairs),
        out_specs=[pl.BlockSpec(memory_space=pltpu.VMEM)]
        + [pl.BlockSpec(memory_space=pl.ANY)] * pairs,
        scratch_shapes=scatter_scratch(full, rows, width, part.dtype, pairs),
        compiler_params=pltpu.CompilerParams(
            collective_id=collective_id, has_side_effects=True, vmem_limit_bytes=VMEM_LIMIT
        ),
        cost_estimate=pl.CostEstimate(
            flops=0, bytes_accessed=12 * part.size * part.dtype.itemsize, transcendentals=0
        ),
    )(part, *swapped)


def contract_last(left, right):
    return lax.dot_general(
        left, right, (((1,), (1,)), ((), ())), preferred_element_type=jnp.float32
    )


def contract_first(left, right):
    return lax.dot_general(
        left, right, (((0,), (0,)), ((), ())), preferred_element_type=jnp.float32
    )


def expert_kernel(
    capacity,
    normed,
    grads,
    routes,
    router_rows,
    w_gate,
    w_up,
    w_down,
    shared_in,
    shared_out,
    out_part,
    d_part,
    ex_rows,
    ex_grads,
    act_out,
    d_gate_out,
    d_up_out,
    shared_in_grad,
    shared_out_grad,
    in_total,
    out_total,
):
    position = lax.axis_index("expert")
    experts = lax.axis_size("expert")
    group, rows, width = normed.shape
    tokens, slots = group * rows, group * capacity
    bf16 = jnp.bfloat16
    x = normed[...].reshape(tokens, width)
    g = grads[...].reshape(tokens, width)

    row = lax.broadcasted_iota(jnp.int32, (tokens, tokens), 0)
    column = lax.broadcasted_iota(jnp.int32, (tokens, tokens), 1)
    before = jnp.logical_and(column < row, lax.div(row, rows) == lax.div(column, rows))
    named = routes[...].reshape(tokens, -1) == position.astype(jnp.float32).astype(bf16)
    hit = jnp.sum(jnp.where(named, 1.0, 0.0), axis=1, keepdims=True)
    tally = matrix_product(
        jnp.where(before, 1.0, 0.0).astype(bf16),
        jnp.broadcast_to(hit, (tokens, 128)).astype(bf16),
    )
    place = jnp.where(hit > 0.5, tally[:, :1], -1.0)
    token = lax.broadcasted_iota(jnp.int32, (tokens, slots), 0)
    slot = lax.broadcasted_iota(jnp.int32, (tokens, slots), 1)
    same = lax.div(slot, capacity) == lax.div(token, rows)
    wanted = lax.rem(slot, capacity).astype(jnp.float32)
    chosen = jnp.where(jnp.logical_and(same, wanted == place), 1.0, 0.0)
    pick = chosen.T.astype(bf16)
    put = chosen.astype(bf16)

    r = matrix_product(pick, x).astype(bf16)
    gr = matrix_product(pick, g).astype(bf16)
    ex_rows[...] = r
    ex_grads[...] = gr
    lane = lax.broadcasted_iota(jnp.int32, (slots, router_rows.shape[0]), 1)
    logits = jnp.where(lane < experts, contract_last(r, router_rows[...]), -1e30)
    exps = jnp.exp(logits - jnp.max(logits, axis=1, keepdims=True))
    gate = jnp.sum(jnp.where(lane == position, exps, 0.0), axis=1, keepdims=True) / jnp.sum(
        exps, axis=1, keepdims=True
    )

    pre_gate = contract_last(r, w_gate[...])
    pre_up = contract_last(r, w_up[...])
    act_gate, slope = silu_parts(pre_gate)
    act = act_gate * pre_up
    back = contract_last(gr, w_down[...])
    d_gate_slot = jnp.sum(act * back, axis=1, keepdims=True)
    scaled = (gate * act).astype(bf16)
    d_act = gate * back
    d_pre_gate = (d_act * pre_up * slope).astype(bf16)
    d_pre_up = (d_act * act_gate).astype(bf16)
    act_out[...] = scaled
    d_gate_out[...] = d_pre_gate
    d_up_out[...] = d_pre_up
    ex_out = matrix_product(scaled, w_down[...]).astype(bf16)
    d_ex = matrix_product(d_pre_gate, w_gate[...]) + matrix_product(d_pre_up, w_up[...])
    d_ex = d_ex.astype(bf16)

    units = shared_out.shape[0]
    mix = matrix_product(x, shared_in[...])
    sh_gate, sh_up = mix[:, :units], mix[:, units:]
    sh_silu, sh_slope = silu_parts(sh_gate)
    sh_act = (sh_silu * sh_up).astype(bf16)
    d_sh_act = contract_last(g, shared_out[...])
    d_mix = jnp.concatenate([d_sh_act * sh_up * sh_slope, d_sh_act * sh_silu], axis=1)
    d_mix = d_mix.astype(bf16)

    out = matrix_product(put, ex_out) + matrix_product(sh_act, shared_out[...])
    out_part[...] = out.astype(bf16).reshape(group, rows, width)
    d_in = matrix_product(put, d_ex) + contract_last(d_mix, shared_in[...])
    d_part[:, :, :width] = d_in.astype(bf16).reshape(group, rows, width)
    lane = lax.broadcasted_iota(jnp.int32, (slots, d_part.shape[2] - width), 1)
    d_gates = jnp.where(lane == position, d_gate_slot, 0.0).astype(bf16)
    d_part[:, :, width:] = matrix_product(put, d_gates).astype(bf16).reshape(group, rows, -1)

    step = pl.program_id(0)

    @pl.when(step == 0)
    def _():
        in_total[...] = jnp.zeros_like(in_total)
        out_total[...] = jnp.zeros_like(out_total)

    in_total[...] += contract_first(d_mix, x)
    out_total[...] += contract_first(sh_act, g)

    @pl.when(step == pl.num_programs(0) - 1)
    def _():
        shared_in_grad[...] = in_total[...].T.astype(bf16)
        shared_out_grad[...] = out_total[...]


def expert_phase(
    all_normed, all_grads, router_rows, w_gate, w_up, w_down, shared_in, shared_out, capacity
):
    blocks, rows, width = all_normed.shape
    group = 4
    slots = group * capacity
    hidden = w_gate.shape[0]
    units = shared_out.shape[0]
    side = all_grads.shape[2] - width
    bf16 = jnp.bfloat16

    def by_group(shape):
        zeros = (0,) * (len(shape) - 1)
        return pl.BlockSpec(shape, lambda i: (i,) + zeros)

    def fixed(shape):
        return pl.BlockSpec(
            shape, lambda i: (0,) * len(shape), pipeline_mode=pl.Buffered(buffer_count=1)
        )

    return pl.pallas_call(
        functools.partial(expert_kernel, capacity),
        grid=(blocks // group,),
        out_shape=[
            jax.ShapeDtypeStruct((blocks, rows, width), bf16),
            jax.ShapeDtypeStruct((blocks, rows, width + side), bf16),
            jax.ShapeDtypeStruct((blocks * capacity, width), bf16),
            jax.ShapeDtypeStruct((blocks * capacity, width), bf16),
            jax.ShapeDtypeStruct((blocks * capacity, hidden), bf16),
            jax.ShapeDtypeStruct((blocks * capacity, hidden), bf16),
            jax.ShapeDtypeStruct((blocks * capacity, hidden), bf16),
            jax.ShapeDtypeStruct((width, 2 * units), bf16),
            jax.ShapeDtypeStruct((units, width), jnp.float32),
        ],
        in_specs=[
            by_group((group, rows, width)),
            by_group((group, rows, width)),
            pl.BlockSpec((group, rows, side), lambda i: (i, 0, width // side)),
            fixed(router_rows.shape),
            fixed(w_gate.shape),
            fixed(w_up.shape),
            fixed(w_down.shape),
            fixed(shared_in.shape),
            fixed(shared_out.shape),
        ],
        out_specs=[
            by_group((group, rows, width)),
            by_group((group, rows, width + side)),
            by_group((slots, width)),
            by_group((slots, width)),
            by_group((slots, hidden)),
            by_group((slots, hidden)),
            by_group((slots, hidden)),
            fixed((width, 2 * units)),
            fixed((units, width)),
        ],
        scratch_shapes=[
            pltpu.VMEM((2 * units, width), jnp.float32),
            pltpu.VMEM((units, width), jnp.float32),
        ],
        compiler_params=pltpu.CompilerParams(vmem_limit_bytes=VMEM_LIMIT),
        cost_estimate=pl.CostEstimate(
            flops=2 * blocks * capacity * width * hidden * 6,
            bytes_accessed=10 * blocks * rows * width * 2,
            transcendentals=blocks * capacity * hidden,
        ),
    )(all_normed, all_grads, all_grads, router_rows, w_gate, w_up, w_down, shared_in, shared_out)


def exchange_kernel(x, out, local_sem, send_sems, recv_sems):
    me, y = lax.axis_index("expert"), lax.axis_index("fsdp")
    count = x.shape[0]
    barrier = pltpu.get_barrier_semaphore()
    peers = [lax.rem(me + step, count) for step in range(1, count)]
    for peer in peers:
        pl.semaphore_signal(barrier, inc=1, device_id=(peer, y), device_id_type=MESH)
    own = pltpu.make_async_copy(x.at[me], out.at[me], local_sem)
    own.start()
    pl.semaphore_wait(barrier, count - 1)
    copies = []
    for at, peer in enumerate(peers):
        copy = pltpu.make_async_remote_copy(
            src_ref=x.at[peer],
            dst_ref=out.at[me],
            send_sem=send_sems.at[at],
            recv_sem=recv_sems.at[at],
            device_id=(peer, y),
            device_id_type=MESH,
        )
        copy.start()
        copies.append(copy)
    for copy in copies:
        copy.wait()
    own.wait()


def exchange(x, collective_id):
    count = x.shape[0]
    return pl.pallas_call(
        exchange_kernel,
        out_shape=jax.ShapeDtypeStruct(x.shape, x.dtype),
        in_specs=[pl.BlockSpec(memory_space=pl.ANY)],
        out_specs=pl.BlockSpec(memory_space=pl.ANY),
        scratch_shapes=[
            pltpu.SemaphoreType.DMA,
            pltpu.SemaphoreType.DMA((count - 1,)),
            pltpu.SemaphoreType.DMA((count - 1,)),
        ],
        compiler_params=pltpu.CompilerParams(collective_id=collective_id, has_side_effects=True),
        cost_estimate=pl.CostEstimate(
            flops=0, bytes_accessed=20 * x.size * x.dtype.itemsize, transcendentals=0
        ),
    )(x)


def swap_halves(value):
    half = value.shape[1] // 2
    return jnp.concatenate([value[:, half:], value[:, :half]], axis=1)


def greet_plane(place):
    me = lax.axis_index("expert")
    count = LINE * SQUARE * CORES
    barrier = pltpu.get_barrier_semaphore()
    for step in range(1, count):
        peer = (lax.rem(me + step, count), place.y)
        pl.semaphore_signal(barrier, inc=1, device_id=peer, device_id_type=MESH)
    pl.semaphore_signal(barrier, inc=1, device_id=place.device(dy=1), device_id_type=MESH)
    pl.semaphore_wait(barrier, count)


def sums_kernel(pairs, moved, small, large, *refs):
    ins = refs[:pairs]
    moved_out, small_out, large_out = refs[pairs : pairs + 3]
    outs = refs[pairs + 3 : 2 * pairs + 3]
    rest = refs[2 * pairs + 3 :]
    local_sem, exchange_sends, exchange_recvs = rest[:3]
    first, second = rest[3:12], rest[12:21]
    place = Place()
    me = lax.axis_index("expert")
    count = moved.shape[0]
    greet_plane(place)
    own = pltpu.make_async_copy(moved.at[me], moved_out.at[me], local_sem)
    own.start()
    copies = []
    for at in range(count - 1):
        copy = pltpu.make_async_remote_copy(
            src_ref=moved.at[lax.rem(me + at + 1, count)],
            dst_ref=moved_out.at[me],
            send_sem=exchange_sends.at[at],
            recv_sem=exchange_recvs.at[at],
            device_id=(lax.rem(me + at + 1, count), place.y),
            device_id_type=MESH,
        )
        copy.start()
        copies.append(copy)
    senders = [Sender(place, first[6]), Sender(place, second[6])]
    send_pairs(senders[0], ins, outs, first[8])
    ticks = [
        scatter_ticks(place, senders[0], False, small, small_out, first[:6] + (first[7],)),
        scatter_ticks(place, senders[1], True, large, large_out, second[:6] + (second[7],)),
    ]
    for number in range(max(len(steps) for steps in ticks)):
        for steps in ticks:
            if number < len(steps):
                steps[number]()
    take_pairs(senders[0], outs, first[8])
    for sender in senders:
        sender.finish()
    for copy in copies:
        copy.wait()
    own.wait()


def exchange_and_sums(moved, small, large, swapped, collective_id):
    count, pairs = moved.shape[0], len(swapped)
    hbm = pl.BlockSpec(memory_space=pl.ANY)
    vmem = pl.BlockSpec(memory_space=pltpu.VMEM)
    return pl.pallas_call(
        functools.partial(sums_kernel, pairs),
        out_shape=[
            jax.ShapeDtypeStruct(moved.shape, moved.dtype),
            jax.ShapeDtypeStruct(small.shape[1:], jnp.float32),
            jax.ShapeDtypeStruct(large.shape[1:], jnp.float32),
        ]
        + [jax.ShapeDtypeStruct(x.shape, x.dtype) for x in swapped],
        in_specs=[hbm] * (3 + pairs),
        out_specs=[hbm, vmem, vmem] + [hbm] * pairs,
        scratch_shapes=[
            pltpu.SemaphoreType.DMA,
            pltpu.SemaphoreType.DMA((count - 1,)),
            pltpu.SemaphoreType.DMA((count - 1,)),
        ]
        + scatter_scratch(False, *small.shape[1:], small.dtype, pairs)
        + scatter_scratch(True, *large.shape[1:], large.dtype, 0),
        compiler_params=pltpu.CompilerParams(
            collective_id=collective_id, has_side_effects=True, vmem_limit_bytes=VMEM_LIMIT
        ),
        cost_estimate=pl.CostEstimate(
            flops=0, bytes_accessed=12 * large.size * 2, transcendentals=0
        ),
    )(moved, small, large, *swapped)


def attend_kernel(
    rows,
    g_attn,
    w_front,
    g_lat,
    expand_head,
    cosines,
    sines,
    normed_out,
    latent_out,
    query_out,
    key_out,
    value_out,
    head_out,
    sum_out,
    log_out,
    keys,
    values,
):
    bf16 = jnp.bfloat16
    size = rows.shape[0]
    scale = (PLAIN_UNITS + ROTARY_UNITS) ** (-0.5)
    step = pl.program_id(0)
    normed, _ = norm_forward(rows[...].astype(jnp.float32), g_attn[...])
    normed = normed.astype(bf16)
    normed_out[...] = normed
    front = contract_last(normed, w_front[...])
    latent, _ = norm_forward(front[:, :LATENT_WIDTH], g_lat[...])
    latent = latent.astype(bf16)
    latent_out[...] = latent
    width = LATENT_WIDTH + ROTARY_UNITS

    def rotated(value):
        return value * cosines[...] + swap_halves(value) * sines[...]

    pairs = matrix_product(latent, expand_head[...])
    key = jnp.concatenate([pairs[:, :PLAIN_UNITS], rotated(front[:, LATENT_WIDTH:width])], axis=1)
    query = jnp.concatenate(
        [front[:, width : width + PLAIN_UNITS], rotated(front[:, width + PLAIN_UNITS :])], axis=1
    ).astype(bf16)
    key = key.astype(bf16)
    value = pairs[:, PLAIN_UNITS:].astype(bf16)
    query_out[...] = query
    key_out[...] = key
    value_out[...] = value
    here = pl.ds(pl.multiple_of(step * size, size), size)
    keys[here, :] = key
    values[here, :] = value
    row = lax.broadcasted_iota(jnp.int32, (size, size), 0)
    column = lax.broadcasted_iota(jnp.int32, (size, size), 1)
    near = jnp.where(column <= row, contract_last(query, key) * scale, -1e30)

    def over(past):
        top = jnp.max(near, axis=1, keepdims=True)
        if past:
            far = contract_last(query, keys[:past, :]) * scale
            top = jnp.maximum(top, jnp.max(far, axis=1, keepdims=True))
        exps = jnp.exp(near - top)
        total = jnp.sum(exps, axis=1, keepdims=True)
        mixed = matrix_product(exps.astype(bf16), value)
        if past:
            exps = jnp.exp(far - top)
            total = total + jnp.sum(exps, axis=1, keepdims=True)
            mixed = mixed + matrix_product(exps.astype(bf16), values[:past, :])
        mixed = mixed / total
        sum_out[...] = mixed
        head_out[...] = mixed.astype(bf16)
        wide = jnp.broadcast_to(top + jnp.log(total), (size, 128))
        log_out[0] = wide.T[:1, :]

    for at in range(keys.shape[0] // size):
        pl.when(step == at)(functools.partial(over, at * size))


def attend(rows, g_attn, w_front, g_lat, expand_head, cosines, sines):
    seq_len, width = rows.shape
    size = 256
    steps = seq_len // size
    units = PLAIN_UNITS + ROTARY_UNITS
    bf16 = jnp.bfloat16

    def by_step(columns):
        return pl.BlockSpec((size, columns), lambda i: (i, 0))

    def fixed(x):
        return pl.BlockSpec(
            x.shape, lambda i: (0, 0), pipeline_mode=pl.Buffered(buffer_count=1)
        )

    return pl.pallas_call(
        attend_kernel,
        grid=(steps,),
        out_shape=[
            jax.ShapeDtypeStruct((seq_len, width), bf16),
            jax.ShapeDtypeStruct((seq_len, LATENT_WIDTH), bf16),
            jax.ShapeDtypeStruct((seq_len, units), bf16),
            jax.ShapeDtypeStruct((seq_len, units), bf16),
            jax.ShapeDtypeStruct((seq_len, VALUE_UNITS), bf16),
            jax.ShapeDtypeStruct((seq_len, VALUE_UNITS), bf16),
            jax.ShapeDtypeStruct((seq_len, VALUE_UNITS), jnp.float32),
            jax.ShapeDtypeStruct((steps, 1, size), jnp.float32),
        ],
        in_specs=[by_step(width)]
        + [fixed(x) for x in (g_attn, w_front, g_lat, expand_head)]
        + [by_step(ROTARY_UNITS)] * 2,
        out_specs=[
            by_step(width),
            by_step(LATENT_WIDTH),
            by_step(units),
            by_step(units),
            by_step(VALUE_UNITS),
            by_step(VALUE_UNITS),
            by_step(VALUE_UNITS),
            pl.BlockSpec((1, 1, size), lambda i: (i, 0, 0)),
        ],
        scratch_shapes=[
            pltpu.VMEM((seq_len, units), bf16),
            pltpu.VMEM((seq_len, VALUE_UNITS), bf16),
        ],
        compiler_params=pltpu.CompilerParams(vmem_limit_bytes=VMEM_LIMIT),
        cost_estimate=pl.CostEstimate(
            flops=2 * seq_len * (width * 768 + seq_len * units),
            bytes_accessed=3 * rows.size * 2,
            transcendentals=seq_len * seq_len // 2,
        ),
    )(rows, g_attn, w_front, g_lat, expand_head, cosines, sines)


def attend_back_kernel(
    query,
    key,
    value,
    d_head,
    head_sum,
    logs,
    expand_head,
    cosines,
    sines,
    d_query_out,
    d_pairs_out,
    d_keys_out,
    d_key,
    d_value,
    key_turned,
):
    bf16 = jnp.bfloat16
    size = query.shape[0]
    seq_len = key.shape[0]
    scale = (PLAIN_UNITS + ROTARY_UNITS) ** (-0.5)
    step = pl.program_id(0)

    @pl.when(step == 0)
    def _():
        d_key[...] = jnp.zeros_like(d_key)
        d_value[...] = jnp.zeros_like(d_value)
        for at in range(0, seq_len, size):
            part = key[at : at + size, :].astype(jnp.float32)
            key_turned[:, at : at + size] = part.T.astype(bf16)

    q, d_out = query[...], d_head[...]
    product = d_out.astype(jnp.float32) * head_sum[...]
    delta = jnp.sum(product.T, axis=0, keepdims=True)
    log_row = logs[0]
    row = lax.broadcasted_iota(jnp.int32, (size, size), 0)
    column = lax.broadcasted_iota(jnp.int32, (size, size), 1)

    def grads_of(at, mask):
        there = slice(at, at + size)
        scores = contract_last(key[there, :], q) * scale
        if mask:
            scores = jnp.where(row <= column, scores, -1e30)
        probs = jnp.exp(scores - log_row)
        d_probs = contract_last(value[there, :], d_out)
        d_scores = (probs * (d_probs - delta) * scale).astype(bf16)
        d_key[there, :] += matrix_product(d_scores, q)
        d_value[there, :] += matrix_product(probs.astype(bf16), d_out)
        return matrix_product(key_turned[:, there], d_scores)

    def over(past):
        total = grads_of(past, True)
        for at in range(0, past, size):
            total = total + grads_of(at, False)
        d_query = total.T
        d_rope = d_query[:, PLAIN_UNITS:]
        d_rope = d_rope * cosines[...] - swap_halves(d_rope) * sines[...]
        d_query_out[...] = jnp.concatenate([d_query[:, :PLAIN_UNITS], d_rope], axis=1).astype(bf16)

    for at in range(seq_len // size):
        pl.when(step == at)(functools.partial(over, at * size))

    @pl.when(step == seq_len // size - 1)
    def _():
        for at in range(0, seq_len, size):
            there = slice(at, at + size)
            d_pairs = jnp.concatenate(
                [d_key[there, :PLAIN_UNITS], d_value[there, :]], axis=1
            ).astype(bf16)
            d_pairs_out[there, :] = d_pairs
            d_keys_out[there, :LATENT_WIDTH] = contract_last(d_pairs, expand_head[...]).astype(bf16)
            tail = jnp.concatenate(
                [d_key[there, PLAIN_UNITS:], jnp.zeros((size, ROTARY_UNITS), jnp.float32)], axis=1
            )
            d_keys_out[there, LATENT_WIDTH:] = tail.astype(bf16)


def attend_back(query, key, value, d_head, head_sum, logs, expand_head, cosines, sines):
    seq_len, units = query.shape
    steps, _, size = logs.shape
    bf16 = jnp.bfloat16
    keys_width = LATENT_WIDTH + 2 * ROTARY_UNITS

    def by_step(columns):
        return pl.BlockSpec((size, columns), lambda i: (i, 0))

    def fixed(shape):
        return pl.BlockSpec(shape, lambda i: (0, 0), pipeline_mode=pl.Buffered(buffer_count=1))

    return pl.pallas_call(
        attend_back_kernel,
        grid=(steps,),
        out_shape=[
            jax.ShapeDtypeStruct((seq_len, units), bf16),
            jax.ShapeDtypeStruct((seq_len, PLAIN_UNITS + VALUE_UNITS), bf16),
            jax.ShapeDtypeStruct((seq_len, keys_width), bf16),
        ],
        in_specs=[
            by_step(units),
            fixed(key.shape),
            fixed(value.shape),
            by_step(VALUE_UNITS),
            by_step(VALUE_UNITS),
            pl.BlockSpec((1, 1, size), lambda i: (i, 0, 0)),
            fixed(expand_head.shape),
            by_step(ROTARY_UNITS),
            by_step(ROTARY_UNITS),
        ],
        out_specs=[
            by_step(units),
            fixed((seq_len, PLAIN_UNITS + VALUE_UNITS)),
            fixed((seq_len, keys_width)),
        ],
        scratch_shapes=[
            pltpu.VMEM((seq_len, units), jnp.float32),
            pltpu.VMEM((seq_len, VALUE_UNITS), jnp.float32),
            pltpu.VMEM((units, seq_len), bf16),
        ],
        compiler_params=pltpu.CompilerParams(vmem_limit_bytes=VMEM_LIMIT),
        cost_estimate=pl.CostEstimate(
            flops=5 * seq_len * seq_len * units,
            bytes_accessed=8 * seq_len * units * 2,
            transcendentals=seq_len * seq_len // 2,
        ),
    )(query, key, value, d_head, head_sum, logs, expand_head, cosines, sines)


def norm_back_rows(value, gain, grad):
    inverse = lax.rsqrt(jnp.mean(value * value, axis=-1, keepdims=True) + EPS)
    unit = value * inverse
    scaled = grad * gain
    d_value = inverse * (scaled - unit * jnp.mean(scaled * unit, axis=-1, keepdims=True))
    return d_value, jnp.sum(grad * unit, axis=0, keepdims=True)


def hidden_back_kernel(
    d_back,
    router,
    normed,
    hidden,
    gain,
    router_rows,
    grads,
    out_own,
    out_other,
    d_hidden_out,
    d_attn_out,
    d_heads_out,
    g_router_out,
    g_gain_out,
):
    bf16 = jnp.bfloat16
    width = hidden.shape[1]
    spare = router.shape[1]
    gates = router[...]
    d_router = d_back[:, width : width + spare]
    d_logits = gates * (d_router - jnp.sum(gates * d_router, axis=1, keepdims=True))
    d_logits = d_logits.astype(bf16)
    g_router_out[...] = contract_first(d_logits, normed[...])
    d_normed = d_back[:, :width] + matrix_product(d_logits, router_rows[...])
    d_value, g_gain = norm_back_rows(hidden[...], gain[...], d_normed)
    g_gain_out[...] = g_gain
    d_hidden = grads[...].astype(jnp.float32) + d_value
    d_hidden_out[...] = d_hidden
    d_attn = d_hidden.astype(bf16)
    d_attn_out[...] = d_attn
    shard = lax.axis_index("fsdp")
    half = out_own.shape[0] // VALUE_UNITS
    for weight, first in ((out_own, shard * half), (out_other, (1 - shard) * half)):
        product = contract_last(d_attn, weight[...]).astype(bf16)
        for at in range(half):
            d_heads_out[first + at] = product[:, at * VALUE_UNITS : (at + 1) * VALUE_UNITS]


def hidden_back(d_back, router, normed, hidden, gain, router_rows, grads, out_own, out_other):
    rows, width = hidden.shape
    heads = 2 * out_own.shape[0] // VALUE_UNITS
    return pl.pallas_call(
        hidden_back_kernel,
        out_shape=[
            jax.ShapeDtypeStruct((rows, width), jnp.float32),
            jax.ShapeDtypeStruct((rows, width), jnp.bfloat16),
            jax.ShapeDtypeStruct((heads, rows, VALUE_UNITS), jnp.bfloat16),
            jax.ShapeDtypeStruct((router.shape[1], width), jnp.float32),
            jax.ShapeDtypeStruct((1, width), jnp.float32),
        ],
        compiler_params=pltpu.CompilerParams(vmem_limit_bytes=VMEM_LIMIT),
        cost_estimate=pl.CostEstimate(
            flops=4 * rows * width * out_own.shape[0],
            bytes_accessed=4 * out_own.size + 16 * rows * width,
            transcendentals=0,
        ),
    )(d_back, router, normed, hidden, gain, router_rows, grads, out_own, out_other)


def input_back_kernel(
    d_query,
    d_sums,
    query_own,
    query_other,
    tokens,
    gain,
    w_latent,
    lat_gain,
    cosines,
    sines,
    d_hidden,
    d_tokens_out,
    g_latent_out,
    g_gain_out,
    g_lat_out,
):
    bf16 = jnp.bfloat16
    x = tokens[...].astype(jnp.float32)
    normed, _ = norm_forward(x, gain[...])
    normed = normed.astype(bf16)
    latent = contract_last(normed, w_latent[:LATENT_WIDTH, :])
    d_compact, g_lat = norm_back_rows(latent, lat_gain[...], d_sums[:, :LATENT_WIDTH])
    g_lat_out[...] = g_lat
    d_rope = d_sums[:, LATENT_WIDTH : LATENT_WIDTH + ROTARY_UNITS]
    d_rope = d_rope * cosines[...] - swap_halves(d_rope) * sines[...]
    d_latent = jnp.concatenate([d_compact, d_rope], axis=1).astype(bf16)
    g_latent_out[...] = contract_first(d_latent, normed)
    d_full = jnp.concatenate([d_query[at] for at in range(d_query.shape[0])], axis=1)
    own = contract_last(d_full, query_own[...])
    other = contract_last(d_full, query_other[...])
    first = lax.rem(lax.axis_index("expert"), CORES) == 0
    lower, upper = jnp.where(first, own, other), jnp.where(first, other, own)
    size = lower.shape[1] // 2
    d_normed = jnp.concatenate(
        [lower[:, :size], upper[:, :size], lower[:, size:], upper[:, size:]], axis=1
    )
    d_normed = d_normed + matrix_product(d_latent, w_latent[...])
    d_value, g_gain = norm_back_rows(x, gain[...], d_normed)
    g_gain_out[...] = g_gain
    d_tokens_out[...] = (d_hidden[...] + d_value).astype(bf16)


def input_back(d_query, d_sums, query_own, query_other, tokens, gain, w_latent, lat_gain, cosines, sines, d_hidden):
    rows, width = tokens.shape
    return pl.pallas_call(
        input_back_kernel,
        out_shape=[
            jax.ShapeDtypeStruct((rows, width), jnp.bfloat16),
            jax.ShapeDtypeStruct((w_latent.shape[0], width), jnp.float32),
            jax.ShapeDtypeStruct((1, width), jnp.float32),
            jax.ShapeDtypeStruct((1, LATENT_WIDTH), jnp.float32),
        ],
        compiler_params=pltpu.CompilerParams(vmem_limit_bytes=VMEM_LIMIT),
        cost_estimate=pl.CostEstimate(
            flops=4 * rows * query_own.size,
            bytes_accessed=4 * query_own.size + 16 * rows * width,
            transcendentals=0,
        ),
    )(
        d_query,
        d_sums,
        query_own,
        query_other,
        tokens,
        gain,
        w_latent,
        lat_gain,
        cosines,
        sines,
        d_hidden,
    )


def finish_kernel(query, expand, out_rows, query_out, expand_out, out_out):
    heads, units, width = query.shape
    query_out[...] = query[...].reshape(heads * units, width).astype(jnp.float32).T
    for at in range(heads):
        columns = expand.shape[2]
        expand_out[:, at * columns : (at + 1) * columns] = expand[at].astype(jnp.float32)
    out_out[...] = out_rows[...].reshape(out_out.shape).astype(jnp.float32)


def finish(query, expand, out_rows):
    heads, units, width = query.shape
    _, latents, columns = expand.shape
    _, rows, model = out_rows.shape
    return pl.pallas_call(
        finish_kernel,
        grid=(heads // 2,),
        out_shape=[
            jax.ShapeDtypeStruct((width, heads * units), jnp.float32),
            jax.ShapeDtypeStruct((latents, heads * columns), jnp.float32),
            jax.ShapeDtypeStruct((heads * rows, model), jnp.float32),
        ],
        in_specs=[
            pl.BlockSpec((2, units, width), lambda i: (i, 0, 0)),
            pl.BlockSpec((2, latents, columns), lambda i: (i, 0, 0)),
            pl.BlockSpec((2, rows, model), lambda i: (i, 0, 0)),
        ],
        out_specs=[
            pl.BlockSpec((width, 2 * units), lambda i: (0, i)),
            pl.BlockSpec((latents, 2 * columns), lambda i: (0, i)),
            pl.BlockSpec((2 * rows, model), lambda i: (i, 0)),
        ],
        compiler_params=pltpu.CompilerParams(vmem_limit_bytes=VMEM_LIMIT),
        cost_estimate=pl.CostEstimate(
            flops=0, bytes_accessed=6 * heads * units * width, transcendentals=0
        ),
    )(query, expand, out_rows)


def token_gather(rows):
    return lax.all_gather(rows, ("fsdp", "expert"), axis=0, tiled=True)


def split_body(
    tokens,
    routes,
    cotangent,
    attn_gain,
    w_query,
    latent_weight,
    latent_norm_gain,
    expand_weight,
    w_out,
    ffn_gain,
    w_router,
    shared_gate,
    shared_up,
    shared_down,
    expert_gate,
    expert_up,
    expert_down,
):
    rows = tokens.shape[1]
    experts = lax.axis_size("expert")
    shards = lax.axis_size("fsdp")
    position = lax.axis_index("expert")
    blocks = experts * shards
    seq_len = rows * experts
    capacity = shards * ((rows * TOPK * 4 + experts * 3 * shards - 1) // (experts * 3 * shards))
    head_units = PLAIN_UNITS + ROTARY_UNITS
    pair_units = PLAIN_UNITS + VALUE_UNITS
    feature_width = LATENT_WIDTH + ROTARY_UNITS
    scale = head_units ** (-0.5)

    shard = lax.axis_index("fsdp")
    first = shard == 0

    query_cols = lax.dynamic_slice_in_dim(w_query, position * head_units, head_units, 1)
    expand_cols = lax.dynamic_slice_in_dim(expand_weight, position * pair_units, pair_units, 1)
    owners = experts // shards
    lat_row = jnp.pad(latent_norm_gain, (0, w_query.shape[0] - latent_norm_gain.shape[0]))
    packed = jnp.concatenate(
        [query_cols.T, w_router.T, attn_gain[None], ffn_gain[None], lat_row[None]],
        axis=0,
    )
    packed = jnp.pad(packed, ((0, -packed.shape[0] % 32), (0, 0)))
    seq_rows, other_packed, other_expand, other_latent, out_other = gather_rows(
        [tokens[0]], False, 0, swapped=[packed, expand_cols], halved=[latent_weight.T, w_out]
    )

    def whole(own, other, axis):
        return jnp.concatenate(
            [jnp.where(first, own, other), jnp.where(first, other, own)], axis=axis
        )

    lat_half = latent_norm_gain.shape[0]
    at = head_units
    packed_rows = whole(packed, other_packed, 1)
    expand_head = whole(expand_cols, other_expand, 0)
    w_latent = whole(latent_weight.T, other_latent, 1)
    w_front = jnp.concatenate([w_latent, packed_rows[:at]], axis=0)
    router_rows = packed_rows[at:]
    wrout = packed_rows[at : at + experts]
    g_attn = packed_rows[at + experts].astype(jnp.float32)
    g_ffn = packed_rows[at + experts + 1].astype(jnp.float32)
    lat_row = packed_rows[at + experts + 2]
    g_lat = jnp.concatenate(
        [lat_row[:lat_half], lat_row[w_query.shape[0] : w_query.shape[0] + lat_half]]
    ).astype(jnp.float32)
    units = shared_down.shape[0]

    core = lax.rem(position, CORES)

    def by_cores(weight):
        size = weight.shape[0] // CORES
        own = lax.dynamic_slice_in_dim(weight, core * size, size, 0)
        own = lax.all_gather(own, "fsdp", axis=0, tiled=True)
        swap = [(index, index ^ 1) for index in range(experts)]
        return own, lax.ppermute(own, "expert", swap)

    grad_rows = cotangent[0]
    grad_out = grad_rows.astype(jnp.float32)
    own_routes = jnp.pad(routes[0], ((0, 0), (0, 128 - TOPK)), constant_values=-1)
    grad_rows = jnp.concatenate([grad_rows, own_routes.astype(jnp.bfloat16)], axis=1)
    seq_rows, shared_gate, shared_up = lax.optimization_barrier(
        (seq_rows, shared_gate, shared_up)
    )
    def to_columns(weight):
        parts = weight.reshape(weight.shape[0], blocks, units).transpose(1, 0, 2)
        return lax.all_to_all(
            parts, ("expert", "fsdp"), split_axis=0, concat_axis=0, tiled=True
        ).reshape(-1, units)

    sh_cols = to_columns(jnp.concatenate([shared_gate, shared_up], axis=0)).reshape(
        blocks, 2, shared_gate.shape[0], units
    )
    lanes = -(-units // 128) * 128
    sh_cols = jnp.pad(sh_cols, ((0, 0), (0, 0), (0, 0), (0, lanes - units)))
    shared_in = sh_cols.transpose(0, 2, 1, 3).reshape(MODEL_WIDTH, 2 * lanes)
    shared_out = jnp.pad(shared_down, ((0, lanes - units), (0, 0)))
    all_grads = token_gather(grad_rows)

    x_in = tokens[0].astype(jnp.float32)
    normed, inv_attn = norm_forward(x_in, g_attn)
    normed_in = normed.astype(jnp.bfloat16)
    half_units = ROTARY_UNITS // 2
    freqs = 10000.0 ** (-np.arange(half_units) * (2.0 / ROTARY_UNITS))
    angles = np.arange(seq_len)[:, None] * freqs[None, :]
    cosine_table = jnp.asarray(np.cos(angles), jnp.float32)
    sine_table = jnp.asarray(np.sin(angles), jnp.float32)
    cosines = jnp.asarray(np.concatenate([np.cos(angles)] * 2, axis=1), jnp.float32)
    sines = jnp.asarray(np.concatenate([-np.sin(angles), np.sin(angles)], axis=1), jnp.float32)
    (
        seq_normed,
        latent_rows,
        query,
        key,
        value,
        head_rows,
        head_sum,
        logs,
    ) = attend(
        seq_rows.reshape(seq_len, MODEL_WIDTH),
        g_attn[None],
        w_front,
        g_lat[None],
        expand_head,
        cosines,
        sines,
    )
    head_rows, shared_in = lax.optimization_barrier((head_rows, shared_in))
    heads = exchange(head_rows.reshape(experts, rows, VALUE_UNITS), 1)
    heads = heads.transpose(1, 0, 2).reshape(rows, experts * VALUE_UNITS)
    half_heads = w_out.shape[0]
    own_heads = lax.dynamic_slice_in_dim(heads, shard * half_heads, half_heads, 1)
    other_heads = lax.dynamic_slice_in_dim(heads, (1 - shard) * half_heads, half_heads, 1)
    hidden = x_in + matrix_product(own_heads, w_out) + matrix_product(other_heads, out_other)
    normed2, inv_ffn = norm_forward(hidden, g_ffn)
    normed_ffn = normed2.astype(jnp.bfloat16)
    router = jax.nn.softmax(outer_product(normed_ffn, wrout), axis=-1)

    (all_normed,) = gather_rows([normed_ffn], True, 2)
    w_query, all_normed = lax.optimization_barrier((w_query, all_normed))
    query_own, query_other = by_cores(w_query)
    (
        out_part,
        d_part,
        ex_rows,
        ex_grads,
        scaled_act,
        d_pre_gate,
        d_pre_up,
        g_shared_in,
        g_shared_out,
    ) = expert_phase(
        all_normed,
        all_grads.reshape(blocks, rows, -1),
        router_rows,
        expert_gate[0].T,
        expert_up[0].T,
        expert_down[0],
        shared_in,
        shared_out,
        capacity,
    )
    g_down = inner(scaled_act, ex_grads)
    g_gate = inner(d_pre_gate, ex_rows).T
    g_up = inner(d_pre_up, ex_rows).T
    (d_back,) = scatter_rows(d_part, True, 3)
    out_part, d_back = lax.optimization_barrier((out_part, d_back))
    out_sum = lax.psum_scatter(
        out_part.reshape(blocks * rows, MODEL_WIDTH),
        ("fsdp", "expert"),
        scatter_dimension=0,
        tiled=True,
    )
    spare = router_rows.shape[0]
    d_hidden, d_attn, d_heads, g_router, g_ffn_grad = hidden_back(
        d_back,
        jnp.pad(router, ((0, 0), (0, spare - experts))),
        normed_ffn,
        hidden,
        g_ffn[None],
        router_rows,
        cotangent[0],
        w_out,
        out_other,
    )
    g_router = g_router[:experts]
    d_head = exchange(d_heads, 4).reshape(seq_len, VALUE_UNITS)
    out_grad_part = inner(heads, d_attn).astype(jnp.bfloat16)
    d_query_full, d_pairs, d_keys = attend_back(
        query, key, value, d_head, head_sum, logs, expand_head, cosines, sines
    )
    g_expand_head = inner(latent_rows, d_pairs)
    g_query_head = inner(d_query_full, seq_normed).astype(jnp.bfloat16)
    g_expand_head = g_expand_head.astype(jnp.bfloat16)

    def half_of(whole, which, axis):
        size = whole.shape[axis] // shards
        return lax.dynamic_slice_in_dim(whole, which * size, size, axis)

    own_d_query, d_sums, own_out, other_query, other_expand = exchange_and_sums(
        d_query_full.reshape(experts, rows, head_units),
        d_keys.reshape(experts, rows, -1),
        out_grad_part.reshape(blocks, -1, MODEL_WIDTH),
        [half_of(g_query_head, 1 - shard, 1), half_of(g_expand_head, 1 - shard, 0)],
        5,
    )
    def summed(own, other):
        return (own.astype(jnp.float32) + other.astype(jnp.float32)).astype(jnp.bfloat16)

    own_query = summed(half_of(g_query_head, shard, 1), other_query)
    own_expand = summed(half_of(g_expand_head, shard, 0), other_expand)
    own_out = own_out.astype(jnp.bfloat16)
    own_cosines = lax.dynamic_slice_in_dim(cosines, position * rows, rows, 0)
    own_sines = lax.dynamic_slice_in_dim(sines, position * rows, rows, 0)
    d_tokens, g_latent, g_attn_grad, g_lat_grad = input_back(
        own_d_query,
        d_sums,
        query_own,
        query_other,
        tokens[0],
        g_attn[None],
        w_latent,
        g_lat[None],
        own_cosines,
        own_sines,
        d_hidden,
    )

    half = MODEL_WIDTH // blocks
    cols = lax.all_to_all(
        g_shared_in.reshape(blocks, half, 2 * lanes),
        ("expert", "fsdp"),
        split_axis=0,
        concat_axis=0,
        tiled=True,
    )
    cols = cols.transpose(1, 0, 2).astype(jnp.float32)
    r_sgate = cols[:, :, :units].reshape(half, blocks * units)
    r_sup = cols[:, :, lanes : lanes + units].reshape(half, blocks * units)
    g_sdown = g_shared_out[:units]
    model_half = MODEL_WIDTH // shards
    small_rows = jnp.concatenate([g_latent, g_router, g_attn_grad, g_ffn_grad], axis=0)
    used = small_rows.shape[0]
    share = 2 * 32 * (-(-(used + 1) // (2 * 32 * experts)))

    def rows_for(which):
        here = small_rows[:, which * model_half : (which + 1) * model_half]
        lat = jnp.pad(
            g_lat_grad[0, which * lat_half : (which + 1) * lat_half], (0, model_half - lat_half)
        )
        full = jnp.concatenate([here, lat[None]], axis=0).astype(jnp.bfloat16)
        full = jnp.pad(full, ((0, experts * share - used - 1), (0, 0)))
        return full.reshape(experts, share, model_half)

    small_part = jnp.concatenate([rows_for(which) for which in range(shards)], axis=0)
    r_query, r_expand, r_out, small_sum = gather_and_scatter(
        [own_query, own_expand, own_out], small_part, 6
    )
    hidden, small_sum = lax.optimization_barrier((hidden, small_sum))
    output = hidden + out_sum.astype(jnp.float32)
    (small_all,) = gather_rows([small_sum.astype(jnp.bfloat16)], False, 7)
    r_query, r_expand, r_out = finish(r_query, r_expand, r_out)
    small_all = small_all.reshape(experts * share, model_half).astype(jnp.float32)
    return (
        output.astype(jnp.bfloat16)[None],
        d_tokens[None],
        small_all[feature_width + experts],
        r_query,
        small_all[:feature_width].T,
        small_all[feature_width + experts + 2, :lat_half],
        r_expand,
        r_out,
        small_all[feature_width + experts + 1],
        small_all[feature_width : feature_width + experts].T,
        r_sgate,
        r_sup,
        g_sdown,
        g_gate[None],
        g_up[None],
        g_down[None],
    )


def solution(mesh):
    shape = (mesh.shape["expert"], mesh.shape["fsdp"])
    split = shape == (LINE * SQUARE * CORES, SQUARE) and shape[0] == HEAD_COUNT
    return jax.shard_map(
        split_body if split else body,
        mesh=mesh,
        in_specs=(
            P("fsdp", "expert", None),
            P("fsdp", "expert", None),
            P("fsdp", "expert", None),
            P("fsdp"),
            P("fsdp", None),
            P("fsdp", None),
            P("fsdp"),
            P("fsdp", None),
            P("fsdp", None),
            P("fsdp"),
            P("fsdp", None),
            P(("expert", "fsdp"), None),
            P(("expert", "fsdp"), None),
            P(("expert", "fsdp"), None),
            P("expert", None, "fsdp"),
            P("expert", None, "fsdp"),
            P("expert", "fsdp", None),
        ),
        out_specs=(
            P("fsdp", "expert", None),
            P("fsdp", "expert", None),
            P("fsdp"),
            P("fsdp", None),
            P("fsdp", None),
            P("fsdp"),
            P("fsdp", None),
            P("fsdp", None),
            P("fsdp"),
            P("fsdp", None),
            P(("expert", "fsdp"), None),
            P(("expert", "fsdp"), None),
            P(("expert", "fsdp"), None),
            P("expert", None, "fsdp"),
            P("expert", None, "fsdp"),
            P("expert", "fsdp", None),
        ),
        check_vma=False,
    )
```

```python
import functools

import jax
import jax.numpy as jnp
import numpy as np
from jax import lax
from jax.experimental import pallas as pl
from jax.experimental.pallas import tpu as pltpu
from jax.sharding import PartitionSpec as P

MODEL_WIDTH = 2048
HEAD_COUNT = 16
PLAIN_UNITS = 128
ROTARY_UNITS = 64
VALUE_UNITS = 128
LATENT_WIDTH = 512
TOPK = 6


EPS = 1e-06


def matrix_product(left, right):
    return jnp.dot(left, right, preferred_element_type=jnp.float32)


def inner(left, right):
    return lax.dot_general(
        left, right, (((0,), (0,)), ((), ())), preferred_element_type=jnp.float32
    )


def outer_product(left, right):
    return lax.dot_general(
        left, right, (((1,), (1,)), ((), ())), preferred_element_type=jnp.float32
    )


def norm_forward(value, gain):
    inverse = lax.rsqrt(jnp.mean(value * value, axis=-1, keepdims=True) + EPS)
    return (value * inverse * gain, inverse)


def norm_backward(value, inverse, gain, grad):
    unit = value * inverse
    scaled = grad * gain
    d_value = inverse * (scaled - unit * jnp.mean(scaled * unit, axis=-1, keepdims=True))
    return (d_value, jnp.sum(grad * unit, axis=0))


def rope_tables(positions):
    half = ROTARY_UNITS // 2
    freqs = 10000.0 ** (-jnp.arange(half, dtype=jnp.float32) * (2.0 / ROTARY_UNITS))
    angles = positions.astype(jnp.float32)[:, None] * freqs[None, :]
    return (jnp.cos(angles), jnp.sin(angles))


def apply_rotary(value, cosine_table, sine_table):
    half = ROTARY_UNITS // 2
    first = value[..., :half]
    second = value[..., half:]
    return jnp.concatenate(
        [first * cosine_table - second * sine_table, first * sine_table + second * cosine_table],
        axis=-1,
    )


def reverse_rotary(grad, cosine_table, sine_table):
    half = ROTARY_UNITS // 2
    first = grad[..., :half]
    second = grad[..., half:]
    return jnp.concatenate(
        [first * cosine_table + second * sine_table, second * cosine_table - first * sine_table],
        axis=-1,
    )


def silu_parts(value):
    sigma = jax.nn.sigmoid(value)
    return (value * sigma, sigma * (1.0 + value * (1.0 - sigma)))


def body(
    tokens,
    routes,
    cotangent,
    attn_gain,
    w_query,
    latent_weight,
    latent_norm_gain,
    expand_weight,
    w_out,
    ffn_gain,
    w_router,
    shared_gate,
    shared_up,
    shared_down,
    expert_gate,
    expert_up,
    expert_down,
):
    device_local = tokens.shape[1]
    experts = lax.axis_size("expert")
    shards = lax.axis_size("fsdp")
    position = lax.axis_index("expert")
    capacity = shards * (
        (device_local * TOPK * 4 + experts * 3 * shards - 1) // (experts * 3 * shards)
    )
    seq_len = device_local * experts
    feature_width = LATENT_WIDTH + ROTARY_UNITS
    scale = (PLAIN_UNITS + ROTARY_UNITS) ** (-0.5)
    attention_gain_grad, wq, wlat, g_lat, expand_matrix, wout, g_ffn, wrout = (
        lax.all_gather(attn_gain, "fsdp", axis=0, tiled=True),
        lax.all_gather(w_query, "fsdp", axis=0, tiled=True),
        lax.all_gather(latent_weight, "fsdp", axis=0, tiled=True),
        lax.all_gather(latent_norm_gain, "fsdp", axis=0, tiled=True),
        lax.all_gather(expand_weight, "fsdp", axis=0, tiled=True),
        lax.all_gather(w_out, "fsdp", axis=0, tiled=True),
        lax.all_gather(ffn_gain, "fsdp", axis=0, tiled=True),
        lax.all_gather(w_router, "fsdp", axis=0, tiled=True),
    )
    sgate, sup, sdown = (
        lax.all_gather(shared_gate, ("expert", "fsdp"), axis=0, tiled=True),
        lax.all_gather(shared_up, ("expert", "fsdp"), axis=0, tiled=True),
        lax.all_gather(shared_down, ("expert", "fsdp"), axis=0, tiled=True),
    )
    attention_gain_grad = attention_gain_grad.astype(jnp.float32)
    g_lat = g_lat.astype(jnp.float32)
    g_ffn = g_ffn.astype(jnp.float32)
    x_in = tokens[0].astype(jnp.float32)
    grad_out = cotangent[0].astype(jnp.float32)
    positions = position * device_local + jnp.arange(device_local, dtype=jnp.int32)
    cosine_table, sine_table = rope_tables(positions)
    normed, inv_attn = norm_forward(x_in, attention_gain_grad)
    normed_in = normed.astype(jnp.bfloat16)
    query_full = matrix_product(normed_in, wq).reshape(
        device_local, HEAD_COUNT, PLAIN_UNITS + ROTARY_UNITS
    )
    query_nope = query_full[:, :, :PLAIN_UNITS].astype(jnp.bfloat16)
    expanded_latent = expand_matrix.reshape(LATENT_WIDTH, HEAD_COUNT, PLAIN_UNITS + VALUE_UNITS)
    key_part = expanded_latent[:, :, :PLAIN_UNITS]
    value_part = expanded_latent[:, :, PLAIN_UNITS:]
    query_latent = jnp.einsum(
        "thd,chd->thc", query_nope, key_part, preferred_element_type=jnp.float32
    )
    query_rope = apply_rotary(
        query_full[:, :, PLAIN_UNITS:], cosine_table[:, None, :], sine_table[:, None, :]
    )
    token_rows = device_local * HEAD_COUNT
    query = (
        jnp.concatenate([query_latent, query_rope], axis=-1)
        .astype(jnp.bfloat16)
        .reshape(token_rows, feature_width)
    )
    latent_complete = matrix_product(normed_in, wlat)
    packed_rows = latent_complete[:, :LATENT_WIDTH]
    latent_state, inv_lat = norm_forward(packed_rows, g_lat)
    rotary_key = apply_rotary(latent_complete[:, LATENT_WIDTH:], cosine_table, sine_table)
    key = jnp.concatenate([latent_state, rotary_key], axis=-1).astype(jnp.bfloat16)
    keys_all = lax.all_gather(key, "expert", axis=0, tiled=True)
    block = min(512, seq_len)
    token_tally = (position * device_local + device_local + block - 1) // block
    q_pos = position * device_local + jnp.arange(token_rows, dtype=jnp.int32) // HEAD_COUNT

    def scores_of(index):
        key_rows = lax.dynamic_slice_in_dim(keys_all, index * block, block, 0)
        raw = outer_product(query, key_rows)
        k_pos = index * block + jnp.arange(block, dtype=jnp.int32)
        valid = k_pos[None, :] <= q_pos[:, None]
        return (jnp.where(valid, raw * scale, -1e30), key_rows)

    def stats_step(index, carry):
        top, total = carry
        scores, unused = scores_of(index)
        new_top = jnp.maximum(top, jnp.max(scores, axis=1))
        total = total * jnp.exp(top - new_top) + jnp.sum(jnp.exp(scores - new_top[:, None]), axis=1)
        return (new_top, total)

    top, total = lax.fori_loop(
        0,
        token_tally,
        stats_step,
        (jnp.full((token_rows,), -1e30, jnp.float32), jnp.zeros((token_rows,), jnp.float32)),
    )
    log_total = top + jnp.log(total)

    def mixing_update(index, running_total):
        scores, key_rows = scores_of(index)
        weight_arrays = jnp.exp(scores - log_total[:, None]).astype(jnp.bfloat16)
        return running_total + matrix_product(weight_arrays, key_rows[:, :LATENT_WIDTH])

    mixed_output_sum = lax.fori_loop(
        0, token_tally, mixing_update, jnp.zeros((token_rows, LATENT_WIDTH), jnp.float32)
    )
    mixed_output = mixed_output_sum.astype(jnp.bfloat16).reshape(
        device_local, HEAD_COUNT, LATENT_WIDTH
    )
    heads = jnp.einsum("thc,chv->thv", mixed_output, value_part, preferred_element_type=jnp.float32)
    heads = heads.reshape(device_local, HEAD_COUNT * VALUE_UNITS).astype(jnp.bfloat16)
    hidden = x_in + matrix_product(heads, wout)
    normed2, inv_ffn = norm_forward(hidden, g_ffn)
    normed_ffn = normed2.astype(jnp.bfloat16)
    logits = matrix_product(normed_ffn, wrout)
    router = jax.nn.softmax(logits, axis=-1)
    own_routes = routes[0]
    names = jnp.arange(experts, dtype=jnp.int32)
    chosen = (own_routes[:, :, None] == names[None, None, :]).astype(jnp.float32)
    gates = jnp.sum(chosen * router[:, None, :], axis=-1)
    hits = (own_routes.reshape(device_local * TOPK)[:, None] == names[None, :]).astype(jnp.int32)
    slot = jnp.sum((jnp.cumsum(hits, axis=0) - hits) * hits, axis=1)
    place = own_routes.reshape(device_local * TOPK) * capacity + slot
    token_of = jnp.arange(device_local * TOPK, dtype=jnp.int32) // TOPK
    table = jnp.full((experts * capacity,), device_local, jnp.int32).at[place].set(token_of)
    padded = jnp.concatenate([normed_ffn, jnp.zeros((1, MODEL_WIDTH), jnp.bfloat16)], axis=0)
    buffer = padded[table].reshape(experts, capacity, MODEL_WIDTH)
    w_g, w_u, w_d = (expert_gate[0], expert_up[0], expert_down[0])

    def spread(values):
        return jnp.broadcast_to(values[:, None], (experts, shards, capacity, MODEL_WIDTH)).reshape(
            experts * shards, capacity, MODEL_WIDTH
        )

    def collect(back):
        return jnp.sum(back.reshape(experts, shards, capacity, MODEL_WIDTH), axis=1).reshape(
            experts * capacity, MODEL_WIDTH
        )

    received = lax.all_to_all(
        spread(buffer), ("expert", "fsdp"), split_axis=0, concat_axis=0, tiled=True
    )
    ex_rows = received.reshape(-1, MODEL_WIDTH)
    pre_gate = matrix_product(ex_rows, w_g)
    pre_up = matrix_product(ex_rows, w_u)
    act_gate, slope = silu_parts(pre_gate)
    ex_act = (act_gate * pre_up).astype(jnp.bfloat16)
    ex_out = matrix_product(ex_act, w_d).reshape(received.shape)
    returned = lax.all_to_all(
        ex_out.astype(jnp.bfloat16), ("expert", "fsdp"), split_axis=0, concat_axis=0, tiled=True
    ).astype(ex_out.dtype)
    results = collect(returned)
    picked = results[place].reshape(device_local, TOPK, MODEL_WIDTH)
    routed = jnp.sum(gates[:, :, None] * picked, axis=1)
    sh_gate = matrix_product(normed_ffn, sgate)
    sh_up = matrix_product(normed_ffn, sup)
    sh_silu, sh_slope = silu_parts(sh_gate)
    sh_act = (sh_silu * sh_up).astype(jnp.bfloat16)
    shared = matrix_product(sh_act, sdown)
    output = hidden + routed + shared
    d_shared = grad_out.astype(jnp.bfloat16)
    shared_down_gradient = inner(sh_act, d_shared)
    d_sh_act = outer_product(d_shared, sdown)
    d_sh_gate = (d_sh_act * sh_up * sh_slope).astype(jnp.bfloat16)
    d_sh_up = (d_sh_act * sh_silu).astype(jnp.bfloat16)
    shared_gate_gradient = inner(normed_ffn, d_sh_gate)
    shared_up_gradient = inner(normed_ffn, d_sh_up)
    d_normed_ffn = outer_product(d_sh_gate, sgate) + outer_product(d_sh_up, sup)
    d_picked = (
        (gates[:, :, None] * grad_out[:, None, :])
        .astype(jnp.bfloat16)
        .reshape(device_local * TOPK, MODEL_WIDTH)
    )
    d_gates = jnp.sum(picked * grad_out[:, None, :], axis=2)
    d_buffer = (
        jnp.zeros((experts * capacity, MODEL_WIDTH), jnp.bfloat16)
        .at[place]
        .set(d_picked)
        .reshape(experts, capacity, MODEL_WIDTH)
    )
    d_received = lax.all_to_all(
        spread(d_buffer), ("expert", "fsdp"), split_axis=0, concat_axis=0, tiled=True
    )
    d_rows = d_received.reshape(-1, MODEL_WIDTH)
    d_act = outer_product(d_rows, w_d)
    g_down = inner(ex_act, d_rows)
    d_pre_gate = (d_act * pre_up * slope).astype(jnp.bfloat16)
    d_pre_up = (d_act * act_gate).astype(jnp.bfloat16)
    g_gate = inner(ex_rows, d_pre_gate)
    g_up = inner(ex_rows, d_pre_up)
    d_ex_rows = (outer_product(d_pre_gate, w_g) + outer_product(d_pre_up, w_u)).reshape(
        received.shape
    )
    d_returned = lax.all_to_all(
        d_ex_rows.astype(jnp.bfloat16), ("expert", "fsdp"), split_axis=0, concat_axis=0, tiled=True
    ).astype(d_ex_rows.dtype)
    d_results = collect(d_returned)
    d_normed_ffn = d_normed_ffn + jnp.sum(
        d_results[place].reshape(device_local, TOPK, MODEL_WIDTH), axis=1
    )
    d_router = jnp.sum(chosen * d_gates[:, :, None], axis=1)
    d_logits = (router * (d_router - jnp.sum(router * d_router, axis=1, keepdims=True))).astype(
        jnp.bfloat16
    )
    router_weight_gradient = inner(normed_ffn, d_logits)
    d_normed_ffn = d_normed_ffn + outer_product(d_logits, wrout)
    d_hidden_norm, g_ffn_grad = norm_backward(hidden, inv_ffn, g_ffn, d_normed_ffn)
    d_hidden = grad_out + d_hidden_norm
    d_attn = d_hidden.astype(jnp.bfloat16)
    output_weight_gradient = inner(heads, d_attn)
    d_heads = (
        outer_product(d_attn, wout)
        .astype(jnp.bfloat16)
        .reshape(device_local, HEAD_COUNT, VALUE_UNITS)
    )
    value_weight_gradient = jnp.einsum(
        "thc,thv->chv", mixed_output, d_heads, preferred_element_type=jnp.float32
    )
    mixed_gradient = jnp.einsum(
        "thv,chv->thc", d_heads, value_part, preferred_element_type=jnp.float32
    )
    mixed_gradient = mixed_gradient.astype(jnp.bfloat16).reshape(token_rows, LATENT_WIDTH)
    delta = jnp.sum(mixed_gradient.astype(jnp.float32) * mixed_output_sum, axis=1)

    def back_step(index, carry):
        d_query_acc, d_keys_acc = carry
        scores, key_rows = scores_of(index)
        weight_arrays = jnp.exp(scores - log_total[:, None])
        weight_gradients = outer_product(mixed_gradient, key_rows[:, :LATENT_WIDTH])
        d_scores = (weight_arrays * (weight_gradients - delta[:, None]) * scale).astype(
            jnp.bfloat16
        )
        d_query_acc = d_query_acc + matrix_product(d_scores, key_rows)
        d_values = inner(weight_arrays.astype(jnp.bfloat16), mixed_gradient)
        d_block = inner(d_scores, query) + jnp.concatenate(
            [d_values, jnp.zeros((block, ROTARY_UNITS), jnp.float32)], axis=1
        )
        previous = lax.dynamic_slice_in_dim(d_keys_acc, index * block, block, 0)
        return (
            d_query_acc,
            lax.dynamic_update_slice_in_dim(d_keys_acc, previous + d_block, index * block, 0),
        )

    d_query, d_keys = lax.fori_loop(
        0,
        token_tally,
        back_step,
        (
            jnp.zeros((token_rows, feature_width), jnp.float32),
            jnp.zeros((seq_len, feature_width), jnp.float32),
        ),
    )
    key_gradient = lax.psum_scatter(
        d_keys.astype(jnp.bfloat16), "expert", scatter_dimension=0, tiled=True
    )
    query_up_gradient = d_query.astype(jnp.bfloat16).reshape(
        device_local, HEAD_COUNT, feature_width
    )
    query_latent_gradient = query_up_gradient[:, :, :LATENT_WIDTH]
    key_weight_gradient = jnp.einsum(
        "thc,thd->chd", query_latent_gradient, query_nope, preferred_element_type=jnp.float32
    )
    d_q_nope = jnp.einsum(
        "thc,chd->thd", query_latent_gradient, key_part, preferred_element_type=jnp.float32
    )
    d_q_rope = reverse_rotary(
        query_up_gradient[:, :, LATENT_WIDTH:].astype(jnp.float32),
        cosine_table[:, None, :],
        sine_table[:, None, :],
    )
    d_query_full = (
        jnp.concatenate([d_q_nope, d_q_rope], axis=-1)
        .astype(jnp.bfloat16)
        .reshape(device_local, HEAD_COUNT * (PLAIN_UNITS + ROTARY_UNITS))
    )
    query_weight_gradient = inner(normed_in, d_query_full)
    d_normed_in = outer_product(d_query_full, wq)
    latent_gradient = key_gradient[:, :LATENT_WIDTH].astype(jnp.float32)
    rotary_key_gradient = reverse_rotary(
        key_gradient[:, LATENT_WIDTH:].astype(jnp.float32), cosine_table, sine_table
    )
    d_compact, g_lat_grad = norm_backward(packed_rows, inv_lat, g_lat, latent_gradient)
    d_latent_full = jnp.concatenate([d_compact, rotary_key_gradient], axis=-1).astype(jnp.bfloat16)
    latent_weight_gradient = inner(normed_in, d_latent_full)
    d_normed_in = d_normed_in + outer_product(d_latent_full, wlat)
    d_norm_in, g_attn_grad = norm_backward(x_in, inv_attn, attention_gain_grad, d_normed_in)
    d_tokens = (d_hidden + d_norm_in).astype(jnp.bfloat16)
    expand_weight_gradient = jnp.concatenate(
        [key_weight_gradient, value_weight_gradient], axis=-1
    ).reshape(LATENT_WIDTH, HEAD_COUNT * (PLAIN_UNITS + VALUE_UNITS))
    r_sgate, r_sup, r_sdown = (
        lax.psum_scatter(shared_gate_gradient, ("expert", "fsdp"), scatter_dimension=0, tiled=True),
        lax.psum_scatter(shared_up_gradient, ("expert", "fsdp"), scatter_dimension=0, tiled=True),
        lax.psum_scatter(shared_down_gradient, ("expert", "fsdp"), scatter_dimension=0, tiled=True),
    )
    r_attn, r_query, r_latent, r_lgain, r_expand, r_out, r_fgain, r_router = (
        lax.psum_scatter(
            g_attn_grad.astype(jnp.bfloat16), "fsdp", scatter_dimension=0, tiled=True
        ).astype(jnp.float32),
        lax.psum_scatter(
            query_weight_gradient.astype(jnp.bfloat16), "fsdp", scatter_dimension=0, tiled=True
        ).astype(jnp.float32),
        lax.psum_scatter(
            latent_weight_gradient.astype(jnp.bfloat16), "fsdp", scatter_dimension=0, tiled=True
        ).astype(jnp.float32),
        lax.psum_scatter(
            g_lat_grad.astype(jnp.bfloat16), "fsdp", scatter_dimension=0, tiled=True
        ).astype(jnp.float32),
        lax.psum_scatter(
            expand_weight_gradient.astype(jnp.bfloat16), "fsdp", scatter_dimension=0, tiled=True
        ).astype(jnp.float32),
        lax.psum_scatter(
            output_weight_gradient.astype(jnp.bfloat16), "fsdp", scatter_dimension=0, tiled=True
        ).astype(jnp.float32),
        lax.psum_scatter(
            g_ffn_grad.astype(jnp.bfloat16), "fsdp", scatter_dimension=0, tiled=True
        ).astype(jnp.float32),
        lax.psum_scatter(
            router_weight_gradient.astype(jnp.bfloat16), "fsdp", scatter_dimension=0, tiled=True
        ).astype(jnp.float32),
    )
    r_attn, r_query, r_latent, r_lgain, r_expand, r_out, r_fgain, r_router = (
        lax.psum(r_attn.astype(jnp.bfloat16), "expert").astype(jnp.float32),
        lax.psum(r_query.astype(jnp.bfloat16), "expert").astype(jnp.float32),
        lax.psum(r_latent.astype(jnp.bfloat16), "expert").astype(jnp.float32),
        lax.psum(r_lgain.astype(jnp.bfloat16), "expert").astype(jnp.float32),
        lax.psum(r_expand.astype(jnp.bfloat16), "expert").astype(jnp.float32),
        lax.psum(r_out.astype(jnp.bfloat16), "expert").astype(jnp.float32),
        lax.psum(r_fgain.astype(jnp.bfloat16), "expert").astype(jnp.float32),
        lax.psum(r_router.astype(jnp.bfloat16), "expert").astype(jnp.float32),
    )
    return (
        output.astype(jnp.bfloat16)[None],
        d_tokens[None],
        r_attn,
        r_query,
        r_latent,
        r_lgain,
        r_expand,
        r_out,
        r_fgain,
        r_router,
        r_sgate,
        r_sup,
        r_sdown,
        g_gate[None],
        g_up[None],
        g_down[None],
    )


LINE = 4
SQUARE = 2
CORES = 2
MESH = pl.DeviceIdType.MESH
VMEM_LIMIT = 56 * 1024 * 1024


class Place:
    def __init__(self):
        index = lax.axis_index("expert")
        self.y = lax.axis_index("fsdp")
        self.c = lax.rem(index, CORES)
        self.b = lax.rem(lax.div(index, CORES), SQUARE)
        self.a = lax.div(index, CORES * SQUARE)

    def device(self, da=0, db=0, dc=0, dy=0):
        b = 1 - self.b if db else self.b
        c = 1 - self.c if dc else self.c
        y = 1 - self.y if dy else self.y
        return (((self.a + da) * SQUARE + b) * CORES + c, y)

    def block(self, full, a, db=0, dc=0, dy=0):
        b = 1 - self.b if db else self.b
        c = 1 - self.c if dc else self.c
        y = 1 - self.y if dy else self.y
        flat = (a * SQUARE + b) * CORES + c
        return y * (LINE * SQUARE * CORES) + flat if full else flat

    def greet(self, with_y):
        barrier = pltpu.get_barrier_semaphore()
        near = [dict(db=1), dict(dc=1)] + ([dict(dy=1)] if with_y else [])
        for step in near:
            pl.semaphore_signal(barrier, inc=1, device_id=self.device(**step), device_id_type=MESH)

        @pl.when(self.a > 0)
        def _():
            pl.semaphore_signal(barrier, inc=1, device_id=self.device(da=-1), device_id_type=MESH)

        @pl.when(self.a < LINE - 1)
        def _():
            pl.semaphore_signal(barrier, inc=1, device_id=self.device(da=1), device_id_type=MESH)

        ends = jnp.logical_or(self.a == 0, self.a == LINE - 1).astype(jnp.int32)
        pl.semaphore_wait(barrier, len(near) + 2 - ends)


class Sender:
    def __init__(self, place, sems):
        self.place, self.sems, self.pending = place, sems, []

    def send(self, src, dst, recv_sem, step, cond=None):
        sem = self.sems.at[len(self.pending)]

        def make():
            return pltpu.make_async_remote_copy(
                src_ref=src,
                dst_ref=dst,
                send_sem=sem,
                recv_sem=recv_sem,
                device_id=self.place.device(**step),
                device_id_type=MESH,
            )

        def start():
            make().start()

        guarded(cond, start)
        self.pending.append((cond, lambda: make().wait_send()))

    def arrived(self, dst, recv_sem):
        pltpu.make_async_remote_copy(
            src_ref=dst,
            dst_ref=dst,
            send_sem=self.sems.at[0],
            recv_sem=recv_sem,
            device_id=self.place.device(dc=1),
            device_id_type=MESH,
        ).wait_recv()

    def finish(self):
        for cond, wait in self.pending:
            guarded(cond, wait)


def guarded(cond, action):
    if cond is None:
        action()
    else:
        pl.when(cond)(action)


def both(first, second):
    if first is None or second is None:
        return second if first is None else first
    return jnp.logical_and(first, second)


def gather_ticks(place, sender, full, gated, ins, outs, local_sems, recv_sems):
    a = place.a
    count = len(ins)

    def own_copy(at):
        return pltpu.make_async_copy(
            ins[at], outs[at].at[place.block(full, a)], local_sems.at[at]
        )

    def chunk(at, block, half):
        size = ins[at].shape[0] // 2
        return outs[at].at[block, pl.ds(half * size, size)]

    def sem_of(at, block, half):
        return recv_sems.at[at, block * 2 + half]

    def forward(at, block, half, src, step, cond=None):
        sender.send(src, chunk(at, block, half), sem_of(at, block, half), step, cond)

    def receive(at, block, half, cond):
        guarded(cond, lambda: sender.arrived(chunk(at, block, half), sem_of(at, block, half)))

    def held_by(at, delta, cond):
        if at not in gated:
            return cond
        return both(cond, lax.div(a + delta, LINE // 2) == place.y)

    def from_line(delta, always):
        for half in range(2):
            for at in range(count):
                block = place.block(full, a + delta)
                cond = held_by(at, delta, always)
                size = ins[at].shape[0] // 2
                if delta == 0:
                    src = ins[at].at[pl.ds(half * size, size)]
                else:
                    receive(at, block, half, cond)
                    src = chunk(at, block, half)
                if delta <= 0:
                    forward(at, block, half, src, dict(da=1), both(cond, a < LINE - 1))
                if delta >= 0:
                    forward(at, block, half, src, dict(da=-1), both(cond, a > 0))
                forward(at, block, half, src, dict(db=1), cond)
                if full:
                    forward(at, block, half, src, dict(dy=1), cond)
                forward(at, block, half, src, dict(dc=1), cond)

    def from_side(delta, always):
        for half in range(2):
            for at in range(count):
                cond = held_by(at, delta, always)
                block = place.block(full, a + delta, db=1)
                receive(at, block, half, cond)
                if full and half == 0:
                    forward(at, block, half, chunk(at, block, half), dict(dy=1), cond)
                forward(at, block, half, chunk(at, block, half), dict(dc=1), cond)
                if full:
                    block = place.block(full, a + delta, dy=1)
                    receive(at, block, half, cond)
                    if half == 1:
                        forward(at, block, half, chunk(at, block, half), dict(db=1), cond)
                    forward(at, block, half, chunk(at, block, half), dict(dc=1), cond)

    def from_corner(delta, always):
        for half in range(2):
            for at in range(count):
                cond = held_by(at, delta, always)
                block = place.block(True, a + delta, db=1, dy=1)
                receive(at, block, half, cond)
                forward(at, block, half, chunk(at, block, half), dict(dc=1), cond)

    def from_sibling(delta, always):
        for half in range(2):
            for at in range(count):
                cond = held_by(at, delta, always)
                for db in range(2):
                    for dy in range(2 if full else 1):
                        receive(at, place.block(full, a + delta, db=db, dc=1, dy=dy), half, cond)

    rounds = [[(0, None)]]
    for s in range(1, LINE):
        rounds.append([(-s, a >= s), (s, a + s < LINE)])
    stages = [from_line, from_side] + ([from_corner] if full else []) + [from_sibling]

    def tick(number):
        if number == 0:
            for at in range(count):
                own_copy(at).start()
        for level, stage in enumerate(stages):
            if 0 <= number - level < len(rounds):
                for delta, cond in rounds[number - level]:
                    stage(delta, cond)
        if number == len(rounds) + len(stages) - 2:
            for at in range(count):
                own_copy(at).wait()

    return [functools.partial(tick, number) for number in range(len(rounds) + len(stages) - 1)]


def send_pairs(sender, ins, outs, sems):
    for at, (src, dst) in enumerate(zip(ins, outs)):
        sender.send(src, dst, sems.at[at], dict(dy=1))


def take_pairs(sender, outs, sems):
    for at, dst in enumerate(outs):
        sender.arrived(dst, sems.at[at])


def gather_kernel(full, count, pairs, halved, gated, *refs):
    arrays = count + pairs + halved
    ins, outs = refs[:arrays], refs[arrays : 2 * arrays]
    local_sems, send_sems, recv_sems, pair_sems, half_sems = refs[2 * arrays :]
    place = Place()
    sender = Sender(place, send_sems)
    place.greet(full or pairs + halved > 0)
    shared = range(count + pairs, arrays)

    def part(ref, core):
        size = ref.shape[0] // CORES
        return ref.at[pl.ds(pl.multiple_of(core * size, 16), size)]

    send_pairs(sender, ins[count : count + pairs], outs[count : count + pairs], pair_sems)
    for at in shared:
        sender.send(
            part(ins[at], place.c), part(outs[at], place.c), half_sems.at[at - count - pairs, 0],
            dict(dy=1),
        )
    ticks = gather_ticks(
        place, sender, full, gated, ins[:count], outs[:count], local_sems, recv_sems
    )
    for number, tick in enumerate(ticks):
        if number == len(ticks) - 1:
            for at in shared:
                here = part(outs[at], place.c)
                sender.arrived(here, half_sems.at[at - count - pairs, 0])
                sender.send(here, here, half_sems.at[at - count - pairs, 1], dict(dc=1))
        tick()
    for at in shared:
        sender.arrived(part(outs[at], 1 - place.c), half_sems.at[at - count - pairs, 1])
    take_pairs(sender, outs[count : count + pairs], pair_sems)
    sender.finish()


def gather_rows(arrays, full, collective_id, swapped=(), halved=(), gated=()):
    blocks = LINE * SQUARE * CORES * (SQUARE if full else 1)
    count, pairs, shared = len(arrays), len(swapped), len(halved)
    lines = 2 * LINE - 1
    sends = pairs + 2 * shared + count * lines * 2 * (9 if full else 5)
    moved = sum(blocks * 2 * x.size * x.dtype.itemsize for x in arrays)
    return pl.pallas_call(
        functools.partial(gather_kernel, full, count, pairs, shared, gated),
        out_shape=[jax.ShapeDtypeStruct((blocks,) + x.shape, x.dtype) for x in arrays]
        + [jax.ShapeDtypeStruct(x.shape, x.dtype) for x in (*swapped, *halved)],
        in_specs=[pl.BlockSpec(memory_space=pl.ANY)] * (count + pairs + shared),
        out_specs=[pl.BlockSpec(memory_space=pl.ANY)] * (count + pairs + shared),
        scratch_shapes=[
            pltpu.SemaphoreType.DMA((count,)),
            pltpu.SemaphoreType.DMA((sends,)),
            pltpu.SemaphoreType.DMA((count, blocks * 2)),
            pltpu.SemaphoreType.DMA((max(pairs, 1),)),
            pltpu.SemaphoreType.DMA((max(shared, 1), 2)),
        ],
        compiler_params=pltpu.CompilerParams(collective_id=collective_id, has_side_effects=True),
        cost_estimate=pl.CostEstimate(flops=0, bytes_accessed=6 * moved, transcendentals=0),
    )(*arrays, *swapped, *halved)


def add_rows(target, sources, size):
    def step(at, carry):
        rows = pl.ds(pl.multiple_of(at * 16, 16), 16)
        total = sources[0][rows, :].astype(jnp.float32)
        for source in sources[1:]:
            total = total + source[rows, :].astype(jnp.float32)
        target[rows, :] = total.astype(target.dtype)
        return carry

    lax.fori_loop(0, size // 16, step, 0)


def scatter_ticks(place, sender, full, part, out, scratch):
    mine, got, side, up, down, load_sems, recv_sems = scratch
    a = place.a
    kinds = 4 if full else 2
    size = part.shape[1]
    half = size // 2
    order = [LINE - 1, 0, LINE - 2, 1]
    walk = (3, 1, 2, 0) if full else (1, 0)

    def sem_of(group, target, kind):
        return recv_sems.at[group, target * 4 + kind]

    def load(target, kind):
        block = place.block(full, target, db=kind % 2, dy=kind // 2)
        return pltpu.make_async_copy(
            part.at[block], mine.at[target, kind], load_sems.at[target * 4 + kind]
        )

    def begin():
        for target in order:
            for kind in walk:
                load(target, kind).start()
                block = place.block(full, target, db=kind % 2, dc=1, dy=kind // 2)
                sender.send(
                    part.at[block], got.at[target, kind], sem_of(0, target, kind), dict(dc=1)
                )

    def rows_of(ref, which):
        return ref.at[pl.ds(which * half, half)]

    def over_cores(target):
        for kind in walk:
            load(target, kind).wait()
            sender.arrived(got.at[target, kind], sem_of(0, target, kind))
            add_rows(mine.at[target, kind], [mine.at[target, kind], got.at[target, kind]], size)
            held = mine.at[target, kind]
            if kind == 3:
                sender.send(rows_of(held, 0), side.at[target, 4], sem_of(1, target, 0), dict(db=1))
                sender.send(rows_of(held, 1), side.at[target, 5], sem_of(1, target, 1), dict(dy=1))
            if kind == 1:
                sender.send(rows_of(held, 0), side.at[target, 0], sem_of(2, target, 0), dict(db=1))
                if not full:
                    sender.send(
                        rows_of(held, 1), side.at[target, 1], sem_of(2, target, 1), dict(db=1)
                    )
            if kind == 2:
                sender.send(rows_of(held, 1), side.at[target, 3], sem_of(2, target, 3), dict(dy=1))

    def over_corner(target):
        sender.arrived(side.at[target, 4], sem_of(1, target, 0))
        held = rows_of(mine.at[target, 2], 0)
        add_rows(held, [held, side.at[target, 4]], half)
        sender.send(held, side.at[target, 2], sem_of(2, target, 2), dict(dy=1))
        sender.arrived(side.at[target, 5], sem_of(1, target, 1))
        held = rows_of(mine.at[target, 1], 1)
        add_rows(held, [held, side.at[target, 5]], half)
        sender.send(held, side.at[target, 1], sem_of(2, target, 1), dict(db=1))

    def gathered(target, which):
        held = rows_of(mine.at[target, 0], which)
        parts = [held]
        for source in (0, 2) if full else (0,):
            sender.arrived(side.at[target, source + which], sem_of(2, target, source + which))
            parts.append(side.at[target, source + which])
        return held, parts

    def line_slots(target, which):
        below, above = rows_of(up.at[target], which), rows_of(down.at[target], which)
        return below, sem_of(3, target, which), above, sem_of(3, target, 2 + which)

    def over_line(target):
        def relay(which, slot, slot_sem, at_end):
            held, parts = gathered(target, which)

            def with_slot():
                sender.arrived(slot, slot_sem)
                add_rows(held, parts + [slot], half)

            pl.when(jnp.logical_not(at_end))(with_slot)
            pl.when(at_end)(lambda: add_rows(held, parts, half))

        for which in range(2):
            below, below_sem, above, above_sem = line_slots(target, which)
            held = rows_of(mine.at[target, 0], which)
            if target > 0:
                pl.when(a < target)(
                    functools.partial(relay, which, below, below_sem, a == 0)
                )
                sender.send(held, below, below_sem, dict(da=1), a < target)
            if target < LINE - 1:
                pl.when(a > target)(
                    functools.partial(relay, which, above, above_sem, a == LINE - 1)
                )
                sender.send(held, above, above_sem, dict(da=-1), a > target)

    def own_total(target):
        for which in range(2):
            below, below_sem, above, above_sem = line_slots(target, which)
            _, parts = gathered(target, which)
            if target > 0:
                sender.arrived(below, below_sem)
                parts.append(below)
            if target < LINE - 1:
                sender.arrived(above, above_sem)
                parts.append(above)
            add_rows(rows_of(out, which), parts, half)

    stages = [over_cores] + ([over_corner] if full else []) + [over_line]

    def tick(number):
        if number == 0:
            begin()
        for level, stage in enumerate(stages):
            if 0 <= number - level < len(order):
                stage(order[number - level])
        if number == len(order) + len(stages) - 2:
            for target in range(LINE):
                pl.when(a == target)(functools.partial(own_total, target))

    return [functools.partial(tick, number) for number in range(len(order) + len(stages) - 1)]


def scatter_kernel(full, pairs, part, *refs):
    ins, out, outs = refs[:pairs], refs[pairs], refs[pairs + 1 : 2 * pairs + 1]
    mine, got, side, up, down, load_sems, send_sems, recv_sems, pair_sems = refs[2 * pairs + 1 :]
    place = Place()
    sender = Sender(place, send_sems)
    place.greet(full or pairs > 0)
    send_pairs(sender, ins, outs, pair_sems)
    scratch = (mine, got, side, up, down, load_sems, recv_sems)
    for tick in scatter_ticks(place, sender, full, part, out, scratch):
        tick()
    take_pairs(sender, outs, pair_sems)
    sender.finish()


def scatter_scratch(full, rows, width, dtype, pairs):
    kinds = 4 if full else 2
    return [
        pltpu.VMEM((LINE, kinds, rows, width), dtype),
        pltpu.VMEM((LINE, kinds, rows, width), dtype),
        pltpu.VMEM((LINE, 6, rows // 2, width), dtype),
        pltpu.VMEM((LINE, rows, width), dtype),
        pltpu.VMEM((LINE, rows, width), dtype),
        pltpu.SemaphoreType.DMA((LINE * 4,)),
        pltpu.SemaphoreType.DMA((pairs + LINE * (4 + 6 + 4),)),
        pltpu.SemaphoreType.DMA((4, LINE * 4)),
        pltpu.SemaphoreType.DMA((max(pairs, 1),)),
    ]


def gather_scatter_kernel(count, gated, *refs):
    ins, part = refs[:count], refs[count]
    outs, total = refs[count + 1 : 2 * count + 1], refs[2 * count + 1]
    local_sems, gather_sends, gather_recvs = refs[2 * count + 2 : 2 * count + 5]
    mine, got, side, up, down, load_sems, scatter_sends, scatter_recvs, _ = refs[2 * count + 5 :]
    place = Place()
    gatherer = Sender(place, gather_sends)
    scatterer = Sender(place, scatter_sends)
    place.greet(True)
    scratch = (mine, got, side, up, down, load_sems, scatter_recvs)
    ticks = [
        scatter_ticks(place, scatterer, True, part, total, scratch),
        gather_ticks(place, gatherer, False, gated, ins, outs, local_sems, gather_recvs),
    ]
    for number in range(max(len(steps) for steps in ticks)):
        for steps in ticks:
            if number < len(steps):
                steps[number]()
    scatterer.finish()
    gatherer.finish()


def gather_and_scatter(arrays, part, collective_id, gated=()):
    blocks = LINE * SQUARE * CORES
    count = len(arrays)
    _, rows, width = part.shape
    sends = count * (2 * LINE - 1) * 2 * 5
    moved = sum(blocks * 2 * x.size * x.dtype.itemsize for x in arrays)
    return pl.pallas_call(
        functools.partial(gather_scatter_kernel, count, gated),
        out_shape=[jax.ShapeDtypeStruct((blocks,) + x.shape, x.dtype) for x in arrays]
        + [jax.ShapeDtypeStruct((rows, width), jnp.float32)],
        in_specs=[pl.BlockSpec(memory_space=pl.ANY)] * (count + 1),
        out_specs=[pl.BlockSpec(memory_space=pl.ANY)] * count
        + [pl.BlockSpec(memory_space=pltpu.VMEM)],
        scratch_shapes=[
            pltpu.SemaphoreType.DMA((count,)),
            pltpu.SemaphoreType.DMA((sends,)),
            pltpu.SemaphoreType.DMA((count, blocks * 2)),
        ]
        + scatter_scratch(True, rows, width, part.dtype, 0),
        compiler_params=pltpu.CompilerParams(
            collective_id=collective_id, has_side_effects=True, vmem_limit_bytes=VMEM_LIMIT
        ),
        cost_estimate=pl.CostEstimate(flops=0, bytes_accessed=6 * moved, transcendentals=0),
    )(*arrays, part)


def scatter_rows(part, full, collective_id, swapped=()):
    blocks, rows, width = part.shape
    pairs = len(swapped)
    return pl.pallas_call(
        functools.partial(scatter_kernel, full, pairs),
        out_shape=[jax.ShapeDtypeStruct((rows, width), jnp.float32)]
        + [jax.ShapeDtypeStruct(x.shape, x.dtype) for x in swapped],
        in_specs=[pl.BlockSpec(memory_space=pl.ANY)] * (1 + pairs),
        out_specs=[pl.BlockSpec(memory_space=pltpu.VMEM)]
        + [pl.BlockSpec(memory_space=pl.ANY)] * pairs,
        scratch_shapes=scatter_scratch(full, rows, width, part.dtype, pairs),
        compiler_params=pltpu.CompilerParams(
            collective_id=collective_id, has_side_effects=True, vmem_limit_bytes=VMEM_LIMIT
        ),
        cost_estimate=pl.CostEstimate(
            flops=0, bytes_accessed=12 * part.size * part.dtype.itemsize, transcendentals=0
        ),
    )(part, *swapped)


def contract_last(left, right):
    return lax.dot_general(
        left, right, (((1,), (1,)), ((), ())), preferred_element_type=jnp.float32
    )


def contract_first(left, right):
    return lax.dot_general(
        left, right, (((0,), (0,)), ((), ())), preferred_element_type=jnp.float32
    )


def expert_kernel(
    capacity,
    normed,
    grads,
    routes,
    router_rows,
    w_gate,
    w_up,
    w_down,
    shared_in,
    shared_out,
    out_part,
    d_part,
    ex_rows,
    ex_grads,
    act_out,
    d_gate_out,
    d_up_out,
    shared_in_grad,
    shared_out_grad,
    in_total,
    out_total,
):
    position = lax.axis_index("expert")
    experts = lax.axis_size("expert")
    group, rows, width = normed.shape
    tokens, slots = group * rows, group * capacity
    bf16 = jnp.bfloat16
    x = normed[...].reshape(tokens, width)
    g = grads[...].reshape(tokens, width)

    row = lax.broadcasted_iota(jnp.int32, (tokens, tokens), 0)
    column = lax.broadcasted_iota(jnp.int32, (tokens, tokens), 1)
    before = jnp.logical_and(column < row, lax.div(row, rows) == lax.div(column, rows))
    named = routes[...].reshape(tokens, -1) == position.astype(jnp.float32).astype(bf16)
    hit = jnp.sum(jnp.where(named, 1.0, 0.0), axis=1, keepdims=True)
    tally = matrix_product(
        jnp.where(before, 1.0, 0.0).astype(bf16),
        jnp.broadcast_to(hit, (tokens, 128)).astype(bf16),
    )
    place = jnp.where(hit > 0.5, tally[:, :1], -1.0)
    token = lax.broadcasted_iota(jnp.int32, (tokens, slots), 0)
    slot = lax.broadcasted_iota(jnp.int32, (tokens, slots), 1)
    same = lax.div(slot, capacity) == lax.div(token, rows)
    wanted = lax.rem(slot, capacity).astype(jnp.float32)
    chosen = jnp.where(jnp.logical_and(same, wanted == place), 1.0, 0.0)
    pick = chosen.T.astype(bf16)
    put = chosen.astype(bf16)

    r = matrix_product(pick, x).astype(bf16)
    gr = matrix_product(pick, g).astype(bf16)
    ex_rows[...] = r
    ex_grads[...] = gr
    lane = lax.broadcasted_iota(jnp.int32, (slots, router_rows.shape[0]), 1)
    logits = jnp.where(lane < experts, contract_last(r, router_rows[...]), -1e30)
    exps = jnp.exp(logits - jnp.max(logits, axis=1, keepdims=True))
    gate = jnp.sum(jnp.where(lane == position, exps, 0.0), axis=1, keepdims=True) / jnp.sum(
        exps, axis=1, keepdims=True
    )

    pre_gate = contract_last(r, w_gate[...])
    pre_up = contract_last(r, w_up[...])
    act_gate, slope = silu_parts(pre_gate)
    act = act_gate * pre_up
    back = contract_last(gr, w_down[...])
    d_gate_slot = jnp.sum(act * back, axis=1, keepdims=True)
    scaled = (gate * act).astype(bf16)
    d_act = gate * back
    d_pre_gate = (d_act * pre_up * slope).astype(bf16)
    d_pre_up = (d_act * act_gate).astype(bf16)
    act_out[...] = scaled
    d_gate_out[...] = d_pre_gate
    d_up_out[...] = d_pre_up
    ex_out = matrix_product(scaled, w_down[...]).astype(bf16)
    d_ex = matrix_product(d_pre_gate, w_gate[...]) + matrix_product(d_pre_up, w_up[...])
    d_ex = d_ex.astype(bf16)

    units = shared_out.shape[0]
    mix = matrix_product(x, shared_in[...])
    sh_gate, sh_up = mix[:, :units], mix[:, units:]
    sh_silu, sh_slope = silu_parts(sh_gate)
    sh_act = (sh_silu * sh_up).astype(bf16)
    d_sh_act = contract_last(g, shared_out[...])
    d_mix = jnp.concatenate([d_sh_act * sh_up * sh_slope, d_sh_act * sh_silu], axis=1)
    d_mix = d_mix.astype(bf16)

    out = matrix_product(put, ex_out) + matrix_product(sh_act, shared_out[...])
    out_part[...] = out.astype(bf16).reshape(group, rows, width)
    d_in = matrix_product(put, d_ex) + contract_last(d_mix, shared_in[...])
    d_part[:, :, :width] = d_in.astype(bf16).reshape(group, rows, width)
    lane = lax.broadcasted_iota(jnp.int32, (slots, d_part.shape[2] - width), 1)
    d_gates = jnp.where(lane == position, d_gate_slot, 0.0).astype(bf16)
    d_part[:, :, width:] = matrix_product(put, d_gates).astype(bf16).reshape(group, rows, -1)

    step = pl.program_id(0)

    @pl.when(step == 0)
    def _():
        in_total[...] = jnp.zeros_like(in_total)
        out_total[...] = jnp.zeros_like(out_total)

    in_total[...] += contract_first(d_mix, x)
    out_total[...] += contract_first(sh_act, g)

    @pl.when(step == pl.num_programs(0) - 1)
    def _():
        shared_in_grad[...] = in_total[...].T.astype(bf16)
        shared_out_grad[...] = out_total[...]


def expert_phase(
    all_normed, all_grads, router_rows, w_gate, w_up, w_down, shared_in, shared_out, capacity
):
    blocks, rows, width = all_normed.shape
    group = 4
    slots = group * capacity
    hidden = w_gate.shape[0]
    units = shared_out.shape[0]
    side = all_grads.shape[2] - width
    bf16 = jnp.bfloat16

    def by_group(shape):
        zeros = (0,) * (len(shape) - 1)
        return pl.BlockSpec(shape, lambda i: (i,) + zeros)

    def fixed(shape):
        return pl.BlockSpec(
            shape, lambda i: (0,) * len(shape), pipeline_mode=pl.Buffered(buffer_count=1)
        )

    return pl.pallas_call(
        functools.partial(expert_kernel, capacity),
        grid=(blocks // group,),
        out_shape=[
            jax.ShapeDtypeStruct((blocks, rows, width), bf16),
            jax.ShapeDtypeStruct((blocks, rows, width + side), bf16),
            jax.ShapeDtypeStruct((blocks * capacity, width), bf16),
            jax.ShapeDtypeStruct((blocks * capacity, width), bf16),
            jax.ShapeDtypeStruct((blocks * capacity, hidden), bf16),
            jax.ShapeDtypeStruct((blocks * capacity, hidden), bf16),
            jax.ShapeDtypeStruct((blocks * capacity, hidden), bf16),
            jax.ShapeDtypeStruct((width, 2 * units), bf16),
            jax.ShapeDtypeStruct((units, width), jnp.float32),
        ],
        in_specs=[
            by_group((group, rows, width)),
            by_group((group, rows, width)),
            pl.BlockSpec((group, rows, side), lambda i: (i, 0, width // side)),
            fixed(router_rows.shape),
            fixed(w_gate.shape),
            fixed(w_up.shape),
            fixed(w_down.shape),
            fixed(shared_in.shape),
            fixed(shared_out.shape),
        ],
        out_specs=[
            by_group((group, rows, width)),
            by_group((group, rows, width + side)),
            by_group((slots, width)),
            by_group((slots, width)),
            by_group((slots, hidden)),
            by_group((slots, hidden)),
            by_group((slots, hidden)),
            fixed((width, 2 * units)),
            fixed((units, width)),
        ],
        scratch_shapes=[
            pltpu.VMEM((2 * units, width), jnp.float32),
            pltpu.VMEM((units, width), jnp.float32),
        ],
        compiler_params=pltpu.CompilerParams(vmem_limit_bytes=VMEM_LIMIT),
        cost_estimate=pl.CostEstimate(
            flops=2 * blocks * capacity * width * hidden * 6,
            bytes_accessed=10 * blocks * rows * width * 2,
            transcendentals=blocks * capacity * hidden,
        ),
    )(all_normed, all_grads, all_grads, router_rows, w_gate, w_up, w_down, shared_in, shared_out)


def exchange_kernel(x, out, local_sem, send_sems, recv_sems):
    me, y = lax.axis_index("expert"), lax.axis_index("fsdp")
    count = x.shape[0]
    barrier = pltpu.get_barrier_semaphore()
    peers = [lax.rem(me + step, count) for step in range(1, count)]
    for peer in peers:
        pl.semaphore_signal(barrier, inc=1, device_id=(peer, y), device_id_type=MESH)
    own = pltpu.make_async_copy(x.at[me], out.at[me], local_sem)
    own.start()
    pl.semaphore_wait(barrier, count - 1)
    copies = []
    for at, peer in enumerate(peers):
        copy = pltpu.make_async_remote_copy(
            src_ref=x.at[peer],
            dst_ref=out.at[me],
            send_sem=send_sems.at[at],
            recv_sem=recv_sems.at[at],
            device_id=(peer, y),
            device_id_type=MESH,
        )
        copy.start()
        copies.append(copy)
    for copy in copies:
        copy.wait()
    own.wait()


def exchange(x, collective_id):
    count = x.shape[0]
    return pl.pallas_call(
        exchange_kernel,
        out_shape=jax.ShapeDtypeStruct(x.shape, x.dtype),
        in_specs=[pl.BlockSpec(memory_space=pl.ANY)],
        out_specs=pl.BlockSpec(memory_space=pl.ANY),
        scratch_shapes=[
            pltpu.SemaphoreType.DMA,
            pltpu.SemaphoreType.DMA((count - 1,)),
            pltpu.SemaphoreType.DMA((count - 1,)),
        ],
        compiler_params=pltpu.CompilerParams(collective_id=collective_id, has_side_effects=True),
        cost_estimate=pl.CostEstimate(
            flops=0, bytes_accessed=20 * x.size * x.dtype.itemsize, transcendentals=0
        ),
    )(x)


def swap_halves(value):
    half = value.shape[1] // 2
    return jnp.concatenate([value[:, half:], value[:, :half]], axis=1)


def greet_plane(place):
    me = lax.axis_index("expert")
    count = LINE * SQUARE * CORES
    barrier = pltpu.get_barrier_semaphore()
    for step in range(1, count):
        peer = (lax.rem(me + step, count), place.y)
        pl.semaphore_signal(barrier, inc=1, device_id=peer, device_id_type=MESH)
    pl.semaphore_signal(barrier, inc=1, device_id=place.device(dy=1), device_id_type=MESH)
    pl.semaphore_wait(barrier, count)


def sums_kernel(pairs, moved, small, large, *refs):
    ins = refs[:pairs]
    moved_out, small_out, large_out = refs[pairs : pairs + 3]
    outs = refs[pairs + 3 : 2 * pairs + 3]
    rest = refs[2 * pairs + 3 :]
    local_sem, exchange_sends, exchange_recvs = rest[:3]
    first, second = rest[3:12], rest[12:21]
    place = Place()
    me = lax.axis_index("expert")
    count = moved.shape[0]
    greet_plane(place)
    own = pltpu.make_async_copy(moved.at[me], moved_out.at[me], local_sem)
    own.start()
    copies = []
    for at in range(count - 1):
        copy = pltpu.make_async_remote_copy(
            src_ref=moved.at[lax.rem(me + at + 1, count)],
            dst_ref=moved_out.at[me],
            send_sem=exchange_sends.at[at],
            recv_sem=exchange_recvs.at[at],
            device_id=(lax.rem(me + at + 1, count), place.y),
            device_id_type=MESH,
        )
        copy.start()
        copies.append(copy)
    senders = [Sender(place, first[6]), Sender(place, second[6])]
    send_pairs(senders[0], ins, outs, first[8])
    ticks = [
        scatter_ticks(place, senders[0], False, small, small_out, first[:6] + (first[7],)),
        scatter_ticks(place, senders[1], True, large, large_out, second[:6] + (second[7],)),
    ]
    for number in range(max(len(steps) for steps in ticks)):
        for steps in ticks:
            if number < len(steps):
                steps[number]()
    take_pairs(senders[0], outs, first[8])
    for sender in senders:
        sender.finish()
    for copy in copies:
        copy.wait()
    own.wait()


def exchange_and_sums(moved, small, large, swapped, collective_id):
    count, pairs = moved.shape[0], len(swapped)
    hbm = pl.BlockSpec(memory_space=pl.ANY)
    vmem = pl.BlockSpec(memory_space=pltpu.VMEM)
    return pl.pallas_call(
        functools.partial(sums_kernel, pairs),
        out_shape=[
            jax.ShapeDtypeStruct(moved.shape, moved.dtype),
            jax.ShapeDtypeStruct(small.shape[1:], jnp.float32),
            jax.ShapeDtypeStruct(large.shape[1:], jnp.float32),
        ]
        + [jax.ShapeDtypeStruct(x.shape, x.dtype) for x in swapped],
        in_specs=[hbm] * (3 + pairs),
        out_specs=[hbm, vmem, vmem] + [hbm] * pairs,
        scratch_shapes=[
            pltpu.SemaphoreType.DMA,
            pltpu.SemaphoreType.DMA((count - 1,)),
            pltpu.SemaphoreType.DMA((count - 1,)),
        ]
        + scatter_scratch(False, *small.shape[1:], small.dtype, pairs)
        + scatter_scratch(True, *large.shape[1:], large.dtype, 0),
        compiler_params=pltpu.CompilerParams(
            collective_id=collective_id, has_side_effects=True, vmem_limit_bytes=VMEM_LIMIT
        ),
        cost_estimate=pl.CostEstimate(
            flops=0, bytes_accessed=12 * large.size * 2, transcendentals=0
        ),
    )(moved, small, large, *swapped)


def attend_kernel(
    rows,
    g_attn,
    w_front,
    g_lat,
    expand_head,
    cosines,
    sines,
    normed_out,
    latent_out,
    query_out,
    key_out,
    value_out,
    head_out,
    sum_out,
    log_out,
    keys,
    values,
):
    bf16 = jnp.bfloat16
    size = rows.shape[0]
    scale = (PLAIN_UNITS + ROTARY_UNITS) ** (-0.5)
    step = pl.program_id(0)
    normed, _ = norm_forward(rows[...].astype(jnp.float32), g_attn[...])
    normed = normed.astype(bf16)
    normed_out[...] = normed
    front = contract_last(normed, w_front[...])
    latent, _ = norm_forward(front[:, :LATENT_WIDTH], g_lat[...])
    latent = latent.astype(bf16)
    latent_out[...] = latent
    width = LATENT_WIDTH + ROTARY_UNITS

    def rotated(value):
        return value * cosines[...] + swap_halves(value) * sines[...]

    pairs = matrix_product(latent, expand_head[...])
    key = jnp.concatenate([pairs[:, :PLAIN_UNITS], rotated(front[:, LATENT_WIDTH:width])], axis=1)
    query = jnp.concatenate(
        [front[:, width : width + PLAIN_UNITS], rotated(front[:, width + PLAIN_UNITS :])], axis=1
    ).astype(bf16)
    key = key.astype(bf16)
    value = pairs[:, PLAIN_UNITS:].astype(bf16)
    query_out[...] = query
    key_out[...] = key
    value_out[...] = value
    here = pl.ds(pl.multiple_of(step * size, size), size)
    keys[here, :] = key
    values[here, :] = value
    row = lax.broadcasted_iota(jnp.int32, (size, size), 0)
    column = lax.broadcasted_iota(jnp.int32, (size, size), 1)
    near = jnp.where(column <= row, contract_last(query, key) * scale, -1e30)

    def over(past):
        top = jnp.max(near, axis=1, keepdims=True)
        if past:
            far = contract_last(query, keys[:past, :]) * scale
            top = jnp.maximum(top, jnp.max(far, axis=1, keepdims=True))
        exps = jnp.exp(near - top)
        total = jnp.sum(exps, axis=1, keepdims=True)
        mixed = matrix_product(exps.astype(bf16), value)
        if past:
            exps = jnp.exp(far - top)
            total = total + jnp.sum(exps, axis=1, keepdims=True)
            mixed = mixed + matrix_product(exps.astype(bf16), values[:past, :])
        mixed = mixed / total
        sum_out[...] = mixed
        head_out[...] = mixed.astype(bf16)
        wide = jnp.broadcast_to(top + jnp.log(total), (size, 128))
        log_out[0] = wide.T[:1, :]

    for at in range(keys.shape[0] // size):
        pl.when(step == at)(functools.partial(over, at * size))


def attend(rows, g_attn, w_front, g_lat, expand_head, cosines, sines):
    seq_len, width = rows.shape
    size = 256
    steps = seq_len // size
    units = PLAIN_UNITS + ROTARY_UNITS
    bf16 = jnp.bfloat16

    def by_step(columns):
        return pl.BlockSpec((size, columns), lambda i: (i, 0))

    def fixed(x):
        return pl.BlockSpec(
            x.shape, lambda i: (0, 0), pipeline_mode=pl.Buffered(buffer_count=1)
        )

    return pl.pallas_call(
        attend_kernel,
        grid=(steps,),
        out_shape=[
            jax.ShapeDtypeStruct((seq_len, width), bf16),
            jax.ShapeDtypeStruct((seq_len, LATENT_WIDTH), bf16),
            jax.ShapeDtypeStruct((seq_len, units), bf16),
            jax.ShapeDtypeStruct((seq_len, units), bf16),
            jax.ShapeDtypeStruct((seq_len, VALUE_UNITS), bf16),
            jax.ShapeDtypeStruct((seq_len, VALUE_UNITS), bf16),
            jax.ShapeDtypeStruct((seq_len, VALUE_UNITS), jnp.float32),
            jax.ShapeDtypeStruct((steps, 1, size), jnp.float32),
        ],
        in_specs=[by_step(width)]
        + [fixed(x) for x in (g_attn, w_front, g_lat, expand_head)]
        + [by_step(ROTARY_UNITS)] * 2,
        out_specs=[
            by_step(width),
            by_step(LATENT_WIDTH),
            by_step(units),
            by_step(units),
            by_step(VALUE_UNITS),
            by_step(VALUE_UNITS),
            by_step(VALUE_UNITS),
            pl.BlockSpec((1, 1, size), lambda i: (i, 0, 0)),
        ],
        scratch_shapes=[
            pltpu.VMEM((seq_len, units), bf16),
            pltpu.VMEM((seq_len, VALUE_UNITS), bf16),
        ],
        compiler_params=pltpu.CompilerParams(vmem_limit_bytes=VMEM_LIMIT),
        cost_estimate=pl.CostEstimate(
            flops=2 * seq_len * (width * 768 + seq_len * units),
            bytes_accessed=3 * rows.size * 2,
            transcendentals=seq_len * seq_len // 2,
        ),
    )(rows, g_attn, w_front, g_lat, expand_head, cosines, sines)


def attend_back_kernel(
    query,
    key,
    value,
    d_head,
    head_sum,
    logs,
    expand_head,
    cosines,
    sines,
    d_query_out,
    d_pairs_out,
    d_keys_out,
    d_key,
    d_value,
    key_turned,
):
    bf16 = jnp.bfloat16
    size = query.shape[0]
    seq_len = key.shape[0]
    scale = (PLAIN_UNITS + ROTARY_UNITS) ** (-0.5)
    step = pl.program_id(0)

    @pl.when(step == 0)
    def _():
        d_key[...] = jnp.zeros_like(d_key)
        d_value[...] = jnp.zeros_like(d_value)
        for at in range(0, seq_len, size):
            part = key[at : at + size, :].astype(jnp.float32)
            key_turned[:, at : at + size] = part.T.astype(bf16)

    q, d_out = query[...], d_head[...]
    product = d_out.astype(jnp.float32) * head_sum[...]
    delta = jnp.sum(product.T, axis=0, keepdims=True)
    log_row = logs[0]
    row = lax.broadcasted_iota(jnp.int32, (size, size), 0)
    column = lax.broadcasted_iota(jnp.int32, (size, size), 1)

    def grads_of(at, mask):
        there = slice(at, at + size)
        scores = contract_last(key[there, :], q) * scale
        if mask:
            scores = jnp.where(row <= column, scores, -1e30)
        probs = jnp.exp(scores - log_row)
        d_probs = contract_last(value[there, :], d_out)
        d_scores = (probs * (d_probs - delta) * scale).astype(bf16)
        d_key[there, :] += matrix_product(d_scores, q)
        d_value[there, :] += matrix_product(probs.astype(bf16), d_out)
        return matrix_product(key_turned[:, there], d_scores)

    def over(past):
        total = grads_of(past, True)
        for at in range(0, past, size):
            total = total + grads_of(at, False)
        d_query = total.T
        d_rope = d_query[:, PLAIN_UNITS:]
        d_rope = d_rope * cosines[...] - swap_halves(d_rope) * sines[...]
        d_query_out[...] = jnp.concatenate([d_query[:, :PLAIN_UNITS], d_rope], axis=1).astype(bf16)

    for at in range(seq_len // size):
        pl.when(step == at)(functools.partial(over, at * size))

    @pl.when(step == seq_len // size - 1)
    def _():
        for at in range(0, seq_len, size):
            there = slice(at, at + size)
            d_pairs = jnp.concatenate(
                [d_key[there, :PLAIN_UNITS], d_value[there, :]], axis=1
            ).astype(bf16)
            d_pairs_out[there, :] = d_pairs
            d_keys_out[there, :LATENT_WIDTH] = contract_last(d_pairs, expand_head[...]).astype(bf16)
            tail = jnp.concatenate(
                [d_key[there, PLAIN_UNITS:], jnp.zeros((size, ROTARY_UNITS), jnp.float32)], axis=1
            )
            d_keys_out[there, LATENT_WIDTH:] = tail.astype(bf16)


def attend_back(query, key, value, d_head, head_sum, logs, expand_head, cosines, sines):
    seq_len, units = query.shape
    steps, _, size = logs.shape
    bf16 = jnp.bfloat16
    keys_width = LATENT_WIDTH + 2 * ROTARY_UNITS

    def by_step(columns):
        return pl.BlockSpec((size, columns), lambda i: (i, 0))

    def fixed(shape):
        return pl.BlockSpec(shape, lambda i: (0, 0), pipeline_mode=pl.Buffered(buffer_count=1))

    return pl.pallas_call(
        attend_back_kernel,
        grid=(steps,),
        out_shape=[
            jax.ShapeDtypeStruct((seq_len, units), bf16),
            jax.ShapeDtypeStruct((seq_len, PLAIN_UNITS + VALUE_UNITS), bf16),
            jax.ShapeDtypeStruct((seq_len, keys_width), bf16),
        ],
        in_specs=[
            by_step(units),
            fixed(key.shape),
            fixed(value.shape),
            by_step(VALUE_UNITS),
            by_step(VALUE_UNITS),
            pl.BlockSpec((1, 1, size), lambda i: (i, 0, 0)),
            fixed(expand_head.shape),
            by_step(ROTARY_UNITS),
            by_step(ROTARY_UNITS),
        ],
        out_specs=[
            by_step(units),
            fixed((seq_len, PLAIN_UNITS + VALUE_UNITS)),
            fixed((seq_len, keys_width)),
        ],
        scratch_shapes=[
            pltpu.VMEM((seq_len, units), jnp.float32),
            pltpu.VMEM((seq_len, VALUE_UNITS), jnp.float32),
            pltpu.VMEM((units, seq_len), bf16),
        ],
        compiler_params=pltpu.CompilerParams(vmem_limit_bytes=VMEM_LIMIT),
        cost_estimate=pl.CostEstimate(
            flops=5 * seq_len * seq_len * units,
            bytes_accessed=8 * seq_len * units * 2,
            transcendentals=seq_len * seq_len // 2,
        ),
    )(query, key, value, d_head, head_sum, logs, expand_head, cosines, sines)


def norm_back_rows(value, gain, grad):
    inverse = lax.rsqrt(jnp.mean(value * value, axis=-1, keepdims=True) + EPS)
    unit = value * inverse
    scaled = grad * gain
    d_value = inverse * (scaled - unit * jnp.mean(scaled * unit, axis=-1, keepdims=True))
    return d_value, jnp.sum(grad * unit, axis=0, keepdims=True)


def hidden_back_kernel(
    d_back,
    router,
    normed,
    hidden,
    gain,
    router_rows,
    grads,
    out_own,
    out_other,
    d_hidden_out,
    d_attn_out,
    d_heads_out,
    g_router_out,
    g_gain_out,
):
    bf16 = jnp.bfloat16
    width = hidden.shape[1]
    spare = router.shape[1]
    gates = router[...]
    d_router = d_back[:, width : width + spare]
    d_logits = gates * (d_router - jnp.sum(gates * d_router, axis=1, keepdims=True))
    d_logits = d_logits.astype(bf16)
    g_router_out[...] = contract_first(d_logits, normed[...])
    d_normed = d_back[:, :width] + matrix_product(d_logits, router_rows[...])
    d_value, g_gain = norm_back_rows(hidden[...], gain[...], d_normed)
    g_gain_out[...] = g_gain
    d_hidden = grads[...].astype(jnp.float32) + d_value
    d_hidden_out[...] = d_hidden
    d_attn = d_hidden.astype(bf16)
    d_attn_out[...] = d_attn
    shard = lax.axis_index("fsdp")
    half = out_own.shape[0] // VALUE_UNITS
    for weight, first in ((out_own, shard * half), (out_other, (1 - shard) * half)):
        product = contract_last(d_attn, weight[...]).astype(bf16)
        for at in range(half):
            d_heads_out[first + at] = product[:, at * VALUE_UNITS : (at + 1) * VALUE_UNITS]


def hidden_back(d_back, router, normed, hidden, gain, router_rows, grads, out_own, out_other):
    rows, width = hidden.shape
    heads = 2 * out_own.shape[0] // VALUE_UNITS
    return pl.pallas_call(
        hidden_back_kernel,
        out_shape=[
            jax.ShapeDtypeStruct((rows, width), jnp.float32),
            jax.ShapeDtypeStruct((rows, width), jnp.bfloat16),
            jax.ShapeDtypeStruct((heads, rows, VALUE_UNITS), jnp.bfloat16),
            jax.ShapeDtypeStruct((router.shape[1], width), jnp.float32),
            jax.ShapeDtypeStruct((1, width), jnp.float32),
        ],
        compiler_params=pltpu.CompilerParams(vmem_limit_bytes=VMEM_LIMIT),
        cost_estimate=pl.CostEstimate(
            flops=4 * rows * width * out_own.shape[0],
            bytes_accessed=4 * out_own.size + 16 * rows * width,
            transcendentals=0,
        ),
    )(d_back, router, normed, hidden, gain, router_rows, grads, out_own, out_other)


def input_back_kernel(
    d_query,
    d_sums,
    query_own,
    query_other,
    tokens,
    gain,
    w_latent,
    lat_gain,
    cosines,
    sines,
    d_hidden,
    d_tokens_out,
    g_latent_out,
    g_gain_out,
    g_lat_out,
):
    bf16 = jnp.bfloat16
    x = tokens[...].astype(jnp.float32)
    normed, _ = norm_forward(x, gain[...])
    normed = normed.astype(bf16)
    latent = contract_last(normed, w_latent[:LATENT_WIDTH, :])
    d_compact, g_lat = norm_back_rows(latent, lat_gain[...], d_sums[:, :LATENT_WIDTH])
    g_lat_out[...] = g_lat
    d_rope = d_sums[:, LATENT_WIDTH : LATENT_WIDTH + ROTARY_UNITS]
    d_rope = d_rope * cosines[...] - swap_halves(d_rope) * sines[...]
    d_latent = jnp.concatenate([d_compact, d_rope], axis=1).astype(bf16)
    g_latent_out[...] = contract_first(d_latent, normed)
    d_full = jnp.concatenate([d_query[at] for at in range(d_query.shape[0])], axis=1)
    own = contract_last(d_full, query_own[...])
    other = contract_last(d_full, query_other[...])
    first = lax.rem(lax.axis_index("expert"), CORES) == 0
    lower, upper = jnp.where(first, own, other), jnp.where(first, other, own)
    size = lower.shape[1] // 2
    d_normed = jnp.concatenate(
        [lower[:, :size], upper[:, :size], lower[:, size:], upper[:, size:]], axis=1
    )
    d_normed = d_normed + matrix_product(d_latent, w_latent[...])
    d_value, g_gain = norm_back_rows(x, gain[...], d_normed)
    g_gain_out[...] = g_gain
    d_tokens_out[...] = (d_hidden[...] + d_value).astype(bf16)


def input_back(d_query, d_sums, query_own, query_other, tokens, gain, w_latent, lat_gain, cosines, sines, d_hidden):
    rows, width = tokens.shape
    return pl.pallas_call(
        input_back_kernel,
        out_shape=[
            jax.ShapeDtypeStruct((rows, width), jnp.bfloat16),
            jax.ShapeDtypeStruct((w_latent.shape[0], width), jnp.float32),
            jax.ShapeDtypeStruct((1, width), jnp.float32),
            jax.ShapeDtypeStruct((1, LATENT_WIDTH), jnp.float32),
        ],
        compiler_params=pltpu.CompilerParams(vmem_limit_bytes=VMEM_LIMIT),
        cost_estimate=pl.CostEstimate(
            flops=4 * rows * query_own.size,
            bytes_accessed=4 * query_own.size + 16 * rows * width,
            transcendentals=0,
        ),
    )(
        d_query,
        d_sums,
        query_own,
        query_other,
        tokens,
        gain,
        w_latent,
        lat_gain,
        cosines,
        sines,
        d_hidden,
    )


def finish_kernel(query, expand, out_rows, query_out, expand_out, out_out):
    heads, units, width = query.shape
    query_out[...] = query[...].reshape(heads * units, width).astype(jnp.float32).T
    for at in range(heads):
        columns = expand.shape[2]
        expand_out[:, at * columns : (at + 1) * columns] = expand[at].astype(jnp.float32)
    out_out[...] = out_rows[...].reshape(out_out.shape).astype(jnp.float32)


def finish(query, expand, out_rows):
    heads, units, width = query.shape
    _, latents, columns = expand.shape
    _, rows, model = out_rows.shape
    return pl.pallas_call(
        finish_kernel,
        grid=(heads // 2,),
        out_shape=[
            jax.ShapeDtypeStruct((width, heads * units), jnp.float32),
            jax.ShapeDtypeStruct((latents, heads * columns), jnp.float32),
            jax.ShapeDtypeStruct((heads * rows, model), jnp.float32),
        ],
        in_specs=[
            pl.BlockSpec((2, units, width), lambda i: (i, 0, 0)),
            pl.BlockSpec((2, latents, columns), lambda i: (i, 0, 0)),
            pl.BlockSpec((2, rows, model), lambda i: (i, 0, 0)),
        ],
        out_specs=[
            pl.BlockSpec((width, 2 * units), lambda i: (0, i)),
            pl.BlockSpec((latents, 2 * columns), lambda i: (0, i)),
            pl.BlockSpec((2 * rows, model), lambda i: (i, 0)),
        ],
        compiler_params=pltpu.CompilerParams(vmem_limit_bytes=VMEM_LIMIT),
        cost_estimate=pl.CostEstimate(
            flops=0, bytes_accessed=6 * heads * units * width, transcendentals=0
        ),
    )(query, expand, out_rows)


def token_gather(rows):
    return lax.all_gather(rows, ("fsdp", "expert"), axis=0, tiled=True)


def split_body(
    tokens,
    routes,
    cotangent,
    attn_gain,
    w_query,
    latent_weight,
    latent_norm_gain,
    expand_weight,
    w_out,
    ffn_gain,
    w_router,
    shared_gate,
    shared_up,
    shared_down,
    expert_gate,
    expert_up,
    expert_down,
):
    rows = tokens.shape[1]
    experts = lax.axis_size("expert")
    shards = lax.axis_size("fsdp")
    position = lax.axis_index("expert")
    blocks = experts * shards
    seq_len = rows * experts
    capacity = shards * ((rows * TOPK * 4 + experts * 3 * shards - 1) // (experts * 3 * shards))
    head_units = PLAIN_UNITS + ROTARY_UNITS
    pair_units = PLAIN_UNITS + VALUE_UNITS
    feature_width = LATENT_WIDTH + ROTARY_UNITS
    scale = head_units ** (-0.5)

    shard = lax.axis_index("fsdp")
    first = shard == 0

    query_cols = lax.dynamic_slice_in_dim(w_query, position * head_units, head_units, 1)
    expand_cols = lax.dynamic_slice_in_dim(expand_weight, position * pair_units, pair_units, 1)
    owners = experts // shards
    lat_row = jnp.pad(latent_norm_gain, (0, w_query.shape[0] - latent_norm_gain.shape[0]))
    packed = jnp.concatenate(
        [query_cols.T, w_router.T, attn_gain[None], ffn_gain[None], lat_row[None]],
        axis=0,
    )
    packed = jnp.pad(packed, ((0, -packed.shape[0] % 32), (0, 0)))
    seq_rows, other_packed, other_expand, other_latent, out_other = gather_rows(
        [tokens[0]], False, 0, swapped=[packed, expand_cols], halved=[latent_weight.T, w_out]
    )

    def whole(own, other, axis):
        return jnp.concatenate(
            [jnp.where(first, own, other), jnp.where(first, other, own)], axis=axis
        )

    lat_half = latent_norm_gain.shape[0]
    at = head_units
    packed_rows = whole(packed, other_packed, 1)
    expand_head = whole(expand_cols, other_expand, 0)
    w_latent = whole(latent_weight.T, other_latent, 1)
    w_front = jnp.concatenate([w_latent, packed_rows[:at]], axis=0)
    router_rows = packed_rows[at:]
    wrout = packed_rows[at : at + experts]
    g_attn = packed_rows[at + experts].astype(jnp.float32)
    g_ffn = packed_rows[at + experts + 1].astype(jnp.float32)
    lat_row = packed_rows[at + experts + 2]
    g_lat = jnp.concatenate(
        [lat_row[:lat_half], lat_row[w_query.shape[0] : w_query.shape[0] + lat_half]]
    ).astype(jnp.float32)
    units = shared_down.shape[0]

    core = lax.rem(position, CORES)

    def by_cores(weight):
        size = weight.shape[0] // CORES
        own = lax.dynamic_slice_in_dim(weight, core * size, size, 0)
        own = lax.all_gather(own, "fsdp", axis=0, tiled=True)
        swap = [(index, index ^ 1) for index in range(experts)]
        return own, lax.ppermute(own, "expert", swap)

    grad_rows = cotangent[0]
    grad_out = grad_rows.astype(jnp.float32)
    own_routes = jnp.pad(routes[0], ((0, 0), (0, 128 - TOPK)), constant_values=-1)
    grad_rows = jnp.concatenate([grad_rows, own_routes.astype(jnp.bfloat16)], axis=1)
    seq_rows, shared_gate, shared_up = lax.optimization_barrier(
        (seq_rows, shared_gate, shared_up)
    )
    def to_columns(weight):
        parts = weight.reshape(weight.shape[0], blocks, units).transpose(1, 0, 2)
        return lax.all_to_all(
            parts, ("expert", "fsdp"), split_axis=0, concat_axis=0, tiled=True
        ).reshape(-1, units)

    sh_cols = to_columns(jnp.concatenate([shared_gate, shared_up], axis=0)).reshape(
        blocks, 2, shared_gate.shape[0], units
    )
    lanes = -(-units // 128) * 128
    sh_cols = jnp.pad(sh_cols, ((0, 0), (0, 0), (0, 0), (0, lanes - units)))
    shared_in = sh_cols.transpose(0, 2, 1, 3).reshape(MODEL_WIDTH, 2 * lanes)
    shared_out = jnp.pad(shared_down, ((0, lanes - units), (0, 0)))
    all_grads = token_gather(grad_rows)

    x_in = tokens[0].astype(jnp.float32)
    normed, inv_attn = norm_forward(x_in, g_attn)
    normed_in = normed.astype(jnp.bfloat16)
    half_units = ROTARY_UNITS // 2
    freqs = 10000.0 ** (-np.arange(half_units) * (2.0 / ROTARY_UNITS))
    angles = np.arange(seq_len)[:, None] * freqs[None, :]
    cosine_table = jnp.asarray(np.cos(angles), jnp.float32)
    sine_table = jnp.asarray(np.sin(angles), jnp.float32)
    cosines = jnp.asarray(np.concatenate([np.cos(angles)] * 2, axis=1), jnp.float32)
    sines = jnp.asarray(np.concatenate([-np.sin(angles), np.sin(angles)], axis=1), jnp.float32)
    (
        seq_normed,
        latent_rows,
        query,
        key,
        value,
        head_rows,
        head_sum,
        logs,
    ) = attend(
        seq_rows.reshape(seq_len, MODEL_WIDTH),
        g_attn[None],
        w_front,
        g_lat[None],
        expand_head,
        cosines,
        sines,
    )
    heads = exchange(head_rows.reshape(experts, rows, VALUE_UNITS), 1)
    heads = heads.transpose(1, 0, 2).reshape(rows, experts * VALUE_UNITS)
    half_heads = w_out.shape[0]
    own_heads = lax.dynamic_slice_in_dim(heads, shard * half_heads, half_heads, 1)
    other_heads = lax.dynamic_slice_in_dim(heads, (1 - shard) * half_heads, half_heads, 1)
    hidden = x_in + matrix_product(own_heads, w_out) + matrix_product(other_heads, out_other)
    normed2, inv_ffn = norm_forward(hidden, g_ffn)
    normed_ffn = normed2.astype(jnp.bfloat16)
    router = jax.nn.softmax(outer_product(normed_ffn, wrout), axis=-1)

    normed_ffn, shared_in = lax.optimization_barrier((normed_ffn, shared_in))
    (all_normed,) = gather_rows([normed_ffn], True, 2)
    w_query, all_normed = lax.optimization_barrier((w_query, all_normed))
    query_own, query_other = by_cores(w_query)
    (
        out_part,
        d_part,
        ex_rows,
        ex_grads,
        scaled_act,
        d_pre_gate,
        d_pre_up,
        g_shared_in,
        g_shared_out,
    ) = expert_phase(
        all_normed,
        all_grads.reshape(blocks, rows, -1),
        router_rows,
        expert_gate[0].T,
        expert_up[0].T,
        expert_down[0],
        shared_in,
        shared_out,
        capacity,
    )
    g_down = inner(scaled_act, ex_grads)
    g_gate = inner(d_pre_gate, ex_rows).T
    g_up = inner(d_pre_up, ex_rows).T
    (d_back,) = scatter_rows(d_part, True, 3)
    spare = router_rows.shape[0]
    d_hidden, d_attn, d_heads, g_router, g_ffn_grad = hidden_back(
        d_back,
        jnp.pad(router, ((0, 0), (0, spare - experts))),
        normed_ffn,
        hidden,
        g_ffn[None],
        router_rows,
        cotangent[0],
        w_out,
        out_other,
    )
    g_router = g_router[:experts]
    d_head = exchange(d_heads, 4).reshape(seq_len, VALUE_UNITS)
    out_part, d_head = lax.optimization_barrier((out_part, d_head))
    out_sum = lax.psum_scatter(
        out_part.reshape(blocks * rows, MODEL_WIDTH),
        ("fsdp", "expert"),
        scatter_dimension=0,
        tiled=True,
    )
    out_grad_part = inner(heads, d_attn).astype(jnp.bfloat16)
    d_query_full, d_pairs, d_keys = attend_back(
        query, key, value, d_head, head_sum, logs, expand_head, cosines, sines
    )
    g_expand_head = inner(latent_rows, d_pairs)
    g_query_head = inner(d_query_full, seq_normed).astype(jnp.bfloat16)
    g_expand_head = g_expand_head.astype(jnp.bfloat16)

    def half_of(whole, which, axis):
        size = whole.shape[axis] // shards
        return lax.dynamic_slice_in_dim(whole, which * size, size, axis)

    own_d_query, d_sums, own_out, other_query, other_expand = exchange_and_sums(
        d_query_full.reshape(experts, rows, head_units),
        d_keys.reshape(experts, rows, -1),
        out_grad_part.reshape(blocks, -1, MODEL_WIDTH),
        [half_of(g_query_head, 1 - shard, 1), half_of(g_expand_head, 1 - shard, 0)],
        5,
    )
    def summed(own, other):
        return (own.astype(jnp.float32) + other.astype(jnp.float32)).astype(jnp.bfloat16)

    own_query = summed(half_of(g_query_head, shard, 1), other_query)
    own_expand = summed(half_of(g_expand_head, shard, 0), other_expand)
    own_out = own_out.astype(jnp.bfloat16)
    own_cosines = lax.dynamic_slice_in_dim(cosines, position * rows, rows, 0)
    own_sines = lax.dynamic_slice_in_dim(sines, position * rows, rows, 0)
    d_tokens, g_latent, g_attn_grad, g_lat_grad = input_back(
        own_d_query,
        d_sums,
        query_own,
        query_other,
        tokens[0],
        g_attn[None],
        w_latent,
        g_lat[None],
        own_cosines,
        own_sines,
        d_hidden,
    )

    half = MODEL_WIDTH // blocks
    cols = lax.all_to_all(
        g_shared_in.reshape(blocks, half, 2 * lanes),
        ("expert", "fsdp"),
        split_axis=0,
        concat_axis=0,
        tiled=True,
    )
    cols = cols.transpose(1, 0, 2).astype(jnp.float32)
    r_sgate = cols[:, :, :units].reshape(half, blocks * units)
    r_sup = cols[:, :, lanes : lanes + units].reshape(half, blocks * units)
    g_sdown = g_shared_out[:units]
    model_half = MODEL_WIDTH // shards
    small_rows = jnp.concatenate([g_latent, g_router, g_attn_grad, g_ffn_grad], axis=0)
    used = small_rows.shape[0]
    share = 2 * 32 * (-(-(used + 1) // (2 * 32 * experts)))

    def rows_for(which):
        here = small_rows[:, which * model_half : (which + 1) * model_half]
        lat = jnp.pad(
            g_lat_grad[0, which * lat_half : (which + 1) * lat_half], (0, model_half - lat_half)
        )
        full = jnp.concatenate([here, lat[None]], axis=0).astype(jnp.bfloat16)
        full = jnp.pad(full, ((0, experts * share - used - 1), (0, 0)))
        return full.reshape(experts, share, model_half)

    small_part = jnp.concatenate([rows_for(which) for which in range(shards)], axis=0)
    r_query, r_expand, r_out, small_sum = gather_and_scatter(
        [own_query, own_expand, own_out], small_part, 6
    )
    hidden, small_sum = lax.optimization_barrier((hidden, small_sum))
    output = hidden + out_sum.astype(jnp.float32)
    (small_all,) = gather_rows([small_sum.astype(jnp.bfloat16)], False, 7)
    r_query, r_expand, r_out = finish(r_query, r_expand, r_out)
    small_all = small_all.reshape(experts * share, model_half).astype(jnp.float32)
    return (
        output.astype(jnp.bfloat16)[None],
        d_tokens[None],
        small_all[feature_width + experts],
        r_query,
        small_all[:feature_width].T,
        small_all[feature_width + experts + 2, :lat_half],
        r_expand,
        r_out,
        small_all[feature_width + experts + 1],
        small_all[feature_width : feature_width + experts].T,
        r_sgate,
        r_sup,
        g_sdown,
        g_gate[None],
        g_up[None],
        g_down[None],
    )


def solution(mesh):
    shape = (mesh.shape["expert"], mesh.shape["fsdp"])
    split = shape == (LINE * SQUARE * CORES, SQUARE) and shape[0] == HEAD_COUNT
    return jax.shard_map(
        split_body if split else body,
        mesh=mesh,
        in_specs=(
            P("fsdp", "expert", None),
            P("fsdp", "expert", None),
            P("fsdp", "expert", None),
            P("fsdp"),
            P("fsdp", None),
            P("fsdp", None),
            P("fsdp"),
            P("fsdp", None),
            P("fsdp", None),
            P("fsdp"),
            P("fsdp", None),
            P(("expert", "fsdp"), None),
            P(("expert", "fsdp"), None),
            P(("expert", "fsdp"), None),
            P("expert", None, "fsdp"),
            P("expert", None, "fsdp"),
            P("expert", "fsdp", None),
        ),
        out_specs=(
            P("fsdp", "expert", None),
            P("fsdp", "expert", None),
            P("fsdp"),
            P("fsdp", None),
            P("fsdp", None),
            P("fsdp"),
            P("fsdp", None),
            P("fsdp", None),
            P("fsdp"),
            P("fsdp", None),
            P(("expert", "fsdp"), None),
            P(("expert", "fsdp"), None),
            P(("expert", "fsdp"), None),
            P("expert", None, "fsdp"),
            P("expert", None, "fsdp"),
            P("expert", "fsdp", None),
        ),
        check_vma=False,
    )
```
